32 devices in a mesh: dp: 8 (over y, x, core), mp: 4 (over z).
Axes of the slice: x: 2, y: 2, z: 4, core: 2. Of those that a mesh axis runs over, the one named last changes fastest.
Arguments:
- tokens: bfloat16 [384, 256, 384], P(('dp', 'mp')), may hold values from -6 to 6
- segment_ids: int32 [384, 256], P(('dp', 'mp')), may hold values from 0 to 3, never falling along the last dimension, each value on 1 to 160 neighbouring positions
- valid_len: int32 [384], P(('dp', 'mp')), may hold values from 192 to 256
- qkv_weight: bfloat16 [384, 1152], P('dp'), may hold values from -0.3125 to 0.3125
- out_weight: bfloat16 [384, 384], P('dp'), may hold values from -1.25 to 1.25
- up_weight: bfloat16 [384, 1536], P('dp', 'mp'), may hold values from -0.3125 to 0.3125
- down_weight: bfloat16 [384, 1536], P('dp', 'mp'), may hold values from -0.3125 to 0.3125
- conv_weight: bfloat16 [3, 384], P(None, 'dp'), may hold values from -3 to 3
- ln1_gain: bfloat16 [384], P('dp'), may hold values from 0.099609375 to 1.8984375
- ln1_shift: bfloat16 [384], P('dp'), may hold values from -3 to 3
- ln2_gain: bfloat16 [384], P('dp'), may hold values from 0.099609375 to 1.8984375
- ln2_shift: bfloat16 [384], P('dp'), may hold values from -3 to 3
- cotangent: bfloat16 [384, 256, 384], P(('dp', 'mp')), may hold values from -6 to 6
Outputs:
- layer_out: bfloat16 [384, 256, 384], P(('dp', 'mp'))
- input_grad: bfloat16 [384, 256, 384], P(('dp', 'mp'))
- grad_qkv: float32 [384, 1152], P('dp')
- grad_out: float32 [384, 384], P('dp')
- grad_up: float32 [384, 1536], P('dp', 'mp')
- grad_down: float32 [384, 1536], P('dp', 'mp')
- grad_conv: float32 [3, 384], P(None, 'dp')
- grad_ln1_gain: float32 [384], P('dp')
- grad_ln1_shift: float32 [384], P('dp')
- grad_ln2_gain: float32 [384], P('dp')
- grad_ln2_shift: float32 [384], P('dp')
The draws below stay inside these ranges and needn't reach their ends.
Inputs may be any that keep to these rules, and one draw needn't show every extreme that they name: `segment_ids`: within a row the numbers never fall, so each image is a run of consecutive positions, the longest of 160.
All inputs are finite; a program needn't handle non-finite values.
Results may differ from the reference program's by a relative error of at most 0.02.
Values may be sent and summed in bfloat16 or wider, within the bound.
No kernel may reach another device: no remote copies, remote signals or barrier semaphores. Data moves between devices by JAX's collectives and lax.ppermute only.
A program may use at most 192 MiB of HBM per device.

```python
import math
import jax
import jax.numpy as jnp
import numpy as np
from jax import lax

D = 384
HEADS = 6
FF = 1536
TAPS = 3
SEQ = 256
ROWS_DEV = 12
ROWS = 384


def set_ends(entries, stream_key, low, largest):
    spot = [jax.random.randint(jax.random.fold_in(stream_key, axis), (), 0, length) for axis, length in enumerate(entries.shape)]
    widest = entries.shape.index(max(entries.shape))
    next_to = spot[:widest] + [(spot[widest] + 1) % entries.shape[widest]] + spot[widest + 1:]
    return entries.at[tuple(spot)].set(low).at[tuple(next_to)].set(largest)


def block_scale(stream_key, dims, shards, least, largest):
    gain = 1.0
    for dim, shards_of in shards:
        draws = jax.random.uniform(jax.random.fold_in(jax.random.fold_in(stream_key, 6), dim), (shards_of,), jnp.float32, least / len(shards), largest / len(shards))
        gain = gain * jnp.repeat(jnp.exp(draws), dims[dim] // shards_of).reshape((-1,) + (1,) * (len(dims) - 1 - dim))
    return gain


def profile(amount, total, reach, skew):
    loads = [(1 << 20) // math.isqrt(standing ** skew) + 1 for standing in range(2, amount + 1)]
    spare, counts = total - reach - (amount - 1), [1] * (amount - 1)
    while spare > 0:
        candidates = [i for i in range(amount - 1) if counts[i] < reach]
        mass, left = sum([loads[i] for i in candidates]), spare
        for i in candidates:
            more = min(reach - counts[i], max(1, left * loads[i] // mass), spare)
            counts[i] = counts[i] + more
            spare = spare - more
    return np.array([reach] + counts)


def ragged(rng, amount, total, reach, lean):
    if amount == 2:
        one = jax.random.randint(rng, (), max(1, total - reach), min(reach, total - 1) + 1)
        return jnp.stack([one, total - one])
    sizes = jnp.asarray(profile(amount, total, reach, lean), jnp.int32)
    twos = (amount - 1) // 2
    giver, receiver = sizes[1:1 + 2 * twos:2], sizes[2:2 + 2 * twos:2]
    margin = jnp.minimum(giver - 1, reach - receiver)
    shifted = jax.random.randint(jax.random.fold_in(rng, 1), (twos,), 0, 1 << 20) % (margin + 1)
    sizes = sizes.at[1:1 + 2 * twos:2].set(giver - shifted).at[2:2 + 2 * twos:2].set(receiver + shifted)
    return sizes[jax.random.permutation(jax.random.fold_in(rng, 2), amount)]


def normal_values(own_key, extent, scale, reach, shards=(), held_as=jnp.bfloat16):
    loudness = block_scale(own_key, extent, shards, -0.22, 0.18) if shards else 1.0
    values = jax.random.normal(own_key, extent, jnp.float32) * scale * loudness
    return jnp.minimum(jnp.maximum(values, -reach), reach).astype(held_as)


def setup_inputs(seed: int = 0) -> dict:
    splits = jax.random.split(jax.random.key(seed), 14)
    return {
        "tokens": normal_values(splits[0], (ROWS, SEQ, D), 1.0, 6.0, ((0, 32),)),
        "segment_ids": jax.vmap(lambda own: jnp.searchsorted(jnp.cumsum(ragged(own, max(2, SEQ // 64), SEQ, SEQ // 2 + SEQ // 8, 2)), jnp.arange(SEQ), side="right"))(jax.random.split(splits[1], ROWS)).reshape((ROWS, SEQ)).astype(jnp.int32),
        "valid_len": set_ends(jax.random.randint(splits[2], (ROWS,), SEQ - SEQ // 4, SEQ + 1), jax.random.fold_in(splits[2], 1), SEQ - SEQ // 4, SEQ).astype(jnp.int32),
        "qkv_weight": normal_values(splits[3], (D, 3 * D), D ** -0.5, 0.3125, ((0, 8),)),
        "out_weight": normal_values(splits[4], (D, D), (D // 16) ** -0.5, 1.25, ((0, 8),)),
        "up_weight": normal_values(splits[5], (D, FF), D ** -0.5, 0.3125, ((0, 8), (1, 4))),
        "down_weight": normal_values(splits[6], (D, FF), (FF // 4) ** -0.5, 0.3125, ((0, 8), (1, 4))),
        "conv_weight": normal_values(splits[7], (TAPS, D), 0.5, 3.0, ((1, 8),)),
        "ln1_gain": jnp.clip(1.0 + 0.18 * jax.random.normal(splits[8], (D,), jnp.float32), 0.099609375, 1.8984375).astype(jnp.bfloat16),
        "ln1_shift": normal_values(splits[9], (D,), 0.5, 3.0, ((0, 8),)),
        "ln2_gain": jnp.clip(1.0 + 0.18 * jax.random.normal(splits[10], (D,), jnp.float32), 0.099609375, 1.8984375).astype(jnp.bfloat16),
        "ln2_shift": normal_values(splits[11], (D,), 0.5, 3.0, ((0, 8),)),
        "cotangent": normal_values(splits[12], (ROWS, SEQ, D), 1.0, 6.0, ((0, 32),)),
    }


highest = lax.Precision.HIGHEST

@jax.custom_vjp
def low(v):
    return lax.optimization_barrier(v.astype(jnp.bfloat16)).astype(jnp.float32)

@jax.custom_vjp
def low_back(v):
    return v

def low_keep(v):
    return (low(v), None)

def low_pass(kept, grad):
    return (grad,)

def back_keep(v):
    return (v, None)

def back_low(kept, grad):
    return (low(grad),)
low.defvjp(low_keep, low_pass)
low_back.defvjp(back_keep, back_low)

def exact_gelu(values):
    return jax.nn.gelu(values, approximate=False)

def layer_norm(values, ln_gain, ln_shift):
    average = lax.optimization_barrier(jnp.mean(values, axis=-1, keepdims=True))
    centred = values - average
    spread = lax.optimization_barrier(jnp.mean(centred * centred, axis=-1, keepdims=True))
    return centred * lax.rsqrt(spread + 1e-06) * ln_gain + ln_shift

def row_links(segment_ids, valid_len):
    positions = lax.broadcasted_iota(jnp.int32, segment_ids.shape, 1)
    in_range = positions < valid_len[:, None]
    joined = (segment_ids[:, 1:] == segment_ids[:, :-1]) & in_range[:, 1:] & in_range[:, :-1]
    zero_first = jnp.zeros_like(joined[:, :1])
    return jnp.concatenate([zero_first, joined], axis=1).astype(jnp.float32)

def depthwise(values, conv_weight, links):
    zero_edge = jnp.zeros_like(values[:, :1])
    preceding = jnp.concatenate([zero_edge, values[:, :-1]], axis=1) * links[:, :, None]
    next_links = jnp.concatenate([links[:, 1:], jnp.zeros_like(links[:, :1])], axis=1)
    following = jnp.concatenate([values[:, 1:], zero_edge], axis=1) * next_links[:, :, None]
    return preceding * conv_weight[0] + values * conv_weight[1] + following * conv_weight[2]

def attention_mask(segment_ids, valid_len):
    positions = lax.broadcasted_iota(jnp.int32, segment_ids.shape, 1)
    in_range = positions < valid_len[:, None]
    same_image = segment_ids[:, :, None] == segment_ids[:, None, :]
    self_pair = positions[:, :, None] == positions[:, None, :]
    return same_image & in_range[:, None, :] | self_pair

def forward_rows(tokens, segment_ids, valid_len, params):
    qkv_weight, out_weight, up_weight, down_weight, conv_weight, ln1_gain, ln1_shift, ln2_gain, ln2_shift = params
    row_count, seq_len, model_width = tokens.shape
    head_dim = model_width // HEADS
    links = row_links(segment_ids, valid_len)
    allowed = attention_mask(segment_ids, valid_len)
    mixed_conv = tokens + depthwise(tokens, conv_weight, links)
    normed = low(layer_norm(mixed_conv, ln1_gain, ln1_shift))
    projected = low(low_back(jnp.einsum('rsd,de->rse', normed, qkv_weight, precision=highest)))
    projected = projected.reshape(row_count, seq_len, 3, HEADS, head_dim)
    queries = projected[:, :, 0]
    key_heads = projected[:, :, 1]
    value_heads = projected[:, :, 2]
    logits = low_back(jnp.einsum('rqhc,rkhc->rhqk', queries, key_heads, precision=highest))
    scores = jnp.where(allowed[:, None], logits * head_dim ** (-0.5), -1e+30)
    softened = low(jax.nn.softmax(scores, axis=-1))
    attended = low(low_back(jnp.einsum('rhqk,rkhc->rqhc', softened, value_heads, precision=highest)))
    attended = attended.reshape(row_count, seq_len, model_width)
    branch = low_back(jnp.einsum('rsd,de->rse', attended, out_weight, precision=highest))
    mixed_attn = mixed_conv + branch
    normed_mlp = low(layer_norm(mixed_attn, ln2_gain, ln2_shift))
    hidden_pre = low_back(jnp.einsum('rsd,df->rsf', normed_mlp, up_weight, precision=highest))
    hidden = low(exact_gelu(hidden_pre))
    mlp_out = low_back(jnp.einsum('rsf,df->rsd', hidden, down_weight, precision=highest))
    return mixed_attn + mlp_out

def reference(tokens, segment_ids, valid_len, qkv_weight, out_weight, up_weight, down_weight, conv_weight, ln1_gain, ln1_shift, ln2_gain, ln2_shift, cotangent):
    params = tuple((item.astype(jnp.float32) for item in (qkv_weight, out_weight, up_weight, down_weight, conv_weight, ln1_gain, ln1_shift, ln2_gain, ln2_shift)))
    groups = tokens.shape[0] // ROWS_DEV
    shaped = tokens.astype(jnp.float32).reshape(groups, ROWS_DEV, SEQ, D)
    seg_groups = segment_ids.reshape(groups, ROWS_DEV, SEQ)
    len_groups = valid_len.reshape(groups, ROWS_DEV)

    def whole(inputs, weights):

        def one_group(item):
            return forward_rows(item[0], item[1], item[2], weights)
        return lax.map(jax.checkpoint(one_group), (inputs, seg_groups, len_groups))
    result, pullback = jax.vjp(whole, shaped, params)
    grad_in, grad_params = pullback(cotangent.astype(jnp.float32).reshape(groups, ROWS_DEV, SEQ, D))
    layer_out = result.reshape(tokens.shape).astype(jnp.bfloat16)
    input_grad = grad_in.reshape(tokens.shape).astype(jnp.bfloat16)
    return (layer_out, input_grad, grad_params[0], grad_params[1], grad_params[2], grad_params[3], grad_params[4], grad_params[5], grad_params[6], grad_params[7], grad_params[8])
```

```python
import functools
import math

import jax
import jax.numpy as jnp
from jax import lax
from jax.experimental import pallas as pl
from jax.experimental.pallas import tpu as pltpu
from jax.sharding import PartitionSpec as P

HEADS = 6
BF = jnp.bfloat16
F32 = jnp.float32
VMEM_LIMIT = 60 * 1024 * 1024


def mm(lhs, rhs):
    return lax.dot_general(lhs, rhs, (((1,), (0,)), ((), ())), preferred_element_type=F32)


def mm_nt(lhs, rhs):
    return lax.dot_general(lhs, rhs, (((1,), (1,)), ((), ())), preferred_element_type=F32)


def lane_mean(values):
    return jnp.sum(values, axis=-1, keepdims=True) * (1.0 / values.shape[-1])


def normalize(values):
    centred = values - lane_mean(values)
    spread = lane_mean(centred * centred)
    scale = lax.rsqrt(spread + 1e-06)
    return centred * scale, scale


def fold_rows(values):
    rows, width = values.shape
    return jnp.sum(values.reshape(rows // 8, 8, width), axis=0)


def forward_attention(
    tok_ref, aux_ref, w_ref, q_ref, k_ref, v_ref, e_ref, att_ref, inv_ref, mc_ref, small_ref, wt_ref
):
    rows, seq, width = tok_ref.shape
    head = width // HEADS

    @pl.when(pl.program_id(0) == 0)
    def _():
        wt_ref[...] = w_ref[:, : 3 * width].T
        small_ref[...] = w_ref[:, 4 * width :].T[:8].astype(F32)

    conv0, conv1, conv2 = small_ref[0:1], small_ref[1:2], small_ref[2:3]
    gain, shift = small_ref[3:4], small_ref[4:5]
    row_id = lax.broadcasted_iota(jnp.int32, (seq, seq), 0)
    col_id = lax.broadcasted_iota(jnp.int32, (seq, seq), 1)
    for r in range(rows):
        aux = aux_ref[r]
        aux_t = aux.T
        base = tok_ref[r].astype(F32)
        before = pltpu.roll(base, 1, 0) * aux_t[:, 0:1]
        after = pltpu.roll(base, seq - 1, 0) * aux_t[:, 1:2]
        mixed = base + before * conv0 + base * conv1 + after * conv2
        mc_ref[r] = mixed
        normed = (normalize(mixed)[0] * gain + shift).astype(BF)
        allowed = (aux_t[:, 2:3] == aux[2:3]) & (aux_t[:, 3:4] > 0.5) | (row_id == col_id)
        bias = jnp.where(allowed, 0.0, -1e30)
        proj = mm_nt(wt_ref[...], normed)
        q_t = (proj[:width].astype(BF).astype(F32) * head ** (-0.5)).astype(BF)
        k_t = proj[width : 2 * width].astype(BF)
        v_t = proj[2 * width :].astype(BF)
        q_ref[r] = q_t
        k_ref[r] = k_t
        keys = k_t.T
        v_ref[r] = v_t.T
        zero = jnp.zeros((head, seq), BF)
        for h in range(HEADS):
            own = q_t[h * head : (h + 1) * head]
            pair = [own, zero] if h % 2 == 0 else [zero, own]
            lanes = slice(h // 2 * 2 * head, (h // 2 + 1) * 2 * head)
            scores = mm(keys[:, lanes], jnp.concatenate(pair, axis=0)) + bias
            raised = jnp.exp(scores - jnp.max(scores, axis=0, keepdims=True))
            inverse = 1.0 / jnp.sum(raised, axis=0, keepdims=True)
            raised = raised.astype(BF)
            e_ref[r, h] = raised
            inv_ref[r, h : h + 1] = inverse
            att = mm(v_t[h * head : (h + 1) * head], raised) * inverse
            att_ref[r, h * head : (h + 1) * head] = att.astype(BF)


def gelu_parts(x):
    size = jnp.abs(x)
    t = 1.0 / (1.0 + (0.3275911 * math.sqrt(0.5)) * size)
    poly = t * (
        0.127414796 + t * (-0.142248368 + t * (0.7107068705 + t * (-0.7265760135 + t * 0.5307027145)))
    )
    bell = jnp.exp(-0.5 * (x * x))
    tail = poly * bell
    cdf = jnp.where(x >= 0.0, 1.0 - tail, tail)
    return x * cdf, cdf + x * (bell * 0.3989422804014327)


def feed_forward(
    att_ref, mc_ref, ct_ref, up_ref, down_ref, out_ref, small_ref,
    lo_ref, gm_ref, ga_ref, gw_ref, go_ref, gs_ref,
    up_acc, down_acc, out_acc, gain_acc, shift_acc,
):
    rows, seq, width = ct_ref.shape
    ff = up_ref.shape[1]
    chunk = 512 if ff % 512 == 0 else ff
    step = pl.program_id(0)

    @pl.when(step == 0)
    def _():
        for acc in (up_acc, down_acc, out_acc, gain_acc, shift_acc):
            acc[...] = jnp.zeros_like(acc)

    gain, shift = small_ref[5:6], small_ref[6:7]
    for r in range(rows):
        att_t = att_ref[r]
        mixed = mc_ref[r] + mm(att_t.T, out_ref[...])
        n, scale = normalize(mixed)
        normed = (n * gain + shift).astype(BF)
        normed_t = normed.T
        ct = ct_ref[r]
        ct_t = ct.T
        mlp = jnp.zeros((seq, width), F32)
        grad_n = jnp.zeros((seq, width), F32)
        for c in range(0, ff, chunk):
            cols = slice(c, c + chunk)
            pre = mm(normed, up_ref[:, cols])
            grad_hidden = mm(ct, down_ref[:, cols])
            hidden, slope = gelu_parts(pre)
            hidden = hidden.astype(BF)
            grad_pre = (grad_hidden * slope).astype(BF)
            down_acc[:, cols] += mm(ct_t, hidden)
            up_acc[:, cols] += mm(normed_t, grad_pre)
            mlp += mm_nt(hidden, down_ref[:, cols])
            grad_n += mm_nt(grad_pre, up_ref[:, cols])
        lo_ref[r] = (mixed + mlp).astype(BF)
        gain_acc[...] += fold_rows(grad_n * n)
        shift_acc[...] += fold_rows(grad_n)
        e = grad_n * gain
        grad_mixed = ct.astype(F32) + scale * (e - lane_mean(e) - n * lane_mean(e * n))
        gm_ref[r] = grad_mixed
        branch = grad_mixed.astype(BF)
        out_acc[...] += mm(att_t, branch)
        ga_ref[r] = mm_nt(out_ref[...], branch).astype(BF)

    @pl.when(step == pl.num_programs(0) - 1)
    def _():
        gw_ref[:, :ff] = up_acc[...].astype(BF)
        gw_ref[:, ff:] = down_acc[...].astype(BF)
        go_ref[...] = out_acc[...].astype(BF)
        gs_ref[...] = jnp.zeros_like(gs_ref)
        gs_ref[5:6] = jnp.sum(gain_acc[...], axis=0, keepdims=True)
        gs_ref[6:7] = jnp.sum(shift_acc[...], axis=0, keepdims=True)


def backward_attention(
    tok_ref, aux_ref, w_ref, q_ref, k_ref, v_ref, e_ref, att_ref, inv_ref, mc_ref, ga_ref, gm_ref, small_ref,
    ig_ref, gw_ref, gs_ref,
    proj_ref, w_acc, sum_acc,
):
    rows, seq, width = tok_ref.shape
    head = width // HEADS
    step = pl.program_id(0)

    @pl.when(step == 0)
    def _():
        w_acc[...] = jnp.zeros_like(w_acc)
        sum_acc[...] = jnp.zeros_like(sum_acc)

    conv0, conv1, conv2 = small_ref[0:1], small_ref[1:2], small_ref[2:3]
    gain, shift = small_ref[3:4], small_ref[4:5]
    zero = jnp.zeros((head, seq), BF)
    for r in range(rows):
        for h in range(HEADS):
            part = slice(h * head, (h + 1) * head)
            lanes = slice(h // 2 * 2 * head, (h // 2 + 1) * 2 * head)
            inverse = inv_ref[r, h : h + 1]
            grad_att = ga_ref[r, part].astype(F32) * inverse
            inner = jnp.sum(grad_att * att_ref[r, part].astype(F32), axis=0, keepdims=True)
            grad_att = grad_att.astype(BF)
            pair = [grad_att, zero] if h % 2 == 0 else [zero, grad_att]
            grad_soft = mm(v_ref[r, :, lanes], jnp.concatenate(pair, axis=0))
            raised = e_ref[r, h]
            grad_logits = (raised.astype(F32) * (grad_soft - inner)).astype(BF)
            grad_q = mm(k_ref[r, part], grad_logits) * head ** (-0.5)
            grad_k = mm_nt(q_ref[r, part], grad_logits)
            grad_v = mm_nt(grad_att, raised)
            proj_ref[h * head : (h + 1) * head] = grad_q.astype(BF)
            proj_ref[width + h * head : width + (h + 1) * head] = grad_k.astype(BF)
            proj_ref[2 * width + h * head : 2 * width + (h + 1) * head] = grad_v.astype(BF)
        n, scale = normalize(mc_ref[r])
        normed = (n * gain + shift).astype(BF)
        grad_proj = proj_ref[...]
        w_acc[...] += mm(grad_proj, normed)
        grad_n = mm(w_ref[...], grad_proj).T
        sum_acc[3] += fold_rows(grad_n * n)
        sum_acc[4] += fold_rows(grad_n)
        e = grad_n * gain
        g = gm_ref[r] + scale * (e - lane_mean(e) - n * lane_mean(e * n))
        aux_t = aux_ref[r].T
        before = pltpu.roll(g, 1, 0) * aux_t[:, 0:1]
        after = pltpu.roll(g, seq - 1, 0) * aux_t[:, 1:2]
        base = tok_ref[r].astype(F32)
        sum_acc[0] += fold_rows(base * after)
        sum_acc[1] += fold_rows(base * g)
        sum_acc[2] += fold_rows(base * before)
        ig_ref[r] = (g + conv1 * g + conv0 * after + conv2 * before).astype(BF)

    @pl.when(step == pl.num_programs(0) - 1)
    def _():
        gw_ref[...] = w_acc[...].astype(BF).T
        gs_ref[...] = jnp.zeros_like(gs_ref)
        for i in range(5):
            gs_ref[i : i + 1] = jnp.sum(sum_acc[i], axis=0, keepdims=True)


def by_row(shape, rows):
    tail = tuple(shape[1:])
    return pl.BlockSpec((rows,) + tail, lambda i: (i,) + (0,) * len(tail))


def whole(shape, at=None):
    place = at or (0,) * len(shape)
    return pl.BlockSpec(tuple(shape), lambda i: place)


def step_rows(count, most):
    return max(r for r in range(1, most + 1) if count % r == 0)


def params():
    return pltpu.CompilerParams(dimension_semantics=("arbitrary",), vmem_limit_bytes=VMEM_LIMIT)


def run_forward(tokens, aux, wide):
    count, seq, width = tokens.shape
    rows = step_rows(count, 2)
    flipped = (count, width, seq)
    outs = [
        (flipped, BF), (flipped, BF), ((count, seq, width), BF), ((count, HEADS, seq, seq), BF),
        (flipped, BF), ((count, 8, seq), F32), ((count, seq, width), F32),
    ]
    return pl.pallas_call(
        forward_attention,
        grid=(count // rows,),
        in_specs=[by_row(tokens.shape, rows), by_row(aux.shape, rows), whole(wide.shape)],
        out_specs=[by_row(s, rows) for s, _ in outs] + [whole((8, width))],
        out_shape=[jax.ShapeDtypeStruct(s, t) for s, t in outs] + [jax.ShapeDtypeStruct((8, width), F32)],
        scratch_shapes=[pltpu.VMEM((3 * width, width), BF)],
        compiler_params=params(),
        name="forward_attention",
    )(tokens, aux, wide)


def run_feed_forward(att, mixed, cotangent, up, down, wide, small):
    count, seq, width = cotangent.shape
    ff = up.shape[1]
    rows = step_rows(count, 2)
    row_outs = [((count, seq, width), BF), ((count, seq, width), F32), ((count, width, seq), BF)]
    sum_outs = [((width, 2 * ff), BF), ((width, width), BF), ((8, width), F32)]
    return pl.pallas_call(
        feed_forward,
        grid=(count // rows,),
        in_specs=[
            by_row(att.shape, rows), by_row(mixed.shape, rows), by_row(cotangent.shape, rows),
            whole(up.shape), whole(down.shape), whole((width, width), (0, 3)), whole(small.shape),
        ],
        out_specs=[by_row(s, rows) for s, _ in row_outs] + [whole(s) for s, _ in sum_outs],
        out_shape=[jax.ShapeDtypeStruct(s, t) for s, t in row_outs + sum_outs],
        scratch_shapes=[
            pltpu.VMEM((width, ff), F32), pltpu.VMEM((width, ff), F32), pltpu.VMEM((width, width), F32),
            pltpu.VMEM((8, width), F32), pltpu.VMEM((8, width), F32),
        ],
        compiler_params=params(),
        name="feed_forward",
    )(att, mixed, cotangent, up, down, wide, small)


def run_backward(tokens, aux, wide, kept, grad_att, grad_mixed, small):
    count, seq, width = tokens.shape
    rows = step_rows(count, 2)
    row_args = (tokens, aux), (*kept, grad_att, grad_mixed)
    sum_outs = [((width, 3 * width), BF), ((8, width), F32)]
    return pl.pallas_call(
        backward_attention,
        grid=(count // rows,),
        in_specs=[by_row(a.shape, rows) for a in row_args[0]]
        + [whole((width, 3 * width))]
        + [by_row(a.shape, rows) for a in row_args[1]]
        + [whole(small.shape)],
        out_specs=[by_row(tokens.shape, rows)] + [whole(s) for s, _ in sum_outs],
        out_shape=[jax.ShapeDtypeStruct(tokens.shape, BF)] + [jax.ShapeDtypeStruct(s, t) for s, t in sum_outs],
        scratch_shapes=[
            pltpu.VMEM((3 * width, seq), BF), pltpu.VMEM((3 * width, width), F32), pltpu.VMEM((5, 8, width), F32),
        ],
        compiler_params=params(),
        name="backward_attention",
    )(*row_args[0], wide, *row_args[1], small)


def row_facts(segment_ids, valid_len):
    positions = lax.broadcasted_iota(jnp.int32, segment_ids.shape, 1)
    valid = positions < valid_len[:, None]
    joined = (segment_ids[:, 1:] == segment_ids[:, :-1]) & valid[:, 1:] & valid[:, :-1]
    edge = jnp.zeros_like(joined[:, :1])
    links = jnp.concatenate([edge, joined], axis=1).astype(F32)
    next_links = jnp.concatenate([joined, edge], axis=1).astype(F32)
    none = jnp.zeros_like(links)
    facts = [links, next_links, segment_ids.astype(F32), valid.astype(F32), none, none, none, none]
    return jnp.stack(facts, axis=1)


def on_device(
    tokens, segment_ids, valid_len, qkv_weight, out_weight, up_weight, down_weight, conv_weight,
    ln1_gain, ln1_shift, ln2_gain, ln2_shift, cotangent,
):
    count, seq, width = tokens.shape
    own = qkv_weight.shape[0]
    dp = width // own
    aux = row_facts(segment_ids, valid_len)
    vectors = jnp.stack([conv_weight[0], conv_weight[1], conv_weight[2], ln1_gain, ln1_shift, ln2_gain, ln2_shift], axis=1)
    narrow = jnp.concatenate([qkv_weight, out_weight, jnp.pad(vectors, ((0, 0), (0, 121)))], axis=1)
    wide = lax.all_gather(narrow, "dp", axis=0, tiled=True)
    both = lax.all_gather(jnp.concatenate([up_weight, down_weight], axis=0), "mp", axis=1, tiled=True)
    ff = both.shape[1]
    both = lax.all_gather(both, "dp", axis=0).reshape(dp, 2, own, ff)
    up = both[:, 0].reshape(width, ff)
    down = both[:, 1].reshape(width, ff)
    q, k, v, raised, att, inverse, mixed, small = run_forward(tokens, aux, wide)
    layer_out, grad_mixed, grad_att, grad_ff, grad_out, grad_small2 = run_feed_forward(
        att, mixed, cotangent, up, down, wide, small
    )
    input_grad, grad_qkv, grad_small1 = run_backward(
        tokens, aux, wide, (q, k, v, raised, att, inverse, mixed), grad_att, grad_mixed, small
    )
    grad_ff = lax.psum_scatter(grad_ff, "dp", scatter_dimension=0, tiled=True).reshape(own, 2, ff)
    grad_ff = lax.psum_scatter(grad_ff, "mp", scatter_dimension=2, tiled=True).astype(F32)
    grad_attn = jnp.concatenate([grad_qkv, grad_out], axis=1)
    grad_attn = lax.psum_scatter(grad_attn, "dp", scatter_dimension=0, tiled=True)
    grad_attn = lax.psum(grad_attn, "mp").astype(F32)
    sums = lax.psum(grad_small1 + grad_small2, ("dp", "mp"))
    sums = lax.dynamic_slice_in_dim(sums, lax.axis_index("dp") * own, own, axis=1)
    return (
        layer_out, input_grad, grad_attn[:, : 3 * width], grad_attn[:, 3 * width :],
        grad_ff[:, 0], grad_ff[:, 1], sums[0:3], sums[3], sums[4], sums[5], sums[6],
    )


def solution(mesh):
    rows = P(("dp", "mp"), None, None)
    weights = (P("dp", None), P("dp", None), P("dp", "mp"), P("dp", "mp"), P(None, "dp"))
    vectors = (P("dp"),) * 4
    return jax.shard_map(
        on_device,
        mesh=mesh,
        in_specs=(rows, P(("dp", "mp"), None), P(("dp", "mp"))) + weights + vectors + (rows,),
        out_specs=(rows, rows) + weights + vectors,
        check_vma=False,
    )
```

```python
import functools
import math

import jax
import jax.numpy as jnp
from jax import lax
from jax.experimental import pallas as pl
from jax.experimental.pallas import tpu as pltpu
from jax.sharding import PartitionSpec as P

HEADS = 6
VECTORS = 128
BF = jnp.bfloat16
F32 = jnp.float32
VMEM_LIMIT = 60 * 1024 * 1024


def mm(lhs, rhs):
    return lax.dot_general(lhs, rhs, (((1,), (0,)), ((), ())), preferred_element_type=F32)


def mm_nt(lhs, rhs):
    return lax.dot_general(lhs, rhs, (((1,), (1,)), ((), ())), preferred_element_type=F32)


def lane_mean(values):
    return jnp.sum(values, axis=-1, keepdims=True) * (1.0 / values.shape[-1])


def normalize(values):
    centred = values - lane_mean(values)
    spread = lane_mean(centred * centred)
    scale = lax.rsqrt(spread + 1e-06)
    return centred * scale, scale


def fold_rows(values):
    rows, width = values.shape
    return jnp.sum(values.reshape(rows // 8, 8, width), axis=0)


def tree_sum(items):
    items = list(items)
    while len(items) > 1:
        items = [a + b for a, b in zip(items[::2], items[1::2])]
    return items[0]


def pack_weights(qkv_ref, up_ref, down_ref, conv_ref, g1_ref, s1_ref, g2_ref, s2_ref, narrow_ref, ff_ref, rows_ref):
    own, ffs = up_ref.shape
    rows_ref[...] = jnp.zeros_like(rows_ref)
    rows_ref[0:3, :own] = conv_ref[...].astype(F32)
    for i, ref in enumerate((g1_ref, s1_ref, g2_ref, s2_ref)):
        rows_ref[3 + i : 4 + i, :own] = ref[...].astype(F32)
    wide = qkv_ref.shape[1]
    narrow_ref[:, :wide] = qkv_ref[...]
    narrow_ref[:, wide:] = rows_ref[...].T[:own].astype(BF)
    ff_ref[:own] = up_ref[...]
    ff_ref[own:] = down_ref[...]


def forward_attention(
    index_ref, len_ref, tok_ref, seg_ref, *refs, pieces
):
    piece_refs = refs[:pieces]
    q_ref, k_ref, v_ref, e_ref, att_ref, inv_ref, mc_ref, aux_ref, small_ref, w_ref, wt_ref, wide_ref = refs[pieces:]
    rows, seq, width = tok_ref.shape
    head = width // HEADS
    step = pl.program_id(0)

    @pl.when(step == 0)
    def _():
        own = width // pieces
        for i, ref in enumerate(piece_refs):
            wide_ref[pl.ds(pl.multiple_of(index_ref[i] * own, 16), own), :] = ref[...]
        w_ref[...] = wide_ref[:, : 3 * width]
        wt_ref[...] = wide_ref[:, : 3 * width].T
        small_ref[...] = wide_ref[:, 3 * width :].T[:8].astype(F32)

    conv0, conv1, conv2 = small_ref[0:1], small_ref[1:2], small_ref[2:3]
    gain, shift = small_ref[3:4], small_ref[4:5]
    row_id = lax.broadcasted_iota(jnp.int32, (seq, seq), 0)
    col_id = lax.broadcasted_iota(jnp.int32, (seq, seq), 1)
    place = lax.broadcasted_iota(jnp.int32, (1, seq), 1)
    for r in range(rows):
        segs = seg_ref[r].astype(F32)
        valid = place < len_ref[step * rows + r]
        number = jnp.where(valid, segs, -1.0)
        links = jnp.where(valid & (place > 0) & (number == pltpu.roll(number, 1, 1)), 1.0, 0.0)
        next_links = jnp.where(place < seq - 1, pltpu.roll(links, seq - 1, 1), 0.0)
        none = jnp.zeros_like(links)
        aux = jnp.concatenate([links, next_links, number, none, none, none, none, none], axis=0)
        aux_ref[r] = aux
        aux_t = aux.T
        base = tok_ref[r].astype(F32)
        before = pltpu.roll(base, 1, 0) * aux_t[:, 0:1]
        after = pltpu.roll(base, seq - 1, 0) * aux_t[:, 1:2]
        mixed = base + before * conv0 + base * conv1 + after * conv2
        mc_ref[r] = mixed
        normed = (normalize(mixed)[0] * gain + shift).astype(BF)
        allowed = (aux_t[:, 2:3] == segs) | (row_id == col_id)
        bias = jnp.where(allowed, 0.0, -1e30)
        proj = mm_nt(wt_ref[...], normed)
        q_t = (proj[:width].astype(BF).astype(F32) * head ** (-0.5)).astype(BF)
        k_t = proj[width : 2 * width].astype(BF)
        v_t = proj[2 * width :].astype(BF)
        q_ref[r] = q_t
        k_ref[r] = k_t
        keys = k_t.T
        v_ref[r] = v_t.T
        zero = jnp.zeros((head, seq), BF)
        for h in range(HEADS):
            own = q_t[h * head : (h + 1) * head]
            pair = [own, zero] if h % 2 == 0 else [zero, own]
            lanes = slice(h // 2 * 2 * head, (h // 2 + 1) * 2 * head)
            scores = mm(keys[:, lanes], jnp.concatenate(pair, axis=0)) + bias
            raised = jnp.exp(scores - jnp.max(scores, axis=0, keepdims=True))
            inverse = 1.0 / jnp.sum(raised, axis=0, keepdims=True)
            raised = raised.astype(BF)
            e_ref[r, h] = raised
            inv_ref[r, h : h + 1] = inverse
            att = mm(v_t[h * head : (h + 1) * head], raised) * inverse
            att_ref[r, h * head : (h + 1) * head] = att.astype(BF)


def gelu_parts(x):
    size = jnp.abs(x)
    t = 1.0 / (1.0 + (0.3275911 * math.sqrt(0.5)) * size)
    poly = t * (
        0.127414796 + t * (-0.142248368 + t * (0.7107068705 + t * (-0.7265760135 + t * 0.5307027145)))
    )
    bell = jnp.exp(-0.5 * (x * x))
    tail = poly * bell
    cdf = jnp.where(x >= 0.0, 1.0 - tail, tail)
    return x * cdf, cdf + x * (bell * 0.3989422804014327)


def feed_forward(index_ref, att_ref, mc_ref, ct_ref, small_ref, *refs, pieces, shards):
    piece_refs = refs[:pieces]
    groups = 2 if pieces > 1 else 1
    lo_ref, gm_ref, ga_ref, gs_ref = refs[pieces : pieces + 4]
    gw_refs = refs[pieces + 4 : pieces + 4 + groups]
    up_ref, down_ref, out_ref, up_acc, down_acc, out_acc, gain_acc, shift_acc = refs[pieces + 4 + groups :]
    rows, seq, width = ct_ref.shape
    ff = up_ref.shape[1]
    ffs = ff // shards
    own = width // pieces
    chunk = 512 if ff % 512 == 0 else ff
    step = pl.program_id(0)

    @pl.when(step == 0)
    def _():
        for acc in (up_acc, down_acc, out_acc, gain_acc, shift_acc):
            acc[...] = jnp.zeros_like(acc)
        for i, ref in enumerate(piece_refs):
            here = pl.ds(pl.multiple_of(index_ref[i] * own, 16), own)
            for j in range(shards):
                up_ref[here, j * ffs : (j + 1) * ffs] = ref[2 * j * own : (2 * j + 1) * own]
                down_ref[here, j * ffs : (j + 1) * ffs] = ref[(2 * j + 1) * own : (2 * j + 2) * own]
            out_ref[here, :] = ref[2 * shards * own :]

    gain, shift = small_ref[5:6], small_ref[6:7]
    for r in range(rows):
        att_t = att_ref[r]
        mixed = mc_ref[r] + mm(att_t.T, out_ref[...])
        n, scale = normalize(mixed)
        normed = (n * gain + shift).astype(BF)
        normed_t = normed.T
        ct = ct_ref[r]
        ct_t = ct.T
        mlp = jnp.zeros((seq, width), F32)
        grad_n = jnp.zeros((seq, width), F32)
        for c in range(0, ff, chunk):
            cols = slice(c, c + chunk)
            pre = mm(normed, up_ref[:, cols])
            grad_hidden = mm(ct, down_ref[:, cols])
            hidden, slope = gelu_parts(pre)
            hidden = hidden.astype(BF)
            grad_pre = (grad_hidden * slope).astype(BF)
            down_acc[:, cols] += mm(ct_t, hidden)
            up_acc[:, cols] += mm(normed_t, grad_pre)
            mlp += mm_nt(hidden, down_ref[:, cols])
            grad_n += mm_nt(grad_pre, up_ref[:, cols])
        lo_ref[r] = (mixed + mlp).astype(BF)
        gain_acc[...] += fold_rows(grad_n * n)
        shift_acc[...] += fold_rows(grad_n)
        e = grad_n * gain
        grad_mixed = ct.astype(F32) + scale * (e - lane_mean(e) - n * lane_mean(e * n))
        gm_ref[r] = grad_mixed
        branch = grad_mixed.astype(BF)
        out_acc[...] += mm(att_t, branch)
        ga_ref[r] = mm_nt(out_ref[...], branch).astype(BF)

    @pl.when(step == pl.num_programs(0) - 1)
    def _():
        for i in range(pieces):
            here = pl.ds(pl.multiple_of(index_ref[i] * own, 16), own)
            place = gw_refs[i % groups]
            for j in range(shards):
                cols = slice(j * ffs, (j + 1) * ffs)
                place[i // groups, :, 2 * j * ffs : (2 * j + 1) * ffs] = up_acc[here, cols].astype(BF)
                place[i // groups, :, (2 * j + 1) * ffs : (2 * j + 2) * ffs] = down_acc[here, cols].astype(BF)
            place[i // groups, :, 2 * ff :] = out_acc[here, :].astype(BF)
        gs_ref[...] = jnp.zeros_like(gs_ref)
        gs_ref[5:6] = jnp.sum(gain_acc[...], axis=0, keepdims=True)
        gs_ref[6:7] = jnp.sum(shift_acc[...], axis=0, keepdims=True)


def backward_attention(
    index_ref, w_ref, q_ref, k_ref, v_ref, e_ref, att_ref, inv_ref, mc_ref, ga_ref, small_ref, *refs, pieces
):
    groups = 2 if pieces > 1 else 1
    gn_ref = refs[0]
    gw_refs = refs[1 : 1 + groups]
    proj_ref, w_acc, flat_ref = refs[1 + groups :]
    rows, seq, width = v_ref.shape
    own = width // pieces
    head = width // HEADS
    step = pl.program_id(0)

    @pl.when(step == 0)
    def _():
        w_acc[...] = jnp.zeros_like(w_acc)

    gain, shift = small_ref[3:4], small_ref[4:5]
    zero = jnp.zeros((head, seq), BF)
    for r in range(rows):
        for h in range(HEADS):
            part = slice(h * head, (h + 1) * head)
            lanes = slice(h // 2 * 2 * head, (h // 2 + 1) * 2 * head)
            inverse = inv_ref[r, h : h + 1]
            grad_att = ga_ref[r, part].astype(F32) * inverse
            inner = jnp.sum(grad_att * att_ref[r, part].astype(F32), axis=0, keepdims=True)
            grad_att = grad_att.astype(BF)
            pair = [grad_att, zero] if h % 2 == 0 else [zero, grad_att]
            grad_soft = mm(v_ref[r, :, lanes], jnp.concatenate(pair, axis=0))
            raised = e_ref[r, h]
            grad_logits = (raised.astype(F32) * (grad_soft - inner)).astype(BF)
            grad_q = mm(k_ref[r, part], grad_logits) * head ** (-0.5)
            grad_k = mm_nt(q_ref[r, part], grad_logits)
            grad_v = mm_nt(grad_att, raised)
            proj_ref[h * head : (h + 1) * head] = grad_q.astype(BF)
            proj_ref[width + h * head : width + (h + 1) * head] = grad_k.astype(BF)
            proj_ref[2 * width + h * head : 2 * width + (h + 1) * head] = grad_v.astype(BF)
        normed = (normalize(mc_ref[r])[0] * gain + shift).astype(BF)
        grad_proj = proj_ref[...]
        w_acc[...] += mm(grad_proj, normed)
        gn_ref[r] = mm(w_ref[...], grad_proj).astype(BF)

    @pl.when(step == pl.num_programs(0) - 1)
    def _():
        flat_ref[...] = w_acc[...].astype(BF).T
        for i in range(pieces):
            here = pl.ds(pl.multiple_of(index_ref[i] * own, 16), own)
            gw_refs[i % groups][i // groups] = flat_ref[here, :]


def backward_conv(tok_ref, aux_ref, mc_ref, gm_ref, gn_ref, small_ref, other_ref, ig_ref, gs_ref, sum_acc):
    rows, seq, width = tok_ref.shape
    step = pl.program_id(0)

    @pl.when(step == 0)
    def _():
        sum_acc[...] = jnp.zeros_like(sum_acc)

    conv0, conv1, conv2 = small_ref[0:1], small_ref[1:2], small_ref[2:3]
    gain = small_ref[3:4]
    for r in range(rows):
        n, scale = normalize(mc_ref[r])
        grad_n = gn_ref[r].T.astype(F32)
        sum_acc[3] += fold_rows(grad_n * n)
        sum_acc[4] += fold_rows(grad_n)
        e = grad_n * gain
        g = gm_ref[r] + scale * (e - lane_mean(e) - n * lane_mean(e * n))
        aux_t = aux_ref[r].T
        before = pltpu.roll(g, 1, 0) * aux_t[:, 0:1]
        after = pltpu.roll(g, seq - 1, 0) * aux_t[:, 1:2]
        base = tok_ref[r].astype(F32)
        sum_acc[0] += fold_rows(base * after)
        sum_acc[1] += fold_rows(base * g)
        sum_acc[2] += fold_rows(base * before)
        ig_ref[r] = (g + conv1 * g + conv0 * after + conv2 * before).astype(BF)

    @pl.when(step == pl.num_programs(0) - 1)
    def _():
        gs_ref[...] = other_ref[...]
        for i in range(5):
            gs_ref[i : i + 1] = jnp.sum(sum_acc[i], axis=0, keepdims=True)


def by_row(shape, rows):
    tail = tuple(shape[1:])
    return pl.BlockSpec((rows,) + tail, lambda i, *_: (i,) + (0,) * len(tail))


def whole(shape):
    place = (0,) * len(shape)
    return pl.BlockSpec(tuple(shape), lambda i, *_: place)


def step_rows(count, most):
    return max(r for r in range(1, most + 1) if count % r == 0)


def call(body, name, scalars, rows, row_args, args, row_outs, outs, scratch):
    count = row_args[0].shape[0]
    spec = pltpu.PrefetchScalarGridSpec(
        num_scalar_prefetch=len(scalars),
        grid=(count // rows,),
        in_specs=[by_row(a.shape, rows) for a in row_args] + [whole(a.shape) for a in args],
        out_specs=[by_row(s, rows) for s, _ in row_outs] + [whole(s) for s, _ in outs],
        scratch_shapes=[pltpu.VMEM(s, t) for s, t in scratch],
    )
    return pl.pallas_call(
        body,
        grid_spec=spec,
        out_shape=[jax.ShapeDtypeStruct(s, t) for s, t in row_outs + outs],
        compiler_params=pltpu.CompilerParams(dimension_semantics=("arbitrary",), vmem_limit_bytes=VMEM_LIMIT),
        name=name,
    )(*scalars, *row_args, *args)


def small_call(body, name, args, outs, scratch=()):
    return pl.pallas_call(
        body,
        out_shape=[jax.ShapeDtypeStruct(s, t) for s, t in outs],
        scratch_shapes=[pltpu.VMEM(s, t) for s, t in scratch],
        compiler_params=pltpu.CompilerParams(vmem_limit_bytes=VMEM_LIMIT),
        name=name,
    )(*args)


def run_forward(index, tokens, segment_ids, valid_len, pieces):
    count, seq, width = tokens.shape
    flipped = (count, width, seq)
    row_outs = [
        (flipped, BF), (flipped, BF), ((count, seq, width), BF), ((count, HEADS, seq, seq), BF),
        (flipped, BF), ((count, 8, seq), F32), ((count, seq, width), F32), ((count, 8, seq), F32),
    ]
    return call(
        functools.partial(forward_attention, pieces=len(pieces)), "forward_attention", (index, valid_len),
        step_rows(count, 2), (tokens, segment_ids.reshape(count, 1, seq)), pieces,
        row_outs, [((8, width), F32), ((width, 3 * width), BF)],
        [((3 * width, width), BF), ((width, 3 * width + VECTORS), BF)],
    )


def run_feed_forward(index, att, mixed, cotangent, small, pieces, shards):
    count, seq, width = cotangent.shape
    own = width // len(pieces)
    ff = shards * width
    groups = 2 if len(pieces) > 1 else 1
    row_outs = [((count, seq, width), BF), ((count, seq, width), F32), ((count, width, seq), BF)]
    grads = ((len(pieces) // groups, own, 2 * ff + width), BF)
    return call(
        functools.partial(feed_forward, pieces=len(pieces), shards=shards), "feed_forward", (index,),
        step_rows(count, 2), (att, mixed, cotangent), (small, *pieces),
        row_outs, [((8, width), F32)] + [grads] * groups,
        [((width, ff), BF)] * 2 + [((width, width), BF)] + [((width, ff), F32)] * 2
        + [((width, width), F32)] + [((8, width), F32)] * 2,
    )


def run_backward_attention(index, weight, q, k, v, raised, att, inverse, mixed, grad_att, small, pieces):
    count, seq, width = v.shape
    own = width // pieces
    groups = 2 if pieces > 1 else 1
    rows = step_rows(count, 2)
    row_args = (q, k, v, raised, att, inverse, mixed, grad_att)
    body = functools.partial(backward_attention, pieces=pieces)

    def ordered(index_ref, *refs):
        body(index_ref, refs[len(row_args)], *refs[: len(row_args)], *refs[len(row_args) + 1 :])

    return call(
        ordered, "backward_attention", (index,), rows, row_args, (weight, small),
        [((count, width, seq), BF)], [((pieces // groups, own, 3 * width), BF)] * groups,
        [((3 * width, seq), BF), ((3 * width, width), F32), ((width, 3 * width), BF)],
    )


def run_backward_conv(tokens, aux, mixed, grad_mixed, grad_normed, small, other):
    return call(
        backward_conv, "backward_conv", (), step_rows(tokens.shape[0], 2),
        (tokens, aux, mixed, grad_mixed, grad_normed), (small, other),
        [(tokens.shape, BF)], [((8, tokens.shape[2]), F32)], [((5, 8, tokens.shape[2]), F32)],
    )


def exchange(values, axis, offset):
    size = lax.axis_size(axis)
    return lax.ppermute(values, axis, [(i, i ^ offset) for i in range(size)])


def add_halves(mine, received):
    count, own, cols = mine.shape

    def body(mine_ref, received_ref, *out_refs):
        for i, ref in enumerate(out_refs):
            ref[...] = (mine_ref[i].astype(F32) + received_ref[i].astype(F32)).astype(BF)

    return small_call(body, "add_halves", (mine, received), [((own, cols), BF)] * count)


def add_plane_ff(items, shards, ffs, width):
    own = items[0].shape[0]
    count = len(items)

    def body(*refs):
        total = tree_sum(ref[...].astype(F32) for ref in refs[:count])
        for j, ref in enumerate(refs[count:]):
            ref[:, : 2 * ffs] = total[:, 2 * j * ffs : (2 * j + 2) * ffs].astype(BF)
            ref[:, 2 * ffs :] = total[:, 2 * shards * ffs :].astype(BF)

    return small_call(body, "add_plane_ff", items, [((own, 2 * ffs + width), BF)] * shards)


def add_shards_ff(items, ffs, width):
    own = items[0].shape[0]

    def body(*refs):
        total = tree_sum(ref[...].astype(F32) for ref in refs[:-3])
        up_ref, down_ref, out_ref = refs[-3:]
        up_ref[...] = total[:, :ffs]
        down_ref[...] = total[:, ffs : 2 * ffs]
        out_ref[...] = total[:, 2 * ffs :]

    return small_call(body, "add_shards_ff", items, [((own, ffs), F32)] * 2 + [((own, width), F32)])


def add_plane_attn(place, items, sums):
    own, cols = items[0].shape
    count = len(items)
    width = sums[0].shape[1]

    def body(place_ref, *refs):
        total = tree_sum(ref[...].astype(F32) for ref in refs[:count])
        out_ref, turned_ref = refs[-2:]
        out_ref[:, :cols] = total.astype(BF)
        vectors = tree_sum(ref[...] for ref in refs[count:-2])
        turned_ref[...] = jnp.concatenate([vectors, jnp.zeros((VECTORS - 8, width), F32)], axis=0).T
        mine = turned_ref[pl.ds(pl.multiple_of(place_ref[0] * own, 16), own), :]
        out_ref[:, cols:] = mine.astype(BF)

    spec = pltpu.PrefetchScalarGridSpec(
        num_scalar_prefetch=1, grid=(1,),
        in_specs=[whole(a.shape) for a in (*items, *sums)],
        out_specs=whole((own, cols + VECTORS)),
        scratch_shapes=[pltpu.VMEM((width, VECTORS), F32)],
    )
    return pl.pallas_call(
        body, grid_spec=spec, out_shape=jax.ShapeDtypeStruct((own, cols + VECTORS), BF), name="add_plane_attn",
    )(place, *items, *sums)


def add_shards_attn(items, cols):
    own = items[0].shape[0]

    def body(*refs):
        total = tree_sum(ref[...].astype(F32) for ref in refs[:-6])
        refs[-6][...] = total[:, :cols]
        vectors = jnp.concatenate([total[:, cols:], jnp.zeros((VECTORS - own, VECTORS), F32)], axis=0).T
        refs[-5][...] = vectors[0:3, :own]
        for i in range(4):
            refs[i - 4][...] = vectors[3 + i : 4 + i, :own]

    outs = [((own, cols), F32), ((3, own), F32)] + [((1, own), F32)] * 4
    return small_call(body, "add_shards_attn", items, outs)


def direct_plan(tokens, segment_ids, valid_len, qkv_weight, out_weight, up_weight, down_weight, conv_weight, vectors, cotangent):
    count, seq, width = tokens.shape
    own, ffs = up_weight.shape
    dp, mp = lax.axis_size("dp"), lax.axis_size("mp")
    me = lax.axis_index("dp")
    offsets = [2 * p for p in range(dp // 2)]
    index = jnp.stack([me ^ (p ^ c) for p in offsets for c in range(2)]).astype(jnp.int32)
    narrow, ff_own = small_call(
        pack_weights, "pack_weights",
        (qkv_weight, up_weight, down_weight, conv_weight, *[v.reshape(1, own) for v in vectors]),
        [((own, 3 * width + VECTORS), BF), ((2 * own, ffs), BF)], [((VECTORS, VECTORS), F32)],
    )
    plane = [narrow] + [exchange(narrow, "dp", p) for p in offsets[1:]]
    shards = [ff_own] + [exchange(ff_own, "mp", j) for j in range(1, mp)]
    pieces = [piece for a in plane for piece in (a, exchange(a, "dp", 1))]
    column = jnp.concatenate(shards + [out_weight], axis=0)
    columns = [column] + [exchange(column, "dp", p) for p in offsets[1:]]
    q, k, v, raised, att, inverse, mixed, aux, small, weight = run_forward(index, tokens, segment_ids, valid_len, pieces)
    columns, att = lax.optimization_barrier((columns, att))
    pieces = [piece for a in columns for piece in (a, exchange(a, "dp", 1))]
    layer_out, grad_mixed, grad_att, sums2, mine, theirs = run_feed_forward(
        index, att, mixed, cotangent, small, pieces, mp
    )
    received = exchange(theirs, "dp", 1)
    grad_normed, mine_a, theirs_a = run_backward_attention(
        index, weight, q, k, v, raised, att, inverse, mixed, grad_att, small, dp
    )
    received, grad_normed, theirs_a = lax.optimization_barrier((received, grad_normed, theirs_a))
    received_a = exchange(theirs_a, "dp", 1)
    parts = add_halves(mine, received)
    plane = [parts[0]] + [exchange(parts[i], "dp", p) for i, p in enumerate(offsets) if i]
    input_grad, sums = run_backward_conv(tokens, aux, mixed, grad_mixed, grad_normed, small, sums2)
    received_a, plane, sums = lax.optimization_barrier((received_a, plane, sums))
    parts = add_halves(mine_a, received_a)
    plane_a = [parts[0]] + [exchange(parts[i], "dp", p) for i, p in enumerate(offsets) if i]
    all_sums = [sums] + [exchange(sums, "dp", i) for i in range(1, dp)]
    parts = add_plane_ff(plane, mp, ffs, width)
    last = [parts[0]] + [exchange(parts[j], "mp", j) for j in range(1, mp)]
    total = add_plane_attn(index[:1], plane_a, all_sums)
    last_a = [total] + [exchange(total, "mp", j) for j in range(1, mp)]
    grad_up, grad_down, grad_out = add_shards_ff(last, ffs, width)
    grad_qkv, grad_conv, *grads = add_shards_attn(last_a, 3 * width)
    return (layer_out, input_grad, grad_qkv, grad_out, grad_up, grad_down, grad_conv, *[g.reshape(own) for g in grads])


def gathered_plan(tokens, segment_ids, valid_len, qkv_weight, out_weight, up_weight, down_weight, conv_weight, vectors, cotangent):
    count, seq, width = tokens.shape
    own = qkv_weight.shape[0]
    dp = width // own
    columns = jnp.stack([conv_weight[0], conv_weight[1], conv_weight[2], *vectors], axis=1)
    narrow = jnp.concatenate([qkv_weight, jnp.pad(columns, ((0, 0), (0, VECTORS - 7))), out_weight], axis=1)
    wide = lax.all_gather(narrow, "dp", axis=0, tiled=True)
    both = lax.all_gather(jnp.concatenate([up_weight, down_weight], axis=0), "mp", axis=1, tiled=True)
    ff = both.shape[1]
    shards = ff // width
    both = lax.all_gather(both, "dp", axis=0).reshape(dp, 2, own, shards, width)
    both = both.transpose(3, 1, 0, 2, 4).reshape(2 * ff, width)
    column = jnp.concatenate([both, wide[:, 3 * width + VECTORS :]], axis=0)
    index = jnp.zeros((1,), jnp.int32)
    q, k, v, raised, att, inverse, mixed, aux, small, weight = run_forward(
        index, tokens, segment_ids, valid_len, [wide[:, : 3 * width + VECTORS]]
    )
    layer_out, grad_mixed, grad_att, sums2, grads = run_feed_forward(
        index, att, mixed, cotangent, small, [column], shards
    )
    grad_normed, grad_qkv = run_backward_attention(
        index, weight, q, k, v, raised, att, inverse, mixed, grad_att, small, 1
    )
    input_grad, sums = run_backward_conv(tokens, aux, mixed, grad_mixed, grad_normed, small, sums2)
    grad_ff = grads[0, :, : 2 * ff].reshape(width, shards, 2, width).transpose(0, 2, 1, 3).reshape(width, 2 * ff)
    grad_ff = lax.psum_scatter(grad_ff, "dp", scatter_dimension=0, tiled=True).reshape(own, 2, ff)
    grad_ff = lax.psum_scatter(grad_ff, "mp", scatter_dimension=2, tiled=True).astype(F32)
    grad_attn = jnp.concatenate([grad_qkv[0], grads[0, :, 2 * ff :]], axis=1)
    grad_attn = lax.psum_scatter(grad_attn, "dp", scatter_dimension=0, tiled=True)
    grad_attn = lax.psum(grad_attn, "mp").astype(F32)
    sums = lax.psum(sums, ("dp", "mp"))
    sums = lax.dynamic_slice_in_dim(sums, lax.axis_index("dp") * own, own, axis=1)
    return (
        layer_out, input_grad, grad_attn[:, : 3 * width], grad_attn[:, 3 * width :],
        grad_ff[:, 0], grad_ff[:, 1], sums[0:3], sums[3], sums[4], sums[5], sums[6],
    )


def on_device(
    tokens, segment_ids, valid_len, qkv_weight, out_weight, up_weight, down_weight, conv_weight,
    ln1_gain, ln1_shift, ln2_gain, ln2_shift, cotangent,
):
    own, ffs = up_weight.shape
    direct = own % 16 == 0 and ffs == tokens.shape[2] and own <= VECTORS
    plan = direct_plan if direct else gathered_plan
    return plan(
        tokens, segment_ids, valid_len, qkv_weight, out_weight, up_weight, down_weight, conv_weight,
        (ln1_gain, ln1_shift, ln2_gain, ln2_shift), cotangent,
    )


def solution(mesh):
    rows = P(("dp", "mp"), None, None)
    weights = (P("dp", None), P("dp", None), P("dp", "mp"), P("dp", "mp"), P(None, "dp"))
    vectors = (P("dp"),) * 4
    return jax.shard_map(
        on_device,
        mesh=mesh,
        in_specs=(rows, P(("dp", "mp"), None), P(("dp", "mp"))) + weights + vectors + (rows,),
        out_specs=(rows, rows) + weights + vectors,
        check_vma=False,
    )
```

```python
import functools
import math

import jax
import jax.numpy as jnp
from jax import lax
from jax.experimental import pallas as pl
from jax.experimental.pallas import tpu as pltpu
from jax.sharding import PartitionSpec as P

HEADS = 6
VECTORS = 128
LANES = 128
BF = jnp.bfloat16
F32 = jnp.float32
VMEM_LIMIT = 60 * 1024 * 1024


def mm(lhs, rhs):
    return lax.dot_general(lhs, rhs, (((1,), (0,)), ((), ())), preferred_element_type=F32)


def mm_nt(lhs, rhs):
    return lax.dot_general(lhs, rhs, (((1,), (1,)), ((), ())), preferred_element_type=F32)


def tree_sum(items):
    items = list(items)
    while len(items) > 1:
        items = [a + b for a, b in zip(items[::2], items[1::2])]
    return items[0]


def pack_weights(qkv_ref, up_ref, down_ref, conv_ref, g1_ref, s1_ref, g2_ref, s2_ref, narrow_ref, ff_ref, rows_ref):
    own, ffs = up_ref.shape
    rows_ref[...] = jnp.zeros_like(rows_ref)
    rows_ref[0:3, :own] = conv_ref[...].astype(F32)
    for i, ref in enumerate((g1_ref, s1_ref, g2_ref, s2_ref)):
        rows_ref[3 + i : 4 + i, :own] = ref[...].astype(F32)
    wide = qkv_ref.shape[1]
    narrow_ref[:, :wide] = qkv_ref[...]
    narrow_ref[:, wide:] = rows_ref[...].T[:own].astype(BF)
    ff_ref[:own] = up_ref[...]
    ff_ref[own:] = down_ref[...]


def tiles(total, size):
    return [slice(at, at + size) for at in range(0, total, size)]


def twice(tile, lanes):
    return jnp.concatenate([tile] * (lanes // LANES), axis=1)


def load_columns(packed_ref, col_ref, places):
    for i, place in enumerate(places):
        column = packed_ref[:, place : place + 1].astype(F32)
        col_ref[i] = jnp.broadcast_to(column, (column.shape[0], LANES))


def column_mean(values):
    return jnp.sum(values, axis=0, keepdims=True) * (1.0 / values.shape[0])


def norm_columns(values):
    centred = values - column_mean(values)
    scale = lax.rsqrt(column_mean(centred * centred) + 1e-06)
    return centred * scale, scale


def fold(values):
    rows, lanes = values.shape
    return jnp.sum(values.reshape(rows // 8, 8, lanes), axis=0)


def fold_lanes(values):
    return sum(values[:, t] for t in tiles(values.shape[1], LANES))


def forward_attention(index_ref, len_ref, tok_ref, seg_ref, *refs, pieces):
    piece_refs = refs[:pieces]
    (
        x_ref, mc_ref, norm_ref, q_ref, k_ref, v_ref, e_ref, att_ref, inv_ref, aux_ref, packed_ref, w_ref,
        wt_ref, wide_ref, col_ref, bias_ref, key_ref, value_ref, score_ref,
    ) = refs[pieces:]
    rows, seq, width = tok_ref.shape
    head = width // HEADS
    step = pl.program_id(0)

    @pl.when(step == 0)
    def _():
        own = width // pieces
        for i, ref in enumerate(piece_refs):
            wide_ref[pl.ds(pl.multiple_of(index_ref[i] * own, 16), own), :] = ref[...]
        w_ref[...] = wide_ref[:, : 3 * width]
        wt_ref[:width] = (wide_ref[:, :width].astype(F32) * head ** (-0.5)).astype(BF).T
        wt_ref[width:] = wide_ref[:, width : 3 * width].T
        packed_ref[...] = wide_ref[:, 3 * width :]
        load_columns(packed_ref, col_ref, range(5))

    place = lax.broadcasted_iota(jnp.int32, (1, seq), 1)
    for r in range(rows):
        segs = seg_ref[pl.ds(step * rows + r, 1), :].astype(F32)
        valid = place < len_ref[step * rows + r]
        number = jnp.where(valid, segs, -1.0)
        links = jnp.where(valid & (place > 0) & (number == pltpu.roll(number, 1, 1)), 1.0, 0.0)
        next_links = jnp.where(place < seq - 1, pltpu.roll(links, seq - 1, 1), 0.0)
        none = jnp.zeros_like(links)
        aux = jnp.concatenate([links, next_links, number, none, none, none, none, none], axis=0)
        aux_ref[r] = aux
        key_number = aux.T[:, 2:3]
        for t in tiles(seq, 64):
            row_id = lax.broadcasted_iota(jnp.int32, (64, seq), 0) + t.start
            col_id = lax.broadcasted_iota(jnp.int32, (64, seq), 1)
            bias_ref[r, t] = jnp.where((key_number[t] == segs) | (row_id == col_id), 0.0, -1e30)
        x_ref[r] = tok_ref[r].T
        for t in tiles(width, 64):
            base = x_ref[r, t].astype(F32)
            before = pltpu.roll(base, 1, 1) * links
            after = pltpu.roll(base, seq - 1, 1) * next_links
            conv0, conv1, conv2 = [twice(col_ref[i, t], seq) for i in range(3)]
            mc_ref[r, t] = base + before * conv0 + base * conv1 + after * conv2
        for t in tiles(seq, LANES):
            n, _ = norm_columns(mc_ref[r, :, t])
            norm_ref[r, :, t] = (n * col_ref[3] + col_ref[4]).astype(BF)
    for r in range(rows):
        normed = norm_ref[r]
        q_ref[r] = mm(wt_ref[:width], normed).astype(BF)
        k_ref[r] = mm(wt_ref[width : 2 * width], normed).astype(BF)
        key_ref[r] = k_ref[r].T
        value_ref[r] = mm(wt_ref[2 * width :], normed).astype(BF)
        v_ref[r] = value_ref[r].T
    zero = jnp.zeros((head, seq), BF)

    def scores(r, h):
        own = q_ref[r, h * head : (h + 1) * head]
        pair = [own, zero] if h % 2 == 0 else [zero, own]
        lanes = slice(h // 2 * 2 * head, (h // 2 + 1) * 2 * head)
        score_ref[r, h] = mm(key_ref[r, :, lanes], jnp.concatenate(pair, axis=0))

    work = [(r, h) for r in range(rows) for h in range(HEADS)]
    scores(*work[0])
    for at, (r, h) in enumerate(work):
        if at + 1 < len(work):
            scores(*work[at + 1])
        for t in tiles(seq, LANES):
            masked = score_ref[r, h, :, t] + bias_ref[r, :, t]
            raised = jnp.exp(masked - jnp.max(masked, axis=0, keepdims=True))
            inv_ref[r, h : h + 1, t] = 1.0 / jnp.sum(raised, axis=0, keepdims=True)
            e_ref[r, h, :, t] = raised.astype(BF)
        part = slice(h * head, (h + 1) * head)
        att = mm(value_ref[r, part], e_ref[r, h]) * inv_ref[r, h : h + 1]
        att_ref[r, part] = att.astype(BF)


def gelu_parts(x):
    size = jnp.abs(x)
    t = 1.0 / (1.0 + (0.3275911 * math.sqrt(0.5)) * size)
    poly = t * (
        0.127414796 + t * (-0.142248368 + t * (0.7107068705 + t * (-0.7265760135 + t * 0.5307027145)))
    )
    bell = jnp.exp(-0.5 * (x * x))
    tail = poly * bell
    cdf = jnp.where(x >= 0.0, 1.0 - tail, tail)
    return x * cdf, cdf + x * (bell * 0.3989422804014327)


def feed_forward(index_ref, att_ref, mc_ref, ct_ref, packed_ref, *refs, pieces, shards):
    piece_refs = refs[:pieces]
    groups = 2 if pieces > 1 else 1
    lo_ref, gm_ref, ga_ref, gs_ref = refs[pieces : pieces + 4]
    gw_refs = refs[pieces + 4 : pieces + 4 + groups]
    (
        up_ref, down_ref, upt_ref, downt_ref, out_ref, outt_ref, up_acc, down_acc, out_acc, col_acc, col_ref,
        att_cat, mixed_ref, n_ref, norm_ref, ctt_ref, pre_ref, gh_ref, hidden_ref, gp_ref, gn_ref, scale_ref, lot_ref,
        branch_ref,
    ) = refs[pieces + 4 + groups :]
    rows, seq, width = ct_ref.shape
    ff = up_ref.shape[1]
    ffs = ff // shards
    own = width // pieces
    step = pl.program_id(0)

    @pl.when(step == 0)
    def _():
        for acc in (up_acc, down_acc, out_acc, col_acc):
            acc[...] = jnp.zeros_like(acc)
        for i, ref in enumerate(piece_refs):
            here = pl.ds(pl.multiple_of(index_ref[i] * own, 16), own)
            for j in range(shards):
                up_ref[here, j * ffs : (j + 1) * ffs] = ref[2 * j * own : (2 * j + 1) * own]
                down_ref[here, j * ffs : (j + 1) * ffs] = ref[(2 * j + 1) * own : (2 * j + 2) * own]
            out_ref[here, :] = ref[2 * shards * own :]
        upt_ref[...] = up_ref[...].T
        downt_ref[...] = down_ref[...].T
        outt_ref[...] = out_ref[...].T
        load_columns(packed_ref, col_ref, (5, 6))

    for r in range(rows):
        lanes = slice(r * seq, (r + 1) * seq)
        ctt_ref[:, lanes] = ct_ref[r].T
        att_cat[:, lanes] = att_ref[r]
        mixed_ref[:, lanes] = mc_ref[r] + mm(outt_ref[...], att_ref[r])
    for t in tiles(rows * seq, LANES):
        n, scale = norm_columns(mixed_ref[:, t])
        n_ref[:, t] = n
        scale_ref[0:1, t] = scale
        norm_ref[:, t] = (n * col_ref[0] + col_ref[1]).astype(BF)

    blocks = tiles(ff, 256)

    def opening(rows_of):
        pre_ref[rows_of] = mm(upt_ref[rows_of], norm_ref[...])
        gh_ref[rows_of] = mm(downt_ref[rows_of], ctt_ref[...])

    opening(blocks[0])
    for at, block in enumerate(blocks):
        if at + 1 < len(blocks):
            opening(blocks[at + 1])
        for low in range(block.start, block.stop, 16):
            t = slice(low, low + 16)
            hidden, slope = gelu_parts(pre_ref[t])
            hidden_ref[t] = hidden.astype(BF)
            gp_ref[t] = (gh_ref[t] * slope).astype(BF)
        down_acc[:, block] += mm_nt(ctt_ref[...], hidden_ref[block])
        up_acc[:, block] += mm_nt(norm_ref[...], gp_ref[block])
    gn_ref[...] = mm(up_ref[...], gp_ref[...])
    lot_ref[...] = (mixed_ref[...] + mm(down_ref[...], hidden_ref[...])).astype(BF)
    for t in tiles(rows * seq, LANES):
        mean_e = jnp.zeros((8, LANES), F32)
        mean_en = jnp.zeros((8, LANES), F32)
        for d in tiles(width, 64):
            grad_n = gn_ref[d, t]
            product = grad_n * n_ref[d, t]
            col_acc[0, d] += product
            col_acc[1, d] += grad_n
            mean_e += fold(grad_n * col_ref[0, d])
            mean_en += fold(product * col_ref[0, d])
        mean_e = jnp.sum(mean_e, axis=0, keepdims=True) * (1.0 / width)
        mean_en = jnp.sum(mean_en, axis=0, keepdims=True) * (1.0 / width)
        scale = scale_ref[0:1, t]
        row, inside = divmod(t.start, seq)
        for d in tiles(width, 64):
            change = scale * (gn_ref[d, t] * col_ref[0, d] - mean_e - n_ref[d, t] * mean_en)
            grad_mixed = ctt_ref[d, t].astype(F32) + change
            gm_ref[row, d, inside : inside + LANES] = grad_mixed
            branch_ref[d, t] = grad_mixed.astype(BF)
    out_acc[...] += mm_nt(att_cat[...], branch_ref[...])
    for r in range(rows):
        lanes = slice(r * seq, (r + 1) * seq)
        ga_ref[r] = mm(out_ref[...], branch_ref[:, lanes]).astype(BF)
        lo_ref[r] = lot_ref[:, lanes].T

    @pl.when(step == pl.num_programs(0) - 1)
    def _():
        for i in range(pieces):
            here = pl.ds(pl.multiple_of(index_ref[i] * own, 16), own)
            place = gw_refs[i % groups]
            for j in range(shards):
                cols = slice(j * ffs, (j + 1) * ffs)
                place[i // groups, :, 2 * j * ffs : (2 * j + 1) * ffs] = up_acc[here, cols].astype(BF)
                place[i // groups, :, (2 * j + 1) * ffs : (2 * j + 2) * ffs] = down_acc[here, cols].astype(BF)
            place[i // groups, :, 2 * ff :] = out_acc[here, :].astype(BF)
        gs_ref[...] = jnp.zeros_like(gs_ref)
        for i in range(2):
            gs_ref[5 + i : 6 + i] = jnp.sum(col_acc[i].T, axis=0, keepdims=True)


def backward_attention(q_ref, k_ref, v_ref, e_ref, att_ref, inv_ref, norm_ref, ga_ref, index_ref, w_ref, *refs, pieces):
    groups = 2 if pieces > 1 else 1
    gn_ref = refs[0]
    gw_refs = refs[1 : 1 + groups]
    proj_ref, w_acc, norm_cat, soft_ref, logit_ref = refs[1 + groups :]
    rows, seq, width = v_ref.shape
    own = width // pieces
    head = width // HEADS
    step = pl.program_id(0)

    @pl.when(step == 0)
    def _():
        w_acc[...] = jnp.zeros_like(w_acc)

    zero = jnp.zeros((head, seq), BF)
    work = [(r, h) for r in range(rows) for h in range(HEADS)]

    def opening(r, h):
        part = slice(h * head, (h + 1) * head)
        lanes = slice(h // 2 * 2 * head, (h // 2 + 1) * 2 * head)
        grad_att = ga_ref[r, part].astype(F32) * inv_ref[r, h : h + 1]
        inner = jnp.sum(grad_att * att_ref[r, part].astype(F32), axis=0, keepdims=True)
        grad_att = grad_att.astype(BF)
        pair = [grad_att, zero] if h % 2 == 0 else [zero, grad_att]
        soft_ref[r, h] = mm(v_ref[r, :, lanes], jnp.concatenate(pair, axis=0))
        return grad_att, inner

    ready = opening(*work[0])
    for at, (r, h) in enumerate(work):
        grad_att, inner = ready
        if at + 1 < len(work):
            ready = opening(*work[at + 1])
        for t in tiles(seq, 32):
            raised = e_ref[r, h, t].astype(F32)
            logit_ref[r, h, t] = (raised * (soft_ref[r, h, t] - inner)).astype(BF)
        part = slice(h * head, (h + 1) * head)
        place = slice(r * seq, (r + 1) * seq)
        grad_logits = logit_ref[r, h]
        grad_q = mm(k_ref[r, part], grad_logits) * head ** (-0.5)
        proj_ref[h * head : (h + 1) * head, place] = grad_q.astype(BF)
        grad_k = mm_nt(q_ref[r, part], grad_logits)
        proj_ref[width + h * head : width + (h + 1) * head, place] = grad_k.astype(BF)
        grad_v = mm_nt(grad_att, e_ref[r, h])
        proj_ref[2 * width + h * head : 2 * width + (h + 1) * head, place] = grad_v.astype(BF)
    for r in range(rows):
        norm_cat[:, r * seq : (r + 1) * seq] = norm_ref[r]
        gn_ref[r] = mm(w_ref[...], proj_ref[:, r * seq : (r + 1) * seq]).astype(BF)
    w_acc[...] += mm_nt(norm_cat[...], proj_ref[...])

    @pl.when(step == pl.num_programs(0) - 1)
    def _():
        for i in range(pieces):
            here = pl.ds(pl.multiple_of(index_ref[i] * own, 16), own)
            gw_refs[i % groups][i // groups] = w_acc[here, :].astype(BF)


def backward_conv(x_ref, aux_ref, mc_ref, gm_ref, gn_ref, packed_ref, other_ref, ig_ref, gs_ref, acc_ref, col_ref, n_ref, g_ref, turn_ref):
    rows, width, seq = x_ref.shape
    step = pl.program_id(0)

    @pl.when(step == 0)
    def _():
        acc_ref[...] = jnp.zeros_like(acc_ref)
        load_columns(packed_ref, col_ref, range(4))

    for r in range(rows):
        for t in tiles(seq, LANES):
            n, scale = norm_columns(mc_ref[r, :, t])
            n_ref[r, :, t] = n
            mean_e = jnp.zeros((8, LANES), F32)
            mean_en = jnp.zeros((8, LANES), F32)
            for d in tiles(width, 64):
                grad_n = gn_ref[r, d, t].astype(F32)
                product = grad_n * n_ref[r, d, t]
                acc_ref[3, d] += product
                acc_ref[4, d] += grad_n
                mean_e += fold(grad_n * col_ref[3, d])
                mean_en += fold(product * col_ref[3, d])
            mean_e = jnp.sum(mean_e, axis=0, keepdims=True) * (1.0 / width)
            mean_en = jnp.sum(mean_en, axis=0, keepdims=True) * (1.0 / width)
            for d in tiles(width, 64):
                e = gn_ref[r, d, t].astype(F32) * col_ref[3, d]
                g_ref[r, d, t] = gm_ref[r, d, t] + scale * (e - mean_e - n_ref[r, d, t] * mean_en)
        links, next_links = aux_ref[r, 0:1], aux_ref[r, 1:2]
        for d in tiles(width, 32):
            g = g_ref[r, d]
            base = x_ref[r, d].astype(F32)
            before = pltpu.roll(g, 1, 1) * links
            after = pltpu.roll(g, seq - 1, 1) * next_links
            acc_ref[0, d] += fold_lanes(base * after)
            acc_ref[1, d] += fold_lanes(base * g)
            acc_ref[2, d] += fold_lanes(base * before)
            conv0, conv1, conv2 = [twice(col_ref[i, d], seq) for i in range(3)]
            turn_ref[r, d] = (g + conv1 * g + conv0 * after + conv2 * before).astype(BF)
        ig_ref[r] = turn_ref[r].T

    @pl.when(step == pl.num_programs(0) - 1)
    def _():
        gs_ref[...] = other_ref[...]
        for i in range(5):
            gs_ref[i : i + 1] = jnp.sum(acc_ref[i].T, axis=0, keepdims=True)


def by_row(shape, rows):
    tail = tuple(shape[1:])
    return pl.BlockSpec((rows,) + tail, lambda i, *_: (i,) + (0,) * len(tail))


def whole(shape):
    place = (0,) * len(shape)
    return pl.BlockSpec(tuple(shape), lambda i, *_: place)


def step_rows(count, most):
    return max(r for r in range(1, most + 1) if count % r == 0)


def call(body, name, scalars, rows, row_args, args, row_outs, outs, scratch):
    count = row_args[0].shape[0]
    spec = pltpu.PrefetchScalarGridSpec(
        num_scalar_prefetch=len(scalars),
        grid=(count // rows,),
        in_specs=[by_row(a.shape, rows) for a in row_args] + [whole(a.shape) for a in args],
        out_specs=[by_row(s, rows) for s, _ in row_outs] + [whole(s) for s, _ in outs],
        scratch_shapes=[pltpu.VMEM(s, t) for s, t in scratch],
    )
    return pl.pallas_call(
        body,
        grid_spec=spec,
        out_shape=[jax.ShapeDtypeStruct(s, t) for s, t in row_outs + outs],
        compiler_params=pltpu.CompilerParams(dimension_semantics=("arbitrary",), vmem_limit_bytes=VMEM_LIMIT),
        name=name,
    )(*scalars, *row_args, *args)


def small_call(body, name, args, outs, scratch=()):
    return pl.pallas_call(
        body,
        out_shape=[jax.ShapeDtypeStruct(s, t) for s, t in outs],
        scratch_shapes=[pltpu.VMEM(s, t) for s, t in scratch],
        compiler_params=pltpu.CompilerParams(vmem_limit_bytes=VMEM_LIMIT),
        name=name,
    )(*args)


def run_forward(index, tokens, segment_ids, valid_len, pieces):
    count, seq, width = tokens.shape
    flipped = (count, width, seq)
    rows = step_rows(count, 2)
    row_outs = [
        (flipped, BF), (flipped, F32), (flipped, BF), (flipped, BF), (flipped, BF), ((count, seq, width), BF),
        ((count, HEADS, seq, seq), BF), (flipped, BF), ((count, 8, seq), F32), ((count, 8, seq), F32),
    ]
    return call(
        functools.partial(forward_attention, pieces=len(pieces)), "forward_attention", (index, valid_len),
        rows, (tokens,), (segment_ids, *pieces),
        row_outs, [((width, VECTORS), BF), ((width, 3 * width), BF)],
        [
            ((3 * width, width), BF), ((width, 3 * width + VECTORS), BF), ((5, width, LANES), F32),
            ((rows, seq, seq), F32), ((rows, seq, width), BF), ((rows, width, seq), BF), ((rows, HEADS, seq, seq), F32),
        ],
    )


def run_feed_forward(index, att, mixed, cotangent, packed, pieces, shards):
    count, seq, width = cotangent.shape
    own = width // len(pieces)
    ff = shards * width
    groups = 2 if len(pieces) > 1 else 1
    rows = step_rows(count, 2)
    wide = rows * seq
    row_outs = [((count, seq, width), BF), ((count, width, seq), F32), ((count, width, seq), BF)]
    grads = ((len(pieces) // groups, own, 2 * ff + width), BF)
    return call(
        functools.partial(feed_forward, pieces=len(pieces), shards=shards), "feed_forward", (index,),
        rows, (att, mixed, cotangent), (packed, *pieces),
        row_outs, [((8, width), F32)] + [grads] * groups,
        [((width, ff), BF)] * 2 + [((ff, width), BF)] * 2 + [((width, width), BF)] * 2
        + [((width, ff), F32)] * 2 + [((width, width), F32), ((2, width, LANES), F32), ((2, width, LANES), F32)]
        + [((width, wide), BF), ((width, wide), F32), ((width, wide), F32), ((width, wide), BF), ((width, wide), BF)]
        + [((ff, wide), F32)] * 2 + [((ff, wide), BF)] * 2
        + [((width, wide), F32), ((8, wide), F32), ((width, wide), BF), ((width, wide), BF)],
    )


def run_backward_attention(index, weight, q, k, v, raised, att, inverse, normed, grad_att, pieces):
    count, seq, width = v.shape
    own = width // pieces
    groups = 2 if pieces > 1 else 1
    rows = step_rows(count, 2)
    row_args = (q, k, v, raised, att, inverse, normed, grad_att)

    def body(index_ref, *refs):
        backward_attention(*refs[: len(row_args)], index_ref, *refs[len(row_args) :], pieces=pieces)

    return call(
        body, "backward_attention", (index,), rows, row_args, (weight,),
        [((count, width, seq), BF)], [((pieces // groups, own, 3 * width), BF)] * groups,
        [
            ((3 * width, rows * seq), BF), ((width, 3 * width), F32), ((width, rows * seq), BF),
            ((rows, HEADS, seq, seq), F32), ((rows, HEADS, seq, seq), BF),
        ],
    )


def run_backward_conv(x, aux, mixed, grad_mixed, grad_normed, packed, other):
    count, width, seq = x.shape
    rows = step_rows(count, 2)
    return call(
        backward_conv, "backward_conv", (), rows,
        (x, aux, mixed, grad_mixed, grad_normed), (packed, other),
        [((count, seq, width), BF)], [((8, width), F32)],
        [
            ((5, width, LANES), F32), ((4, width, LANES), F32), ((rows, width, seq), F32), ((rows, width, seq), F32),
            ((rows, width, seq), BF),
        ],
    )


def exchange(values, axis, offset):
    size = lax.axis_size(axis)
    return lax.ppermute(values, axis, [(i, i ^ offset) for i in range(size)])


def add_halves(mine, received):
    count, own, cols = mine.shape

    def body(mine_ref, received_ref, *out_refs):
        for i, ref in enumerate(out_refs):
            ref[...] = (mine_ref[i].astype(F32) + received_ref[i].astype(F32)).astype(BF)

    return small_call(body, "add_halves", (mine, received), [((own, cols), BF)] * count)


def add_pair(first, second):
    def body(first_ref, second_ref, out_ref):
        out_ref[...] = first_ref[...] + second_ref[...]

    return small_call(body, "add_pair", (first, second), [(first.shape, first.dtype)])[0]


def add_plane_ff(items, shards, ffs, width):
    own = items[0].shape[0]
    count = len(items)

    def body(*refs):
        total = tree_sum(ref[...].astype(F32) for ref in refs[:count])
        for j, ref in enumerate(refs[count:]):
            ref[:, : 2 * ffs] = total[:, 2 * j * ffs : (2 * j + 2) * ffs].astype(BF)
            ref[:, 2 * ffs :] = total[:, 2 * shards * ffs :].astype(BF)

    return small_call(body, "add_plane_ff", items, [((own, 2 * ffs + width), BF)] * shards)


def add_shards_ff(items, ffs, width):
    own = items[0].shape[0]

    def body(*refs):
        total = tree_sum(ref[...].astype(F32) for ref in refs[:-3])
        up_ref, down_ref, out_ref = refs[-3:]
        up_ref[...] = total[:, :ffs]
        down_ref[...] = total[:, ffs : 2 * ffs]
        out_ref[...] = total[:, 2 * ffs :]

    return small_call(body, "add_shards_ff", items, [((own, ffs), F32)] * 2 + [((own, width), F32)])


def add_plane_attn(place, items, sums):
    own, cols = items[0].shape
    count = len(items)
    width = sums[0].shape[1]

    def body(place_ref, *refs):
        total = tree_sum(ref[...].astype(F32) for ref in refs[:count])
        out_ref, turned_ref = refs[-2:]
        out_ref[:, :cols] = total.astype(BF)
        vectors = tree_sum(ref[...] for ref in refs[count:-2])
        turned_ref[...] = jnp.concatenate([vectors, jnp.zeros((VECTORS - 8, width), F32)], axis=0).T
        mine = turned_ref[pl.ds(pl.multiple_of(place_ref[0] * own, 16), own), :]
        out_ref[:, cols:] = mine.astype(BF)

    spec = pltpu.PrefetchScalarGridSpec(
        num_scalar_prefetch=1, grid=(1,),
        in_specs=[whole(a.shape) for a in (*items, *sums)],
        out_specs=whole((own, cols + VECTORS)),
        scratch_shapes=[pltpu.VMEM((width, VECTORS), F32)],
    )
    return pl.pallas_call(
        body, grid_spec=spec, out_shape=jax.ShapeDtypeStruct((own, cols + VECTORS), BF), name="add_plane_attn",
    )(place, *items, *sums)


def add_shards_attn(items, cols):
    own = items[0].shape[0]

    def body(*refs):
        total = tree_sum(ref[...].astype(F32) for ref in refs[:-6])
        refs[-6][...] = total[:, :cols]
        vectors = jnp.concatenate([total[:, cols:], jnp.zeros((VECTORS - own, VECTORS), F32)], axis=0).T
        refs[-5][...] = vectors[0:3, :own]
        for i in range(4):
            refs[i - 4][...] = vectors[3 + i : 4 + i, :own]

    outs = [((own, cols), F32), ((3, own), F32)] + [((1, own), F32)] * 4
    return small_call(body, "add_shards_attn", items, outs)


def direct_plan(tokens, segment_ids, valid_len, qkv_weight, out_weight, up_weight, down_weight, conv_weight, vectors, cotangent):
    count, seq, width = tokens.shape
    own, ffs = up_weight.shape
    dp, mp = lax.axis_size("dp"), lax.axis_size("mp")
    me = lax.axis_index("dp")
    offsets = [2 * p for p in range(dp // 2)]
    index = jnp.stack([me ^ (p ^ c) for p in offsets for c in range(2)]).astype(jnp.int32)
    narrow, ff_own = small_call(
        pack_weights, "pack_weights",
        (qkv_weight, up_weight, down_weight, conv_weight, *[v.reshape(1, own) for v in vectors]),
        [((own, 3 * width + VECTORS), BF), ((2 * own, ffs), BF)], [((VECTORS, VECTORS), F32)],
    )
    plane = [narrow] + [exchange(narrow, "dp", p) for p in offsets[1:]]
    shards = [ff_own] + [exchange(ff_own, "mp", j) for j in range(1, mp)]
    pieces = [piece for a in plane for piece in (a, exchange(a, "dp", 1))]
    column = jnp.concatenate(shards + [out_weight], axis=0)
    columns = [column] + [exchange(column, "dp", p) for p in offsets[1:]]
    x, mixed, normed, q, k, v, raised, att, inverse, aux, packed, weight = run_forward(
        index, tokens, segment_ids, valid_len, pieces
    )
    columns, att = lax.optimization_barrier((columns, att))
    pieces = [piece for a in columns for piece in (a, exchange(a, "dp", 1))]
    layer_out, grad_mixed, grad_att, sums2, mine, theirs = run_feed_forward(
        index, att, mixed, cotangent, packed, pieces, mp
    )
    received = exchange(theirs, "dp", 1)
    grad_normed, mine_a, theirs_a = run_backward_attention(
        index, weight, q, k, v, raised, att, inverse, normed, grad_att, dp
    )
    received, grad_normed, theirs_a = lax.optimization_barrier((received, grad_normed, theirs_a))
    received_a = exchange(theirs_a, "dp", 1)
    parts = add_halves(mine, received)
    plane = [parts[0]] + [exchange(parts[i], "dp", p) for i, p in enumerate(offsets) if i]
    input_grad, sums = run_backward_conv(x, aux, mixed, grad_mixed, grad_normed, packed, sums2)
    received_a, plane, sums = lax.optimization_barrier((received_a, plane, sums))
    parts = add_halves(mine_a, received_a)
    plane_a = [parts[0]] + [exchange(parts[i], "dp", p) for i, p in enumerate(offsets) if i]
    sums = add_pair(sums, exchange(sums, "dp", 1))
    all_sums = [sums] + [exchange(sums, "dp", p) for p in offsets[1:]]
    parts = add_plane_ff(plane, mp, ffs, width)
    last = [parts[0]] + [exchange(parts[j], "mp", j) for j in range(1, mp)]
    total = add_plane_attn(index[:1], plane_a, all_sums)
    last_a = [total] + [exchange(total, "mp", j) for j in range(1, mp)]
    grad_up, grad_down, grad_out = add_shards_ff(last, ffs, width)
    grad_qkv, grad_conv, *grads = add_shards_attn(last_a, 3 * width)
    return (layer_out, input_grad, grad_qkv, grad_out, grad_up, grad_down, grad_conv, *[g.reshape(own) for g in grads])


def gathered_plan(tokens, segment_ids, valid_len, qkv_weight, out_weight, up_weight, down_weight, conv_weight, vectors, cotangent):
    count, seq, width = tokens.shape
    own = qkv_weight.shape[0]
    dp = width // own
    columns = jnp.stack([conv_weight[0], conv_weight[1], conv_weight[2], *vectors], axis=1)
    narrow = jnp.concatenate([qkv_weight, jnp.pad(columns, ((0, 0), (0, VECTORS - 7))), out_weight], axis=1)
    wide = lax.all_gather(narrow, "dp", axis=0, tiled=True)
    both = lax.all_gather(jnp.concatenate([up_weight, down_weight], axis=0), "mp", axis=1, tiled=True)
    ff = both.shape[1]
    shards = ff // width
    both = lax.all_gather(both, "dp", axis=0).reshape(dp, 2, own, shards, width)
    both = both.transpose(3, 1, 0, 2, 4).reshape(2 * ff, width)
    column = jnp.concatenate([both, wide[:, 3 * width + VECTORS :]], axis=0)
    index = jnp.zeros((1,), jnp.int32)
    x, mixed, normed, q, k, v, raised, att, inverse, aux, packed, weight = run_forward(
        index, tokens, segment_ids, valid_len, [wide[:, : 3 * width + VECTORS]]
    )
    layer_out, grad_mixed, grad_att, sums2, grads = run_feed_forward(
        index, att, mixed, cotangent, packed, [column], shards
    )
    grad_normed, grad_qkv = run_backward_attention(
        index, weight, q, k, v, raised, att, inverse, normed, grad_att, 1
    )
    input_grad, sums = run_backward_conv(x, aux, mixed, grad_mixed, grad_normed, packed, sums2)
    grad_ff = grads[0, :, : 2 * ff].reshape(width, shards, 2, width).transpose(0, 2, 1, 3).reshape(width, 2 * ff)
    grad_ff = lax.psum_scatter(grad_ff, "dp", scatter_dimension=0, tiled=True).reshape(own, 2, ff)
    grad_ff = lax.psum_scatter(grad_ff, "mp", scatter_dimension=2, tiled=True).astype(F32)
    grad_attn = jnp.concatenate([grad_qkv[0], grads[0, :, 2 * ff :]], axis=1)
    grad_attn = lax.psum_scatter(grad_attn, "dp", scatter_dimension=0, tiled=True)
    grad_attn = lax.psum(grad_attn, "mp").astype(F32)
    sums = lax.psum(sums, ("dp", "mp"))
    sums = lax.dynamic_slice_in_dim(sums, lax.axis_index("dp") * own, own, axis=1)
    return (
        layer_out, input_grad, grad_attn[:, : 3 * width], grad_attn[:, 3 * width :],
        grad_ff[:, 0], grad_ff[:, 1], sums[0:3], sums[3], sums[4], sums[5], sums[6],
    )


def on_device(
    tokens, segment_ids, valid_len, qkv_weight, out_weight, up_weight, down_weight, conv_weight,
    ln1_gain, ln1_shift, ln2_gain, ln2_shift, cotangent,
):
    own, ffs = up_weight.shape
    direct = own % 16 == 0 and ffs == tokens.shape[2] and own <= VECTORS
    plan = direct_plan if direct else gathered_plan
    return plan(
        tokens, segment_ids, valid_len, qkv_weight, out_weight, up_weight, down_weight, conv_weight,
        (ln1_gain, ln1_shift, ln2_gain, ln2_shift), cotangent,
    )


def solution(mesh):
    rows = P(("dp", "mp"), None, None)
    weights = (P("dp", None), P("dp", None), P("dp", "mp"), P("dp", "mp"), P(None, "dp"))
    vectors = (P("dp"),) * 4
    return jax.shard_map(
        on_device,
        mesh=mesh,
        in_specs=(rows, P(("dp", "mp"), None), P(("dp", "mp"))) + weights + vectors + (rows,),
        out_specs=(rows, rows) + weights + vectors,
        check_vma=False,
    )
```

```python
import functools
import math

import jax
import jax.numpy as jnp
from jax import lax
from jax.experimental import pallas as pl
from jax.experimental.pallas import tpu as pltpu
from jax.sharding import PartitionSpec as P

HEADS = 6
VECTORS = 128
LANES = 128
BF = jnp.bfloat16
F32 = jnp.float32
VMEM_LIMIT = 60 * 1024 * 1024


def mm(lhs, rhs):
    return lax.dot_general(lhs, rhs, (((1,), (0,)), ((), ())), preferred_element_type=F32)


def mm_nt(lhs, rhs):
    return lax.dot_general(lhs, rhs, (((1,), (1,)), ((), ())), preferred_element_type=F32)


def tree_sum(items):
    items = list(items)
    while len(items) > 1:
        items = [a + b for a, b in zip(items[::2], items[1::2])]
    return items[0]


def pack_weights(qkv_ref, up_ref, down_ref, conv_ref, g1_ref, s1_ref, g2_ref, s2_ref, narrow_ref, ff_ref, rows_ref):
    own, ffs = up_ref.shape
    rows_ref[...] = jnp.zeros_like(rows_ref)
    rows_ref[0:3, :own] = conv_ref[...].astype(F32)
    for i, ref in enumerate((g1_ref, s1_ref, g2_ref, s2_ref)):
        rows_ref[3 + i : 4 + i, :own] = ref[...].astype(F32)
    wide = qkv_ref.shape[1]
    narrow_ref[:, :wide] = qkv_ref[...]
    narrow_ref[:, wide:] = rows_ref[...].T[:own].astype(BF)
    ff_ref[:own] = up_ref[...]
    ff_ref[own:] = down_ref[...]


def tiles(total, size):
    return [slice(at, at + size) for at in range(0, total, size)]


def twice(tile, lanes):
    return jnp.concatenate([tile] * (lanes // LANES), axis=1)


def load_columns(packed_ref, col_ref, places):
    for i, place in enumerate(places):
        column = packed_ref[:, place : place + 1].astype(F32)
        col_ref[i] = jnp.broadcast_to(column, (column.shape[0], LANES))


def column_mean(values):
    return jnp.sum(values, axis=0, keepdims=True) * (1.0 / values.shape[0])


def norm_columns(values):
    centred = values - column_mean(values)
    scale = lax.rsqrt(column_mean(centred * centred) + 1e-06)
    return centred * scale, scale


def fold(values):
    rows, lanes = values.shape
    return jnp.sum(values.reshape(rows // 8, 8, lanes), axis=0)


def fold_lanes(values):
    return sum(values[:, t] for t in tiles(values.shape[1], LANES))


def forward_attention(index_ref, len_ref, tok_ref, seg_ref, *refs, pieces):
    piece_refs = refs[:pieces]
    (
        x_ref, mc_ref, norm_ref, q_ref, k_ref, v_ref, e_ref, att_ref, inv_ref, aux_ref, packed_ref, w_ref,
        wt_ref, wide_ref, col_ref, bias_ref, key_ref, value_ref, score_ref,
    ) = refs[pieces:]
    rows, seq, width = tok_ref.shape
    head = width // HEADS
    step = pl.program_id(0)

    @pl.when(step == 0)
    def _():
        own = width // pieces
        for i, ref in enumerate(piece_refs):
            wide_ref[pl.ds(pl.multiple_of(index_ref[i] * own, 16), own), :] = ref[...]
        w_ref[...] = wide_ref[:, : 3 * width]
        wt_ref[:width] = (wide_ref[:, :width].astype(F32) * head ** (-0.5)).astype(BF).T
        wt_ref[width:] = wide_ref[:, width : 3 * width].T
        packed_ref[...] = wide_ref[:, 3 * width :]
        load_columns(packed_ref, col_ref, range(5))

    place = lax.broadcasted_iota(jnp.int32, (1, seq), 1)
    for r in range(rows):
        segs = seg_ref[pl.ds(step * rows + r, 1), :].astype(F32)
        valid = place < len_ref[step * rows + r]
        number = jnp.where(valid, segs, -1.0)
        links = jnp.where(valid & (place > 0) & (number == pltpu.roll(number, 1, 1)), 1.0, 0.0)
        next_links = jnp.where(place < seq - 1, pltpu.roll(links, seq - 1, 1), 0.0)
        none = jnp.zeros_like(links)
        aux = jnp.concatenate([links, next_links, number, none, none, none, none, none], axis=0)
        aux_ref[r] = aux
        key_number = aux.T[:, 2:3]
        for t in tiles(seq, 64):
            row_id = lax.broadcasted_iota(jnp.int32, (64, seq), 0) + t.start
            col_id = lax.broadcasted_iota(jnp.int32, (64, seq), 1)
            bias_ref[r, t] = jnp.where((key_number[t] == segs) | (row_id == col_id), 0.0, -1e30)
        x_ref[r] = tok_ref[r].T
        for t in tiles(width, 64):
            base = x_ref[r, t].astype(F32)
            before = pltpu.roll(base, 1, 1) * links
            after = pltpu.roll(base, seq - 1, 1) * next_links
            conv0, conv1, conv2 = [twice(col_ref[i, t], seq) for i in range(3)]
            mc_ref[r, t] = base + before * conv0 + base * conv1 + after * conv2
        for t in tiles(seq, LANES):
            n, _ = norm_columns(mc_ref[r, :, t])
            norm_ref[r, :, t] = (n * col_ref[3] + col_ref[4]).astype(BF)
    for r in range(rows):
        normed = norm_ref[r]
        q_ref[r] = mm(wt_ref[:width], normed).astype(BF)
        k_ref[r] = mm(wt_ref[width : 2 * width], normed).astype(BF)
        key_ref[r] = k_ref[r].T
        value_ref[r] = mm(wt_ref[2 * width :], normed).astype(BF)
        v_ref[r] = value_ref[r].T
    zero = jnp.zeros((head, seq), BF)

    def scores(r, h):
        own = q_ref[r, h * head : (h + 1) * head]
        pair = [own, zero] if h % 2 == 0 else [zero, own]
        lanes = slice(h // 2 * 2 * head, (h // 2 + 1) * 2 * head)
        score_ref[r, h] = mm(key_ref[r, :, lanes], jnp.concatenate(pair, axis=0))

    work = [(r, h) for r in range(rows) for h in range(HEADS)]
    scores(*work[0])
    for at, (r, h) in enumerate(work):
        if at + 1 < len(work):
            scores(*work[at + 1])
        for t in tiles(seq, LANES):
            masked = score_ref[r, h, :, t] + bias_ref[r, :, t]
            raised = jnp.exp(masked - jnp.max(masked, axis=0, keepdims=True))
            inv_ref[r, h : h + 1, t] = 1.0 / jnp.sum(raised, axis=0, keepdims=True)
            e_ref[r, h, :, t] = raised.astype(BF)
        part = slice(h * head, (h + 1) * head)
        att = mm(value_ref[r, part], e_ref[r, h]) * inv_ref[r, h : h + 1]
        att_ref[r, part] = att.astype(BF)


def gelu_parts(x):
    cdf = 0.5 * lax.erf(x * math.sqrt(0.5)) + 0.5
    bell = jnp.exp2(x * x * (-0.5 / math.log(2.0)) - 0.5 * math.log2(2.0 * math.pi))
    return x * cdf, cdf + x * bell


def feed_forward(index_ref, att_ref, mc_ref, ct_ref, packed_ref, *refs, pieces, shards):
    piece_refs = refs[:pieces]
    groups = 2 if pieces > 1 else 1
    lo_ref, gm_ref, ga_ref, gs_ref = refs[pieces : pieces + 4]
    gw_refs = refs[pieces + 4 : pieces + 4 + groups]
    (
        up_ref, down_ref, upt_ref, downt_ref, out_ref, outt_ref, up_acc, down_acc, out_acc, col_acc, col_ref,
        att_cat, mixed_ref, n_ref, norm_ref, ctt_ref, pre_ref, gh_ref, hidden_ref, gp_ref, gn_ref, scale_ref, lot_ref,
        branch_ref,
    ) = refs[pieces + 4 + groups :]
    rows, seq, width = ct_ref.shape
    ff = up_ref.shape[1]
    ffs = ff // shards
    own = width // pieces
    step = pl.program_id(0)

    @pl.when(step == 0)
    def _():
        for acc in (up_acc, down_acc, out_acc, col_acc):
            acc[...] = jnp.zeros_like(acc)
        for i, ref in enumerate(piece_refs):
            here = pl.ds(pl.multiple_of(index_ref[i] * own, 16), own)
            for j in range(shards):
                up_ref[here, j * ffs : (j + 1) * ffs] = ref[2 * j * own : (2 * j + 1) * own]
                down_ref[here, j * ffs : (j + 1) * ffs] = ref[(2 * j + 1) * own : (2 * j + 2) * own]
            out_ref[here, :] = ref[2 * shards * own :]
        upt_ref[...] = up_ref[...].T
        downt_ref[...] = down_ref[...].T
        outt_ref[...] = out_ref[...].T
        load_columns(packed_ref, col_ref, (5, 6))

    for r in range(rows):
        lanes = slice(r * seq, (r + 1) * seq)
        ctt_ref[:, lanes] = ct_ref[r].T
        att_cat[:, lanes] = att_ref[r]
        mixed_ref[:, lanes] = mc_ref[r] + mm(outt_ref[...], att_ref[r])
    for t in tiles(rows * seq, LANES):
        n, scale = norm_columns(mixed_ref[:, t])
        n_ref[:, t] = n
        scale_ref[0:1, t] = scale
        norm_ref[:, t] = (n * col_ref[0] + col_ref[1]).astype(BF)

    blocks = tiles(ff, 256)

    def opening(rows_of):
        pre_ref[rows_of] = mm(upt_ref[rows_of], norm_ref[...])
        gh_ref[rows_of] = mm(downt_ref[rows_of], ctt_ref[...])

    opening(blocks[0])
    for at, block in enumerate(blocks):
        if at + 1 < len(blocks):
            opening(blocks[at + 1])
        for low in range(block.start, block.stop, 16):
            t = slice(low, low + 16)
            hidden, slope = gelu_parts(pre_ref[t])
            hidden_ref[t] = hidden.astype(BF)
            gp_ref[t] = (gh_ref[t] * slope).astype(BF)
        down_acc[:, block] += mm_nt(ctt_ref[...], hidden_ref[block])
        up_acc[:, block] += mm_nt(norm_ref[...], gp_ref[block])
    gn_ref[...] = mm(up_ref[...], gp_ref[...])
    lot_ref[...] = (mixed_ref[...] + mm(down_ref[...], hidden_ref[...])).astype(BF)
    spots = tiles(rows * seq, LANES)
    mean_e = [jnp.zeros((8, LANES), F32) for _ in spots]
    mean_en = [jnp.zeros((8, LANES), F32) for _ in spots]
    for d in tiles(width, 32):
        column = col_ref[0, d]
        gain_sum, shift_sum = col_acc[0, d], col_acc[1, d]
        for i, t in enumerate(spots):
            grad_n = gn_ref[d, t]
            product = grad_n * n_ref[d, t]
            gain_sum += product
            shift_sum += grad_n
            mean_e[i] += fold(grad_n * column)
            mean_en[i] += fold(product * column)
        col_acc[0, d] = gain_sum
        col_acc[1, d] = shift_sum
    for i, t in enumerate(spots):
        me = jnp.sum(mean_e[i], axis=0, keepdims=True) * (1.0 / width)
        men = jnp.sum(mean_en[i], axis=0, keepdims=True) * (1.0 / width)
        scale = scale_ref[0:1, t]
        row, inside = divmod(t.start, seq)
        for d in tiles(width, 64):
            change = scale * (gn_ref[d, t] * col_ref[0, d] - me - n_ref[d, t] * men)
            grad_mixed = ctt_ref[d, t].astype(F32) + change
            gm_ref[row, d, inside : inside + LANES] = grad_mixed
            branch_ref[d, t] = grad_mixed.astype(BF)
    out_acc[...] += mm_nt(att_cat[...], branch_ref[...])
    for r in range(rows):
        lanes = slice(r * seq, (r + 1) * seq)
        ga_ref[r] = mm(out_ref[...], branch_ref[:, lanes]).astype(BF)
        lo_ref[r] = lot_ref[:, lanes].T

    @pl.when(step == pl.num_programs(0) - 1)
    def _():
        for i in range(pieces):
            here = pl.ds(pl.multiple_of(index_ref[i] * own, 16), own)
            place = gw_refs[i % groups]
            for j in range(shards):
                cols = slice(j * ffs, (j + 1) * ffs)
                place[i // groups, :, 2 * j * ffs : (2 * j + 1) * ffs] = up_acc[here, cols].astype(BF)
                place[i // groups, :, (2 * j + 1) * ffs : (2 * j + 2) * ffs] = down_acc[here, cols].astype(BF)
            place[i // groups, :, 2 * ff :] = out_acc[here, :].astype(BF)
        gs_ref[...] = jnp.zeros_like(gs_ref)
        for i in range(2):
            gs_ref[5 + i : 6 + i] = jnp.sum(col_acc[i].T, axis=0, keepdims=True)


def backward_attention(
    q_ref, k_ref, v_ref, e_ref, att_ref, inv_ref, norm_ref, ga_ref, index_ref, w_ref, start_ref, gn_ref, *refs, pieces
):
    gw_refs = refs[:-5]
    proj_ref, w_acc, norm_cat, soft_ref, logit_ref = refs[-5:]
    rows, seq, width = v_ref.shape
    own = width // pieces
    head = width // HEADS
    step = pl.program_id(0)

    @pl.when(step == 0)
    def _():
        w_acc[...] = jnp.zeros_like(w_acc) if start_ref is None else start_ref[...]

    zero = jnp.zeros((head, seq), BF)
    work = [(r, h) for r in range(rows) for h in range(HEADS)]

    def opening(r, h):
        part = slice(h * head, (h + 1) * head)
        lanes = slice(h // 2 * 2 * head, (h // 2 + 1) * 2 * head)
        grad_att = ga_ref[r, part].astype(F32) * inv_ref[r, h : h + 1]
        inner = jnp.sum(grad_att * att_ref[r, part].astype(F32), axis=0, keepdims=True)
        grad_att = grad_att.astype(BF)
        pair = [grad_att, zero] if h % 2 == 0 else [zero, grad_att]
        soft_ref[r, h] = mm(v_ref[r, :, lanes], jnp.concatenate(pair, axis=0))
        return grad_att, inner

    ready = opening(*work[0])
    for at, (r, h) in enumerate(work):
        grad_att, inner = ready
        if at + 1 < len(work):
            ready = opening(*work[at + 1])
        for t in tiles(seq, 32):
            raised = e_ref[r, h, t].astype(F32)
            logit_ref[r, h, t] = (raised * (soft_ref[r, h, t] - inner)).astype(BF)
        part = slice(h * head, (h + 1) * head)
        place = slice(r * seq, (r + 1) * seq)
        grad_logits = logit_ref[r, h]
        grad_q = mm(k_ref[r, part], grad_logits) * head ** (-0.5)
        proj_ref[h * head : (h + 1) * head, place] = grad_q.astype(BF)
        grad_k = mm_nt(q_ref[r, part], grad_logits)
        proj_ref[width + h * head : width + (h + 1) * head, place] = grad_k.astype(BF)
        grad_v = mm_nt(grad_att, e_ref[r, h])
        proj_ref[2 * width + h * head : 2 * width + (h + 1) * head, place] = grad_v.astype(BF)
    for r in range(rows):
        norm_cat[:, r * seq : (r + 1) * seq] = norm_ref[r]
        gn_ref[r] = mm(w_ref[...], proj_ref[:, r * seq : (r + 1) * seq]).astype(BF)
    w_acc[...] += mm_nt(norm_cat[...], proj_ref[...])

    @pl.when(step == pl.num_programs(0) - 1)
    def _():
        if start_ref is None:
            gw_refs[0][...] = w_acc[...]
        else:
            groups = len(gw_refs)
            for i in range(pieces):
                here = pl.ds(pl.multiple_of(index_ref[i] * own, 16), own)
                gw_refs[i % groups][i // groups] = w_acc[here, :].astype(BF)


def backward_conv(
    x_ref, aux_ref, mc_ref, gm_ref, gn_ref, packed_ref, other_ref, part_ref, ig_ref, gs_ref,
    acc_ref, col_ref, n_ref, g_ref, turn_ref,
):
    rows, width, seq = x_ref.shape
    step = pl.program_id(0)

    @pl.when(step == 0)
    def _():
        acc_ref[...] = jnp.zeros_like(acc_ref)
        load_columns(packed_ref, col_ref, range(4))

    spots = tiles(seq, LANES)
    for r in range(rows):
        scales = []
        for t in spots:
            n, scale = norm_columns(mc_ref[r, :, t])
            n_ref[r, :, t] = n
            scales.append(scale)
        mean_e = [jnp.zeros((8, LANES), F32) for _ in spots]
        mean_en = [jnp.zeros((8, LANES), F32) for _ in spots]
        for d in tiles(width, 32):
            column = col_ref[3, d]
            gain_sum, shift_sum = acc_ref[3, d], acc_ref[4, d]
            for i, t in enumerate(spots):
                grad_n = gn_ref[r, d, t].astype(F32)
                product = grad_n * n_ref[r, d, t]
                gain_sum += product
                shift_sum += grad_n
                mean_e[i] += fold(grad_n * column)
                mean_en[i] += fold(product * column)
            acc_ref[3, d] = gain_sum
            acc_ref[4, d] = shift_sum
        for i, t in enumerate(spots):
            me = jnp.sum(mean_e[i], axis=0, keepdims=True) * (1.0 / width)
            men = jnp.sum(mean_en[i], axis=0, keepdims=True) * (1.0 / width)
            for d in tiles(width, 64):
                e = gn_ref[r, d, t].astype(F32) * col_ref[3, d]
                g_ref[r, d, t] = gm_ref[r, d, t] + scales[i] * (e - me - n_ref[r, d, t] * men)
        links, next_links = aux_ref[r, 0:1], aux_ref[r, 1:2]
        for d in tiles(width, 32):
            g = g_ref[r, d]
            base = x_ref[r, d].astype(F32)
            before = pltpu.roll(g, 1, 1) * links
            after = pltpu.roll(g, seq - 1, 1) * next_links
            acc_ref[0, d] += fold_lanes(base * after)
            acc_ref[1, d] += fold_lanes(base * g)
            acc_ref[2, d] += fold_lanes(base * before)
            conv0, conv1, conv2 = [twice(col_ref[i, d], seq) for i in range(3)]
            turn_ref[r, d] = (g + conv1 * g + conv0 * after + conv2 * before).astype(BF)
        ig_ref[r] = turn_ref[r].T

    @pl.when(step == pl.num_programs(0) - 1)
    def _():
        gs_ref[...] = other_ref[...]
        for i in range(5):
            gs_ref[i : i + 1] += jnp.sum(acc_ref[i].T, axis=0, keepdims=True)


def by_row(shape, rows, first=0):
    tail = tuple(shape[1:])
    return pl.BlockSpec((rows,) + tail, lambda i, *_: (i + first,) + (0,) * len(tail))


def whole(shape):
    place = (0,) * len(shape)
    return pl.BlockSpec(tuple(shape), lambda i, *_: place)


def step_rows(count, most):
    return max(r for r in range(1, most + 1) if count % r == 0)


def call(body, name, scalars, rows, row_args, args, row_outs, outs, scratch, span=None, into=None):
    first, count = span or (0, row_args[0].shape[0])
    skip = first // rows
    in_specs = [by_row(a.shape, rows, skip if a.shape[0] > count else 0) for a in row_args]
    in_specs += [whole(a.shape) for a in args]
    aliases = {}
    if into is not None:
        in_specs.append(pl.BlockSpec(memory_space=pl.ANY))
        aliases = {len(scalars) + len(in_specs) - 1: 0}
    spec = pltpu.PrefetchScalarGridSpec(
        num_scalar_prefetch=len(scalars),
        grid=(count // rows,),
        in_specs=in_specs,
        out_specs=[by_row(s, rows, skip if s[0] > count else 0) for s, _ in row_outs] + [whole(s) for s, _ in outs],
        scratch_shapes=[pltpu.VMEM(s, t) for s, t in scratch],
    )
    return pl.pallas_call(
        body,
        grid_spec=spec,
        out_shape=[jax.ShapeDtypeStruct(s, t) for s, t in row_outs + outs],
        input_output_aliases=aliases,
        compiler_params=pltpu.CompilerParams(dimension_semantics=("arbitrary",), vmem_limit_bytes=VMEM_LIMIT),
        name=name,
    )(*scalars, *row_args, *args, *(() if into is None else (into,)))


def small_call(body, name, args, outs, scratch=()):
    return pl.pallas_call(
        body,
        out_shape=[jax.ShapeDtypeStruct(s, t) for s, t in outs],
        scratch_shapes=[pltpu.VMEM(s, t) for s, t in scratch],
        compiler_params=pltpu.CompilerParams(vmem_limit_bytes=VMEM_LIMIT),
        name=name,
    )(*args)


def run_forward(index, tokens, segment_ids, valid_len, pieces):
    count, seq, width = tokens.shape
    flipped = (count, width, seq)
    rows = step_rows(count, 2)
    row_outs = [
        (flipped, BF), (flipped, F32), (flipped, BF), (flipped, BF), (flipped, BF), ((count, seq, width), BF),
        ((count, HEADS, seq, seq), BF), (flipped, BF), ((count, 8, seq), F32), ((count, 8, seq), F32),
    ]
    return call(
        functools.partial(forward_attention, pieces=len(pieces)), "forward_attention", (index, valid_len),
        rows, (tokens,), (segment_ids, *pieces),
        row_outs, [((width, VECTORS), BF), ((width, 3 * width), BF)],
        [
            ((3 * width, width), BF), ((width, 3 * width + VECTORS), BF), ((5, width, LANES), F32),
            ((rows, seq, seq), F32), ((rows, seq, width), BF), ((rows, width, seq), BF), ((rows, HEADS, seq, seq), F32),
        ],
    )


def run_feed_forward(index, att, mixed, cotangent, packed, pieces, shards):
    count, seq, width = cotangent.shape
    own = width // len(pieces)
    ff = shards * width
    groups = 2 if len(pieces) > 1 else 1
    rows = step_rows(count, 2)
    wide = rows * seq
    row_outs = [((count, seq, width), BF), ((count, width, seq), F32), ((count, width, seq), BF)]
    grads = ((len(pieces) // groups, own, 2 * ff + width), BF)
    return call(
        functools.partial(feed_forward, pieces=len(pieces), shards=shards), "feed_forward", (index,),
        rows, (att, mixed, cotangent), (packed, *pieces),
        row_outs, [((8, width), F32)] + [grads] * groups,
        [((width, ff), BF)] * 2 + [((ff, width), BF)] * 2 + [((width, width), BF)] * 2
        + [((width, ff), F32)] * 2 + [((width, width), F32), ((2, width, LANES), F32), ((2, width, LANES), F32)]
        + [((width, wide), BF), ((width, wide), F32), ((width, wide), F32), ((width, wide), BF), ((width, wide), BF)]
        + [((ff, wide), F32)] * 2 + [((ff, wide), BF)] * 2
        + [((width, wide), F32), ((8, wide), F32), ((width, wide), BF), ((width, wide), BF)],
    )


def run_backward_attention(index, weight, kept, grad_att, pieces, span, start):
    count, seq, width = kept[2].shape
    own = width // pieces
    groups = 2 if pieces > 1 else 1
    rows = step_rows(span[1], 2)
    row_args = (*kept, grad_att)
    many = len(row_args)

    def body(index_ref, *refs):
        w_ref, rest = refs[many], refs[many + 1 :]
        start_ref, rest = (None, rest) if start is None else (rest[0], rest[1:])
        backward_attention(*refs[:many], index_ref, w_ref, start_ref, *rest, pieces=pieces)

    outs = [((width, 3 * width), F32)] if start is None else [((pieces // groups, own, 3 * width), BF)] * groups
    return call(
        body, "backward_attention", (index,), rows, row_args, (weight,) if start is None else (weight, start),
        [((span[1], width, seq), BF)], outs,
        [
            ((3 * width, rows * seq), BF), ((width, 3 * width), F32), ((width, rows * seq), BF),
            ((rows, HEADS, seq, seq), F32), ((rows, HEADS, seq, seq), BF),
        ],
        span=span,
    )


def run_backward_conv(x, aux, mixed, grad_mixed, grad_normed, packed, other, span, into):
    count, width, seq = x.shape
    rows = step_rows(span[1], 2)

    def body(*refs):
        if into is None:
            backward_conv(*refs[:7], None, *refs[7:])
        else:
            backward_conv(*refs)

    return call(
        body, "backward_conv", (), rows,
        (x, aux, mixed, grad_mixed, grad_normed), (packed, other),
        [((count, seq, width), BF)], [((8, width), F32)],
        [
            ((5, width, LANES), F32), ((4, width, LANES), F32), ((rows, width, seq), F32), ((rows, width, seq), F32),
            ((rows, width, seq), BF),
        ],
        span=span, into=into,
    )


def halves(count):
    early = count // 3
    return ((0, early), (early, count - early)) if early % 2 == 0 and early else ((0, count // 2), (count // 2, count - count // 2))


def exchange(values, axis, offset):
    size = lax.axis_size(axis)
    return lax.ppermute(values, axis, [(i, i ^ offset) for i in range(size)])


def add_halves(mine, received):
    count, own, cols = mine.shape

    def body(mine_ref, received_ref, *out_refs):
        for i, ref in enumerate(out_refs):
            ref[...] = (mine_ref[i].astype(F32) + received_ref[i].astype(F32)).astype(BF)

    return small_call(body, "add_halves", (mine, received), [((own, cols), BF)] * count)


def add_wide(*items):
    return tree_sum(item.astype(F32) for item in items)


def add_shard_vectors(items, own):
    def body(*refs):
        total = tree_sum(ref[...] for ref in refs[:-5])
        refs[-5][...] = total[0:3, :own]
        for i in range(4):
            refs[i - 4][...] = total[3 + i : 4 + i, :own]

    return small_call(body, "add_shard_vectors", items, [((3, own), F32)] + [((1, own), F32)] * 4)


def direct_plan(tokens, segment_ids, valid_len, qkv_weight, out_weight, up_weight, down_weight, conv_weight, vectors, cotangent):
    count, seq, width = tokens.shape
    own, ffs = up_weight.shape
    dp, mp = lax.axis_size("dp"), lax.axis_size("mp")
    me = lax.axis_index("dp")
    offsets = [2 * p for p in range(dp // 2)]
    index = jnp.stack([me ^ (p ^ c) for p in offsets for c in range(2)]).astype(jnp.int32)
    narrow, ff_own = small_call(
        pack_weights, "pack_weights",
        (qkv_weight, up_weight, down_weight, conv_weight, *[v.reshape(1, own) for v in vectors]),
        [((own, 3 * width + VECTORS), BF), ((2 * own, ffs), BF)], [((VECTORS, VECTORS), F32)],
    )
    plane = [narrow] + [exchange(narrow, "dp", p) for p in offsets[1:]]
    shards = [ff_own] + [exchange(ff_own, "mp", j) for j in range(1, mp)]
    pieces = [piece for a in plane for piece in (a, exchange(a, "dp", 1))]
    column = jnp.concatenate(shards + [out_weight], axis=0)
    columns = [column] + [exchange(column, "dp", p) for p in offsets[1:]]
    x, mixed, normed, q, k, v, raised, att, inverse, aux, packed, weight = run_forward(
        index, tokens, segment_ids, valid_len, pieces
    )
    columns, att = lax.optimization_barrier((columns, att))
    pieces = [piece for a in columns for piece in (a, exchange(a, "dp", 1))]
    layer_out, grad_mixed, grad_att, sums2, mine, theirs = run_feed_forward(
        index, att, mixed, cotangent, packed, pieces, mp
    )
    received = exchange(theirs, "dp", 1)
    early, late = halves(count)
    kept = (q, k, v, raised, att, inverse, normed)
    grad_normed1, start = run_backward_attention(index, weight, kept, grad_att, dp, early, None)
    received, start = lax.optimization_barrier((received, start))
    parts = list(add_halves(mine, received))
    parts[0], start = lax.optimization_barrier((parts[0], start))
    plane = [parts[0]] + [exchange(parts[i], "dp", p) for i, p in enumerate(offsets) if i]
    grad_normed2, mine_a, theirs_a = run_backward_attention(index, weight, kept, grad_att, dp, late, start)
    plane, theirs_a = lax.optimization_barrier((plane, theirs_a))
    received_a = exchange(theirs_a, "dp", 1)
    total = add_wide(*plane).astype(BF)
    half = 2 * ffs * (mp // 2)
    near, far, out_part = total[:, :half], total[:, half:], total[:, 2 * half :]
    received_f = exchange(far, "mp", 2)
    near, grad_normed1 = lax.optimization_barrier((near, grad_normed1))
    some_grad, sums = run_backward_conv(x, aux, mixed, grad_mixed, grad_normed1, packed, sums2, early, None)
    received_a, sums = lax.optimization_barrier((received_a, sums))
    parts = list(add_halves(mine_a, received_a))
    parts[0], sums = lax.optimization_barrier((parts[0], sums))
    plane_a = [parts[0]] + [exchange(parts[i], "dp", p) for i, p in enumerate(offsets) if i]
    input_grad, sums = run_backward_conv(x, aux, mixed, grad_mixed, grad_normed2, packed, sums, late, some_grad)
    received_s = exchange(sums, "dp", 1)
    plane_a, received_f, sums = lax.optimization_barrier((plane_a, received_f, sums))
    total = add_wide(*plane_a).astype(BF)
    received_s, total = lax.optimization_barrier((received_s, total))
    received_1 = exchange(total, "mp", 2)
    sums = sums + received_s
    plane_s = [sums] + [exchange(sums, "dp", p) for p in offsets[1:]]
    near_sum = add_wide(near, received_f[:, :half])
    out_sum = lax.optimization_barrier(add_wide(out_part, received_f[:, half:]).astype(BF))
    keep = near_sum[:, : 2 * ffs]
    send = jnp.concatenate([near_sum[:, 2 * ffs :].astype(BF), out_sum], axis=1)
    received_n = exchange(send, "mp", 1)
    plane_s, received_1 = lax.optimization_barrier((plane_s, received_1))
    total = lax.optimization_barrier(add_wide(total, received_1).astype(BF))
    received_2 = exchange(total, "mp", 1)
    vectors = lax.dynamic_slice_in_dim(tree_sum(plane_s), me * own, own, axis=1)
    shards = [vectors] + [exchange(vectors, "mp", j) for j in range(1, mp)]
    grad_up = keep[:, :ffs] + received_n[:, :ffs].astype(F32)
    grad_down = keep[:, ffs:] + received_n[:, ffs : 2 * ffs].astype(F32)
    grad_out = add_wide(out_sum, received_n[:, 2 * ffs :])
    grad_qkv = add_wide(total, received_2)
    grad_conv, *grads = add_shard_vectors(shards, own)
    return (layer_out, input_grad, grad_qkv, grad_out, grad_up, grad_down, grad_conv, *[g.reshape(own) for g in grads])


def gathered_plan(tokens, segment_ids, valid_len, qkv_weight, out_weight, up_weight, down_weight, conv_weight, vectors, cotangent):
    count, seq, width = tokens.shape
    own = qkv_weight.shape[0]
    dp = width // own
    columns = jnp.stack([conv_weight[0], conv_weight[1], conv_weight[2], *vectors], axis=1)
    narrow = jnp.concatenate([qkv_weight, jnp.pad(columns, ((0, 0), (0, VECTORS - 7))), out_weight], axis=1)
    wide = lax.all_gather(narrow, "dp", axis=0, tiled=True)
    both = lax.all_gather(jnp.concatenate([up_weight, down_weight], axis=0), "mp", axis=1, tiled=True)
    ff = both.shape[1]
    shards = ff // width
    both = lax.all_gather(both, "dp", axis=0).reshape(dp, 2, own, shards, width)
    both = both.transpose(3, 1, 0, 2, 4).reshape(2 * ff, width)
    column = jnp.concatenate([both, wide[:, 3 * width + VECTORS :]], axis=0)
    index = jnp.zeros((1,), jnp.int32)
    x, mixed, normed, q, k, v, raised, att, inverse, aux, packed, weight = run_forward(
        index, tokens, segment_ids, valid_len, [wide[:, : 3 * width + VECTORS]]
    )
    layer_out, grad_mixed, grad_att, sums2, grads = run_feed_forward(
        index, att, mixed, cotangent, packed, [column], shards
    )
    early, late = halves(count)
    kept = (q, k, v, raised, att, inverse, normed)
    grad_normed1, start = run_backward_attention(index, weight, kept, grad_att, 1, early, None)
    grad_normed2, grad_qkv = run_backward_attention(index, weight, kept, grad_att, 1, late, start)
    some_grad, sums = run_backward_conv(x, aux, mixed, grad_mixed, grad_normed1, packed, sums2, early, None)
    input_grad, sums = run_backward_conv(x, aux, mixed, grad_mixed, grad_normed2, packed, sums, late, some_grad)
    grad_ff = grads[0, :, : 2 * ff].reshape(width, shards, 2, width).transpose(0, 2, 1, 3).reshape(width, 2 * ff)
    grad_ff = lax.psum_scatter(grad_ff, "dp", scatter_dimension=0, tiled=True).reshape(own, 2, ff)
    grad_ff = lax.psum_scatter(grad_ff, "mp", scatter_dimension=2, tiled=True).astype(F32)
    grad_attn = jnp.concatenate([grad_qkv[0], grads[0, :, 2 * ff :]], axis=1)
    grad_attn = lax.psum_scatter(grad_attn, "dp", scatter_dimension=0, tiled=True)
    grad_attn = lax.psum(grad_attn, "mp").astype(F32)
    sums = lax.psum(sums, ("dp", "mp"))
    sums = lax.dynamic_slice_in_dim(sums, lax.axis_index("dp") * own, own, axis=1)
    return (
        layer_out, input_grad, grad_attn[:, : 3 * width], grad_attn[:, 3 * width :],
        grad_ff[:, 0], grad_ff[:, 1], sums[0:3], sums[3], sums[4], sums[5], sums[6],
    )


def on_device(
    tokens, segment_ids, valid_len, qkv_weight, out_weight, up_weight, down_weight, conv_weight,
    ln1_gain, ln1_shift, ln2_gain, ln2_shift, cotangent,
):
    own, ffs = up_weight.shape
    direct = own % 16 == 0 and ffs == tokens.shape[2] and own <= VECTORS and lax.axis_size("mp") == 4
    plan = direct_plan if direct else gathered_plan
    return plan(
        tokens, segment_ids, valid_len, qkv_weight, out_weight, up_weight, down_weight, conv_weight,
        (ln1_gain, ln1_shift, ln2_gain, ln2_shift), cotangent,
    )


def solution(mesh):
    rows = P(("dp", "mp"), None, None)
    weights = (P("dp", None), P("dp", None), P("dp", "mp"), P("dp", "mp"), P(None, "dp"))
    vectors = (P("dp"),) * 4
    return jax.shard_map(
        on_device,
        mesh=mesh,
        in_specs=(rows, P(("dp", "mp"), None), P(("dp", "mp"))) + weights + vectors + (rows,),
        out_specs=(rows, rows) + weights + vectors,
        check_vma=False,
    )
```

```python
import functools
import math

import jax
import jax.numpy as jnp
from jax import lax
from jax.experimental import pallas as pl
from jax.experimental.pallas import tpu as pltpu
from jax.sharding import PartitionSpec as P

HEADS = 6
VECTORS = 128
LANES = 128
BF = jnp.bfloat16
F32 = jnp.float32
MIB = 1024 * 1024
VMEM_LIMITS = dict(forward_attention=26, feed_forward=42, backward_attention=28, backward_conv=14)


def mm(lhs, rhs):
    return lax.dot_general(lhs, rhs, (((1,), (0,)), ((), ())), preferred_element_type=F32)


def mm_nt(lhs, rhs):
    return lax.dot_general(lhs, rhs, (((1,), (1,)), ((), ())), preferred_element_type=F32)


def tree_sum(items):
    items = list(items)
    while len(items) > 1:
        items = [a + b for a, b in zip(items[::2], items[1::2])]
    return items[0]


def pack_weights(qkv_ref, up_ref, down_ref, conv_ref, g1_ref, s1_ref, g2_ref, s2_ref, narrow_ref, ff_ref, rows_ref):
    own, ffs = up_ref.shape
    rows_ref[...] = jnp.zeros_like(rows_ref)
    rows_ref[0:3, :own] = conv_ref[...].astype(F32)
    for i, ref in enumerate((g1_ref, s1_ref, g2_ref, s2_ref)):
        rows_ref[3 + i : 4 + i, :own] = ref[...].astype(F32)
    wide = qkv_ref.shape[1]
    narrow_ref[:, :wide] = qkv_ref[...]
    narrow_ref[:, wide:] = rows_ref[...].T[:own].astype(BF)
    ff_ref[:own] = up_ref[...]
    ff_ref[own:] = down_ref[...]


def tiles(total, size):
    return [slice(at, at + size) for at in range(0, total, size)]


def twice(tile, lanes):
    return jnp.concatenate([tile] * (lanes // LANES), axis=1)


def load_columns(packed_ref, col_ref, places):
    for i, place in enumerate(places):
        column = packed_ref[:, place : place + 1].astype(F32)
        col_ref[i] = jnp.broadcast_to(column, (column.shape[0], LANES))


def column_mean(values):
    return jnp.sum(values, axis=0, keepdims=True) * (1.0 / values.shape[0])


def norm_columns(values):
    centred = values - column_mean(values)
    scale = lax.rsqrt(column_mean(centred * centred) + 1e-06)
    return centred * scale, scale


def fold(values):
    rows, lanes = values.shape
    return jnp.sum(values.reshape(rows // 8, 8, lanes), axis=0)


def fold_lanes(values):
    return sum(values[:, t] for t in tiles(values.shape[1], LANES))


def forward_attention(index_ref, len_ref, tok_ref, seg_ref, *refs, pieces):
    piece_refs = refs[:pieces]
    (
        x_ref, mc_ref, norm_ref, q_ref, k_ref, v_ref, e_ref, att_ref, inv_ref, aux_ref, packed_ref, w_ref,
        wt_ref, wide_ref, col_ref, bias_ref, key_ref, value_ref, score_ref,
    ) = refs[pieces:]
    rows, seq, width = tok_ref.shape
    head = width // HEADS
    step = pl.program_id(0)

    @pl.when(step == 0)
    def _():
        own = width // pieces
        for i, ref in enumerate(piece_refs):
            wide_ref[pl.ds(pl.multiple_of(index_ref[i] * own, 16), own), :] = ref[...]
        w_ref[...] = wide_ref[:, : 3 * width]
        wt_ref[:width] = (wide_ref[:, :width].astype(F32) * head ** (-0.5)).astype(BF).T
        wt_ref[width:] = wide_ref[:, width : 3 * width].T
        packed_ref[...] = wide_ref[:, 3 * width :]
        load_columns(packed_ref, col_ref, range(5))

    place = lax.broadcasted_iota(jnp.int32, (1, seq), 1)
    for r in range(rows):
        segs = seg_ref[pl.ds(step * rows + r, 1), :].astype(F32)
        valid = place < len_ref[step * rows + r]
        number = jnp.where(valid, segs, -1.0)
        links = jnp.where(valid & (place > 0) & (number == pltpu.roll(number, 1, 1)), 1.0, 0.0)
        next_links = jnp.where(place < seq - 1, pltpu.roll(links, seq - 1, 1), 0.0)
        none = jnp.zeros_like(links)
        aux = jnp.concatenate([links, next_links, number, none, none, none, none, none], axis=0)
        aux_ref[r] = aux
        key_number = aux.T[:, 2:3]
        for t in tiles(seq, 64):
            row_id = lax.broadcasted_iota(jnp.int32, (64, seq), 0) + t.start
            col_id = lax.broadcasted_iota(jnp.int32, (64, seq), 1)
            bias_ref[r, t] = jnp.where((key_number[t] == segs) | (row_id == col_id), 0.0, -1e30)
        x_ref[r] = tok_ref[r].T
        for t in tiles(width, 64):
            base = x_ref[r, t].astype(F32)
            before = pltpu.roll(base, 1, 1) * links
            after = pltpu.roll(base, seq - 1, 1) * next_links
            conv0, conv1, conv2 = [twice(col_ref[i, t], seq) for i in range(3)]
            mc_ref[r, t] = base + before * conv0 + base * conv1 + after * conv2
        for t in tiles(seq, LANES):
            n, _ = norm_columns(mc_ref[r, :, t])
            norm_ref[r, :, t] = (n * col_ref[3] + col_ref[4]).astype(BF)
    for r in range(rows):
        normed = norm_ref[r]
        q_ref[r] = mm(wt_ref[:width], normed).astype(BF)
        k_ref[r] = mm(wt_ref[width : 2 * width], normed).astype(BF)
        key_ref[r] = k_ref[r].T
        value_ref[r] = mm(wt_ref[2 * width :], normed).astype(BF)
        v_ref[r] = value_ref[r].T
    zero = jnp.zeros((head, seq), BF)

    def scores(r, h):
        own = q_ref[r, h * head : (h + 1) * head]
        pair = [own, zero] if h % 2 == 0 else [zero, own]
        lanes = slice(h // 2 * 2 * head, (h // 2 + 1) * 2 * head)
        score_ref[r, h] = mm(key_ref[r, :, lanes], jnp.concatenate(pair, axis=0))

    work = [(r, h) for r in range(rows) for h in range(HEADS)]
    scores(*work[0])
    for at, (r, h) in enumerate(work):
        if at + 1 < len(work):
            scores(*work[at + 1])
        for t in tiles(seq, LANES):
            masked = score_ref[r, h, :, t] + bias_ref[r, :, t]
            raised = jnp.exp(masked - jnp.max(masked, axis=0, keepdims=True))
            inv_ref[r, h : h + 1, t] = 1.0 / jnp.sum(raised, axis=0, keepdims=True)
            e_ref[r, h, :, t] = raised.astype(BF)
        part = slice(h * head, (h + 1) * head)
        att = mm(value_ref[r, part], e_ref[r, h]) * inv_ref[r, h : h + 1]
        att_ref[r, part] = att.astype(BF)


def gelu_parts(x):
    cdf = 0.5 * lax.erf(x * math.sqrt(0.5)) + 0.5
    bell = jnp.exp2(x * x * (-0.5 / math.log(2.0)) - 0.5 * math.log2(2.0 * math.pi))
    return x * cdf, cdf + x * bell


def feed_forward(index_ref, att_ref, mc_ref, ct_ref, packed_ref, *refs, pieces, shards):
    piece_refs = refs[:pieces]
    groups = 2 if pieces > 1 else 1
    lo_ref, gm_ref, ga_ref, gs_ref = refs[pieces : pieces + 4]
    gw_refs = refs[pieces + 4 : pieces + 4 + groups]
    (
        up_ref, down_ref, upt_ref, downt_ref, out_ref, outt_ref, up_acc, down_acc, out_acc, col_acc, col_ref,
        att_cat, mixed_ref, n_ref, norm_ref, ctt_ref, pre_ref, gh_ref, hidden_ref, gp_ref, gn_ref, scale_ref, lot_ref,
        branch_ref,
    ) = refs[pieces + 4 + groups :]
    rows, seq, width = ct_ref.shape
    ff = up_ref.shape[1]
    ffs = ff // shards
    own = width // pieces
    step = pl.program_id(0)

    @pl.when(step == 0)
    def _():
        for acc in (up_acc, down_acc, out_acc, col_acc):
            acc[...] = jnp.zeros_like(acc)
        for i, ref in enumerate(piece_refs):
            here = pl.ds(pl.multiple_of(index_ref[i] * own, 16), own)
            for j in range(shards):
                up_ref[here, j * ffs : (j + 1) * ffs] = ref[2 * j * own : (2 * j + 1) * own]
                down_ref[here, j * ffs : (j + 1) * ffs] = ref[(2 * j + 1) * own : (2 * j + 2) * own]
            out_ref[here, :] = ref[2 * shards * own :]
        upt_ref[...] = up_ref[...].T
        downt_ref[...] = down_ref[...].T
        outt_ref[...] = out_ref[...].T
        load_columns(packed_ref, col_ref, (5, 6))

    for r in range(rows):
        lanes = slice(r * seq, (r + 1) * seq)
        ctt_ref[:, lanes] = ct_ref[r].T
        att_cat[:, lanes] = att_ref[r]
        mixed_ref[:, lanes] = mc_ref[r] + mm(outt_ref[...], att_ref[r])
    for t in tiles(rows * seq, LANES):
        n, scale = norm_columns(mixed_ref[:, t])
        n_ref[:, t] = n
        scale_ref[0:1, t] = scale
        norm_ref[:, t] = (n * col_ref[0] + col_ref[1]).astype(BF)

    blocks = tiles(ff, 256)

    def opening(rows_of):
        pre_ref[rows_of] = mm(upt_ref[rows_of], norm_ref[...])
        gh_ref[rows_of] = mm(downt_ref[rows_of], ctt_ref[...])

    opening(blocks[0])
    for at, block in enumerate(blocks):
        if at + 1 < len(blocks):
            opening(blocks[at + 1])
        for low in range(block.start, block.stop, 16):
            t = slice(low, low + 16)
            hidden, slope = gelu_parts(pre_ref[t])
            hidden_ref[t] = hidden.astype(BF)
            gp_ref[t] = (gh_ref[t] * slope).astype(BF)
        down_acc[:, block] += mm_nt(ctt_ref[...], hidden_ref[block])
        up_acc[:, block] += mm_nt(norm_ref[...], gp_ref[block])
    gn_ref[...] = mm(up_ref[...], gp_ref[...])
    lot_ref[...] = (mixed_ref[...] + mm(down_ref[...], hidden_ref[...])).astype(BF)
    spots = tiles(rows * seq, LANES)
    mean_e = [jnp.zeros((8, LANES), F32) for _ in spots]
    mean_en = [jnp.zeros((8, LANES), F32) for _ in spots]
    for d in tiles(width, 32):
        column = col_ref[0, d]
        gain_sum, shift_sum = col_acc[0, d], col_acc[1, d]
        for i, t in enumerate(spots):
            grad_n = gn_ref[d, t]
            product = grad_n * n_ref[d, t]
            gain_sum += product
            shift_sum += grad_n
            mean_e[i] += fold(grad_n * column)
            mean_en[i] += fold(product * column)
        col_acc[0, d] = gain_sum
        col_acc[1, d] = shift_sum
    for i, t in enumerate(spots):
        me = jnp.sum(mean_e[i], axis=0, keepdims=True) * (1.0 / width)
        men = jnp.sum(mean_en[i], axis=0, keepdims=True) * (1.0 / width)
        scale = scale_ref[0:1, t]
        row, inside = divmod(t.start, seq)
        for d in tiles(width, 64):
            change = scale * (gn_ref[d, t] * col_ref[0, d] - me - n_ref[d, t] * men)
            grad_mixed = ctt_ref[d, t].astype(F32) + change
            gm_ref[row, d, inside : inside + LANES] = grad_mixed
            branch_ref[d, t] = grad_mixed.astype(BF)
    out_acc[...] += mm_nt(att_cat[...], branch_ref[...])
    for r in range(rows):
        lanes = slice(r * seq, (r + 1) * seq)
        ga_ref[r] = mm(out_ref[...], branch_ref[:, lanes]).astype(BF)
        lo_ref[r] = lot_ref[:, lanes].T

    @pl.when(step == pl.num_programs(0) - 1)
    def _():
        for i in range(pieces):
            here = pl.ds(pl.multiple_of(index_ref[i] * own, 16), own)
            place = gw_refs[i % groups]
            for j in range(shards):
                cols = slice(j * ffs, (j + 1) * ffs)
                place[i // groups, :, 2 * j * ffs : (2 * j + 1) * ffs] = up_acc[here, cols].astype(BF)
                place[i // groups, :, (2 * j + 1) * ffs : (2 * j + 2) * ffs] = down_acc[here, cols].astype(BF)
            place[i // groups, :, 2 * ff :] = out_acc[here, :].astype(BF)
        gs_ref[...] = jnp.zeros_like(gs_ref)
        for i in range(2):
            gs_ref[5 + i : 6 + i] = jnp.sum(col_acc[i].T, axis=0, keepdims=True)


def backward_attention(
    q_ref, k_ref, v_ref, e_ref, att_ref, inv_ref, norm_ref, ga_ref, index_ref, w_ref, start_ref, gn_ref, *refs, pieces
):
    gw_refs = refs[:-5]
    proj_ref, w_acc, norm_cat, soft_ref, logit_ref = refs[-5:]
    rows, seq, width = v_ref.shape
    own = width // pieces
    head = width // HEADS
    step = pl.program_id(0)

    @pl.when(step == 0)
    def _():
        w_acc[...] = jnp.zeros_like(w_acc) if start_ref is None else start_ref[...]

    zero = jnp.zeros((head, seq), BF)
    work = [(r, h) for r in range(rows) for h in range(HEADS)]

    def opening(r, h):
        part = slice(h * head, (h + 1) * head)
        lanes = slice(h // 2 * 2 * head, (h // 2 + 1) * 2 * head)
        grad_att = ga_ref[r, part].astype(F32) * inv_ref[r, h : h + 1]
        inner = jnp.sum(grad_att * att_ref[r, part].astype(F32), axis=0, keepdims=True)
        grad_att = grad_att.astype(BF)
        pair = [grad_att, zero] if h % 2 == 0 else [zero, grad_att]
        soft_ref[r, h] = mm(v_ref[r, :, lanes], jnp.concatenate(pair, axis=0))
        return grad_att, inner

    ready = opening(*work[0])
    for at, (r, h) in enumerate(work):
        grad_att, inner = ready
        if at + 1 < len(work):
            ready = opening(*work[at + 1])
        for t in tiles(seq, 32):
            raised = e_ref[r, h, t].astype(F32)
            logit_ref[r, h, t] = (raised * (soft_ref[r, h, t] - inner)).astype(BF)
        part = slice(h * head, (h + 1) * head)
        place = slice(r * seq, (r + 1) * seq)
        grad_logits = logit_ref[r, h]
        grad_q = mm(k_ref[r, part], grad_logits) * head ** (-0.5)
        proj_ref[h * head : (h + 1) * head, place] = grad_q.astype(BF)
        grad_k = mm_nt(q_ref[r, part], grad_logits)
        proj_ref[width + h * head : width + (h + 1) * head, place] = grad_k.astype(BF)
        grad_v = mm_nt(grad_att, e_ref[r, h])
        proj_ref[2 * width + h * head : 2 * width + (h + 1) * head, place] = grad_v.astype(BF)
    for r in range(rows):
        norm_cat[:, r * seq : (r + 1) * seq] = norm_ref[r]
        gn_ref[r] = mm(w_ref[...], proj_ref[:, r * seq : (r + 1) * seq]).astype(BF)
    w_acc[...] += mm_nt(norm_cat[...], proj_ref[...])

    @pl.when(step == pl.num_programs(0) - 1)
    def _():
        if start_ref is None:
            gw_refs[0][...] = w_acc[...]
        else:
            groups = len(gw_refs)
            for i in range(pieces):
                here = pl.ds(pl.multiple_of(index_ref[i] * own, 16), own)
                gw_refs[i % groups][i // groups] = w_acc[here, :].astype(BF)


def backward_conv(
    x_ref, aux_ref, mc_ref, gm_ref, gn_ref, packed_ref, other_ref, part_ref, ig_ref, gs_ref,
    acc_ref, col_ref, n_ref, g_ref, turn_ref,
):
    rows, width, seq = x_ref.shape
    step = pl.program_id(0)

    @pl.when(step == 0)
    def _():
        acc_ref[...] = jnp.zeros_like(acc_ref)
        load_columns(packed_ref, col_ref, range(4))

    spots = tiles(seq, LANES)
    for r in range(rows):
        scales = []
        for t in spots:
            n, scale = norm_columns(mc_ref[r, :, t])
            n_ref[r, :, t] = n
            scales.append(scale)
        mean_e = [jnp.zeros((8, LANES), F32) for _ in spots]
        mean_en = [jnp.zeros((8, LANES), F32) for _ in spots]
        for d in tiles(width, 32):
            column = col_ref[3, d]
            gain_sum, shift_sum = acc_ref[3, d], acc_ref[4, d]
            for i, t in enumerate(spots):
                grad_n = gn_ref[r, d, t].astype(F32)
                product = grad_n * n_ref[r, d, t]
                gain_sum += product
                shift_sum += grad_n
                mean_e[i] += fold(grad_n * column)
                mean_en[i] += fold(product * column)
            acc_ref[3, d] = gain_sum
            acc_ref[4, d] = shift_sum
        for i, t in enumerate(spots):
            me = jnp.sum(mean_e[i], axis=0, keepdims=True) * (1.0 / width)
            men = jnp.sum(mean_en[i], axis=0, keepdims=True) * (1.0 / width)
            for d in tiles(width, 64):
                e = gn_ref[r, d, t].astype(F32) * col_ref[3, d]
                g_ref[r, d, t] = gm_ref[r, d, t] + scales[i] * (e - me - n_ref[r, d, t] * men)
        links, next_links = aux_ref[r, 0:1], aux_ref[r, 1:2]
        for d in tiles(width, 32):
            g = g_ref[r, d]
            base = x_ref[r, d].astype(F32)
            before = pltpu.roll(g, 1, 1) * links
            after = pltpu.roll(g, seq - 1, 1) * next_links
            acc_ref[0, d] += fold_lanes(base * after)
            acc_ref[1, d] += fold_lanes(base * g)
            acc_ref[2, d] += fold_lanes(base * before)
            conv0, conv1, conv2 = [twice(col_ref[i, d], seq) for i in range(3)]
            turn_ref[r, d] = (g + conv1 * g + conv0 * after + conv2 * before).astype(BF)
        ig_ref[r] = turn_ref[r].T

    @pl.when(step == pl.num_programs(0) - 1)
    def _():
        gs_ref[...] = other_ref[...]
        for i in range(5):
            gs_ref[i : i + 1] += jnp.sum(acc_ref[i].T, axis=0, keepdims=True)


def by_row(shape, rows, first=0):
    tail = tuple(shape[1:])
    return pl.BlockSpec((rows,) + tail, lambda i, *_: (i + first,) + (0,) * len(tail))


def whole(shape):
    place = (0,) * len(shape)
    return pl.BlockSpec(tuple(shape), lambda i, *_: place)


def step_rows(count, most):
    return max(r for r in range(1, most + 1) if count % r == 0)


def call(body, name, scalars, rows, row_args, args, row_outs, outs, scratch, span=None, into=None):
    first, count = span or (0, row_args[0].shape[0])
    skip = first // rows
    in_specs = [by_row(a.shape, rows, skip if a.shape[0] > count else 0) for a in row_args]
    in_specs += [whole(a.shape) for a in args]
    aliases = {}
    if into is not None:
        in_specs.append(pl.BlockSpec(memory_space=pl.ANY))
        aliases = {len(scalars) + len(in_specs) - 1: 0}
    spec = pltpu.PrefetchScalarGridSpec(
        num_scalar_prefetch=len(scalars),
        grid=(count // rows,),
        in_specs=in_specs,
        out_specs=[by_row(s, rows, skip if s[0] > count else 0) for s, _ in row_outs] + [whole(s) for s, _ in outs],
        scratch_shapes=[pltpu.VMEM(s, t) for s, t in scratch],
    )
    return pl.pallas_call(
        body,
        grid_spec=spec,
        out_shape=[jax.ShapeDtypeStruct(s, t) for s, t in row_outs + outs],
        input_output_aliases=aliases,
        compiler_params=pltpu.CompilerParams(dimension_semantics=("arbitrary",), vmem_limit_bytes=VMEM_LIMITS[name] * MIB),
        name=name,
    )(*scalars, *row_args, *args, *(() if into is None else (into,)))


def small_call(body, name, args, outs, scratch=()):
    return pl.pallas_call(
        body,
        out_shape=[jax.ShapeDtypeStruct(s, t) for s, t in outs],
        scratch_shapes=[pltpu.VMEM(s, t) for s, t in scratch],
        compiler_params=pltpu.CompilerParams(vmem_limit_bytes=16 * MIB),
        name=name,
    )(*args)


def run_forward(index, tokens, segment_ids, valid_len, pieces):
    count, seq, width = tokens.shape
    flipped = (count, width, seq)
    rows = step_rows(count, 2)
    row_outs = [
        (flipped, BF), (flipped, F32), (flipped, BF), (flipped, BF), (flipped, BF), ((count, seq, width), BF),
        ((count, HEADS, seq, seq), BF), (flipped, BF), ((count, 8, seq), F32), ((count, 8, seq), F32),
    ]
    return call(
        functools.partial(forward_attention, pieces=len(pieces)), "forward_attention", (index, valid_len),
        rows, (tokens,), (segment_ids, *pieces),
        row_outs, [((width, VECTORS), BF), ((width, 3 * width), BF)],
        [
            ((3 * width, width), BF), ((width, 3 * width + VECTORS), BF), ((5, width, LANES), F32),
            ((rows, seq, seq), F32), ((rows, seq, width), BF), ((rows, width, seq), BF), ((rows, HEADS, seq, seq), F32),
        ],
    )


def run_feed_forward(index, att, mixed, cotangent, packed, pieces, shards):
    count, seq, width = cotangent.shape
    own = width // len(pieces)
    ff = shards * width
    groups = 2 if len(pieces) > 1 else 1
    rows = step_rows(count, 2)
    wide = rows * seq
    row_outs = [((count, seq, width), BF), ((count, width, seq), F32), ((count, width, seq), BF)]
    grads = ((len(pieces) // groups, own, 2 * ff + width), BF)
    return call(
        functools.partial(feed_forward, pieces=len(pieces), shards=shards), "feed_forward", (index,),
        rows, (att, mixed, cotangent), (packed, *pieces),
        row_outs, [((8, width), F32)] + [grads] * groups,
        [((width, ff), BF)] * 2 + [((ff, width), BF)] * 2 + [((width, width), BF)] * 2
        + [((width, ff), F32)] * 2 + [((width, width), F32), ((2, width, LANES), F32), ((2, width, LANES), F32)]
        + [((width, wide), BF), ((width, wide), F32), ((width, wide), F32), ((width, wide), BF), ((width, wide), BF)]
        + [((ff, wide), F32)] * 2 + [((ff, wide), BF)] * 2
        + [((width, wide), F32), ((8, wide), F32), ((width, wide), BF), ((width, wide), BF)],
    )


def run_backward_attention(index, weight, kept, grad_att, pieces, span, start):
    count, seq, width = kept[2].shape
    own = width // pieces
    groups = 2 if pieces > 1 else 1
    rows = step_rows(span[1], 2)
    row_args = (*kept, grad_att)
    many = len(row_args)

    def body(index_ref, *refs):
        w_ref, rest = refs[many], refs[many + 1 :]
        start_ref, rest = (None, rest) if start is None else (rest[0], rest[1:])
        backward_attention(*refs[:many], index_ref, w_ref, start_ref, *rest, pieces=pieces)

    outs = [((width, 3 * width), F32)] if start is None else [((pieces // groups, own, 3 * width), BF)] * groups
    return call(
        body, "backward_attention", (index,), rows, row_args, (weight,) if start is None else (weight, start),
        [((span[1], width, seq), BF)], outs,
        [
            ((3 * width, rows * seq), BF), ((width, 3 * width), F32), ((width, rows * seq), BF),
            ((rows, HEADS, seq, seq), F32), ((rows, HEADS, seq, seq), BF),
        ],
        span=span,
    )


def run_backward_conv(x, aux, mixed, grad_mixed, grad_normed, packed, other, span, into):
    count, width, seq = x.shape
    rows = step_rows(span[1], 2)

    def body(*refs):
        if into is None:
            backward_conv(*refs[:7], None, *refs[7:])
        else:
            backward_conv(*refs)

    return call(
        body, "backward_conv", (), rows,
        (x, aux, mixed, grad_mixed, grad_normed), (packed, other),
        [((count, seq, width), BF)], [((8, width), F32)],
        [
            ((5, width, LANES), F32), ((4, width, LANES), F32), ((rows, width, seq), F32), ((rows, width, seq), F32),
            ((rows, width, seq), BF),
        ],
        span=span, into=into,
    )


def halves(count):
    early = count // 3
    return ((0, early), (early, count - early)) if early % 2 == 0 and early else ((0, count // 2), (count // 2, count - count // 2))


def exchange(values, axis, offset):
    size = lax.axis_size(axis)
    return lax.ppermute(values, axis, [(i, i ^ offset) for i in range(size)])


def add_halves(mine, received):
    count, own, cols = mine.shape

    def body(mine_ref, received_ref, *out_refs):
        for i, ref in enumerate(out_refs):
            ref[...] = (mine_ref[i].astype(F32) + received_ref[i].astype(F32)).astype(BF)

    return small_call(body, "add_halves", (mine, received), [((own, cols), BF)] * count)


def add_wide(*items):
    return tree_sum(item.astype(F32) for item in items)


def add_shard_vectors(items, own):
    def body(*refs):
        total = tree_sum(ref[...] for ref in refs[:-5])
        refs[-5][...] = total[0:3, :own]
        for i in range(4):
            refs[i - 4][...] = total[3 + i : 4 + i, :own]

    return small_call(body, "add_shard_vectors", items, [((3, own), F32)] + [((1, own), F32)] * 4)


def direct_plan(tokens, segment_ids, valid_len, qkv_weight, out_weight, up_weight, down_weight, conv_weight, vectors, cotangent):
    count, seq, width = tokens.shape
    own, ffs = up_weight.shape
    dp, mp = lax.axis_size("dp"), lax.axis_size("mp")
    me = lax.axis_index("dp")
    offsets = [2 * p for p in range(dp // 2)]
    index = jnp.stack([me ^ (p ^ c) for p in offsets for c in range(2)]).astype(jnp.int32)
    narrow, ff_own = small_call(
        pack_weights, "pack_weights",
        (qkv_weight, up_weight, down_weight, conv_weight, *[v.reshape(1, own) for v in vectors]),
        [((own, 3 * width + VECTORS), BF), ((2 * own, ffs), BF)], [((VECTORS, VECTORS), F32)],
    )
    plane = [narrow] + [exchange(narrow, "dp", p) for p in offsets[1:]]
    shards = [ff_own] + [exchange(ff_own, "mp", j) for j in range(1, mp)]
    pieces = [piece for a in plane for piece in (a, exchange(a, "dp", 1))]
    column = jnp.concatenate(shards + [out_weight], axis=0)
    columns = [column] + [exchange(column, "dp", p) for p in offsets[1:]]
    x, mixed, normed, q, k, v, raised, att, inverse, aux, packed, weight = run_forward(
        index, tokens, segment_ids, valid_len, pieces
    )
    columns, att = lax.optimization_barrier((columns, att))
    pieces = [piece for a in columns for piece in (a, exchange(a, "dp", 1))]
    layer_out, grad_mixed, grad_att, sums2, mine, theirs = run_feed_forward(
        index, att, mixed, cotangent, packed, pieces, mp
    )
    received = exchange(theirs, "dp", 1)
    early, late = halves(count)
    kept = (q, k, v, raised, att, inverse, normed)
    grad_normed1, start = run_backward_attention(index, weight, kept, grad_att, dp, early, None)
    received, start = lax.optimization_barrier((received, start))
    parts = list(add_halves(mine, received))
    parts[0], start = lax.optimization_barrier((parts[0], start))
    plane = [parts[0]] + [exchange(parts[i], "dp", p) for i, p in enumerate(offsets) if i]
    grad_normed2, mine_a, theirs_a = run_backward_attention(index, weight, kept, grad_att, dp, late, start)
    plane, theirs_a = lax.optimization_barrier((plane, theirs_a))
    received_a = exchange(theirs_a, "dp", 1)
    total = add_wide(*plane).astype(BF)
    half = 2 * ffs * (mp // 2)
    near, far, out_part = total[:, :half], total[:, half:], total[:, 2 * half :]
    received_f = exchange(far, "mp", 2)
    near, grad_normed1 = lax.optimization_barrier((near, grad_normed1))
    some_grad, sums = run_backward_conv(x, aux, mixed, grad_mixed, grad_normed1, packed, sums2, early, None)
    received_a, sums = lax.optimization_barrier((received_a, sums))
    parts = list(add_halves(mine_a, received_a))
    parts[0], sums = lax.optimization_barrier((parts[0], sums))
    plane_a = [parts[0]] + [exchange(parts[i], "dp", p) for i, p in enumerate(offsets) if i]
    input_grad, sums = run_backward_conv(x, aux, mixed, grad_mixed, grad_normed2, packed, sums, late, some_grad)
    received_s = exchange(sums, "dp", 1)
    plane_a, received_f, sums = lax.optimization_barrier((plane_a, received_f, sums))
    total = add_wide(*plane_a).astype(BF)
    received_s, total = lax.optimization_barrier((received_s, total))
    received_1 = exchange(total, "mp", 2)
    sums = sums + received_s
    plane_s = [sums] + [exchange(sums, "dp", p) for p in offsets[1:]]
    near_sum = add_wide(near, received_f[:, :half])
    out_sum = lax.optimization_barrier(add_wide(out_part, received_f[:, half:]).astype(BF))
    keep = near_sum[:, : 2 * ffs]
    send = jnp.concatenate([near_sum[:, 2 * ffs :].astype(BF), out_sum], axis=1)
    received_n = exchange(send, "mp", 1)
    plane_s, received_1 = lax.optimization_barrier((plane_s, received_1))
    total = lax.optimization_barrier(add_wide(total, received_1).astype(BF))
    received_2 = exchange(total, "mp", 1)
    vectors = lax.dynamic_slice_in_dim(tree_sum(plane_s), me * own, own, axis=1)
    shards = [vectors] + [exchange(vectors, "mp", j) for j in range(1, mp)]
    grad_up = keep[:, :ffs] + received_n[:, :ffs].astype(F32)
    grad_down = keep[:, ffs:] + received_n[:, ffs : 2 * ffs].astype(F32)
    grad_out = add_wide(out_sum, received_n[:, 2 * ffs :])
    grad_qkv = add_wide(total, received_2)
    grad_conv, *grads = add_shard_vectors(shards, own)
    return (layer_out, input_grad, grad_qkv, grad_out, grad_up, grad_down, grad_conv, *[g.reshape(own) for g in grads])


def gathered_plan(tokens, segment_ids, valid_len, qkv_weight, out_weight, up_weight, down_weight, conv_weight, vectors, cotangent):
    count, seq, width = tokens.shape
    own = qkv_weight.shape[0]
    dp = width // own
    columns = jnp.stack([conv_weight[0], conv_weight[1], conv_weight[2], *vectors], axis=1)
    narrow = jnp.concatenate([qkv_weight, jnp.pad(columns, ((0, 0), (0, VECTORS - 7))), out_weight], axis=1)
    wide = lax.all_gather(narrow, "dp", axis=0, tiled=True)
    both = lax.all_gather(jnp.concatenate([up_weight, down_weight], axis=0), "mp", axis=1, tiled=True)
    ff = both.shape[1]
    shards = ff // width
    both = lax.all_gather(both, "dp", axis=0).reshape(dp, 2, own, shards, width)
    both = both.transpose(3, 1, 0, 2, 4).reshape(2 * ff, width)
    column = jnp.concatenate([both, wide[:, 3 * width + VECTORS :]], axis=0)
    index = jnp.zeros((1,), jnp.int32)
    x, mixed, normed, q, k, v, raised, att, inverse, aux, packed, weight = run_forward(
        index, tokens, segment_ids, valid_len, [wide[:, : 3 * width + VECTORS]]
    )
    layer_out, grad_mixed, grad_att, sums2, grads = run_feed_forward(
        index, att, mixed, cotangent, packed, [column], shards
    )
    early, late = halves(count)
    kept = (q, k, v, raised, att, inverse, normed)
    grad_normed1, start = run_backward_attention(index, weight, kept, grad_att, 1, early, None)
    grad_normed2, grad_qkv = run_backward_attention(index, weight, kept, grad_att, 1, late, start)
    some_grad, sums = run_backward_conv(x, aux, mixed, grad_mixed, grad_normed1, packed, sums2, early, None)
    input_grad, sums = run_backward_conv(x, aux, mixed, grad_mixed, grad_normed2, packed, sums, late, some_grad)
    grad_ff = grads[0, :, : 2 * ff].reshape(width, shards, 2, width).transpose(0, 2, 1, 3).reshape(width, 2 * ff)
    grad_ff = lax.psum_scatter(grad_ff, "dp", scatter_dimension=0, tiled=True).reshape(own, 2, ff)
    grad_ff = lax.psum_scatter(grad_ff, "mp", scatter_dimension=2, tiled=True).astype(F32)
    grad_attn = jnp.concatenate([grad_qkv[0], grads[0, :, 2 * ff :]], axis=1)
    grad_attn = lax.psum_scatter(grad_attn, "dp", scatter_dimension=0, tiled=True)
    grad_attn = lax.psum(grad_attn, "mp").astype(F32)
    sums = lax.psum(sums, ("dp", "mp"))
    sums = lax.dynamic_slice_in_dim(sums, lax.axis_index("dp") * own, own, axis=1)
    return (
        layer_out, input_grad, grad_attn[:, : 3 * width], grad_attn[:, 3 * width :],
        grad_ff[:, 0], grad_ff[:, 1], sums[0:3], sums[3], sums[4], sums[5], sums[6],
    )


def on_device(
    tokens, segment_ids, valid_len, qkv_weight, out_weight, up_weight, down_weight, conv_weight,
    ln1_gain, ln1_shift, ln2_gain, ln2_shift, cotangent,
):
    own, ffs = up_weight.shape
    direct = own % 16 == 0 and ffs == tokens.shape[2] and own <= VECTORS and lax.axis_size("mp") == 4
    plan = direct_plan if direct else gathered_plan
    return plan(
        tokens, segment_ids, valid_len, qkv_weight, out_weight, up_weight, down_weight, conv_weight,
        (ln1_gain, ln1_shift, ln2_gain, ln2_shift), cotangent,
    )


def solution(mesh):
    rows = P(("dp", "mp"), None, None)
    weights = (P("dp", None), P("dp", None), P("dp", "mp"), P("dp", "mp"), P(None, "dp"))
    vectors = (P("dp"),) * 4
    return jax.shard_map(
        on_device,
        mesh=mesh,
        in_specs=(rows, P(("dp", "mp"), None), P(("dp", "mp"))) + weights + vectors + (rows,),
        out_specs=(rows, rows) + weights + vectors,
        check_vma=False,
    )
```

```python
import functools
import math

import jax
import jax.numpy as jnp
from jax import lax
from jax.experimental import pallas as pl
from jax.experimental.pallas import tpu as pltpu
from jax.sharding import PartitionSpec as P

HEADS = 6
VECTORS = 128
LANES = 128
BF = jnp.bfloat16
F32 = jnp.float32
MIB = 1024 * 1024
VMEM_LIMITS = dict(forward_attention=26, feed_forward=42, backward_attention=28, backward_conv=14)


def mm(lhs, rhs):
    return lax.dot_general(lhs, rhs, (((1,), (0,)), ((), ())), preferred_element_type=F32)


def mm_nt(lhs, rhs):
    return lax.dot_general(lhs, rhs, (((1,), (1,)), ((), ())), preferred_element_type=F32)


def tree_sum(items):
    items = list(items)
    while len(items) > 1:
        items = [a + b for a, b in zip(items[::2], items[1::2])]
    return items[0]


def pack_weights(qkv_ref, up_ref, down_ref, conv_ref, g1_ref, s1_ref, g2_ref, s2_ref, narrow_ref, ff_ref, rows_ref):
    own, ffs = up_ref.shape
    rows_ref[...] = jnp.zeros_like(rows_ref)
    rows_ref[0:3, :own] = conv_ref[...].astype(F32)
    for i, ref in enumerate((g1_ref, s1_ref, g2_ref, s2_ref)):
        rows_ref[3 + i : 4 + i, :own] = ref[...].astype(F32)
    wide = qkv_ref.shape[1]
    narrow_ref[:, :wide] = qkv_ref[...]
    narrow_ref[:, wide:] = rows_ref[...].T[:own].astype(BF)
    ff_ref[:own] = up_ref[...]
    ff_ref[own:] = down_ref[...]


def tiles(total, size):
    return [slice(at, at + size) for at in range(0, total, size)]


def twice(tile, lanes):
    return jnp.concatenate([tile] * (lanes // LANES), axis=1)


def load_columns(packed_ref, col_ref, places):
    for i, place in enumerate(places):
        column = packed_ref[:, place : place + 1].astype(F32)
        col_ref[i] = jnp.broadcast_to(column, (column.shape[0], LANES))


def column_mean(values):
    return jnp.sum(values, axis=0, keepdims=True) * (1.0 / values.shape[0])


def norm_columns(values):
    centred = values - column_mean(values)
    scale = lax.rsqrt(column_mean(centred * centred) + 1e-06)
    return centred * scale, scale


def fold(values):
    rows, lanes = values.shape
    return jnp.sum(values.reshape(rows // 8, 8, lanes), axis=0)


def fold_lanes(values):
    return sum(values[:, t] for t in tiles(values.shape[1], LANES))


def forward_attention(index_ref, len_ref, tok_ref, seg_ref, *refs, pieces):
    piece_refs = refs[:pieces]
    (
        x_ref, mc_ref, norm_ref, q_ref, k_ref, v_ref, e_ref, att_ref, inv_ref, aux_ref, packed_ref, w_ref,
        wt_ref, wide_ref, col_ref, bias_ref, key_ref, value_ref, score_ref,
    ) = refs[pieces:]
    rows, seq, width = tok_ref.shape
    head = width // HEADS
    step = pl.program_id(0)

    @pl.when(step == 0)
    def _():
        own = width // pieces
        for i, ref in enumerate(piece_refs):
            wide_ref[pl.ds(pl.multiple_of(index_ref[i] * own, 16), own), :] = ref[...]
        w_ref[...] = wide_ref[:, : 3 * width]
        wt_ref[:width] = (wide_ref[:, :width].astype(F32) * head ** (-0.5)).astype(BF).T
        wt_ref[width:] = wide_ref[:, width : 3 * width].T
        packed_ref[...] = wide_ref[:, 3 * width :]
        load_columns(packed_ref, col_ref, range(5))

    place = lax.broadcasted_iota(jnp.int32, (1, seq), 1)
    for r in range(rows):
        segs = seg_ref[pl.ds(step * rows + r, 1), :].astype(F32)
        valid = place < len_ref[step * rows + r]
        number = jnp.where(valid, segs, -1.0)
        links = jnp.where(valid & (place > 0) & (number == pltpu.roll(number, 1, 1)), 1.0, 0.0)
        next_links = jnp.where(place < seq - 1, pltpu.roll(links, seq - 1, 1), 0.0)
        none = jnp.zeros_like(links)
        aux = jnp.concatenate([links, next_links, number, none, none, none, none, none], axis=0)
        aux_ref[r] = aux
        key_number = aux.T[:, 2:3]
        for t in tiles(seq, 64):
            row_id = lax.broadcasted_iota(jnp.int32, (64, seq), 0) + t.start
            col_id = lax.broadcasted_iota(jnp.int32, (64, seq), 1)
            bias_ref[r, t] = jnp.where((key_number[t] == segs) | (row_id == col_id), 0.0, -1e30)
        x_ref[r] = tok_ref[r].T
        for t in tiles(width, 64):
            base = x_ref[r, t].astype(F32)
            before = pltpu.roll(base, 1, 1) * links
            after = pltpu.roll(base, seq - 1, 1) * next_links
            conv0, conv1, conv2 = [twice(col_ref[i, t], seq) for i in range(3)]
            mc_ref[r, t] = base + before * conv0 + base * conv1 + after * conv2
        for t in tiles(seq, LANES):
            n, _ = norm_columns(mc_ref[r, :, t])
            norm_ref[r, :, t] = (n * col_ref[3] + col_ref[4]).astype(BF)
    for r in range(rows):
        normed = norm_ref[r]
        q_ref[r] = mm(wt_ref[:width], normed).astype(BF)
        k_ref[r] = mm(wt_ref[width : 2 * width], normed).astype(BF)
        key_ref[r] = k_ref[r].T
        value_ref[r] = mm(wt_ref[2 * width :], normed).astype(BF)
        v_ref[r] = value_ref[r].T
    zero = jnp.zeros((head, seq), BF)

    def scores(r, h):
        own = q_ref[r, h * head : (h + 1) * head]
        pair = [own, zero] if h % 2 == 0 else [zero, own]
        lanes = slice(h // 2 * 2 * head, (h // 2 + 1) * 2 * head)
        score_ref[r, h] = mm(key_ref[r, :, lanes], jnp.concatenate(pair, axis=0))

    work = [(r, h) for r in range(rows) for h in range(HEADS)]
    scores(*work[0])
    for at, (r, h) in enumerate(work):
        if at + 1 < len(work):
            scores(*work[at + 1])
        for t in tiles(seq, LANES):
            masked = score_ref[r, h, :, t] + bias_ref[r, :, t]
            raised = jnp.exp(masked - jnp.max(masked, axis=0, keepdims=True))
            inv_ref[r, h : h + 1, t] = 1.0 / jnp.sum(raised, axis=0, keepdims=True)
            e_ref[r, h, :, t] = raised.astype(BF)
        part = slice(h * head, (h + 1) * head)
        att = mm(value_ref[r, part], e_ref[r, h]) * inv_ref[r, h : h + 1]
        att_ref[r, part] = att.astype(BF)


def gelu_parts(x):
    cdf = 0.5 * lax.erf(x * math.sqrt(0.5)) + 0.5
    bell = jnp.exp2(x * x * (-0.5 / math.log(2.0)) - 0.5 * math.log2(2.0 * math.pi))
    return x * cdf, cdf + x * bell


def feed_forward(index_ref, att_ref, mc_ref, ct_ref, packed_ref, *refs, pieces, shards):
    piece_refs = refs[:pieces]
    groups = 2 if pieces > 1 else 1
    lo_ref, gm_ref, ga_ref, gs_ref = refs[pieces : pieces + 4]
    gw_refs = refs[pieces + 4 : pieces + 4 + groups]
    (
        up_ref, down_ref, upt_ref, downt_ref, out_ref, outt_ref, up_acc, down_acc, out_acc, col_acc, col_ref,
        att_cat, mixed_ref, n_ref, norm_ref, ctt_ref, pre_ref, gh_ref, hidden_ref, gp_ref, gn_ref, scale_ref, lot_ref,
        branch_ref,
    ) = refs[pieces + 4 + groups :]
    rows, seq, width = ct_ref.shape
    ff = up_ref.shape[1]
    ffs = ff // shards
    own = width // pieces
    step = pl.program_id(0)

    @pl.when(step == 0)
    def _():
        for acc in (up_acc, down_acc, out_acc, col_acc):
            acc[...] = jnp.zeros_like(acc)
        for i, ref in enumerate(piece_refs):
            here = pl.ds(pl.multiple_of(index_ref[i] * own, 16), own)
            for j in range(shards):
                up_ref[here, j * ffs : (j + 1) * ffs] = ref[2 * j * own : (2 * j + 1) * own]
                down_ref[here, j * ffs : (j + 1) * ffs] = ref[(2 * j + 1) * own : (2 * j + 2) * own]
            out_ref[here, :] = ref[2 * shards * own :]
        upt_ref[...] = up_ref[...].T
        downt_ref[...] = down_ref[...].T
        outt_ref[...] = out_ref[...].T
        load_columns(packed_ref, col_ref, (5, 6))

    for r in range(rows):
        lanes = slice(r * seq, (r + 1) * seq)
        ctt_ref[:, lanes] = ct_ref[r].T
        att_cat[:, lanes] = att_ref[r]
        mixed_ref[:, lanes] = mc_ref[r] + mm(outt_ref[...], att_ref[r])
    for t in tiles(rows * seq, LANES):
        n, scale = norm_columns(mixed_ref[:, t])
        n_ref[:, t] = n
        scale_ref[0:1, t] = scale
        norm_ref[:, t] = (n * col_ref[0] + col_ref[1]).astype(BF)

    blocks = tiles(ff, 256)

    def opening(rows_of):
        pre_ref[rows_of] = mm(upt_ref[rows_of], norm_ref[...])
        gh_ref[rows_of] = mm(downt_ref[rows_of], ctt_ref[...])

    opening(blocks[0])
    for at, block in enumerate(blocks):
        if at + 1 < len(blocks):
            opening(blocks[at + 1])
        for low in range(block.start, block.stop, 16):
            t = slice(low, low + 16)
            hidden, slope = gelu_parts(pre_ref[t])
            hidden_ref[t] = hidden.astype(BF)
            gp_ref[t] = (gh_ref[t] * slope).astype(BF)
        down_acc[:, block] += mm_nt(ctt_ref[...], hidden_ref[block])
        up_acc[:, block] += mm_nt(norm_ref[...], gp_ref[block])
    gn_ref[...] = mm(up_ref[...], gp_ref[...])
    lot_ref[...] = (mixed_ref[...] + mm(down_ref[...], hidden_ref[...])).astype(BF)
    spots = tiles(rows * seq, LANES)
    mean_e = [jnp.zeros((8, LANES), F32) for _ in spots]
    mean_en = [jnp.zeros((8, LANES), F32) for _ in spots]
    for d in tiles(width, 32):
        column = col_ref[0, d]
        gain_sum, shift_sum = col_acc[0, d], col_acc[1, d]
        for i, t in enumerate(spots):
            grad_n = gn_ref[d, t]
            product = grad_n * n_ref[d, t]
            gain_sum += product
            shift_sum += grad_n
            mean_e[i] += fold(grad_n * column)
            mean_en[i] += fold(product * column)
        col_acc[0, d] = gain_sum
        col_acc[1, d] = shift_sum
    for i, t in enumerate(spots):
        me = jnp.sum(mean_e[i], axis=0, keepdims=True) * (1.0 / width)
        men = jnp.sum(mean_en[i], axis=0, keepdims=True) * (1.0 / width)
        scale = scale_ref[0:1, t]
        row, inside = divmod(t.start, seq)
        for d in tiles(width, 64):
            change = scale * (gn_ref[d, t] * col_ref[0, d] - me - n_ref[d, t] * men)
            grad_mixed = ctt_ref[d, t].astype(F32) + change
            gm_ref[row, d, inside : inside + LANES] = grad_mixed
            branch_ref[d, t] = grad_mixed.astype(BF)
    out_acc[...] += mm_nt(att_cat[...], branch_ref[...])
    for r in range(rows):
        lanes = slice(r * seq, (r + 1) * seq)
        ga_ref[r] = mm(out_ref[...], branch_ref[:, lanes]).astype(BF)
        lo_ref[r] = lot_ref[:, lanes].T

    @pl.when(step == pl.num_programs(0) - 1)
    def _():
        for i in range(pieces):
            here = pl.ds(pl.multiple_of(index_ref[i] * own, 16), own)
            place = gw_refs[i % groups]
            for j in range(shards):
                cols = slice(j * ffs, (j + 1) * ffs)
                place[i // groups, :, 2 * j * ffs : (2 * j + 1) * ffs] = up_acc[here, cols].astype(BF)
                place[i // groups, :, (2 * j + 1) * ffs : (2 * j + 2) * ffs] = down_acc[here, cols].astype(BF)
            place[i // groups, :, 2 * ff :] = out_acc[here, :].astype(BF)
        gs_ref[...] = jnp.zeros_like(gs_ref)
        for i in range(2):
            gs_ref[5 + i : 6 + i] = jnp.sum(col_acc[i].T, axis=0, keepdims=True)


def backward_attention(
    q_ref, k_ref, v_ref, e_ref, att_ref, inv_ref, norm_ref, ga_ref, index_ref, w_ref, start_ref, gn_ref, *refs, pieces
):
    gw_refs = refs[:-5]
    proj_ref, w_acc, norm_cat, soft_ref, logit_ref = refs[-5:]
    rows, seq, width = v_ref.shape
    own = width // pieces
    head = width // HEADS
    step = pl.program_id(0)

    @pl.when(step == 0)
    def _():
        w_acc[...] = jnp.zeros_like(w_acc) if start_ref is None else start_ref[...]

    zero = jnp.zeros((head, seq), BF)
    work = [(r, h) for r in range(rows) for h in range(HEADS)]

    def opening(r, h):
        part = slice(h * head, (h + 1) * head)
        lanes = slice(h // 2 * 2 * head, (h // 2 + 1) * 2 * head)
        grad_att = ga_ref[r, part].astype(F32) * inv_ref[r, h : h + 1]
        inner = jnp.sum(grad_att * att_ref[r, part].astype(F32), axis=0, keepdims=True)
        grad_att = grad_att.astype(BF)
        pair = [grad_att, zero] if h % 2 == 0 else [zero, grad_att]
        soft_ref[r, h] = mm(v_ref[r, :, lanes], jnp.concatenate(pair, axis=0))
        return grad_att, inner

    ready = opening(*work[0])
    for at, (r, h) in enumerate(work):
        grad_att, inner = ready
        if at + 1 < len(work):
            ready = opening(*work[at + 1])
        for t in tiles(seq, 32):
            raised = e_ref[r, h, t].astype(F32)
            logit_ref[r, h, t] = (raised * (soft_ref[r, h, t] - inner)).astype(BF)
        part = slice(h * head, (h + 1) * head)
        place = slice(r * seq, (r + 1) * seq)
        grad_logits = logit_ref[r, h]
        grad_q = mm(k_ref[r, part], grad_logits) * head ** (-0.5)
        proj_ref[h * head : (h + 1) * head, place] = grad_q.astype(BF)
        grad_k = mm_nt(q_ref[r, part], grad_logits)
        proj_ref[width + h * head : width + (h + 1) * head, place] = grad_k.astype(BF)
        grad_v = mm_nt(grad_att, e_ref[r, h])
        proj_ref[2 * width + h * head : 2 * width + (h + 1) * head, place] = grad_v.astype(BF)
    for r in range(rows):
        norm_cat[:, r * seq : (r + 1) * seq] = norm_ref[r]
        gn_ref[r] = mm(w_ref[...], proj_ref[:, r * seq : (r + 1) * seq]).astype(BF)
    w_acc[...] += mm_nt(norm_cat[...], proj_ref[...])

    @pl.when(step == pl.num_programs(0) - 1)
    def _():
        if start_ref is None:
            gw_refs[0][...] = w_acc[...]
        else:
            groups = len(gw_refs)
            for i in range(pieces):
                here = pl.ds(pl.multiple_of(index_ref[i] * own, 16), own)
                gw_refs[i % groups][i // groups] = w_acc[here, :].astype(BF)


def backward_conv(
    x_ref, aux_ref, mc_ref, gm_ref, gn_ref, packed_ref, other_ref, part_ref, ig_ref, gs_ref,
    acc_ref, col_ref, n_ref, g_ref, turn_ref,
):
    rows, width, seq = x_ref.shape
    step = pl.program_id(0)

    @pl.when(step == 0)
    def _():
        acc_ref[...] = jnp.zeros_like(acc_ref)
        load_columns(packed_ref, col_ref, range(4))

    spots = tiles(seq, LANES)
    for r in range(rows):
        scales = []
        for t in spots:
            n, scale = norm_columns(mc_ref[r, :, t])
            n_ref[r, :, t] = n
            scales.append(scale)
        mean_e = [jnp.zeros((8, LANES), F32) for _ in spots]
        mean_en = [jnp.zeros((8, LANES), F32) for _ in spots]
        for d in tiles(width, 32):
            column = col_ref[3, d]
            gain_sum, shift_sum = acc_ref[3, d], acc_ref[4, d]
            for i, t in enumerate(spots):
                grad_n = gn_ref[r, d, t].astype(F32)
                product = grad_n * n_ref[r, d, t]
                gain_sum += product
                shift_sum += grad_n
                mean_e[i] += fold(grad_n * column)
                mean_en[i] += fold(product * column)
            acc_ref[3, d] = gain_sum
            acc_ref[4, d] = shift_sum
        for i, t in enumerate(spots):
            me = jnp.sum(mean_e[i], axis=0, keepdims=True) * (1.0 / width)
            men = jnp.sum(mean_en[i], axis=0, keepdims=True) * (1.0 / width)
            for d in tiles(width, 64):
                e = gn_ref[r, d, t].astype(F32) * col_ref[3, d]
                g_ref[r, d, t] = gm_ref[r, d, t] + scales[i] * (e - me - n_ref[r, d, t] * men)
        links, next_links = aux_ref[r, 0:1], aux_ref[r, 1:2]
        for d in tiles(width, 32):
            g = g_ref[r, d]
            base = x_ref[r, d].astype(F32)
            before = pltpu.roll(g, 1, 1) * links
            after = pltpu.roll(g, seq - 1, 1) * next_links
            acc_ref[0, d] += fold_lanes(base * after)
            acc_ref[1, d] += fold_lanes(base * g)
            acc_ref[2, d] += fold_lanes(base * before)
            conv0, conv1, conv2 = [twice(col_ref[i, d], seq) for i in range(3)]
            turn_ref[r, d] = (g + conv1 * g + conv0 * after + conv2 * before).astype(BF)
        ig_ref[r] = turn_ref[r].T

    @pl.when(step == pl.num_programs(0) - 1)
    def _():
        gs_ref[...] = other_ref[...]
        for i in range(5):
            gs_ref[i : i + 1] += jnp.sum(acc_ref[i].T, axis=0, keepdims=True)


def in_hbm(values):
    return pltpu.with_memory_space_constraint(values, pltpu.HBM)


def by_row(shape, rows, first=0):
    tail = tuple(shape[1:])
    return pl.BlockSpec((rows,) + tail, lambda i, *_: (i + first,) + (0,) * len(tail))


def whole(shape):
    place = (0,) * len(shape)
    return pl.BlockSpec(tuple(shape), lambda i, *_: place)


def step_rows(count, most):
    return max(r for r in range(1, most + 1) if count % r == 0)


def call(body, name, scalars, rows, row_args, args, row_outs, outs, scratch, span=None, into=None, near=()):
    first, count = span or (0, row_args[0].shape[0])
    skip = first // rows
    in_specs = [by_row(a.shape, rows, skip if a.shape[0] > count else 0) for a in row_args]
    in_specs += [whole(a.shape) for a in args]
    aliases = {}
    if into is not None:
        in_specs.append(pl.BlockSpec(memory_space=pl.ANY))
        aliases = {len(scalars) + len(in_specs) - 1: 0}
    spec = pltpu.PrefetchScalarGridSpec(
        num_scalar_prefetch=len(scalars),
        grid=(count // rows,),
        in_specs=in_specs,
        out_specs=[by_row(s, rows, skip if s[0] > count else 0) for s, _ in row_outs] + [whole(s) for s, _ in outs],
        scratch_shapes=[pltpu.VMEM(s, t) for s, t in scratch],
    )
    return pl.pallas_call(
        body,
        grid_spec=spec,
        out_shape=[(jax.ShapeDtypeStruct if "out" + str(i) in near else pltpu.HBM)(s, t) for i, (s, t) in enumerate(row_outs)]
        + [jax.ShapeDtypeStruct(s, t) for s, t in outs],
        input_output_aliases=aliases,
        compiler_params=pltpu.CompilerParams(dimension_semantics=("arbitrary",), vmem_limit_bytes=VMEM_LIMITS[name] * MIB),
        name=name,
    )(*scalars, *[a if i in near else in_hbm(a) for i, a in enumerate(row_args)], *args, *(() if into is None else (into,)))


def small_call(body, name, args, outs, scratch=()):
    return pl.pallas_call(
        body,
        out_shape=[jax.ShapeDtypeStruct(s, t) for s, t in outs],
        scratch_shapes=[pltpu.VMEM(s, t) for s, t in scratch],
        compiler_params=pltpu.CompilerParams(vmem_limit_bytes=16 * MIB),
        name=name,
    )(*args)


def run_forward(index, tokens, segment_ids, valid_len, pieces):
    count, seq, width = tokens.shape
    flipped = (count, width, seq)
    rows = step_rows(count, 2)
    row_outs = [
        (flipped, BF), (flipped, F32), (flipped, BF), (flipped, BF), (flipped, BF), ((count, seq, width), BF),
        ((count, HEADS, seq, seq), BF), (flipped, BF), ((count, 8, seq), F32), ((count, 8, seq), F32),
    ]
    return call(
        functools.partial(forward_attention, pieces=len(pieces)), "forward_attention", (index, valid_len),
        rows, (tokens,), (in_hbm(segment_ids), *pieces),
        row_outs, [((width, VECTORS), BF), ((width, 3 * width), BF)],
        [
            ((3 * width, width), BF), ((width, 3 * width + VECTORS), BF), ((5, width, LANES), F32),
            ((rows, seq, seq), F32), ((rows, seq, width), BF), ((rows, width, seq), BF), ((rows, HEADS, seq, seq), F32),
        ],
    )


def run_feed_forward(index, att, mixed, cotangent, packed, pieces, shards):
    count, seq, width = cotangent.shape
    own = width // len(pieces)
    ff = shards * width
    groups = 2 if len(pieces) > 1 else 1
    rows = step_rows(count, 2)
    wide = rows * seq
    row_outs = [((count, seq, width), BF), ((count, width, seq), F32), ((count, width, seq), BF)]
    grads = ((len(pieces) // groups, own, 2 * ff + width), BF)
    return call(
        functools.partial(feed_forward, pieces=len(pieces), shards=shards), "feed_forward", (index,),
        rows, (att, mixed, cotangent), (packed, *pieces),
        row_outs, [((8, width), F32)] + [grads] * groups,
        [((width, ff), BF)] * 2 + [((ff, width), BF)] * 2 + [((width, width), BF)] * 2
        + [((width, ff), F32)] * 2 + [((width, width), F32), ((2, width, LANES), F32), ((2, width, LANES), F32)]
        + [((width, wide), BF), ((width, wide), F32), ((width, wide), F32), ((width, wide), BF), ((width, wide), BF)]
        + [((ff, wide), F32)] * 2 + [((ff, wide), BF)] * 2
        + [((width, wide), F32), ((8, wide), F32), ((width, wide), BF), ((width, wide), BF)],
        near=("out2",),
    )


def run_backward_attention(index, weight, kept, grad_att, pieces, span, start):
    count, seq, width = kept[2].shape
    own = width // pieces
    groups = 2 if pieces > 1 else 1
    rows = step_rows(span[1], 2)
    row_args = (*kept, grad_att)
    many = len(row_args)

    def body(index_ref, *refs):
        w_ref, rest = refs[many], refs[many + 1 :]
        start_ref, rest = (None, rest) if start is None else (rest[0], rest[1:])
        backward_attention(*refs[:many], index_ref, w_ref, start_ref, *rest, pieces=pieces)

    outs = [((width, 3 * width), F32)] if start is None else [((pieces // groups, own, 3 * width), BF)] * groups
    return call(
        body, "backward_attention", (index,), rows, row_args, (weight,) if start is None else (weight, start),
        [((span[1], width, seq), BF)], outs,
        [
            ((3 * width, rows * seq), BF), ((width, 3 * width), F32), ((width, rows * seq), BF),
            ((rows, HEADS, seq, seq), F32), ((rows, HEADS, seq, seq), BF),
        ],
        span=span, near=("out0", many - 1),
    )


def run_backward_conv(x, aux, mixed, grad_mixed, grad_normed, packed, other, span, into):
    count, width, seq = x.shape
    rows = step_rows(span[1], 2)

    def body(*refs):
        if into is None:
            backward_conv(*refs[:7], None, *refs[7:])
        else:
            backward_conv(*refs)

    return call(
        body, "backward_conv", (), rows,
        (x, aux, mixed, grad_mixed, grad_normed), (packed, other),
        [((count, seq, width), BF)], [((8, width), F32)],
        [
            ((5, width, LANES), F32), ((4, width, LANES), F32), ((rows, width, seq), F32), ((rows, width, seq), F32),
            ((rows, width, seq), BF),
        ],
        span=span, into=into, near=(4,),
    )


def halves(count):
    early = count // 3
    return ((0, early), (early, count - early)) if early % 2 == 0 and early else ((0, count // 2), (count // 2, count - count // 2))


def exchange(values, axis, offset):
    size = lax.axis_size(axis)
    return lax.ppermute(values, axis, [(i, i ^ offset) for i in range(size)])


def add_halves(mine, received):
    count, own, cols = mine.shape

    def body(mine_ref, received_ref, *out_refs):
        for i, ref in enumerate(out_refs):
            ref[...] = (mine_ref[i].astype(F32) + received_ref[i].astype(F32)).astype(BF)

    return small_call(body, "add_halves", (mine, received), [((own, cols), BF)] * count)


def add_wide(*items):
    return tree_sum(item.astype(F32) for item in items)


def add_shard_vectors(items, own):
    def body(*refs):
        total = tree_sum(ref[...] for ref in refs[:-5])
        refs[-5][...] = total[0:3, :own]
        for i in range(4):
            refs[i - 4][...] = total[3 + i : 4 + i, :own]

    return small_call(body, "add_shard_vectors", items, [((3, own), F32)] + [((1, own), F32)] * 4)


def direct_plan(tokens, segment_ids, valid_len, qkv_weight, out_weight, up_weight, down_weight, conv_weight, vectors, cotangent):
    count, seq, width = tokens.shape
    own, ffs = up_weight.shape
    dp, mp = lax.axis_size("dp"), lax.axis_size("mp")
    me = lax.axis_index("dp")
    offsets = [2 * p for p in range(dp // 2)]
    index = jnp.stack([me ^ (p ^ c) for p in offsets for c in range(2)]).astype(jnp.int32)
    narrow, ff_own = small_call(
        pack_weights, "pack_weights",
        [in_hbm(a) for a in (qkv_weight, up_weight, down_weight, conv_weight, *[v.reshape(1, own) for v in vectors])],
        [((own, 3 * width + VECTORS), BF), ((2 * own, ffs), BF)], [((VECTORS, VECTORS), F32)],
    )
    plane = [narrow] + [exchange(narrow, "dp", p) for p in offsets[1:]]
    shards = [ff_own] + [exchange(ff_own, "mp", j) for j in range(1, mp)]
    pieces = [piece for a in plane for piece in (a, exchange(a, "dp", 1))]
    column = jnp.concatenate(shards + [out_weight], axis=0)
    columns = [column] + [exchange(column, "dp", p) for p in offsets[1:]]
    x, mixed, normed, q, k, v, raised, att, inverse, aux, packed, weight = run_forward(
        index, tokens, segment_ids, valid_len, pieces
    )
    columns, att = lax.optimization_barrier((columns, att))
    pieces = [piece for a in columns for piece in (a, exchange(a, "dp", 1))]
    layer_out, grad_mixed, grad_att, sums2, mine, theirs = run_feed_forward(
        index, att, mixed, cotangent, packed, pieces, mp
    )
    received = exchange(theirs, "dp", 1)
    early, late = halves(count)
    kept = (q, k, v, raised, att, inverse, normed)
    grad_normed1, start = run_backward_attention(index, weight, kept, grad_att, dp, early, None)
    received, start = lax.optimization_barrier((received, start))
    parts = list(add_halves(mine, received))
    parts[0], start = lax.optimization_barrier((parts[0], start))
    plane = [parts[0]] + [exchange(parts[i], "dp", p) for i, p in enumerate(offsets) if i]
    grad_normed2, mine_a, theirs_a = run_backward_attention(index, weight, kept, grad_att, dp, late, start)
    plane, theirs_a = lax.optimization_barrier((plane, theirs_a))
    received_a = exchange(theirs_a, "dp", 1)
    total = add_wide(*plane).astype(BF)
    half = 2 * ffs * (mp // 2)
    near, far, out_part = total[:, :half], total[:, half:], total[:, 2 * half :]
    received_f = exchange(far, "mp", 2)
    near, grad_normed1 = lax.optimization_barrier((near, grad_normed1))
    some_grad, sums = run_backward_conv(x, aux, mixed, grad_mixed, grad_normed1, packed, sums2, early, None)
    received_a, sums = lax.optimization_barrier((received_a, sums))
    parts = list(add_halves(mine_a, received_a))
    parts[0], sums = lax.optimization_barrier((parts[0], sums))
    plane_a = [parts[0]] + [exchange(parts[i], "dp", p) for i, p in enumerate(offsets) if i]
    input_grad, sums = run_backward_conv(x, aux, mixed, grad_mixed, grad_normed2, packed, sums, late, some_grad)
    received_s = exchange(sums, "dp", 1)
    plane_a, received_f, sums = lax.optimization_barrier((plane_a, received_f, sums))
    total = add_wide(*plane_a).astype(BF)
    received_s, total = lax.optimization_barrier((received_s, total))
    received_1 = exchange(total, "mp", 2)
    sums = sums + received_s
    plane_s = [sums] + [exchange(sums, "dp", p) for p in offsets[1:]]
    near_sum = add_wide(near, received_f[:, :half])
    out_sum = lax.optimization_barrier(add_wide(out_part, received_f[:, half:]).astype(BF))
    keep = near_sum[:, : 2 * ffs]
    send = jnp.concatenate([near_sum[:, 2 * ffs :].astype(BF), out_sum], axis=1)
    received_n = exchange(send, "mp", 1)
    plane_s, received_1 = lax.optimization_barrier((plane_s, received_1))
    total = lax.optimization_barrier(add_wide(total, received_1).astype(BF))
    received_2 = exchange(total, "mp", 1)
    vectors = lax.dynamic_slice_in_dim(tree_sum(plane_s), me * own, own, axis=1)
    shards = [vectors] + [exchange(vectors, "mp", j) for j in range(1, mp)]
    grad_up = keep[:, :ffs] + received_n[:, :ffs].astype(F32)
    grad_down = keep[:, ffs:] + received_n[:, ffs : 2 * ffs].astype(F32)
    grad_out = add_wide(out_sum, received_n[:, 2 * ffs :])
    grad_qkv = add_wide(total, received_2)
    grad_conv, *grads = add_shard_vectors(shards, own)
    return (layer_out, input_grad, grad_qkv, grad_out, grad_up, grad_down, grad_conv, *[g.reshape(own) for g in grads])


def gathered_plan(tokens, segment_ids, valid_len, qkv_weight, out_weight, up_weight, down_weight, conv_weight, vectors, cotangent):
    count, seq, width = tokens.shape
    own = qkv_weight.shape[0]
    dp = width // own
    columns = jnp.stack([conv_weight[0], conv_weight[1], conv_weight[2], *vectors], axis=1)
    narrow = jnp.concatenate([qkv_weight, jnp.pad(columns, ((0, 0), (0, VECTORS - 7))), out_weight], axis=1)
    wide = lax.all_gather(narrow, "dp", axis=0, tiled=True)
    both = lax.all_gather(jnp.concatenate([up_weight, down_weight], axis=0), "mp", axis=1, tiled=True)
    ff = both.shape[1]
    shards = ff // width
    both = lax.all_gather(both, "dp", axis=0).reshape(dp, 2, own, shards, width)
    both = both.transpose(3, 1, 0, 2, 4).reshape(2 * ff, width)
    column = jnp.concatenate([both, wide[:, 3 * width + VECTORS :]], axis=0)
    index = jnp.zeros((1,), jnp.int32)
    x, mixed, normed, q, k, v, raised, att, inverse, aux, packed, weight = run_forward(
        index, tokens, segment_ids, valid_len, [wide[:, : 3 * width + VECTORS]]
    )
    layer_out, grad_mixed, grad_att, sums2, grads = run_feed_forward(
        index, att, mixed, cotangent, packed, [column], shards
    )
    early, late = halves(count)
    kept = (q, k, v, raised, att, inverse, normed)
    grad_normed1, start = run_backward_attention(index, weight, kept, grad_att, 1, early, None)
    grad_normed2, grad_qkv = run_backward_attention(index, weight, kept, grad_att, 1, late, start)
    some_grad, sums = run_backward_conv(x, aux, mixed, grad_mixed, grad_normed1, packed, sums2, early, None)
    input_grad, sums = run_backward_conv(x, aux, mixed, grad_mixed, grad_normed2, packed, sums, late, some_grad)
    grad_ff = grads[0, :, : 2 * ff].reshape(width, shards, 2, width).transpose(0, 2, 1, 3).reshape(width, 2 * ff)
    grad_ff = lax.psum_scatter(grad_ff, "dp", scatter_dimension=0, tiled=True).reshape(own, 2, ff)
    grad_ff = lax.psum_scatter(grad_ff, "mp", scatter_dimension=2, tiled=True).astype(F32)
    grad_attn = jnp.concatenate([grad_qkv[0], grads[0, :, 2 * ff :]], axis=1)
    grad_attn = lax.psum_scatter(grad_attn, "dp", scatter_dimension=0, tiled=True)
    grad_attn = lax.psum(grad_attn, "mp").astype(F32)
    sums = lax.psum(sums, ("dp", "mp"))
    sums = lax.dynamic_slice_in_dim(sums, lax.axis_index("dp") * own, own, axis=1)
    return (
        layer_out, input_grad, grad_attn[:, : 3 * width], grad_attn[:, 3 * width :],
        grad_ff[:, 0], grad_ff[:, 1], sums[0:3], sums[3], sums[4], sums[5], sums[6],
    )


def on_device(
    tokens, segment_ids, valid_len, qkv_weight, out_weight, up_weight, down_weight, conv_weight,
    ln1_gain, ln1_shift, ln2_gain, ln2_shift, cotangent,
):
    own, ffs = up_weight.shape
    direct = own % 16 == 0 and ffs == tokens.shape[2] and own <= VECTORS and lax.axis_size("mp") == 4
    plan = direct_plan if direct else gathered_plan
    return plan(
        tokens, segment_ids, valid_len, qkv_weight, out_weight, up_weight, down_weight, conv_weight,
        (ln1_gain, ln1_shift, ln2_gain, ln2_shift), cotangent,
    )


def solution(mesh):
    rows = P(("dp", "mp"), None, None)
    weights = (P("dp", None), P("dp", None), P("dp", "mp"), P("dp", "mp"), P(None, "dp"))
    vectors = (P("dp"),) * 4
    return jax.shard_map(
        on_device,
        mesh=mesh,
        in_specs=(rows, P(("dp", "mp"), None), P(("dp", "mp"))) + weights + vectors + (rows,),
        out_specs=(rows, rows) + weights + vectors,
        check_vma=False,
    )
```

```python
import functools
import math

import jax
import jax.numpy as jnp
from jax import lax
from jax.experimental import pallas as pl
from jax.experimental.pallas import tpu as pltpu
from jax.sharding import PartitionSpec as P

HEADS = 6
VECTORS = 128
LANES = 128
BF = jnp.bfloat16
F32 = jnp.float32
MIB = 1024 * 1024
VMEM_LIMITS = dict(forward_attention=26, feed_forward=42, backward_attention=28, backward_conv=14)


def mm(lhs, rhs):
    return lax.dot_general(lhs, rhs, (((1,), (0,)), ((), ())), preferred_element_type=F32)


def mm_nt(lhs, rhs):
    return lax.dot_general(lhs, rhs, (((1,), (1,)), ((), ())), preferred_element_type=F32)


def tree_sum(items):
    items = list(items)
    while len(items) > 1:
        items = [a + b for a, b in zip(items[::2], items[1::2])]
    return items[0]


def pack_weights(qkv_ref, up_ref, down_ref, conv_ref, g1_ref, s1_ref, g2_ref, s2_ref, narrow_ref, ff_ref, rows_ref):
    own, ffs = up_ref.shape
    rows_ref[...] = jnp.zeros_like(rows_ref)
    rows_ref[0:3, :own] = conv_ref[...].astype(F32)
    for i, ref in enumerate((g1_ref, s1_ref, g2_ref, s2_ref)):
        rows_ref[3 + i : 4 + i, :own] = ref[...].astype(F32)
    wide = qkv_ref.shape[1]
    narrow_ref[:, :wide] = qkv_ref[...]
    narrow_ref[:, wide:] = rows_ref[...].T[:own].astype(BF)
    ff_ref[:own] = up_ref[...]
    ff_ref[own:] = down_ref[...]


def tiles(total, size):
    return [slice(at, at + size) for at in range(0, total, size)]


def twice(tile, lanes):
    return jnp.concatenate([tile] * (lanes // LANES), axis=1)


def load_columns(packed_ref, col_ref, places):
    for i, place in enumerate(places):
        column = packed_ref[:, place : place + 1].astype(F32)
        col_ref[i] = jnp.broadcast_to(column, (column.shape[0], LANES))


def column_mean(values):
    return jnp.sum(values, axis=0, keepdims=True) * (1.0 / values.shape[0])


def norm_columns(values):
    centred = values - column_mean(values)
    scale = lax.rsqrt(column_mean(centred * centred) + 1e-06)
    return centred * scale, scale


def fold(values):
    rows, lanes = values.shape
    return jnp.sum(values.reshape(rows // 8, 8, lanes), axis=0)


def fold_lanes(values):
    return sum(values[:, t] for t in tiles(values.shape[1], LANES))


def forward_attention(index_ref, len_ref, tok_ref, seg_ref, *refs, pieces):
    piece_refs = refs[:pieces]
    (
        x_ref, mc_ref, norm_ref, q_ref, k_ref, v_ref, e_ref, att_ref, inv_ref, aux_ref, packed_ref, w_ref,
        wt_ref, wide_ref, col_ref, bias_ref, key_ref, value_ref, score_ref,
    ) = refs[pieces:]
    rows, seq, width = tok_ref.shape
    head = width // HEADS
    step = pl.program_id(0)

    @pl.when(step == 0)
    def _():
        own = width // pieces
        for i, ref in enumerate(piece_refs):
            wide_ref[pl.ds(pl.multiple_of(index_ref[i] * own, 16), own), :] = ref[...]
        w_ref[...] = wide_ref[:, : 3 * width]
        wt_ref[:width] = (wide_ref[:, :width].astype(F32) * head ** (-0.5)).astype(BF).T
        wt_ref[width:] = wide_ref[:, width : 3 * width].T
        packed_ref[...] = wide_ref[:, 3 * width :]
        load_columns(packed_ref, col_ref, range(5))

    place = lax.broadcasted_iota(jnp.int32, (1, seq), 1)
    for r in range(rows):
        segs = seg_ref[pl.ds(step * rows + r, 1), :].astype(F32)
        valid = place < len_ref[step * rows + r]
        number = jnp.where(valid, segs, -1.0)
        links = jnp.where(valid & (place > 0) & (number == pltpu.roll(number, 1, 1)), 1.0, 0.0)
        next_links = jnp.where(place < seq - 1, pltpu.roll(links, seq - 1, 1), 0.0)
        none = jnp.zeros_like(links)
        aux = jnp.concatenate([links, next_links, number, none, none, none, none, none], axis=0)
        aux_ref[r] = aux
        key_number = aux.T[:, 2:3]
        for t in tiles(seq, 64):
            row_id = lax.broadcasted_iota(jnp.int32, (64, seq), 0) + t.start
            col_id = lax.broadcasted_iota(jnp.int32, (64, seq), 1)
            bias_ref[r, t] = jnp.where((key_number[t] == segs) | (row_id == col_id), 0.0, -1e30)
        x_ref[r] = tok_ref[r].T
        for t in tiles(width, 64):
            base = x_ref[r, t].astype(F32)
            before = pltpu.roll(base, 1, 1) * links
            after = pltpu.roll(base, seq - 1, 1) * next_links
            conv0, conv1, conv2 = [twice(col_ref[i, t], seq) for i in range(3)]
            mc_ref[r, t] = base + before * conv0 + base * conv1 + after * conv2
        for t in tiles(seq, LANES):
            n, _ = norm_columns(mc_ref[r, :, t])
            norm_ref[r, :, t] = (n * col_ref[3] + col_ref[4]).astype(BF)
    for r in range(rows):
        normed = norm_ref[r]
        proj = mm(wt_ref[...], normed).astype(BF)
        q_ref[r] = proj[:width]
        k_ref[r] = proj[width : 2 * width]
        value_ref[r] = proj[2 * width :]
        key_ref[r] = k_ref[r].T
        v_ref[r] = value_ref[r].T
    zero = jnp.zeros((head, seq), BF)

    def scores(r, h):
        own = q_ref[r, h * head : (h + 1) * head]
        pair = [own, zero] if h % 2 == 0 else [zero, own]
        lanes = slice(h // 2 * 2 * head, (h // 2 + 1) * 2 * head)
        score_ref[r, h] = mm(key_ref[r, :, lanes], jnp.concatenate(pair, axis=0))

    work = [(r, h) for r in range(rows) for h in range(HEADS)]
    scores(*work[0])
    for at, (r, h) in enumerate(work):
        if at + 1 < len(work):
            scores(*work[at + 1])
        for t in tiles(seq, LANES):
            masked = score_ref[r, h, :, t] + bias_ref[r, :, t]
            raised = jnp.exp(masked - jnp.max(masked, axis=0, keepdims=True))
            inv_ref[r, h : h + 1, t] = 1.0 / jnp.sum(raised, axis=0, keepdims=True)
            e_ref[r, h, :, t] = raised.astype(BF)
        part = slice(h * head, (h + 1) * head)
        att = mm(value_ref[r, part], e_ref[r, h]) * inv_ref[r, h : h + 1]
        att_ref[r, part] = att.astype(BF)


def gelu_parts(x):
    cdf = 0.5 * lax.erf(x * math.sqrt(0.5)) + 0.5
    bell = jnp.exp2(x * x * (-0.5 / math.log(2.0)) - 0.5 * math.log2(2.0 * math.pi))
    return x * cdf, cdf + x * bell


def feed_forward(index_ref, att_ref, mc_ref, ct_ref, packed_ref, *refs, pieces, shards):
    piece_refs = refs[:pieces]
    groups = 2 if pieces > 1 else 1
    lo_ref, gm_ref, ga_ref, gs_ref = refs[pieces : pieces + 4]
    gw_refs = refs[pieces + 4 : pieces + 4 + groups]
    (
        up_ref, down_ref, upt_ref, downt_ref, out_ref, outt_ref, up_acc, down_acc, out_acc, col_acc, col_ref,
        att_cat, mixed_ref, n_ref, norm_ref, ctt_ref, pre_ref, gh_ref, hidden_ref, gp_ref, gn_ref, scale_ref, lot_ref,
        branch_ref,
    ) = refs[pieces + 4 + groups :]
    rows, seq, width = ct_ref.shape
    ff = up_ref.shape[1]
    ffs = ff // shards
    own = width // pieces
    step = pl.program_id(0)

    @pl.when(step == 0)
    def _():
        for acc in (up_acc, down_acc, out_acc, col_acc):
            acc[...] = jnp.zeros_like(acc)
        for i, ref in enumerate(piece_refs):
            here = pl.ds(pl.multiple_of(index_ref[i] * own, 16), own)
            for j in range(shards):
                up_ref[here, j * ffs : (j + 1) * ffs] = ref[2 * j * own : (2 * j + 1) * own]
                down_ref[here, j * ffs : (j + 1) * ffs] = ref[(2 * j + 1) * own : (2 * j + 2) * own]
            out_ref[here, :] = ref[2 * shards * own :]
        upt_ref[...] = up_ref[...].T
        downt_ref[...] = down_ref[...].T
        outt_ref[...] = out_ref[...].T
        load_columns(packed_ref, col_ref, (5, 6))

    for r in range(rows):
        lanes = slice(r * seq, (r + 1) * seq)
        ctt_ref[:, lanes] = ct_ref[r].T
        att_cat[:, lanes] = att_ref[r]
        mixed_ref[:, lanes] = mc_ref[r] + mm(outt_ref[...], att_ref[r])
    for t in tiles(rows * seq, LANES):
        n, scale = norm_columns(mixed_ref[:, t])
        n_ref[:, t] = n
        scale_ref[0:1, t] = scale
        norm_ref[:, t] = (n * col_ref[0] + col_ref[1]).astype(BF)

    for r in range(rows):
        lanes = slice(r * seq, (r + 1) * seq)
        pre_ref[:, lanes] = mm(upt_ref[...], norm_ref[:, lanes])
        gh_ref[:, lanes] = mm(downt_ref[...], ctt_ref[:, lanes])
    for r in range(rows):
        lanes = slice(r * seq, (r + 1) * seq)
        for t in tiles(ff, 32):
            hidden, slope = gelu_parts(pre_ref[t, lanes])
            hidden_ref[t, lanes] = hidden.astype(BF)
            gp_ref[t, lanes] = (gh_ref[t, lanes] * slope).astype(BF)
        gn_ref[:, lanes] = mm(up_ref[...], gp_ref[:, lanes])
        lot_ref[:, lanes] = (mixed_ref[:, lanes] + mm(down_ref[...], hidden_ref[:, lanes])).astype(BF)
    down_acc[...] += mm_nt(ctt_ref[...], hidden_ref[...])
    up_acc[...] += mm_nt(norm_ref[...], gp_ref[...])
    spots = tiles(rows * seq, LANES)
    mean_e = [jnp.zeros((8, LANES), F32) for _ in spots]
    mean_en = [jnp.zeros((8, LANES), F32) for _ in spots]
    for d in tiles(width, 32):
        column = col_ref[0, d]
        gain_sum, shift_sum = col_acc[0, d], col_acc[1, d]
        for i, t in enumerate(spots):
            grad_n = gn_ref[d, t]
            product = grad_n * n_ref[d, t]
            gain_sum += product
            shift_sum += grad_n
            mean_e[i] += fold(grad_n * column)
            mean_en[i] += fold(product * column)
        col_acc[0, d] = gain_sum
        col_acc[1, d] = shift_sum
    for i, t in enumerate(spots):
        me = jnp.sum(mean_e[i], axis=0, keepdims=True) * (1.0 / width)
        men = jnp.sum(mean_en[i], axis=0, keepdims=True) * (1.0 / width)
        scale = scale_ref[0:1, t]
        row, inside = divmod(t.start, seq)
        for d in tiles(width, 64):
            change = scale * (gn_ref[d, t] * col_ref[0, d] - me - n_ref[d, t] * men)
            grad_mixed = ctt_ref[d, t].astype(F32) + change
            gm_ref[row, d, inside : inside + LANES] = grad_mixed
            branch_ref[d, t] = grad_mixed.astype(BF)
    out_acc[...] += mm_nt(att_cat[...], branch_ref[...])
    for r in range(rows):
        lanes = slice(r * seq, (r + 1) * seq)
        ga_ref[r] = mm(out_ref[...], branch_ref[:, lanes]).astype(BF)
        lo_ref[r] = lot_ref[:, lanes].T

    @pl.when(step == pl.num_programs(0) - 1)
    def _():
        for i in range(pieces):
            here = pl.ds(pl.multiple_of(index_ref[i] * own, 16), own)
            place = gw_refs[i % groups]
            for j in range(shards):
                cols = slice(j * ffs, (j + 1) * ffs)
                place[i // groups, :, 2 * j * ffs : (2 * j + 1) * ffs] = up_acc[here, cols].astype(BF)
                place[i // groups, :, (2 * j + 1) * ffs : (2 * j + 2) * ffs] = down_acc[here, cols].astype(BF)
            place[i // groups, :, 2 * ff :] = out_acc[here, :].astype(BF)
        gs_ref[...] = jnp.zeros_like(gs_ref)
        for i in range(2):
            gs_ref[5 + i : 6 + i] = jnp.sum(col_acc[i].T, axis=0, keepdims=True)


def backward_attention(
    q_ref, k_ref, v_ref, e_ref, att_ref, inv_ref, norm_ref, ga_ref, index_ref, w_ref, start_ref, gn_ref, *refs, pieces
):
    gw_refs = refs[:-5]
    proj_ref, w_acc, norm_cat, soft_ref, logit_ref = refs[-5:]
    rows, seq, width = v_ref.shape
    own = width // pieces
    head = width // HEADS
    step = pl.program_id(0)

    @pl.when(step == 0)
    def _():
        w_acc[...] = jnp.zeros_like(w_acc) if start_ref is None else start_ref[...]

    zero = jnp.zeros((head, seq), BF)
    work = [(r, h) for r in range(rows) for h in range(HEADS)]

    def opening(r, h):
        part = slice(h * head, (h + 1) * head)
        lanes = slice(h // 2 * 2 * head, (h // 2 + 1) * 2 * head)
        grad_att = ga_ref[r, part].astype(F32) * inv_ref[r, h : h + 1]
        inner = jnp.sum(grad_att * att_ref[r, part].astype(F32), axis=0, keepdims=True)
        grad_att = grad_att.astype(BF)
        pair = [grad_att, zero] if h % 2 == 0 else [zero, grad_att]
        soft_ref[r, h] = mm(v_ref[r, :, lanes], jnp.concatenate(pair, axis=0))
        return grad_att, inner

    ready = opening(*work[0])
    for at, (r, h) in enumerate(work):
        grad_att, inner = ready
        if at + 1 < len(work):
            ready = opening(*work[at + 1])
        for t in tiles(seq, 32):
            raised = e_ref[r, h, t].astype(F32)
            logit_ref[r, h, t] = (raised * (soft_ref[r, h, t] - inner)).astype(BF)
        part = slice(h * head, (h + 1) * head)
        place = slice(r * seq, (r + 1) * seq)
        grad_logits = logit_ref[r, h]
        grad_q = mm(k_ref[r, part], grad_logits) * head ** (-0.5)
        proj_ref[h * head : (h + 1) * head, place] = grad_q.astype(BF)
        grad_k = mm_nt(q_ref[r, part], grad_logits)
        proj_ref[width + h * head : width + (h + 1) * head, place] = grad_k.astype(BF)
        grad_v = mm_nt(grad_att, e_ref[r, h])
        proj_ref[2 * width + h * head : 2 * width + (h + 1) * head, place] = grad_v.astype(BF)
    for r in range(rows):
        norm_cat[:, r * seq : (r + 1) * seq] = norm_ref[r]
        gn_ref[r] = mm(w_ref[...], proj_ref[:, r * seq : (r + 1) * seq]).astype(BF)
    w_acc[...] += mm_nt(norm_cat[...], proj_ref[...])

    @pl.when(step == pl.num_programs(0) - 1)
    def _():
        if start_ref is None:
            gw_refs[0][...] = w_acc[...]
        else:
            groups = len(gw_refs)
            for i in range(pieces):
                here = pl.ds(pl.multiple_of(index_ref[i] * own, 16), own)
                gw_refs[i % groups][i // groups] = w_acc[here, :].astype(BF)


def backward_conv(
    x_ref, aux_ref, mc_ref, gm_ref, gn_ref, packed_ref, other_ref, part_ref, ig_ref, gs_ref,
    acc_ref, col_ref, n_ref, g_ref, turn_ref,
):
    rows, width, seq = x_ref.shape
    step = pl.program_id(0)

    @pl.when(step == 0)
    def _():
        acc_ref[...] = jnp.zeros_like(acc_ref)
        load_columns(packed_ref, col_ref, range(4))

    spots = tiles(seq, LANES)
    for r in range(rows):
        scales = []
        for t in spots:
            n, scale = norm_columns(mc_ref[r, :, t])
            n_ref[r, :, t] = n
            scales.append(scale)
        mean_e = [jnp.zeros((8, LANES), F32) for _ in spots]
        mean_en = [jnp.zeros((8, LANES), F32) for _ in spots]
        for d in tiles(width, 32):
            column = col_ref[3, d]
            gain_sum, shift_sum = acc_ref[3, d], acc_ref[4, d]
            for i, t in enumerate(spots):
                grad_n = gn_ref[r, d, t].astype(F32)
                product = grad_n * n_ref[r, d, t]
                gain_sum += product
                shift_sum += grad_n
                mean_e[i] += fold(grad_n * column)
                mean_en[i] += fold(product * column)
            acc_ref[3, d] = gain_sum
            acc_ref[4, d] = shift_sum
        for i, t in enumerate(spots):
            me = jnp.sum(mean_e[i], axis=0, keepdims=True) * (1.0 / width)
            men = jnp.sum(mean_en[i], axis=0, keepdims=True) * (1.0 / width)
            for d in tiles(width, 64):
                e = gn_ref[r, d, t].astype(F32) * col_ref[3, d]
                g_ref[r, d, t] = gm_ref[r, d, t] + scales[i] * (e - me - n_ref[r, d, t] * men)
        links, next_links = aux_ref[r, 0:1], aux_ref[r, 1:2]
        for d in tiles(width, 32):
            g = g_ref[r, d]
            base = x_ref[r, d].astype(F32)
            before = pltpu.roll(g, 1, 1) * links
            after = pltpu.roll(g, seq - 1, 1) * next_links
            acc_ref[0, d] += fold_lanes(base * after)
            acc_ref[1, d] += fold_lanes(base * g)
            acc_ref[2, d] += fold_lanes(base * before)
            conv0, conv1, conv2 = [twice(col_ref[i, d], seq) for i in range(3)]
            turn_ref[r, d] = (g + conv1 * g + conv0 * after + conv2 * before).astype(BF)
        ig_ref[r] = turn_ref[r].T

    @pl.when(step == pl.num_programs(0) - 1)
    def _():
        gs_ref[...] = other_ref[...]
        for i in range(5):
            gs_ref[i : i + 1] += jnp.sum(acc_ref[i].T, axis=0, keepdims=True)


def in_hbm(values):
    return pltpu.with_memory_space_constraint(values, pltpu.HBM)


def by_row(shape, rows, first=0):
    tail = tuple(shape[1:])
    return pl.BlockSpec((rows,) + tail, lambda i, *_: (i + first,) + (0,) * len(tail))


def whole(shape):
    place = (0,) * len(shape)
    return pl.BlockSpec(tuple(shape), lambda i, *_: place)


def step_rows(count, most):
    return max(r for r in range(1, most + 1) if count % r == 0)


def call(body, name, scalars, rows, row_args, args, row_outs, outs, scratch, span=None, into=None, near=()):
    first, count = span or (0, row_args[0].shape[0])
    skip = first // rows
    in_specs = [by_row(a.shape, rows, skip if a.shape[0] > count else 0) for a in row_args]
    in_specs += [whole(a.shape) for a in args]
    aliases = {}
    if into is not None:
        in_specs.append(pl.BlockSpec(memory_space=pl.ANY))
        aliases = {len(scalars) + len(in_specs) - 1: 0}
    spec = pltpu.PrefetchScalarGridSpec(
        num_scalar_prefetch=len(scalars),
        grid=(count // rows,),
        in_specs=in_specs,
        out_specs=[by_row(s, rows, skip if s[0] > count else 0) for s, _ in row_outs] + [whole(s) for s, _ in outs],
        scratch_shapes=[pltpu.VMEM(s, t) for s, t in scratch],
    )
    return pl.pallas_call(
        body,
        grid_spec=spec,
        out_shape=[(jax.ShapeDtypeStruct if "out" + str(i) in near else pltpu.HBM)(s, t) for i, (s, t) in enumerate(row_outs)]
        + [jax.ShapeDtypeStruct(s, t) for s, t in outs],
        input_output_aliases=aliases,
        compiler_params=pltpu.CompilerParams(dimension_semantics=("arbitrary",), vmem_limit_bytes=VMEM_LIMITS[name] * MIB),
        name=name,
    )(*scalars, *[a if i in near else in_hbm(a) for i, a in enumerate(row_args)], *args, *(() if into is None else (into,)))


def small_call(body, name, args, outs, scratch=()):
    return pl.pallas_call(
        body,
        out_shape=[jax.ShapeDtypeStruct(s, t) for s, t in outs],
        scratch_shapes=[pltpu.VMEM(s, t) for s, t in scratch],
        compiler_params=pltpu.CompilerParams(vmem_limit_bytes=16 * MIB),
        name=name,
    )(*args)


def run_forward(index, tokens, segment_ids, valid_len, pieces):
    count, seq, width = tokens.shape
    flipped = (count, width, seq)
    rows = step_rows(count, 2)
    row_outs = [
        (flipped, BF), (flipped, F32), (flipped, BF), (flipped, BF), (flipped, BF), ((count, seq, width), BF),
        ((count, HEADS, seq, seq), BF), (flipped, BF), ((count, 8, seq), F32), ((count, 8, seq), F32),
    ]
    return call(
        functools.partial(forward_attention, pieces=len(pieces)), "forward_attention", (index, valid_len),
        rows, (tokens,), (in_hbm(segment_ids), *pieces),
        row_outs, [((width, VECTORS), BF), ((width, 3 * width), BF)],
        [
            ((3 * width, width), BF), ((width, 3 * width + VECTORS), BF), ((5, width, LANES), F32),
            ((rows, seq, seq), F32), ((rows, seq, width), BF), ((rows, width, seq), BF), ((rows, HEADS, seq, seq), F32),
        ],
    )


def run_feed_forward(index, att, mixed, cotangent, packed, pieces, shards):
    count, seq, width = cotangent.shape
    own = width // len(pieces)
    ff = shards * width
    groups = 2 if len(pieces) > 1 else 1
    rows = step_rows(count, 2)
    wide = rows * seq
    row_outs = [((count, seq, width), BF), ((count, width, seq), F32), ((count, width, seq), BF)]
    grads = ((len(pieces) // groups, own, 2 * ff + width), BF)
    return call(
        functools.partial(feed_forward, pieces=len(pieces), shards=shards), "feed_forward", (index,),
        rows, (att, mixed, cotangent), (packed, *pieces),
        row_outs, [((8, width), F32)] + [grads] * groups,
        [((width, ff), BF)] * 2 + [((ff, width), BF)] * 2 + [((width, width), BF)] * 2
        + [((width, ff), F32)] * 2 + [((width, width), F32), ((2, width, LANES), F32), ((2, width, LANES), F32)]
        + [((width, wide), BF), ((width, wide), F32), ((width, wide), F32), ((width, wide), BF), ((width, wide), BF)]
        + [((ff, wide), F32)] * 2 + [((ff, wide), BF)] * 2
        + [((width, wide), F32), ((8, wide), F32), ((width, wide), BF), ((width, wide), BF)],
        near=("out2",),
    )


def run_backward_attention(index, weight, kept, grad_att, pieces, span, start):
    count, seq, width = kept[2].shape
    own = width // pieces
    groups = 2 if pieces > 1 else 1
    rows = step_rows(span[1], 2)
    row_args = (*kept, grad_att)
    many = len(row_args)

    def body(index_ref, *refs):
        w_ref, rest = refs[many], refs[many + 1 :]
        start_ref, rest = (None, rest) if start is None else (rest[0], rest[1:])
        backward_attention(*refs[:many], index_ref, w_ref, start_ref, *rest, pieces=pieces)

    outs = [((width, 3 * width), F32)] if start is None else [((pieces // groups, own, 3 * width), BF)] * groups
    return call(
        body, "backward_attention", (index,), rows, row_args, (weight,) if start is None else (weight, start),
        [((span[1], width, seq), BF)], outs,
        [
            ((3 * width, rows * seq), BF), ((width, 3 * width), F32), ((width, rows * seq), BF),
            ((rows, HEADS, seq, seq), F32), ((rows, HEADS, seq, seq), BF),
        ],
        span=span, near=("out0", many - 1),
    )


def run_backward_conv(x, aux, mixed, grad_mixed, grad_normed, packed, other, span, into):
    count, width, seq = x.shape
    rows = step_rows(span[1], 2)

    def body(*refs):
        if into is None:
            backward_conv(*refs[:7], None, *refs[7:])
        else:
            backward_conv(*refs)

    return call(
        body, "backward_conv", (), rows,
        (x, aux, mixed, grad_mixed, grad_normed), (packed, other),
        [((count, seq, width), BF)], [((8, width), F32)],
        [
            ((5, width, LANES), F32), ((4, width, LANES), F32), ((rows, width, seq), F32), ((rows, width, seq), F32),
            ((rows, width, seq), BF),
        ],
        span=span, into=into, near=(4,),
    )


def halves(count):
    early = count // 3
    return ((0, early), (early, count - early)) if early % 2 == 0 and early else ((0, count // 2), (count // 2, count - count // 2))


def exchange(values, axis, offset):
    size = lax.axis_size(axis)
    return lax.ppermute(values, axis, [(i, i ^ offset) for i in range(size)])


def add_halves(mine, received):
    count, own, cols = mine.shape

    def body(mine_ref, received_ref, *out_refs):
        for i, ref in enumerate(out_refs):
            ref[...] = (mine_ref[i].astype(F32) + received_ref[i].astype(F32)).astype(BF)

    return small_call(body, "add_halves", (mine, received), [((own, cols), BF)] * count)


def add_wide(*items):
    return tree_sum(item.astype(F32) for item in items)


def add_shard_vectors(items, own):
    def body(*refs):
        total = tree_sum(ref[...] for ref in refs[:-5])
        refs[-5][...] = total[0:3, :own]
        for i in range(4):
            refs[i - 4][...] = total[3 + i : 4 + i, :own]

    return small_call(body, "add_shard_vectors", items, [((3, own), F32)] + [((1, own), F32)] * 4)


def direct_plan(tokens, segment_ids, valid_len, qkv_weight, out_weight, up_weight, down_weight, conv_weight, vectors, cotangent):
    count, seq, width = tokens.shape
    own, ffs = up_weight.shape
    dp, mp = lax.axis_size("dp"), lax.axis_size("mp")
    me = lax.axis_index("dp")
    offsets = [2 * p for p in range(dp // 2)]
    index = jnp.stack([me ^ (p ^ c) for p in offsets for c in range(2)]).astype(jnp.int32)
    narrow, ff_own = small_call(
        pack_weights, "pack_weights",
        [in_hbm(a) for a in (qkv_weight, up_weight, down_weight, conv_weight, *[v.reshape(1, own) for v in vectors])],
        [((own, 3 * width + VECTORS), BF), ((2 * own, ffs), BF)], [((VECTORS, VECTORS), F32)],
    )
    plane = [narrow] + [exchange(narrow, "dp", p) for p in offsets[1:]]
    shards = [ff_own] + [exchange(ff_own, "mp", j) for j in range(1, mp)]
    pieces = [piece for a in plane for piece in (a, exchange(a, "dp", 1))]
    column = jnp.concatenate(shards + [out_weight], axis=0)
    columns = [column] + [exchange(column, "dp", p) for p in offsets[1:]]
    x, mixed, normed, q, k, v, raised, att, inverse, aux, packed, weight = run_forward(
        index, tokens, segment_ids, valid_len, pieces
    )
    columns, att = lax.optimization_barrier((columns, att))
    pieces = [piece for a in columns for piece in (a, exchange(a, "dp", 1))]
    layer_out, grad_mixed, grad_att, sums2, mine, theirs = run_feed_forward(
        index, att, mixed, cotangent, packed, pieces, mp
    )
    received = exchange(theirs, "dp", 1)
    early, late = halves(count)
    kept = (q, k, v, raised, att, inverse, normed)
    grad_normed1, start = run_backward_attention(index, weight, kept, grad_att, dp, early, None)
    received, start = lax.optimization_barrier((received, start))
    parts = list(add_halves(mine, received))
    parts[0], start = lax.optimization_barrier((parts[0], start))
    plane = [parts[0]] + [exchange(parts[i], "dp", p) for i, p in enumerate(offsets) if i]
    grad_normed2, mine_a, theirs_a = run_backward_attention(index, weight, kept, grad_att, dp, late, start)
    plane, theirs_a = lax.optimization_barrier((plane, theirs_a))
    received_a = exchange(theirs_a, "dp", 1)
    total = add_wide(*plane).astype(BF)
    half = 2 * ffs * (mp // 2)
    near, far, out_part = total[:, :half], total[:, half:], total[:, 2 * half :]
    received_f = exchange(far, "mp", 2)
    near, grad_normed1 = lax.optimization_barrier((near, grad_normed1))
    some_grad, sums = run_backward_conv(x, aux, mixed, grad_mixed, grad_normed1, packed, sums2, early, None)
    received_a, sums = lax.optimization_barrier((received_a, sums))
    parts = list(add_halves(mine_a, received_a))
    parts[0], sums = lax.optimization_barrier((parts[0], sums))
    plane_a = [parts[0]] + [exchange(parts[i], "dp", p) for i, p in enumerate(offsets) if i]
    input_grad, sums = run_backward_conv(x, aux, mixed, grad_mixed, grad_normed2, packed, sums, late, some_grad)
    received_s = exchange(sums, "dp", 1)
    plane_a, received_f, sums = lax.optimization_barrier((plane_a, received_f, sums))
    total = add_wide(*plane_a).astype(BF)
    received_s, total = lax.optimization_barrier((received_s, total))
    received_1 = exchange(total, "mp", 2)
    sums = sums + received_s
    plane_s = [sums] + [exchange(sums, "dp", p) for p in offsets[1:]]
    near_sum = add_wide(near, received_f[:, :half])
    out_sum = lax.optimization_barrier(add_wide(out_part, received_f[:, half:]).astype(BF))
    keep = near_sum[:, : 2 * ffs]
    send = jnp.concatenate([near_sum[:, 2 * ffs :].astype(BF), out_sum], axis=1)
    received_n = exchange(send, "mp", 1)
    plane_s, received_1 = lax.optimization_barrier((plane_s, received_1))
    total = lax.optimization_barrier(add_wide(total, received_1).astype(BF))
    received_2 = exchange(total, "mp", 1)
    vectors = lax.dynamic_slice_in_dim(tree_sum(plane_s), me * own, own, axis=1)
    shards = [vectors] + [exchange(vectors, "mp", j) for j in range(1, mp)]
    grad_up = keep[:, :ffs] + received_n[:, :ffs].astype(F32)
    grad_down = keep[:, ffs:] + received_n[:, ffs : 2 * ffs].astype(F32)
    grad_out = add_wide(out_sum, received_n[:, 2 * ffs :])
    grad_qkv = add_wide(total, received_2)
    grad_conv, *grads = add_shard_vectors(shards, own)
    return (layer_out, input_grad, grad_qkv, grad_out, grad_up, grad_down, grad_conv, *[g.reshape(own) for g in grads])


def gathered_plan(tokens, segment_ids, valid_len, qkv_weight, out_weight, up_weight, down_weight, conv_weight, vectors, cotangent):
    count, seq, width = tokens.shape
    own = qkv_weight.shape[0]
    dp = width // own
    columns = jnp.stack([conv_weight[0], conv_weight[1], conv_weight[2], *vectors], axis=1)
    narrow = jnp.concatenate([qkv_weight, jnp.pad(columns, ((0, 0), (0, VECTORS - 7))), out_weight], axis=1)
    wide = lax.all_gather(narrow, "dp", axis=0, tiled=True)
    both = lax.all_gather(jnp.concatenate([up_weight, down_weight], axis=0), "mp", axis=1, tiled=True)
    ff = both.shape[1]
    shards = ff // width
    both = lax.all_gather(both, "dp", axis=0).reshape(dp, 2, own, shards, width)
    both = both.transpose(3, 1, 0, 2, 4).reshape(2 * ff, width)
    column = jnp.concatenate([both, wide[:, 3 * width + VECTORS :]], axis=0)
    index = jnp.zeros((1,), jnp.int32)
    x, mixed, normed, q, k, v, raised, att, inverse, aux, packed, weight = run_forward(
        index, tokens, segment_ids, valid_len, [wide[:, : 3 * width + VECTORS]]
    )
    layer_out, grad_mixed, grad_att, sums2, grads = run_feed_forward(
        index, att, mixed, cotangent, packed, [column], shards
    )
    early, late = halves(count)
    kept = (q, k, v, raised, att, inverse, normed)
    grad_normed1, start = run_backward_attention(index, weight, kept, grad_att, 1, early, None)
    grad_normed2, grad_qkv = run_backward_attention(index, weight, kept, grad_att, 1, late, start)
    some_grad, sums = run_backward_conv(x, aux, mixed, grad_mixed, grad_normed1, packed, sums2, early, None)
    input_grad, sums = run_backward_conv(x, aux, mixed, grad_mixed, grad_normed2, packed, sums, late, some_grad)
    grad_ff = grads[0, :, : 2 * ff].reshape(width, shards, 2, width).transpose(0, 2, 1, 3).reshape(width, 2 * ff)
    grad_ff = lax.psum_scatter(grad_ff, "dp", scatter_dimension=0, tiled=True).reshape(own, 2, ff)
    grad_ff = lax.psum_scatter(grad_ff, "mp", scatter_dimension=2, tiled=True).astype(F32)
    grad_attn = jnp.concatenate([grad_qkv[0], grads[0, :, 2 * ff :]], axis=1)
    grad_attn = lax.psum_scatter(grad_attn, "dp", scatter_dimension=0, tiled=True)
    grad_attn = lax.psum(grad_attn, "mp").astype(F32)
    sums = lax.psum(sums, ("dp", "mp"))
    sums = lax.dynamic_slice_in_dim(sums, lax.axis_index("dp") * own, own, axis=1)
    return (
        layer_out, input_grad, grad_attn[:, : 3 * width], grad_attn[:, 3 * width :],
        grad_ff[:, 0], grad_ff[:, 1], sums[0:3], sums[3], sums[4], sums[5], sums[6],
    )


def on_device(
    tokens, segment_ids, valid_len, qkv_weight, out_weight, up_weight, down_weight, conv_weight,
    ln1_gain, ln1_shift, ln2_gain, ln2_shift, cotangent,
):
    own, ffs = up_weight.shape
    direct = own % 16 == 0 and ffs == tokens.shape[2] and own <= VECTORS and lax.axis_size("mp") == 4
    plan = direct_plan if direct else gathered_plan
    return plan(
        tokens, segment_ids, valid_len, qkv_weight, out_weight, up_weight, down_weight, conv_weight,
        (ln1_gain, ln1_shift, ln2_gain, ln2_shift), cotangent,
    )


def solution(mesh):
    rows = P(("dp", "mp"), None, None)
    weights = (P("dp", None), P("dp", None), P("dp", "mp"), P("dp", "mp"), P(None, "dp"))
    vectors = (P("dp"),) * 4
    return jax.shard_map(
        on_device,
        mesh=mesh,
        in_specs=(rows, P(("dp", "mp"), None), P(("dp", "mp"))) + weights + vectors + (rows,),
        out_specs=(rows, rows) + weights + vectors,
        check_vma=False,
    )
```

```python
import functools
import math

import jax
import jax.numpy as jnp
from jax import lax
from jax.experimental import pallas as pl
from jax.experimental.pallas import tpu as pltpu
from jax.sharding import PartitionSpec as P

HEADS = 6
VECTORS = 128
LANES = 128
BF = jnp.bfloat16
F32 = jnp.float32
MIB = 1024 * 1024
VMEM_LIMITS = dict(forward_attention=30, feed_forward=44, backward_attention=28, backward_conv=14)


def mm(lhs, rhs):
    return lax.dot_general(lhs, rhs, (((1,), (0,)), ((), ())), preferred_element_type=F32)


def mm_nt(lhs, rhs):
    return lax.dot_general(lhs, rhs, (((1,), (1,)), ((), ())), preferred_element_type=F32)


def tree_sum(items):
    items = list(items)
    while len(items) > 1:
        items = [a + b for a, b in zip(items[::2], items[1::2])]
    return items[0]


def pack_weights(qkv_ref, up_ref, down_ref, conv_ref, g1_ref, s1_ref, g2_ref, s2_ref, narrow_ref, ff_ref, rows_ref):
    own, ffs = up_ref.shape
    rows_ref[...] = jnp.zeros_like(rows_ref)
    rows_ref[0:3, :own] = conv_ref[...].astype(F32)
    for i, ref in enumerate((g1_ref, s1_ref, g2_ref, s2_ref)):
        rows_ref[3 + i : 4 + i, :own] = ref[...].astype(F32)
    wide = qkv_ref.shape[1]
    narrow_ref[:, :wide] = qkv_ref[...]
    narrow_ref[:, wide:] = rows_ref[...].T[:own].astype(BF)
    ff_ref[:own] = up_ref[...]
    ff_ref[own:] = down_ref[...]


def tiles(total, size):
    return [slice(at, at + size) for at in range(0, total, size)]


def weave(*strands):
    strands = [strand for strand in strands if strand]
    total = sum(len(strand) for strand in strands)
    pieces = [((i + 0.5) / len(strand), j, piece) for j, strand in enumerate(strands) for i, piece in enumerate(strand)]
    assert len(pieces) == total
    for _, _, piece in sorted(pieces, key=lambda item: item[:2]):
        piece()


def twice(tile, lanes):
    return jnp.concatenate([tile] * (lanes // LANES), axis=1)


def load_columns(packed_ref, col_ref, places):
    for i, place in enumerate(places):
        column = packed_ref[:, place : place + 1].astype(F32)
        col_ref[i] = jnp.broadcast_to(column, (column.shape[0], LANES))


def column_mean(values):
    return jnp.sum(values, axis=0, keepdims=True) * (1.0 / values.shape[0])


def norm_columns(values):
    centred = values - column_mean(values)
    scale = lax.rsqrt(column_mean(centred * centred) + 1e-06)
    return centred * scale, scale


def fold(values):
    rows, lanes = values.shape
    return jnp.sum(values.reshape(rows // 8, 8, lanes), axis=0)


def fold_lanes(values):
    return sum(values[:, t] for t in tiles(values.shape[1], LANES))


def forward_attention(index_ref, len_ref, tok_ref, seg_ref, *refs, pieces):
    piece_refs = refs[:pieces]
    (
        x_ref, mc_ref, norm_ref, q_ref, k_ref, v_ref, e_ref, att_ref, inv_ref, aux_ref, packed_ref, w_ref,
        wt_ref, wide_ref, col_ref, bias_ref, key_ref, value_ref, score_ref,
    ) = refs[pieces:]
    rows, seq, width = tok_ref.shape
    head = width // HEADS
    step = pl.program_id(0)

    @pl.when(step == 0)
    def _():
        own = width // pieces
        for i, ref in enumerate(piece_refs):
            wide_ref[pl.ds(pl.multiple_of(index_ref[i] * own, 16), own), :] = ref[...]
        w_ref[...] = wide_ref[:, : 3 * width]
        wt_ref[:width] = (wide_ref[:, :width].astype(F32) * head ** (-0.5)).astype(BF).T
        wt_ref[width:] = wide_ref[:, width : 3 * width].T
        packed_ref[...] = wide_ref[:, 3 * width :]
        load_columns(packed_ref, col_ref, range(5))

    place = lax.broadcasted_iota(jnp.int32, (1, seq), 1)
    zero = jnp.zeros((head, seq), BF)

    def preparation(r):
        known = {}

        def start():
            segs = seg_ref[pl.ds(step * rows + r, 1), :].astype(F32)
            valid = place < len_ref[step * rows + r]
            number = jnp.where(valid, segs, -1.0)
            links = jnp.where(valid & (place > 0) & (number == pltpu.roll(number, 1, 1)), 1.0, 0.0)
            next_links = jnp.where(place < seq - 1, pltpu.roll(links, seq - 1, 1), 0.0)
            none = jnp.zeros_like(links)
            aux = jnp.concatenate([links, next_links, number, none, none, none, none, none], axis=0)
            aux_ref[r] = aux
            x_ref[r] = tok_ref[r].T
            known.update(segs=segs, links=links, next_links=next_links, key_number=aux.T[:, 2:3])

        def mask(t):
            row_id = lax.broadcasted_iota(jnp.int32, (64, seq), 0) + t.start
            col_id = lax.broadcasted_iota(jnp.int32, (64, seq), 1)
            allowed = (known["key_number"][t] == known["segs"]) | (row_id == col_id)
            bias_ref[r, t] = jnp.where(allowed, 0.0, -1e30)

        def conv(t):
            base = x_ref[r, t].astype(F32)
            before = pltpu.roll(base, 1, 1) * known["links"]
            after = pltpu.roll(base, seq - 1, 1) * known["next_links"]
            conv0, conv1, conv2 = [twice(col_ref[i, t], seq) for i in range(3)]
            mc_ref[r, t] = base + before * conv0 + base * conv1 + after * conv2

        def norm(t):
            n, _ = norm_columns(mc_ref[r, :, t])
            norm_ref[r, :, t] = (n * col_ref[3] + col_ref[4]).astype(BF)

        def project(i):
            part = mm(wt_ref[i * width : (i + 1) * width], norm_ref[r]).astype(BF)
            if i == 0:
                q_ref[r] = part
            elif i == 1:
                k_ref[r] = part
                key_ref[r] = part.T
            else:
                value_ref[r] = part
                v_ref[r] = part.T

        pieces = [start] + [functools.partial(conv, t) for t in tiles(width, 32)]
        pieces += [functools.partial(norm, t) for t in tiles(seq, LANES)]
        pieces += [functools.partial(project, i) for i in range(3)]
        return pieces + [functools.partial(mask, t) for t in tiles(seq, 64)]

    def scores(r, h):
        own = q_ref[r, h * head : (h + 1) * head]
        pair = [own, zero] if h % 2 == 0 else [zero, own]
        lanes = slice(h // 2 * 2 * head, (h // 2 + 1) * 2 * head)
        score_ref[r, h] = mm(key_ref[r, :, lanes], jnp.concatenate(pair, axis=0))

    def soften(r, h, t):
        masked = score_ref[r, h, :, t] + bias_ref[r, :, t]
        raised = jnp.exp(masked - jnp.max(masked, axis=0, keepdims=True))
        inv_ref[r, h : h + 1, t] = 1.0 / jnp.sum(raised, axis=0, keepdims=True)
        e_ref[r, h, :, t] = raised.astype(BF)

    def attend(r, h):
        part = slice(h * head, (h + 1) * head)
        att = mm(value_ref[r, part], e_ref[r, h]) * inv_ref[r, h : h + 1]
        att_ref[r, part] = att.astype(BF)

    def heads(r):
        pieces = [functools.partial(scores, r, 0)]
        for h in range(HEADS):
            if h + 1 < HEADS:
                pieces.append(functools.partial(scores, r, h + 1))
            pieces += [functools.partial(soften, r, h, t) for t in tiles(seq, LANES)]
            pieces.append(functools.partial(attend, r, h))
        return pieces

    weave(preparation(0))
    for r in range(rows):
        weave(heads(r), preparation(r + 1) if r + 1 < rows else [])


def gelu_parts(x):
    cdf = 0.5 * lax.erf(x * math.sqrt(0.5)) + 0.5
    bell = jnp.exp2(x * x * (-0.5 / math.log(2.0)) - 0.5 * math.log2(2.0 * math.pi))
    return x * cdf, cdf + x * bell


def feed_forward(index_ref, att_ref, mc_ref, ct_ref, packed_ref, *refs, pieces, shards):
    piece_refs = refs[:pieces]
    groups = 2 if pieces > 1 else 1
    lo_ref, gm_ref, ga_ref, gs_ref = refs[pieces : pieces + 4]
    gw_refs = refs[pieces + 4 : pieces + 4 + groups]
    (
        up_ref, down_ref, upt_ref, downt_ref, out_ref, outt_ref, up_acc, down_acc, out_acc, col_acc, col_ref,
        att_cat, mixed_ref, n_ref, norm_ref, ctt_ref, pre_ref, gh_ref, hidden_ref, gp_ref, gn_ref, scale_ref, lot_ref,
        branch_ref,
    ) = refs[pieces + 4 + groups :]
    rows, seq, width = ct_ref.shape
    ff = up_ref.shape[1]
    ffs = ff // shards
    own = width // pieces
    step = pl.program_id(0)

    @pl.when(step == 0)
    def _():
        for acc in (up_acc, down_acc, out_acc, col_acc):
            acc[...] = jnp.zeros_like(acc)
        for i, ref in enumerate(piece_refs):
            here = pl.ds(pl.multiple_of(index_ref[i] * own, 16), own)
            for j in range(shards):
                up_ref[here, j * ffs : (j + 1) * ffs] = ref[2 * j * own : (2 * j + 1) * own]
                down_ref[here, j * ffs : (j + 1) * ffs] = ref[(2 * j + 1) * own : (2 * j + 2) * own]
            out_ref[here, :] = ref[2 * shards * own :]
        upt_ref[...] = up_ref[...].T
        downt_ref[...] = down_ref[...].T
        outt_ref[...] = out_ref[...].T
        load_columns(packed_ref, col_ref, (5, 6))

    def lanes_of(r):
        return slice(r * seq, (r + 1) * seq)

    def spots_of(r):
        return [slice(at, at + LANES) for at in range(r * seq, (r + 1) * seq, LANES)]

    def preparation(r):
        lanes = lanes_of(r)

        def turn():
            ctt_ref[:, lanes] = ct_ref[r].T
            att_cat[:, lanes] = att_ref[r]

        def branch():
            mixed_ref[:, lanes] = mc_ref[r] + mm(outt_ref[...], att_ref[r])

        def norm(t):
            n, scale = norm_columns(mixed_ref[:, t])
            n_ref[:, t] = n
            scale_ref[0:1, t] = scale
            norm_ref[:, t] = (n * col_ref[0] + col_ref[1]).astype(BF)

        return [turn, branch] + [functools.partial(norm, t) for t in spots_of(r)]

    def opening(r):
        lanes = lanes_of(r)

        def up(block):
            pre_ref[block, lanes] = mm(upt_ref[block], norm_ref[:, lanes])

        def down(block):
            gh_ref[block, lanes] = mm(downt_ref[block], ctt_ref[:, lanes])

        return [functools.partial(f, block) for block in tiles(ff, 256) for f in (up, down)]

    def activation(r):
        lanes = lanes_of(r)

        def piece(block):
            for low in range(block.start, block.stop, 32):
                t = slice(low, low + 32)
                hidden, slope = gelu_parts(pre_ref[t, lanes])
                hidden_ref[t, lanes] = hidden.astype(BF)
                gp_ref[t, lanes] = (gh_ref[t, lanes] * slope).astype(BF)

        return [functools.partial(piece, block) for block in tiles(ff, 128)]

    def closing(r):
        lanes = lanes_of(r)

        def grad(part):
            gn_ref[part, lanes] = mm(up_ref[part], gp_ref[:, lanes])

        def out(part):
            mlp = mm(down_ref[part], hidden_ref[:, lanes])
            lot_ref[part, lanes] = (mixed_ref[part, lanes] + mlp).astype(BF)

        return [functools.partial(f, part) for f in (grad, out) for part in tiles(width, width // 3)]

    def norm_back(r):
        spots = spots_of(r)
        mean_e = [jnp.zeros((8, LANES), F32) for _ in spots]
        mean_en = [jnp.zeros((8, LANES), F32) for _ in spots]
        means = []

        def sums(d):
            column = col_ref[0, d]
            gain_sum, shift_sum = col_acc[0, d], col_acc[1, d]
            for i, t in enumerate(spots):
                grad_n = gn_ref[d, t]
                product = grad_n * n_ref[d, t]
                gain_sum += product
                shift_sum += grad_n
                mean_e[i] += fold(grad_n * column)
                mean_en[i] += fold(product * column)
            col_acc[0, d] = gain_sum
            col_acc[1, d] = shift_sum

        def finish():
            for i in range(len(spots)):
                me = jnp.sum(mean_e[i], axis=0, keepdims=True) * (1.0 / width)
                men = jnp.sum(mean_en[i], axis=0, keepdims=True) * (1.0 / width)
                means.append((me, men))

        def apply(d):
            for i, t in enumerate(spots):
                me, men = means[i]
                change = scale_ref[0:1, t] * (gn_ref[d, t] * col_ref[0, d] - me - n_ref[d, t] * men)
                grad_mixed = ctt_ref[d, t].astype(F32) + change
                gm_ref[r, d, i * LANES : (i + 1) * LANES] = grad_mixed
                branch_ref[d, t] = grad_mixed.astype(BF)

        def attended():
            ga_ref[r] = mm(out_ref[...], branch_ref[:, lanes_of(r)]).astype(BF)

        def turn():
            lo_ref[r] = lot_ref[:, lanes_of(r)].T

        pieces = [functools.partial(sums, d) for d in tiles(width, 32)] + [finish]
        return pieces + [functools.partial(apply, d) for d in tiles(width, 32)] + [attended, turn]

    def weights():
        def down(block):
            down_acc[:, block] += mm_nt(ctt_ref[...], hidden_ref[block])

        def up(block):
            up_acc[:, block] += mm_nt(norm_ref[...], gp_ref[block])

        return [functools.partial(f, block) for block in tiles(ff, 256) for f in (down, up)]

    weave(preparation(0))
    weave(opening(0), preparation(1) if rows > 1 else [])
    for r in range(rows):
        beside = opening(r + 1) if r + 1 < rows else []
        beside = (closing(r - 1) if r else []) + beside
        weave(activation(r), beside, preparation(r + 2) if r + 2 < rows else [], norm_back(r - 2) if r > 1 else [])
    weave(closing(rows - 1))
    left = [piece for r in range(max(0, rows - 2), rows) for piece in norm_back(r)]
    weave(weights(), left)
    out_acc[...] += mm_nt(att_cat[...], branch_ref[...])

    @pl.when(step == pl.num_programs(0) - 1)
    def _():
        for i in range(pieces):
            here = pl.ds(pl.multiple_of(index_ref[i] * own, 16), own)
            place = gw_refs[i % groups]
            for j in range(shards):
                cols = slice(j * ffs, (j + 1) * ffs)
                place[i // groups, :, 2 * j * ffs : (2 * j + 1) * ffs] = up_acc[here, cols].astype(BF)
                place[i // groups, :, (2 * j + 1) * ffs : (2 * j + 2) * ffs] = down_acc[here, cols].astype(BF)
            place[i // groups, :, 2 * ff :] = out_acc[here, :].astype(BF)
        gs_ref[...] = jnp.zeros_like(gs_ref)
        for i in range(2):
            gs_ref[5 + i : 6 + i] = jnp.sum(col_acc[i].T, axis=0, keepdims=True)


def backward_attention(
    q_ref, k_ref, v_ref, e_ref, att_ref, inv_ref, norm_ref, ga_ref, index_ref, w_ref, start_ref, gn_ref, *refs, pieces
):
    gw_refs = refs[:-5]
    proj_ref, w_acc, norm_cat, soft_ref, logit_ref = refs[-5:]
    rows, seq, width = v_ref.shape
    own = width // pieces
    head = width // HEADS
    step = pl.program_id(0)

    @pl.when(step == 0)
    def _():
        w_acc[...] = jnp.zeros_like(w_acc) if start_ref is None else start_ref[...]

    zero = jnp.zeros((head, seq), BF)
    work = [(r, h) for r in range(rows) for h in range(HEADS)]

    def opening(r, h):
        part = slice(h * head, (h + 1) * head)
        lanes = slice(h // 2 * 2 * head, (h // 2 + 1) * 2 * head)
        grad_att = ga_ref[r, part].astype(F32) * inv_ref[r, h : h + 1]
        inner = jnp.sum(grad_att * att_ref[r, part].astype(F32), axis=0, keepdims=True)
        grad_att = grad_att.astype(BF)
        pair = [grad_att, zero] if h % 2 == 0 else [zero, grad_att]
        soft_ref[r, h] = mm(v_ref[r, :, lanes], jnp.concatenate(pair, axis=0))
        return grad_att, inner

    ready = opening(*work[0])
    for at, (r, h) in enumerate(work):
        grad_att, inner = ready
        if at + 1 < len(work):
            ready = opening(*work[at + 1])
        for t in tiles(seq, 32):
            raised = e_ref[r, h, t].astype(F32)
            logit_ref[r, h, t] = (raised * (soft_ref[r, h, t] - inner)).astype(BF)
        part = slice(h * head, (h + 1) * head)
        place = slice(r * seq, (r + 1) * seq)
        grad_logits = logit_ref[r, h]
        grad_q = mm(k_ref[r, part], grad_logits) * head ** (-0.5)
        proj_ref[h * head : (h + 1) * head, place] = grad_q.astype(BF)
        grad_k = mm_nt(q_ref[r, part], grad_logits)
        proj_ref[width + h * head : width + (h + 1) * head, place] = grad_k.astype(BF)
        grad_v = mm_nt(grad_att, e_ref[r, h])
        proj_ref[2 * width + h * head : 2 * width + (h + 1) * head, place] = grad_v.astype(BF)
    for r in range(rows):
        norm_cat[:, r * seq : (r + 1) * seq] = norm_ref[r]
        gn_ref[r] = mm(w_ref[...], proj_ref[:, r * seq : (r + 1) * seq]).astype(BF)
    w_acc[...] += mm_nt(norm_cat[...], proj_ref[...])

    @pl.when(step == pl.num_programs(0) - 1)
    def _():
        if start_ref is None:
            gw_refs[0][...] = w_acc[...]
        else:
            groups = len(gw_refs)
            for i in range(pieces):
                here = pl.ds(pl.multiple_of(index_ref[i] * own, 16), own)
                gw_refs[i % groups][i // groups] = w_acc[here, :].astype(BF)


def backward_conv(
    x_ref, aux_ref, mc_ref, gm_ref, gn_ref, packed_ref, other_ref, part_ref, ig_ref, gs_ref,
    acc_ref, col_ref, n_ref, g_ref, turn_ref,
):
    rows, width, seq = x_ref.shape
    step = pl.program_id(0)

    @pl.when(step == 0)
    def _():
        acc_ref[...] = jnp.zeros_like(acc_ref)
        load_columns(packed_ref, col_ref, range(4))

    spots = tiles(seq, LANES)
    for r in range(rows):
        scales = []
        for t in spots:
            n, scale = norm_columns(mc_ref[r, :, t])
            n_ref[r, :, t] = n
            scales.append(scale)
        mean_e = [jnp.zeros((8, LANES), F32) for _ in spots]
        mean_en = [jnp.zeros((8, LANES), F32) for _ in spots]
        for d in tiles(width, 32):
            column = col_ref[3, d]
            gain_sum, shift_sum = acc_ref[3, d], acc_ref[4, d]
            for i, t in enumerate(spots):
                grad_n = gn_ref[r, d, t].astype(F32)
                product = grad_n * n_ref[r, d, t]
                gain_sum += product
                shift_sum += grad_n
                mean_e[i] += fold(grad_n * column)
                mean_en[i] += fold(product * column)
            acc_ref[3, d] = gain_sum
            acc_ref[4, d] = shift_sum
        for i, t in enumerate(spots):
            me = jnp.sum(mean_e[i], axis=0, keepdims=True) * (1.0 / width)
            men = jnp.sum(mean_en[i], axis=0, keepdims=True) * (1.0 / width)
            for d in tiles(width, 64):
                e = gn_ref[r, d, t].astype(F32) * col_ref[3, d]
                g_ref[r, d, t] = gm_ref[r, d, t] + scales[i] * (e - me - n_ref[r, d, t] * men)
        links, next_links = aux_ref[r, 0:1], aux_ref[r, 1:2]
        for d in tiles(width, 32):
            g = g_ref[r, d]
            base = x_ref[r, d].astype(F32)
            before = pltpu.roll(g, 1, 1) * links
            after = pltpu.roll(g, seq - 1, 1) * next_links
            acc_ref[0, d] += fold_lanes(base * after)
            acc_ref[1, d] += fold_lanes(base * g)
            acc_ref[2, d] += fold_lanes(base * before)
            conv0, conv1, conv2 = [twice(col_ref[i, d], seq) for i in range(3)]
            turn_ref[r, d] = (g + conv1 * g + conv0 * after + conv2 * before).astype(BF)
        ig_ref[r] = turn_ref[r].T

    @pl.when(step == pl.num_programs(0) - 1)
    def _():
        gs_ref[...] = other_ref[...]
        for i in range(5):
            gs_ref[i : i + 1] += jnp.sum(acc_ref[i].T, axis=0, keepdims=True)


def in_hbm(values):
    return pltpu.with_memory_space_constraint(values, pltpu.HBM)


def by_row(shape, rows, first=0):
    tail = tuple(shape[1:])
    return pl.BlockSpec((rows,) + tail, lambda i, *_: (i + first,) + (0,) * len(tail))


def whole(shape):
    place = (0,) * len(shape)
    return pl.BlockSpec(tuple(shape), lambda i, *_: place, pipeline_mode=pl.Buffered(1))


def step_rows(count, most):
    return max(r for r in range(1, most + 1) if count % r == 0)


def call(body, name, scalars, rows, row_args, args, row_outs, outs, scratch, span=None, into=None, near=()):
    first, count = span or (0, row_args[0].shape[0])
    skip = first // rows
    in_specs = [by_row(a.shape, rows, skip if a.shape[0] > count else 0) for a in row_args]
    in_specs += [whole(a.shape) for a in args]
    aliases = {}
    if into is not None:
        in_specs.append(pl.BlockSpec(memory_space=pl.ANY))
        aliases = {len(scalars) + len(in_specs) - 1: 0}
    spec = pltpu.PrefetchScalarGridSpec(
        num_scalar_prefetch=len(scalars),
        grid=(count // rows,),
        in_specs=in_specs,
        out_specs=[by_row(s, rows, skip if s[0] > count else 0) for s, _ in row_outs] + [whole(s) for s, _ in outs],
        scratch_shapes=[pltpu.VMEM(s, t) for s, t in scratch],
    )
    return pl.pallas_call(
        body,
        grid_spec=spec,
        out_shape=[(jax.ShapeDtypeStruct if "out" + str(i) in near else pltpu.HBM)(s, t) for i, (s, t) in enumerate(row_outs)]
        + [jax.ShapeDtypeStruct(s, t) for s, t in outs],
        input_output_aliases=aliases,
        compiler_params=pltpu.CompilerParams(dimension_semantics=("arbitrary",), vmem_limit_bytes=VMEM_LIMITS[name] * MIB),
        name=name,
    )(*scalars, *[a if i in near else in_hbm(a) for i, a in enumerate(row_args)], *args, *(() if into is None else (into,)))


def small_call(body, name, args, outs, scratch=()):
    return pl.pallas_call(
        body,
        out_shape=[jax.ShapeDtypeStruct(s, t) for s, t in outs],
        scratch_shapes=[pltpu.VMEM(s, t) for s, t in scratch],
        compiler_params=pltpu.CompilerParams(vmem_limit_bytes=16 * MIB),
        name=name,
    )(*args)


def run_forward(index, tokens, segment_ids, valid_len, pieces):
    count, seq, width = tokens.shape
    flipped = (count, width, seq)
    rows = step_rows(count, 3)
    row_outs = [
        (flipped, BF), (flipped, F32), (flipped, BF), (flipped, BF), (flipped, BF), ((count, seq, width), BF),
        ((count, HEADS, seq, seq), BF), (flipped, BF), ((count, 8, seq), F32), ((count, 8, seq), F32),
    ]
    return call(
        functools.partial(forward_attention, pieces=len(pieces)), "forward_attention", (index, valid_len),
        rows, (tokens,), (in_hbm(segment_ids), *pieces),
        row_outs, [((width, VECTORS), BF), ((width, 3 * width), BF)],
        [
            ((3 * width, width), BF), ((width, 3 * width + VECTORS), BF), ((5, width, LANES), F32),
            ((rows, seq, seq), F32), ((rows, seq, width), BF), ((rows, width, seq), BF), ((rows, HEADS, seq, seq), F32),
        ],
    )


def run_feed_forward(index, att, mixed, cotangent, packed, pieces, shards):
    count, seq, width = cotangent.shape
    own = width // len(pieces)
    ff = shards * width
    groups = 2 if len(pieces) > 1 else 1
    rows = step_rows(count, 3)
    wide = rows * seq
    row_outs = [((count, seq, width), BF), ((count, width, seq), F32), ((count, width, seq), BF)]
    grads = ((len(pieces) // groups, own, 2 * ff + width), BF)
    return call(
        functools.partial(feed_forward, pieces=len(pieces), shards=shards), "feed_forward", (index,),
        rows, (att, mixed, cotangent), (packed, *pieces),
        row_outs, [((8, width), F32)] + [grads] * groups,
        [((width, ff), BF)] * 2 + [((ff, width), BF)] * 2 + [((width, width), BF)] * 2
        + [((width, ff), F32)] * 2 + [((width, width), F32), ((2, width, LANES), F32), ((2, width, LANES), F32)]
        + [((width, wide), BF), ((width, wide), F32), ((width, wide), F32), ((width, wide), BF), ((width, wide), BF)]
        + [((ff, wide), F32)] * 2 + [((ff, wide), BF)] * 2
        + [((width, wide), F32), ((8, wide), F32), ((width, wide), BF), ((width, wide), BF)],
        near=("out2",),
    )


def run_backward_attention(index, weight, kept, grad_att, pieces, span, start):
    count, seq, width = kept[2].shape
    own = width // pieces
    groups = 2 if pieces > 1 else 1
    rows = step_rows(span[1], 2)
    row_args = (*kept, grad_att)
    many = len(row_args)

    def body(index_ref, *refs):
        w_ref, rest = refs[many], refs[many + 1 :]
        start_ref, rest = (None, rest) if start is None else (rest[0], rest[1:])
        backward_attention(*refs[:many], index_ref, w_ref, start_ref, *rest, pieces=pieces)

    outs = [((width, 3 * width), F32)] if start is None else [((pieces // groups, own, 3 * width), BF)] * groups
    return call(
        body, "backward_attention", (index,), rows, row_args, (weight,) if start is None else (weight, start),
        [((span[1], width, seq), BF)], outs,
        [
            ((3 * width, rows * seq), BF), ((width, 3 * width), F32), ((width, rows * seq), BF),
            ((rows, HEADS, seq, seq), F32), ((rows, HEADS, seq, seq), BF),
        ],
        span=span, near=("out0", many - 1),
    )


def run_backward_conv(x, aux, mixed, grad_mixed, grad_normed, packed, other, span, into):
    count, width, seq = x.shape
    rows = step_rows(span[1], 2)

    def body(*refs):
        if into is None:
            backward_conv(*refs[:7], None, *refs[7:])
        else:
            backward_conv(*refs)

    return call(
        body, "backward_conv", (), rows,
        (x, aux, mixed, grad_mixed, grad_normed), (packed, other),
        [((count, seq, width), BF)], [((8, width), F32)],
        [
            ((5, width, LANES), F32), ((4, width, LANES), F32), ((rows, width, seq), F32), ((rows, width, seq), F32),
            ((rows, width, seq), BF),
        ],
        span=span, into=into, near=(4,),
    )


def halves(count):
    early = count // 3
    return ((0, early), (early, count - early)) if early % 2 == 0 and early else ((0, count // 2), (count // 2, count - count // 2))


def exchange(values, axis, offset):
    size = lax.axis_size(axis)
    return lax.ppermute(values, axis, [(i, i ^ offset) for i in range(size)])


def add_halves(mine, received):
    count, own, cols = mine.shape

    def body(mine_ref, received_ref, *out_refs):
        for i, ref in enumerate(out_refs):
            ref[...] = (mine_ref[i].astype(F32) + received_ref[i].astype(F32)).astype(BF)

    return small_call(body, "add_halves", (mine, received), [((own, cols), BF)] * count)


def add_wide(*items):
    return tree_sum(item.astype(F32) for item in items)


def add_shard_vectors(items, own):
    def body(*refs):
        total = tree_sum(ref[...] for ref in refs[:-5])
        refs[-5][...] = total[0:3, :own]
        for i in range(4):
            refs[i - 4][...] = total[3 + i : 4 + i, :own]

    return small_call(body, "add_shard_vectors", items, [((3, own), F32)] + [((1, own), F32)] * 4)


def direct_plan(tokens, segment_ids, valid_len, qkv_weight, out_weight, up_weight, down_weight, conv_weight, vectors, cotangent):
    count, seq, width = tokens.shape
    own, ffs = up_weight.shape
    dp, mp = lax.axis_size("dp"), lax.axis_size("mp")
    me = lax.axis_index("dp")
    offsets = [2 * p for p in range(dp // 2)]
    index = jnp.stack([me ^ (p ^ c) for p in offsets for c in range(2)]).astype(jnp.int32)
    narrow, ff_own = small_call(
        pack_weights, "pack_weights",
        [in_hbm(a) for a in (qkv_weight, up_weight, down_weight, conv_weight, *[v.reshape(1, own) for v in vectors])],
        [((own, 3 * width + VECTORS), BF), ((2 * own, ffs), BF)], [((VECTORS, VECTORS), F32)],
    )
    plane = [narrow] + [exchange(narrow, "dp", p) for p in offsets[1:]]
    shards = [ff_own] + [exchange(ff_own, "mp", j) for j in range(1, mp)]
    pieces = [piece for a in plane for piece in (a, exchange(a, "dp", 1))]
    column = jnp.concatenate(shards + [out_weight], axis=0)
    columns = [column] + [exchange(column, "dp", p) for p in offsets[1:]]
    x, mixed, normed, q, k, v, raised, att, inverse, aux, packed, weight = run_forward(
        index, tokens, segment_ids, valid_len, pieces
    )
    columns, att = lax.optimization_barrier((columns, att))
    pieces = [piece for a in columns for piece in (a, exchange(a, "dp", 1))]
    layer_out, grad_mixed, grad_att, sums2, mine, theirs = run_feed_forward(
        index, att, mixed, cotangent, packed, pieces, mp
    )
    received = exchange(theirs, "dp", 1)
    early, late = halves(count)
    kept = (q, k, v, raised, att, inverse, normed)
    grad_normed1, start = run_backward_attention(index, weight, kept, grad_att, dp, early, None)
    received, start = lax.optimization_barrier((received, start))
    parts = list(add_halves(mine, received))
    parts[0], start = lax.optimization_barrier((parts[0], start))
    plane = [parts[0]] + [exchange(parts[i], "dp", p) for i, p in enumerate(offsets) if i]
    grad_normed2, mine_a, theirs_a = run_backward_attention(index, weight, kept, grad_att, dp, late, start)
    plane, theirs_a = lax.optimization_barrier((plane, theirs_a))
    received_a = exchange(theirs_a, "dp", 1)
    total = add_wide(*plane).astype(BF)
    half = 2 * ffs * (mp // 2)
    near, far, out_part = total[:, :half], total[:, half:], total[:, 2 * half :]
    received_f = exchange(far, "mp", 2)
    near, grad_normed1 = lax.optimization_barrier((near, grad_normed1))
    some_grad, sums = run_backward_conv(x, aux, mixed, grad_mixed, grad_normed1, packed, sums2, early, None)
    received_a, sums = lax.optimization_barrier((received_a, sums))
    parts = list(add_halves(mine_a, received_a))
    parts[0], sums = lax.optimization_barrier((parts[0], sums))
    plane_a = [parts[0]] + [exchange(parts[i], "dp", p) for i, p in enumerate(offsets) if i]
    input_grad, sums = run_backward_conv(x, aux, mixed, grad_mixed, grad_normed2, packed, sums, late, some_grad)
    received_s = exchange(sums, "dp", 1)
    plane_a, received_f, sums = lax.optimization_barrier((plane_a, received_f, sums))
    total = add_wide(*plane_a).astype(BF)
    received_s, total = lax.optimization_barrier((received_s, total))
    received_1 = exchange(total, "mp", 2)
    sums = sums + received_s
    plane_s = [sums] + [exchange(sums, "dp", p) for p in offsets[1:]]
    near_sum = add_wide(near, received_f[:, :half])
    out_sum = lax.optimization_barrier(add_wide(out_part, received_f[:, half:]).astype(BF))
    keep = near_sum[:, : 2 * ffs]
    send = jnp.concatenate([near_sum[:, 2 * ffs :].astype(BF), out_sum], axis=1)
    received_n = exchange(send, "mp", 1)
    plane_s, received_1 = lax.optimization_barrier((plane_s, received_1))
    total = lax.optimization_barrier(add_wide(total, received_1).astype(BF))
    received_2 = exchange(total, "mp", 1)
    vectors = lax.dynamic_slice_in_dim(tree_sum(plane_s), me * own, own, axis=1)
    shards = [vectors] + [exchange(vectors, "mp", j) for j in range(1, mp)]
    grad_up = keep[:, :ffs] + received_n[:, :ffs].astype(F32)
    grad_down = keep[:, ffs:] + received_n[:, ffs : 2 * ffs].astype(F32)
    grad_out = add_wide(out_sum, received_n[:, 2 * ffs :])
    grad_qkv = add_wide(total, received_2)
    grad_conv, *grads = add_shard_vectors(shards, own)
    return (layer_out, input_grad, grad_qkv, grad_out, grad_up, grad_down, grad_conv, *[g.reshape(own) for g in grads])


def gathered_plan(tokens, segment_ids, valid_len, qkv_weight, out_weight, up_weight, down_weight, conv_weight, vectors, cotangent):
    count, seq, width = tokens.shape
    own = qkv_weight.shape[0]
    dp = width // own
    columns = jnp.stack([conv_weight[0], conv_weight[1], conv_weight[2], *vectors], axis=1)
    narrow = jnp.concatenate([qkv_weight, jnp.pad(columns, ((0, 0), (0, VECTORS - 7))), out_weight], axis=1)
    wide = lax.all_gather(narrow, "dp", axis=0, tiled=True)
    both = lax.all_gather(jnp.concatenate([up_weight, down_weight], axis=0), "mp", axis=1, tiled=True)
    ff = both.shape[1]
    shards = ff // width
    both = lax.all_gather(both, "dp", axis=0).reshape(dp, 2, own, shards, width)
    both = both.transpose(3, 1, 0, 2, 4).reshape(2 * ff, width)
    column = jnp.concatenate([both, wide[:, 3 * width + VECTORS :]], axis=0)
    index = jnp.zeros((1,), jnp.int32)
    x, mixed, normed, q, k, v, raised, att, inverse, aux, packed, weight = run_forward(
        index, tokens, segment_ids, valid_len, [wide[:, : 3 * width + VECTORS]]
    )
    layer_out, grad_mixed, grad_att, sums2, grads = run_feed_forward(
        index, att, mixed, cotangent, packed, [column], shards
    )
    early, late = halves(count)
    kept = (q, k, v, raised, att, inverse, normed)
    grad_normed1, start = run_backward_attention(index, weight, kept, grad_att, 1, early, None)
    grad_normed2, grad_qkv = run_backward_attention(index, weight, kept, grad_att, 1, late, start)
    some_grad, sums = run_backward_conv(x, aux, mixed, grad_mixed, grad_normed1, packed, sums2, early, None)
    input_grad, sums = run_backward_conv(x, aux, mixed, grad_mixed, grad_normed2, packed, sums, late, some_grad)
    grad_ff = grads[0, :, : 2 * ff].reshape(width, shards, 2, width).transpose(0, 2, 1, 3).reshape(width, 2 * ff)
    grad_ff = lax.psum_scatter(grad_ff, "dp", scatter_dimension=0, tiled=True).reshape(own, 2, ff)
    grad_ff = lax.psum_scatter(grad_ff, "mp", scatter_dimension=2, tiled=True).astype(F32)
    grad_attn = jnp.concatenate([grad_qkv[0], grads[0, :, 2 * ff :]], axis=1)
    grad_attn = lax.psum_scatter(grad_attn, "dp", scatter_dimension=0, tiled=True)
    grad_attn = lax.psum(grad_attn, "mp").astype(F32)
    sums = lax.psum(sums, ("dp", "mp"))
    sums = lax.dynamic_slice_in_dim(sums, lax.axis_index("dp") * own, own, axis=1)
    return (
        layer_out, input_grad, grad_attn[:, : 3 * width], grad_attn[:, 3 * width :],
        grad_ff[:, 0], grad_ff[:, 1], sums[0:3], sums[3], sums[4], sums[5], sums[6],
    )


def on_device(
    tokens, segment_ids, valid_len, qkv_weight, out_weight, up_weight, down_weight, conv_weight,
    ln1_gain, ln1_shift, ln2_gain, ln2_shift, cotangent,
):
    own, ffs = up_weight.shape
    direct = own % 16 == 0 and ffs == tokens.shape[2] and own <= VECTORS and lax.axis_size("mp") == 4
    plan = direct_plan if direct else gathered_plan
    return plan(
        tokens, segment_ids, valid_len, qkv_weight, out_weight, up_weight, down_weight, conv_weight,
        (ln1_gain, ln1_shift, ln2_gain, ln2_shift), cotangent,
    )


def solution(mesh):
    rows = P(("dp", "mp"), None, None)
    weights = (P("dp", None), P("dp", None), P("dp", "mp"), P("dp", "mp"), P(None, "dp"))
    vectors = (P("dp"),) * 4
    return jax.shard_map(
        on_device,
        mesh=mesh,
        in_specs=(rows, P(("dp", "mp"), None), P(("dp", "mp"))) + weights + vectors + (rows,),
        out_specs=(rows, rows) + weights + vectors,
        check_vma=False,
    )
```

```python
import functools
import math

import jax
import jax.numpy as jnp
from jax import lax
from jax.experimental import pallas as pl
from jax.experimental.pallas import tpu as pltpu
from jax.sharding import PartitionSpec as P

HEADS = 6
VECTORS = 128
LANES = 128
BF = jnp.bfloat16
F32 = jnp.float32
MIB = 1024 * 1024
VMEM_LIMITS = dict(forward_attention=26, feed_forward=36, backward_attention=28, backward_conv=14)


def mm(lhs, rhs):
    return lax.dot_general(lhs, rhs, (((1,), (0,)), ((), ())), preferred_element_type=F32)


def mm_nt(lhs, rhs):
    return lax.dot_general(lhs, rhs, (((1,), (1,)), ((), ())), preferred_element_type=F32)


def tree_sum(items):
    items = list(items)
    while len(items) > 1:
        items = [a + b for a, b in zip(items[::2], items[1::2])]
    return items[0]


def pack_weights(qkv_ref, up_ref, down_ref, conv_ref, g1_ref, s1_ref, g2_ref, s2_ref, narrow_ref, ff_ref, rows_ref):
    own, ffs = up_ref.shape
    rows_ref[...] = jnp.zeros_like(rows_ref)
    rows_ref[0:3, :own] = conv_ref[...].astype(F32)
    for i, ref in enumerate((g1_ref, s1_ref, g2_ref, s2_ref)):
        rows_ref[3 + i : 4 + i, :own] = ref[...].astype(F32)
    wide = qkv_ref.shape[1]
    narrow_ref[:, :wide] = qkv_ref[...]
    narrow_ref[:, wide:] = rows_ref[...].T[:own].astype(BF)
    ff_ref[:own] = up_ref[...]
    ff_ref[own:] = down_ref[...]


def tiles(total, size):
    return [slice(at, at + size) for at in range(0, total, size)]


def weave(*strands):
    strands = [strand for strand in strands if strand]
    total = sum(len(strand) for strand in strands)
    pieces = [((i + 0.5) / len(strand), j, piece) for j, strand in enumerate(strands) for i, piece in enumerate(strand)]
    assert len(pieces) == total
    for _, _, piece in sorted(pieces, key=lambda item: item[:2]):
        piece()


def twice(tile, lanes):
    return jnp.concatenate([tile] * (lanes // LANES), axis=1)


def load_columns(packed_ref, col_ref, places):
    for i, place in enumerate(places):
        column = packed_ref[:, place : place + 1].astype(F32)
        col_ref[i] = jnp.broadcast_to(column, (column.shape[0], LANES))


def column_mean(values):
    return jnp.sum(values, axis=0, keepdims=True) * (1.0 / values.shape[0])


def norm_columns(values):
    centred = values - column_mean(values)
    scale = lax.rsqrt(column_mean(centred * centred) + 1e-06)
    return centred * scale, scale


def fold(values):
    rows, lanes = values.shape
    return jnp.sum(values.reshape(rows // 8, 8, lanes), axis=0)


def fold_lanes(values):
    return sum(values[:, t] for t in tiles(values.shape[1], LANES))


def forward_attention(index_ref, len_ref, tok_ref, seg_ref, *refs, pieces):
    piece_refs = refs[:pieces]
    (
        x_ref, mc_ref, norm_ref, q_ref, k_ref, v_ref, e_ref, att_ref, inv_ref, aux_ref, packed_ref, w_ref,
        wt_ref, wide_ref, col_ref, bias_ref, key_ref, value_ref, score_ref,
    ) = refs[pieces:]
    rows, seq, width = tok_ref.shape
    head = width // HEADS
    step = pl.program_id(0)

    @pl.when(step == 0)
    def _():
        own = width // pieces
        for i, ref in enumerate(piece_refs):
            wide_ref[pl.ds(pl.multiple_of(index_ref[i] * own, 16), own), :] = ref[...]
        w_ref[...] = wide_ref[:, : 3 * width]
        wt_ref[:width] = (wide_ref[:, :width].astype(F32) * head ** (-0.5)).astype(BF).T
        wt_ref[width:] = wide_ref[:, width : 3 * width].T
        packed_ref[...] = wide_ref[:, 3 * width :]
        load_columns(packed_ref, col_ref, range(5))

    place = lax.broadcasted_iota(jnp.int32, (1, seq), 1)
    zero = jnp.zeros((head, seq), BF)

    def preparation(r):
        known = {}

        def start():
            segs = seg_ref[pl.ds(step * rows + r, 1), :].astype(F32)
            valid = place < len_ref[step * rows + r]
            number = jnp.where(valid, segs, -1.0)
            links = jnp.where(valid & (place > 0) & (number == pltpu.roll(number, 1, 1)), 1.0, 0.0)
            next_links = jnp.where(place < seq - 1, pltpu.roll(links, seq - 1, 1), 0.0)
            none = jnp.zeros_like(links)
            aux = jnp.concatenate([links, next_links, number, none, none, none, none, none], axis=0)
            aux_ref[r] = aux
            x_ref[r] = tok_ref[r].T
            known.update(segs=segs, links=links, next_links=next_links, key_number=aux.T[:, 2:3])

        def mask(t):
            row_id = lax.broadcasted_iota(jnp.int32, (64, seq), 0) + t.start
            col_id = lax.broadcasted_iota(jnp.int32, (64, seq), 1)
            allowed = (known["key_number"][t] == known["segs"]) | (row_id == col_id)
            bias_ref[r, t] = jnp.where(allowed, 0.0, -1e30)

        def conv(t):
            base = x_ref[r, t].astype(F32)
            before = pltpu.roll(base, 1, 1) * known["links"]
            after = pltpu.roll(base, seq - 1, 1) * known["next_links"]
            conv0, conv1, conv2 = [twice(col_ref[i, t], seq) for i in range(3)]
            mc_ref[r, t] = base + before * conv0 + base * conv1 + after * conv2

        def norm(t):
            n, _ = norm_columns(mc_ref[r, :, t])
            norm_ref[r, :, t] = (n * col_ref[3] + col_ref[4]).astype(BF)

        pieces = [start] + [functools.partial(conv, t) for t in tiles(width, 32)]
        pieces += [functools.partial(norm, t) for t in tiles(seq, LANES)]
        return pieces + [functools.partial(mask, t) for t in tiles(seq, 64)]

    def project():
        normed = jnp.concatenate([norm_ref[r] for r in range(rows)], axis=1)
        for i, ref in enumerate((q_ref, k_ref, value_ref)):
            part = mm(wt_ref[i * width : (i + 1) * width], normed).astype(BF)
            for r in range(rows):
                ref[r] = part[:, r * seq : (r + 1) * seq]
        for r in range(rows):
            key_ref[r] = k_ref[r].T
            v_ref[r] = value_ref[r].T

    def scores(r, p):
        low, high = [q_ref[r, h * head : (h + 1) * head] for h in (2 * p, 2 * p + 1)]
        both = jnp.concatenate([jnp.concatenate([low, zero], axis=1), jnp.concatenate([zero, high], axis=1)], axis=0)
        product = mm(key_ref[r, :, 2 * p * head : 2 * (p + 1) * head], both)
        score_ref[r, 2 * p] = product[:, :seq]
        score_ref[r, 2 * p + 1] = product[:, seq:]

    def soften(r, h, t):
        masked = score_ref[r, h, :, t] + bias_ref[r, :, t]
        raised = jnp.exp(masked - jnp.max(masked, axis=0, keepdims=True))
        inv_ref[r, h : h + 1, t] = 1.0 / jnp.sum(raised, axis=0, keepdims=True)
        e_ref[r, h, :, t] = raised.astype(BF)

    def attend(r, p):
        both = jnp.concatenate([e_ref[r, 2 * p], e_ref[r, 2 * p + 1]], axis=1)
        product = mm(value_ref[r, 2 * p * head : 2 * (p + 1) * head], both)
        for i in range(2):
            h = 2 * p + i
            att = product[i * head : (i + 1) * head, i * seq : (i + 1) * seq] * inv_ref[r, h : h + 1]
            att_ref[r, h * head : (h + 1) * head] = att.astype(BF)

    weave(*[preparation(r) for r in range(rows)])
    project()
    work = [(r, p) for r in range(rows) for p in range(HEADS // 2)]
    scores(*work[0])
    for at, (r, p) in enumerate(work):
        if at + 1 < len(work):
            scores(*work[at + 1])
        for h in (2 * p, 2 * p + 1):
            for t in tiles(seq, LANES):
                soften(r, h, t)
        attend(r, p)


def gelu_parts(x):
    cdf = 0.5 * lax.erf(x * math.sqrt(0.5)) + 0.5
    bell = jnp.exp2(x * x * (-0.5 / math.log(2.0)) - 0.5 * math.log2(2.0 * math.pi))
    return x * cdf, cdf + x * bell


def feed_forward(index_ref, att_ref, mc_ref, ct_ref, packed_ref, *refs, pieces, shards):
    piece_refs = refs[:pieces]
    groups = 2 if pieces > 1 else 1
    lo_ref, gm_ref, ga_ref, gs_ref = refs[pieces : pieces + 4]
    gw_refs = refs[pieces + 4 : pieces + 4 + groups]
    (
        up_ref, down_ref, upt_ref, downt_ref, out_ref, outt_ref, up_acc, down_acc, out_acc, col_acc, col_ref,
        att_cat, mixed_ref, n_ref, norm_ref, ctt_ref, hidden_ref, gp_ref, gn_ref, scale_ref, lot_ref,
        branch_ref,
    ) = refs[pieces + 4 + groups :]
    rows, seq, width = ct_ref.shape
    ff = up_ref.shape[1]
    ffs = ff // shards
    own = width // pieces
    step = pl.program_id(0)

    @pl.when(step == 0)
    def _():
        for acc in (up_acc, down_acc, out_acc, col_acc):
            acc[...] = jnp.zeros_like(acc)
        for i, ref in enumerate(piece_refs):
            here = pl.ds(pl.multiple_of(index_ref[i] * own, 16), own)
            for j in range(shards):
                up_ref[here, j * ffs : (j + 1) * ffs] = ref[2 * j * own : (2 * j + 1) * own]
                down_ref[here, j * ffs : (j + 1) * ffs] = ref[(2 * j + 1) * own : (2 * j + 2) * own]
            out_ref[here, :] = ref[2 * shards * own :]
        upt_ref[...] = up_ref[...].T
        downt_ref[...] = down_ref[...].T
        outt_ref[...] = out_ref[...].T
        load_columns(packed_ref, col_ref, (5, 6))

    def lanes_of(r):
        return slice(r * seq, (r + 1) * seq)

    def spots_of(r):
        return [slice(at, at + LANES) for at in range(r * seq, (r + 1) * seq, LANES)]

    def preparation(r):
        lanes = lanes_of(r)

        def turn():
            ctt_ref[:, lanes] = ct_ref[r].T
            att_cat[:, lanes] = att_ref[r]

        def branch():
            mixed_ref[:, lanes] = mc_ref[r] + mm(outt_ref[...], att_ref[r])

        def norm(t):
            n, scale = norm_columns(mixed_ref[:, t])
            n_ref[:, t] = n
            scale_ref[0:1, t] = scale
            norm_ref[:, t] = (n * col_ref[0] + col_ref[1]).astype(BF)

        return [turn, branch] + [functools.partial(norm, t) for t in spots_of(r)]

    def activation(block):
        pre = mm(upt_ref[block], norm_ref[...])
        grad_hidden = mm(downt_ref[block], ctt_ref[...])
        for low in range(0, block.stop - block.start, 16):
            part = slice(low, low + 16)
            here = slice(block.start + low, block.start + low + 16)
            hidden, slope = gelu_parts(pre[part])
            hidden_ref[here] = hidden.astype(BF)
            gp_ref[here] = (grad_hidden[part] * slope).astype(BF)

    def norm_back(r):
        spots = spots_of(r)
        mean_e = [jnp.zeros((8, LANES), F32) for _ in spots]
        mean_en = [jnp.zeros((8, LANES), F32) for _ in spots]
        means = []

        def sums(d):
            column = col_ref[0, d]
            gain_sum, shift_sum = col_acc[0, d], col_acc[1, d]
            for i, t in enumerate(spots):
                grad_n = gn_ref[d, t]
                product = grad_n * n_ref[d, t]
                gain_sum += product
                shift_sum += grad_n
                mean_e[i] += fold(grad_n * column)
                mean_en[i] += fold(product * column)
            col_acc[0, d] = gain_sum
            col_acc[1, d] = shift_sum

        def finish():
            for i in range(len(spots)):
                me = jnp.sum(mean_e[i], axis=0, keepdims=True) * (1.0 / width)
                men = jnp.sum(mean_en[i], axis=0, keepdims=True) * (1.0 / width)
                means.append((me, men))

        def apply(d):
            for i, t in enumerate(spots):
                me, men = means[i]
                change = scale_ref[0:1, t] * (gn_ref[d, t] * col_ref[0, d] - me - n_ref[d, t] * men)
                grad_mixed = ctt_ref[d, t].astype(F32) + change
                gm_ref[r, d, i * LANES : (i + 1) * LANES] = grad_mixed
                branch_ref[d, t] = grad_mixed.astype(BF)

        def attended():
            ga_ref[r] = mm(out_ref[...], branch_ref[:, lanes_of(r)]).astype(BF)

        def turn():
            lo_ref[r] = lot_ref[:, lanes_of(r)].T

        pieces = [functools.partial(sums, d) for d in tiles(width, 32)] + [finish]
        return pieces + [functools.partial(apply, d) for d in tiles(width, 32)] + [attended, turn]

    weave(*[preparation(r) for r in range(rows)])
    for block in tiles(ff, 128):
        activation(block)
    gn_ref[...] = mm(up_ref[...], gp_ref[...])
    lot_ref[...] = (mixed_ref[...] + mm(down_ref[...], hidden_ref[...])).astype(BF)
    down_acc[...] += mm_nt(ctt_ref[...], hidden_ref[...])
    up_acc[...] += mm_nt(norm_ref[...], gp_ref[...])
    weave(*[norm_back(r) for r in range(rows)])
    out_acc[...] += mm_nt(att_cat[...], branch_ref[...])

    @pl.when(step == pl.num_programs(0) - 1)
    def _():
        for i in range(pieces):
            here = pl.ds(pl.multiple_of(index_ref[i] * own, 16), own)
            place = gw_refs[i % groups]
            for j in range(shards):
                cols = slice(j * ffs, (j + 1) * ffs)
                place[i // groups, :, 2 * j * ffs : (2 * j + 1) * ffs] = up_acc[here, cols].astype(BF)
                place[i // groups, :, (2 * j + 1) * ffs : (2 * j + 2) * ffs] = down_acc[here, cols].astype(BF)
            place[i // groups, :, 2 * ff :] = out_acc[here, :].astype(BF)
        gs_ref[...] = jnp.zeros_like(gs_ref)
        for i in range(2):
            gs_ref[5 + i : 6 + i] = jnp.sum(col_acc[i].T, axis=0, keepdims=True)


def backward_attention(
    q_ref, k_ref, v_ref, e_ref, att_ref, inv_ref, norm_ref, ga_ref, index_ref, w_ref, start_ref, gn_ref, *refs, pieces
):
    gw_refs = refs[:-5]
    proj_ref, w_acc, norm_cat, soft_ref, logit_ref = refs[-5:]
    rows, seq, width = v_ref.shape
    own = width // pieces
    head = width // HEADS
    step = pl.program_id(0)

    @pl.when(step == 0)
    def _():
        w_acc[...] = jnp.zeros_like(w_acc) if start_ref is None else start_ref[...]

    zero = jnp.zeros((head, seq), BF)
    work = [(r, p) for r in range(rows) for p in range(HEADS // 2)]

    def opening(r, p):
        grads, inners = [], []
        for h in (2 * p, 2 * p + 1):
            part = slice(h * head, (h + 1) * head)
            grad_att = ga_ref[r, part].astype(F32) * inv_ref[r, h : h + 1]
            inners.append(jnp.sum(grad_att * att_ref[r, part].astype(F32), axis=0, keepdims=True))
            grads.append(grad_att.astype(BF))
        low, high = grads
        both = jnp.concatenate([jnp.concatenate([low, zero], axis=1), jnp.concatenate([zero, high], axis=1)], axis=0)
        product = mm(v_ref[r, :, 2 * p * head : 2 * (p + 1) * head], both)
        soft_ref[r, 2 * p] = product[:, :seq]
        soft_ref[r, 2 * p + 1] = product[:, seq:]
        return jnp.concatenate(grads, axis=0), inners

    ready = opening(*work[0])
    for at, (r, p) in enumerate(work):
        grad_att, inners = ready
        if at + 1 < len(work):
            ready = opening(*work[at + 1])
        for i, h in enumerate((2 * p, 2 * p + 1)):
            for t in tiles(seq, 32):
                raised = e_ref[r, h, t].astype(F32)
                logit_ref[r, h, t] = (raised * (soft_ref[r, h, t] - inners[i])).astype(BF)
        part = slice(2 * p * head, 2 * (p + 1) * head)
        pair = slice(2 * p, 2 * p + 2)
        beside = jnp.concatenate([logit_ref[r, 2 * p], logit_ref[r, 2 * p + 1]], axis=1)
        grad_q = mm(k_ref[r, part], beside)
        grad_k = mm_nt(q_ref[r, part], logit_ref[r, pair].reshape(2 * seq, seq))
        grad_v = mm_nt(grad_att, e_ref[r, pair].reshape(2 * seq, seq))
        for i in range(2):
            place = slice(r * seq, (r + 1) * seq)
            own_rows, own_cols = slice(i * head, (i + 1) * head), slice(i * seq, (i + 1) * seq)
            for j, grad in enumerate((grad_q, grad_k, grad_v)):
                first = j * width + (2 * p + i) * head
                mine = grad[own_rows, own_cols]
                proj_ref[first : first + head, place] = (mine * head ** (-0.5) if j == 0 else mine).astype(BF)
    grad_normed = mm(w_ref[...], proj_ref[...]).astype(BF)
    for r in range(rows):
        norm_cat[:, r * seq : (r + 1) * seq] = norm_ref[r]
        gn_ref[r] = grad_normed[:, r * seq : (r + 1) * seq]
    w_acc[...] += mm_nt(norm_cat[...], proj_ref[...])

    @pl.when(step == pl.num_programs(0) - 1)
    def _():
        if start_ref is None:
            gw_refs[0][...] = w_acc[...]
        else:
            groups = len(gw_refs)
            for i in range(pieces):
                here = pl.ds(pl.multiple_of(index_ref[i] * own, 16), own)
                gw_refs[i % groups][i // groups] = w_acc[here, :].astype(BF)


def backward_conv(
    x_ref, aux_ref, mc_ref, gm_ref, gn_ref, packed_ref, other_ref, part_ref, ig_ref, gs_ref,
    acc_ref, col_ref, n_ref, g_ref, turn_ref,
):
    rows, width, seq = x_ref.shape
    step = pl.program_id(0)

    @pl.when(step == 0)
    def _():
        acc_ref[...] = jnp.zeros_like(acc_ref)
        load_columns(packed_ref, col_ref, range(4))

    spots = tiles(seq, LANES)
    for r in range(rows):
        scales = []
        for t in spots:
            n, scale = norm_columns(mc_ref[r, :, t])
            n_ref[r, :, t] = n
            scales.append(scale)
        mean_e = [jnp.zeros((8, LANES), F32) for _ in spots]
        mean_en = [jnp.zeros((8, LANES), F32) for _ in spots]
        for d in tiles(width, 32):
            column = col_ref[3, d]
            gain_sum, shift_sum = acc_ref[3, d], acc_ref[4, d]
            for i, t in enumerate(spots):
                grad_n = gn_ref[r, d, t].astype(F32)
                product = grad_n * n_ref[r, d, t]
                gain_sum += product
                shift_sum += grad_n
                mean_e[i] += fold(grad_n * column)
                mean_en[i] += fold(product * column)
            acc_ref[3, d] = gain_sum
            acc_ref[4, d] = shift_sum
        for i, t in enumerate(spots):
            me = jnp.sum(mean_e[i], axis=0, keepdims=True) * (1.0 / width)
            men = jnp.sum(mean_en[i], axis=0, keepdims=True) * (1.0 / width)
            for d in tiles(width, 64):
                e = gn_ref[r, d, t].astype(F32) * col_ref[3, d]
                g_ref[r, d, t] = gm_ref[r, d, t] + scales[i] * (e - me - n_ref[r, d, t] * men)
        links, next_links = aux_ref[r, 0:1], aux_ref[r, 1:2]
        for d in tiles(width, 32):
            g = g_ref[r, d]
            base = x_ref[r, d].astype(F32)
            before = pltpu.roll(g, 1, 1) * links
            after = pltpu.roll(g, seq - 1, 1) * next_links
            acc_ref[0, d] += fold_lanes(base * after)
            acc_ref[1, d] += fold_lanes(base * g)
            acc_ref[2, d] += fold_lanes(base * before)
            conv0, conv1, conv2 = [twice(col_ref[i, d], seq) for i in range(3)]
            turn_ref[r, d] = (g + conv1 * g + conv0 * after + conv2 * before).astype(BF)
        ig_ref[r] = turn_ref[r].T

    @pl.when(step == pl.num_programs(0) - 1)
    def _():
        gs_ref[...] = other_ref[...]
        for i in range(5):
            gs_ref[i : i + 1] += jnp.sum(acc_ref[i].T, axis=0, keepdims=True)


def in_hbm(values):
    return pltpu.with_memory_space_constraint(values, pltpu.HBM)


def by_row(shape, rows, first=0):
    tail = tuple(shape[1:])
    return pl.BlockSpec((rows,) + tail, lambda i, *_: (i + first,) + (0,) * len(tail))


def whole(shape):
    place = (0,) * len(shape)
    return pl.BlockSpec(tuple(shape), lambda i, *_: place, pipeline_mode=pl.Buffered(1))


def step_rows(count, most):
    return max(r for r in range(1, most + 1) if count % r == 0)


def call(body, name, scalars, rows, row_args, args, row_outs, outs, scratch, span=None, into=None, near=()):
    first, count = span or (0, row_args[0].shape[0])
    skip = first // rows
    in_specs = [by_row(a.shape, rows, skip if a.shape[0] > count else 0) for a in row_args]
    in_specs += [whole(a.shape) for a in args]
    aliases = {}
    if into is not None:
        in_specs.append(pl.BlockSpec(memory_space=pl.ANY))
        aliases = {len(scalars) + len(in_specs) - 1: 0}
    spec = pltpu.PrefetchScalarGridSpec(
        num_scalar_prefetch=len(scalars),
        grid=(count // rows,),
        in_specs=in_specs,
        out_specs=[by_row(s, rows, skip if s[0] > count else 0) for s, _ in row_outs] + [whole(s) for s, _ in outs],
        scratch_shapes=[pltpu.VMEM(s, t) for s, t in scratch],
    )
    return pl.pallas_call(
        body,
        grid_spec=spec,
        out_shape=[(jax.ShapeDtypeStruct if "out" + str(i) in near else pltpu.HBM)(s, t) for i, (s, t) in enumerate(row_outs)]
        + [jax.ShapeDtypeStruct(s, t) for s, t in outs],
        input_output_aliases=aliases,
        compiler_params=pltpu.CompilerParams(dimension_semantics=("arbitrary",), vmem_limit_bytes=VMEM_LIMITS[name] * MIB),
        name=name,
    )(*scalars, *[a if i in near else in_hbm(a) for i, a in enumerate(row_args)], *args, *(() if into is None else (into,)))


def small_call(body, name, args, outs, scratch=()):
    return pl.pallas_call(
        body,
        out_shape=[jax.ShapeDtypeStruct(s, t) for s, t in outs],
        scratch_shapes=[pltpu.VMEM(s, t) for s, t in scratch],
        compiler_params=pltpu.CompilerParams(vmem_limit_bytes=16 * MIB),
        name=name,
    )(*args)


def run_forward(index, tokens, segment_ids, valid_len, pieces):
    count, seq, width = tokens.shape
    flipped = (count, width, seq)
    rows = step_rows(count, 2)
    row_outs = [
        (flipped, BF), (flipped, F32), (flipped, BF), (flipped, BF), (flipped, BF), ((count, seq, width), BF),
        ((count, HEADS, seq, seq), BF), (flipped, BF), ((count, 8, seq), F32), ((count, 8, seq), F32),
    ]
    return call(
        functools.partial(forward_attention, pieces=len(pieces)), "forward_attention", (index, valid_len),
        rows, (tokens,), (in_hbm(segment_ids), *pieces),
        row_outs, [((width, VECTORS), BF), ((width, 3 * width), BF)],
        [
            ((3 * width, width), BF), ((width, 3 * width + VECTORS), BF), ((5, width, LANES), F32),
            ((rows, seq, seq), F32), ((rows, seq, width), BF), ((rows, width, seq), BF), ((rows, HEADS, seq, seq), F32),
        ],
    )


def run_feed_forward(index, att, mixed, cotangent, packed, pieces, shards):
    count, seq, width = cotangent.shape
    own = width // len(pieces)
    ff = shards * width
    groups = 2 if len(pieces) > 1 else 1
    rows = step_rows(count, 2)
    wide = rows * seq
    row_outs = [((count, seq, width), BF), ((count, width, seq), F32), ((count, width, seq), BF)]
    grads = ((len(pieces) // groups, own, 2 * ff + width), BF)
    return call(
        functools.partial(feed_forward, pieces=len(pieces), shards=shards), "feed_forward", (index,),
        rows, (att, mixed, cotangent), (packed, *pieces),
        row_outs, [((8, width), F32)] + [grads] * groups,
        [((width, ff), BF)] * 2 + [((ff, width), BF)] * 2 + [((width, width), BF)] * 2
        + [((width, ff), F32)] * 2 + [((width, width), F32), ((2, width, LANES), F32), ((2, width, LANES), F32)]
        + [((width, wide), BF), ((width, wide), F32), ((width, wide), F32), ((width, wide), BF), ((width, wide), BF)]
        + [((ff, wide), BF)] * 2
        + [((width, wide), F32), ((8, wide), F32), ((width, wide), BF), ((width, wide), BF)],
        near=("out2",),
    )


def run_backward_attention(index, weight, kept, grad_att, pieces, span, start):
    count, seq, width = kept[2].shape
    own = width // pieces
    groups = 2 if pieces > 1 else 1
    rows = step_rows(span[1], 2)
    row_args = (*kept, grad_att)
    many = len(row_args)

    def body(index_ref, *refs):
        w_ref, rest = refs[many], refs[many + 1 :]
        start_ref, rest = (None, rest) if start is None else (rest[0], rest[1:])
        backward_attention(*refs[:many], index_ref, w_ref, start_ref, *rest, pieces=pieces)

    outs = [((width, 3 * width), F32)] if start is None else [((pieces // groups, own, 3 * width), BF)] * groups
    return call(
        body, "backward_attention", (index,), rows, row_args, (weight,) if start is None else (weight, start),
        [((span[1], width, seq), BF)], outs,
        [
            ((3 * width, rows * seq), BF), ((width, 3 * width), F32), ((width, rows * seq), BF),
            ((rows, HEADS, seq, seq), F32), ((rows, HEADS, seq, seq), BF),
        ],
        span=span, near=("out0", many - 1),
    )


def run_backward_conv(x, aux, mixed, grad_mixed, grad_normed, packed, other, span, into):
    count, width, seq = x.shape
    rows = step_rows(span[1], 2)

    def body(*refs):
        if into is None:
            backward_conv(*refs[:7], None, *refs[7:])
        else:
            backward_conv(*refs)

    return call(
        body, "backward_conv", (), rows,
        (x, aux, mixed, grad_mixed, grad_normed), (packed, other),
        [((count, seq, width), BF)], [((8, width), F32)],
        [
            ((5, width, LANES), F32), ((4, width, LANES), F32), ((rows, width, seq), F32), ((rows, width, seq), F32),
            ((rows, width, seq), BF),
        ],
        span=span, into=into, near=(4,),
    )


def halves(count):
    early = count // 3
    return ((0, early), (early, count - early)) if early % 2 == 0 and early else ((0, count // 2), (count // 2, count - count // 2))


def exchange(values, axis, offset):
    size = lax.axis_size(axis)
    return lax.ppermute(values, axis, [(i, i ^ offset) for i in range(size)])


def add_halves(mine, received):
    count, own, cols = mine.shape

    def body(mine_ref, received_ref, *out_refs):
        for i, ref in enumerate(out_refs):
            ref[...] = (mine_ref[i].astype(F32) + received_ref[i].astype(F32)).astype(BF)

    return small_call(body, "add_halves", (mine, received), [((own, cols), BF)] * count)


def add_wide(*items):
    return tree_sum(item.astype(F32) for item in items)


def add_shard_vectors(items, own):
    def body(*refs):
        total = tree_sum(ref[...] for ref in refs[:-5])
        refs[-5][...] = total[0:3, :own]
        for i in range(4):
            refs[i - 4][...] = total[3 + i : 4 + i, :own]

    return small_call(body, "add_shard_vectors", items, [((3, own), F32)] + [((1, own), F32)] * 4)


def direct_plan(tokens, segment_ids, valid_len, qkv_weight, out_weight, up_weight, down_weight, conv_weight, vectors, cotangent):
    count, seq, width = tokens.shape
    own, ffs = up_weight.shape
    dp, mp = lax.axis_size("dp"), lax.axis_size("mp")
    me = lax.axis_index("dp")
    offsets = [2 * p for p in range(dp // 2)]
    index = jnp.stack([me ^ (p ^ c) for p in offsets for c in range(2)]).astype(jnp.int32)
    narrow, ff_own = small_call(
        pack_weights, "pack_weights",
        [in_hbm(a) for a in (qkv_weight, up_weight, down_weight, conv_weight, *[v.reshape(1, own) for v in vectors])],
        [((own, 3 * width + VECTORS), BF), ((2 * own, ffs), BF)], [((VECTORS, VECTORS), F32)],
    )
    plane = [narrow] + [exchange(narrow, "dp", p) for p in offsets[1:]]
    shards = [ff_own] + [exchange(ff_own, "mp", j) for j in range(1, mp)]
    pieces = [piece for a in plane for piece in (a, exchange(a, "dp", 1))]
    column = jnp.concatenate(shards + [out_weight], axis=0)
    columns = [column] + [exchange(column, "dp", p) for p in offsets[1:]]
    x, mixed, normed, q, k, v, raised, att, inverse, aux, packed, weight = run_forward(
        index, tokens, segment_ids, valid_len, pieces
    )
    columns, att = lax.optimization_barrier((columns, att))
    pieces = [piece for a in columns for piece in (a, exchange(a, "dp", 1))]
    layer_out, grad_mixed, grad_att, sums2, mine, theirs = run_feed_forward(
        index, att, mixed, cotangent, packed, pieces, mp
    )
    received = exchange(theirs, "dp", 1)
    early, late = halves(count)
    kept = (q, k, v, raised, att, inverse, normed)
    grad_normed1, start = run_backward_attention(index, weight, kept, grad_att, dp, early, None)
    received, start = lax.optimization_barrier((received, start))
    parts = list(add_halves(mine, received))
    parts[0], start = lax.optimization_barrier((parts[0], start))
    plane = [parts[0]] + [exchange(parts[i], "dp", p) for i, p in enumerate(offsets) if i]
    grad_normed2, mine_a, theirs_a = run_backward_attention(index, weight, kept, grad_att, dp, late, start)
    plane, theirs_a = lax.optimization_barrier((plane, theirs_a))
    received_a = exchange(theirs_a, "dp", 1)
    total = add_wide(*plane).astype(BF)
    half = 2 * ffs * (mp // 2)
    near, far, out_part = total[:, :half], total[:, half:], total[:, 2 * half :]
    received_f = exchange(far, "mp", 2)
    near, grad_normed1 = lax.optimization_barrier((near, grad_normed1))
    some_grad, sums = run_backward_conv(x, aux, mixed, grad_mixed, grad_normed1, packed, sums2, early, None)
    received_a, sums = lax.optimization_barrier((received_a, sums))
    parts = list(add_halves(mine_a, received_a))
    parts[0], sums = lax.optimization_barrier((parts[0], sums))
    plane_a = [parts[0]] + [exchange(parts[i], "dp", p) for i, p in enumerate(offsets) if i]
    input_grad, sums = run_backward_conv(x, aux, mixed, grad_mixed, grad_normed2, packed, sums, late, some_grad)
    received_s = exchange(sums, "dp", 1)
    plane_a, received_f, sums = lax.optimization_barrier((plane_a, received_f, sums))
    total = add_wide(*plane_a).astype(BF)
    received_s, total = lax.optimization_barrier((received_s, total))
    received_1 = exchange(total, "mp", 2)
    sums = sums + received_s
    plane_s = [sums] + [exchange(sums, "dp", p) for p in offsets[1:]]
    near_sum = add_wide(near, received_f[:, :half])
    out_sum = lax.optimization_barrier(add_wide(out_part, received_f[:, half:]).astype(BF))
    keep = near_sum[:, : 2 * ffs]
    send = jnp.concatenate([near_sum[:, 2 * ffs :].astype(BF), out_sum], axis=1)
    received_n = exchange(send, "mp", 1)
    plane_s, received_1 = lax.optimization_barrier((plane_s, received_1))
    total = lax.optimization_barrier(add_wide(total, received_1).astype(BF))
    received_2 = exchange(total, "mp", 1)
    vectors = lax.dynamic_slice_in_dim(tree_sum(plane_s), me * own, own, axis=1)
    shards = [vectors] + [exchange(vectors, "mp", j) for j in range(1, mp)]
    grad_up = keep[:, :ffs] + received_n[:, :ffs].astype(F32)
    grad_down = keep[:, ffs:] + received_n[:, ffs : 2 * ffs].astype(F32)
    grad_out = add_wide(out_sum, received_n[:, 2 * ffs :])
    grad_qkv = add_wide(total, received_2)
    grad_conv, *grads = add_shard_vectors(shards, own)
    return (layer_out, input_grad, grad_qkv, grad_out, grad_up, grad_down, grad_conv, *[g.reshape(own) for g in grads])


def gathered_plan(tokens, segment_ids, valid_len, qkv_weight, out_weight, up_weight, down_weight, conv_weight, vectors, cotangent):
    count, seq, width = tokens.shape
    own = qkv_weight.shape[0]
    dp = width // own
    columns = jnp.stack([conv_weight[0], conv_weight[1], conv_weight[2], *vectors], axis=1)
    narrow = jnp.concatenate([qkv_weight, jnp.pad(columns, ((0, 0), (0, VECTORS - 7))), out_weight], axis=1)
    wide = lax.all_gather(narrow, "dp", axis=0, tiled=True)
    both = lax.all_gather(jnp.concatenate([up_weight, down_weight], axis=0), "mp", axis=1, tiled=True)
    ff = both.shape[1]
    shards = ff // width
    both = lax.all_gather(both, "dp", axis=0).reshape(dp, 2, own, shards, width)
    both = both.transpose(3, 1, 0, 2, 4).reshape(2 * ff, width)
    column = jnp.concatenate([both, wide[:, 3 * width + VECTORS :]], axis=0)
    index = jnp.zeros((1,), jnp.int32)
    x, mixed, normed, q, k, v, raised, att, inverse, aux, packed, weight = run_forward(
        index, tokens, segment_ids, valid_len, [wide[:, : 3 * width + VECTORS]]
    )
    layer_out, grad_mixed, grad_att, sums2, grads = run_feed_forward(
        index, att, mixed, cotangent, packed, [column], shards
    )
    early, late = halves(count)
    kept = (q, k, v, raised, att, inverse, normed)
    grad_normed1, start = run_backward_attention(index, weight, kept, grad_att, 1, early, None)
    grad_normed2, grad_qkv = run_backward_attention(index, weight, kept, grad_att, 1, late, start)
    some_grad, sums = run_backward_conv(x, aux, mixed, grad_mixed, grad_normed1, packed, sums2, early, None)
    input_grad, sums = run_backward_conv(x, aux, mixed, grad_mixed, grad_normed2, packed, sums, late, some_grad)
    grad_ff = grads[0, :, : 2 * ff].reshape(width, shards, 2, width).transpose(0, 2, 1, 3).reshape(width, 2 * ff)
    grad_ff = lax.psum_scatter(grad_ff, "dp", scatter_dimension=0, tiled=True).reshape(own, 2, ff)
    grad_ff = lax.psum_scatter(grad_ff, "mp", scatter_dimension=2, tiled=True).astype(F32)
    grad_attn = jnp.concatenate([grad_qkv[0], grads[0, :, 2 * ff :]], axis=1)
    grad_attn = lax.psum_scatter(grad_attn, "dp", scatter_dimension=0, tiled=True)
    grad_attn = lax.psum(grad_attn, "mp").astype(F32)
    sums = lax.psum(sums, ("dp", "mp"))
    sums = lax.dynamic_slice_in_dim(sums, lax.axis_index("dp") * own, own, axis=1)
    return (
        layer_out, input_grad, grad_attn[:, : 3 * width], grad_attn[:, 3 * width :],
        grad_ff[:, 0], grad_ff[:, 1], sums[0:3], sums[3], sums[4], sums[5], sums[6],
    )


def on_device(
    tokens, segment_ids, valid_len, qkv_weight, out_weight, up_weight, down_weight, conv_weight,
    ln1_gain, ln1_shift, ln2_gain, ln2_shift, cotangent,
):
    own, ffs = up_weight.shape
    direct = own % 16 == 0 and ffs == tokens.shape[2] and own <= VECTORS and lax.axis_size("mp") == 4
    plan = direct_plan if direct else gathered_plan
    return plan(
        tokens, segment_ids, valid_len, qkv_weight, out_weight, up_weight, down_weight, conv_weight,
        (ln1_gain, ln1_shift, ln2_gain, ln2_shift), cotangent,
    )


def solution(mesh):
    rows = P(("dp", "mp"), None, None)
    weights = (P("dp", None), P("dp", None), P("dp", "mp"), P("dp", "mp"), P(None, "dp"))
    vectors = (P("dp"),) * 4
    return jax.shard_map(
        on_device,
        mesh=mesh,
        in_specs=(rows, P(("dp", "mp"), None), P(("dp", "mp"))) + weights + vectors + (rows,),
        out_specs=(rows, rows) + weights + vectors,
        check_vma=False,
    )
```

```python
import functools
import math

import jax
import jax.numpy as jnp
from jax import lax
from jax.experimental import pallas as pl
from jax.experimental.pallas import tpu as pltpu
from jax.sharding import PartitionSpec as P

HEADS = 6
VECTORS = 128
LANES = 128
BF = jnp.bfloat16
F32 = jnp.float32
MIB = 1024 * 1024
VMEM_LIMITS = dict(forward_attention=26, feed_forward=36, backward_attention=28, backward_conv=14)


def mm(lhs, rhs):
    return lax.dot_general(lhs, rhs, (((1,), (0,)), ((), ())), preferred_element_type=F32)


def mm_nt(lhs, rhs):
    return lax.dot_general(lhs, rhs, (((1,), (1,)), ((), ())), preferred_element_type=F32)


def tree_sum(items):
    items = list(items)
    while len(items) > 1:
        items = [a + b for a, b in zip(items[::2], items[1::2])]
    return items[0]


def pack_weights(qkv_ref, up_ref, down_ref, conv_ref, g1_ref, s1_ref, g2_ref, s2_ref, narrow_ref, ff_ref, rows_ref):
    own, ffs = up_ref.shape
    rows_ref[...] = jnp.zeros_like(rows_ref)
    rows_ref[0:3, :own] = conv_ref[...].astype(F32)
    for i, ref in enumerate((g1_ref, s1_ref, g2_ref, s2_ref)):
        rows_ref[3 + i : 4 + i, :own] = ref[...].astype(F32)
    wide = qkv_ref.shape[1]
    narrow_ref[:, :wide] = qkv_ref[...]
    narrow_ref[:, wide:] = rows_ref[...].T[:own].astype(BF)
    ff_ref[:own] = up_ref[...]
    ff_ref[own:] = down_ref[...]


def tiles(total, size):
    return [slice(at, at + size) for at in range(0, total, size)]


def weave(*strands):
    strands = [strand for strand in strands if strand]
    total = sum(len(strand) for strand in strands)
    pieces = [((i + 0.5) / len(strand), j, piece) for j, strand in enumerate(strands) for i, piece in enumerate(strand)]
    assert len(pieces) == total
    for _, _, piece in sorted(pieces, key=lambda item: item[:2]):
        piece()


def twice(tile, lanes):
    return jnp.concatenate([tile] * (lanes // LANES), axis=1)


def load_columns(packed_ref, col_ref, places):
    for i, place in enumerate(places):
        column = packed_ref[:, place : place + 1].astype(F32)
        col_ref[i] = jnp.broadcast_to(column, (column.shape[0], LANES))


def column_mean(values):
    return jnp.sum(values, axis=0, keepdims=True) * (1.0 / values.shape[0])


def norm_columns(values):
    centred = values - column_mean(values)
    scale = lax.rsqrt(column_mean(centred * centred) + 1e-06)
    return centred * scale, scale


def fold(values):
    rows, lanes = values.shape
    return jnp.sum(values.reshape(rows // 8, 8, lanes), axis=0)


def fold_lanes(values):
    return sum(values[:, t] for t in tiles(values.shape[1], LANES))


def forward_attention(index_ref, len_ref, tok_ref, seg_ref, *refs, pieces):
    piece_refs = refs[:pieces]
    (
        x_ref, mc_ref, norm_ref, q_ref, k_ref, v_ref, e_ref, att_ref, inv_ref, aux_ref, packed_ref, w_ref,
        wt_ref, wide_ref, col_ref, bias_ref, key_ref, value_ref,
    ) = refs[pieces:]
    rows, seq, width = tok_ref.shape
    head = width // HEADS
    step = pl.program_id(0)

    @pl.when(step == 0)
    def _():
        own = width // pieces
        for i, ref in enumerate(piece_refs):
            wide_ref[pl.ds(pl.multiple_of(index_ref[i] * own, 16), own), :] = ref[...]
        w_ref[...] = wide_ref[:, : 3 * width]
        wt_ref[:width] = (wide_ref[:, :width].astype(F32) * head ** (-0.5)).astype(BF).T
        wt_ref[width:] = wide_ref[:, width : 3 * width].T
        packed_ref[...] = wide_ref[:, 3 * width :]
        load_columns(packed_ref, col_ref, range(5))

    place = lax.broadcasted_iota(jnp.int32, (1, seq), 1)
    zero = jnp.zeros((head, seq), BF)

    def preparation(r):
        known = {}

        def start():
            segs = seg_ref[pl.ds(step * rows + r, 1), :].astype(F32)
            valid = place < len_ref[step * rows + r]
            number = jnp.where(valid, segs, -1.0)
            links = jnp.where(valid & (place > 0) & (number == pltpu.roll(number, 1, 1)), 1.0, 0.0)
            next_links = jnp.where(place < seq - 1, pltpu.roll(links, seq - 1, 1), 0.0)
            none = jnp.zeros_like(links)
            aux = jnp.concatenate([links, next_links, number, none, none, none, none, none], axis=0)
            aux_ref[r] = aux
            x_ref[r] = tok_ref[r].T
            known.update(segs=segs, links=links, next_links=next_links, key_number=aux.T[:, 2:3])

        def mask(t):
            row_id = lax.broadcasted_iota(jnp.int32, (64, seq), 0) + t.start
            col_id = lax.broadcasted_iota(jnp.int32, (64, seq), 1)
            allowed = (known["key_number"][t] == known["segs"]) | (row_id == col_id)
            bias_ref[r, t] = jnp.where(allowed, 0.0, -1e30)

        def conv(t):
            base = x_ref[r, t].astype(F32)
            before = pltpu.roll(base, 1, 1) * known["links"]
            after = pltpu.roll(base, seq - 1, 1) * known["next_links"]
            conv0, conv1, conv2 = [twice(col_ref[i, t], seq) for i in range(3)]
            mc_ref[r, t] = base + before * conv0 + base * conv1 + after * conv2

        def norm(t):
            n, _ = norm_columns(mc_ref[r, :, t])
            norm_ref[r, :, t] = (n * col_ref[3] + col_ref[4]).astype(BF)

        pieces = [start] + [functools.partial(conv, t) for t in tiles(width, 32)]
        pieces += [functools.partial(norm, t) for t in tiles(seq, LANES)]
        return pieces + [functools.partial(mask, t) for t in tiles(seq, 64)]

    def project():
        normed = jnp.concatenate([norm_ref[r] for r in range(rows)], axis=1)
        for i, ref in enumerate((q_ref, k_ref, value_ref)):
            part = mm(wt_ref[i * width : (i + 1) * width], normed).astype(BF)
            for r in range(rows):
                ref[r] = part[:, r * seq : (r + 1) * seq]
        for r in range(rows):
            key_ref[r] = k_ref[r].T
            v_ref[r] = value_ref[r].T

    def scores(r, p):
        low, high = [q_ref[r, h * head : (h + 1) * head] for h in (2 * p, 2 * p + 1)]
        both = jnp.concatenate([jnp.concatenate([low, zero], axis=1), jnp.concatenate([zero, high], axis=1)], axis=0)
        return mm(key_ref[r, :, 2 * p * head : 2 * (p + 1) * head], both)

    def attended(r, p):
        both = jnp.concatenate([e_ref[r, 2 * p], e_ref[r, 2 * p + 1]], axis=1)
        product = mm(value_ref[r, 2 * p * head : 2 * (p + 1) * head], both)
        parts = []
        for i in range(2):
            att = product[i * head : (i + 1) * head, i * seq : (i + 1) * seq] * inv_ref[r, 2 * p + i : 2 * p + i + 1]
            parts.append(att.astype(BF))
        return jnp.concatenate(parts, axis=0)

    def soften(r, p, product):
        for i in range(2):
            for t in tiles(seq, LANES):
                masked = product[:, i * seq + t.start : i * seq + t.stop] + bias_ref[r, :, t]
                raised = jnp.exp(masked - jnp.max(masked, axis=0, keepdims=True))
                inv_ref[r, 2 * p + i : 2 * p + i + 1, t] = 1.0 / jnp.sum(raised, axis=0, keepdims=True)
                e_ref[r, 2 * p + i, :, t] = raised.astype(BF)

    weave(*[preparation(r) for r in range(rows)])
    project()
    work = [(r, p) for r in range(rows) for p in range(HEADS // 2)]
    current, last = scores(*work[0]), None
    for at, (r, p) in enumerate(work):
        following = scores(*work[at + 1]) if at + 1 < len(work) else None
        finished = attended(*last) if last else None
        soften(r, p, current)
        if last:
            att_ref[last[0], 2 * last[1] * head : 2 * (last[1] + 1) * head] = finished
        current, last = following, (r, p)
    att_ref[last[0], 2 * last[1] * head : 2 * (last[1] + 1) * head] = attended(*last)


def gelu_parts(x):
    cdf = 0.5 * lax.erf(x * math.sqrt(0.5)) + 0.5
    bell = jnp.exp2(x * x * (-0.5 / math.log(2.0)) - 0.5 * math.log2(2.0 * math.pi))
    return x * cdf, cdf + x * bell


def feed_forward(index_ref, att_ref, mc_ref, ct_ref, packed_ref, *refs, pieces, shards):
    piece_refs = refs[:pieces]
    groups = 2 if pieces > 1 else 1
    lo_ref, gm_ref, ga_ref, gs_ref = refs[pieces : pieces + 4]
    gw_refs = refs[pieces + 4 : pieces + 4 + groups]
    (
        up_ref, down_ref, upt_ref, downt_ref, out_ref, outt_ref, up_acc, down_acc, out_acc, col_acc, col_ref,
        att_cat, mixed_ref, n_ref, norm_ref, ctt_ref, hidden_ref, gp_ref, gn_ref, scale_ref, lot_ref,
        branch_ref,
    ) = refs[pieces + 4 + groups :]
    rows, seq, width = ct_ref.shape
    ff = up_ref.shape[1]
    ffs = ff // shards
    own = width // pieces
    step = pl.program_id(0)

    @pl.when(step == 0)
    def _():
        for acc in (up_acc, down_acc, out_acc, col_acc):
            acc[...] = jnp.zeros_like(acc)
        for i, ref in enumerate(piece_refs):
            here = pl.ds(pl.multiple_of(index_ref[i] * own, 16), own)
            for j in range(shards):
                up_ref[here, j * ffs : (j + 1) * ffs] = ref[2 * j * own : (2 * j + 1) * own]
                down_ref[here, j * ffs : (j + 1) * ffs] = ref[(2 * j + 1) * own : (2 * j + 2) * own]
            out_ref[here, :] = ref[2 * shards * own :]
        upt_ref[...] = up_ref[...].T
        downt_ref[...] = down_ref[...].T
        outt_ref[...] = out_ref[...].T
        load_columns(packed_ref, col_ref, (5, 6))

    def lanes_of(r):
        return slice(r * seq, (r + 1) * seq)

    def spots_of(r):
        return [slice(at, at + LANES) for at in range(r * seq, (r + 1) * seq, LANES)]

    def preparation(r):
        lanes = lanes_of(r)

        def turn():
            ctt_ref[:, lanes] = ct_ref[r].T
            att_cat[:, lanes] = att_ref[r]

        def branch():
            mixed_ref[:, lanes] = mc_ref[r] + mm(outt_ref[...], att_ref[r])

        def norm(t):
            n, scale = norm_columns(mixed_ref[:, t])
            n_ref[:, t] = n
            scale_ref[0:1, t] = scale
            norm_ref[:, t] = (n * col_ref[0] + col_ref[1]).astype(BF)

        return [turn, branch] + [functools.partial(norm, t) for t in spots_of(r)]

    def opening(block):
        return mm(upt_ref[block], norm_ref[...]), mm(downt_ref[block], ctt_ref[...])

    def activation(block, products):
        pre, grad_hidden = products
        for low in range(0, block.stop - block.start, 16):
            part = slice(low, low + 16)
            here = slice(block.start + low, block.start + low + 16)
            hidden, slope = gelu_parts(pre[part])
            hidden_ref[here] = hidden.astype(BF)
            gp_ref[here] = (grad_hidden[part] * slope).astype(BF)

    def norm_back(r):
        spots = spots_of(r)
        mean_e = [jnp.zeros((8, LANES), F32) for _ in spots]
        mean_en = [jnp.zeros((8, LANES), F32) for _ in spots]
        means = []

        def sums(d):
            column = col_ref[0, d]
            gain_sum, shift_sum = col_acc[0, d], col_acc[1, d]
            for i, t in enumerate(spots):
                grad_n = gn_ref[d, t]
                product = grad_n * n_ref[d, t]
                gain_sum += product
                shift_sum += grad_n
                mean_e[i] += fold(grad_n * column)
                mean_en[i] += fold(product * column)
            col_acc[0, d] = gain_sum
            col_acc[1, d] = shift_sum

        def finish():
            for i in range(len(spots)):
                me = jnp.sum(mean_e[i], axis=0, keepdims=True) * (1.0 / width)
                men = jnp.sum(mean_en[i], axis=0, keepdims=True) * (1.0 / width)
                means.append((me, men))

        def apply(d):
            for i, t in enumerate(spots):
                me, men = means[i]
                change = scale_ref[0:1, t] * (gn_ref[d, t] * col_ref[0, d] - me - n_ref[d, t] * men)
                grad_mixed = ctt_ref[d, t].astype(F32) + change
                gm_ref[r, d, i * LANES : (i + 1) * LANES] = grad_mixed
                branch_ref[d, t] = grad_mixed.astype(BF)

        def attended():
            ga_ref[r] = mm(out_ref[...], branch_ref[:, lanes_of(r)]).astype(BF)

        def turn():
            lo_ref[r] = lot_ref[:, lanes_of(r)].T

        pieces = [functools.partial(sums, d) for d in tiles(width, 32)] + [finish]
        return pieces + [functools.partial(apply, d) for d in tiles(width, 32)] + [attended, turn]

    weave(*[preparation(r) for r in range(rows)])
    blocks = tiles(ff, 128)
    current = opening(blocks[0])
    for at, block in enumerate(blocks):
        following = opening(blocks[at + 1]) if at + 1 < len(blocks) else None
        activation(block, current)
        current = following
    gn_ref[...] = mm(up_ref[...], gp_ref[...])
    lot_ref[...] = (mixed_ref[...] + mm(down_ref[...], hidden_ref[...])).astype(BF)
    steps = [piece for pieces_of in zip(*[norm_back(r) for r in range(rows)]) for piece in pieces_of]
    grads = [(acc, left, right, block) for block in tiles(ff, 256) for acc, left, right in ((down_acc, ctt_ref, hidden_ref), (up_acc, norm_ref, gp_ref))]
    share = -(-len(steps) // len(grads))
    for i, (acc, left, right, block) in enumerate(grads):
        total = acc[:, block] + mm_nt(left[...], right[block])
        for piece in steps[i * share : (i + 1) * share]:
            piece()
        acc[:, block] = total
    out_acc[...] += mm_nt(att_cat[...], branch_ref[...])

    @pl.when(step == pl.num_programs(0) - 1)
    def _():
        for i in range(pieces):
            here = pl.ds(pl.multiple_of(index_ref[i] * own, 16), own)
            place = gw_refs[i % groups]
            for j in range(shards):
                cols = slice(j * ffs, (j + 1) * ffs)
                place[i // groups, :, 2 * j * ffs : (2 * j + 1) * ffs] = up_acc[here, cols].astype(BF)
                place[i // groups, :, (2 * j + 1) * ffs : (2 * j + 2) * ffs] = down_acc[here, cols].astype(BF)
            place[i // groups, :, 2 * ff :] = out_acc[here, :].astype(BF)
        gs_ref[...] = jnp.zeros_like(gs_ref)
        for i in range(2):
            gs_ref[5 + i : 6 + i] = jnp.sum(col_acc[i].T, axis=0, keepdims=True)


def backward_attention(
    q_ref, k_ref, v_ref, e_ref, att_ref, inv_ref, norm_ref, ga_ref, index_ref, w_ref, start_ref, gn_ref, *refs, pieces
):
    gw_refs = refs[:-5]
    proj_ref, w_acc, norm_cat, soft_ref, logit_ref = refs[-5:]
    rows, seq, width = v_ref.shape
    own = width // pieces
    head = width // HEADS
    step = pl.program_id(0)

    @pl.when(step == 0)
    def _():
        w_acc[...] = jnp.zeros_like(w_acc) if start_ref is None else start_ref[...]

    zero = jnp.zeros((head, seq), BF)
    work = [(r, p) for r in range(rows) for p in range(HEADS // 2)]

    def opening(r, p):
        grads, inners = [], []
        for h in (2 * p, 2 * p + 1):
            part = slice(h * head, (h + 1) * head)
            grad_att = ga_ref[r, part].astype(F32) * inv_ref[r, h : h + 1]
            inners.append(jnp.sum(grad_att * att_ref[r, part].astype(F32), axis=0, keepdims=True))
            grads.append(grad_att.astype(BF))
        low, high = grads
        both = jnp.concatenate([jnp.concatenate([low, zero], axis=1), jnp.concatenate([zero, high], axis=1)], axis=0)
        product = mm(v_ref[r, :, 2 * p * head : 2 * (p + 1) * head], both)
        soft_ref[r, 2 * p] = product[:, :seq]
        soft_ref[r, 2 * p + 1] = product[:, seq:]
        return jnp.concatenate(grads, axis=0), inners

    ready = opening(*work[0])
    for at, (r, p) in enumerate(work):
        grad_att, inners = ready
        if at + 1 < len(work):
            ready = opening(*work[at + 1])
        for i, h in enumerate((2 * p, 2 * p + 1)):
            for t in tiles(seq, 32):
                raised = e_ref[r, h, t].astype(F32)
                logit_ref[r, h, t] = (raised * (soft_ref[r, h, t] - inners[i])).astype(BF)
        part = slice(2 * p * head, 2 * (p + 1) * head)
        pair = slice(2 * p, 2 * p + 2)
        beside = jnp.concatenate([logit_ref[r, 2 * p], logit_ref[r, 2 * p + 1]], axis=1)
        grad_q = mm(k_ref[r, part], beside)
        grad_k = mm_nt(q_ref[r, part], logit_ref[r, pair].reshape(2 * seq, seq))
        grad_v = mm_nt(grad_att, e_ref[r, pair].reshape(2 * seq, seq))
        for i in range(2):
            place = slice(r * seq, (r + 1) * seq)
            own_rows, own_cols = slice(i * head, (i + 1) * head), slice(i * seq, (i + 1) * seq)
            for j, grad in enumerate((grad_q, grad_k, grad_v)):
                first = j * width + (2 * p + i) * head
                mine = grad[own_rows, own_cols]
                proj_ref[first : first + head, place] = (mine * head ** (-0.5) if j == 0 else mine).astype(BF)
    grad_normed = mm(w_ref[...], proj_ref[...]).astype(BF)
    for r in range(rows):
        norm_cat[:, r * seq : (r + 1) * seq] = norm_ref[r]
        gn_ref[r] = grad_normed[:, r * seq : (r + 1) * seq]
    w_acc[...] += mm_nt(norm_cat[...], proj_ref[...])

    @pl.when(step == pl.num_programs(0) - 1)
    def _():
        if start_ref is None:
            gw_refs[0][...] = w_acc[...]
        else:
            groups = len(gw_refs)
            for i in range(pieces):
                here = pl.ds(pl.multiple_of(index_ref[i] * own, 16), own)
                gw_refs[i % groups][i // groups] = w_acc[here, :].astype(BF)


def backward_conv(
    x_ref, aux_ref, mc_ref, gm_ref, gn_ref, packed_ref, other_ref, part_ref, ig_ref, gs_ref,
    acc_ref, col_ref, n_ref, g_ref, turn_ref,
):
    rows, width, seq = x_ref.shape
    step = pl.program_id(0)

    @pl.when(step == 0)
    def _():
        acc_ref[...] = jnp.zeros_like(acc_ref)
        load_columns(packed_ref, col_ref, range(4))

    spots = tiles(seq, LANES)
    for r in range(rows):
        scales = []
        for t in spots:
            n, scale = norm_columns(mc_ref[r, :, t])
            n_ref[r, :, t] = n
            scales.append(scale)
        mean_e = [jnp.zeros((8, LANES), F32) for _ in spots]
        mean_en = [jnp.zeros((8, LANES), F32) for _ in spots]
        for d in tiles(width, 32):
            column = col_ref[3, d]
            gain_sum, shift_sum = acc_ref[3, d], acc_ref[4, d]
            for i, t in enumerate(spots):
                grad_n = gn_ref[r, d, t].astype(F32)
                product = grad_n * n_ref[r, d, t]
                gain_sum += product
                shift_sum += grad_n
                mean_e[i] += fold(grad_n * column)
                mean_en[i] += fold(product * column)
            acc_ref[3, d] = gain_sum
            acc_ref[4, d] = shift_sum
        for i, t in enumerate(spots):
            me = jnp.sum(mean_e[i], axis=0, keepdims=True) * (1.0 / width)
            men = jnp.sum(mean_en[i], axis=0, keepdims=True) * (1.0 / width)
            for d in tiles(width, 64):
                e = gn_ref[r, d, t].astype(F32) * col_ref[3, d]
                g_ref[r, d, t] = gm_ref[r, d, t] + scales[i] * (e - me - n_ref[r, d, t] * men)
        links, next_links = aux_ref[r, 0:1], aux_ref[r, 1:2]
        for d in tiles(width, 32):
            g = g_ref[r, d]
            base = x_ref[r, d].astype(F32)
            before = pltpu.roll(g, 1, 1) * links
            after = pltpu.roll(g, seq - 1, 1) * next_links
            acc_ref[0, d] += fold_lanes(base * after)
            acc_ref[1, d] += fold_lanes(base * g)
            acc_ref[2, d] += fold_lanes(base * before)
            conv0, conv1, conv2 = [twice(col_ref[i, d], seq) for i in range(3)]
            turn_ref[r, d] = (g + conv1 * g + conv0 * after + conv2 * before).astype(BF)
        ig_ref[r] = turn_ref[r].T

    @pl.when(step == pl.num_programs(0) - 1)
    def _():
        gs_ref[...] = other_ref[...]
        for i in range(5):
            gs_ref[i : i + 1] += jnp.sum(acc_ref[i].T, axis=0, keepdims=True)


def in_hbm(values):
    return pltpu.with_memory_space_constraint(values, pltpu.HBM)


def by_row(shape, rows, first=0):
    tail = tuple(shape[1:])
    return pl.BlockSpec((rows,) + tail, lambda i, *_: (i + first,) + (0,) * len(tail))


def whole(shape):
    place = (0,) * len(shape)
    return pl.BlockSpec(tuple(shape), lambda i, *_: place, pipeline_mode=pl.Buffered(1))


def step_rows(count, most):
    return max(r for r in range(1, most + 1) if count % r == 0)


def call(body, name, scalars, rows, row_args, args, row_outs, outs, scratch, span=None, into=None, near=()):
    first, count = span or (0, row_args[0].shape[0])
    skip = first // rows
    in_specs = [by_row(a.shape, rows, skip if a.shape[0] > count else 0) for a in row_args]
    in_specs += [whole(a.shape) for a in args]
    aliases = {}
    if into is not None:
        in_specs.append(pl.BlockSpec(memory_space=pl.ANY))
        aliases = {len(scalars) + len(in_specs) - 1: 0}
    spec = pltpu.PrefetchScalarGridSpec(
        num_scalar_prefetch=len(scalars),
        grid=(count // rows,),
        in_specs=in_specs,
        out_specs=[by_row(s, rows, skip if s[0] > count else 0) for s, _ in row_outs] + [whole(s) for s, _ in outs],
        scratch_shapes=[pltpu.VMEM(s, t) for s, t in scratch],
    )
    return pl.pallas_call(
        body,
        grid_spec=spec,
        out_shape=[(jax.ShapeDtypeStruct if "out" + str(i) in near else pltpu.HBM)(s, t) for i, (s, t) in enumerate(row_outs)]
        + [jax.ShapeDtypeStruct(s, t) for s, t in outs],
        input_output_aliases=aliases,
        compiler_params=pltpu.CompilerParams(dimension_semantics=("arbitrary",), vmem_limit_bytes=VMEM_LIMITS[name] * MIB),
        name=name,
    )(*scalars, *[a if i in near else in_hbm(a) for i, a in enumerate(row_args)], *args, *(() if into is None else (into,)))


def small_call(body, name, args, outs, scratch=()):
    return pl.pallas_call(
        body,
        out_shape=[jax.ShapeDtypeStruct(s, t) for s, t in outs],
        scratch_shapes=[pltpu.VMEM(s, t) for s, t in scratch],
        compiler_params=pltpu.CompilerParams(vmem_limit_bytes=16 * MIB),
        name=name,
    )(*args)


def run_forward(index, tokens, segment_ids, valid_len, pieces):
    count, seq, width = tokens.shape
    flipped = (count, width, seq)
    rows = step_rows(count, 2)
    row_outs = [
        (flipped, BF), (flipped, F32), (flipped, BF), (flipped, BF), (flipped, BF), ((count, seq, width), BF),
        ((count, HEADS, seq, seq), BF), (flipped, BF), ((count, 8, seq), F32), ((count, 8, seq), F32),
    ]
    return call(
        functools.partial(forward_attention, pieces=len(pieces)), "forward_attention", (index, valid_len),
        rows, (tokens,), (in_hbm(segment_ids), *pieces),
        row_outs, [((width, VECTORS), BF), ((width, 3 * width), BF)],
        [
            ((3 * width, width), BF), ((width, 3 * width + VECTORS), BF), ((5, width, LANES), F32),
            ((rows, seq, seq), F32), ((rows, seq, width), BF), ((rows, width, seq), BF),
        ],
    )


def run_feed_forward(index, att, mixed, cotangent, packed, pieces, shards):
    count, seq, width = cotangent.shape
    own = width // len(pieces)
    ff = shards * width
    groups = 2 if len(pieces) > 1 else 1
    rows = step_rows(count, 2)
    wide = rows * seq
    row_outs = [((count, seq, width), BF), ((count, width, seq), F32), ((count, width, seq), BF)]
    grads = ((len(pieces) // groups, own, 2 * ff + width), BF)
    return call(
        functools.partial(feed_forward, pieces=len(pieces), shards=shards), "feed_forward", (index,),
        rows, (att, mixed, cotangent), (packed, *pieces),
        row_outs, [((8, width), F32)] + [grads] * groups,
        [((width, ff), BF)] * 2 + [((ff, width), BF)] * 2 + [((width, width), BF)] * 2
        + [((width, ff), F32)] * 2 + [((width, width), F32), ((2, width, LANES), F32), ((2, width, LANES), F32)]
        + [((width, wide), BF), ((width, wide), F32), ((width, wide), F32), ((width, wide), BF), ((width, wide), BF)]
        + [((ff, wide), BF)] * 2
        + [((width, wide), F32), ((8, wide), F32), ((width, wide), BF), ((width, wide), BF)],
        near=("out2",),
    )


def run_backward_attention(index, weight, kept, grad_att, pieces, span, start):
    count, seq, width = kept[2].shape
    own = width // pieces
    groups = 2 if pieces > 1 else 1
    rows = step_rows(span[1], 2)
    row_args = (*kept, grad_att)
    many = len(row_args)

    def body(index_ref, *refs):
        w_ref, rest = refs[many], refs[many + 1 :]
        start_ref, rest = (None, rest) if start is None else (rest[0], rest[1:])
        backward_attention(*refs[:many], index_ref, w_ref, start_ref, *rest, pieces=pieces)

    outs = [((width, 3 * width), F32)] if start is None else [((pieces // groups, own, 3 * width), BF)] * groups
    return call(
        body, "backward_attention", (index,), rows, row_args, (weight,) if start is None else (weight, start),
        [((span[1], width, seq), BF)], outs,
        [
            ((3 * width, rows * seq), BF), ((width, 3 * width), F32), ((width, rows * seq), BF),
            ((rows, HEADS, seq, seq), F32), ((rows, HEADS, seq, seq), BF),
        ],
        span=span, near=("out0", many - 1),
    )


def run_backward_conv(x, aux, mixed, grad_mixed, grad_normed, packed, other, span, into):
    count, width, seq = x.shape
    rows = step_rows(span[1], 2)

    def body(*refs):
        if into is None:
            backward_conv(*refs[:7], None, *refs[7:])
        else:
            backward_conv(*refs)

    return call(
        body, "backward_conv", (), rows,
        (x, aux, mixed, grad_mixed, grad_normed), (packed, other),
        [((count, seq, width), BF)], [((8, width), F32)],
        [
            ((5, width, LANES), F32), ((4, width, LANES), F32), ((rows, width, seq), F32), ((rows, width, seq), F32),
            ((rows, width, seq), BF),
        ],
        span=span, into=into, near=(4,),
    )


def halves(count):
    early = count // 3
    return ((0, early), (early, count - early)) if early % 2 == 0 and early else ((0, count // 2), (count // 2, count - count // 2))


def exchange(values, axis, offset):
    size = lax.axis_size(axis)
    return lax.ppermute(values, axis, [(i, i ^ offset) for i in range(size)])


def add_halves(mine, received):
    count, own, cols = mine.shape

    def body(mine_ref, received_ref, *out_refs):
        for i, ref in enumerate(out_refs):
            ref[...] = (mine_ref[i].astype(F32) + received_ref[i].astype(F32)).astype(BF)

    return small_call(body, "add_halves", (mine, received), [((own, cols), BF)] * count)


def add_wide(*items):
    return tree_sum(item.astype(F32) for item in items)


def add_shard_vectors(items, own):
    def body(*refs):
        total = tree_sum(ref[...] for ref in refs[:-5])
        refs[-5][...] = total[0:3, :own]
        for i in range(4):
            refs[i - 4][...] = total[3 + i : 4 + i, :own]

    return small_call(body, "add_shard_vectors", items, [((3, own), F32)] + [((1, own), F32)] * 4)


def direct_plan(tokens, segment_ids, valid_len, qkv_weight, out_weight, up_weight, down_weight, conv_weight, vectors, cotangent):
    count, seq, width = tokens.shape
    own, ffs = up_weight.shape
    dp, mp = lax.axis_size("dp"), lax.axis_size("mp")
    me = lax.axis_index("dp")
    offsets = [2 * p for p in range(dp // 2)]
    index = jnp.stack([me ^ (p ^ c) for p in offsets for c in range(2)]).astype(jnp.int32)
    narrow, ff_own = small_call(
        pack_weights, "pack_weights",
        [in_hbm(a) for a in (qkv_weight, up_weight, down_weight, conv_weight, *[v.reshape(1, own) for v in vectors])],
        [((own, 3 * width + VECTORS), BF), ((2 * own, ffs), BF)], [((VECTORS, VECTORS), F32)],
    )
    plane = [narrow] + [exchange(narrow, "dp", p) for p in offsets[1:]]
    shards = [ff_own] + [exchange(ff_own, "mp", j) for j in range(1, mp)]
    pieces = [piece for a in plane for piece in (a, exchange(a, "dp", 1))]
    column = jnp.concatenate(shards + [out_weight], axis=0)
    columns = [column] + [exchange(column, "dp", p) for p in offsets[1:]]
    x, mixed, normed, q, k, v, raised, att, inverse, aux, packed, weight = run_forward(
        index, tokens, segment_ids, valid_len, pieces
    )
    columns, att = lax.optimization_barrier((columns, att))
    pieces = [piece for a in columns for piece in (a, exchange(a, "dp", 1))]
    layer_out, grad_mixed, grad_att, sums2, mine, theirs = run_feed_forward(
        index, att, mixed, cotangent, packed, pieces, mp
    )
    received = exchange(theirs, "dp", 1)
    early, late = halves(count)
    kept = (q, k, v, raised, att, inverse, normed)
    grad_normed1, start = run_backward_attention(index, weight, kept, grad_att, dp, early, None)
    received, start = lax.optimization_barrier((received, start))
    parts = list(add_halves(mine, received))
    parts[0], start = lax.optimization_barrier((parts[0], start))
    plane = [parts[0]] + [exchange(parts[i], "dp", p) for i, p in enumerate(offsets) if i]
    grad_normed2, mine_a, theirs_a = run_backward_attention(index, weight, kept, grad_att, dp, late, start)
    plane, theirs_a = lax.optimization_barrier((plane, theirs_a))
    received_a = exchange(theirs_a, "dp", 1)
    total = add_wide(*plane).astype(BF)
    half = 2 * ffs * (mp // 2)
    near, far, out_part = total[:, :half], total[:, half:], total[:, 2 * half :]
    received_f = exchange(far, "mp", 2)
    near, grad_normed1 = lax.optimization_barrier((near, grad_normed1))
    some_grad, sums = run_backward_conv(x, aux, mixed, grad_mixed, grad_normed1, packed, sums2, early, None)
    received_a, sums = lax.optimization_barrier((received_a, sums))
    parts = list(add_halves(mine_a, received_a))
    parts[0], sums = lax.optimization_barrier((parts[0], sums))
    plane_a = [parts[0]] + [exchange(parts[i], "dp", p) for i, p in enumerate(offsets) if i]
    input_grad, sums = run_backward_conv(x, aux, mixed, grad_mixed, grad_normed2, packed, sums, late, some_grad)
    received_s = exchange(sums, "dp", 1)
    plane_a, received_f, sums = lax.optimization_barrier((plane_a, received_f, sums))
    total = add_wide(*plane_a).astype(BF)
    received_s, total = lax.optimization_barrier((received_s, total))
    received_1 = exchange(total, "mp", 2)
    sums = sums + received_s
    plane_s = [sums] + [exchange(sums, "dp", p) for p in offsets[1:]]
    near_sum = add_wide(near, received_f[:, :half])
    out_sum = lax.optimization_barrier(add_wide(out_part, received_f[:, half:]).astype(BF))
    keep = near_sum[:, : 2 * ffs]
    send = jnp.concatenate([near_sum[:, 2 * ffs :].astype(BF), out_sum], axis=1)
    received_n = exchange(send, "mp", 1)
    plane_s, received_1 = lax.optimization_barrier((plane_s, received_1))
    total = lax.optimization_barrier(add_wide(total, received_1).astype(BF))
    received_2 = exchange(total, "mp", 1)
    vectors = lax.dynamic_slice_in_dim(tree_sum(plane_s), me * own, own, axis=1)
    shards = [vectors] + [exchange(vectors, "mp", j) for j in range(1, mp)]
    grad_up = keep[:, :ffs] + received_n[:, :ffs].astype(F32)
    grad_down = keep[:, ffs:] + received_n[:, ffs : 2 * ffs].astype(F32)
    grad_out = add_wide(out_sum, received_n[:, 2 * ffs :])
    grad_qkv = add_wide(total, received_2)
    grad_conv, *grads = add_shard_vectors(shards, own)
    return (layer_out, input_grad, grad_qkv, grad_out, grad_up, grad_down, grad_conv, *[g.reshape(own) for g in grads])


def gathered_plan(tokens, segment_ids, valid_len, qkv_weight, out_weight, up_weight, down_weight, conv_weight, vectors, cotangent):
    count, seq, width = tokens.shape
    own = qkv_weight.shape[0]
    dp = width // own
    columns = jnp.stack([conv_weight[0], conv_weight[1], conv_weight[2], *vectors], axis=1)
    narrow = jnp.concatenate([qkv_weight, jnp.pad(columns, ((0, 0), (0, VECTORS - 7))), out_weight], axis=1)
    wide = lax.all_gather(narrow, "dp", axis=0, tiled=True)
    both = lax.all_gather(jnp.concatenate([up_weight, down_weight], axis=0), "mp", axis=1, tiled=True)
    ff = both.shape[1]
    shards = ff // width
    both = lax.all_gather(both, "dp", axis=0).reshape(dp, 2, own, shards, width)
    both = both.transpose(3, 1, 0, 2, 4).reshape(2 * ff, width)
    column = jnp.concatenate([both, wide[:, 3 * width + VECTORS :]], axis=0)
    index = jnp.zeros((1,), jnp.int32)
    x, mixed, normed, q, k, v, raised, att, inverse, aux, packed, weight = run_forward(
        index, tokens, segment_ids, valid_len, [wide[:, : 3 * width + VECTORS]]
    )
    layer_out, grad_mixed, grad_att, sums2, grads = run_feed_forward(
        index, att, mixed, cotangent, packed, [column], shards
    )
    early, late = halves(count)
    kept = (q, k, v, raised, att, inverse, normed)
    grad_normed1, start = run_backward_attention(index, weight, kept, grad_att, 1, early, None)
    grad_normed2, grad_qkv = run_backward_attention(index, weight, kept, grad_att, 1, late, start)
    some_grad, sums = run_backward_conv(x, aux, mixed, grad_mixed, grad_normed1, packed, sums2, early, None)
    input_grad, sums = run_backward_conv(x, aux, mixed, grad_mixed, grad_normed2, packed, sums, late, some_grad)
    grad_ff = grads[0, :, : 2 * ff].reshape(width, shards, 2, width).transpose(0, 2, 1, 3).reshape(width, 2 * ff)
    grad_ff = lax.psum_scatter(grad_ff, "dp", scatter_dimension=0, tiled=True).reshape(own, 2, ff)
    grad_ff = lax.psum_scatter(grad_ff, "mp", scatter_dimension=2, tiled=True).astype(F32)
    grad_attn = jnp.concatenate([grad_qkv[0], grads[0, :, 2 * ff :]], axis=1)
    grad_attn = lax.psum_scatter(grad_attn, "dp", scatter_dimension=0, tiled=True)
    grad_attn = lax.psum(grad_attn, "mp").astype(F32)
    sums = lax.psum(sums, ("dp", "mp"))
    sums = lax.dynamic_slice_in_dim(sums, lax.axis_index("dp") * own, own, axis=1)
    return (
        layer_out, input_grad, grad_attn[:, : 3 * width], grad_attn[:, 3 * width :],
        grad_ff[:, 0], grad_ff[:, 1], sums[0:3], sums[3], sums[4], sums[5], sums[6],
    )


def on_device(
    tokens, segment_ids, valid_len, qkv_weight, out_weight, up_weight, down_weight, conv_weight,
    ln1_gain, ln1_shift, ln2_gain, ln2_shift, cotangent,
):
    own, ffs = up_weight.shape
    direct = own % 16 == 0 and ffs == tokens.shape[2] and own <= VECTORS and lax.axis_size("mp") == 4
    plan = direct_plan if direct else gathered_plan
    return plan(
        tokens, segment_ids, valid_len, qkv_weight, out_weight, up_weight, down_weight, conv_weight,
        (ln1_gain, ln1_shift, ln2_gain, ln2_shift), cotangent,
    )


def solution(mesh):
    rows = P(("dp", "mp"), None, None)
    weights = (P("dp", None), P("dp", None), P("dp", "mp"), P("dp", "mp"), P(None, "dp"))
    vectors = (P("dp"),) * 4
    return jax.shard_map(
        on_device,
        mesh=mesh,
        in_specs=(rows, P(("dp", "mp"), None), P(("dp", "mp"))) + weights + vectors + (rows,),
        out_specs=(rows, rows) + weights + vectors,
        check_vma=False,
    )
```

```python
import functools
import math

import jax
import jax.numpy as jnp
from jax import lax
from jax.experimental import pallas as pl
from jax.experimental.pallas import tpu as pltpu
from jax.sharding import PartitionSpec as P

HEADS = 6
VECTORS = 128
LANES = 128
BF = jnp.bfloat16
F32 = jnp.float32
MIB = 1024 * 1024
VMEM_LIMITS = dict(forward_attention=26, feed_forward=36, backward_attention=28, backward_conv=14)


def mm(lhs, rhs):
    return lax.dot_general(lhs, rhs, (((1,), (0,)), ((), ())), preferred_element_type=F32)


def mm_nt(lhs, rhs):
    return lax.dot_general(lhs, rhs, (((1,), (1,)), ((), ())), preferred_element_type=F32)


def tree_sum(items):
    items = list(items)
    while len(items) > 1:
        items = [a + b for a, b in zip(items[::2], items[1::2])]
    return items[0]


def pack_weights(qkv_ref, up_ref, down_ref, conv_ref, g1_ref, s1_ref, g2_ref, s2_ref, narrow_ref, ff_ref, rows_ref):
    own, ffs = up_ref.shape
    rows_ref[...] = jnp.zeros_like(rows_ref)
    rows_ref[0:3, :own] = conv_ref[...].astype(F32)
    for i, ref in enumerate((g1_ref, s1_ref, g2_ref, s2_ref)):
        rows_ref[3 + i : 4 + i, :own] = ref[...].astype(F32)
    wide = qkv_ref.shape[1]
    narrow_ref[:, :wide] = qkv_ref[...]
    narrow_ref[:, wide:] = rows_ref[...].T[:own].astype(BF)
    ff_ref[:own] = up_ref[...]
    ff_ref[own:] = down_ref[...]


def tiles(total, size):
    return [slice(at, at + size) for at in range(0, total, size)]


def weave(*strands):
    strands = [strand for strand in strands if strand]
    total = sum(len(strand) for strand in strands)
    pieces = [((i + 0.5) / len(strand), j, piece) for j, strand in enumerate(strands) for i, piece in enumerate(strand)]
    assert len(pieces) == total
    for _, _, piece in sorted(pieces, key=lambda item: item[:2]):
        piece()


def twice(tile, lanes):
    return jnp.concatenate([tile] * (lanes // LANES), axis=1)


def load_columns(packed_ref, col_ref, places):
    for i, place in enumerate(places):
        column = packed_ref[:, place : place + 1].astype(F32)
        col_ref[i] = jnp.broadcast_to(column, (column.shape[0], LANES))


def column_mean(values):
    return jnp.sum(values, axis=0, keepdims=True) * (1.0 / values.shape[0])


def norm_columns(values):
    centred = values - column_mean(values)
    scale = lax.rsqrt(column_mean(centred * centred) + 1e-06)
    return centred * scale, scale


def fold(values):
    rows, lanes = values.shape
    return jnp.sum(values.reshape(rows // 8, 8, lanes), axis=0)


def fold_lanes(values):
    return sum(values[:, t] for t in tiles(values.shape[1], LANES))


def forward_attention(index_ref, len_ref, tok_ref, seg_ref, *refs, pieces):
    piece_refs = refs[:pieces]
    (
        x_ref, mc_ref, norm_ref, q_ref, k_ref, v_ref, e_ref, att_ref, inv_ref, aux_ref, packed_ref, w_ref,
        wt_ref, wide_ref, col_ref, bias_ref, key_ref, value_ref,
    ) = refs[pieces:]
    rows, seq, width = tok_ref.shape
    head = width // HEADS
    step = pl.program_id(0)

    @pl.when(step == 0)
    def _():
        own = width // pieces
        for i, ref in enumerate(piece_refs):
            wide_ref[pl.ds(pl.multiple_of(index_ref[i] * own, 16), own), :] = ref[...]
        w_ref[...] = wide_ref[:, : 3 * width]
        wt_ref[:width] = (wide_ref[:, :width].astype(F32) * head ** (-0.5)).astype(BF).T
        wt_ref[width:] = wide_ref[:, width : 3 * width].T
        packed_ref[...] = wide_ref[:, 3 * width :]
        load_columns(packed_ref, col_ref, range(5))

    place = lax.broadcasted_iota(jnp.int32, (1, seq), 1)
    zero = jnp.zeros((head, seq), BF)

    def preparation(r):
        known = {}

        def start():
            segs = seg_ref[pl.ds(step * rows + r, 1), :].astype(F32)
            valid = place < len_ref[step * rows + r]
            number = jnp.where(valid, segs, -1.0)
            links = jnp.where(valid & (place > 0) & (number == pltpu.roll(number, 1, 1)), 1.0, 0.0)
            next_links = jnp.where(place < seq - 1, pltpu.roll(links, seq - 1, 1), 0.0)
            none = jnp.zeros_like(links)
            aux = jnp.concatenate([links, next_links, number, none, none, none, none, none], axis=0)
            aux_ref[r] = aux
            x_ref[r] = tok_ref[r].T
            known.update(segs=segs, links=links, next_links=next_links, key_number=aux.T[:, 2:3])

        def mask(t):
            row_id = lax.broadcasted_iota(jnp.int32, (64, seq), 0) + t.start
            col_id = lax.broadcasted_iota(jnp.int32, (64, seq), 1)
            allowed = (known["key_number"][t] == known["segs"]) | (row_id == col_id)
            bias_ref[r, t] = jnp.where(allowed, 0.0, -1e30)

        def conv(t):
            base = x_ref[r, t].astype(F32)
            before = pltpu.roll(base, 1, 1) * known["links"]
            after = pltpu.roll(base, seq - 1, 1) * known["next_links"]
            conv0, conv1, conv2 = [twice(col_ref[i, t], seq) for i in range(3)]
            mc_ref[r, t] = base + before * conv0 + base * conv1 + after * conv2

        def norm(t):
            n, _ = norm_columns(mc_ref[r, :, t])
            norm_ref[r, :, t] = (n * col_ref[3] + col_ref[4]).astype(BF)

        pieces = [start] + [functools.partial(conv, t) for t in tiles(width, 32)]
        pieces += [functools.partial(norm, t) for t in tiles(seq, LANES)]
        return pieces + [functools.partial(mask, t) for t in tiles(seq, 64)]

    def project():
        normed = jnp.concatenate([norm_ref[r] for r in range(rows)], axis=1)
        for i, ref in enumerate((q_ref, k_ref, value_ref)):
            part = mm(wt_ref[i * width : (i + 1) * width], normed).astype(BF)
            for r in range(rows):
                ref[r] = part[:, r * seq : (r + 1) * seq]
        for r in range(rows):
            key_ref[r] = k_ref[r].T
            v_ref[r] = value_ref[r].T

    def scores(r, p):
        low, high = [q_ref[r, h * head : (h + 1) * head] for h in (2 * p, 2 * p + 1)]
        both = jnp.concatenate([jnp.concatenate([low, zero], axis=1), jnp.concatenate([zero, high], axis=1)], axis=0)
        return mm(key_ref[r, :, 2 * p * head : 2 * (p + 1) * head], both)

    def attended(r, p):
        both = jnp.concatenate([e_ref[r, 2 * p], e_ref[r, 2 * p + 1]], axis=1)
        product = mm(value_ref[r, 2 * p * head : 2 * (p + 1) * head], both)
        parts = []
        for i in range(2):
            att = product[i * head : (i + 1) * head, i * seq : (i + 1) * seq] * inv_ref[r, 2 * p + i : 2 * p + i + 1]
            parts.append(att.astype(BF))
        return jnp.concatenate(parts, axis=0)

    def soften(r, p, product):
        for i in range(2):
            for t in tiles(seq, LANES):
                masked = product[:, i * seq + t.start : i * seq + t.stop] + bias_ref[r, :, t]
                raised = jnp.exp(masked - jnp.max(masked, axis=0, keepdims=True))
                inv_ref[r, 2 * p + i : 2 * p + i + 1, t] = 1.0 / jnp.sum(raised, axis=0, keepdims=True)
                e_ref[r, 2 * p + i, :, t] = raised.astype(BF)

    weave(*[preparation(r) for r in range(rows)])
    project()
    work = [(r, p) for r in range(rows) for p in range(HEADS // 2)]
    current, last = scores(*work[0]), None
    for at, (r, p) in enumerate(work):
        following = scores(*work[at + 1]) if at + 1 < len(work) else None
        finished = attended(*last) if last else None
        soften(r, p, current)
        if last:
            att_ref[last[0], 2 * last[1] * head : 2 * (last[1] + 1) * head] = finished
        current, last = following, (r, p)
    att_ref[last[0], 2 * last[1] * head : 2 * (last[1] + 1) * head] = attended(*last)


def gelu_parts(x):
    cdf = 0.5 * lax.erf(x * math.sqrt(0.5)) + 0.5
    bell = jnp.exp2(x * x * (-0.5 / math.log(2.0)) - 0.5 * math.log2(2.0 * math.pi))
    return x * cdf, cdf + x * bell


def feed_forward(index_ref, att_ref, mc_ref, ct_ref, packed_ref, *refs, pieces, shards):
    piece_refs = refs[:pieces]
    groups = 2 if pieces > 1 else 1
    lo_ref, gm_ref, ga_ref, gs_ref = refs[pieces : pieces + 4]
    gw_refs = refs[pieces + 4 : pieces + 4 + groups]
    (
        up_ref, down_ref, upt_ref, downt_ref, out_ref, outt_ref, up_acc, down_acc, out_acc, col_acc, col_ref,
        att_cat, mixed_ref, n_ref, norm_ref, ctt_ref, hidden_ref, gp_ref, gn_ref, scale_ref, lot_ref,
        branch_ref,
    ) = refs[pieces + 4 + groups :]
    rows, seq, width = ct_ref.shape
    ff = up_ref.shape[1]
    ffs = ff // shards
    own = width // pieces
    step = pl.program_id(0)

    @pl.when(step == 0)
    def _():
        for acc in (up_acc, down_acc, out_acc, col_acc):
            acc[...] = jnp.zeros_like(acc)
        for i, ref in enumerate(piece_refs):
            here = pl.ds(pl.multiple_of(index_ref[i] * own, 16), own)
            for j in range(shards):
                up_ref[here, j * ffs : (j + 1) * ffs] = ref[2 * j * own : (2 * j + 1) * own]
                down_ref[here, j * ffs : (j + 1) * ffs] = ref[(2 * j + 1) * own : (2 * j + 2) * own]
            out_ref[here, :] = ref[2 * shards * own :]
        upt_ref[...] = up_ref[...].T
        downt_ref[...] = down_ref[...].T
        outt_ref[...] = out_ref[...].T
        load_columns(packed_ref, col_ref, (5, 6))

    def lanes_of(r):
        return slice(r * seq, (r + 1) * seq)

    def spots_of(r):
        return [slice(at, at + LANES) for at in range(r * seq, (r + 1) * seq, LANES)]

    def preparation(r):
        lanes = lanes_of(r)

        def turn():
            ctt_ref[:, lanes] = ct_ref[r].T
            att_cat[:, lanes] = att_ref[r]

        def branch():
            mixed_ref[:, lanes] = mc_ref[r] + mm(outt_ref[...], att_ref[r])

        def norm(t):
            n, scale = norm_columns(mixed_ref[:, t])
            n_ref[:, t] = n
            scale_ref[0:1, t] = scale
            norm_ref[:, t] = (n * col_ref[0] + col_ref[1]).astype(BF)

        return [turn, branch] + [functools.partial(norm, t) for t in spots_of(r)]

    def activation(block):
        pre = mm(upt_ref[block], norm_ref[...])
        grad_hidden = mm(downt_ref[block], ctt_ref[...])
        for low in range(0, block.stop - block.start, 16):
            part = slice(low, low + 16)
            here = slice(block.start + low, block.start + low + 16)
            hidden, slope = gelu_parts(pre[part])
            hidden_ref[here] = hidden.astype(BF)
            gp_ref[here] = (grad_hidden[part] * slope).astype(BF)

    def norm_back(r):
        spots = spots_of(r)
        mean_e = [jnp.zeros((8, LANES), F32) for _ in spots]
        mean_en = [jnp.zeros((8, LANES), F32) for _ in spots]
        means = []

        def sums(d):
            column = col_ref[0, d]
            gain_sum, shift_sum = col_acc[0, d], col_acc[1, d]
            for i, t in enumerate(spots):
                grad_n = gn_ref[d, t]
                product = grad_n * n_ref[d, t]
                gain_sum += product
                shift_sum += grad_n
                mean_e[i] += fold(grad_n * column)
                mean_en[i] += fold(product * column)
            col_acc[0, d] = gain_sum
            col_acc[1, d] = shift_sum

        def finish():
            for i in range(len(spots)):
                me = jnp.sum(mean_e[i], axis=0, keepdims=True) * (1.0 / width)
                men = jnp.sum(mean_en[i], axis=0, keepdims=True) * (1.0 / width)
                means.append((me, men))

        def apply(d):
            for i, t in enumerate(spots):
                me, men = means[i]
                change = scale_ref[0:1, t] * (gn_ref[d, t] * col_ref[0, d] - me - n_ref[d, t] * men)
                grad_mixed = ctt_ref[d, t].astype(F32) + change
                gm_ref[r, d, i * LANES : (i + 1) * LANES] = grad_mixed
                branch_ref[d, t] = grad_mixed.astype(BF)

        def attended():
            ga_ref[r] = mm(out_ref[...], branch_ref[:, lanes_of(r)]).astype(BF)

        def turn():
            lo_ref[r] = lot_ref[:, lanes_of(r)].T

        pieces = [functools.partial(sums, d) for d in tiles(width, 32)] + [finish]
        return pieces + [functools.partial(apply, d) for d in tiles(width, 32)] + [attended, turn]

    weave(*[preparation(r) for r in range(rows)])
    for block in tiles(ff, 128):
        activation(block)
    gn_ref[...] = mm(up_ref[...], gp_ref[...])
    lot_ref[...] = (mixed_ref[...] + mm(down_ref[...], hidden_ref[...])).astype(BF)
    down_acc[...] += mm_nt(ctt_ref[...], hidden_ref[...])
    up_acc[...] += mm_nt(norm_ref[...], gp_ref[...])
    weave(*[norm_back(r) for r in range(rows)])
    out_acc[...] += mm_nt(att_cat[...], branch_ref[...])

    @pl.when(step == pl.num_programs(0) - 1)
    def _():
        for i in range(pieces):
            here = pl.ds(pl.multiple_of(index_ref[i] * own, 16), own)
            place = gw_refs[i % groups]
            for j in range(shards):
                cols = slice(j * ffs, (j + 1) * ffs)
                place[i // groups, :, 2 * j * ffs : (2 * j + 1) * ffs] = up_acc[here, cols].astype(BF)
                place[i // groups, :, (2 * j + 1) * ffs : (2 * j + 2) * ffs] = down_acc[here, cols].astype(BF)
            place[i // groups, :, 2 * ff :] = out_acc[here, :].astype(BF)
        gs_ref[...] = jnp.zeros_like(gs_ref)
        for i in range(2):
            gs_ref[5 + i : 6 + i] = jnp.sum(col_acc[i].T, axis=0, keepdims=True)


def backward_attention(
    q_ref, k_ref, v_ref, e_ref, att_ref, inv_ref, norm_ref, ga_ref, index_ref, w_ref, start_ref, gn_ref, *refs, pieces
):
    gw_refs = refs[:-5]
    proj_ref, w_acc, norm_cat, soft_ref, logit_ref = refs[-5:]
    rows, seq, width = v_ref.shape
    own = width // pieces
    head = width // HEADS
    step = pl.program_id(0)

    @pl.when(step == 0)
    def _():
        w_acc[...] = jnp.zeros_like(w_acc) if start_ref is None else start_ref[...]

    zero = jnp.zeros((head, seq), BF)
    work = [(r, p) for r in range(rows) for p in range(HEADS // 2)]

    def opening(r, p):
        grads, inners = [], []
        for h in (2 * p, 2 * p + 1):
            part = slice(h * head, (h + 1) * head)
            grad_att = ga_ref[r, part].astype(F32) * inv_ref[r, h : h + 1]
            inners.append(jnp.sum(grad_att * att_ref[r, part].astype(F32), axis=0, keepdims=True))
            grads.append(grad_att.astype(BF))
        low, high = grads
        both = jnp.concatenate([jnp.concatenate([low, zero], axis=1), jnp.concatenate([zero, high], axis=1)], axis=0)
        product = mm(v_ref[r, :, 2 * p * head : 2 * (p + 1) * head], both)
        soft_ref[r, 2 * p] = product[:, :seq]
        soft_ref[r, 2 * p + 1] = product[:, seq:]
        return jnp.concatenate(grads, axis=0), inners

    ready = opening(*work[0])
    for at, (r, p) in enumerate(work):
        grad_att, inners = ready
        if at + 1 < len(work):
            ready = opening(*work[at + 1])
        for i, h in enumerate((2 * p, 2 * p + 1)):
            for t in tiles(seq, 32):
                raised = e_ref[r, h, t].astype(F32)
                logit_ref[r, h, t] = (raised * (soft_ref[r, h, t] - inners[i])).astype(BF)
        part = slice(2 * p * head, 2 * (p + 1) * head)
        pair = slice(2 * p, 2 * p + 2)
        beside = jnp.concatenate([logit_ref[r, 2 * p], logit_ref[r, 2 * p + 1]], axis=1)
        grad_q = mm(k_ref[r, part], beside)
        grad_k = mm_nt(q_ref[r, part], logit_ref[r, pair].reshape(2 * seq, seq))
        grad_v = mm_nt(grad_att, e_ref[r, pair].reshape(2 * seq, seq))
        for i in range(2):
            place = slice(r * seq, (r + 1) * seq)
            own_rows, own_cols = slice(i * head, (i + 1) * head), slice(i * seq, (i + 1) * seq)
            for j, grad in enumerate((grad_q, grad_k, grad_v)):
                first = j * width + (2 * p + i) * head
                mine = grad[own_rows, own_cols]
                proj_ref[first : first + head, place] = (mine * head ** (-0.5) if j == 0 else mine).astype(BF)
    grad_normed = mm(w_ref[...], proj_ref[...]).astype(BF)
    for r in range(rows):
        norm_cat[:, r * seq : (r + 1) * seq] = norm_ref[r]
        gn_ref[r] = grad_normed[:, r * seq : (r + 1) * seq]
    w_acc[...] += mm_nt(norm_cat[...], proj_ref[...])

    @pl.when(step == pl.num_programs(0) - 1)
    def _():
        if start_ref is None:
            gw_refs[0][...] = w_acc[...]
        else:
            groups = len(gw_refs)
            for i in range(pieces):
                here = pl.ds(pl.multiple_of(index_ref[i] * own, 16), own)
                gw_refs[i % groups][i // groups] = w_acc[here, :].astype(BF)


def backward_conv(
    x_ref, aux_ref, mc_ref, gm_ref, gn_ref, packed_ref, other_ref, part_ref, ig_ref, gs_ref,
    acc_ref, col_ref, n_ref, g_ref, turn_ref,
):
    rows, width, seq = x_ref.shape
    step = pl.program_id(0)

    @pl.when(step == 0)
    def _():
        acc_ref[...] = jnp.zeros_like(acc_ref)
        load_columns(packed_ref, col_ref, range(4))

    spots = tiles(seq, LANES)
    for r in range(rows):
        scales = []
        for t in spots:
            n, scale = norm_columns(mc_ref[r, :, t])
            n_ref[r, :, t] = n
            scales.append(scale)
        mean_e = [jnp.zeros((8, LANES), F32) for _ in spots]
        mean_en = [jnp.zeros((8, LANES), F32) for _ in spots]
        for d in tiles(width, 32):
            column = col_ref[3, d]
            gain_sum, shift_sum = acc_ref[3, d], acc_ref[4, d]
            for i, t in enumerate(spots):
                grad_n = gn_ref[r, d, t].astype(F32)
                product = grad_n * n_ref[r, d, t]
                gain_sum += product
                shift_sum += grad_n
                mean_e[i] += fold(grad_n * column)
                mean_en[i] += fold(product * column)
            acc_ref[3, d] = gain_sum
            acc_ref[4, d] = shift_sum
        for i, t in enumerate(spots):
            me = jnp.sum(mean_e[i], axis=0, keepdims=True) * (1.0 / width)
            men = jnp.sum(mean_en[i], axis=0, keepdims=True) * (1.0 / width)
            for d in tiles(width, 64):
                e = gn_ref[r, d, t].astype(F32) * col_ref[3, d]
                g_ref[r, d, t] = gm_ref[r, d, t] + scales[i] * (e - me - n_ref[r, d, t] * men)
        links, next_links = aux_ref[r, 0:1], aux_ref[r, 1:2]
        for d in tiles(width, 32):
            g = g_ref[r, d]
            base = x_ref[r, d].astype(F32)
            before = pltpu.roll(g, 1, 1) * links
            after = pltpu.roll(g, seq - 1, 1) * next_links
            acc_ref[0, d] += fold_lanes(base * after)
            acc_ref[1, d] += fold_lanes(base * g)
            acc_ref[2, d] += fold_lanes(base * before)
            conv0, conv1, conv2 = [twice(col_ref[i, d], seq) for i in range(3)]
            turn_ref[r, d] = (g + conv1 * g + conv0 * after + conv2 * before).astype(BF)
        ig_ref[r] = turn_ref[r].T

    @pl.when(step == pl.num_programs(0) - 1)
    def _():
        gs_ref[...] = other_ref[...]
        for i in range(5):
            gs_ref[i : i + 1] += jnp.sum(acc_ref[i].T, axis=0, keepdims=True)


def in_hbm(values):
    return pltpu.with_memory_space_constraint(values, pltpu.HBM)


def by_row(shape, rows, first=0):
    tail = tuple(shape[1:])
    return pl.BlockSpec((rows,) + tail, lambda i, *_: (i + first,) + (0,) * len(tail))


def whole(shape):
    place = (0,) * len(shape)
    return pl.BlockSpec(tuple(shape), lambda i, *_: place, pipeline_mode=pl.Buffered(1))


def step_rows(count, most):
    return max(r for r in range(1, most + 1) if count % r == 0)


def call(body, name, scalars, rows, row_args, args, row_outs, outs, scratch, span=None, into=None, near=()):
    first, count = span or (0, row_args[0].shape[0])
    skip = first // rows
    in_specs = [by_row(a.shape, rows, skip if a.shape[0] > count else 0) for a in row_args]
    in_specs += [whole(a.shape) for a in args]
    aliases = {}
    if into is not None:
        in_specs.append(pl.BlockSpec(memory_space=pl.ANY))
        aliases = {len(scalars) + len(in_specs) - 1: 0}
    spec = pltpu.PrefetchScalarGridSpec(
        num_scalar_prefetch=len(scalars),
        grid=(count // rows,),
        in_specs=in_specs,
        out_specs=[by_row(s, rows, skip if s[0] > count else 0) for s, _ in row_outs] + [whole(s) for s, _ in outs],
        scratch_shapes=[pltpu.VMEM(s, t) for s, t in scratch],
    )
    return pl.pallas_call(
        body,
        grid_spec=spec,
        out_shape=[(jax.ShapeDtypeStruct if "out" + str(i) in near else pltpu.HBM)(s, t) for i, (s, t) in enumerate(row_outs)]
        + [jax.ShapeDtypeStruct(s, t) for s, t in outs],
        input_output_aliases=aliases,
        compiler_params=pltpu.CompilerParams(dimension_semantics=("arbitrary",), vmem_limit_bytes=VMEM_LIMITS[name] * MIB),
        name=name,
    )(*scalars, *[a if i in near else in_hbm(a) for i, a in enumerate(row_args)], *args, *(() if into is None else (into,)))


def small_call(body, name, args, outs, scratch=()):
    return pl.pallas_call(
        body,
        out_shape=[jax.ShapeDtypeStruct(s, t) for s, t in outs],
        scratch_shapes=[pltpu.VMEM(s, t) for s, t in scratch],
        compiler_params=pltpu.CompilerParams(vmem_limit_bytes=16 * MIB),
        name=name,
    )(*args)


def run_forward(index, tokens, segment_ids, valid_len, pieces):
    count, seq, width = tokens.shape
    flipped = (count, width, seq)
    rows = step_rows(count, 2)
    row_outs = [
        (flipped, BF), (flipped, F32), (flipped, BF), (flipped, BF), (flipped, BF), ((count, seq, width), BF),
        ((count, HEADS, seq, seq), BF), (flipped, BF), ((count, 8, seq), F32), ((count, 8, seq), F32),
    ]
    return call(
        functools.partial(forward_attention, pieces=len(pieces)), "forward_attention", (index, valid_len),
        rows, (tokens,), (in_hbm(segment_ids), *pieces),
        row_outs, [((width, VECTORS), BF), ((width, 3 * width), BF)],
        [
            ((3 * width, width), BF), ((width, 3 * width + VECTORS), BF), ((5, width, LANES), F32),
            ((rows, seq, seq), F32), ((rows, seq, width), BF), ((rows, width, seq), BF),
        ],
    )


def run_feed_forward(index, att, mixed, cotangent, packed, pieces, shards):
    count, seq, width = cotangent.shape
    own = width // len(pieces)
    ff = shards * width
    groups = 2 if len(pieces) > 1 else 1
    rows = step_rows(count, 2)
    wide = rows * seq
    row_outs = [((count, seq, width), BF), ((count, width, seq), F32), ((count, width, seq), BF)]
    grads = ((len(pieces) // groups, own, 2 * ff + width), BF)
    return call(
        functools.partial(feed_forward, pieces=len(pieces), shards=shards), "feed_forward", (index,),
        rows, (att, mixed, cotangent), (packed, *pieces),
        row_outs, [((8, width), F32)] + [grads] * groups,
        [((width, ff), BF)] * 2 + [((ff, width), BF)] * 2 + [((width, width), BF)] * 2
        + [((width, ff), F32)] * 2 + [((width, width), F32), ((2, width, LANES), F32), ((2, width, LANES), F32)]
        + [((width, wide), BF), ((width, wide), F32), ((width, wide), F32), ((width, wide), BF), ((width, wide), BF)]
        + [((ff, wide), BF)] * 2
        + [((width, wide), F32), ((8, wide), F32), ((width, wide), BF), ((width, wide), BF)],
        near=("out2",),
    )


def run_backward_attention(index, weight, kept, grad_att, pieces, span, start):
    count, seq, width = kept[2].shape
    own = width // pieces
    groups = 2 if pieces > 1 else 1
    rows = step_rows(span[1], 2)
    row_args = (*kept, grad_att)
    many = len(row_args)

    def body(index_ref, *refs):
        w_ref, rest = refs[many], refs[many + 1 :]
        start_ref, rest = (None, rest) if start is None else (rest[0], rest[1:])
        backward_attention(*refs[:many], index_ref, w_ref, start_ref, *rest, pieces=pieces)

    outs = [((width, 3 * width), F32)] if start is None else [((pieces // groups, own, 3 * width), BF)] * groups
    return call(
        body, "backward_attention", (index,), rows, row_args, (weight,) if start is None else (weight, start),
        [((span[1], width, seq), BF)], outs,
        [
            ((3 * width, rows * seq), BF), ((width, 3 * width), F32), ((width, rows * seq), BF),
            ((rows, HEADS, seq, seq), F32), ((rows, HEADS, seq, seq), BF),
        ],
        span=span, near=("out0", many - 1),
    )


def run_backward_conv(x, aux, mixed, grad_mixed, grad_normed, packed, other, span, into):
    count, width, seq = x.shape
    rows = step_rows(span[1], 2)

    def body(*refs):
        if into is None:
            backward_conv(*refs[:7], None, *refs[7:])
        else:
            backward_conv(*refs)

    return call(
        body, "backward_conv", (), rows,
        (x, aux, mixed, grad_mixed, grad_normed), (packed, other),
        [((count, seq, width), BF)], [((8, width), F32)],
        [
            ((5, width, LANES), F32), ((4, width, LANES), F32), ((rows, width, seq), F32), ((rows, width, seq), F32),
            ((rows, width, seq), BF),
        ],
        span=span, into=into, near=(4,),
    )


def halves(count):
    early = count // 3
    return ((0, early), (early, count - early)) if early % 2 == 0 and early else ((0, count // 2), (count // 2, count - count // 2))


def exchange(values, axis, offset):
    size = lax.axis_size(axis)
    return lax.ppermute(values, axis, [(i, i ^ offset) for i in range(size)])


def add_halves(mine, received):
    count, own, cols = mine.shape

    def body(mine_ref, received_ref, *out_refs):
        for i, ref in enumerate(out_refs):
            ref[...] = (mine_ref[i].astype(F32) + received_ref[i].astype(F32)).astype(BF)

    return small_call(body, "add_halves", (mine, received), [((own, cols), BF)] * count)


def add_wide(*items):
    return tree_sum(item.astype(F32) for item in items)


def add_shard_vectors(items, own):
    def body(*refs):
        total = tree_sum(ref[...] for ref in refs[:-5])
        refs[-5][...] = total[0:3, :own]
        for i in range(4):
            refs[i - 4][...] = total[3 + i : 4 + i, :own]

    return small_call(body, "add_shard_vectors", items, [((3, own), F32)] + [((1, own), F32)] * 4)


def direct_plan(tokens, segment_ids, valid_len, qkv_weight, out_weight, up_weight, down_weight, conv_weight, vectors, cotangent):
    count, seq, width = tokens.shape
    own, ffs = up_weight.shape
    dp, mp = lax.axis_size("dp"), lax.axis_size("mp")
    me = lax.axis_index("dp")
    offsets = [2 * p for p in range(dp // 2)]
    index = jnp.stack([me ^ (p ^ c) for p in offsets for c in range(2)]).astype(jnp.int32)
    narrow, ff_own = small_call(
        pack_weights, "pack_weights",
        [in_hbm(a) for a in (qkv_weight, up_weight, down_weight, conv_weight, *[v.reshape(1, own) for v in vectors])],
        [((own, 3 * width + VECTORS), BF), ((2 * own, ffs), BF)], [((VECTORS, VECTORS), F32)],
    )
    plane = [narrow] + [exchange(narrow, "dp", p) for p in offsets[1:]]
    shards = [ff_own] + [exchange(ff_own, "mp", j) for j in range(1, mp)]
    pieces = [piece for a in plane for piece in (a, exchange(a, "dp", 1))]
    column = jnp.concatenate(shards + [out_weight], axis=0)
    columns = [column] + [exchange(column, "dp", p) for p in offsets[1:]]
    x, mixed, normed, q, k, v, raised, att, inverse, aux, packed, weight = run_forward(
        index, tokens, segment_ids, valid_len, pieces
    )
    columns, att = lax.optimization_barrier((columns, att))
    pieces = [piece for a in columns for piece in (a, exchange(a, "dp", 1))]
    layer_out, grad_mixed, grad_att, sums2, mine, theirs = run_feed_forward(
        index, att, mixed, cotangent, packed, pieces, mp
    )
    received = exchange(theirs, "dp", 1)
    early, late = halves(count)
    kept = (q, k, v, raised, att, inverse, normed)
    grad_normed1, start = run_backward_attention(index, weight, kept, grad_att, dp, early, None)
    received, start = lax.optimization_barrier((received, start))
    parts = list(add_halves(mine, received))
    parts[0], start = lax.optimization_barrier((parts[0], start))
    plane = [parts[0]] + [exchange(parts[i], "dp", p) for i, p in enumerate(offsets) if i]
    grad_normed2, mine_a, theirs_a = run_backward_attention(index, weight, kept, grad_att, dp, late, start)
    plane, theirs_a = lax.optimization_barrier((plane, theirs_a))
    received_a = exchange(theirs_a, "dp", 1)
    total = add_wide(*plane).astype(BF)
    half = 2 * ffs * (mp // 2)
    near, far, out_part = total[:, :half], total[:, half:], total[:, 2 * half :]
    received_f = exchange(far, "mp", 2)
    near, grad_normed1 = lax.optimization_barrier((near, grad_normed1))
    some_grad, sums = run_backward_conv(x, aux, mixed, grad_mixed, grad_normed1, packed, sums2, early, None)
    received_a, sums = lax.optimization_barrier((received_a, sums))
    parts = list(add_halves(mine_a, received_a))
    parts[0], sums = lax.optimization_barrier((parts[0], sums))
    plane_a = [parts[0]] + [exchange(parts[i], "dp", p) for i, p in enumerate(offsets) if i]
    input_grad, sums = run_backward_conv(x, aux, mixed, grad_mixed, grad_normed2, packed, sums, late, some_grad)
    received_s = exchange(sums, "dp", 1)
    plane_a, received_f, sums = lax.optimization_barrier((plane_a, received_f, sums))
    total = lax.optimization_barrier(add_wide(*plane_a).astype(BF))
    received_1 = exchange(total, "mp", 2)
    near_sum = add_wide(near, received_f[:, :half])
    out_sum = lax.optimization_barrier(add_wide(out_part, received_f[:, half:]).astype(BF))
    keep = near_sum[:, : 2 * ffs]
    send = jnp.concatenate([near_sum[:, 2 * ffs :].astype(BF), out_sum], axis=1)
    received_n = exchange(send, "mp", 1)
    received_s, _, _ = lax.optimization_barrier((received_s, total, send))
    sums = sums + received_s
    for offset in offsets[1:]:
        if offset & (offset - 1) == 0:
            sums = sums + exchange(sums, "dp", offset)
    vectors = lax.dynamic_slice_in_dim(sums, me * own, own, axis=1)
    vectors = vectors + exchange(vectors, "mp", 2)
    received_v = exchange(vectors, "mp", 1)
    received_1, _ = lax.optimization_barrier((received_1, vectors))
    total = lax.optimization_barrier(add_wide(total, received_1).astype(BF))
    received_2 = exchange(total, "mp", 1)
    grad_up = keep[:, :ffs] + received_n[:, :ffs].astype(F32)
    grad_down = keep[:, ffs:] + received_n[:, ffs : 2 * ffs].astype(F32)
    grad_out = add_wide(out_sum, received_n[:, 2 * ffs :])
    grad_qkv = add_wide(total, received_2)
    grad_conv, *grads = add_shard_vectors((vectors, received_v), own)
    return (layer_out, input_grad, grad_qkv, grad_out, grad_up, grad_down, grad_conv, *[g.reshape(own) for g in grads])


def gathered_plan(tokens, segment_ids, valid_len, qkv_weight, out_weight, up_weight, down_weight, conv_weight, vectors, cotangent):
    count, seq, width = tokens.shape
    own = qkv_weight.shape[0]
    dp = width // own
    columns = jnp.stack([conv_weight[0], conv_weight[1], conv_weight[2], *vectors], axis=1)
    narrow = jnp.concatenate([qkv_weight, jnp.pad(columns, ((0, 0), (0, VECTORS - 7))), out_weight], axis=1)
    wide = lax.all_gather(narrow, "dp", axis=0, tiled=True)
    both = lax.all_gather(jnp.concatenate([up_weight, down_weight], axis=0), "mp", axis=1, tiled=True)
    ff = both.shape[1]
    shards = ff // width
    both = lax.all_gather(both, "dp", axis=0).reshape(dp, 2, own, shards, width)
    both = both.transpose(3, 1, 0, 2, 4).reshape(2 * ff, width)
    column = jnp.concatenate([both, wide[:, 3 * width + VECTORS :]], axis=0)
    index = jnp.zeros((1,), jnp.int32)
    x, mixed, normed, q, k, v, raised, att, inverse, aux, packed, weight = run_forward(
        index, tokens, segment_ids, valid_len, [wide[:, : 3 * width + VECTORS]]
    )
    layer_out, grad_mixed, grad_att, sums2, grads = run_feed_forward(
        index, att, mixed, cotangent, packed, [column], shards
    )
    early, late = halves(count)
    kept = (q, k, v, raised, att, inverse, normed)
    grad_normed1, start = run_backward_attention(index, weight, kept, grad_att, 1, early, None)
    grad_normed2, grad_qkv = run_backward_attention(index, weight, kept, grad_att, 1, late, start)
    some_grad, sums = run_backward_conv(x, aux, mixed, grad_mixed, grad_normed1, packed, sums2, early, None)
    input_grad, sums = run_backward_conv(x, aux, mixed, grad_mixed, grad_normed2, packed, sums, late, some_grad)
    grad_ff = grads[0, :, : 2 * ff].reshape(width, shards, 2, width).transpose(0, 2, 1, 3).reshape(width, 2 * ff)
    grad_ff = lax.psum_scatter(grad_ff, "dp", scatter_dimension=0, tiled=True).reshape(own, 2, ff)
    grad_ff = lax.psum_scatter(grad_ff, "mp", scatter_dimension=2, tiled=True).astype(F32)
    grad_attn = jnp.concatenate([grad_qkv[0], grads[0, :, 2 * ff :]], axis=1)
    grad_attn = lax.psum_scatter(grad_attn, "dp", scatter_dimension=0, tiled=True)
    grad_attn = lax.psum(grad_attn, "mp").astype(F32)
    sums = lax.psum(sums, ("dp", "mp"))
    sums = lax.dynamic_slice_in_dim(sums, lax.axis_index("dp") * own, own, axis=1)
    return (
        layer_out, input_grad, grad_attn[:, : 3 * width], grad_attn[:, 3 * width :],
        grad_ff[:, 0], grad_ff[:, 1], sums[0:3], sums[3], sums[4], sums[5], sums[6],
    )


def on_device(
    tokens, segment_ids, valid_len, qkv_weight, out_weight, up_weight, down_weight, conv_weight,
    ln1_gain, ln1_shift, ln2_gain, ln2_shift, cotangent,
):
    own, ffs = up_weight.shape
    direct = own % 16 == 0 and ffs == tokens.shape[2] and own <= VECTORS and lax.axis_size("mp") == 4
    plan = direct_plan if direct else gathered_plan
    return plan(
        tokens, segment_ids, valid_len, qkv_weight, out_weight, up_weight, down_weight, conv_weight,
        (ln1_gain, ln1_shift, ln2_gain, ln2_shift), cotangent,
    )


def solution(mesh):
    rows = P(("dp", "mp"), None, None)
    weights = (P("dp", None), P("dp", None), P("dp", "mp"), P("dp", "mp"), P(None, "dp"))
    vectors = (P("dp"),) * 4
    return jax.shard_map(
        on_device,
        mesh=mesh,
        in_specs=(rows, P(("dp", "mp"), None), P(("dp", "mp"))) + weights + vectors + (rows,),
        out_specs=(rows, rows) + weights + vectors,
        check_vma=False,
    )
```

```python
import functools
import math

import jax
import jax.numpy as jnp
from jax import lax
from jax.experimental import pallas as pl
from jax.experimental.pallas import tpu as pltpu
from jax.sharding import PartitionSpec as P

HEADS = 6
VECTORS = 128
LANES = 128
BF = jnp.bfloat16
F32 = jnp.float32
MIB = 1024 * 1024
VMEM_LIMITS = dict(forward_attention=26, feed_forward=36, backward=36)


def mm(lhs, rhs):
    return lax.dot_general(lhs, rhs, (((1,), (0,)), ((), ())), preferred_element_type=F32)


def mm_nt(lhs, rhs):
    return lax.dot_general(lhs, rhs, (((1,), (1,)), ((), ())), preferred_element_type=F32)


def tree_sum(items):
    items = list(items)
    while len(items) > 1:
        items = [a + b for a, b in zip(items[::2], items[1::2])]
    return items[0]


def pack_weights(qkv_ref, up_ref, down_ref, conv_ref, g1_ref, s1_ref, g2_ref, s2_ref, narrow_ref, ff_ref, rows_ref):
    own, ffs = up_ref.shape
    rows_ref[...] = jnp.zeros_like(rows_ref)
    rows_ref[0:3, :own] = conv_ref[...].astype(F32)
    for i, ref in enumerate((g1_ref, s1_ref, g2_ref, s2_ref)):
        rows_ref[3 + i : 4 + i, :own] = ref[...].astype(F32)
    wide = qkv_ref.shape[1]
    narrow_ref[:, :wide] = qkv_ref[...]
    narrow_ref[:, wide:] = rows_ref[...].T[:own].astype(BF)
    ff_ref[:own] = up_ref[...]
    ff_ref[own:] = down_ref[...]


def tiles(total, size):
    return [slice(at, at + size) for at in range(0, total, size)]


def weave(*strands):
    strands = [strand for strand in strands if strand]
    total = sum(len(strand) for strand in strands)
    pieces = [((i + 0.5) / len(strand), j, piece) for j, strand in enumerate(strands) for i, piece in enumerate(strand)]
    assert len(pieces) == total
    for _, _, piece in sorted(pieces, key=lambda item: item[:2]):
        piece()


def twice(tile, lanes):
    return jnp.concatenate([tile] * (lanes // LANES), axis=1)


def load_columns(packed_ref, col_ref, places):
    for i, place in enumerate(places):
        column = packed_ref[:, place : place + 1].astype(F32)
        col_ref[i] = jnp.broadcast_to(column, (column.shape[0], LANES))


def column_mean(values):
    return jnp.sum(values, axis=0, keepdims=True) * (1.0 / values.shape[0])


def norm_columns(values):
    centred = values - column_mean(values)
    scale = lax.rsqrt(column_mean(centred * centred) + 1e-06)
    return centred * scale, scale


def fold(values):
    rows, lanes = values.shape
    return jnp.sum(values.reshape(rows // 8, 8, lanes), axis=0)


def fold_lanes(values):
    return sum(values[:, t] for t in tiles(values.shape[1], LANES))


def forward_attention(index_ref, len_ref, tok_ref, seg_ref, *refs, pieces):
    piece_refs = refs[:pieces]
    (
        x_ref, mc_ref, norm_ref, q_ref, k_ref, v_ref, e_ref, att_ref, inv_ref, aux_ref, packed_ref, w_ref,
        wt_ref, wide_ref, col_ref, bias_ref, key_ref, value_ref,
    ) = refs[pieces:]
    rows, seq, width = tok_ref.shape
    head = width // HEADS
    step = pl.program_id(0)

    @pl.when(step == 0)
    def _():
        own = width // pieces
        for i, ref in enumerate(piece_refs):
            wide_ref[pl.ds(pl.multiple_of(index_ref[i] * own, 16), own), :] = ref[...]
        w_ref[...] = wide_ref[:, : 3 * width]
        wt_ref[:width] = (wide_ref[:, :width].astype(F32) * head ** (-0.5)).astype(BF).T
        wt_ref[width:] = wide_ref[:, width : 3 * width].T
        packed_ref[...] = wide_ref[:, 3 * width :]
        load_columns(packed_ref, col_ref, range(5))

    place = lax.broadcasted_iota(jnp.int32, (1, seq), 1)
    zero = jnp.zeros((head, seq), BF)

    def preparation(r):
        known = {}

        def start():
            segs = seg_ref[pl.ds(step * rows + r, 1), :].astype(F32)
            valid = place < len_ref[step * rows + r]
            number = jnp.where(valid, segs, -1.0)
            links = jnp.where(valid & (place > 0) & (number == pltpu.roll(number, 1, 1)), 1.0, 0.0)
            next_links = jnp.where(place < seq - 1, pltpu.roll(links, seq - 1, 1), 0.0)
            none = jnp.zeros_like(links)
            aux = jnp.concatenate([links, next_links, number, none, none, none, none, none], axis=0)
            aux_ref[r] = aux
            x_ref[r] = tok_ref[r].T
            known.update(segs=segs, links=links, next_links=next_links, key_number=aux.T[:, 2:3])

        def mask(t):
            row_id = lax.broadcasted_iota(jnp.int32, (64, seq), 0) + t.start
            col_id = lax.broadcasted_iota(jnp.int32, (64, seq), 1)
            allowed = (known["key_number"][t] == known["segs"]) | (row_id == col_id)
            bias_ref[r, t] = jnp.where(allowed, 0.0, -1e30)

        def conv(t):
            base = x_ref[r, t].astype(F32)
            before = pltpu.roll(base, 1, 1) * known["links"]
            after = pltpu.roll(base, seq - 1, 1) * known["next_links"]
            conv0, conv1, conv2 = [twice(col_ref[i, t], seq) for i in range(3)]
            mc_ref[r, t] = base + before * conv0 + base * conv1 + after * conv2

        def norm(t):
            n, _ = norm_columns(mc_ref[r, :, t])
            norm_ref[r, :, t] = (n * col_ref[3] + col_ref[4]).astype(BF)

        pieces = [start] + [functools.partial(conv, t) for t in tiles(width, 32)]
        pieces += [functools.partial(norm, t) for t in tiles(seq, LANES)]
        return pieces + [functools.partial(mask, t) for t in tiles(seq, 64)]

    def project():
        normed = jnp.concatenate([norm_ref[r] for r in range(rows)], axis=1)
        for i, ref in enumerate((q_ref, k_ref, value_ref)):
            part = mm(wt_ref[i * width : (i + 1) * width], normed).astype(BF)
            for r in range(rows):
                ref[r] = part[:, r * seq : (r + 1) * seq]
        for r in range(rows):
            key_ref[r] = k_ref[r].T
            v_ref[r] = value_ref[r].T

    def scores(r, p):
        low, high = [q_ref[r, h * head : (h + 1) * head] for h in (2 * p, 2 * p + 1)]
        both = jnp.concatenate([jnp.concatenate([low, zero], axis=1), jnp.concatenate([zero, high], axis=1)], axis=0)
        return mm(key_ref[r, :, 2 * p * head : 2 * (p + 1) * head], both)

    def attended(r, p):
        both = jnp.concatenate([e_ref[r, 2 * p], e_ref[r, 2 * p + 1]], axis=1)
        product = mm(value_ref[r, 2 * p * head : 2 * (p + 1) * head], both)
        parts = []
        for i in range(2):
            att = product[i * head : (i + 1) * head, i * seq : (i + 1) * seq] * inv_ref[r, 2 * p + i : 2 * p + i + 1]
            parts.append(att.astype(BF))
        return jnp.concatenate(parts, axis=0)

    def soften(r, p, product):
        for i in range(2):
            for t in tiles(seq, LANES):
                masked = product[:, i * seq + t.start : i * seq + t.stop] + bias_ref[r, :, t]
                raised = jnp.exp(masked - jnp.max(masked, axis=0, keepdims=True))
                inv_ref[r, 2 * p + i : 2 * p + i + 1, t] = 1.0 / jnp.sum(raised, axis=0, keepdims=True)
                e_ref[r, 2 * p + i, :, t] = raised.astype(BF)

    weave(*[preparation(r) for r in range(rows)])
    project()
    work = [(r, p) for r in range(rows) for p in range(HEADS // 2)]
    current, last = scores(*work[0]), None
    for at, (r, p) in enumerate(work):
        following = scores(*work[at + 1]) if at + 1 < len(work) else None
        finished = attended(*last) if last else None
        soften(r, p, current)
        if last:
            att_ref[last[0], 2 * last[1] * head : 2 * (last[1] + 1) * head] = finished
        current, last = following, (r, p)
    att_ref[last[0], 2 * last[1] * head : 2 * (last[1] + 1) * head] = attended(*last)


def gelu_parts(x):
    cdf = 0.5 * lax.erf(x * math.sqrt(0.5)) + 0.5
    bell = jnp.exp2(x * x * (-0.5 / math.log(2.0)) - 0.5 * math.log2(2.0 * math.pi))
    return x * cdf, cdf + x * bell


def feed_forward(index_ref, att_ref, mc_ref, ct_ref, packed_ref, *refs, pieces, shards):
    piece_refs = refs[:pieces]
    groups = 2 if pieces > 1 else 1
    lo_ref, gm_ref, ga_ref, gs_ref = refs[pieces : pieces + 4]
    gw_refs = refs[pieces + 4 : pieces + 4 + groups]
    (
        up_ref, down_ref, upt_ref, downt_ref, out_ref, outt_ref, up_acc, down_acc, out_acc, col_acc, col_ref,
        att_cat, mixed_ref, n_ref, norm_ref, ctt_ref, hidden_ref, gp_ref, gn_ref, scale_ref, lot_ref,
        branch_ref,
    ) = refs[pieces + 4 + groups :]
    rows, seq, width = ct_ref.shape
    ff = up_ref.shape[1]
    ffs = ff // shards
    own = width // pieces
    step = pl.program_id(0)

    @pl.when(step == 0)
    def _():
        for acc in (up_acc, down_acc, out_acc, col_acc):
            acc[...] = jnp.zeros_like(acc)
        for i, ref in enumerate(piece_refs):
            here = pl.ds(pl.multiple_of(index_ref[i] * own, 16), own)
            for j in range(shards):
                up_ref[here, j * ffs : (j + 1) * ffs] = ref[2 * j * own : (2 * j + 1) * own]
                down_ref[here, j * ffs : (j + 1) * ffs] = ref[(2 * j + 1) * own : (2 * j + 2) * own]
            out_ref[here, :] = ref[2 * shards * own :]
        upt_ref[...] = up_ref[...].T
        downt_ref[...] = down_ref[...].T
        outt_ref[...] = out_ref[...].T
        load_columns(packed_ref, col_ref, (5, 6))

    def lanes_of(r):
        return slice(r * seq, (r + 1) * seq)

    def spots_of(r):
        return [slice(at, at + LANES) for at in range(r * seq, (r + 1) * seq, LANES)]

    def preparation(r):
        lanes = lanes_of(r)

        def turn():
            ctt_ref[:, lanes] = ct_ref[r].T
            att_cat[:, lanes] = att_ref[r]

        def branch():
            mixed_ref[:, lanes] = mc_ref[r] + mm(outt_ref[...], att_ref[r])

        def norm(t):
            n, scale = norm_columns(mixed_ref[:, t])
            n_ref[:, t] = n
            scale_ref[0:1, t] = scale
            norm_ref[:, t] = (n * col_ref[0] + col_ref[1]).astype(BF)

        return [turn, branch] + [functools.partial(norm, t) for t in spots_of(r)]

    def activation(block):
        pre = mm(upt_ref[block], norm_ref[...])
        grad_hidden = mm(downt_ref[block], ctt_ref[...])
        for low in range(0, block.stop - block.start, 16):
            part = slice(low, low + 16)
            here = slice(block.start + low, block.start + low + 16)
            hidden, slope = gelu_parts(pre[part])
            hidden_ref[here] = hidden.astype(BF)
            gp_ref[here] = (grad_hidden[part] * slope).astype(BF)

    def norm_back(r):
        spots = spots_of(r)
        mean_e = [jnp.zeros((8, LANES), F32) for _ in spots]
        mean_en = [jnp.zeros((8, LANES), F32) for _ in spots]
        means = []

        def sums(d):
            column = col_ref[0, d]
            gain_sum, shift_sum = col_acc[0, d], col_acc[1, d]
            for i, t in enumerate(spots):
                grad_n = gn_ref[d, t]
                product = grad_n * n_ref[d, t]
                gain_sum += product
                shift_sum += grad_n
                mean_e[i] += fold(grad_n * column)
                mean_en[i] += fold(product * column)
            col_acc[0, d] = gain_sum
            col_acc[1, d] = shift_sum

        def finish():
            for i in range(len(spots)):
                me = jnp.sum(mean_e[i], axis=0, keepdims=True) * (1.0 / width)
                men = jnp.sum(mean_en[i], axis=0, keepdims=True) * (1.0 / width)
                means.append((me, men))

        def apply(d):
            for i, t in enumerate(spots):
                me, men = means[i]
                change = scale_ref[0:1, t] * (gn_ref[d, t] * col_ref[0, d] - me - n_ref[d, t] * men)
                grad_mixed = ctt_ref[d, t].astype(F32) + change
                gm_ref[r, d, i * LANES : (i + 1) * LANES] = grad_mixed
                branch_ref[d, t] = grad_mixed.astype(BF)

        def attended():
            ga_ref[r] = mm(out_ref[...], branch_ref[:, lanes_of(r)]).astype(BF)

        def turn():
            lo_ref[r] = lot_ref[:, lanes_of(r)].T

        pieces = [functools.partial(sums, d) for d in tiles(width, 32)] + [finish]
        return pieces + [functools.partial(apply, d) for d in tiles(width, 32)] + [attended, turn]

    weave(*[preparation(r) for r in range(rows)])
    for block in tiles(ff, 128):
        activation(block)
    gn_ref[...] = mm(up_ref[...], gp_ref[...])
    lot_ref[...] = (mixed_ref[...] + mm(down_ref[...], hidden_ref[...])).astype(BF)
    down_acc[...] += mm_nt(ctt_ref[...], hidden_ref[...])
    up_acc[...] += mm_nt(norm_ref[...], gp_ref[...])
    weave(*[norm_back(r) for r in range(rows)])
    out_acc[...] += mm_nt(att_cat[...], branch_ref[...])

    @pl.when(step == pl.num_programs(0) - 1)
    def _():
        for i in range(pieces):
            here = pl.ds(pl.multiple_of(index_ref[i] * own, 16), own)
            place = gw_refs[i % groups]
            for j in range(shards):
                cols = slice(j * ffs, (j + 1) * ffs)
                place[i // groups, :, 2 * j * ffs : (2 * j + 1) * ffs] = up_acc[here, cols].astype(BF)
                place[i // groups, :, (2 * j + 1) * ffs : (2 * j + 2) * ffs] = down_acc[here, cols].astype(BF)
            place[i // groups, :, 2 * ff :] = out_acc[here, :].astype(BF)
        gs_ref[...] = jnp.zeros_like(gs_ref)
        for i in range(2):
            gs_ref[5 + i : 6 + i] = jnp.sum(col_acc[i].T, axis=0, keepdims=True)


def backward(
    q_ref, k_ref, v_ref, e_ref, att_ref, inv_ref, norm_ref, ga_ref, x_ref, aux_ref, mc_ref, gm_ref,
    index_ref, w_ref, packed_ref, other_ref, start_ref, ig_ref, gs_ref, *refs, pieces,
):
    gw_refs = refs[:-11]
    (
        proj_ref, w_acc, norm_cat, soft_ref, logit_ref, gn_ref, acc_ref, col_ref, n_ref, g_ref, turn_ref
    ) = refs[-11:]
    rows, seq, width = v_ref.shape
    own = width // pieces
    head = width // HEADS
    step = pl.program_id(0)

    @pl.when(step == 0)
    def _():
        w_acc[...] = jnp.zeros_like(w_acc) if start_ref is None else start_ref[...]
        acc_ref[...] = jnp.zeros_like(acc_ref)
        load_columns(packed_ref, col_ref, range(4))

    zero = jnp.zeros((head, seq), BF)
    work = [(r, p) for r in range(rows) for p in range(HEADS // 2)]

    def opening(r, p):
        grads, inners = [], []
        for h in (2 * p, 2 * p + 1):
            part = slice(h * head, (h + 1) * head)
            grad_att = ga_ref[r, part].astype(F32) * inv_ref[r, h : h + 1]
            inners.append(jnp.sum(grad_att * att_ref[r, part].astype(F32), axis=0, keepdims=True))
            grads.append(grad_att.astype(BF))
        low, high = grads
        both = jnp.concatenate([jnp.concatenate([low, zero], axis=1), jnp.concatenate([zero, high], axis=1)], axis=0)
        product = mm(v_ref[r, :, 2 * p * head : 2 * (p + 1) * head], both)
        soft_ref[r, 2 * p] = product[:, :seq]
        soft_ref[r, 2 * p + 1] = product[:, seq:]
        return jnp.concatenate(grads, axis=0), inners

    ready = opening(*work[0])
    for at, (r, p) in enumerate(work):
        grad_att, inners = ready
        if at + 1 < len(work):
            ready = opening(*work[at + 1])
        for i, h in enumerate((2 * p, 2 * p + 1)):
            for t in tiles(seq, 32):
                raised = e_ref[r, h, t].astype(F32)
                logit_ref[r, h, t] = (raised * (soft_ref[r, h, t] - inners[i])).astype(BF)
        part = slice(2 * p * head, 2 * (p + 1) * head)
        pair = slice(2 * p, 2 * p + 2)
        beside = jnp.concatenate([logit_ref[r, 2 * p], logit_ref[r, 2 * p + 1]], axis=1)
        grad_q = mm(k_ref[r, part], beside)
        grad_k = mm_nt(q_ref[r, part], logit_ref[r, pair].reshape(2 * seq, seq))
        grad_v = mm_nt(grad_att, e_ref[r, pair].reshape(2 * seq, seq))
        for i in range(2):
            place = slice(r * seq, (r + 1) * seq)
            own_rows, own_cols = slice(i * head, (i + 1) * head), slice(i * seq, (i + 1) * seq)
            for j, grad in enumerate((grad_q, grad_k, grad_v)):
                first = j * width + (2 * p + i) * head
                mine = grad[own_rows, own_cols]
                proj_ref[first : first + head, place] = (mine * head ** (-0.5) if j == 0 else mine).astype(BF)
    gn_ref[...] = mm(w_ref[...], proj_ref[...])
    for r in range(rows):
        norm_cat[:, r * seq : (r + 1) * seq] = norm_ref[r]
    w_acc[...] += mm_nt(norm_cat[...], proj_ref[...])

    spots = tiles(seq, LANES)
    for r in range(rows):
        wide = [slice(r * seq + t.start, r * seq + t.stop) for t in spots]
        scales = []
        for t in spots:
            n, scale = norm_columns(mc_ref[r, :, t])
            n_ref[r, :, t] = n
            scales.append(scale)
        mean_e = [jnp.zeros((8, LANES), F32) for _ in spots]
        mean_en = [jnp.zeros((8, LANES), F32) for _ in spots]
        for d in tiles(width, 32):
            column = col_ref[3, d]
            gain_sum, shift_sum = acc_ref[3, d], acc_ref[4, d]
            for i, t in enumerate(spots):
                grad_n = gn_ref[d, wide[i]]
                product = grad_n * n_ref[r, d, t]
                gain_sum += product
                shift_sum += grad_n
                mean_e[i] += fold(grad_n * column)
                mean_en[i] += fold(product * column)
            acc_ref[3, d] = gain_sum
            acc_ref[4, d] = shift_sum
        for i, t in enumerate(spots):
            me = jnp.sum(mean_e[i], axis=0, keepdims=True) * (1.0 / width)
            men = jnp.sum(mean_en[i], axis=0, keepdims=True) * (1.0 / width)
            for d in tiles(width, 64):
                e = gn_ref[d, wide[i]] * col_ref[3, d]
                g_ref[r, d, t] = gm_ref[r, d, t] + scales[i] * (e - me - n_ref[r, d, t] * men)
        links, next_links = aux_ref[r, 0:1], aux_ref[r, 1:2]
        for d in tiles(width, 32):
            g = g_ref[r, d]
            base = x_ref[r, d].astype(F32)
            before = pltpu.roll(g, 1, 1) * links
            after = pltpu.roll(g, seq - 1, 1) * next_links
            acc_ref[0, d] += fold_lanes(base * after)
            acc_ref[1, d] += fold_lanes(base * g)
            acc_ref[2, d] += fold_lanes(base * before)
            conv0, conv1, conv2 = [twice(col_ref[i, d], seq) for i in range(3)]
            turn_ref[r, d] = (g + conv1 * g + conv0 * after + conv2 * before).astype(BF)
        ig_ref[r] = turn_ref[r].T

    @pl.when(step == pl.num_programs(0) - 1)
    def _():
        gs_ref[...] = other_ref[...]
        for i in range(5):
            gs_ref[i : i + 1] += jnp.sum(acc_ref[i].T, axis=0, keepdims=True)
        if start_ref is None:
            gw_refs[0][...] = w_acc[...]
        else:
            groups = len(gw_refs)
            for i in range(pieces):
                here = pl.ds(pl.multiple_of(index_ref[i] * own, 16), own)
                gw_refs[i % groups][i // groups] = w_acc[here, :].astype(BF)


def in_hbm(values):
    return pltpu.with_memory_space_constraint(values, pltpu.HBM)


def by_row(shape, rows, first=0):
    tail = tuple(shape[1:])
    return pl.BlockSpec((rows,) + tail, lambda i, *_: (i + first,) + (0,) * len(tail))


def whole(shape):
    place = (0,) * len(shape)
    return pl.BlockSpec(tuple(shape), lambda i, *_: place, pipeline_mode=pl.Buffered(1))


def step_rows(count, most):
    return max(r for r in range(1, most + 1) if count % r == 0)


def call(body, name, scalars, rows, row_args, args, row_outs, outs, scratch, span=None, into=None, near=()):
    first, count = span or (0, row_args[0].shape[0])
    skip = first // rows
    in_specs = [by_row(a.shape, rows, skip if a.shape[0] > count else 0) for a in row_args]
    in_specs += [whole(a.shape) for a in args]
    aliases = {}
    if into is not None:
        in_specs.append(pl.BlockSpec(memory_space=pl.ANY))
        aliases = {len(scalars) + len(in_specs) - 1: 0}
    spec = pltpu.PrefetchScalarGridSpec(
        num_scalar_prefetch=len(scalars),
        grid=(count // rows,),
        in_specs=in_specs,
        out_specs=[by_row(s, rows, skip if s[0] > count else 0) for s, _ in row_outs] + [whole(s) for s, _ in outs],
        scratch_shapes=[pltpu.VMEM(s, t) for s, t in scratch],
    )
    return pl.pallas_call(
        body,
        grid_spec=spec,
        out_shape=[(jax.ShapeDtypeStruct if "out" + str(i) in near else pltpu.HBM)(s, t) for i, (s, t) in enumerate(row_outs)]
        + [jax.ShapeDtypeStruct(s, t) for s, t in outs],
        input_output_aliases=aliases,
        compiler_params=pltpu.CompilerParams(dimension_semantics=("arbitrary",), vmem_limit_bytes=VMEM_LIMITS[name] * MIB),
        name=name,
    )(*scalars, *[a if i in near else in_hbm(a) for i, a in enumerate(row_args)], *args, *(() if into is None else (into,)))


def small_call(body, name, args, outs, scratch=()):
    return pl.pallas_call(
        body,
        out_shape=[jax.ShapeDtypeStruct(s, t) for s, t in outs],
        scratch_shapes=[pltpu.VMEM(s, t) for s, t in scratch],
        compiler_params=pltpu.CompilerParams(vmem_limit_bytes=16 * MIB),
        name=name,
    )(*args)


def run_forward(index, tokens, segment_ids, valid_len, pieces):
    count, seq, width = tokens.shape
    flipped = (count, width, seq)
    rows = step_rows(count, 2)
    row_outs = [
        (flipped, BF), (flipped, F32), (flipped, BF), (flipped, BF), (flipped, BF), ((count, seq, width), BF),
        ((count, HEADS, seq, seq), BF), (flipped, BF), ((count, 8, seq), F32), ((count, 8, seq), F32),
    ]
    return call(
        functools.partial(forward_attention, pieces=len(pieces)), "forward_attention", (index, valid_len),
        rows, (tokens,), (in_hbm(segment_ids), *pieces),
        row_outs, [((width, VECTORS), BF), ((width, 3 * width), BF)],
        [
            ((3 * width, width), BF), ((width, 3 * width + VECTORS), BF), ((5, width, LANES), F32),
            ((rows, seq, seq), F32), ((rows, seq, width), BF), ((rows, width, seq), BF),
        ],
    )


def run_feed_forward(index, att, mixed, cotangent, packed, pieces, shards):
    count, seq, width = cotangent.shape
    own = width // len(pieces)
    ff = shards * width
    groups = 2 if len(pieces) > 1 else 1
    rows = step_rows(count, 2)
    wide = rows * seq
    row_outs = [((count, seq, width), BF), ((count, width, seq), F32), ((count, width, seq), BF)]
    grads = ((len(pieces) // groups, own, 2 * ff + width), BF)
    return call(
        functools.partial(feed_forward, pieces=len(pieces), shards=shards), "feed_forward", (index,),
        rows, (att, mixed, cotangent), (packed, *pieces),
        row_outs, [((8, width), F32)] + [grads] * groups,
        [((width, ff), BF)] * 2 + [((ff, width), BF)] * 2 + [((width, width), BF)] * 2
        + [((width, ff), F32)] * 2 + [((width, width), F32), ((2, width, LANES), F32), ((2, width, LANES), F32)]
        + [((width, wide), BF), ((width, wide), F32), ((width, wide), F32), ((width, wide), BF), ((width, wide), BF)]
        + [((ff, wide), BF)] * 2
        + [((width, wide), F32), ((8, wide), F32), ((width, wide), BF), ((width, wide), BF)],
        near=("out2",),
    )


def run_backward(index, weight, kept, grads, packed, other, pieces, span, start, into):
    count, seq, width = kept[2].shape
    own = width // pieces
    groups = 2 if pieces > 1 else 1
    rows = step_rows(math.gcd(*span) or span[1], 2)
    row_args = (*kept[:7], grads[0], *kept[7:], grads[1])
    many = len(row_args)

    def body(index_ref, *refs):
        rest = list(refs[many:])
        w_ref, packed_ref, other_ref = rest[:3]
        start_ref = None if start is None else rest[3]
        rest = rest[3 if start is None else 5 :]
        backward(*refs[:many], index_ref, w_ref, packed_ref, other_ref, start_ref, *rest, pieces=pieces)

    outs = [((width, 3 * width), F32)] if start is None else [((pieces // groups, own, 3 * width), BF)] * groups
    return call(
        body, "backward", (index,), rows, row_args, (weight, packed, other) + (() if start is None else (start,)),
        [((count, seq, width), BF)], [((8, width), F32)] + outs,
        [
            ((3 * width, rows * seq), BF), ((width, 3 * width), F32), ((width, rows * seq), BF),
            ((rows, HEADS, seq, seq), F32), ((rows, HEADS, seq, seq), BF), ((width, rows * seq), F32),
            ((5, width, LANES), F32), ((4, width, LANES), F32), ((rows, width, seq), F32), ((rows, width, seq), F32),
            ((rows, width, seq), BF),
        ],
        span=span, into=into, near=(7,),
    )


def halves(count):
    early = 2 if count % 2 == 0 and count > 2 else count // 2
    return (0, early), (early, count - early)


def exchange(values, axis, offset):
    size = lax.axis_size(axis)
    return lax.ppermute(values, axis, [(i, i ^ offset) for i in range(size)])


def add_halves(mine, received):
    count, own, cols = mine.shape

    def body(mine_ref, received_ref, *out_refs):
        for i, ref in enumerate(out_refs):
            ref[...] = (mine_ref[i].astype(F32) + received_ref[i].astype(F32)).astype(BF)

    return small_call(body, "add_halves", (mine, received), [((own, cols), BF)] * count)


def add_wide(*items):
    return tree_sum(item.astype(F32) for item in items)


def split_high_low(values):
    high = values.astype(BF)
    return high, (values - high.astype(F32)).astype(BF)


def add_halves_and_sums(index, mine, received, sums, received_sums):
    count, own, cols = mine.shape
    width = sums.shape[1]

    def body(index_ref, mine_ref, received_ref, sums_ref, received_sums_ref, *out_refs):
        total = sums_ref[...] + received_sums_ref[...]
        for i, ref in enumerate(out_refs):
            ref[:own] = (mine_ref[i].astype(F32) + received_ref[i].astype(F32)).astype(BF)
            turned = pltpu.roll(total, lax.rem(width - index_ref[2 * i] * own, width), 1)[:, :LANES]
            high, low = split_high_low(turned)
            ref[own:, :LANES] = jnp.concatenate([high, low], axis=0)
            ref[own:, LANES:] = jnp.zeros((16, cols - LANES), BF)

    spec = pltpu.PrefetchScalarGridSpec(
        num_scalar_prefetch=1, grid=(1,),
        in_specs=[whole(a.shape) for a in (mine, received, sums, received_sums)],
        out_specs=[whole((own + 16, cols))] * count,
    )
    return pl.pallas_call(
        body, grid_spec=spec, out_shape=[jax.ShapeDtypeStruct((own + 16, cols), BF)] * count,
        compiler_params=pltpu.CompilerParams(vmem_limit_bytes=16 * MIB), name="add_halves_and_sums",
    )(index, mine, received, sums, received_sums)


def add_packed(name, items):
    own, cols = items[0].shape[0] - 16, items[0].shape[1]

    def body(*refs):
        out_ref = refs[-1]
        out_ref[:own] = tree_sum(ref[:own].astype(F32) for ref in refs[:-1]).astype(BF)
        sums = [ref[own:, :LANES].astype(F32) for ref in refs[:-1]]
        high, low = split_high_low(tree_sum(s[:8] + s[8:] for s in sums))
        out_ref[own:, :LANES] = jnp.concatenate([high, low], axis=0)
        out_ref[own:, LANES:] = jnp.zeros((16, cols - LANES), BF)

    return small_call(body, name, items, [(items[0].shape, BF)])[0]


def add_last(items):
    own, cols = items[0].shape[0] - 16, items[0].shape[1]

    def body(*refs):
        ins, outs = refs[: len(items)], refs[len(items) :]
        outs[0][...] = tree_sum(ref[:own].astype(F32) for ref in ins)
        sums = [ref[own:, :LANES].astype(F32) for ref in ins]
        vectors = tree_sum(s[:8] + s[8:] for s in sums)
        outs[1][...] = vectors[0:3, :own]
        for i in range(4):
            outs[2 + i][...] = vectors[3 + i : 4 + i, :own]

    return small_call(body, "add_last", items, [((own, cols), F32), ((3, own), F32)] + [((1, own), F32)] * 4)


def direct_plan(tokens, segment_ids, valid_len, qkv_weight, out_weight, up_weight, down_weight, conv_weight, vectors, cotangent):
    count, seq, width = tokens.shape
    own, ffs = up_weight.shape
    dp, mp = lax.axis_size("dp"), lax.axis_size("mp")
    me = lax.axis_index("dp")
    offsets = [2 * p for p in range(dp // 2)]
    index = jnp.stack([me ^ (p ^ c) for p in offsets for c in range(2)]).astype(jnp.int32)
    narrow, ff_own = small_call(
        pack_weights, "pack_weights",
        [in_hbm(a) for a in (qkv_weight, up_weight, down_weight, conv_weight, *[v.reshape(1, own) for v in vectors])],
        [((own, 3 * width + VECTORS), BF), ((2 * own, ffs), BF)], [((VECTORS, VECTORS), F32)],
    )
    plane = [narrow] + [exchange(narrow, "dp", p) for p in offsets[1:]]
    shards = [ff_own] + [exchange(ff_own, "mp", j) for j in range(1, mp)]
    pieces = [piece for a in plane for piece in (a, exchange(a, "dp", 1))]
    column = jnp.concatenate(shards + [out_weight], axis=0)
    columns = [column] + [exchange(column, "dp", p) for p in offsets[1:]]
    x, mixed, normed, q, k, v, raised, att, inverse, aux, packed, weight = run_forward(
        index, tokens, segment_ids, valid_len, pieces
    )
    columns, att = lax.optimization_barrier((columns, att))
    pieces = [piece for a in columns for piece in (a, exchange(a, "dp", 1))]
    layer_out, grad_mixed, grad_att, sums2, mine, theirs = run_feed_forward(
        index, att, mixed, cotangent, packed, pieces, mp
    )
    received = exchange(theirs, "dp", 1)
    early, late = halves(count)
    kept = (q, k, v, raised, att, inverse, normed, x, aux, mixed)
    grads = (grad_att, grad_mixed)
    some_grad, sums, start = run_backward(index, weight, kept, grads, packed, sums2, dp, early, None, None)
    received, start = lax.optimization_barrier((received, start))
    parts = list(add_halves(mine, received))
    parts[0], start = lax.optimization_barrier((parts[0], start))
    plane = [parts[0]] + [exchange(parts[i], "dp", p) for i, p in enumerate(offsets) if i]
    input_grad, sums, mine_a, theirs_a = run_backward(
        index, weight, kept, grads, packed, sums, dp, late, start, some_grad
    )
    plane, theirs_a, sums = lax.optimization_barrier((plane, theirs_a, sums))
    received_a = exchange(theirs_a, "dp", 1)
    received_s = exchange(sums, "dp", 1)
    total = add_wide(*plane).astype(BF)
    half = 2 * ffs * (mp // 2)
    near, far, out_part = total[:, :half], total[:, half:], total[:, 2 * half :]
    received_f = exchange(far, "mp", 2)
    parts = add_halves_and_sums(index, mine_a, received_a, sums, received_s)
    plane_a = [parts[0]] + [exchange(parts[i], "dp", p) for i, p in enumerate(offsets) if i]
    total = add_packed("add_plane", plane_a)
    received_1 = exchange(total, "mp", 2)
    near_sum = add_wide(near, received_f[:, :half])
    out_sum = lax.optimization_barrier(add_wide(out_part, received_f[:, half:]).astype(BF))
    keep = near_sum[:, : 2 * ffs]
    send = jnp.concatenate([near_sum[:, 2 * ffs :].astype(BF), out_sum], axis=1)
    received_n = exchange(send, "mp", 1)
    total = add_packed("add_far", (total, received_1))
    received_2 = exchange(total, "mp", 1)
    grad_up = keep[:, :ffs] + received_n[:, :ffs].astype(F32)
    grad_down = keep[:, ffs:] + received_n[:, ffs : 2 * ffs].astype(F32)
    grad_out = add_wide(out_sum, received_n[:, 2 * ffs :])
    grad_qkv, grad_conv, *grads = add_last((total, received_2))
    return (layer_out, input_grad, grad_qkv, grad_out, grad_up, grad_down, grad_conv, *[g.reshape(own) for g in grads])


def gathered_plan(tokens, segment_ids, valid_len, qkv_weight, out_weight, up_weight, down_weight, conv_weight, vectors, cotangent):
    count, seq, width = tokens.shape
    own = qkv_weight.shape[0]
    dp = width // own
    columns = jnp.stack([conv_weight[0], conv_weight[1], conv_weight[2], *vectors], axis=1)
    narrow = jnp.concatenate([qkv_weight, jnp.pad(columns, ((0, 0), (0, VECTORS - 7))), out_weight], axis=1)
    wide = lax.all_gather(narrow, "dp", axis=0, tiled=True)
    both = lax.all_gather(jnp.concatenate([up_weight, down_weight], axis=0), "mp", axis=1, tiled=True)
    ff = both.shape[1]
    shards = ff // width
    both = lax.all_gather(both, "dp", axis=0).reshape(dp, 2, own, shards, width)
    both = both.transpose(3, 1, 0, 2, 4).reshape(2 * ff, width)
    column = jnp.concatenate([both, wide[:, 3 * width + VECTORS :]], axis=0)
    index = jnp.zeros((1,), jnp.int32)
    x, mixed, normed, q, k, v, raised, att, inverse, aux, packed, weight = run_forward(
        index, tokens, segment_ids, valid_len, [wide[:, : 3 * width + VECTORS]]
    )
    layer_out, grad_mixed, grad_att, sums2, grads = run_feed_forward(
        index, att, mixed, cotangent, packed, [column], shards
    )
    early, late = halves(count)
    kept = (q, k, v, raised, att, inverse, normed, x, aux, mixed)
    grad_rows = (grad_att, grad_mixed)
    some_grad, sums, start = run_backward(index, weight, kept, grad_rows, packed, sums2, 1, early, None, None)
    input_grad, sums, grad_qkv = run_backward(index, weight, kept, grad_rows, packed, sums, 1, late, start, some_grad)
    grad_ff = grads[0, :, : 2 * ff].reshape(width, shards, 2, width).transpose(0, 2, 1, 3).reshape(width, 2 * ff)
    grad_ff = lax.psum_scatter(grad_ff, "dp", scatter_dimension=0, tiled=True).reshape(own, 2, ff)
    grad_ff = lax.psum_scatter(grad_ff, "mp", scatter_dimension=2, tiled=True).astype(F32)
    grad_attn = jnp.concatenate([grad_qkv[0], grads[0, :, 2 * ff :]], axis=1)
    grad_attn = lax.psum_scatter(grad_attn, "dp", scatter_dimension=0, tiled=True)
    grad_attn = lax.psum(grad_attn, "mp").astype(F32)
    sums = lax.psum(sums, ("dp", "mp"))
    sums = lax.dynamic_slice_in_dim(sums, lax.axis_index("dp") * own, own, axis=1)
    return (
        layer_out, input_grad, grad_attn[:, : 3 * width], grad_attn[:, 3 * width :],
        grad_ff[:, 0], grad_ff[:, 1], sums[0:3], sums[3], sums[4], sums[5], sums[6],
    )


def on_device(
    tokens, segment_ids, valid_len, qkv_weight, out_weight, up_weight, down_weight, conv_weight,
    ln1_gain, ln1_shift, ln2_gain, ln2_shift, cotangent,
):
    own, ffs = up_weight.shape
    direct = own % 16 == 0 and ffs == tokens.shape[2] and own <= VECTORS and lax.axis_size("mp") == 4
    plan = direct_plan if direct else gathered_plan
    return plan(
        tokens, segment_ids, valid_len, qkv_weight, out_weight, up_weight, down_weight, conv_weight,
        (ln1_gain, ln1_shift, ln2_gain, ln2_shift), cotangent,
    )


def solution(mesh):
    rows = P(("dp", "mp"), None, None)
    weights = (P("dp", None), P("dp", None), P("dp", "mp"), P("dp", "mp"), P(None, "dp"))
    vectors = (P("dp"),) * 4
    return jax.shard_map(
        on_device,
        mesh=mesh,
        in_specs=(rows, P(("dp", "mp"), None), P(("dp", "mp"))) + weights + vectors + (rows,),
        out_specs=(rows, rows) + weights + vectors,
        check_vma=False,
    )
```

```python
import functools
import math

import jax
import jax.numpy as jnp
from jax import lax
from jax.experimental import pallas as pl
from jax.experimental.pallas import tpu as pltpu
from jax.sharding import PartitionSpec as P

HEADS = 6
VECTORS = 128
LANES = 128
BF = jnp.bfloat16
F32 = jnp.float32
MIB = 1024 * 1024
VMEM_LIMITS = dict(forward_attention=26, feed_forward=40, backward=36, layer_output=16)


def mm(lhs, rhs):
    return lax.dot_general(lhs, rhs, (((1,), (0,)), ((), ())), preferred_element_type=F32)


def mm_nt(lhs, rhs):
    return lax.dot_general(lhs, rhs, (((1,), (1,)), ((), ())), preferred_element_type=F32)


def tree_sum(items):
    items = list(items)
    while len(items) > 1:
        items = [a + b for a, b in zip(items[::2], items[1::2])]
    return items[0]


def pack_weights(qkv_ref, up_ref, down_ref, conv_ref, g1_ref, s1_ref, g2_ref, s2_ref, narrow_ref, ff_ref, rows_ref):
    own, ffs = up_ref.shape
    rows_ref[...] = jnp.zeros_like(rows_ref)
    rows_ref[0:3, :own] = conv_ref[...].astype(F32)
    for i, ref in enumerate((g1_ref, s1_ref, g2_ref, s2_ref)):
        rows_ref[3 + i : 4 + i, :own] = ref[...].astype(F32)
    wide = qkv_ref.shape[1]
    narrow_ref[:, :wide] = qkv_ref[...]
    narrow_ref[:, wide:] = rows_ref[...].T[:own].astype(BF)
    ff_ref[:own] = up_ref[...]
    ff_ref[own:] = down_ref[...]


def tiles(total, size):
    return [slice(at, at + size) for at in range(0, total, size)]


def weave(*strands):
    strands = [strand for strand in strands if strand]
    total = sum(len(strand) for strand in strands)
    pieces = [((i + 0.5) / len(strand), j, piece) for j, strand in enumerate(strands) for i, piece in enumerate(strand)]
    assert len(pieces) == total
    for _, _, piece in sorted(pieces, key=lambda item: item[:2]):
        piece()


def twice(tile, lanes):
    return jnp.concatenate([tile] * (lanes // LANES), axis=1)


def load_columns(packed_ref, col_ref, places):
    for i, place in enumerate(places):
        column = packed_ref[:, place : place + 1].astype(F32)
        col_ref[i] = jnp.broadcast_to(column, (column.shape[0], LANES))


def column_mean(values):
    return jnp.sum(values, axis=0, keepdims=True) * (1.0 / values.shape[0])


def norm_columns(values):
    centred = values - column_mean(values)
    scale = lax.rsqrt(column_mean(centred * centred) + 1e-06)
    return centred * scale, scale


def fold(values):
    rows, lanes = values.shape
    return jnp.sum(values.reshape(rows // 8, 8, lanes), axis=0)


def fold_lanes(values):
    return sum(values[:, t] for t in tiles(values.shape[1], LANES))


def forward_attention(index_ref, len_ref, tok_ref, seg_ref, *refs, pieces):
    piece_refs = refs[:pieces]
    (
        x_ref, mc_ref, norm_ref, q_ref, k_ref, v_ref, e_ref, att_ref, inv_ref, aux_ref, packed_ref, w_ref,
        wt_ref, wide_ref, col_ref, bias_ref, key_ref, value_ref,
    ) = refs[pieces:]
    rows, seq, width = tok_ref.shape
    head = width // HEADS
    step = pl.program_id(0)

    @pl.when(step == 0)
    def _():
        own = width // pieces
        for i, ref in enumerate(piece_refs):
            wide_ref[pl.ds(pl.multiple_of(index_ref[i] * own, 16), own), :] = ref[...]
        w_ref[...] = wide_ref[:, : 3 * width]
        wt_ref[:width] = (wide_ref[:, :width].astype(F32) * head ** (-0.5)).astype(BF).T
        wt_ref[width:] = wide_ref[:, width : 3 * width].T
        packed_ref[...] = wide_ref[:, 3 * width :]
        load_columns(packed_ref, col_ref, range(5))

    place = lax.broadcasted_iota(jnp.int32, (1, seq), 1)
    zero = jnp.zeros((head, seq), BF)

    def preparation(r):
        known = {}

        def start():
            segs = seg_ref[pl.ds(step * rows + r, 1), :].astype(F32)
            valid = place < len_ref[step * rows + r]
            number = jnp.where(valid, segs, -1.0)
            links = jnp.where(valid & (place > 0) & (number == pltpu.roll(number, 1, 1)), 1.0, 0.0)
            next_links = jnp.where(place < seq - 1, pltpu.roll(links, seq - 1, 1), 0.0)
            none = jnp.zeros_like(links)
            aux = jnp.concatenate([links, next_links, number, none, none, none, none, none], axis=0)
            aux_ref[r] = aux
            x_ref[r] = tok_ref[r].T
            known.update(segs=segs, links=links, next_links=next_links, key_number=aux.T[:, 2:3])

        def mask(t):
            row_id = lax.broadcasted_iota(jnp.int32, (64, seq), 0) + t.start
            col_id = lax.broadcasted_iota(jnp.int32, (64, seq), 1)
            allowed = (known["key_number"][t] == known["segs"]) | (row_id == col_id)
            bias_ref[r, t] = jnp.where(allowed, 0.0, -1e30)

        def conv(t):
            base = x_ref[r, t].astype(F32)
            before = pltpu.roll(base, 1, 1) * known["links"]
            after = pltpu.roll(base, seq - 1, 1) * known["next_links"]
            conv0, conv1, conv2 = [twice(col_ref[i, t], seq) for i in range(3)]
            mc_ref[r, t] = base + before * conv0 + base * conv1 + after * conv2

        def norm(t):
            n, _ = norm_columns(mc_ref[r, :, t])
            norm_ref[r, :, t] = (n * col_ref[3] + col_ref[4]).astype(BF)

        pieces = [start] + [functools.partial(conv, t) for t in tiles(width, 32)]
        pieces += [functools.partial(norm, t) for t in tiles(seq, LANES)]
        return pieces + [functools.partial(mask, t) for t in tiles(seq, 64)]

    def project():
        normed = jnp.concatenate([norm_ref[r] for r in range(rows)], axis=1)
        for i, ref in enumerate((q_ref, k_ref, value_ref)):
            part = mm(wt_ref[i * width : (i + 1) * width], normed).astype(BF)
            for r in range(rows):
                ref[r] = part[:, r * seq : (r + 1) * seq]
        for r in range(rows):
            key_ref[r] = k_ref[r].T
            v_ref[r] = value_ref[r].T

    def scores(r, p):
        low, high = [q_ref[r, h * head : (h + 1) * head] for h in (2 * p, 2 * p + 1)]
        both = jnp.concatenate([jnp.concatenate([low, zero], axis=1), jnp.concatenate([zero, high], axis=1)], axis=0)
        return mm(key_ref[r, :, 2 * p * head : 2 * (p + 1) * head], both)

    def attended(r, p):
        both = jnp.concatenate([e_ref[r, 2 * p], e_ref[r, 2 * p + 1]], axis=1)
        product = mm(value_ref[r, 2 * p * head : 2 * (p + 1) * head], both)
        parts = []
        for i in range(2):
            att = product[i * head : (i + 1) * head, i * seq : (i + 1) * seq] * inv_ref[r, 2 * p + i : 2 * p + i + 1]
            parts.append(att.astype(BF))
        return jnp.concatenate(parts, axis=0)

    def soften(r, p, product):
        for i in range(2):
            for t in tiles(seq, LANES):
                masked = product[:, i * seq + t.start : i * seq + t.stop] + bias_ref[r, :, t]
                raised = jnp.exp(masked - jnp.max(masked, axis=0, keepdims=True))
                inv_ref[r, 2 * p + i : 2 * p + i + 1, t] = 1.0 / jnp.sum(raised, axis=0, keepdims=True)
                e_ref[r, 2 * p + i, :, t] = raised.astype(BF)

    weave(*[preparation(r) for r in range(rows)])
    project()
    work = [(r, p) for r in range(rows) for p in range(HEADS // 2)]
    current, last = scores(*work[0]), None
    for at, (r, p) in enumerate(work):
        following = scores(*work[at + 1]) if at + 1 < len(work) else None
        finished = attended(*last) if last else None
        soften(r, p, current)
        if last:
            att_ref[last[0], 2 * last[1] * head : 2 * (last[1] + 1) * head] = finished
        current, last = following, (r, p)
    att_ref[last[0], 2 * last[1] * head : 2 * (last[1] + 1) * head] = attended(*last)


def gelu_parts(x):
    cdf = 0.5 * lax.erf(x * math.sqrt(0.5)) + 0.5
    bell = jnp.exp2(x * x * (-0.5 / math.log(2.0)) - 0.5 * math.log2(2.0 * math.pi))
    return x * cdf, cdf + x * bell


def feed_forward(index_ref, att_ref, mc_ref, ct_ref, packed_ref, *refs, pieces, shards):
    piece_refs = refs[:pieces]
    groups = 2 if pieces > 1 else 1
    hidden_out, mixed_out, gm_ref, ga_ref, gs_ref, down_ref = refs[pieces : pieces + 6]
    hidden_ref, mixed_ref = hidden_out.at[0], mixed_out.at[0]
    gw_refs = refs[pieces + 6 : pieces + 6 + groups]
    (
        up_ref, upt_ref, downt_ref, out_ref, outt_ref, up_acc, down_acc, out_acc, col_acc, col_ref,
        att_cat, n_ref, norm_ref, ctt_ref, gp_ref, gn_ref, scale_ref, branch_ref,
    ) = refs[pieces + 6 + groups :]
    rows, seq, width = ct_ref.shape
    ff = up_ref.shape[1]
    ffs = ff // shards
    own = width // pieces
    step = pl.program_id(0)

    @pl.when(step == 0)
    def _():
        for acc in (up_acc, down_acc, out_acc, col_acc):
            acc[...] = jnp.zeros_like(acc)
        for i, ref in enumerate(piece_refs):
            here = pl.ds(pl.multiple_of(index_ref[i] * own, 16), own)
            for j in range(shards):
                up_ref[here, j * ffs : (j + 1) * ffs] = ref[2 * j * own : (2 * j + 1) * own]
                down_ref[here, j * ffs : (j + 1) * ffs] = ref[(2 * j + 1) * own : (2 * j + 2) * own]
            out_ref[here, :] = ref[2 * shards * own :]
        upt_ref[...] = up_ref[...].T
        downt_ref[...] = down_ref[...].T
        outt_ref[...] = out_ref[...].T
        load_columns(packed_ref, col_ref, (5, 6))

    def lanes_of(r):
        return slice(r * seq, (r + 1) * seq)

    def spots_of(r):
        return [slice(at, at + LANES) for at in range(r * seq, (r + 1) * seq, LANES)]

    def preparation(r):
        lanes = lanes_of(r)

        def turn():
            ctt_ref[:, lanes] = ct_ref[r].T
            att_cat[:, lanes] = att_ref[r]

        def branch():
            mixed_ref[:, lanes] = mc_ref[r] + mm(outt_ref[...], att_ref[r])

        def norm(t):
            n, scale = norm_columns(mixed_ref[:, t])
            n_ref[:, t] = n
            scale_ref[0:1, t] = scale
            norm_ref[:, t] = (n * col_ref[0] + col_ref[1]).astype(BF)

        return [turn, branch] + [functools.partial(norm, t) for t in spots_of(r)]

    def activation(block):
        pre = mm(upt_ref[block], norm_ref[...])
        grad_hidden = mm(downt_ref[block], ctt_ref[...])
        for low in range(0, block.stop - block.start, 16):
            part = slice(low, low + 16)
            here = slice(block.start + low, block.start + low + 16)
            hidden, slope = gelu_parts(pre[part])
            hidden_ref[here] = hidden.astype(BF)
            gp_ref[here] = (grad_hidden[part] * slope).astype(BF)

    def norm_back(r):
        spots = spots_of(r)
        mean_e = [jnp.zeros((8, LANES), F32) for _ in spots]
        mean_en = [jnp.zeros((8, LANES), F32) for _ in spots]
        means = []

        def sums(d):
            column = col_ref[0, d]
            gain_sum, shift_sum = col_acc[0, d], col_acc[1, d]
            for i, t in enumerate(spots):
                grad_n = gn_ref[d, t]
                product = grad_n * n_ref[d, t]
                gain_sum += product
                shift_sum += grad_n
                mean_e[i] += fold(grad_n * column)
                mean_en[i] += fold(product * column)
            col_acc[0, d] = gain_sum
            col_acc[1, d] = shift_sum

        def finish():
            for i in range(len(spots)):
                me = jnp.sum(mean_e[i], axis=0, keepdims=True) * (1.0 / width)
                men = jnp.sum(mean_en[i], axis=0, keepdims=True) * (1.0 / width)
                means.append((me, men))

        def apply(d):
            for i, t in enumerate(spots):
                me, men = means[i]
                change = scale_ref[0:1, t] * (gn_ref[d, t] * col_ref[0, d] - me - n_ref[d, t] * men)
                grad_mixed = ctt_ref[d, t].astype(F32) + change
                gm_ref[r, d, i * LANES : (i + 1) * LANES] = grad_mixed
                branch_ref[d, t] = grad_mixed.astype(BF)

        def attended():
            ga_ref[r] = mm(out_ref[...], branch_ref[:, lanes_of(r)]).astype(BF)

        pieces = [functools.partial(sums, d) for d in tiles(width, 32)] + [finish]
        return pieces + [functools.partial(apply, d) for d in tiles(width, 32)] + [attended]

    weave(*[preparation(r) for r in range(rows)])
    for block in tiles(ff, 128):
        activation(block)
    gn_ref[...] = mm(up_ref[...], gp_ref[...])
    down_acc[...] += mm_nt(ctt_ref[...], hidden_ref[...])
    up_acc[...] += mm_nt(norm_ref[...], gp_ref[...])
    weave(*[norm_back(r) for r in range(rows)])
    out_acc[...] += mm_nt(att_cat[...], branch_ref[...])

    @pl.when(step == pl.num_programs(0) - 1)
    def _():
        for i in range(pieces):
            here = pl.ds(pl.multiple_of(index_ref[i] * own, 16), own)
            place = gw_refs[i % groups]
            for j in range(shards):
                cols = slice(j * ffs, (j + 1) * ffs)
                place[i // groups, :, 2 * j * ffs : (2 * j + 1) * ffs] = up_acc[here, cols].astype(BF)
                place[i // groups, :, (2 * j + 1) * ffs : (2 * j + 2) * ffs] = down_acc[here, cols].astype(BF)
            place[i // groups, :, 2 * ff :] = out_acc[here, :].astype(BF)
        gs_ref[...] = jnp.zeros_like(gs_ref)
        for i in range(2):
            gs_ref[5 + i : 6 + i] = jnp.sum(col_acc[i].T, axis=0, keepdims=True)


def layer_output(hidden_ref, mixed_ref, down_ref, lo_ref):
    rows, seq, _ = lo_ref.shape
    total = (mixed_ref[0] + mm(down_ref[...], hidden_ref[0])).astype(BF)
    for r in range(rows):
        lo_ref[r] = total[:, r * seq : (r + 1) * seq].T


def backward(
    q_ref, k_ref, v_ref, e_ref, att_ref, inv_ref, norm_ref, ga_ref, x_ref, aux_ref, mc_ref, gm_ref,
    index_ref, w_ref, packed_ref, other_ref, start_ref, ig_ref, gs_ref, *refs, pieces,
):
    gw_refs = refs[:-11]
    (
        proj_ref, w_acc, norm_cat, soft_ref, logit_ref, gn_ref, acc_ref, col_ref, n_ref, g_ref, turn_ref
    ) = refs[-11:]
    rows, seq, width = v_ref.shape
    own = width // pieces
    head = width // HEADS
    step = pl.program_id(0)

    @pl.when(step == 0)
    def _():
        w_acc[...] = jnp.zeros_like(w_acc) if start_ref is None else start_ref[...]
        acc_ref[...] = jnp.zeros_like(acc_ref)
        load_columns(packed_ref, col_ref, range(4))

    zero = jnp.zeros((head, seq), BF)
    work = [(r, p) for r in range(rows) for p in range(HEADS // 2)]

    def opening(r, p):
        grads, inners = [], []
        for h in (2 * p, 2 * p + 1):
            part = slice(h * head, (h + 1) * head)
            grad_att = ga_ref[r, part].astype(F32) * inv_ref[r, h : h + 1]
            inners.append(jnp.sum(grad_att * att_ref[r, part].astype(F32), axis=0, keepdims=True))
            grads.append(grad_att.astype(BF))
        low, high = grads
        both = jnp.concatenate([jnp.concatenate([low, zero], axis=1), jnp.concatenate([zero, high], axis=1)], axis=0)
        product = mm(v_ref[r, :, 2 * p * head : 2 * (p + 1) * head], both)
        soft_ref[r, 2 * p] = product[:, :seq]
        soft_ref[r, 2 * p + 1] = product[:, seq:]
        return jnp.concatenate(grads, axis=0), inners

    ready = opening(*work[0])
    for at, (r, p) in enumerate(work):
        grad_att, inners = ready
        if at + 1 < len(work):
            ready = opening(*work[at + 1])
        for i, h in enumerate((2 * p, 2 * p + 1)):
            for t in tiles(seq, 32):
                raised = e_ref[r, h, t].astype(F32)
                logit_ref[r, h, t] = (raised * (soft_ref[r, h, t] - inners[i])).astype(BF)
        part = slice(2 * p * head, 2 * (p + 1) * head)
        pair = slice(2 * p, 2 * p + 2)
        beside = jnp.concatenate([logit_ref[r, 2 * p], logit_ref[r, 2 * p + 1]], axis=1)
        grad_q = mm(k_ref[r, part], beside)
        grad_k = mm_nt(q_ref[r, part], logit_ref[r, pair].reshape(2 * seq, seq))
        grad_v = mm_nt(grad_att, e_ref[r, pair].reshape(2 * seq, seq))
        for i in range(2):
            place = slice(r * seq, (r + 1) * seq)
            own_rows, own_cols = slice(i * head, (i + 1) * head), slice(i * seq, (i + 1) * seq)
            for j, grad in enumerate((grad_q, grad_k, grad_v)):
                first = j * width + (2 * p + i) * head
                mine = grad[own_rows, own_cols]
                proj_ref[first : first + head, place] = (mine * head ** (-0.5) if j == 0 else mine).astype(BF)
    gn_ref[...] = mm(w_ref[...], proj_ref[...])
    for r in range(rows):
        norm_cat[:, r * seq : (r + 1) * seq] = norm_ref[r]
    w_acc[...] += mm_nt(norm_cat[...], proj_ref[...])

    spots = tiles(seq, LANES)
    for r in range(rows):
        wide = [slice(r * seq + t.start, r * seq + t.stop) for t in spots]
        scales = []
        for t in spots:
            n, scale = norm_columns(mc_ref[r, :, t])
            n_ref[r, :, t] = n
            scales.append(scale)
        mean_e = [jnp.zeros((8, LANES), F32) for _ in spots]
        mean_en = [jnp.zeros((8, LANES), F32) for _ in spots]
        for d in tiles(width, 32):
            column = col_ref[3, d]
            gain_sum, shift_sum = acc_ref[3, d], acc_ref[4, d]
            for i, t in enumerate(spots):
                grad_n = gn_ref[d, wide[i]]
                product = grad_n * n_ref[r, d, t]
                gain_sum += product
                shift_sum += grad_n
                mean_e[i] += fold(grad_n * column)
                mean_en[i] += fold(product * column)
            acc_ref[3, d] = gain_sum
            acc_ref[4, d] = shift_sum
        for i, t in enumerate(spots):
            me = jnp.sum(mean_e[i], axis=0, keepdims=True) * (1.0 / width)
            men = jnp.sum(mean_en[i], axis=0, keepdims=True) * (1.0 / width)
            for d in tiles(width, 64):
                e = gn_ref[d, wide[i]] * col_ref[3, d]
                g_ref[r, d, t] = gm_ref[r, d, t] + scales[i] * (e - me - n_ref[r, d, t] * men)
        links, next_links = aux_ref[r, 0:1], aux_ref[r, 1:2]
        for d in tiles(width, 32):
            g = g_ref[r, d]
            base = x_ref[r, d].astype(F32)
            before = pltpu.roll(g, 1, 1) * links
            after = pltpu.roll(g, seq - 1, 1) * next_links
            acc_ref[0, d] += fold_lanes(base * after)
            acc_ref[1, d] += fold_lanes(base * g)
            acc_ref[2, d] += fold_lanes(base * before)
            conv0, conv1, conv2 = [twice(col_ref[i, d], seq) for i in range(3)]
            turn_ref[r, d] = (g + conv1 * g + conv0 * after + conv2 * before).astype(BF)
        ig_ref[r] = turn_ref[r].T

    @pl.when(step == pl.num_programs(0) - 1)
    def _():
        gs_ref[...] = other_ref[...]
        for i in range(5):
            gs_ref[i : i + 1] += jnp.sum(acc_ref[i].T, axis=0, keepdims=True)
        if start_ref is None:
            gw_refs[0][...] = w_acc[...]
        else:
            groups = len(gw_refs)
            for i in range(pieces):
                here = pl.ds(pl.multiple_of(index_ref[i] * own, 16), own)
                gw_refs[i % groups][i // groups] = w_acc[here, :].astype(BF)


def in_hbm(values):
    return pltpu.with_memory_space_constraint(values, pltpu.HBM)


def by_row(shape, rows, first=0):
    tail = tuple(shape[1:])
    return pl.BlockSpec((rows,) + tail, lambda i, *_: (i + first,) + (0,) * len(tail))


def whole(shape):
    place = (0,) * len(shape)
    return pl.BlockSpec(tuple(shape), lambda i, *_: place, pipeline_mode=pl.Buffered(1))


def step_rows(count, most):
    return max(r for r in range(1, most + 1) if count % r == 0)


def call(body, name, scalars, rows, row_args, args, row_outs, outs, scratch, span=None, into=None, near=()):
    first, count = span or (0, row_args[0].shape[0])
    skip = first // rows
    steps = count // rows

    def rows_of(shape):
        return rows if shape[0] >= count and span else shape[0] // steps

    in_specs = [by_row(a.shape, rows_of(a.shape), skip if a.shape[0] > count else 0) for a in row_args]
    in_specs += [whole(a.shape) for a in args]
    aliases = {}
    if into is not None:
        in_specs.append(pl.BlockSpec(memory_space=pl.ANY))
        aliases = {len(scalars) + len(in_specs) - 1: 0}
    spec = pltpu.PrefetchScalarGridSpec(
        num_scalar_prefetch=len(scalars),
        grid=(steps,),
        in_specs=in_specs,
        out_specs=[by_row(s, rows_of(s), skip if s[0] > count else 0) for s, _ in row_outs] + [whole(s) for s, _ in outs],
        scratch_shapes=[pltpu.VMEM(s, t) for s, t in scratch],
    )
    return pl.pallas_call(
        body,
        grid_spec=spec,
        out_shape=[(jax.ShapeDtypeStruct if "out" + str(i) in near else pltpu.HBM)(s, t) for i, (s, t) in enumerate(row_outs)]
        + [jax.ShapeDtypeStruct(s, t) for s, t in outs],
        input_output_aliases=aliases,
        compiler_params=pltpu.CompilerParams(dimension_semantics=("arbitrary",), vmem_limit_bytes=VMEM_LIMITS[name] * MIB),
        name=name,
    )(*scalars, *[a if i in near else in_hbm(a) for i, a in enumerate(row_args)], *args, *(() if into is None else (into,)))


def small_call(body, name, args, outs, scratch=()):
    return pl.pallas_call(
        body,
        out_shape=[jax.ShapeDtypeStruct(s, t) for s, t in outs],
        scratch_shapes=[pltpu.VMEM(s, t) for s, t in scratch],
        compiler_params=pltpu.CompilerParams(vmem_limit_bytes=16 * MIB),
        name=name,
    )(*args)


def run_forward(index, tokens, segment_ids, valid_len, pieces):
    count, seq, width = tokens.shape
    flipped = (count, width, seq)
    rows = step_rows(count, 2)
    row_outs = [
        (flipped, BF), (flipped, F32), (flipped, BF), (flipped, BF), (flipped, BF), ((count, seq, width), BF),
        ((count, HEADS, seq, seq), BF), (flipped, BF), ((count, 8, seq), F32), ((count, 8, seq), F32),
    ]
    return call(
        functools.partial(forward_attention, pieces=len(pieces)), "forward_attention", (index, valid_len),
        rows, (tokens,), (in_hbm(segment_ids), *pieces),
        row_outs, [((width, VECTORS), BF), ((width, 3 * width), BF)],
        [
            ((3 * width, width), BF), ((width, 3 * width + VECTORS), BF), ((5, width, LANES), F32),
            ((rows, seq, seq), F32), ((rows, seq, width), BF), ((rows, width, seq), BF),
        ],
    )


def run_feed_forward(index, att, mixed, cotangent, packed, pieces, shards):
    count, seq, width = cotangent.shape
    own = width // len(pieces)
    ff = shards * width
    groups = 2 if len(pieces) > 1 else 1
    rows = step_rows(count, 2)
    wide = rows * seq
    row_outs = [
        ((count // rows, ff, wide), BF), ((count // rows, width, wide), F32),
        ((count, width, seq), F32), ((count, width, seq), BF),
    ]
    grads = ((len(pieces) // groups, own, 2 * ff + width), BF)
    return call(
        functools.partial(feed_forward, pieces=len(pieces), shards=shards), "feed_forward", (index,),
        rows, (att, mixed, cotangent), (packed, *pieces),
        row_outs, [((8, width), F32), ((width, ff), BF)] + [grads] * groups,
        [((width, ff), BF)] + [((ff, width), BF)] * 2 + [((width, width), BF)] * 2
        + [((width, ff), F32)] * 2 + [((width, width), F32), ((2, width, LANES), F32), ((2, width, LANES), F32)]
        + [((width, wide), BF), ((width, wide), F32), ((width, wide), BF), ((width, wide), BF)]
        + [((ff, wide), BF)]
        + [((width, wide), F32), ((8, wide), F32), ((width, wide), BF)],
        near=("out3",),
    )


def run_layer_output(hidden, mixed, down, shape):
    return call(layer_output, "layer_output", (), 1, (hidden, mixed), (down,), [(shape, BF)], [], [])[0]


def run_backward(index, weight, kept, grads, packed, other, pieces, span, start, into):
    count, seq, width = kept[2].shape
    own = width // pieces
    groups = 2 if pieces > 1 else 1
    rows = step_rows(math.gcd(*span) or span[1], 2)
    row_args = (*kept[:7], grads[0], *kept[7:], grads[1])
    many = len(row_args)

    def body(index_ref, *refs):
        rest = list(refs[many:])
        w_ref, packed_ref, other_ref = rest[:3]
        start_ref = None if start is None else rest[3]
        rest = rest[3 if start is None else 5 :]
        backward(*refs[:many], index_ref, w_ref, packed_ref, other_ref, start_ref, *rest, pieces=pieces)

    outs = [((width, 3 * width), F32)] if start is None else [((pieces // groups, own, 3 * width), BF)] * groups
    return call(
        body, "backward", (index,), rows, row_args, (weight, packed, other) + (() if start is None else (start,)),
        [((count, seq, width), BF)], [((8, width), F32)] + outs,
        [
            ((3 * width, rows * seq), BF), ((width, 3 * width), F32), ((width, rows * seq), BF),
            ((rows, HEADS, seq, seq), F32), ((rows, HEADS, seq, seq), BF), ((width, rows * seq), F32),
            ((5, width, LANES), F32), ((4, width, LANES), F32), ((rows, width, seq), F32), ((rows, width, seq), F32),
            ((rows, width, seq), BF),
        ],
        span=span, into=into, near=(7,),
    )


def halves(count):
    early = 2 if count % 2 == 0 and count > 2 else count // 2
    return (0, early), (early, count - early)


def exchange(values, axis, offset):
    size = lax.axis_size(axis)
    return lax.ppermute(values, axis, [(i, i ^ offset) for i in range(size)])


def add_halves(mine, received):
    count, own, cols = mine.shape

    def body(mine_ref, received_ref, *out_refs):
        for i, ref in enumerate(out_refs):
            ref[...] = (mine_ref[i].astype(F32) + received_ref[i].astype(F32)).astype(BF)

    return small_call(body, "add_halves", (mine, received), [((own, cols), BF)] * count)


def add_wide(*items):
    return tree_sum(item.astype(F32) for item in items)


def store_high_low(ref, cols, values):
    high = values.astype(BF)
    low = (values - high.astype(F32)).astype(BF)
    ref[:, cols:] = jnp.concatenate([high, low, jnp.zeros((ref.shape[0] - 16, LANES), BF)], axis=0)


def load_high_low(ref, cols):
    both = ref[:16, cols:].astype(F32)
    return both[:8] + both[8:]


def add_halves_and_sums(index, mine, received, sums, received_sums):
    count, own, cols = mine.shape
    width = sums.shape[1]

    def body(index_ref, mine_ref, received_ref, sums_ref, received_sums_ref, *out_refs):
        total = sums_ref[...] + received_sums_ref[...]
        for i, ref in enumerate(out_refs):
            ref[:, :cols] = (mine_ref[i].astype(F32) + received_ref[i].astype(F32)).astype(BF)
            turned = pltpu.roll(total, lax.rem(width - index_ref[2 * i] * own, width), 1)[:, :LANES]
            store_high_low(ref, cols, turned)

    spec = pltpu.PrefetchScalarGridSpec(
        num_scalar_prefetch=1, grid=(1,),
        in_specs=[whole(a.shape) for a in (mine, received, sums, received_sums)],
        out_specs=[whole((own, cols + LANES))] * count,
    )
    return pl.pallas_call(
        body, grid_spec=spec, out_shape=[jax.ShapeDtypeStruct((own, cols + LANES), BF)] * count,
        compiler_params=pltpu.CompilerParams(vmem_limit_bytes=16 * MIB), name="add_halves_and_sums",
    )(index, mine, received, sums, received_sums)


def add_packed(name, items):
    cols = items[0].shape[1] - LANES

    def body(*refs):
        out_ref = refs[-1]
        out_ref[:, :cols] = tree_sum(ref[:, :cols].astype(F32) for ref in refs[:-1]).astype(BF)
        store_high_low(out_ref, cols, tree_sum(load_high_low(ref, cols) for ref in refs[:-1]))

    return small_call(body, name, items, [(items[0].shape, BF)])[0]


def add_last(items):
    own, cols = items[0].shape[0], items[0].shape[1] - LANES

    def body(*refs):
        ins, outs = refs[: len(items)], refs[len(items) :]
        outs[0][...] = tree_sum(ref[:, :cols].astype(F32) for ref in ins)
        vectors = tree_sum(load_high_low(ref, cols) for ref in ins)
        outs[1][...] = vectors[0:3, :own]
        for i in range(4):
            outs[2 + i][...] = vectors[3 + i : 4 + i, :own]

    return small_call(body, "add_last", items, [((own, cols), F32), ((3, own), F32)] + [((1, own), F32)] * 4)


def direct_plan(tokens, segment_ids, valid_len, qkv_weight, out_weight, up_weight, down_weight, conv_weight, vectors, cotangent):
    count, seq, width = tokens.shape
    own, ffs = up_weight.shape
    dp, mp = lax.axis_size("dp"), lax.axis_size("mp")
    me = lax.axis_index("dp")
    offsets = [2 * p for p in range(dp // 2)]
    index = jnp.stack([me ^ (p ^ c) for p in offsets for c in range(2)]).astype(jnp.int32)
    narrow, ff_own = small_call(
        pack_weights, "pack_weights",
        [in_hbm(a) for a in (qkv_weight, up_weight, down_weight, conv_weight, *[v.reshape(1, own) for v in vectors])],
        [((own, 3 * width + VECTORS), BF), ((2 * own, ffs), BF)], [((VECTORS, VECTORS), F32)],
    )
    plane = [narrow] + [exchange(narrow, "dp", p) for p in offsets[1:]]
    shards = [ff_own] + [exchange(ff_own, "mp", j) for j in range(1, mp)]
    pieces = [piece for a in plane for piece in (a, exchange(a, "dp", 1))]
    column = jnp.concatenate(shards + [out_weight], axis=0)
    columns = [column] + [exchange(column, "dp", p) for p in offsets[1:]]
    x, mixed, normed, q, k, v, raised, att, inverse, aux, packed, weight = run_forward(
        index, tokens, segment_ids, valid_len, pieces
    )
    columns, att = lax.optimization_barrier((columns, att))
    pieces = [piece for a in columns for piece in (a, exchange(a, "dp", 1))]
    hidden, mixed_attn, grad_mixed, grad_att, sums2, down, mine, theirs = run_feed_forward(
        index, att, mixed, cotangent, packed, pieces, mp
    )
    received = exchange(theirs, "dp", 1)
    early, late = halves(count)
    kept = (q, k, v, raised, att, inverse, normed, x, aux, mixed)
    grads = (grad_att, grad_mixed)
    some_grad, sums, start = run_backward(index, weight, kept, grads, packed, sums2, dp, early, None, None)
    received, start = lax.optimization_barrier((received, start))
    parts = list(add_halves(mine, received))
    parts[0], start = lax.optimization_barrier((parts[0], start))
    plane = [parts[0]] + [exchange(parts[i], "dp", p) for i, p in enumerate(offsets) if i]
    input_grad, sums, mine_a, theirs_a = run_backward(
        index, weight, kept, grads, packed, sums, dp, late, start, some_grad
    )
    plane, theirs_a, sums = lax.optimization_barrier((plane, theirs_a, sums))
    received_a = exchange(theirs_a, "dp", 1)
    received_s = exchange(sums, "dp", 1)
    total = add_wide(*plane).astype(BF)
    half = 2 * ffs * (mp // 2)
    near, far, out_part = total[:, :half], total[:, half:], total[:, 2 * half :]
    received_f = exchange(far, "mp", 2)
    parts = add_halves_and_sums(index, mine_a, received_a, sums, received_s)
    plane_a = [parts[0]] + [exchange(parts[i], "dp", p) for i, p in enumerate(offsets) if i]
    total = add_packed("add_plane", plane_a)
    received_1 = exchange(total, "mp", 2)
    received_f, hidden, _ = lax.optimization_barrier((received_f, hidden, total))
    near_sum = add_wide(near, received_f[:, :half])
    out_sum = lax.optimization_barrier(add_wide(out_part, received_f[:, half:]).astype(BF))
    keep = near_sum[:, : 2 * ffs]
    send = jnp.concatenate([near_sum[:, 2 * ffs :].astype(BF), out_sum], axis=1)
    received_n = exchange(send, "mp", 1)
    layer_out = run_layer_output(hidden, mixed_attn, down, cotangent.shape)
    received_1, layer_out = lax.optimization_barrier((received_1, layer_out))
    total = add_packed("add_far", (total, received_1))
    received_2 = exchange(total, "mp", 1)
    grad_up = keep[:, :ffs] + received_n[:, :ffs].astype(F32)
    grad_down = keep[:, ffs:] + received_n[:, ffs : 2 * ffs].astype(F32)
    grad_out = add_wide(out_sum, received_n[:, 2 * ffs :])
    grad_qkv, grad_conv, *grads = add_last((total, received_2))
    return (layer_out, input_grad, grad_qkv, grad_out, grad_up, grad_down, grad_conv, *[g.reshape(own) for g in grads])


def gathered_plan(tokens, segment_ids, valid_len, qkv_weight, out_weight, up_weight, down_weight, conv_weight, vectors, cotangent):
    count, seq, width = tokens.shape
    own = qkv_weight.shape[0]
    dp = width // own
    columns = jnp.stack([conv_weight[0], conv_weight[1], conv_weight[2], *vectors], axis=1)
    narrow = jnp.concatenate([qkv_weight, jnp.pad(columns, ((0, 0), (0, VECTORS - 7))), out_weight], axis=1)
    wide = lax.all_gather(narrow, "dp", axis=0, tiled=True)
    both = lax.all_gather(jnp.concatenate([up_weight, down_weight], axis=0), "mp", axis=1, tiled=True)
    ff = both.shape[1]
    shards = ff // width
    both = lax.all_gather(both, "dp", axis=0).reshape(dp, 2, own, shards, width)
    both = both.transpose(3, 1, 0, 2, 4).reshape(2 * ff, width)
    column = jnp.concatenate([both, wide[:, 3 * width + VECTORS :]], axis=0)
    index = jnp.zeros((1,), jnp.int32)
    x, mixed, normed, q, k, v, raised, att, inverse, aux, packed, weight = run_forward(
        index, tokens, segment_ids, valid_len, [wide[:, : 3 * width + VECTORS]]
    )
    hidden, mixed_attn, grad_mixed, grad_att, sums2, down, grads = run_feed_forward(
        index, att, mixed, cotangent, packed, [column], shards
    )
    early, late = halves(count)
    kept = (q, k, v, raised, att, inverse, normed, x, aux, mixed)
    grad_rows = (grad_att, grad_mixed)
    layer_out = run_layer_output(hidden, mixed_attn, down, cotangent.shape)
    some_grad, sums, start = run_backward(index, weight, kept, grad_rows, packed, sums2, 1, early, None, None)
    input_grad, sums, grad_qkv = run_backward(index, weight, kept, grad_rows, packed, sums, 1, late, start, some_grad)
    grad_ff = grads[0, :, : 2 * ff].reshape(width, shards, 2, width).transpose(0, 2, 1, 3).reshape(width, 2 * ff)
    grad_ff = lax.psum_scatter(grad_ff, "dp", scatter_dimension=0, tiled=True).reshape(own, 2, ff)
    grad_ff = lax.psum_scatter(grad_ff, "mp", scatter_dimension=2, tiled=True).astype(F32)
    grad_attn = jnp.concatenate([grad_qkv[0], grads[0, :, 2 * ff :]], axis=1)
    grad_attn = lax.psum_scatter(grad_attn, "dp", scatter_dimension=0, tiled=True)
    grad_attn = lax.psum(grad_attn, "mp").astype(F32)
    sums = lax.psum(sums, ("dp", "mp"))
    sums = lax.dynamic_slice_in_dim(sums, lax.axis_index("dp") * own, own, axis=1)
    return (
        layer_out, input_grad, grad_attn[:, : 3 * width], grad_attn[:, 3 * width :],
        grad_ff[:, 0], grad_ff[:, 1], sums[0:3], sums[3], sums[4], sums[5], sums[6],
    )


def on_device(
    tokens, segment_ids, valid_len, qkv_weight, out_weight, up_weight, down_weight, conv_weight,
    ln1_gain, ln1_shift, ln2_gain, ln2_shift, cotangent,
):
    own, ffs = up_weight.shape
    direct = own % 16 == 0 and ffs == tokens.shape[2] and own <= VECTORS and lax.axis_size("mp") == 4
    plan = direct_plan if direct else gathered_plan
    return plan(
        tokens, segment_ids, valid_len, qkv_weight, out_weight, up_weight, down_weight, conv_weight,
        (ln1_gain, ln1_shift, ln2_gain, ln2_shift), cotangent,
    )


def solution(mesh):
    rows = P(("dp", "mp"), None, None)
    weights = (P("dp", None), P("dp", None), P("dp", "mp"), P("dp", "mp"), P(None, "dp"))
    vectors = (P("dp"),) * 4
    return jax.shard_map(
        on_device,
        mesh=mesh,
        in_specs=(rows, P(("dp", "mp"), None), P(("dp", "mp"))) + weights + vectors + (rows,),
        out_specs=(rows, rows) + weights + vectors,
        check_vma=False,
    )
```

```python
import functools
import math

import jax
import jax.numpy as jnp
from jax import lax
from jax.experimental import pallas as pl
from jax.experimental.pallas import tpu as pltpu
from jax.sharding import PartitionSpec as P

HEADS = 6
VECTORS = 128
LANES = 128
BF = jnp.bfloat16
F32 = jnp.float32
MIB = 1024 * 1024
VMEM_LIMITS = dict(forward_attention=26, feed_forward=40, backward=36, layer_output=16)


def mm(lhs, rhs):
    return lax.dot_general(lhs, rhs, (((1,), (0,)), ((), ())), preferred_element_type=F32)


def mm_nt(lhs, rhs):
    return lax.dot_general(lhs, rhs, (((1,), (1,)), ((), ())), preferred_element_type=F32)


def tree_sum(items):
    items = list(items)
    while len(items) > 1:
        items = [a + b for a, b in zip(items[::2], items[1::2])]
    return items[0]


def pack_weights(qkv_ref, up_ref, down_ref, conv_ref, g1_ref, s1_ref, g2_ref, s2_ref, narrow_ref, ff_ref, rows_ref):
    own, ffs = up_ref.shape
    rows_ref[...] = jnp.zeros_like(rows_ref)
    rows_ref[0:3, :own] = conv_ref[...].astype(F32)
    for i, ref in enumerate((g1_ref, s1_ref, g2_ref, s2_ref)):
        rows_ref[3 + i : 4 + i, :own] = ref[...].astype(F32)
    wide = qkv_ref.shape[1]
    narrow_ref[:, :wide] = qkv_ref[...]
    narrow_ref[:, wide:] = rows_ref[...].T[:own].astype(BF)
    ff_ref[:own] = up_ref[...]
    ff_ref[own:] = down_ref[...]


def tiles(total, size):
    return [slice(at, at + size) for at in range(0, total, size)]


def weave(*strands):
    strands = [strand for strand in strands if strand]
    total = sum(len(strand) for strand in strands)
    pieces = [((i + 0.5) / len(strand), j, piece) for j, strand in enumerate(strands) for i, piece in enumerate(strand)]
    assert len(pieces) == total
    for _, _, piece in sorted(pieces, key=lambda item: item[:2]):
        piece()


def twice(tile, lanes):
    return jnp.concatenate([tile] * (lanes // LANES), axis=1)


def load_columns(packed_ref, col_ref, places):
    for i, place in enumerate(places):
        column = packed_ref[:, place : place + 1].astype(F32)
        col_ref[i] = jnp.broadcast_to(column, (column.shape[0], LANES))


def column_mean(values):
    return jnp.sum(values, axis=0, keepdims=True) * (1.0 / values.shape[0])


def norm_columns(values):
    centred = values - column_mean(values)
    scale = lax.rsqrt(column_mean(centred * centred) + 1e-06)
    return centred * scale, scale


def fold(values):
    rows, lanes = values.shape
    return jnp.sum(values.reshape(rows // 8, 8, lanes), axis=0)


def fold_lanes(values):
    return sum(values[:, t] for t in tiles(values.shape[1], LANES))


def forward_attention(index_ref, len_ref, tok_ref, seg_ref, *refs, pieces):
    piece_refs = refs[:pieces]
    (
        x_ref, mc_ref, norm_ref, q_ref, k_ref, v_ref, e_ref, att_ref, inv_ref, aux_ref, packed_ref, w_ref,
        wt_ref, wide_ref, col_ref, bias_ref, key_ref, value_ref,
    ) = refs[pieces:]
    rows, seq, width = tok_ref.shape
    head = width // HEADS
    step = pl.program_id(0)

    @pl.when(step == 0)
    def _():
        own = width // pieces
        for i, ref in enumerate(piece_refs):
            wide_ref[pl.ds(pl.multiple_of(index_ref[i] * own, 16), own), :] = ref[...]
        w_ref[...] = wide_ref[:, : 3 * width]
        wt_ref[:width] = (wide_ref[:, :width].astype(F32) * head ** (-0.5)).astype(BF).T
        wt_ref[width:] = wide_ref[:, width : 3 * width].T
        packed_ref[...] = wide_ref[:, 3 * width :]
        load_columns(packed_ref, col_ref, range(5))

    place = lax.broadcasted_iota(jnp.int32, (1, seq), 1)
    zero = jnp.zeros((head, seq), BF)

    def preparation(r):
        known = {}

        def start():
            segs = seg_ref[pl.ds(step * rows + r, 1), :].astype(F32)
            valid = place < len_ref[step * rows + r]
            number = jnp.where(valid, segs, -1.0)
            links = jnp.where(valid & (place > 0) & (number == pltpu.roll(number, 1, 1)), 1.0, 0.0)
            next_links = jnp.where(place < seq - 1, pltpu.roll(links, seq - 1, 1), 0.0)
            none = jnp.zeros_like(links)
            aux = jnp.concatenate([links, next_links, number, none, none, none, none, none], axis=0)
            aux_ref[r] = aux
            x_ref[r] = tok_ref[r].T
            known.update(segs=segs, links=links, next_links=next_links, key_number=aux.T[:, 2:3])

        def mask(t):
            row_id = lax.broadcasted_iota(jnp.int32, (64, seq), 0) + t.start
            col_id = lax.broadcasted_iota(jnp.int32, (64, seq), 1)
            allowed = (known["key_number"][t] == known["segs"]) | (row_id == col_id)
            bias_ref[r, t] = jnp.where(allowed, 0.0, -1e30)

        def conv(t):
            base = x_ref[r, t].astype(F32)
            before = pltpu.roll(base, 1, 1) * known["links"]
            after = pltpu.roll(base, seq - 1, 1) * known["next_links"]
            conv0, conv1, conv2 = [twice(col_ref[i, t], seq) for i in range(3)]
            mc_ref[r, t] = base + before * conv0 + base * conv1 + after * conv2

        def norm(t):
            n, _ = norm_columns(mc_ref[r, :, t])
            norm_ref[r, :, t] = (n * col_ref[3] + col_ref[4]).astype(BF)

        pieces = [start] + [functools.partial(conv, t) for t in tiles(width, 32)]
        pieces += [functools.partial(norm, t) for t in tiles(seq, LANES)]
        return pieces + [functools.partial(mask, t) for t in tiles(seq, 64)]

    def project():
        normed = jnp.concatenate([norm_ref[r] for r in range(rows)], axis=1)
        for i, ref in enumerate((q_ref, k_ref, value_ref)):
            part = mm(wt_ref[i * width : (i + 1) * width], normed).astype(BF)
            for r in range(rows):
                ref[r] = part[:, r * seq : (r + 1) * seq]
        for r in range(rows):
            key_ref[r] = k_ref[r].T
            v_ref[r] = value_ref[r].T

    def scores(r, p):
        low, high = [q_ref[r, h * head : (h + 1) * head] for h in (2 * p, 2 * p + 1)]
        both = jnp.concatenate([jnp.concatenate([low, zero], axis=1), jnp.concatenate([zero, high], axis=1)], axis=0)
        return mm(key_ref[r, :, 2 * p * head : 2 * (p + 1) * head], both)

    def attended(r, p):
        both = jnp.concatenate([e_ref[r, 2 * p], e_ref[r, 2 * p + 1]], axis=1)
        product = mm(value_ref[r, 2 * p * head : 2 * (p + 1) * head], both)
        parts = []
        for i in range(2):
            att = product[i * head : (i + 1) * head, i * seq : (i + 1) * seq] * inv_ref[r, 2 * p + i : 2 * p + i + 1]
            parts.append(att.astype(BF))
        return jnp.concatenate(parts, axis=0)

    def soften(r, p, product):
        for i in range(2):
            for t in tiles(seq, LANES):
                masked = product[:, i * seq + t.start : i * seq + t.stop] + bias_ref[r, :, t]
                raised = jnp.exp(masked - jnp.max(masked, axis=0, keepdims=True))
                inv_ref[r, 2 * p + i : 2 * p + i + 1, t] = 1.0 / jnp.sum(raised, axis=0, keepdims=True)
                e_ref[r, 2 * p + i, :, t] = raised.astype(BF)

    weave(*[preparation(r) for r in range(rows)])
    project()
    work = [(r, p) for r in range(rows) for p in range(HEADS // 2)]
    current, last = scores(*work[0]), None
    for at, (r, p) in enumerate(work):
        following = scores(*work[at + 1]) if at + 1 < len(work) else None
        finished = attended(*last) if last else None
        soften(r, p, current)
        if last:
            att_ref[last[0], 2 * last[1] * head : 2 * (last[1] + 1) * head] = finished
        current, last = following, (r, p)
    att_ref[last[0], 2 * last[1] * head : 2 * (last[1] + 1) * head] = attended(*last)


def gelu_parts(x):
    cdf = 0.5 * lax.erf(x * math.sqrt(0.5)) + 0.5
    bell = jnp.exp2(x * x * (-0.5 / math.log(2.0)) - 0.5 * math.log2(2.0 * math.pi))
    return x * cdf, cdf + x * bell


def feed_forward(index_ref, att_ref, mc_ref, ct_ref, packed_ref, *refs, pieces, shards):
    piece_refs = refs[:pieces]
    groups = 2 if pieces > 1 else 1
    hidden_out, mixed_out, gm_ref, ga_ref, gs_ref, down_ref = refs[pieces : pieces + 6]
    hidden_ref, mixed_ref = hidden_out.at[0], mixed_out.at[0]
    gw_refs = refs[pieces + 6 : pieces + 6 + groups]
    (
        up_ref, upt_ref, downt_ref, out_ref, outt_ref, up_acc, down_acc, out_acc, col_acc, col_ref,
        att_cat, n_ref, norm_ref, ctt_ref, gp_ref, gn_ref, scale_ref, branch_ref,
    ) = refs[pieces + 6 + groups :]
    rows, seq, width = ct_ref.shape
    ff = up_ref.shape[1]
    ffs = ff // shards
    own = width // pieces
    step = pl.program_id(0)

    @pl.when(step == 0)
    def _():
        for acc in (up_acc, down_acc, out_acc, col_acc):
            acc[...] = jnp.zeros_like(acc)
        for i, ref in enumerate(piece_refs):
            here = pl.ds(pl.multiple_of(index_ref[i] * own, 16), own)
            for j in range(shards):
                up_ref[here, j * ffs : (j + 1) * ffs] = ref[2 * j * own : (2 * j + 1) * own]
                down_ref[here, j * ffs : (j + 1) * ffs] = ref[(2 * j + 1) * own : (2 * j + 2) * own]
            out_ref[here, :] = ref[2 * shards * own :]
        upt_ref[...] = up_ref[...].T
        downt_ref[...] = down_ref[...].T
        outt_ref[...] = out_ref[...].T
        load_columns(packed_ref, col_ref, (5, 6))

    def lanes_of(r):
        return slice(r * seq, (r + 1) * seq)

    def spots_of(r):
        return [slice(at, at + LANES) for at in range(r * seq, (r + 1) * seq, LANES)]

    def preparation(r):
        lanes = lanes_of(r)

        def turn():
            ctt_ref[:, lanes] = ct_ref[r].T
            att_cat[:, lanes] = att_ref[r]

        def branch():
            mixed_ref[:, lanes] = mc_ref[r] + mm(outt_ref[...], att_ref[r])

        def norm(t):
            n, scale = norm_columns(mixed_ref[:, t])
            n_ref[:, t] = n
            scale_ref[0:1, t] = scale
            norm_ref[:, t] = (n * col_ref[0] + col_ref[1]).astype(BF)

        return [turn, branch] + [functools.partial(norm, t) for t in spots_of(r)]

    def activation(block):
        pre = mm(upt_ref[block], norm_ref[...])
        grad_hidden = mm(downt_ref[block], ctt_ref[...])
        for low in range(0, block.stop - block.start, 16):
            part = slice(low, low + 16)
            here = slice(block.start + low, block.start + low + 16)
            hidden, slope = gelu_parts(pre[part])
            hidden_ref[here] = hidden.astype(BF)
            gp_ref[here] = (grad_hidden[part] * slope).astype(BF)

    def norm_back(r):
        spots = spots_of(r)
        mean_e = [jnp.zeros((8, LANES), F32) for _ in spots]
        mean_en = [jnp.zeros((8, LANES), F32) for _ in spots]
        means = []

        def sums(d):
            column = col_ref[0, d]
            gain_sum, shift_sum = col_acc[0, d], col_acc[1, d]
            for i, t in enumerate(spots):
                grad_n = gn_ref[d, t]
                product = grad_n * n_ref[d, t]
                gain_sum += product
                shift_sum += grad_n
                mean_e[i] += fold(grad_n * column)
                mean_en[i] += fold(product * column)
            col_acc[0, d] = gain_sum
            col_acc[1, d] = shift_sum

        def finish():
            for i in range(len(spots)):
                me = jnp.sum(mean_e[i], axis=0, keepdims=True) * (1.0 / width)
                men = jnp.sum(mean_en[i], axis=0, keepdims=True) * (1.0 / width)
                means.append((me, men))

        def apply(d):
            for i, t in enumerate(spots):
                me, men = means[i]
                change = scale_ref[0:1, t] * (gn_ref[d, t] * col_ref[0, d] - me - n_ref[d, t] * men)
                grad_mixed = ctt_ref[d, t].astype(F32) + change
                gm_ref[r, d, i * LANES : (i + 1) * LANES] = grad_mixed
                branch_ref[d, t] = grad_mixed.astype(BF)

        def attended():
            ga_ref[r] = mm(out_ref[...], branch_ref[:, lanes_of(r)]).astype(BF)

        pieces = [functools.partial(sums, d) for d in tiles(width, 32)] + [finish]
        return pieces + [functools.partial(apply, d) for d in tiles(width, 32)] + [attended]

    weave(*[preparation(r) for r in range(rows)])
    for block in tiles(ff, 128):
        activation(block)
    gn_ref[...] = mm(up_ref[...], gp_ref[...])
    down_acc[...] += mm_nt(ctt_ref[...], hidden_ref[...])
    up_acc[...] += mm_nt(norm_ref[...], gp_ref[...])
    weave(*[norm_back(r) for r in range(rows)])
    out_acc[...] += mm_nt(att_cat[...], branch_ref[...])

    @pl.when(step == pl.num_programs(0) - 1)
    def _():
        for i in range(pieces):
            here = pl.ds(pl.multiple_of(index_ref[i] * own, 16), own)
            place = gw_refs[i % groups]
            for j in range(shards):
                cols = slice(j * ffs, (j + 1) * ffs)
                place[i // groups, :, 2 * j * ffs : (2 * j + 1) * ffs] = up_acc[here, cols].astype(BF)
                place[i // groups, :, (2 * j + 1) * ffs : (2 * j + 2) * ffs] = down_acc[here, cols].astype(BF)
            place[i // groups, :, 2 * ff :] = out_acc[here, :].astype(BF)
        gs_ref[...] = jnp.zeros_like(gs_ref)
        for i in range(2):
            gs_ref[5 + i : 6 + i] = jnp.sum(col_acc[i].T, axis=0, keepdims=True)


def layer_output(hidden_ref, mixed_ref, down_ref, lo_ref):
    rows, seq, _ = lo_ref.shape
    total = (mixed_ref[0] + mm(down_ref[...], hidden_ref[0])).astype(BF)
    for r in range(rows):
        lo_ref[r] = total[:, r * seq : (r + 1) * seq].T


def backward(
    q_ref, k_ref, v_ref, e_ref, att_ref, inv_ref, norm_ref, ga_ref, x_ref, aux_ref, mc_ref, gm_ref,
    index_ref, w_ref, packed_ref, other_ref, ig_ref, gs_ref, *refs, pieces,
):
    gw_refs = refs[:-11]
    (
        proj_ref, w_acc, norm_cat, soft_ref, logit_ref, gn_ref, acc_ref, col_ref, n_ref, g_ref, turn_ref
    ) = refs[-11:]
    rows, seq, width = v_ref.shape
    own = width // pieces
    head = width // HEADS
    step = pl.program_id(0)

    @pl.when(step == 0)
    def _():
        w_acc[...] = jnp.zeros_like(w_acc)
        acc_ref[...] = jnp.zeros_like(acc_ref)
        load_columns(packed_ref, col_ref, range(4))

    zero = jnp.zeros((head, seq), BF)
    work = [(r, p) for r in range(rows) for p in range(HEADS // 2)]

    def opening(r, p):
        grads, inners = [], []
        for h in (2 * p, 2 * p + 1):
            part = slice(h * head, (h + 1) * head)
            grad_att = ga_ref[r, part].astype(F32) * inv_ref[r, h : h + 1]
            inners.append(jnp.sum(grad_att * att_ref[r, part].astype(F32), axis=0, keepdims=True))
            grads.append(grad_att.astype(BF))
        low, high = grads
        both = jnp.concatenate([jnp.concatenate([low, zero], axis=1), jnp.concatenate([zero, high], axis=1)], axis=0)
        product = mm(v_ref[r, :, 2 * p * head : 2 * (p + 1) * head], both)
        soft_ref[r, 2 * p] = product[:, :seq]
        soft_ref[r, 2 * p + 1] = product[:, seq:]
        return jnp.concatenate(grads, axis=0), inners

    ready = opening(*work[0])
    for at, (r, p) in enumerate(work):
        grad_att, inners = ready
        if at + 1 < len(work):
            ready = opening(*work[at + 1])
        for i, h in enumerate((2 * p, 2 * p + 1)):
            for t in tiles(seq, 32):
                raised = e_ref[r, h, t].astype(F32)
                logit_ref[r, h, t] = (raised * (soft_ref[r, h, t] - inners[i])).astype(BF)
        part = slice(2 * p * head, 2 * (p + 1) * head)
        pair = slice(2 * p, 2 * p + 2)
        beside = jnp.concatenate([logit_ref[r, 2 * p], logit_ref[r, 2 * p + 1]], axis=1)
        grad_q = mm(k_ref[r, part], beside)
        grad_k = mm_nt(q_ref[r, part], logit_ref[r, pair].reshape(2 * seq, seq))
        grad_v = mm_nt(grad_att, e_ref[r, pair].reshape(2 * seq, seq))
        for i in range(2):
            place = slice(r * seq, (r + 1) * seq)
            own_rows, own_cols = slice(i * head, (i + 1) * head), slice(i * seq, (i + 1) * seq)
            for j, grad in enumerate((grad_q, grad_k, grad_v)):
                first = j * width + (2 * p + i) * head
                mine = grad[own_rows, own_cols]
                proj_ref[first : first + head, place] = (mine * head ** (-0.5) if j == 0 else mine).astype(BF)
    gn_ref[...] = mm(w_ref[...], proj_ref[...])
    for r in range(rows):
        norm_cat[:, r * seq : (r + 1) * seq] = norm_ref[r]
    w_acc[...] += mm_nt(norm_cat[...], proj_ref[...])

    spots = tiles(seq, LANES)
    for r in range(rows):
        wide = [slice(r * seq + t.start, r * seq + t.stop) for t in spots]
        scales = []
        for t in spots:
            n, scale = norm_columns(mc_ref[r, :, t])
            n_ref[r, :, t] = n
            scales.append(scale)
        mean_e = [jnp.zeros((8, LANES), F32) for _ in spots]
        mean_en = [jnp.zeros((8, LANES), F32) for _ in spots]
        for d in tiles(width, 32):
            column = col_ref[3, d]
            gain_sum, shift_sum = acc_ref[3, d], acc_ref[4, d]
            for i, t in enumerate(spots):
                grad_n = gn_ref[d, wide[i]]
                product = grad_n * n_ref[r, d, t]
                gain_sum += product
                shift_sum += grad_n
                mean_e[i] += fold(grad_n * column)
                mean_en[i] += fold(product * column)
            acc_ref[3, d] = gain_sum
            acc_ref[4, d] = shift_sum
        for i, t in enumerate(spots):
            me = jnp.sum(mean_e[i], axis=0, keepdims=True) * (1.0 / width)
            men = jnp.sum(mean_en[i], axis=0, keepdims=True) * (1.0 / width)
            for d in tiles(width, 64):
                e = gn_ref[d, wide[i]] * col_ref[3, d]
                g_ref[r, d, t] = gm_ref[r, d, t] + scales[i] * (e - me - n_ref[r, d, t] * men)
        links, next_links = aux_ref[r, 0:1], aux_ref[r, 1:2]
        for d in tiles(width, 32):
            g = g_ref[r, d]
            base = x_ref[r, d].astype(F32)
            before = pltpu.roll(g, 1, 1) * links
            after = pltpu.roll(g, seq - 1, 1) * next_links
            acc_ref[0, d] += fold_lanes(base * after)
            acc_ref[1, d] += fold_lanes(base * g)
            acc_ref[2, d] += fold_lanes(base * before)
            conv0, conv1, conv2 = [twice(col_ref[i, d], seq) for i in range(3)]
            turn_ref[r, d] = (g + conv1 * g + conv0 * after + conv2 * before).astype(BF)
        ig_ref[r] = turn_ref[r].T

    @pl.when(step == pl.num_programs(0) - 1)
    def _():
        gs_ref[...] = other_ref[...]
        for i in range(5):
            gs_ref[i : i + 1] += jnp.sum(acc_ref[i].T, axis=0, keepdims=True)
        groups = len(gw_refs)
        for i in range(pieces):
            here = pl.ds(pl.multiple_of(index_ref[i] * own, 16), own)
            gw_refs[i % groups][i // groups] = w_acc[here, :].astype(BF)


def in_hbm(values):
    return pltpu.with_memory_space_constraint(values, pltpu.HBM)


def by_row(shape, rows, first=0):
    tail = tuple(shape[1:])
    return pl.BlockSpec((rows,) + tail, lambda i, *_: (i + first,) + (0,) * len(tail))


def whole(shape):
    place = (0,) * len(shape)
    return pl.BlockSpec(tuple(shape), lambda i, *_: place, pipeline_mode=pl.Buffered(1))


def step_rows(count, most):
    return max(r for r in range(1, most + 1) if count % r == 0)


def call(body, name, scalars, rows, row_args, args, row_outs, outs, scratch, span=None, into=None, near=()):
    first, count = span or (0, row_args[0].shape[0])
    skip = first // rows
    total = row_args[0].shape[0]

    def spec_of(shape):
        return by_row(shape, shape[0] * rows // total, skip)

    in_specs = [spec_of(a.shape) for a in row_args]
    in_specs += [whole(a.shape) for a in args]
    aliases = {}
    if into is not None:
        in_specs.append(pl.BlockSpec(memory_space=pl.ANY))
        aliases = {len(scalars) + len(in_specs) - 1: 0}
    spec = pltpu.PrefetchScalarGridSpec(
        num_scalar_prefetch=len(scalars),
        grid=(count // rows,),
        in_specs=in_specs,
        out_specs=[spec_of(s) for s, _ in row_outs] + [whole(s) for s, _ in outs],
        scratch_shapes=[pltpu.VMEM(s, t) for s, t in scratch],
    )
    return pl.pallas_call(
        body,
        grid_spec=spec,
        out_shape=[(jax.ShapeDtypeStruct if "out" + str(i) in near else pltpu.HBM)(s, t) for i, (s, t) in enumerate(row_outs)]
        + [jax.ShapeDtypeStruct(s, t) for s, t in outs],
        input_output_aliases=aliases,
        compiler_params=pltpu.CompilerParams(dimension_semantics=("arbitrary",), vmem_limit_bytes=VMEM_LIMITS[name] * MIB),
        name=name,
    )(*scalars, *[a if i in near else in_hbm(a) for i, a in enumerate(row_args)], *args, *(() if into is None else (into,)))


def small_call(body, name, args, outs, scratch=()):
    return pl.pallas_call(
        body,
        out_shape=[jax.ShapeDtypeStruct(s, t) for s, t in outs],
        scratch_shapes=[pltpu.VMEM(s, t) for s, t in scratch],
        compiler_params=pltpu.CompilerParams(vmem_limit_bytes=16 * MIB),
        name=name,
    )(*args)


def run_forward(index, tokens, segment_ids, valid_len, pieces):
    count, seq, width = tokens.shape
    flipped = (count, width, seq)
    rows = step_rows(count, 2)
    row_outs = [
        (flipped, BF), (flipped, F32), (flipped, BF), (flipped, BF), (flipped, BF), ((count, seq, width), BF),
        ((count, HEADS, seq, seq), BF), (flipped, BF), ((count, 8, seq), F32), ((count, 8, seq), F32),
    ]
    return call(
        functools.partial(forward_attention, pieces=len(pieces)), "forward_attention", (index, valid_len),
        rows, (tokens,), (in_hbm(segment_ids), *pieces),
        row_outs, [((width, VECTORS), BF), ((width, 3 * width), BF)],
        [
            ((3 * width, width), BF), ((width, 3 * width + VECTORS), BF), ((5, width, LANES), F32),
            ((rows, seq, seq), F32), ((rows, seq, width), BF), ((rows, width, seq), BF),
        ],
    )


def run_feed_forward(index, att, mixed, cotangent, packed, pieces, shards):
    count, seq, width = cotangent.shape
    own = width // len(pieces)
    ff = shards * width
    groups = 2 if len(pieces) > 1 else 1
    rows = step_rows(count, 2)
    wide = rows * seq
    row_outs = [
        ((count // rows, ff, wide), BF), ((count // rows, width, wide), F32),
        ((count, width, seq), F32), ((count, width, seq), BF),
    ]
    grads = ((len(pieces) // groups, own, 2 * ff + width), BF)
    return call(
        functools.partial(feed_forward, pieces=len(pieces), shards=shards), "feed_forward", (index,),
        rows, (att, mixed, cotangent), (packed, *pieces),
        row_outs, [((8, width), F32), ((width, ff), BF)] + [grads] * groups,
        [((width, ff), BF)] + [((ff, width), BF)] * 2 + [((width, width), BF)] * 2
        + [((width, ff), F32)] * 2 + [((width, width), F32), ((2, width, LANES), F32), ((2, width, LANES), F32)]
        + [((width, wide), BF), ((width, wide), F32), ((width, wide), BF), ((width, wide), BF)]
        + [((ff, wide), BF)]
        + [((width, wide), F32), ((8, wide), F32), ((width, wide), BF)],
        near=("out3",),
    )


def run_layer_output(hidden, mixed, down, shape, part, parts, into):
    steps = hidden.shape[0]
    span = (part * steps // parts, (part + 1) * steps // parts - part * steps // parts)

    def body(*refs):
        layer_output(*refs[:3], refs[-1])

    return call(body, "layer_output", (), 1, (hidden, mixed), (down,), [(shape, BF)], [], [], span=span, into=into)[0]


def run_backward(index, weight, kept, grads, packed, other, pieces):
    count, seq, width = kept[2].shape
    own = width // pieces
    groups = 2 if pieces > 1 else 1
    rows = step_rows(count, 2)
    row_args = (*kept[:7], grads[0], *kept[7:], grads[1])
    many = len(row_args)

    def body(index_ref, *refs):
        backward(*refs[:many], index_ref, *refs[many:], pieces=pieces)

    return call(
        body, "backward", (index,), rows, row_args, (weight, packed, other),
        [((count, seq, width), BF)], [((8, width), F32)] + [((pieces // groups, own, 3 * width), BF)] * groups,
        [
            ((3 * width, rows * seq), BF), ((width, 3 * width), F32), ((width, rows * seq), BF),
            ((rows, HEADS, seq, seq), F32), ((rows, HEADS, seq, seq), BF), ((width, rows * seq), F32),
            ((5, width, LANES), F32), ((4, width, LANES), F32), ((rows, width, seq), F32), ((rows, width, seq), F32),
            ((rows, width, seq), BF),
        ],
        near=(7,),
    )


def exchange(values, axis, offset):
    size = lax.axis_size(axis)
    return lax.ppermute(values, axis, [(i, i ^ offset) for i in range(size)])


def add_halves(mine, received):
    count, own, cols = mine.shape

    def body(mine_ref, received_ref, *out_refs):
        for i, ref in enumerate(out_refs):
            ref[...] = (mine_ref[i].astype(F32) + received_ref[i].astype(F32)).astype(BF)

    return small_call(body, "add_halves", (mine, received), [((own, cols), BF)] * count)


def add_wide(*items):
    return tree_sum(item.astype(F32) for item in items)


def store_high_low(ref, cols, values):
    high = values.astype(BF)
    low = (values - high.astype(F32)).astype(BF)
    ref[:, cols:] = jnp.concatenate([high, low, jnp.zeros((ref.shape[0] - 16, LANES), BF)], axis=0)


def load_high_low(ref, cols):
    both = ref[:16, cols:].astype(F32)
    return both[:8] + both[8:]


def add_halves_and_sums(index, mine, received, sums, received_sums):
    count, own, cols = mine.shape
    width = sums.shape[1]

    def body(index_ref, mine_ref, received_ref, sums_ref, received_sums_ref, *out_refs):
        total = sums_ref[...] + received_sums_ref[...]
        for i, ref in enumerate(out_refs):
            ref[:, :cols] = (mine_ref[i].astype(F32) + received_ref[i].astype(F32)).astype(BF)
            turned = pltpu.roll(total, lax.rem(width - index_ref[2 * i] * own, width), 1)[:, :LANES]
            store_high_low(ref, cols, turned)

    spec = pltpu.PrefetchScalarGridSpec(
        num_scalar_prefetch=1, grid=(1,),
        in_specs=[whole(a.shape) for a in (mine, received, sums, received_sums)],
        out_specs=[whole((own, cols + LANES))] * count,
    )
    return pl.pallas_call(
        body, grid_spec=spec, out_shape=[jax.ShapeDtypeStruct((own, cols + LANES), BF)] * count,
        compiler_params=pltpu.CompilerParams(vmem_limit_bytes=16 * MIB), name="add_halves_and_sums",
    )(index, mine, received, sums, received_sums)


def add_packed(name, items):
    cols = items[0].shape[1] - LANES

    def body(*refs):
        out_ref = refs[-1]
        out_ref[:, :cols] = tree_sum(ref[:, :cols].astype(F32) for ref in refs[:-1]).astype(BF)
        store_high_low(out_ref, cols, tree_sum(load_high_low(ref, cols) for ref in refs[:-1]))

    return small_call(body, name, items, [(items[0].shape, BF)])[0]


def add_last(items):
    own, cols = items[0].shape[0], items[0].shape[1] - LANES

    def body(*refs):
        ins, outs = refs[: len(items)], refs[len(items) :]
        outs[0][...] = tree_sum(ref[:, :cols].astype(F32) for ref in ins)
        vectors = tree_sum(load_high_low(ref, cols) for ref in ins)
        outs[1][...] = vectors[0:3, :own]
        for i in range(4):
            outs[2 + i][...] = vectors[3 + i : 4 + i, :own]

    return small_call(body, "add_last", items, [((own, cols), F32), ((3, own), F32)] + [((1, own), F32)] * 4)


def direct_plan(tokens, segment_ids, valid_len, qkv_weight, out_weight, up_weight, down_weight, conv_weight, vectors, cotangent):
    count, seq, width = tokens.shape
    own, ffs = up_weight.shape
    dp, mp = lax.axis_size("dp"), lax.axis_size("mp")
    me = lax.axis_index("dp")
    offsets = [2 * p for p in range(dp // 2)]
    index = jnp.stack([me ^ (p ^ c) for p in offsets for c in range(2)]).astype(jnp.int32)
    narrow, ff_own = small_call(
        pack_weights, "pack_weights",
        [in_hbm(a) for a in (qkv_weight, up_weight, down_weight, conv_weight, *[v.reshape(1, own) for v in vectors])],
        [((own, 3 * width + VECTORS), BF), ((2 * own, ffs), BF)], [((VECTORS, VECTORS), F32)],
    )
    plane = [narrow] + [exchange(narrow, "dp", p) for p in offsets[1:]]
    shards = [ff_own] + [exchange(ff_own, "mp", j) for j in range(1, mp)]
    pieces = [piece for a in plane for piece in (a, exchange(a, "dp", 1))]
    column = jnp.concatenate(shards + [out_weight], axis=0)
    columns = [column] + [exchange(column, "dp", p) for p in offsets[1:]]
    x, mixed, normed, q, k, v, raised, att, inverse, aux, packed, weight = run_forward(
        index, tokens, segment_ids, valid_len, pieces
    )
    columns, att = lax.optimization_barrier((columns, att))
    pieces = [piece for a in columns for piece in (a, exchange(a, "dp", 1))]
    hidden, mixed_attn, grad_mixed, grad_att, sums2, down, mine, theirs = run_feed_forward(
        index, att, mixed, cotangent, packed, pieces, mp
    )
    received = exchange(theirs, "dp", 1)
    shape = cotangent.shape
    layer_out = run_layer_output(hidden, mixed_attn, down, shape, 0, 3, None)
    received, layer_out = lax.optimization_barrier((received, layer_out))
    parts = list(add_halves(mine, received))
    parts[0], grad_att = lax.optimization_barrier((parts[0], grad_att))
    plane = [parts[0]] + [exchange(parts[i], "dp", p) for i, p in enumerate(offsets) if i]
    kept = (q, k, v, raised, att, inverse, normed, x, aux, mixed)
    input_grad, sums, mine_a, theirs_a = run_backward(
        index, weight, kept, (grad_att, grad_mixed), packed, sums2, dp
    )
    plane, theirs_a, sums = lax.optimization_barrier((plane, theirs_a, sums))
    received_a = exchange(theirs_a, "dp", 1)
    received_s = exchange(sums, "dp", 1)
    total = add_wide(*plane).astype(BF)
    half = 2 * ffs * (mp // 2)
    near, far, out_part = total[:, :half], total[:, half:], total[:, 2 * half :]
    parts = list(add_halves_and_sums(index, mine_a, received_a, sums, received_s))
    parts[0], far, hidden, layer_out = lax.optimization_barrier((parts[0], far, hidden, layer_out))
    plane_a = [parts[0]] + [exchange(parts[i], "dp", p) for i, p in enumerate(offsets) if i]
    received_f = exchange(far, "mp", 2)
    layer_out = run_layer_output(hidden, mixed_attn, down, shape, 1, 3, layer_out)
    plane_a, layer_out = lax.optimization_barrier((plane_a, layer_out))
    total = add_packed("add_plane", plane_a)
    received_1 = exchange(total, "mp", 2)
    layer_out, _ = lax.optimization_barrier((layer_out, total))
    layer_out = run_layer_output(hidden, mixed_attn, down, shape, 2, 3, layer_out)
    received_1, received_f, layer_out = lax.optimization_barrier((received_1, received_f, layer_out))
    near_sum = add_wide(near, received_f[:, :half])
    out_sum = lax.optimization_barrier(add_wide(out_part, received_f[:, half:]).astype(BF))
    keep = near_sum[:, : 2 * ffs]
    send = jnp.concatenate([near_sum[:, 2 * ffs :].astype(BF), out_sum], axis=1)
    received_n = exchange(send, "mp", 1)
    total = add_packed("add_far", (total, received_1))
    received_2 = exchange(total, "mp", 1)
    grad_up = keep[:, :ffs] + received_n[:, :ffs].astype(F32)
    grad_down = keep[:, ffs:] + received_n[:, ffs : 2 * ffs].astype(F32)
    grad_out = add_wide(out_sum, received_n[:, 2 * ffs :])
    grad_qkv, grad_conv, *grads = add_last((total, received_2))
    return (layer_out, input_grad, grad_qkv, grad_out, grad_up, grad_down, grad_conv, *[g.reshape(own) for g in grads])


def gathered_plan(tokens, segment_ids, valid_len, qkv_weight, out_weight, up_weight, down_weight, conv_weight, vectors, cotangent):
    count, seq, width = tokens.shape
    own = qkv_weight.shape[0]
    dp = width // own
    columns = jnp.stack([conv_weight[0], conv_weight[1], conv_weight[2], *vectors], axis=1)
    narrow = jnp.concatenate([qkv_weight, jnp.pad(columns, ((0, 0), (0, VECTORS - 7))), out_weight], axis=1)
    wide = lax.all_gather(narrow, "dp", axis=0, tiled=True)
    both = lax.all_gather(jnp.concatenate([up_weight, down_weight], axis=0), "mp", axis=1, tiled=True)
    ff = both.shape[1]
    shards = ff // width
    both = lax.all_gather(both, "dp", axis=0).reshape(dp, 2, own, shards, width)
    both = both.transpose(3, 1, 0, 2, 4).reshape(2 * ff, width)
    column = jnp.concatenate([both, wide[:, 3 * width + VECTORS :]], axis=0)
    index = jnp.zeros((1,), jnp.int32)
    x, mixed, normed, q, k, v, raised, att, inverse, aux, packed, weight = run_forward(
        index, tokens, segment_ids, valid_len, [wide[:, : 3 * width + VECTORS]]
    )
    hidden, mixed_attn, grad_mixed, grad_att, sums2, down, grads = run_feed_forward(
        index, att, mixed, cotangent, packed, [column], shards
    )
    kept = (q, k, v, raised, att, inverse, normed, x, aux, mixed)
    layer_out = run_layer_output(hidden, mixed_attn, down, cotangent.shape, 0, 1, None)
    input_grad, sums, grad_qkv = run_backward(index, weight, kept, (grad_att, grad_mixed), packed, sums2, 1)
    grad_ff = grads[0, :, : 2 * ff].reshape(width, shards, 2, width).transpose(0, 2, 1, 3).reshape(width, 2 * ff)
    grad_ff = lax.psum_scatter(grad_ff, "dp", scatter_dimension=0, tiled=True).reshape(own, 2, ff)
    grad_ff = lax.psum_scatter(grad_ff, "mp", scatter_dimension=2, tiled=True).astype(F32)
    grad_attn = jnp.concatenate([grad_qkv[0], grads[0, :, 2 * ff :]], axis=1)
    grad_attn = lax.psum_scatter(grad_attn, "dp", scatter_dimension=0, tiled=True)
    grad_attn = lax.psum(grad_attn, "mp").astype(F32)
    sums = lax.psum(sums, ("dp", "mp"))
    sums = lax.dynamic_slice_in_dim(sums, lax.axis_index("dp") * own, own, axis=1)
    return (
        layer_out, input_grad, grad_attn[:, : 3 * width], grad_attn[:, 3 * width :],
        grad_ff[:, 0], grad_ff[:, 1], sums[0:3], sums[3], sums[4], sums[5], sums[6],
    )


def on_device(
    tokens, segment_ids, valid_len, qkv_weight, out_weight, up_weight, down_weight, conv_weight,
    ln1_gain, ln1_shift, ln2_gain, ln2_shift, cotangent,
):
    own, ffs = up_weight.shape
    direct = own % 16 == 0 and ffs == tokens.shape[2] and own <= VECTORS and lax.axis_size("mp") == 4
    plan = direct_plan if direct else gathered_plan
    return plan(
        tokens, segment_ids, valid_len, qkv_weight, out_weight, up_weight, down_weight, conv_weight,
        (ln1_gain, ln1_shift, ln2_gain, ln2_shift), cotangent,
    )


def solution(mesh):
    rows = P(("dp", "mp"), None, None)
    weights = (P("dp", None), P("dp", None), P("dp", "mp"), P("dp", "mp"), P(None, "dp"))
    vectors = (P("dp"),) * 4
    return jax.shard_map(
        on_device,
        mesh=mesh,
        in_specs=(rows, P(("dp", "mp"), None), P(("dp", "mp"))) + weights + vectors + (rows,),
        out_specs=(rows, rows) + weights + vectors,
        check_vma=False,
    )
```

```python
import functools
import math

import jax
import jax.numpy as jnp
from jax import lax
from jax.experimental import pallas as pl
from jax.experimental.pallas import tpu as pltpu
from jax.sharding import PartitionSpec as P

HEADS = 6
VECTORS = 128
LANES = 128
BF = jnp.bfloat16
F32 = jnp.float32
MIB = 1024 * 1024
VMEM_LIMITS = dict(forward_attention=26, feed_forward=43, backward=36, layer_output=24)


def mm(lhs, rhs):
    return lax.dot_general(lhs, rhs, (((1,), (0,)), ((), ())), preferred_element_type=F32)


def mm_nt(lhs, rhs):
    return lax.dot_general(lhs, rhs, (((1,), (1,)), ((), ())), preferred_element_type=F32)


def tree_sum(items):
    items = list(items)
    while len(items) > 1:
        items = [a + b for a, b in zip(items[::2], items[1::2])]
    return items[0]


def pack_weights(qkv_ref, up_ref, down_ref, conv_ref, g1_ref, s1_ref, g2_ref, s2_ref, narrow_ref, ff_ref, rows_ref):
    own, ffs = up_ref.shape
    rows_ref[...] = jnp.zeros_like(rows_ref)
    rows_ref[0:3, :own] = conv_ref[...].astype(F32)
    for i, ref in enumerate((g1_ref, s1_ref, g2_ref, s2_ref)):
        rows_ref[3 + i : 4 + i, :own] = ref[...].astype(F32)
    wide = qkv_ref.shape[1]
    narrow_ref[:, :wide] = qkv_ref[...]
    narrow_ref[:, wide:] = rows_ref[...].T[:own].astype(BF)
    ff_ref[:own] = up_ref[...]
    ff_ref[own:] = down_ref[...]


def tiles(total, size):
    return [slice(at, at + size) for at in range(0, total, size)]


def weave(*strands):
    strands = [strand for strand in strands if strand]
    total = sum(len(strand) for strand in strands)
    pieces = [((i + 0.5) / len(strand), j, piece) for j, strand in enumerate(strands) for i, piece in enumerate(strand)]
    assert len(pieces) == total
    for _, _, piece in sorted(pieces, key=lambda item: item[:2]):
        piece()


def twice(tile, lanes):
    return jnp.concatenate([tile] * (lanes // LANES), axis=1)


def load_columns(packed_ref, col_ref, places):
    for i, place in enumerate(places):
        column = packed_ref[:, place : place + 1].astype(F32)
        col_ref[i] = jnp.broadcast_to(column, (column.shape[0], LANES))


def column_mean(values):
    return jnp.sum(values, axis=0, keepdims=True) * (1.0 / values.shape[0])


def norm_columns(values):
    centred = values - column_mean(values)
    scale = lax.rsqrt(column_mean(centred * centred) + 1e-06)
    return centred * scale, scale


def fold(values):
    rows, lanes = values.shape
    return jnp.sum(values.reshape(rows // 8, 8, lanes), axis=0)


def fold_lanes(values):
    return sum(values[:, t] for t in tiles(values.shape[1], LANES))


def forward_attention(index_ref, len_ref, tok_ref, seg_ref, *refs, pieces):
    piece_refs = refs[:pieces]
    (
        five_ref, mc_ref, v_ref, e_ref, facts_ref, packed_ref, w_ref,
        wt_ref, wide_ref, col_ref, bias_ref, key_ref, value_ref,
    ) = refs[pieces:]
    x_ref, norm_ref, q_ref, k_ref, att_ref = [five_ref.at[:, i] for i in range(5)]
    aux_ref, inv_ref = facts_ref.at[:, :8], facts_ref.at[:, 8:]
    rows, seq, width = tok_ref.shape
    head = width // HEADS
    step = pl.program_id(0)

    @pl.when(step == 0)
    def _():
        own = width // pieces
        for i, ref in enumerate(piece_refs):
            wide_ref[pl.ds(pl.multiple_of(index_ref[i] * own, 16), own), :] = ref[...]
        w_ref[...] = wide_ref[:, : 3 * width]
        wt_ref[:width] = (wide_ref[:, :width].astype(F32) * head ** (-0.5)).astype(BF).T
        wt_ref[width:] = wide_ref[:, width : 3 * width].T
        packed_ref[...] = wide_ref[:, 3 * width :]
        load_columns(packed_ref, col_ref, range(5))

    place = lax.broadcasted_iota(jnp.int32, (1, seq), 1)
    zero = jnp.zeros((head, seq), BF)

    def preparation(r):
        known = {}

        def start():
            segs = seg_ref[pl.ds(step * rows + r, 1), :].astype(F32)
            valid = place < len_ref[step * rows + r]
            number = jnp.where(valid, segs, -1.0)
            links = jnp.where(valid & (place > 0) & (number == pltpu.roll(number, 1, 1)), 1.0, 0.0)
            next_links = jnp.where(place < seq - 1, pltpu.roll(links, seq - 1, 1), 0.0)
            none = jnp.zeros_like(links)
            aux = jnp.concatenate([links, next_links, number, none, none, none, none, none], axis=0)
            aux_ref[r] = aux
            x_ref[r] = tok_ref[r].T
            known.update(segs=segs, links=links, next_links=next_links, key_number=aux.T[:, 2:3])

        def mask(t):
            row_id = lax.broadcasted_iota(jnp.int32, (64, seq), 0) + t.start
            col_id = lax.broadcasted_iota(jnp.int32, (64, seq), 1)
            allowed = (known["key_number"][t] == known["segs"]) | (row_id == col_id)
            bias_ref[r, t] = jnp.where(allowed, 0.0, -1e30)

        def conv(t):
            base = x_ref[r, t].astype(F32)
            before = pltpu.roll(base, 1, 1) * known["links"]
            after = pltpu.roll(base, seq - 1, 1) * known["next_links"]
            conv0, conv1, conv2 = [twice(col_ref[i, t], seq) for i in range(3)]
            mc_ref[r, t] = base + before * conv0 + base * conv1 + after * conv2

        def norm(t):
            n, _ = norm_columns(mc_ref[r, :, t])
            norm_ref[r, :, t] = (n * col_ref[3] + col_ref[4]).astype(BF)

        pieces = [start] + [functools.partial(conv, t) for t in tiles(width, 32)]
        pieces += [functools.partial(norm, t) for t in tiles(seq, LANES)]
        return pieces + [functools.partial(mask, t) for t in tiles(seq, 64)]

    def project():
        normed = jnp.concatenate([norm_ref[r] for r in range(rows)], axis=1)
        for i, ref in enumerate((q_ref, k_ref, value_ref)):
            part = mm(wt_ref[i * width : (i + 1) * width], normed).astype(BF)
            for r in range(rows):
                ref[r] = part[:, r * seq : (r + 1) * seq]
        for r in range(rows):
            key_ref[r] = k_ref[r].T
            v_ref[r] = value_ref[r].T

    def scores(r, p):
        low, high = [q_ref[r, h * head : (h + 1) * head] for h in (2 * p, 2 * p + 1)]
        both = jnp.concatenate([jnp.concatenate([low, zero], axis=1), jnp.concatenate([zero, high], axis=1)], axis=0)
        return mm(key_ref[r, :, 2 * p * head : 2 * (p + 1) * head], both)

    def attended(r, p):
        both = jnp.concatenate([e_ref[r, 2 * p], e_ref[r, 2 * p + 1]], axis=1)
        product = mm(value_ref[r, 2 * p * head : 2 * (p + 1) * head], both)
        parts = []
        for i in range(2):
            att = product[i * head : (i + 1) * head, i * seq : (i + 1) * seq] * inv_ref[r, 2 * p + i : 2 * p + i + 1]
            parts.append(att.astype(BF))
        return jnp.concatenate(parts, axis=0)

    def soften(r, p, product):
        for i in range(2):
            for t in tiles(seq, LANES):
                masked = product[:, i * seq + t.start : i * seq + t.stop] + bias_ref[r, :, t]
                raised = jnp.exp(masked - jnp.max(masked, axis=0, keepdims=True))
                inv_ref[r, 2 * p + i : 2 * p + i + 1, t] = 1.0 / jnp.sum(raised, axis=0, keepdims=True)
                e_ref[r, 2 * p + i, :, t] = raised.astype(BF)

    weave(*[preparation(r) for r in range(rows)])
    project()
    work = [(r, p) for r in range(rows) for p in range(HEADS // 2)]
    current, last = scores(*work[0]), None
    for at, (r, p) in enumerate(work):
        following = scores(*work[at + 1]) if at + 1 < len(work) else None
        finished = attended(*last) if last else None
        soften(r, p, current)
        if last:
            att_ref[last[0], 2 * last[1] * head : 2 * (last[1] + 1) * head] = finished
        current, last = following, (r, p)
    att_ref[last[0], 2 * last[1] * head : 2 * (last[1] + 1) * head] = attended(*last)


def gelu_parts(x):
    cdf = 0.5 * lax.erf(x * math.sqrt(0.5)) + 0.5
    bell = jnp.exp2(x * x * (-0.5 / math.log(2.0)) - 0.5 * math.log2(2.0 * math.pi))
    return x * cdf, cdf + x * bell


def feed_forward(index_ref, five_ref, mc_ref, ct_ref, packed_ref, *refs, pieces, shards):
    att_ref = five_ref.at[:, 0]
    piece_refs = refs[:pieces]
    groups = 2 if pieces > 1 else 1
    hidden_out, mixed_out, gm_ref, ga_ref, gs_ref, down_ref = refs[pieces : pieces + 6]
    hidden_ref, mixed_ref = hidden_out.at[0], mixed_out.at[0]
    gw_refs = refs[pieces + 6 : pieces + 6 + groups]
    (
        up_ref, upt_ref, downt_ref, out_ref, outt_ref, up_acc, down_acc, out_acc, col_acc, col_ref,
        att_cat, n_ref, norm_ref, ctt_ref, gp_ref, gn_ref, scale_ref, branch_ref,
    ) = refs[pieces + 6 + groups :]
    rows, seq, width = ct_ref.shape
    ff = up_ref.shape[1]
    ffs = ff // shards
    own = width // pieces
    step = pl.program_id(0)

    @pl.when(step == 0)
    def _():
        for acc in (up_acc, down_acc, out_acc, col_acc):
            acc[...] = jnp.zeros_like(acc)
        for i, ref in enumerate(piece_refs):
            here = pl.ds(pl.multiple_of(index_ref[i] * own, 16), own)
            for j in range(shards):
                up_ref[here, j * ffs : (j + 1) * ffs] = ref[2 * j * own : (2 * j + 1) * own]
                down_ref[here, j * ffs : (j + 1) * ffs] = ref[(2 * j + 1) * own : (2 * j + 2) * own]
            out_ref[here, :] = ref[2 * shards * own :]
        upt_ref[...] = up_ref[...].T
        downt_ref[...] = down_ref[...].T
        outt_ref[...] = out_ref[...].T
        load_columns(packed_ref, col_ref, (5, 6))

    def lanes_of(r):
        return slice(r * seq, (r + 1) * seq)

    def spots_of(r):
        return [slice(at, at + LANES) for at in range(r * seq, (r + 1) * seq, LANES)]

    def preparation(r):
        lanes = lanes_of(r)

        def turn():
            ctt_ref[:, lanes] = ct_ref[r].T
            att_cat[:, lanes] = att_ref[r]

        def branch():
            mixed_ref[:, lanes] = mc_ref[r] + mm(outt_ref[...], att_ref[r])

        def norm(t):
            n, scale = norm_columns(mixed_ref[:, t])
            n_ref[:, t] = n
            scale_ref[0:1, t] = scale
            norm_ref[:, t] = (n * col_ref[0] + col_ref[1]).astype(BF)

        return [turn, branch] + [functools.partial(norm, t) for t in spots_of(r)]

    def activation(block):
        pre = mm(upt_ref[block], norm_ref[...])
        grad_hidden = mm(downt_ref[block], ctt_ref[...])
        for low in range(0, block.stop - block.start, 16):
            part = slice(low, low + 16)
            here = slice(block.start + low, block.start + low + 16)
            hidden, slope = gelu_parts(pre[part])
            hidden_ref[here] = hidden.astype(BF)
            gp_ref[here] = (grad_hidden[part] * slope).astype(BF)

    def norm_back(r):
        spots = spots_of(r)
        mean_e = [jnp.zeros((8, LANES), F32) for _ in spots]
        mean_en = [jnp.zeros((8, LANES), F32) for _ in spots]
        means = []

        def sums(d):
            column = col_ref[0, d]
            gain_sum, shift_sum = col_acc[0, d], col_acc[1, d]
            for i, t in enumerate(spots):
                grad_n = gn_ref[d, t]
                product = grad_n * n_ref[d, t]
                gain_sum += product
                shift_sum += grad_n
                mean_e[i] += fold(grad_n * column)
                mean_en[i] += fold(product * column)
            col_acc[0, d] = gain_sum
            col_acc[1, d] = shift_sum

        def finish():
            for i in range(len(spots)):
                me = jnp.sum(mean_e[i], axis=0, keepdims=True) * (1.0 / width)
                men = jnp.sum(mean_en[i], axis=0, keepdims=True) * (1.0 / width)
                means.append((me, men))

        def apply(d):
            for i, t in enumerate(spots):
                me, men = means[i]
                change = scale_ref[0:1, t] * (gn_ref[d, t] * col_ref[0, d] - me - n_ref[d, t] * men)
                grad_mixed = ctt_ref[d, t].astype(F32) + change
                gm_ref[r, d, i * LANES : (i + 1) * LANES] = grad_mixed
                branch_ref[d, t] = grad_mixed.astype(BF)

        def attended():
            ga_ref[r] = mm(out_ref[...], branch_ref[:, lanes_of(r)]).astype(BF)

        pieces = [functools.partial(sums, d) for d in tiles(width, 32)] + [finish]
        return pieces + [functools.partial(apply, d) for d in tiles(width, 32)] + [attended]

    weave(*[preparation(r) for r in range(rows)])
    for block in tiles(ff, 128):
        activation(block)
    gn_ref[...] = mm(up_ref[...], gp_ref[...])
    down_acc[...] += mm_nt(ctt_ref[...], hidden_ref[...])
    up_acc[...] += mm_nt(norm_ref[...], gp_ref[...])
    weave(*[norm_back(r) for r in range(rows)])
    out_acc[...] += mm_nt(att_cat[...], branch_ref[...])

    @pl.when(step == pl.num_programs(0) - 1)
    def _():
        for i in range(pieces):
            here = pl.ds(pl.multiple_of(index_ref[i] * own, 16), own)
            place = gw_refs[i % groups]
            for j in range(shards):
                cols = slice(j * ffs, (j + 1) * ffs)
                place[i // groups, :, 2 * j * ffs : (2 * j + 1) * ffs] = up_acc[here, cols].astype(BF)
                place[i // groups, :, (2 * j + 1) * ffs : (2 * j + 2) * ffs] = down_acc[here, cols].astype(BF)
            place[i // groups, :, 2 * ff :] = out_acc[here, :].astype(BF)
        gs_ref[...] = jnp.zeros_like(gs_ref)
        for i in range(2):
            gs_ref[5 + i : 6 + i] = jnp.sum(col_acc[i].T, axis=0, keepdims=True)


def layer_output(hidden_ref, mixed_ref, down_ref, lo_ref):
    rows, seq, _ = lo_ref.shape
    total = (mixed_ref[0] + mm(down_ref[...], hidden_ref[0])).astype(BF)
    for r in range(rows):
        lo_ref[r] = total[:, r * seq : (r + 1) * seq].T


def backward(
    five_ref, mc_ref, v_ref, e_ref, facts_ref, ga_ref, gm_ref, index_ref, w_ref, packed_ref, other_ref, ig_ref, gs_ref, *refs, pieces,
):
    x_ref, norm_ref, q_ref, k_ref, att_ref = [five_ref.at[:, i] for i in range(5)]
    aux_ref, inv_ref = facts_ref.at[:, :8], facts_ref.at[:, 8:]
    gw_refs = refs[:-11]
    (
        proj_ref, w_acc, norm_cat, soft_ref, logit_ref, gn_ref, acc_ref, col_ref, n_ref, g_ref, turn_ref
    ) = refs[-11:]
    rows, seq, width = v_ref.shape
    own = width // pieces
    head = width // HEADS
    step = pl.program_id(0)

    @pl.when(step == 0)
    def _():
        w_acc[...] = jnp.zeros_like(w_acc)
        acc_ref[...] = jnp.zeros_like(acc_ref)
        load_columns(packed_ref, col_ref, range(4))

    zero = jnp.zeros((head, seq), BF)
    work = [(r, p) for r in range(rows) for p in range(HEADS // 2)]

    def opening(r, p):
        grads, inners = [], []
        for h in (2 * p, 2 * p + 1):
            part = slice(h * head, (h + 1) * head)
            grad_att = ga_ref[r, part].astype(F32) * inv_ref[r, h : h + 1]
            inners.append(jnp.sum(grad_att * att_ref[r, part].astype(F32), axis=0, keepdims=True))
            grads.append(grad_att.astype(BF))
        low, high = grads
        both = jnp.concatenate([jnp.concatenate([low, zero], axis=1), jnp.concatenate([zero, high], axis=1)], axis=0)
        product = mm(v_ref[r, :, 2 * p * head : 2 * (p + 1) * head], both)
        soft_ref[r, 2 * p] = product[:, :seq]
        soft_ref[r, 2 * p + 1] = product[:, seq:]
        return jnp.concatenate(grads, axis=0), inners

    ready = opening(*work[0])
    for at, (r, p) in enumerate(work):
        grad_att, inners = ready
        if at + 1 < len(work):
            ready = opening(*work[at + 1])
        for i, h in enumerate((2 * p, 2 * p + 1)):
            for t in tiles(seq, 32):
                raised = e_ref[r, h, t].astype(F32)
                logit_ref[r, h, t] = (raised * (soft_ref[r, h, t] - inners[i])).astype(BF)
        part = slice(2 * p * head, 2 * (p + 1) * head)
        pair = slice(2 * p, 2 * p + 2)
        beside = jnp.concatenate([logit_ref[r, 2 * p], logit_ref[r, 2 * p + 1]], axis=1)
        grad_q = mm(k_ref[r, part], beside)
        grad_k = mm_nt(q_ref[r, part], logit_ref[r, pair].reshape(2 * seq, seq))
        grad_v = mm_nt(grad_att, e_ref[r, pair].reshape(2 * seq, seq))
        for i in range(2):
            place = slice(r * seq, (r + 1) * seq)
            own_rows, own_cols = slice(i * head, (i + 1) * head), slice(i * seq, (i + 1) * seq)
            for j, grad in enumerate((grad_q, grad_k, grad_v)):
                first = j * width + (2 * p + i) * head
                mine = grad[own_rows, own_cols]
                proj_ref[first : first + head, place] = (mine * head ** (-0.5) if j == 0 else mine).astype(BF)
    gn_ref[...] = mm(w_ref[...], proj_ref[...])
    for r in range(rows):
        norm_cat[:, r * seq : (r + 1) * seq] = norm_ref[r]
    w_acc[...] += mm_nt(norm_cat[...], proj_ref[...])

    spots = tiles(seq, LANES)
    for r in range(rows):
        wide = [slice(r * seq + t.start, r * seq + t.stop) for t in spots]
        scales = []
        for t in spots:
            n, scale = norm_columns(mc_ref[r, :, t])
            n_ref[r, :, t] = n
            scales.append(scale)
        mean_e = [jnp.zeros((8, LANES), F32) for _ in spots]
        mean_en = [jnp.zeros((8, LANES), F32) for _ in spots]
        for d in tiles(width, 32):
            column = col_ref[3, d]
            gain_sum, shift_sum = acc_ref[3, d], acc_ref[4, d]
            for i, t in enumerate(spots):
                grad_n = gn_ref[d, wide[i]]
                product = grad_n * n_ref[r, d, t]
                gain_sum += product
                shift_sum += grad_n
                mean_e[i] += fold(grad_n * column)
                mean_en[i] += fold(product * column)
            acc_ref[3, d] = gain_sum
            acc_ref[4, d] = shift_sum
        for i, t in enumerate(spots):
            me = jnp.sum(mean_e[i], axis=0, keepdims=True) * (1.0 / width)
            men = jnp.sum(mean_en[i], axis=0, keepdims=True) * (1.0 / width)
            for d in tiles(width, 64):
                e = gn_ref[d, wide[i]] * col_ref[3, d]
                g_ref[r, d, t] = gm_ref[r, d, t] + scales[i] * (e - me - n_ref[r, d, t] * men)
        links, next_links = aux_ref[r, 0:1], aux_ref[r, 1:2]
        for d in tiles(width, 32):
            g = g_ref[r, d]
            base = x_ref[r, d].astype(F32)
            before = pltpu.roll(g, 1, 1) * links
            after = pltpu.roll(g, seq - 1, 1) * next_links
            acc_ref[0, d] += fold_lanes(base * after)
            acc_ref[1, d] += fold_lanes(base * g)
            acc_ref[2, d] += fold_lanes(base * before)
            conv0, conv1, conv2 = [twice(col_ref[i, d], seq) for i in range(3)]
            turn_ref[r, d] = (g + conv1 * g + conv0 * after + conv2 * before).astype(BF)
        ig_ref[r] = turn_ref[r].T

    @pl.when(step == pl.num_programs(0) - 1)
    def _():
        gs_ref[...] = other_ref[...]
        for i in range(5):
            gs_ref[i : i + 1] += jnp.sum(acc_ref[i].T, axis=0, keepdims=True)
        groups = len(gw_refs)
        for i in range(pieces):
            here = pl.ds(pl.multiple_of(index_ref[i] * own, 16), own)
            gw_refs[i % groups][i // groups] = w_acc[here, :].astype(BF)


def in_hbm(values):
    return pltpu.with_memory_space_constraint(values, pltpu.HBM)


def by_row(shape, rows, first=0):
    tail = tuple(shape[1:])
    return pl.BlockSpec((rows,) + tail, lambda i, *_: (i + first,) + (0,) * len(tail))


def whole(shape):
    place = (0,) * len(shape)
    return pl.BlockSpec(tuple(shape), lambda i, *_: place, pipeline_mode=pl.Buffered(1))


def step_rows(count, most):
    return max(r for r in range(1, most + 1) if count % r == 0)


def call(body, name, scalars, rows, row_args, args, row_outs, outs, scratch, span=None, into=None, near=(), only=None):
    first, count = span or (0, row_args[0].shape[0])
    skip = first // rows
    total = row_args[0].shape[0]

    def spec_of(shape):
        return by_row(shape, shape[0] * rows // total, skip)

    in_specs = [spec_of(a.shape) for a in row_args]
    if only:
        tail = row_args[0].shape[2:]
        in_specs[0] = pl.BlockSpec((rows, 1) + tail, lambda i, *_: (i, only) + (0,) * len(tail))
    in_specs += [whole(a.shape) for a in args]
    aliases = {}
    if into is not None:
        in_specs.append(pl.BlockSpec(memory_space=pl.ANY))
        aliases = {len(scalars) + len(in_specs) - 1: 0}
    spec = pltpu.PrefetchScalarGridSpec(
        num_scalar_prefetch=len(scalars),
        grid=(count // rows,),
        in_specs=in_specs,
        out_specs=[spec_of(s) for s, _ in row_outs] + [whole(s) for s, _ in outs],
        scratch_shapes=[pltpu.VMEM(s, t) for s, t in scratch],
    )
    return pl.pallas_call(
        body,
        grid_spec=spec,
        out_shape=[(jax.ShapeDtypeStruct if "out" + str(i) in near else pltpu.HBM)(s, t) for i, (s, t) in enumerate(row_outs)]
        + [jax.ShapeDtypeStruct(s, t) for s, t in outs],
        input_output_aliases=aliases,
        compiler_params=pltpu.CompilerParams(dimension_semantics=("arbitrary",), vmem_limit_bytes=VMEM_LIMITS[name] * MIB),
        name=name,
    )(*scalars, *[a if i in near else in_hbm(a) for i, a in enumerate(row_args)], *args, *(() if into is None else (into,)))


def small_call(body, name, args, outs, scratch=()):
    return pl.pallas_call(
        body,
        out_shape=[jax.ShapeDtypeStruct(s, t) for s, t in outs],
        scratch_shapes=[pltpu.VMEM(s, t) for s, t in scratch],
        compiler_params=pltpu.CompilerParams(vmem_limit_bytes=16 * MIB),
        name=name,
    )(*args)


def run_forward(index, tokens, segment_ids, valid_len, pieces):
    count, seq, width = tokens.shape
    flipped = (count, width, seq)
    rows = step_rows(count, 2)
    row_outs = [
        ((count, 5, width, seq), BF), (flipped, F32), ((count, seq, width), BF),
        ((count, HEADS, seq, seq), BF), ((count, 16, seq), F32),
    ]
    return call(
        functools.partial(forward_attention, pieces=len(pieces)), "forward_attention", (index, in_hbm(valid_len)),
        rows, (tokens,), (in_hbm(segment_ids), *pieces),
        row_outs, [((width, VECTORS), BF), ((width, 3 * width), BF)],
        [
            ((3 * width, width), BF), ((width, 3 * width + VECTORS), BF), ((5, width, LANES), F32),
            ((rows, seq, seq), F32), ((rows, seq, width), BF), ((rows, width, seq), BF),
        ],
    )


def run_feed_forward(index, five, mixed, cotangent, packed, pieces, shards):
    count, seq, width = cotangent.shape
    own = width // len(pieces)
    ff = shards * width
    groups = 2 if len(pieces) > 1 else 1
    rows = step_rows(count, 4)
    wide = rows * seq
    row_outs = [
        ((count // rows, ff, wide), BF), ((count // rows, width, wide), F32),
        ((count, width, seq), F32), ((count, width, seq), BF),
    ]
    grads = ((len(pieces) // groups, own, 2 * ff + width), BF)
    return call(
        functools.partial(feed_forward, pieces=len(pieces), shards=shards), "feed_forward", (index,),
        rows, (five, mixed, cotangent), (packed, *pieces),
        row_outs, [((8, width), F32), ((width, ff), BF)] + [grads] * groups,
        [((width, ff), BF)] + [((ff, width), BF)] * 2 + [((width, width), BF)] * 2
        + [((width, ff), F32)] * 2 + [((width, width), F32), ((2, width, LANES), F32), ((2, width, LANES), F32)]
        + [((width, wide), BF), ((width, wide), F32), ((width, wide), BF), ((width, wide), BF)]
        + [((ff, wide), BF)]
        + [((width, wide), F32), ((8, wide), F32), ((width, wide), BF)],
        near=("out3",), only=4,
    )


def run_layer_output(hidden, mixed, down, shape, part, parts, into):
    steps = hidden.shape[0]
    span = (part * steps // parts, (part + 1) * steps // parts - part * steps // parts)

    def body(*refs):
        layer_output(*refs[:3], refs[-1])

    return call(body, "layer_output", (), 1, (hidden, mixed), (down,), [(shape, BF)], [], [], span=span, into=into)[0]


def run_backward(index, weight, kept, grads, packed, other, pieces):
    count, seq, width = kept[2].shape
    own = width // pieces
    groups = 2 if pieces > 1 else 1
    rows = step_rows(count, 2)
    row_args = (*kept, *grads)
    many = len(row_args)

    def body(index_ref, *refs):
        backward(*refs[:many], index_ref, *refs[many:], pieces=pieces)

    return call(
        body, "backward", (index,), rows, row_args, (weight, packed, other),
        [((count, seq, width), BF)], [((8, width), F32)] + [((pieces // groups, own, 3 * width), BF)] * groups,
        [
            ((3 * width, rows * seq), BF), ((width, 3 * width), F32), ((width, rows * seq), BF),
            ((rows, HEADS, seq, seq), F32), ((rows, HEADS, seq, seq), BF), ((width, rows * seq), F32),
            ((5, width, LANES), F32), ((4, width, LANES), F32), ((rows, width, seq), F32), ((rows, width, seq), F32),
            ((rows, width, seq), BF),
        ],
        near=(5,),
    )


def exchange(values, axis, offset):
    size = lax.axis_size(axis)
    return lax.ppermute(values, axis, [(i, i ^ offset) for i in range(size)])


def add_halves(mine, received):
    count, own, cols = mine.shape

    def body(mine_ref, received_ref, *out_refs):
        for i, ref in enumerate(out_refs):
            ref[...] = (mine_ref[i].astype(F32) + received_ref[i].astype(F32)).astype(BF)

    return small_call(body, "add_halves", (mine, received), [((own, cols), BF)] * count)


def add_wide(*items):
    return tree_sum(item.astype(F32) for item in items)


def store_high_low(ref, cols, values):
    high = values.astype(BF)
    low = (values - high.astype(F32)).astype(BF)
    ref[:, cols:] = jnp.concatenate([high, low, jnp.zeros((ref.shape[0] - 16, LANES), BF)], axis=0)


def load_high_low(ref, cols):
    both = ref[:16, cols:].astype(F32)
    return both[:8] + both[8:]


def add_halves_and_sums(index, mine, received, sums, received_sums):
    count, own, cols = mine.shape
    width = sums.shape[1]

    def body(index_ref, mine_ref, received_ref, sums_ref, received_sums_ref, *out_refs):
        total = sums_ref[...] + received_sums_ref[...]
        for i, ref in enumerate(out_refs):
            ref[:, :cols] = (mine_ref[i].astype(F32) + received_ref[i].astype(F32)).astype(BF)
            turned = pltpu.roll(total, lax.rem(width - index_ref[2 * i] * own, width), 1)[:, :LANES]
            store_high_low(ref, cols, turned)

    spec = pltpu.PrefetchScalarGridSpec(
        num_scalar_prefetch=1, grid=(1,),
        in_specs=[whole(a.shape) for a in (mine, received, sums, received_sums)],
        out_specs=[whole((own, cols + LANES))] * count,
    )
    return pl.pallas_call(
        body, grid_spec=spec, out_shape=[jax.ShapeDtypeStruct((own, cols + LANES), BF)] * count,
        compiler_params=pltpu.CompilerParams(vmem_limit_bytes=16 * MIB), name="add_halves_and_sums",
    )(index, mine, received, sums, received_sums)


def add_packed(name, items):
    cols = items[0].shape[1] - LANES

    def body(*refs):
        out_ref = refs[-1]
        out_ref[:, :cols] = tree_sum(ref[:, :cols].astype(F32) for ref in refs[:-1]).astype(BF)
        store_high_low(out_ref, cols, tree_sum(load_high_low(ref, cols) for ref in refs[:-1]))

    return small_call(body, name, items, [(items[0].shape, BF)])[0]


def add_last(items):
    own, cols = items[0].shape[0], items[0].shape[1] - LANES

    def body(*refs):
        ins, outs = refs[: len(items)], refs[len(items) :]
        outs[0][...] = tree_sum(ref[:, :cols].astype(F32) for ref in ins)
        vectors = tree_sum(load_high_low(ref, cols) for ref in ins)
        outs[1][...] = vectors[0:3, :own]
        for i in range(4):
            outs[2 + i][...] = vectors[3 + i : 4 + i, :own]

    return small_call(body, "add_last", items, [((own, cols), F32), ((3, own), F32)] + [((1, own), F32)] * 4)


def direct_plan(tokens, segment_ids, valid_len, qkv_weight, out_weight, up_weight, down_weight, conv_weight, vectors, cotangent):
    count, seq, width = tokens.shape
    own, ffs = up_weight.shape
    dp, mp = lax.axis_size("dp"), lax.axis_size("mp")
    me = lax.axis_index("dp")
    offsets = [2 * p for p in range(dp // 2)]
    index = jnp.stack([me ^ (p ^ c) for p in offsets for c in range(2)]).astype(jnp.int32)
    narrow, ff_own = small_call(
        pack_weights, "pack_weights",
        [in_hbm(a) for a in (qkv_weight, up_weight, down_weight, conv_weight, *[v.reshape(1, own) for v in vectors])],
        [((own, 3 * width + VECTORS), BF), ((2 * own, ffs), BF)], [((VECTORS, VECTORS), F32)],
    )
    plane = [narrow] + [exchange(narrow, "dp", p) for p in offsets[1:]]
    shards = [ff_own] + [exchange(ff_own, "mp", j) for j in range(1, mp)]
    pieces = [piece for a in plane for piece in (a, exchange(a, "dp", 1))]
    column = jnp.concatenate(shards + [out_weight], axis=0)
    columns = [column] + [exchange(column, "dp", p) for p in offsets[1:]]
    five, mixed, v, raised, facts, packed, weight = run_forward(
        index, tokens, segment_ids, valid_len, pieces
    )
    columns, five = lax.optimization_barrier((columns, five))
    pieces = [piece for a in columns for piece in (a, exchange(a, "dp", 1))]
    hidden, mixed_attn, grad_mixed, grad_att, sums2, down, mine, theirs = run_feed_forward(
        index, five, mixed, cotangent, packed, pieces, mp
    )
    received = exchange(theirs, "dp", 1)
    shape = cotangent.shape
    layer_out = run_layer_output(hidden, mixed_attn, down, shape, 0, 3, None)
    received, layer_out = lax.optimization_barrier((received, layer_out))
    parts = list(add_halves(mine, received))
    parts[0], grad_att = lax.optimization_barrier((parts[0], grad_att))
    plane = [parts[0]] + [exchange(parts[i], "dp", p) for i, p in enumerate(offsets) if i]
    kept = (five, mixed, v, raised, facts)
    input_grad, sums, mine_a, theirs_a = run_backward(
        index, weight, kept, (grad_att, grad_mixed), packed, sums2, dp
    )
    plane, theirs_a, sums = lax.optimization_barrier((plane, theirs_a, sums))
    received_a = exchange(theirs_a, "dp", 1)
    received_s = exchange(sums, "dp", 1)
    total = add_wide(*plane).astype(BF)
    part = 2 * ffs
    near = jnp.concatenate([total[:, :part], total[:, 2 * part : 3 * part]], axis=1)
    out_part = total[:, 4 * part :]
    far = jnp.concatenate([total[:, part : 2 * part], total[:, 3 * part :]], axis=1)
    parts = list(add_halves_and_sums(index, mine_a, received_a, sums, received_s))
    parts[0], far, hidden, layer_out = lax.optimization_barrier((parts[0], far, hidden, layer_out))
    plane_a = [parts[0]] + [exchange(parts[i], "dp", p) for i, p in enumerate(offsets) if i]
    received_f = exchange(far, "mp", 1)
    layer_out = run_layer_output(hidden, mixed_attn, down, shape, 1, 3, layer_out)
    plane_a, layer_out = lax.optimization_barrier((plane_a, layer_out))
    total = add_packed("add_plane", plane_a)
    received_1 = exchange(total, "mp", 2)
    layer_out, _ = lax.optimization_barrier((layer_out, total))
    layer_out = run_layer_output(hidden, mixed_attn, down, shape, 2, 3, layer_out)
    received_1, received_f, layer_out = lax.optimization_barrier((received_1, received_f, layer_out))
    near_sum = add_wide(near, received_f[:, : 2 * part])
    out_sum = lax.optimization_barrier(add_wide(out_part, received_f[:, 2 * part :]).astype(BF))
    keep = near_sum[:, :part]
    send = jnp.concatenate([near_sum[:, part:].astype(BF), out_sum], axis=1)
    received_n = exchange(send, "mp", 2)
    total = add_packed("add_far", (total, received_1))
    received_2 = exchange(total, "mp", 1)
    grad_up = keep[:, :ffs] + received_n[:, :ffs].astype(F32)
    grad_down = keep[:, ffs:] + received_n[:, ffs : 2 * ffs].astype(F32)
    grad_out = add_wide(out_sum, received_n[:, 2 * ffs :])
    grad_qkv, grad_conv, *grads = add_last((total, received_2))
    return (layer_out, input_grad, grad_qkv, grad_out, grad_up, grad_down, grad_conv, *[g.reshape(own) for g in grads])


def gathered_plan(tokens, segment_ids, valid_len, qkv_weight, out_weight, up_weight, down_weight, conv_weight, vectors, cotangent):
    count, seq, width = tokens.shape
    own = qkv_weight.shape[0]
    dp = width // own
    columns = jnp.stack([conv_weight[0], conv_weight[1], conv_weight[2], *vectors], axis=1)
    narrow = jnp.concatenate([qkv_weight, jnp.pad(columns, ((0, 0), (0, VECTORS - 7))), out_weight], axis=1)
    wide = lax.all_gather(narrow, "dp", axis=0, tiled=True)
    both = lax.all_gather(jnp.concatenate([up_weight, down_weight], axis=0), "mp", axis=1, tiled=True)
    ff = both.shape[1]
    shards = ff // width
    both = lax.all_gather(both, "dp", axis=0).reshape(dp, 2, own, shards, width)
    both = both.transpose(3, 1, 0, 2, 4).reshape(2 * ff, width)
    column = jnp.concatenate([both, wide[:, 3 * width + VECTORS :]], axis=0)
    index = jnp.zeros((1,), jnp.int32)
    five, mixed, v, raised, facts, packed, weight = run_forward(
        index, tokens, segment_ids, valid_len, [wide[:, : 3 * width + VECTORS]]
    )
    hidden, mixed_attn, grad_mixed, grad_att, sums2, down, grads = run_feed_forward(
        index, five, mixed, cotangent, packed, [column], shards
    )
    kept = (five, mixed, v, raised, facts)
    layer_out = run_layer_output(hidden, mixed_attn, down, cotangent.shape, 0, 1, None)
    input_grad, sums, grad_qkv = run_backward(index, weight, kept, (grad_att, grad_mixed), packed, sums2, 1)
    grad_ff = grads[0, :, : 2 * ff].reshape(width, shards, 2, width).transpose(0, 2, 1, 3).reshape(width, 2 * ff)
    grad_ff = lax.psum_scatter(grad_ff, "dp", scatter_dimension=0, tiled=True).reshape(own, 2, ff)
    grad_ff = lax.psum_scatter(grad_ff, "mp", scatter_dimension=2, tiled=True).astype(F32)
    grad_attn = jnp.concatenate([grad_qkv[0], grads[0, :, 2 * ff :]], axis=1)
    grad_attn = lax.psum_scatter(grad_attn, "dp", scatter_dimension=0, tiled=True)
    grad_attn = lax.psum(grad_attn, "mp").astype(F32)
    sums = lax.psum(sums, ("dp", "mp"))
    sums = lax.dynamic_slice_in_dim(sums, lax.axis_index("dp") * own, own, axis=1)
    return (
        layer_out, input_grad, grad_attn[:, : 3 * width], grad_attn[:, 3 * width :],
        grad_ff[:, 0], grad_ff[:, 1], sums[0:3], sums[3], sums[4], sums[5], sums[6],
    )


def on_device(
    tokens, segment_ids, valid_len, qkv_weight, out_weight, up_weight, down_weight, conv_weight,
    ln1_gain, ln1_shift, ln2_gain, ln2_shift, cotangent,
):
    own, ffs = up_weight.shape
    direct = own % 16 == 0 and ffs == tokens.shape[2] and own <= VECTORS and lax.axis_size("mp") == 4
    plan = direct_plan if direct else gathered_plan
    return plan(
        tokens, segment_ids, valid_len, qkv_weight, out_weight, up_weight, down_weight, conv_weight,
        (ln1_gain, ln1_shift, ln2_gain, ln2_shift), cotangent,
    )


def solution(mesh):
    rows = P(("dp", "mp"), None, None)
    weights = (P("dp", None), P("dp", None), P("dp", "mp"), P("dp", "mp"), P(None, "dp"))
    vectors = (P("dp"),) * 4
    return jax.shard_map(
        on_device,
        mesh=mesh,
        in_specs=(rows, P(("dp", "mp"), None), P(("dp", "mp"))) + weights + vectors + (rows,),
        out_specs=(rows, rows) + weights + vectors,
        check_vma=False,
    )
```

```python
import functools
import math

import jax
import jax.numpy as jnp
from jax import lax
from jax.experimental import pallas as pl
from jax.experimental.pallas import tpu as pltpu
from jax.sharding import PartitionSpec as P

HEADS = 6
VECTORS = 128
LANES = 128
BF = jnp.bfloat16
F32 = jnp.float32
MIB = 1024 * 1024
VMEM_LIMITS = dict(forward_attention=26, feed_forward=40, backward=36, layer_output=16)


def mm(lhs, rhs):
    return lax.dot_general(lhs, rhs, (((1,), (0,)), ((), ())), preferred_element_type=F32)


def mm_nt(lhs, rhs):
    return lax.dot_general(lhs, rhs, (((1,), (1,)), ((), ())), preferred_element_type=F32)


def tree_sum(items):
    items = list(items)
    while len(items) > 1:
        items = [a + b for a, b in zip(items[::2], items[1::2])]
    return items[0]


def pack_weights(qkv_ref, up_ref, down_ref, conv_ref, g1_ref, s1_ref, g2_ref, s2_ref, narrow_ref, ff_ref, rows_ref):
    own, ffs = up_ref.shape
    rows_ref[...] = jnp.zeros_like(rows_ref)
    rows_ref[0:3, :own] = conv_ref[...].astype(F32)
    for i, ref in enumerate((g1_ref, s1_ref, g2_ref, s2_ref)):
        rows_ref[3 + i : 4 + i, :own] = ref[...].astype(F32)
    wide = qkv_ref.shape[1]
    narrow_ref[:, :wide] = qkv_ref[...]
    narrow_ref[:, wide:] = rows_ref[...].T[:own].astype(BF)
    ff_ref[:own] = up_ref[...]
    ff_ref[own:] = down_ref[...]


def tiles(total, size):
    return [slice(at, at + size) for at in range(0, total, size)]


def weave(*strands):
    strands = [strand for strand in strands if strand]
    total = sum(len(strand) for strand in strands)
    pieces = [((i + 0.5) / len(strand), j, piece) for j, strand in enumerate(strands) for i, piece in enumerate(strand)]
    assert len(pieces) == total
    for _, _, piece in sorted(pieces, key=lambda item: item[:2]):
        piece()


def twice(tile, lanes):
    return jnp.concatenate([tile] * (lanes // LANES), axis=1)


def load_columns(packed_ref, col_ref, places):
    for i, place in enumerate(places):
        column = packed_ref[:, place : place + 1].astype(F32)
        col_ref[i] = jnp.broadcast_to(column, (column.shape[0], LANES))


def column_mean(values):
    return jnp.sum(values, axis=0, keepdims=True) * (1.0 / values.shape[0])


def norm_columns(values):
    centred = values - column_mean(values)
    scale = lax.rsqrt(column_mean(centred * centred) + 1e-06)
    return centred * scale, scale


def fold(values):
    rows, lanes = values.shape
    return jnp.sum(values.reshape(rows // 8, 8, lanes), axis=0)


def fold_lanes(values):
    return sum(values[:, t] for t in tiles(values.shape[1], LANES))


def forward_attention(index_ref, len_ref, tok_ref, seg_ref, *refs, pieces):
    piece_refs = refs[:pieces]
    (
        five_ref, mc_ref, v_ref, e_ref, facts_ref, packed_ref, w_ref,
        wt_ref, wide_ref, col_ref, bias_ref, key_ref, value_ref,
    ) = refs[pieces:]
    x_ref, norm_ref, q_ref, k_ref, att_ref = [five_ref.at[:, i] for i in range(5)]
    aux_ref, inv_ref = facts_ref.at[:, :8], facts_ref.at[:, 8:]
    rows, seq, width = tok_ref.shape
    head = width // HEADS
    step = pl.program_id(0)

    @pl.when(step == 0)
    def _():
        own = width // pieces
        for i, ref in enumerate(piece_refs):
            wide_ref[pl.ds(pl.multiple_of(index_ref[i] * own, 16), own), :] = ref[...]
        w_ref[...] = wide_ref[:, : 3 * width]
        wt_ref[:width] = (wide_ref[:, :width].astype(F32) * head ** (-0.5)).astype(BF).T
        wt_ref[width:] = wide_ref[:, width : 3 * width].T
        packed_ref[...] = wide_ref[:, 3 * width :]
        load_columns(packed_ref, col_ref, range(5))

    place = lax.broadcasted_iota(jnp.int32, (1, seq), 1)
    zero = jnp.zeros((head, seq), BF)

    def preparation(r):
        known = {}

        def start():
            segs = seg_ref[pl.ds(step * rows + r, 1), :].astype(F32)
            valid = place < len_ref[step * rows + r]
            number = jnp.where(valid, segs, -1.0)
            links = jnp.where(valid & (place > 0) & (number == pltpu.roll(number, 1, 1)), 1.0, 0.0)
            next_links = jnp.where(place < seq - 1, pltpu.roll(links, seq - 1, 1), 0.0)
            none = jnp.zeros_like(links)
            aux = jnp.concatenate([links, next_links, number, none, none, none, none, none], axis=0)
            aux_ref[r] = aux
            x_ref[r] = tok_ref[r].T
            known.update(segs=segs, links=links, next_links=next_links, key_number=aux.T[:, 2:3])

        def mask(t):
            row_id = lax.broadcasted_iota(jnp.int32, (64, seq), 0) + t.start
            col_id = lax.broadcasted_iota(jnp.int32, (64, seq), 1)
            allowed = (known["key_number"][t] == known["segs"]) | (row_id == col_id)
            bias_ref[r, t] = jnp.where(allowed, 0.0, -1e30)

        def conv(t):
            base = x_ref[r, t].astype(F32)
            before = pltpu.roll(base, 1, 1) * known["links"]
            after = pltpu.roll(base, seq - 1, 1) * known["next_links"]
            conv0, conv1, conv2 = [twice(col_ref[i, t], seq) for i in range(3)]
            mc_ref[r, t] = base + before * conv0 + base * conv1 + after * conv2

        def norm(t):
            n, _ = norm_columns(mc_ref[r, :, t])
            norm_ref[r, :, t] = (n * col_ref[3] + col_ref[4]).astype(BF)

        pieces = [start] + [functools.partial(conv, t) for t in tiles(width, 32)]
        pieces += [functools.partial(norm, t) for t in tiles(seq, LANES)]
        return pieces + [functools.partial(mask, t) for t in tiles(seq, 64)]

    def project():
        normed = jnp.concatenate([norm_ref[r] for r in range(rows)], axis=1)
        for i, ref in enumerate((q_ref, k_ref, value_ref)):
            part = mm(wt_ref[i * width : (i + 1) * width], normed).astype(BF)
            for r in range(rows):
                ref[r] = part[:, r * seq : (r + 1) * seq]
        for r in range(rows):
            key_ref[r] = k_ref[r].T
            v_ref[r] = value_ref[r].T

    def scores(r, p):
        low, high = [q_ref[r, h * head : (h + 1) * head] for h in (2 * p, 2 * p + 1)]
        both = jnp.concatenate([jnp.concatenate([low, zero], axis=1), jnp.concatenate([zero, high], axis=1)], axis=0)
        return mm(key_ref[r, :, 2 * p * head : 2 * (p + 1) * head], both)

    def attended(r, p):
        both = jnp.concatenate([e_ref[r, 2 * p], e_ref[r, 2 * p + 1]], axis=1)
        product = mm(value_ref[r, 2 * p * head : 2 * (p + 1) * head], both)
        parts = []
        for i in range(2):
            att = product[i * head : (i + 1) * head, i * seq : (i + 1) * seq] * inv_ref[r, 2 * p + i : 2 * p + i + 1]
            parts.append(att.astype(BF))
        return jnp.concatenate(parts, axis=0)

    def soften(r, p, product):
        for i in range(2):
            for t in tiles(seq, LANES):
                masked = product[:, i * seq + t.start : i * seq + t.stop] + bias_ref[r, :, t]
                raised = jnp.exp(masked - jnp.max(masked, axis=0, keepdims=True))
                inv_ref[r, 2 * p + i : 2 * p + i + 1, t] = 1.0 / jnp.sum(raised, axis=0, keepdims=True)
                e_ref[r, 2 * p + i, :, t] = raised.astype(BF)

    weave(*[preparation(r) for r in range(rows)])
    project()
    work = [(r, p) for r in range(rows) for p in range(HEADS // 2)]
    current, last = scores(*work[0]), None
    for at, (r, p) in enumerate(work):
        following = scores(*work[at + 1]) if at + 1 < len(work) else None
        finished = attended(*last) if last else None
        soften(r, p, current)
        if last:
            att_ref[last[0], 2 * last[1] * head : 2 * (last[1] + 1) * head] = finished
        current, last = following, (r, p)
    att_ref[last[0], 2 * last[1] * head : 2 * (last[1] + 1) * head] = attended(*last)


def gelu_parts(x):
    cdf = 0.5 * lax.erf(x * math.sqrt(0.5)) + 0.5
    bell = jnp.exp2(x * x * (-0.5 / math.log(2.0)) - 0.5 * math.log2(2.0 * math.pi))
    return x * cdf, cdf + x * bell


def feed_forward(index_ref, five_ref, mc_ref, ct_ref, packed_ref, *refs, pieces, shards):
    att_ref = five_ref.at[:, 0]
    piece_refs = refs[:pieces]
    groups = 2 if pieces > 1 else 1
    hidden_out, mixed_out, gm_ref, ga_ref, gs_ref, down_ref = refs[pieces : pieces + 6]
    hidden_ref, mixed_ref = hidden_out.at[0], mixed_out.at[0]
    gw_refs = refs[pieces + 6 : pieces + 6 + groups]
    (
        up_ref, upt_ref, downt_ref, out_ref, outt_ref, up_acc, down_acc, out_acc, col_acc, col_ref,
        att_cat, n_ref, norm_ref, ctt_ref, gp_ref, gn_ref, scale_ref, branch_ref,
    ) = refs[pieces + 6 + groups :]
    rows, seq, width = ct_ref.shape
    ff = up_ref.shape[1]
    ffs = ff // shards
    own = width // pieces
    step = pl.program_id(0)

    @pl.when(step == 0)
    def _():
        for acc in (up_acc, down_acc, out_acc, col_acc):
            acc[...] = jnp.zeros_like(acc)
        for i, ref in enumerate(piece_refs):
            here = pl.ds(pl.multiple_of(index_ref[i] * own, 16), own)
            for j in range(shards):
                up_ref[here, j * ffs : (j + 1) * ffs] = ref[2 * j * own : (2 * j + 1) * own]
                down_ref[here, j * ffs : (j + 1) * ffs] = ref[(2 * j + 1) * own : (2 * j + 2) * own]
            out_ref[here, :] = ref[2 * shards * own :]
        upt_ref[...] = up_ref[...].T
        downt_ref[...] = down_ref[...].T
        outt_ref[...] = out_ref[...].T
        load_columns(packed_ref, col_ref, (5, 6))

    def lanes_of(r):
        return slice(r * seq, (r + 1) * seq)

    def spots_of(r):
        return [slice(at, at + LANES) for at in range(r * seq, (r + 1) * seq, LANES)]

    def preparation(r):
        lanes = lanes_of(r)

        def turn():
            ctt_ref[:, lanes] = ct_ref[r].T
            att_cat[:, lanes] = att_ref[r]

        def branch():
            mixed_ref[:, lanes] = mc_ref[r] + mm(outt_ref[...], att_ref[r])

        def norm(t):
            n, scale = norm_columns(mixed_ref[:, t])
            n_ref[:, t] = n
            scale_ref[0:1, t] = scale
            norm_ref[:, t] = (n * col_ref[0] + col_ref[1]).astype(BF)

        return [turn, branch] + [functools.partial(norm, t) for t in spots_of(r)]

    def activation(block):
        pre = mm(upt_ref[block], norm_ref[...])
        grad_hidden = mm(downt_ref[block], ctt_ref[...])
        for low in range(0, block.stop - block.start, 16):
            part = slice(low, low + 16)
            here = slice(block.start + low, block.start + low + 16)
            hidden, slope = gelu_parts(pre[part])
            hidden_ref[here] = hidden.astype(BF)
            gp_ref[here] = (grad_hidden[part] * slope).astype(BF)

    def norm_back(r):
        spots = spots_of(r)
        mean_e = [jnp.zeros((8, LANES), F32) for _ in spots]
        mean_en = [jnp.zeros((8, LANES), F32) for _ in spots]
        means = []

        def sums(d):
            column = col_ref[0, d]
            gain_sum, shift_sum = col_acc[0, d], col_acc[1, d]
            for i, t in enumerate(spots):
                grad_n = gn_ref[d, t]
                product = grad_n * n_ref[d, t]
                gain_sum += product
                shift_sum += grad_n
                mean_e[i] += fold(grad_n * column)
                mean_en[i] += fold(product * column)
            col_acc[0, d] = gain_sum
            col_acc[1, d] = shift_sum

        def finish():
            for i in range(len(spots)):
                me = jnp.sum(mean_e[i], axis=0, keepdims=True) * (1.0 / width)
                men = jnp.sum(mean_en[i], axis=0, keepdims=True) * (1.0 / width)
                means.append((me, men))

        def apply(d):
            for i, t in enumerate(spots):
                me, men = means[i]
                change = scale_ref[0:1, t] * (gn_ref[d, t] * col_ref[0, d] - me - n_ref[d, t] * men)
                grad_mixed = ctt_ref[d, t].astype(F32) + change
                gm_ref[r, d, i * LANES : (i + 1) * LANES] = grad_mixed
                branch_ref[d, t] = grad_mixed.astype(BF)

        def attended():
            ga_ref[r] = mm(out_ref[...], branch_ref[:, lanes_of(r)]).astype(BF)

        pieces = [functools.partial(sums, d) for d in tiles(width, 32)] + [finish]
        return pieces + [functools.partial(apply, d) for d in tiles(width, 32)] + [attended]

    weave(*[preparation(r) for r in range(rows)])
    for block in tiles(ff, 128):
        activation(block)
    gn_ref[...] = mm(up_ref[...], gp_ref[...])
    down_acc[...] += mm_nt(ctt_ref[...], hidden_ref[...])
    up_acc[...] += mm_nt(norm_ref[...], gp_ref[...])
    weave(*[norm_back(r) for r in range(rows)])
    out_acc[...] += mm_nt(att_cat[...], branch_ref[...])

    @pl.when(step == pl.num_programs(0) - 1)
    def _():
        for i in range(pieces):
            here = pl.ds(pl.multiple_of(index_ref[i] * own, 16), own)
            place = gw_refs[i % groups]
            for j in range(shards):
                cols = slice(j * ffs, (j + 1) * ffs)
                place[i // groups, :, 2 * j * ffs : (2 * j + 1) * ffs] = up_acc[here, cols].astype(BF)
                place[i // groups, :, (2 * j + 1) * ffs : (2 * j + 2) * ffs] = down_acc[here, cols].astype(BF)
            place[i // groups, :, 2 * ff :] = out_acc[here, :].astype(BF)
        gs_ref[...] = jnp.zeros_like(gs_ref)
        for i in range(2):
            gs_ref[5 + i : 6 + i] = jnp.sum(col_acc[i].T, axis=0, keepdims=True)


def layer_output(hidden_ref, mixed_ref, down_ref, lo_ref):
    rows, seq, _ = lo_ref.shape
    total = (mixed_ref[0] + mm(down_ref[...], hidden_ref[0])).astype(BF)
    for r in range(rows):
        lo_ref[r] = total[:, r * seq : (r + 1) * seq].T


def backward(
    five_ref, mc_ref, v_ref, e_ref, facts_ref, ga_ref, gm_ref, index_ref, w_ref, packed_ref, other_ref, ig_ref, gs_ref, *refs, pieces,
):
    x_ref, norm_ref, q_ref, k_ref, att_ref = [five_ref.at[:, i] for i in range(5)]
    aux_ref, inv_ref = facts_ref.at[:, :8], facts_ref.at[:, 8:]
    gw_refs = refs[:-11]
    (
        proj_ref, w_acc, norm_cat, soft_ref, logit_ref, gn_ref, acc_ref, col_ref, n_ref, g_ref, turn_ref
    ) = refs[-11:]
    rows, seq, width = v_ref.shape
    own = width // pieces
    head = width // HEADS
    step = pl.program_id(0)

    @pl.when(step == 0)
    def _():
        w_acc[...] = jnp.zeros_like(w_acc)
        acc_ref[...] = jnp.zeros_like(acc_ref)
        load_columns(packed_ref, col_ref, range(4))

    zero = jnp.zeros((head, seq), BF)
    work = [(r, p) for r in range(rows) for p in range(HEADS // 2)]

    def opening(r, p):
        grads, inners = [], []
        for h in (2 * p, 2 * p + 1):
            part = slice(h * head, (h + 1) * head)
            grad_att = ga_ref[r, part].astype(F32) * inv_ref[r, h : h + 1]
            inners.append(jnp.sum(grad_att * att_ref[r, part].astype(F32), axis=0, keepdims=True))
            grads.append(grad_att.astype(BF))
        low, high = grads
        both = jnp.concatenate([jnp.concatenate([low, zero], axis=1), jnp.concatenate([zero, high], axis=1)], axis=0)
        product = mm(v_ref[r, :, 2 * p * head : 2 * (p + 1) * head], both)
        soft_ref[r, 2 * p] = product[:, :seq]
        soft_ref[r, 2 * p + 1] = product[:, seq:]
        return jnp.concatenate(grads, axis=0), inners

    ready = opening(*work[0])
    for at, (r, p) in enumerate(work):
        grad_att, inners = ready
        if at + 1 < len(work):
            ready = opening(*work[at + 1])
        for i, h in enumerate((2 * p, 2 * p + 1)):
            for t in tiles(seq, 32):
                raised = e_ref[r, h, t].astype(F32)
                logit_ref[r, h, t] = (raised * (soft_ref[r, h, t] - inners[i])).astype(BF)
        part = slice(2 * p * head, 2 * (p + 1) * head)
        pair = slice(2 * p, 2 * p + 2)
        beside = jnp.concatenate([logit_ref[r, 2 * p], logit_ref[r, 2 * p + 1]], axis=1)
        grad_q = mm(k_ref[r, part], beside)
        grad_k = mm_nt(q_ref[r, part], logit_ref[r, pair].reshape(2 * seq, seq))
        grad_v = mm_nt(grad_att, e_ref[r, pair].reshape(2 * seq, seq))
        for i in range(2):
            place = slice(r * seq, (r + 1) * seq)
            own_rows, own_cols = slice(i * head, (i + 1) * head), slice(i * seq, (i + 1) * seq)
            for j, grad in enumerate((grad_q, grad_k, grad_v)):
                first = j * width + (2 * p + i) * head
                mine = grad[own_rows, own_cols]
                proj_ref[first : first + head, place] = (mine * head ** (-0.5) if j == 0 else mine).astype(BF)
    gn_ref[...] = mm(w_ref[...], proj_ref[...])
    for r in range(rows):
        norm_cat[:, r * seq : (r + 1) * seq] = norm_ref[r]
    w_acc[...] += mm_nt(norm_cat[...], proj_ref[...])

    spots = tiles(seq, LANES)
    for r in range(rows):
        wide = [slice(r * seq + t.start, r * seq + t.stop) for t in spots]
        scales = []
        for t in spots:
            n, scale = norm_columns(mc_ref[r, :, t])
            n_ref[r, :, t] = n
            scales.append(scale)
        mean_e = [jnp.zeros((8, LANES), F32) for _ in spots]
        mean_en = [jnp.zeros((8, LANES), F32) for _ in spots]
        for d in tiles(width, 32):
            column = col_ref[3, d]
            gain_sum, shift_sum = acc_ref[3, d], acc_ref[4, d]
            for i, t in enumerate(spots):
                grad_n = gn_ref[d, wide[i]]
                product = grad_n * n_ref[r, d, t]
                gain_sum += product
                shift_sum += grad_n
                mean_e[i] += fold(grad_n * column)
                mean_en[i] += fold(product * column)
            acc_ref[3, d] = gain_sum
            acc_ref[4, d] = shift_sum
        for i, t in enumerate(spots):
            me = jnp.sum(mean_e[i], axis=0, keepdims=True) * (1.0 / width)
            men = jnp.sum(mean_en[i], axis=0, keepdims=True) * (1.0 / width)
            for d in tiles(width, 64):
                e = gn_ref[d, wide[i]] * col_ref[3, d]
                g_ref[r, d, t] = gm_ref[r, d, t] + scales[i] * (e - me - n_ref[r, d, t] * men)
        links, next_links = aux_ref[r, 0:1], aux_ref[r, 1:2]
        for d in tiles(width, 32):
            g = g_ref[r, d]
            base = x_ref[r, d].astype(F32)
            before = pltpu.roll(g, 1, 1) * links
            after = pltpu.roll(g, seq - 1, 1) * next_links
            acc_ref[0, d] += fold_lanes(base * after)
            acc_ref[1, d] += fold_lanes(base * g)
            acc_ref[2, d] += fold_lanes(base * before)
            conv0, conv1, conv2 = [twice(col_ref[i, d], seq) for i in range(3)]
            turn_ref[r, d] = (g + conv1 * g + conv0 * after + conv2 * before).astype(BF)
        ig_ref[r] = turn_ref[r].T

    @pl.when(step == pl.num_programs(0) - 1)
    def _():
        gs_ref[...] = other_ref[...]
        for i in range(5):
            gs_ref[i : i + 1] += jnp.sum(acc_ref[i].T, axis=0, keepdims=True)
        groups = len(gw_refs)
        for i in range(pieces):
            here = pl.ds(pl.multiple_of(index_ref[i] * own, 16), own)
            gw_refs[i % groups][i // groups] = w_acc[here, :].astype(BF)


def in_hbm(values):
    return pltpu.with_memory_space_constraint(values, pltpu.HBM)


def by_row(shape, rows, first=0):
    tail = tuple(shape[1:])
    return pl.BlockSpec((rows,) + tail, lambda i, *_: (i + first,) + (0,) * len(tail))


def whole(shape):
    place = (0,) * len(shape)
    return pl.BlockSpec(tuple(shape), lambda i, *_: place, pipeline_mode=pl.Buffered(1))


def step_rows(count, most):
    return max(r for r in range(1, most + 1) if count % r == 0)


def call(body, name, scalars, rows, row_args, args, row_outs, outs, scratch, span=None, into=None, near=(), only=None):
    first, count = span or (0, row_args[0].shape[0])
    skip = first // rows
    total = row_args[0].shape[0]

    def spec_of(shape):
        return by_row(shape, shape[0] * rows // total, skip)

    in_specs = [spec_of(a.shape) for a in row_args]
    if only:
        tail = row_args[0].shape[2:]
        in_specs[0] = pl.BlockSpec((rows, 1) + tail, lambda i, *_: (i, only) + (0,) * len(tail))
    in_specs += [whole(a.shape) for a in args]
    aliases = {}
    if into is not None:
        in_specs.append(pl.BlockSpec(memory_space=pl.ANY))
        aliases = {len(scalars) + len(in_specs) - 1: 0}
    spec = pltpu.PrefetchScalarGridSpec(
        num_scalar_prefetch=len(scalars),
        grid=(count // rows,),
        in_specs=in_specs,
        out_specs=[spec_of(s) for s, _ in row_outs] + [whole(s) for s, _ in outs],
        scratch_shapes=[pltpu.VMEM(s, t) for s, t in scratch],
    )
    return pl.pallas_call(
        body,
        grid_spec=spec,
        out_shape=[(jax.ShapeDtypeStruct if "out" + str(i) in near else pltpu.HBM)(s, t) for i, (s, t) in enumerate(row_outs)]
        + [jax.ShapeDtypeStruct(s, t) for s, t in outs],
        input_output_aliases=aliases,
        compiler_params=pltpu.CompilerParams(dimension_semantics=("arbitrary",), vmem_limit_bytes=VMEM_LIMITS[name] * MIB),
        name=name,
    )(*scalars, *[a if i in near else in_hbm(a) for i, a in enumerate(row_args)], *args, *(() if into is None else (into,)))


def small_call(body, name, args, outs, scratch=()):
    return pl.pallas_call(
        body,
        out_shape=[jax.ShapeDtypeStruct(s, t) for s, t in outs],
        scratch_shapes=[pltpu.VMEM(s, t) for s, t in scratch],
        compiler_params=pltpu.CompilerParams(vmem_limit_bytes=16 * MIB),
        name=name,
    )(*args)


def run_forward(index, tokens, segment_ids, valid_len, pieces):
    count, seq, width = tokens.shape
    flipped = (count, width, seq)
    rows = step_rows(count, 2)
    row_outs = [
        ((count, 5, width, seq), BF), (flipped, F32), ((count, seq, width), BF),
        ((count, HEADS, seq, seq), BF), ((count, 16, seq), F32),
    ]
    return call(
        functools.partial(forward_attention, pieces=len(pieces)), "forward_attention", (index, in_hbm(valid_len)),
        rows, (tokens,), (in_hbm(segment_ids), *pieces),
        row_outs, [((width, VECTORS), BF), ((width, 3 * width), BF)],
        [
            ((3 * width, width), BF), ((width, 3 * width + VECTORS), BF), ((5, width, LANES), F32),
            ((rows, seq, seq), F32), ((rows, seq, width), BF), ((rows, width, seq), BF),
        ],
    )


def run_feed_forward(index, five, mixed, cotangent, packed, pieces, shards):
    count, seq, width = cotangent.shape
    own = width // len(pieces)
    ff = shards * width
    groups = 2 if len(pieces) > 1 else 1
    rows = step_rows(count, 2)
    wide = rows * seq
    row_outs = [
        ((count // rows, ff, wide), BF), ((count // rows, width, wide), F32),
        ((count, width, seq), F32), ((count, width, seq), BF),
    ]
    grads = ((len(pieces) // groups, own, 2 * ff + width), BF)
    return call(
        functools.partial(feed_forward, pieces=len(pieces), shards=shards), "feed_forward", (index,),
        rows, (five, mixed, cotangent), (packed, *pieces),
        row_outs, [((8, width), F32), ((width, ff), BF)] + [grads] * groups,
        [((width, ff), BF)] + [((ff, width), BF)] * 2 + [((width, width), BF)] * 2
        + [((width, ff), F32)] * 2 + [((width, width), F32), ((2, width, LANES), F32), ((2, width, LANES), F32)]
        + [((width, wide), BF), ((width, wide), F32), ((width, wide), BF), ((width, wide), BF)]
        + [((ff, wide), BF)]
        + [((width, wide), F32), ((8, wide), F32), ((width, wide), BF)],
        near=("out3",), only=4,
    )


def run_layer_output(hidden, mixed, down, shape, part, parts, into):
    steps = hidden.shape[0]
    span = (part * steps // parts, (part + 1) * steps // parts - part * steps // parts)

    def body(*refs):
        layer_output(*refs[:3], refs[-1])

    return call(body, "layer_output", (), 1, (hidden, mixed), (down,), [(shape, BF)], [], [], span=span, into=into)[0]


def run_backward(index, weight, kept, grads, packed, other, pieces):
    count, seq, width = kept[2].shape
    own = width // pieces
    groups = 2 if pieces > 1 else 1
    rows = step_rows(count, 2)
    row_args = (*kept, *grads)
    many = len(row_args)

    def body(index_ref, *refs):
        backward(*refs[:many], index_ref, *refs[many:], pieces=pieces)

    return call(
        body, "backward", (index,), rows, row_args, (weight, packed, other),
        [((count, seq, width), BF)], [((8, width), F32)] + [((pieces // groups, own, 3 * width), BF)] * groups,
        [
            ((3 * width, rows * seq), BF), ((width, 3 * width), F32), ((width, rows * seq), BF),
            ((rows, HEADS, seq, seq), F32), ((rows, HEADS, seq, seq), BF), ((width, rows * seq), F32),
            ((5, width, LANES), F32), ((4, width, LANES), F32), ((rows, width, seq), F32), ((rows, width, seq), F32),
            ((rows, width, seq), BF),
        ],
        near=(5,),
    )


def exchange(values, axis, offset):
    size = lax.axis_size(axis)
    return lax.ppermute(values, axis, [(i, i ^ offset) for i in range(size)])


def add_halves(mine, received):
    count, own, cols = mine.shape

    def body(mine_ref, received_ref, *out_refs):
        for i, ref in enumerate(out_refs):
            ref[...] = (mine_ref[i].astype(F32) + received_ref[i].astype(F32)).astype(BF)

    return small_call(body, "add_halves", (mine, received), [((own, cols), BF)] * count)


def add_wide(*items):
    return tree_sum(item.astype(F32) for item in items)


def store_high_low(ref, cols, values):
    high = values.astype(BF)
    low = (values - high.astype(F32)).astype(BF)
    ref[:, cols:] = jnp.concatenate([high, low, jnp.zeros((ref.shape[0] - 16, LANES), BF)], axis=0)


def load_high_low(ref, cols):
    both = ref[:16, cols:].astype(F32)
    return both[:8] + both[8:]


def add_halves_and_sums(index, mine, received, sums, received_sums):
    count, own, cols = mine.shape
    width = sums.shape[1]

    def body(index_ref, mine_ref, received_ref, sums_ref, received_sums_ref, *out_refs):
        total = sums_ref[...] + received_sums_ref[...]
        for i, ref in enumerate(out_refs):
            ref[:, :cols] = (mine_ref[i].astype(F32) + received_ref[i].astype(F32)).astype(BF)
            turned = pltpu.roll(total, lax.rem(width - index_ref[2 * i] * own, width), 1)[:, :LANES]
            store_high_low(ref, cols, turned)

    spec = pltpu.PrefetchScalarGridSpec(
        num_scalar_prefetch=1, grid=(1,),
        in_specs=[whole(a.shape) for a in (mine, received, sums, received_sums)],
        out_specs=[whole((own, cols + LANES))] * count,
    )
    return pl.pallas_call(
        body, grid_spec=spec, out_shape=[jax.ShapeDtypeStruct((own, cols + LANES), BF)] * count,
        compiler_params=pltpu.CompilerParams(vmem_limit_bytes=16 * MIB), name="add_halves_and_sums",
    )(index, mine, received, sums, received_sums)


def add_packed(name, items):
    cols = items[0].shape[1] - LANES

    def body(*refs):
        out_ref = refs[-1]
        out_ref[:, :cols] = tree_sum(ref[:, :cols].astype(F32) for ref in refs[:-1]).astype(BF)
        store_high_low(out_ref, cols, tree_sum(load_high_low(ref, cols) for ref in refs[:-1]))

    return small_call(body, name, items, [(items[0].shape, BF)])[0]


def add_last(items):
    own, cols = items[0].shape[0], items[0].shape[1] - LANES

    def body(*refs):
        ins, outs = refs[: len(items)], refs[len(items) :]
        outs[0][...] = tree_sum(ref[:, :cols].astype(F32) for ref in ins)
        vectors = tree_sum(load_high_low(ref, cols) for ref in ins)
        outs[1][...] = vectors[0:3, :own]
        for i in range(4):
            outs[2 + i][...] = vectors[3 + i : 4 + i, :own]

    return small_call(body, "add_last", items, [((own, cols), F32), ((3, own), F32)] + [((1, own), F32)] * 4)


def direct_plan(tokens, segment_ids, valid_len, qkv_weight, out_weight, up_weight, down_weight, conv_weight, vectors, cotangent):
    count, seq, width = tokens.shape
    own, ffs = up_weight.shape
    dp, mp = lax.axis_size("dp"), lax.axis_size("mp")
    me = lax.axis_index("dp")
    offsets = [2 * p for p in range(dp // 2)]
    index = jnp.stack([me ^ (p ^ c) for p in offsets for c in range(2)]).astype(jnp.int32)
    narrow, ff_own = small_call(
        pack_weights, "pack_weights",
        [in_hbm(a) for a in (qkv_weight, up_weight, down_weight, conv_weight, *[v.reshape(1, own) for v in vectors])],
        [((own, 3 * width + VECTORS), BF), ((2 * own, ffs), BF)], [((VECTORS, VECTORS), F32)],
    )
    plane = [narrow] + [exchange(narrow, "dp", p) for p in offsets[1:]]
    shards = [ff_own] + [exchange(ff_own, "mp", j) for j in range(1, mp)]
    pieces = [piece for a in plane for piece in (a, exchange(a, "dp", 1))]
    column = jnp.concatenate(shards + [out_weight], axis=0)
    columns = [column] + [exchange(column, "dp", p) for p in offsets[1:]]
    five, mixed, v, raised, facts, packed, weight = run_forward(
        index, tokens, segment_ids, valid_len, pieces
    )
    columns, five = lax.optimization_barrier((columns, five))
    pieces = [piece for a in columns for piece in (a, exchange(a, "dp", 1))]
    hidden, mixed_attn, grad_mixed, grad_att, sums2, down, mine, theirs = run_feed_forward(
        index, five, mixed, cotangent, packed, pieces, mp
    )
    received = exchange(theirs, "dp", 1)
    shape = cotangent.shape
    layer_out = run_layer_output(hidden, mixed_attn, down, shape, 0, 3, None)
    received, layer_out = lax.optimization_barrier((received, layer_out))
    parts = list(add_halves(mine, received))
    parts[0], grad_att = lax.optimization_barrier((parts[0], grad_att))
    plane = [parts[0]] + [exchange(parts[i], "dp", p) for i, p in enumerate(offsets) if i]
    kept = (five, mixed, v, raised, facts)
    input_grad, sums, mine_a, theirs_a = run_backward(
        index, weight, kept, (grad_att, grad_mixed), packed, sums2, dp
    )
    plane, theirs_a, sums = lax.optimization_barrier((plane, theirs_a, sums))
    received_a = exchange(theirs_a, "dp", 1)
    received_s = exchange(sums, "dp", 1)
    total = add_wide(*plane).astype(BF)
    part = 2 * ffs
    near = jnp.concatenate([total[:, :part], total[:, 2 * part : 3 * part]], axis=1)
    out_part = total[:, 4 * part :]
    far = jnp.concatenate([total[:, part : 2 * part], total[:, 3 * part :]], axis=1)
    parts = list(add_halves_and_sums(index, mine_a, received_a, sums, received_s))
    parts[0], far, hidden, layer_out = lax.optimization_barrier((parts[0], far, hidden, layer_out))
    plane_a = [parts[0]] + [exchange(parts[i], "dp", p) for i, p in enumerate(offsets) if i]
    received_f = exchange(far, "mp", 1)
    layer_out = run_layer_output(hidden, mixed_attn, down, shape, 1, 3, layer_out)
    plane_a, layer_out = lax.optimization_barrier((plane_a, layer_out))
    total = add_packed("add_plane", plane_a)
    received_1 = exchange(total, "mp", 1)
    received_f, _ = lax.optimization_barrier((received_f, total))
    near_sum = add_wide(near, received_f[:, : 2 * part])
    out_sum = lax.optimization_barrier(add_wide(out_part, received_f[:, 2 * part :]).astype(BF))
    keep = near_sum[:, :part]
    send = jnp.concatenate([near_sum[:, part:].astype(BF), out_sum], axis=1)
    received_n = exchange(send, "mp", 2)
    received_1, layer_out, _ = lax.optimization_barrier((received_1, layer_out, send))
    total = add_packed("add_near", (total, received_1))
    received_2 = exchange(total, "mp", 2)
    layer_out, received_n, _ = lax.optimization_barrier((layer_out, received_n, total))
    layer_out = run_layer_output(hidden, mixed_attn, down, shape, 2, 3, layer_out)
    received_2, layer_out = lax.optimization_barrier((received_2, layer_out))
    grad_up = keep[:, :ffs] + received_n[:, :ffs].astype(F32)
    grad_down = keep[:, ffs:] + received_n[:, ffs : 2 * ffs].astype(F32)
    grad_out = add_wide(out_sum, received_n[:, 2 * ffs :])
    grad_qkv, grad_conv, *grads = add_last((total, received_2))
    return (layer_out, input_grad, grad_qkv, grad_out, grad_up, grad_down, grad_conv, *[g.reshape(own) for g in grads])


def gathered_plan(tokens, segment_ids, valid_len, qkv_weight, out_weight, up_weight, down_weight, conv_weight, vectors, cotangent):
    count, seq, width = tokens.shape
    own = qkv_weight.shape[0]
    dp = width // own
    columns = jnp.stack([conv_weight[0], conv_weight[1], conv_weight[2], *vectors], axis=1)
    narrow = jnp.concatenate([qkv_weight, jnp.pad(columns, ((0, 0), (0, VECTORS - 7))), out_weight], axis=1)
    wide = lax.all_gather(narrow, "dp", axis=0, tiled=True)
    both = lax.all_gather(jnp.concatenate([up_weight, down_weight], axis=0), "mp", axis=1, tiled=True)
    ff = both.shape[1]
    shards = ff // width
    both = lax.all_gather(both, "dp", axis=0).reshape(dp, 2, own, shards, width)
    both = both.transpose(3, 1, 0, 2, 4).reshape(2 * ff, width)
    column = jnp.concatenate([both, wide[:, 3 * width + VECTORS :]], axis=0)
    index = jnp.zeros((1,), jnp.int32)
    five, mixed, v, raised, facts, packed, weight = run_forward(
        index, tokens, segment_ids, valid_len, [wide[:, : 3 * width + VECTORS]]
    )
    hidden, mixed_attn, grad_mixed, grad_att, sums2, down, grads = run_feed_forward(
        index, five, mixed, cotangent, packed, [column], shards
    )
    kept = (five, mixed, v, raised, facts)
    layer_out = run_layer_output(hidden, mixed_attn, down, cotangent.shape, 0, 1, None)
    input_grad, sums, grad_qkv = run_backward(index, weight, kept, (grad_att, grad_mixed), packed, sums2, 1)
    grad_ff = grads[0, :, : 2 * ff].reshape(width, shards, 2, width).transpose(0, 2, 1, 3).reshape(width, 2 * ff)
    grad_ff = lax.psum_scatter(grad_ff, "dp", scatter_dimension=0, tiled=True).reshape(own, 2, ff)
    grad_ff = lax.psum_scatter(grad_ff, "mp", scatter_dimension=2, tiled=True).astype(F32)
    grad_attn = jnp.concatenate([grad_qkv[0], grads[0, :, 2 * ff :]], axis=1)
    grad_attn = lax.psum_scatter(grad_attn, "dp", scatter_dimension=0, tiled=True)
    grad_attn = lax.psum(grad_attn, "mp").astype(F32)
    sums = lax.psum(sums, ("dp", "mp"))
    sums = lax.dynamic_slice_in_dim(sums, lax.axis_index("dp") * own, own, axis=1)
    return (
        layer_out, input_grad, grad_attn[:, : 3 * width], grad_attn[:, 3 * width :],
        grad_ff[:, 0], grad_ff[:, 1], sums[0:3], sums[3], sums[4], sums[5], sums[6],
    )


def on_device(
    tokens, segment_ids, valid_len, qkv_weight, out_weight, up_weight, down_weight, conv_weight,
    ln1_gain, ln1_shift, ln2_gain, ln2_shift, cotangent,
):
    own, ffs = up_weight.shape
    direct = own % 16 == 0 and ffs == tokens.shape[2] and own <= VECTORS and lax.axis_size("mp") == 4
    plan = direct_plan if direct else gathered_plan
    return plan(
        tokens, segment_ids, valid_len, qkv_weight, out_weight, up_weight, down_weight, conv_weight,
        (ln1_gain, ln1_shift, ln2_gain, ln2_shift), cotangent,
    )


def solution(mesh):
    rows = P(("dp", "mp"), None, None)
    weights = (P("dp", None), P("dp", None), P("dp", "mp"), P("dp", "mp"), P(None, "dp"))
    vectors = (P("dp"),) * 4
    return jax.shard_map(
        on_device,
        mesh=mesh,
        in_specs=(rows, P(("dp", "mp"), None), P(("dp", "mp"))) + weights + vectors + (rows,),
        out_specs=(rows, rows) + weights + vectors,
        check_vma=False,
    )
```

```python
import functools
import math

import jax
import jax.numpy as jnp
from jax import lax
from jax.experimental import pallas as pl
from jax.experimental.pallas import tpu as pltpu
from jax.sharding import PartitionSpec as P

HEADS = 6
VECTORS = 128
LANES = 128
BF = jnp.bfloat16
F32 = jnp.float32
MIB = 1024 * 1024
VMEM_LIMITS = dict(forward_attention=26, feed_forward=40, backward=36, layer_output=16)


def mm(lhs, rhs):
    return lax.dot_general(lhs, rhs, (((1,), (0,)), ((), ())), preferred_element_type=F32)


def mm_nt(lhs, rhs):
    return lax.dot_general(lhs, rhs, (((1,), (1,)), ((), ())), preferred_element_type=F32)


def tree_sum(items):
    items = list(items)
    while len(items) > 1:
        items = [a + b for a, b in zip(items[::2], items[1::2])]
    return items[0]


def pack_weights(qkv_ref, up_ref, down_ref, conv_ref, g1_ref, s1_ref, g2_ref, s2_ref, narrow_ref, ff_ref, rows_ref):
    own, ffs = up_ref.shape
    rows_ref[...] = jnp.zeros_like(rows_ref)
    rows_ref[0:3, :own] = conv_ref[...].astype(F32)
    for i, ref in enumerate((g1_ref, s1_ref, g2_ref, s2_ref)):
        rows_ref[3 + i : 4 + i, :own] = ref[...].astype(F32)
    wide = qkv_ref.shape[1]
    narrow_ref[:, :wide] = qkv_ref[...]
    narrow_ref[:, wide:] = rows_ref[...].T[:own].astype(BF)
    ff_ref[:own] = up_ref[...]
    ff_ref[own:] = down_ref[...]


def tiles(total, size):
    return [slice(at, at + size) for at in range(0, total, size)]


def weave(*strands):
    strands = [strand for strand in strands if strand]
    total = sum(len(strand) for strand in strands)
    pieces = [((i + 0.5) / len(strand), j, piece) for j, strand in enumerate(strands) for i, piece in enumerate(strand)]
    assert len(pieces) == total
    for _, _, piece in sorted(pieces, key=lambda item: item[:2]):
        piece()


def twice(tile, lanes):
    return jnp.concatenate([tile] * (lanes // LANES), axis=1)


def load_columns(packed_ref, col_ref, places):
    for i, place in enumerate(places):
        column = packed_ref[:, place : place + 1].astype(F32)
        col_ref[i] = jnp.broadcast_to(column, (column.shape[0], LANES))


def column_mean(values):
    return jnp.sum(values, axis=0, keepdims=True) * (1.0 / values.shape[0])


def norm_columns(values):
    centred = values - column_mean(values)
    scale = lax.rsqrt(column_mean(centred * centred) + 1e-06)
    return centred * scale, scale


def fold(values):
    rows, lanes = values.shape
    return jnp.sum(values.reshape(rows // 8, 8, lanes), axis=0)


def fold_lanes(values):
    return sum(values[:, t] for t in tiles(values.shape[1], LANES))


def forward_attention(index_ref, len_ref, tok_ref, seg_ref, *refs, pieces):
    piece_refs = refs[:pieces]
    (
        five_ref, mc_ref, v_ref, e_ref, facts_ref, packed_ref, w_ref,
        wt_ref, wide_ref, col_ref, key_mask_ref, query_mask_ref, key_ref, value_ref,
    ) = refs[pieces:]
    x_ref, norm_ref, q_ref, k_ref, att_ref = [five_ref.at[:, i] for i in range(5)]
    aux_ref, inv_ref = facts_ref.at[:, :8], facts_ref.at[:, 8:]
    rows, seq, width = tok_ref.shape
    head = width // HEADS
    step = pl.program_id(0)

    @pl.when(step == 0)
    def _():
        own = width // pieces
        for i, ref in enumerate(piece_refs):
            wide_ref[pl.ds(pl.multiple_of(index_ref[i] * own, 16), own), :] = ref[...]
        w_ref[...] = wide_ref[:, : 3 * width]
        wt_ref[...] = wide_ref[:, : 3 * width].T
        packed_ref[...] = wide_ref[:, 3 * width :]
        load_columns(packed_ref, col_ref, range(5))

    place = lax.broadcasted_iota(jnp.int32, (1, seq), 1)
    zero = jnp.zeros((head, seq), BF)

    def preparation(r):
        known = {}

        def start():
            segs = seg_ref[pl.ds(step * rows + r, 1), :].astype(F32)
            valid = place < len_ref[step * rows + r]
            number = jnp.where(valid, segs, -1.0)
            links = jnp.where(valid & (place > 0) & (number == pltpu.roll(number, 1, 1)), 1.0, 0.0)
            next_links = jnp.where(place < seq - 1, pltpu.roll(links, seq - 1, 1), 0.0)
            none = jnp.zeros_like(links)
            aux = jnp.concatenate([links, next_links, number, none, none, none, none, none], axis=0)
            aux_ref[r] = aux
            x_ref[r] = tok_ref[r].T
            known.update(segs=segs, links=links, next_links=next_links, key_number=aux.T[:, 2:3])

        def mask():
            number = known["key_number"]
            lane = lax.broadcasted_iota(jnp.int32, (seq, LANES), 1)
            itself = lax.broadcasted_iota(jnp.int32, (seq, LANES), 0) - (seq - LANES)
            chosen = (lane.astype(F32) == number) | ((number < 0.0) & (lane == itself))
            key_mask_ref[r] = jnp.where(chosen, 1.0, 0.0).astype(BF)
            slot = lax.broadcasted_iota(jnp.int32, (LANES, seq), 0)
            itself = lax.broadcasted_iota(jnp.int32, (LANES, seq), 1) - (seq - LANES)
            open_to = (slot.astype(F32) == known["segs"]) | ((slot >= LANES // 2) & (slot == itself))
            query_mask_ref[r] = jnp.where(open_to, 0.0, -1e30).astype(BF)

        def conv(t):
            base = x_ref[r, t].astype(F32)
            before = pltpu.roll(base, 1, 1) * known["links"]
            after = pltpu.roll(base, seq - 1, 1) * known["next_links"]
            conv0, conv1, conv2 = [twice(col_ref[i, t], seq) for i in range(3)]
            mc_ref[r, t] = base + before * conv0 + base * conv1 + after * conv2

        def norm(t):
            n, _ = norm_columns(mc_ref[r, :, t])
            norm_ref[r, :, t] = (n * col_ref[3] + col_ref[4]).astype(BF)

        pieces = [start] + [functools.partial(conv, t) for t in tiles(width, 32)]
        pieces += [functools.partial(norm, t) for t in tiles(seq, LANES)]
        return pieces + [mask]

    def project():
        normed = jnp.concatenate([norm_ref[r] for r in range(rows)], axis=1)
        for i, ref in enumerate((q_ref, k_ref, value_ref)):
            part = mm(wt_ref[i * width : (i + 1) * width], normed)
            part = (part * (head ** (-0.5) * math.log2(math.e)) if i == 0 else part).astype(BF)
            for r in range(rows):
                ref[r] = part[:, r * seq : (r + 1) * seq]
        for r in range(rows):
            key_ref[r] = k_ref[r].T
            v_ref[r] = value_ref[r].T

    def scores(r, p):
        low, high = [q_ref[r, h * head : (h + 1) * head] for h in (2 * p, 2 * p + 1)]
        both = jnp.concatenate([jnp.concatenate([low, zero], axis=1), jnp.concatenate([zero, high], axis=1)], axis=0)
        keys = jnp.concatenate([key_ref[r, :, 2 * p * head : 2 * (p + 1) * head], key_mask_ref[r]], axis=1)
        masks = jnp.concatenate([query_mask_ref[r], query_mask_ref[r]], axis=1)
        return mm(keys, jnp.concatenate([both, masks], axis=0))

    def attended(r, p):
        both = jnp.concatenate([e_ref[r, 2 * p], e_ref[r, 2 * p + 1]], axis=1)
        product = mm(value_ref[r, 2 * p * head : 2 * (p + 1) * head], both)
        parts = []
        for i in range(2):
            att = product[i * head : (i + 1) * head, i * seq : (i + 1) * seq] * inv_ref[r, 2 * p + i : 2 * p + i + 1]
            parts.append(att.astype(BF))
        return jnp.concatenate(parts, axis=0)

    def soften(r, p, product):
        for i in range(2):
            for t in tiles(seq, LANES):
                masked = product[:, i * seq + t.start : i * seq + t.stop]
                raised = jnp.exp2(masked - jnp.max(masked, axis=0, keepdims=True))
                inv_ref[r, 2 * p + i : 2 * p + i + 1, t] = 1.0 / jnp.sum(raised, axis=0, keepdims=True)
                e_ref[r, 2 * p + i, :, t] = raised.astype(BF)

    weave(*[preparation(r) for r in range(rows)])
    project()
    work = [(r, p) for r in range(rows) for p in range(HEADS // 2)]
    current, last = scores(*work[0]), None
    for at, (r, p) in enumerate(work):
        following = scores(*work[at + 1]) if at + 1 < len(work) else None
        finished = attended(*last) if last else None
        soften(r, p, current)
        if last:
            att_ref[last[0], 2 * last[1] * head : 2 * (last[1] + 1) * head] = finished
        current, last = following, (r, p)
    att_ref[last[0], 2 * last[1] * head : 2 * (last[1] + 1) * head] = attended(*last)


def gelu_parts(x):
    cdf = 0.5 * lax.erf(x * math.sqrt(0.5)) + 0.5
    bell = jnp.exp2(x * x * (-0.5 / math.log(2.0)) - 0.5 * math.log2(2.0 * math.pi))
    return x * cdf, cdf + x * bell


def feed_forward(index_ref, five_ref, mc_ref, ct_ref, packed_ref, *refs, pieces, shards):
    att_ref = five_ref.at[:, 0]
    piece_refs = refs[:pieces]
    groups = 2 if pieces > 1 else 1
    hidden_out, mixed_out, gm_ref, ga_ref, gs_ref, down_ref = refs[pieces : pieces + 6]
    hidden_ref, mixed_ref = hidden_out.at[0], mixed_out.at[0]
    gw_refs = refs[pieces + 6 : pieces + 6 + groups]
    (
        up_ref, upt_ref, downt_ref, out_ref, outt_ref, up_acc, down_acc, out_acc, col_acc, col_ref,
        att_cat, n_ref, norm_ref, ctt_ref, gp_ref, gn_ref, scale_ref, branch_ref,
    ) = refs[pieces + 6 + groups :]
    rows, seq, width = ct_ref.shape
    ff = up_ref.shape[1]
    ffs = ff // shards
    own = width // pieces
    step = pl.program_id(0)

    @pl.when(step == 0)
    def _():
        for acc in (up_acc, down_acc, out_acc, col_acc):
            acc[...] = jnp.zeros_like(acc)
        for i, ref in enumerate(piece_refs):
            here = pl.ds(pl.multiple_of(index_ref[i] * own, 16), own)
            for j in range(shards):
                up_ref[here, j * ffs : (j + 1) * ffs] = ref[2 * j * own : (2 * j + 1) * own]
                down_ref[here, j * ffs : (j + 1) * ffs] = ref[(2 * j + 1) * own : (2 * j + 2) * own]
            out_ref[here, :] = ref[2 * shards * own :]
        upt_ref[...] = up_ref[...].T
        downt_ref[...] = down_ref[...].T
        outt_ref[...] = out_ref[...].T
        load_columns(packed_ref, col_ref, (5, 6))

    def lanes_of(r):
        return slice(r * seq, (r + 1) * seq)

    def spots_of(r):
        return [slice(at, at + LANES) for at in range(r * seq, (r + 1) * seq, LANES)]

    def preparation(r):
        lanes = lanes_of(r)

        def turn():
            ctt_ref[:, lanes] = ct_ref[r].T
            att_cat[:, lanes] = att_ref[r]

        def branch():
            mixed_ref[:, lanes] = mc_ref[r] + mm(outt_ref[...], att_ref[r])

        def norm(t):
            n, scale = norm_columns(mixed_ref[:, t])
            n_ref[:, t] = n
            scale_ref[0:1, t] = scale
            norm_ref[:, t] = (n * col_ref[0] + col_ref[1]).astype(BF)

        return [turn, branch] + [functools.partial(norm, t) for t in spots_of(r)]

    def activation(block):
        pre = mm(upt_ref[block], norm_ref[...])
        grad_hidden = mm(downt_ref[block], ctt_ref[...])
        for low in range(0, block.stop - block.start, 16):
            part = slice(low, low + 16)
            here = slice(block.start + low, block.start + low + 16)
            hidden, slope = gelu_parts(pre[part])
            hidden_ref[here] = hidden.astype(BF)
            gp_ref[here] = (grad_hidden[part] * slope).astype(BF)

    def norm_back(r):
        spots = spots_of(r)
        mean_e = [jnp.zeros((8, LANES), F32) for _ in spots]
        mean_en = [jnp.zeros((8, LANES), F32) for _ in spots]
        means = []

        def sums(d):
            column = col_ref[0, d]
            gain_sum, shift_sum = col_acc[0, d], col_acc[1, d]
            for i, t in enumerate(spots):
                grad_n = gn_ref[d, t]
                product = grad_n * n_ref[d, t]
                gain_sum += product
                shift_sum += grad_n
                mean_e[i] += fold(grad_n * column)
                mean_en[i] += fold(product * column)
            col_acc[0, d] = gain_sum
            col_acc[1, d] = shift_sum

        def finish():
            for i in range(len(spots)):
                me = jnp.sum(mean_e[i], axis=0, keepdims=True) * (1.0 / width)
                men = jnp.sum(mean_en[i], axis=0, keepdims=True) * (1.0 / width)
                means.append((me, men))

        def apply(d):
            for i, t in enumerate(spots):
                me, men = means[i]
                change = scale_ref[0:1, t] * (gn_ref[d, t] * col_ref[0, d] - me - n_ref[d, t] * men)
                grad_mixed = ctt_ref[d, t].astype(F32) + change
                gm_ref[r, d, i * LANES : (i + 1) * LANES] = grad_mixed
                branch_ref[d, t] = grad_mixed.astype(BF)

        def attended():
            ga_ref[r] = mm(out_ref[...], branch_ref[:, lanes_of(r)]).astype(BF)

        pieces = [functools.partial(sums, d) for d in tiles(width, 32)] + [finish]
        return pieces + [functools.partial(apply, d) for d in tiles(width, 32)] + [attended]

    weave(*[preparation(r) for r in range(rows)])
    for block in tiles(ff, 128):
        activation(block)
    gn_ref[...] = mm(up_ref[...], gp_ref[...])
    down_acc[...] += mm_nt(ctt_ref[...], hidden_ref[...])
    up_acc[...] += mm_nt(norm_ref[...], gp_ref[...])
    weave(*[norm_back(r) for r in range(rows)])
    out_acc[...] += mm_nt(att_cat[...], branch_ref[...])

    @pl.when(step == pl.num_programs(0) - 1)
    def _():
        for i in range(pieces):
            here = pl.ds(pl.multiple_of(index_ref[i] * own, 16), own)
            place = gw_refs[i % groups]
            for j in range(shards):
                cols = slice(j * ffs, (j + 1) * ffs)
                place[i // groups, :, 2 * j * ffs : (2 * j + 1) * ffs] = up_acc[here, cols].astype(BF)
                place[i // groups, :, (2 * j + 1) * ffs : (2 * j + 2) * ffs] = down_acc[here, cols].astype(BF)
            place[i // groups, :, 2 * ff :] = out_acc[here, :].astype(BF)
        gs_ref[...] = jnp.zeros_like(gs_ref)
        for i in range(2):
            gs_ref[5 + i : 6 + i] = jnp.sum(col_acc[i].T, axis=0, keepdims=True)


def layer_output(hidden_ref, mixed_ref, down_ref, lo_ref):
    rows, seq, _ = lo_ref.shape
    total = (mixed_ref[0] + mm(down_ref[...], hidden_ref[0])).astype(BF)
    for r in range(rows):
        lo_ref[r] = total[:, r * seq : (r + 1) * seq].T


def backward(
    five_ref, mc_ref, v_ref, e_ref, facts_ref, ga_ref, gm_ref, index_ref, w_ref, packed_ref, other_ref, ig_ref, gs_ref, *refs, pieces,
):
    x_ref, norm_ref, q_ref, k_ref, att_ref = [five_ref.at[:, i] for i in range(5)]
    aux_ref, inv_ref = facts_ref.at[:, :8], facts_ref.at[:, 8:]
    gw_refs = refs[:-11]
    (
        proj_ref, w_acc, norm_cat, soft_ref, logit_ref, gn_ref, acc_ref, col_ref, n_ref, g_ref, turn_ref
    ) = refs[-11:]
    rows, seq, width = v_ref.shape
    own = width // pieces
    head = width // HEADS
    step = pl.program_id(0)

    @pl.when(step == 0)
    def _():
        w_acc[...] = jnp.zeros_like(w_acc)
        acc_ref[...] = jnp.zeros_like(acc_ref)
        load_columns(packed_ref, col_ref, range(4))

    zero = jnp.zeros((head, seq), BF)
    work = [(r, p) for r in range(rows) for p in range(HEADS // 2)]

    def opening(r, p):
        grads, inners = [], []
        for h in (2 * p, 2 * p + 1):
            part = slice(h * head, (h + 1) * head)
            grad_att = ga_ref[r, part].astype(F32) * inv_ref[r, h : h + 1]
            inners.append(jnp.sum(grad_att * att_ref[r, part].astype(F32), axis=0, keepdims=True))
            grads.append(grad_att.astype(BF))
        low, high = grads
        both = jnp.concatenate([jnp.concatenate([low, zero], axis=1), jnp.concatenate([zero, high], axis=1)], axis=0)
        product = mm(v_ref[r, :, 2 * p * head : 2 * (p + 1) * head], both)
        soft_ref[r, 2 * p] = product[:, :seq]
        soft_ref[r, 2 * p + 1] = product[:, seq:]
        return jnp.concatenate(grads, axis=0), inners

    ready = opening(*work[0])
    for at, (r, p) in enumerate(work):
        grad_att, inners = ready
        if at + 1 < len(work):
            ready = opening(*work[at + 1])
        for i, h in enumerate((2 * p, 2 * p + 1)):
            for t in tiles(seq, 32):
                raised = e_ref[r, h, t].astype(F32)
                logit_ref[r, h, t] = (raised * (soft_ref[r, h, t] - inners[i])).astype(BF)
        part = slice(2 * p * head, 2 * (p + 1) * head)
        pair = slice(2 * p, 2 * p + 2)
        beside = jnp.concatenate([logit_ref[r, 2 * p], logit_ref[r, 2 * p + 1]], axis=1)
        grad_q = mm(k_ref[r, part], beside)
        grad_k = mm_nt(q_ref[r, part], logit_ref[r, pair].reshape(2 * seq, seq))
        grad_v = mm_nt(grad_att, e_ref[r, pair].reshape(2 * seq, seq))
        for i in range(2):
            place = slice(r * seq, (r + 1) * seq)
            own_rows, own_cols = slice(i * head, (i + 1) * head), slice(i * seq, (i + 1) * seq)
            for j, (grad, factor) in enumerate(((grad_q, head ** (-0.5)), (grad_k, math.log(2.0)), (grad_v, None))):
                first = j * width + (2 * p + i) * head
                mine = grad[own_rows, own_cols]
                proj_ref[first : first + head, place] = (mine if factor is None else mine * factor).astype(BF)
    gn_ref[...] = mm(w_ref[...], proj_ref[...])
    for r in range(rows):
        norm_cat[:, r * seq : (r + 1) * seq] = norm_ref[r]
    w_acc[...] += mm_nt(norm_cat[...], proj_ref[...])

    spots = tiles(seq, LANES)
    for r in range(rows):
        wide = [slice(r * seq + t.start, r * seq + t.stop) for t in spots]
        scales = []
        for t in spots:
            n, scale = norm_columns(mc_ref[r, :, t])
            n_ref[r, :, t] = n
            scales.append(scale)
        mean_e = [jnp.zeros((8, LANES), F32) for _ in spots]
        mean_en = [jnp.zeros((8, LANES), F32) for _ in spots]
        for d in tiles(width, 32):
            column = col_ref[3, d]
            gain_sum, shift_sum = acc_ref[3, d], acc_ref[4, d]
            for i, t in enumerate(spots):
                grad_n = gn_ref[d, wide[i]]
                product = grad_n * n_ref[r, d, t]
                gain_sum += product
                shift_sum += grad_n
                mean_e[i] += fold(grad_n * column)
                mean_en[i] += fold(product * column)
            acc_ref[3, d] = gain_sum
            acc_ref[4, d] = shift_sum
        for i, t in enumerate(spots):
            me = jnp.sum(mean_e[i], axis=0, keepdims=True) * (1.0 / width)
            men = jnp.sum(mean_en[i], axis=0, keepdims=True) * (1.0 / width)
            for d in tiles(width, 64):
                e = gn_ref[d, wide[i]] * col_ref[3, d]
                g_ref[r, d, t] = gm_ref[r, d, t] + scales[i] * (e - me - n_ref[r, d, t] * men)
        links, next_links = aux_ref[r, 0:1], aux_ref[r, 1:2]
        for d in tiles(width, 32):
            g = g_ref[r, d]
            base = x_ref[r, d].astype(F32)
            before = pltpu.roll(g, 1, 1) * links
            after = pltpu.roll(g, seq - 1, 1) * next_links
            acc_ref[0, d] += fold_lanes(base * after)
            acc_ref[1, d] += fold_lanes(base * g)
            acc_ref[2, d] += fold_lanes(base * before)
            conv0, conv1, conv2 = [twice(col_ref[i, d], seq) for i in range(3)]
            turn_ref[r, d] = (g + conv1 * g + conv0 * after + conv2 * before).astype(BF)
        ig_ref[r] = turn_ref[r].T

    @pl.when(step == pl.num_programs(0) - 1)
    def _():
        gs_ref[...] = other_ref[...]
        for i in range(5):
            gs_ref[i : i + 1] += jnp.sum(acc_ref[i].T, axis=0, keepdims=True)
        groups = len(gw_refs)
        for i in range(pieces):
            here = pl.ds(pl.multiple_of(index_ref[i] * own, 16), own)
            gw_refs[i % groups][i // groups] = w_acc[here, :].astype(BF)


def in_hbm(values):
    return pltpu.with_memory_space_constraint(values, pltpu.HBM)


def by_row(shape, rows, first=0):
    tail = tuple(shape[1:])
    return pl.BlockSpec((rows,) + tail, lambda i, *_: (i + first,) + (0,) * len(tail))


def whole(shape):
    place = (0,) * len(shape)
    return pl.BlockSpec(tuple(shape), lambda i, *_: place, pipeline_mode=pl.Buffered(1))


def step_rows(count, most):
    return max(r for r in range(1, most + 1) if count % r == 0)


def call(body, name, scalars, rows, row_args, args, row_outs, outs, scratch, span=None, into=None, near=(), only=None):
    first, count = span or (0, row_args[0].shape[0])
    skip = first // rows
    total = row_args[0].shape[0]

    def spec_of(shape):
        return by_row(shape, shape[0] * rows // total, skip)

    in_specs = [spec_of(a.shape) for a in row_args]
    if only:
        tail = row_args[0].shape[2:]
        in_specs[0] = pl.BlockSpec((rows, 1) + tail, lambda i, *_: (i, only) + (0,) * len(tail))
    in_specs += [whole(a.shape) for a in args]
    aliases = {}
    if into is not None:
        in_specs.append(pl.BlockSpec(memory_space=pl.ANY))
        aliases = {len(scalars) + len(in_specs) - 1: 0}
    spec = pltpu.PrefetchScalarGridSpec(
        num_scalar_prefetch=len(scalars),
        grid=(count // rows,),
        in_specs=in_specs,
        out_specs=[spec_of(s) for s, _ in row_outs] + [whole(s) for s, _ in outs],
        scratch_shapes=[pltpu.VMEM(s, t) for s, t in scratch],
    )
    return pl.pallas_call(
        body,
        grid_spec=spec,
        out_shape=[(jax.ShapeDtypeStruct if "out" + str(i) in near else pltpu.HBM)(s, t) for i, (s, t) in enumerate(row_outs)]
        + [jax.ShapeDtypeStruct(s, t) for s, t in outs],
        input_output_aliases=aliases,
        compiler_params=pltpu.CompilerParams(dimension_semantics=("arbitrary",), vmem_limit_bytes=VMEM_LIMITS[name] * MIB),
        name=name,
    )(*scalars, *[a if i in near else in_hbm(a) for i, a in enumerate(row_args)], *args, *(() if into is None else (into,)))


def small_call(body, name, args, outs, scratch=()):
    return pl.pallas_call(
        body,
        out_shape=[jax.ShapeDtypeStruct(s, t) for s, t in outs],
        scratch_shapes=[pltpu.VMEM(s, t) for s, t in scratch],
        compiler_params=pltpu.CompilerParams(vmem_limit_bytes=16 * MIB),
        name=name,
    )(*args)


def run_forward(index, tokens, segment_ids, valid_len, pieces):
    count, seq, width = tokens.shape
    flipped = (count, width, seq)
    rows = step_rows(count, 2)
    row_outs = [
        ((count, 5, width, seq), BF), (flipped, F32), ((count, seq, width), BF),
        ((count, HEADS, seq, seq), BF), ((count, 16, seq), F32),
    ]
    return call(
        functools.partial(forward_attention, pieces=len(pieces)), "forward_attention", (index, in_hbm(valid_len)),
        rows, (tokens,), (in_hbm(segment_ids), *pieces),
        row_outs, [((width, VECTORS), BF), ((width, 3 * width), BF)],
        [
            ((3 * width, width), BF), ((width, 3 * width + VECTORS), BF), ((5, width, LANES), F32),
            ((rows, seq, LANES), BF), ((rows, LANES, seq), BF), ((rows, seq, width), BF), ((rows, width, seq), BF),
        ],
    )


def run_feed_forward(index, five, mixed, cotangent, packed, pieces, shards):
    count, seq, width = cotangent.shape
    own = width // len(pieces)
    ff = shards * width
    groups = 2 if len(pieces) > 1 else 1
    rows = step_rows(count, 2)
    wide = rows * seq
    row_outs = [
        ((count // rows, ff, wide), BF), ((count // rows, width, wide), F32),
        ((count, width, seq), F32), ((count, width, seq), BF),
    ]
    grads = ((len(pieces) // groups, own, 2 * ff + width), BF)
    return call(
        functools.partial(feed_forward, pieces=len(pieces), shards=shards), "feed_forward", (index,),
        rows, (five, mixed, cotangent), (packed, *pieces),
        row_outs, [((8, width), F32), ((width, ff), BF)] + [grads] * groups,
        [((width, ff), BF)] + [((ff, width), BF)] * 2 + [((width, width), BF)] * 2
        + [((width, ff), F32)] * 2 + [((width, width), F32), ((2, width, LANES), F32), ((2, width, LANES), F32)]
        + [((width, wide), BF), ((width, wide), F32), ((width, wide), BF), ((width, wide), BF)]
        + [((ff, wide), BF)]
        + [((width, wide), F32), ((8, wide), F32), ((width, wide), BF)],
        near=("out3",), only=4,
    )


def run_layer_output(hidden, mixed, down, shape, into, low, high):
    steps = hidden.shape[0]
    span = (int(low * steps), int(high * steps) - int(low * steps))

    def body(*refs):
        layer_output(*refs[:3], refs[-1])

    return call(body, "layer_output", (), 1, (hidden, mixed), (down,), [(shape, BF)], [], [], span=span, into=into)[0]


def run_backward(index, weight, kept, grads, packed, other, pieces):
    count, seq, width = kept[2].shape
    own = width // pieces
    groups = 2 if pieces > 1 else 1
    rows = step_rows(count, 2)
    row_args = (*kept, *grads)
    many = len(row_args)

    def body(index_ref, *refs):
        backward(*refs[:many], index_ref, *refs[many:], pieces=pieces)

    return call(
        body, "backward", (index,), rows, row_args, (weight, packed, other),
        [((count, seq, width), BF)], [((8, width), F32)] + [((pieces // groups, own, 3 * width), BF)] * groups,
        [
            ((3 * width, rows * seq), BF), ((width, 3 * width), F32), ((width, rows * seq), BF),
            ((rows, HEADS, seq, seq), F32), ((rows, HEADS, seq, seq), BF), ((width, rows * seq), F32),
            ((5, width, LANES), F32), ((4, width, LANES), F32), ((rows, width, seq), F32), ((rows, width, seq), F32),
            ((rows, width, seq), BF),
        ],
        near=(5,),
    )


def exchange(values, axis, offset):
    size = lax.axis_size(axis)
    return lax.ppermute(values, axis, [(i, i ^ offset) for i in range(size)])


def add_halves(mine, received):
    count, own, cols = mine.shape

    def body(mine_ref, received_ref, *out_refs):
        for i, ref in enumerate(out_refs):
            ref[...] = (mine_ref[i].astype(F32) + received_ref[i].astype(F32)).astype(BF)

    return small_call(body, "add_halves", (mine, received), [((own, cols), BF)] * count)


def add_wide(*items):
    return tree_sum(item.astype(F32) for item in items)


def store_high_low(ref, cols, values):
    high = values.astype(BF)
    low = (values - high.astype(F32)).astype(BF)
    ref[:, cols:] = jnp.concatenate([high, low, jnp.zeros((ref.shape[0] - 16, LANES), BF)], axis=0)


def load_high_low(ref, cols):
    both = ref[:16, cols:].astype(F32)
    return both[:8] + both[8:]


def add_halves_and_sums(index, mine, received, sums, received_sums):
    count, own, cols = mine.shape
    width = sums.shape[1]

    def body(index_ref, mine_ref, received_ref, sums_ref, received_sums_ref, *out_refs):
        total = sums_ref[...] + received_sums_ref[...]
        for i, ref in enumerate(out_refs):
            ref[:, :cols] = (mine_ref[i].astype(F32) + received_ref[i].astype(F32)).astype(BF)
            turned = pltpu.roll(total, lax.rem(width - index_ref[2 * i] * own, width), 1)[:, :LANES]
            store_high_low(ref, cols, turned)

    spec = pltpu.PrefetchScalarGridSpec(
        num_scalar_prefetch=1, grid=(1,),
        in_specs=[whole(a.shape) for a in (mine, received, sums, received_sums)],
        out_specs=[whole((own, cols + LANES))] * count,
    )
    return pl.pallas_call(
        body, grid_spec=spec, out_shape=[jax.ShapeDtypeStruct((own, cols + LANES), BF)] * count,
        compiler_params=pltpu.CompilerParams(vmem_limit_bytes=16 * MIB), name="add_halves_and_sums",
    )(index, mine, received, sums, received_sums)


def add_packed(name, items):
    cols = items[0].shape[1] - LANES

    def body(*refs):
        out_ref = refs[-1]
        out_ref[:, :cols] = tree_sum(ref[:, :cols].astype(F32) for ref in refs[:-1]).astype(BF)
        store_high_low(out_ref, cols, tree_sum(load_high_low(ref, cols) for ref in refs[:-1]))

    return small_call(body, name, items, [(items[0].shape, BF)])[0]


def add_last(items):
    own, cols = items[0].shape[0], items[0].shape[1] - LANES

    def body(*refs):
        ins, outs = refs[: len(items)], refs[len(items) :]
        outs[0][...] = tree_sum(ref[:, :cols].astype(F32) for ref in ins)
        vectors = tree_sum(load_high_low(ref, cols) for ref in ins)
        outs[1][...] = vectors[0:3, :own]
        for i in range(4):
            outs[2 + i][...] = vectors[3 + i : 4 + i, :own]

    return small_call(body, "add_last", items, [((own, cols), F32), ((3, own), F32)] + [((1, own), F32)] * 4)


def direct_plan(tokens, segment_ids, valid_len, qkv_weight, out_weight, up_weight, down_weight, conv_weight, vectors, cotangent):
    count, seq, width = tokens.shape
    own, ffs = up_weight.shape
    dp, mp = lax.axis_size("dp"), lax.axis_size("mp")
    me = lax.axis_index("dp")
    offsets = [2 * p for p in range(dp // 2)]
    index = jnp.stack([me ^ (p ^ c) for p in offsets for c in range(2)]).astype(jnp.int32)
    narrow, ff_own = small_call(
        pack_weights, "pack_weights",
        [in_hbm(a) for a in (qkv_weight, up_weight, down_weight, conv_weight, *[v.reshape(1, own) for v in vectors])],
        [((own, 3 * width + VECTORS), BF), ((2 * own, ffs), BF)], [((VECTORS, VECTORS), F32)],
    )
    plane = [narrow] + [exchange(narrow, "dp", p) for p in offsets[1:]]
    shards = [ff_own] + [exchange(ff_own, "mp", j) for j in range(1, mp)]
    pieces = [piece for a in plane for piece in (a, exchange(a, "dp", 1))]
    column = jnp.concatenate(shards + [out_weight], axis=0)
    columns = [column] + [exchange(column, "dp", p) for p in offsets[1:]]
    five, mixed, v, raised, facts, packed, weight = run_forward(
        index, tokens, segment_ids, valid_len, pieces
    )
    columns, five = lax.optimization_barrier((columns, five))
    pieces = [piece for a in columns for piece in (a, exchange(a, "dp", 1))]
    hidden, mixed_attn, grad_mixed, grad_att, sums2, down, mine, theirs = run_feed_forward(
        index, five, mixed, cotangent, packed, pieces, mp
    )
    received = exchange(theirs, "dp", 1)
    shape = cotangent.shape
    layer_out = run_layer_output(hidden, mixed_attn, down, shape, None, 0, 0.34)
    received, layer_out = lax.optimization_barrier((received, layer_out))
    parts = list(add_halves(mine, received))
    parts[0], grad_att = lax.optimization_barrier((parts[0], grad_att))
    plane = [parts[0]] + [exchange(parts[i], "dp", p) for i, p in enumerate(offsets) if i]
    kept = (five, mixed, v, raised, facts)
    input_grad, sums, mine_a, theirs_a = run_backward(
        index, weight, kept, (grad_att, grad_mixed), packed, sums2, dp
    )
    plane, theirs_a, sums = lax.optimization_barrier((plane, theirs_a, sums))
    received_a = exchange(theirs_a, "dp", 1)
    received_s = exchange(sums, "dp", 1)
    total = add_wide(*plane).astype(BF)
    total, received_s = lax.optimization_barrier((total, received_s))
    part = 2 * ffs
    near = jnp.concatenate([total[:, :part], total[:, 2 * part : 3 * part]], axis=1)
    out_part = total[:, 4 * part :]
    far = jnp.concatenate([total[:, part : 2 * part], total[:, 3 * part :]], axis=1)
    parts = list(add_halves_and_sums(index, mine_a, received_a, sums, received_s))
    parts[0], hidden, layer_out = lax.optimization_barrier((parts[0], hidden, layer_out))
    plane_a = [parts[0]] + [exchange(parts[i], "dp", p) for i, p in enumerate(offsets) if i]
    received_f = exchange(far, "mp", 1)
    layer_out = run_layer_output(hidden, mixed_attn, down, shape, layer_out, 0.34, 0.67)
    plane_a, layer_out = lax.optimization_barrier((plane_a, layer_out))
    total = add_packed("add_plane", plane_a)
    received_1 = exchange(total, "mp", 1)
    received_f, _ = lax.optimization_barrier((received_f, total))
    near_sum = add_wide(near, received_f[:, : 2 * part])
    out_sum = lax.optimization_barrier(add_wide(out_part, received_f[:, 2 * part :]).astype(BF))
    keep = near_sum[:, :part]
    send = jnp.concatenate([near_sum[:, part:].astype(BF), out_sum], axis=1)
    received_n = exchange(send, "mp", 2)
    layer_out, _ = lax.optimization_barrier((layer_out, send))
    layer_out = run_layer_output(hidden, mixed_attn, down, shape, layer_out, 0.67, 0.84)
    received_1, layer_out = lax.optimization_barrier((received_1, layer_out))
    total = add_packed("add_near", (total, received_1))
    received_2 = exchange(total, "mp", 2)
    layer_out, received_n, _ = lax.optimization_barrier((layer_out, received_n, total))
    layer_out = run_layer_output(hidden, mixed_attn, down, shape, layer_out, 0.84, 1)
    received_2, layer_out = lax.optimization_barrier((received_2, layer_out))
    grad_up = keep[:, :ffs] + received_n[:, :ffs].astype(F32)
    grad_down = keep[:, ffs:] + received_n[:, ffs : 2 * ffs].astype(F32)
    grad_out = add_wide(out_sum, received_n[:, 2 * ffs :])
    grad_qkv, grad_conv, *grads = add_last((total, received_2))
    return (layer_out, input_grad, grad_qkv, grad_out, grad_up, grad_down, grad_conv, *[g.reshape(own) for g in grads])


def gathered_plan(tokens, segment_ids, valid_len, qkv_weight, out_weight, up_weight, down_weight, conv_weight, vectors, cotangent):
    count, seq, width = tokens.shape
    own = qkv_weight.shape[0]
    dp = width // own
    columns = jnp.stack([conv_weight[0], conv_weight[1], conv_weight[2], *vectors], axis=1)
    narrow = jnp.concatenate([qkv_weight, jnp.pad(columns, ((0, 0), (0, VECTORS - 7))), out_weight], axis=1)
    wide = lax.all_gather(narrow, "dp", axis=0, tiled=True)
    both = lax.all_gather(jnp.concatenate([up_weight, down_weight], axis=0), "mp", axis=1, tiled=True)
    ff = both.shape[1]
    shards = ff // width
    both = lax.all_gather(both, "dp", axis=0).reshape(dp, 2, own, shards, width)
    both = both.transpose(3, 1, 0, 2, 4).reshape(2 * ff, width)
    column = jnp.concatenate([both, wide[:, 3 * width + VECTORS :]], axis=0)
    index = jnp.zeros((1,), jnp.int32)
    five, mixed, v, raised, facts, packed, weight = run_forward(
        index, tokens, segment_ids, valid_len, [wide[:, : 3 * width + VECTORS]]
    )
    hidden, mixed_attn, grad_mixed, grad_att, sums2, down, grads = run_feed_forward(
        index, five, mixed, cotangent, packed, [column], shards
    )
    kept = (five, mixed, v, raised, facts)
    layer_out = run_layer_output(hidden, mixed_attn, down, cotangent.shape, None, 0, 1)
    input_grad, sums, grad_qkv = run_backward(index, weight, kept, (grad_att, grad_mixed), packed, sums2, 1)
    grad_ff = grads[0, :, : 2 * ff].reshape(width, shards, 2, width).transpose(0, 2, 1, 3).reshape(width, 2 * ff)
    grad_ff = lax.psum_scatter(grad_ff, "dp", scatter_dimension=0, tiled=True).reshape(own, 2, ff)
    grad_ff = lax.psum_scatter(grad_ff, "mp", scatter_dimension=2, tiled=True).astype(F32)
    grad_attn = jnp.concatenate([grad_qkv[0], grads[0, :, 2 * ff :]], axis=1)
    grad_attn = lax.psum_scatter(grad_attn, "dp", scatter_dimension=0, tiled=True)
    grad_attn = lax.psum(grad_attn, "mp").astype(F32)
    sums = lax.psum(sums, ("dp", "mp"))
    sums = lax.dynamic_slice_in_dim(sums, lax.axis_index("dp") * own, own, axis=1)
    return (
        layer_out, input_grad, grad_attn[:, : 3 * width], grad_attn[:, 3 * width :],
        grad_ff[:, 0], grad_ff[:, 1], sums[0:3], sums[3], sums[4], sums[5], sums[6],
    )


def on_device(
    tokens, segment_ids, valid_len, qkv_weight, out_weight, up_weight, down_weight, conv_weight,
    ln1_gain, ln1_shift, ln2_gain, ln2_shift, cotangent,
):
    own, ffs = up_weight.shape
    direct = own % 16 == 0 and ffs == tokens.shape[2] and own <= VECTORS and lax.axis_size("mp") == 4
    plan = direct_plan if direct else gathered_plan
    return plan(
        tokens, segment_ids, valid_len, qkv_weight, out_weight, up_weight, down_weight, conv_weight,
        (ln1_gain, ln1_shift, ln2_gain, ln2_shift), cotangent,
    )


def solution(mesh):
    rows = P(("dp", "mp"), None, None)
    weights = (P("dp", None), P("dp", None), P("dp", "mp"), P("dp", "mp"), P(None, "dp"))
    vectors = (P("dp"),) * 4
    return jax.shard_map(
        on_device,
        mesh=mesh,
        in_specs=(rows, P(("dp", "mp"), None), P(("dp", "mp"))) + weights + vectors + (rows,),
        out_specs=(rows, rows) + weights + vectors,
        check_vma=False,
    )
```

```python
import functools
import math

import jax
import jax.numpy as jnp
from jax import lax
from jax.experimental import pallas as pl
from jax.experimental.pallas import tpu as pltpu
from jax.sharding import PartitionSpec as P

HEADS = 6
VECTORS = 128
LANES = 128
BF = jnp.bfloat16
F32 = jnp.float32
MIB = 1024 * 1024
VMEM_LIMITS = dict(forward_attention=32, feed_forward=40, backward=42, layer_output=16)


def mm(lhs, rhs):
    return lax.dot_general(lhs, rhs, (((1,), (0,)), ((), ())), preferred_element_type=F32)


def mm_nt(lhs, rhs):
    return lax.dot_general(lhs, rhs, (((1,), (1,)), ((), ())), preferred_element_type=F32)


def tree_sum(items):
    items = list(items)
    while len(items) > 1:
        items = [a + b for a, b in zip(items[::2], items[1::2])]
    return items[0]


def pack_weights(qkv_ref, up_ref, down_ref, conv_ref, g1_ref, s1_ref, g2_ref, s2_ref, narrow_ref, ff_ref, rows_ref):
    own, ffs = up_ref.shape
    rows_ref[...] = jnp.zeros_like(rows_ref)
    rows_ref[0:3, :own] = conv_ref[...].astype(F32)
    for i, ref in enumerate((g1_ref, s1_ref, g2_ref, s2_ref)):
        rows_ref[3 + i : 4 + i, :own] = ref[...].astype(F32)
    wide = qkv_ref.shape[1]
    narrow_ref[:, :wide] = qkv_ref[...]
    narrow_ref[:, wide:] = rows_ref[...].T[:own].astype(BF)
    ff_ref[:own] = up_ref[...]
    ff_ref[own:] = down_ref[...]


def tiles(total, size):
    return [slice(at, at + size) for at in range(0, total, size)]


def weave(*strands):
    strands = [strand for strand in strands if strand]
    total = sum(len(strand) for strand in strands)
    pieces = [((i + 0.5) / len(strand), j, piece) for j, strand in enumerate(strands) for i, piece in enumerate(strand)]
    assert len(pieces) == total
    for _, _, piece in sorted(pieces, key=lambda item: item[:2]):
        piece()


def twice(tile, lanes):
    return jnp.concatenate([tile] * (lanes // LANES), axis=1)


def load_columns(packed_ref, col_ref, places):
    for i, place in enumerate(places):
        column = packed_ref[:, place : place + 1].astype(F32)
        col_ref[i] = jnp.broadcast_to(column, (column.shape[0], LANES))


def column_mean(values):
    return jnp.sum(values, axis=0, keepdims=True) * (1.0 / values.shape[0])


def norm_columns(values):
    centred = values - column_mean(values)
    scale = lax.rsqrt(column_mean(centred * centred) + 1e-06)
    return centred * scale, scale


def fold(values):
    rows, lanes = values.shape
    return jnp.sum(values.reshape(rows // 8, 8, lanes), axis=0)


def fold_lanes(values):
    return sum(values[:, t] for t in tiles(values.shape[1], LANES))


def forward_attention(index_ref, len_ref, tok_ref, seg_ref, *refs, pieces):
    cores = 2 if pieces > 1 else 1
    piece_refs = refs[:cores]
    (
        five_ref, mc_ref, v_ref, e_ref, facts_ref, packed_ref, w_ref,
        wt_ref, wide_ref, col_ref, key_mask_ref, query_mask_ref, key_ref, value_ref,
    ) = refs[cores:]
    x_ref, norm_ref, q_ref, k_ref, att_ref = [five_ref.at[:, i] for i in range(5)]
    aux_ref, inv_ref = facts_ref.at[:, :8], facts_ref.at[:, 8:]
    rows, seq, width = tok_ref.shape
    head = width // HEADS
    step = pl.program_id(0)

    @pl.when(step == 0)
    def _():
        own = width // pieces
        for i in range(pieces):
            here = pl.ds(pl.multiple_of(index_ref[i] * own, 16), own)
            wide_ref[here, :] = piece_refs[i % cores][i // cores * own : (i // cores + 1) * own]
        w_ref[...] = wide_ref[:, : 3 * width]
        wt_ref[...] = wide_ref[:, : 3 * width].T
        packed_ref[...] = wide_ref[:, 3 * width :]
        load_columns(packed_ref, col_ref, range(5))

    place = lax.broadcasted_iota(jnp.int32, (1, seq), 1)
    zero = jnp.zeros((head, seq), BF)

    def preparation(r):
        known = {}

        def start():
            segs = seg_ref[pl.ds(step * rows + r, 1), :].astype(F32)
            valid = place < len_ref[step * rows + r]
            number = jnp.where(valid, segs, -1.0)
            links = jnp.where(valid & (place > 0) & (number == pltpu.roll(number, 1, 1)), 1.0, 0.0)
            next_links = jnp.where(place < seq - 1, pltpu.roll(links, seq - 1, 1), 0.0)
            none = jnp.zeros_like(links)
            aux = jnp.concatenate([links, next_links, number, none, none, none, none, none], axis=0)
            aux_ref[r] = aux
            x_ref[r] = tok_ref[r].T
            known.update(segs=segs, links=links, next_links=next_links, key_number=aux.T[:, 2:3])

        def mask():
            number = known["key_number"]
            lane = lax.broadcasted_iota(jnp.int32, (seq, LANES), 1)
            itself = lax.broadcasted_iota(jnp.int32, (seq, LANES), 0) - (seq - LANES)
            chosen = (lane.astype(F32) == number) | ((number < 0.0) & (lane == itself))
            key_mask_ref[r] = jnp.where(chosen, 1.0, 0.0).astype(BF)
            slot = lax.broadcasted_iota(jnp.int32, (LANES, seq), 0)
            itself = lax.broadcasted_iota(jnp.int32, (LANES, seq), 1) - (seq - LANES)
            open_to = (slot.astype(F32) == known["segs"]) | ((slot >= LANES // 2) & (slot == itself))
            query_mask_ref[r] = jnp.where(open_to, 0.0, -1e30).astype(BF)

        def conv(t):
            base = x_ref[r, t].astype(F32)
            before = pltpu.roll(base, 1, 1) * known["links"]
            after = pltpu.roll(base, seq - 1, 1) * known["next_links"]
            conv0, conv1, conv2 = [twice(col_ref[i, t], seq) for i in range(3)]
            mc_ref[r, t] = base + before * conv0 + base * conv1 + after * conv2

        def norm(t):
            n, _ = norm_columns(mc_ref[r, :, t])
            norm_ref[r, :, t] = (n * col_ref[3] + col_ref[4]).astype(BF)

        pieces = [start] + [functools.partial(conv, t) for t in tiles(width, 32)]
        pieces += [functools.partial(norm, t) for t in tiles(seq, LANES)]
        return pieces + [mask]

    def project():
        normed = jnp.concatenate([norm_ref[r] for r in range(rows)], axis=1)
        for i, ref in enumerate((q_ref, k_ref, value_ref)):
            part = mm(wt_ref[i * width : (i + 1) * width], normed)
            part = (part * (head ** (-0.5) * math.log2(math.e)) if i == 0 else part).astype(BF)
            for r in range(rows):
                ref[r] = part[:, r * seq : (r + 1) * seq]
        for r in range(rows):
            key_ref[r] = k_ref[r].T
            v_ref[r] = value_ref[r].T

    def scores(r, p):
        low, high = [q_ref[r, h * head : (h + 1) * head] for h in (2 * p, 2 * p + 1)]
        both = jnp.concatenate([jnp.concatenate([low, zero], axis=1), jnp.concatenate([zero, high], axis=1)], axis=0)
        keys = jnp.concatenate([key_ref[r, :, 2 * p * head : 2 * (p + 1) * head], key_mask_ref[r]], axis=1)
        masks = jnp.concatenate([query_mask_ref[r], query_mask_ref[r]], axis=1)
        return mm(keys, jnp.concatenate([both, masks], axis=0))

    def attended(r, p):
        both = jnp.concatenate([e_ref[r, 2 * p], e_ref[r, 2 * p + 1]], axis=1)
        product = mm(value_ref[r, 2 * p * head : 2 * (p + 1) * head], both)
        parts = []
        for i in range(2):
            att = product[i * head : (i + 1) * head, i * seq : (i + 1) * seq] * inv_ref[r, 2 * p + i : 2 * p + i + 1]
            parts.append(att.astype(BF))
        return jnp.concatenate(parts, axis=0)

    def soften(r, p, product):
        for i in range(2):
            for t in tiles(seq, LANES):
                masked = product[:, i * seq + t.start : i * seq + t.stop]
                raised = jnp.exp2(masked - jnp.max(masked, axis=0, keepdims=True))
                inv_ref[r, 2 * p + i : 2 * p + i + 1, t] = 1.0 / jnp.sum(raised, axis=0, keepdims=True)
                e_ref[r, 2 * p + i, :, t] = raised.astype(BF)

    weave(*[preparation(r) for r in range(rows)])
    project()
    work = [(r, p) for r in range(rows) for p in range(HEADS // 2)]
    current, last = scores(*work[0]), None
    for at, (r, p) in enumerate(work):
        following = scores(*work[at + 1]) if at + 1 < len(work) else None
        finished = attended(*last) if last else None
        soften(r, p, current)
        if last:
            att_ref[last[0], 2 * last[1] * head : 2 * (last[1] + 1) * head] = finished
        current, last = following, (r, p)
    att_ref[last[0], 2 * last[1] * head : 2 * (last[1] + 1) * head] = attended(*last)


def gelu_parts(x):
    cdf = 0.5 * lax.erf(x * math.sqrt(0.5)) + 0.5
    bell = jnp.exp2(x * x * (-0.5 / math.log(2.0)) - 0.5 * math.log2(2.0 * math.pi))
    return x * cdf, cdf + x * bell


def feed_forward(index_ref, five_ref, mc_ref, ct_ref, packed_ref, *refs, pieces, shards):
    att_ref = five_ref.at[:, 0]
    groups = 2 if pieces > 1 else 1
    piece_refs = refs[:groups]
    hidden_out, mixed_out, gm_ref, ga_ref, gs_ref, down_ref = refs[groups : groups + 6]
    hidden_ref, mixed_ref = hidden_out.at[0], mixed_out.at[0]
    gw_refs = refs[groups + 6 : 2 * groups + 6]
    (
        up_ref, upt_ref, downt_ref, out_ref, outt_ref, up_acc, down_acc, out_acc, col_acc, col_ref,
        n_ref, norm_ref, ctt_ref, gp_ref, gn_ref, scale_ref, branch_ref,
    ) = refs[2 * groups + 6 :]
    rows, seq, width = ct_ref.shape
    ff = up_ref.shape[1]
    ffs = ff // shards
    own = width // pieces
    step = pl.program_id(0)

    @pl.when(step == 0)
    def _():
        for acc in (up_acc, down_acc, out_acc, col_acc):
            acc[...] = jnp.zeros_like(acc)
        for i in range(pieces):
            here = pl.ds(pl.multiple_of(index_ref[i] * own, 16), own)
            ref, first = piece_refs[i % groups], i // groups * (2 * shards + 1) * own
            for j in range(shards):
                at = first + 2 * j * own
                up_ref[here, j * ffs : (j + 1) * ffs] = ref[at : at + own]
                down_ref[here, j * ffs : (j + 1) * ffs] = ref[at + own : at + 2 * own]
            at = first + 2 * shards * own
            out_ref[here, :] = ref[at : at + own]
        upt_ref[...] = up_ref[...].T
        downt_ref[...] = down_ref[...].T
        outt_ref[...] = out_ref[...].T
        load_columns(packed_ref, col_ref, (5, 6))

    def lanes_of(r):
        return slice(r * seq, (r + 1) * seq)

    def spots_of(r):
        return [slice(at, at + LANES) for at in range(r * seq, (r + 1) * seq, LANES)]

    def preparation(r):
        lanes = lanes_of(r)

        def turn():
            ctt_ref[:, lanes] = ct_ref[r].T

        def norm(t):
            n, scale = norm_columns(mixed_ref[:, t])
            n_ref[:, t] = n
            scale_ref[0:1, t] = scale
            norm_ref[:, t] = (n * col_ref[0] + col_ref[1]).astype(BF)

        return [turn] + [functools.partial(norm, t) for t in spots_of(r)]

    def activation(block):
        pre = mm(upt_ref[block], norm_ref[...])
        grad_hidden = mm(downt_ref[block], ctt_ref[...])
        for low in range(0, block.stop - block.start, 16):
            part = slice(low, low + 16)
            here = slice(block.start + low, block.start + low + 16)
            hidden, slope = gelu_parts(pre[part])
            hidden_ref[here] = hidden.astype(BF)
            gp_ref[here] = (grad_hidden[part] * slope).astype(BF)

    def norm_back(r):
        spots = spots_of(r)
        mean_e = [jnp.zeros((8, LANES), F32) for _ in spots]
        mean_en = [jnp.zeros((8, LANES), F32) for _ in spots]
        means = []

        def sums(d):
            column = col_ref[0, d]
            gain_sum, shift_sum = col_acc[0, d], col_acc[1, d]
            for i, t in enumerate(spots):
                grad_n = gn_ref[d, t]
                product = grad_n * n_ref[d, t]
                gain_sum += product
                shift_sum += grad_n
                mean_e[i] += fold(grad_n * column)
                mean_en[i] += fold(product * column)
            col_acc[0, d] = gain_sum
            col_acc[1, d] = shift_sum

        def finish():
            for i in range(len(spots)):
                me = jnp.sum(mean_e[i], axis=0, keepdims=True) * (1.0 / width)
                men = jnp.sum(mean_en[i], axis=0, keepdims=True) * (1.0 / width)
                means.append((me, men))

        def apply(d):
            for i, t in enumerate(spots):
                me, men = means[i]
                change = scale_ref[0:1, t] * (gn_ref[d, t] * col_ref[0, d] - me - n_ref[d, t] * men)
                grad_mixed = ctt_ref[d, t].astype(F32) + change
                gm_ref[r, d, i * LANES : (i + 1) * LANES] = grad_mixed
                branch_ref[d, t] = grad_mixed.astype(BF)

        pieces = [functools.partial(sums, d) for d in tiles(width, 32)] + [finish]
        return pieces + [functools.partial(apply, d) for d in tiles(width, 32)]

    attended = jnp.concatenate([att_ref[r] for r in range(rows)], axis=1)
    branch = mm(outt_ref[...], attended)
    for r in range(rows):
        mixed_ref[:, lanes_of(r)] = mc_ref[r] + branch[:, lanes_of(r)]
    weave(*[preparation(r) for r in range(rows)])
    for block in tiles(ff, 128):
        activation(block)
    gn_ref[...] = mm(up_ref[...], gp_ref[...])
    down_acc[...] += mm_nt(ctt_ref[...], hidden_ref[...])
    up_acc[...] += mm_nt(norm_ref[...], gp_ref[...])
    weave(*[norm_back(r) for r in range(rows)])
    grad_attended = mm(out_ref[...], branch_ref[...]).astype(BF)
    for r in range(rows):
        ga_ref[r] = grad_attended[:, lanes_of(r)]
    out_acc[...] += mm_nt(attended, branch_ref[...])

    @pl.when(step == pl.num_programs(0) - 1)
    def _():
        for i in range(pieces):
            here = pl.ds(pl.multiple_of(index_ref[i] * own, 16), own)
            place = gw_refs[i % groups]
            for j in range(shards):
                cols = slice(j * ffs, (j + 1) * ffs)
                place[i // groups, :, 2 * j * ffs : (2 * j + 1) * ffs] = up_acc[here, cols].astype(BF)
                place[i // groups, :, (2 * j + 1) * ffs : (2 * j + 2) * ffs] = down_acc[here, cols].astype(BF)
            place[i // groups, :, 2 * ff :] = out_acc[here, :].astype(BF)
        gs_ref[...] = jnp.zeros_like(gs_ref)
        for i in range(2):
            gs_ref[5 + i : 6 + i] = jnp.sum(col_acc[i].T, axis=0, keepdims=True)


def layer_output(hidden_ref, mixed_ref, down_ref, lo_ref):
    rows, seq, _ = lo_ref.shape
    total = (mixed_ref[0] + mm(down_ref[...], hidden_ref[0])).astype(BF)
    for r in range(rows):
        lo_ref[r] = total[:, r * seq : (r + 1) * seq].T


def backward(
    five_ref, mc_ref, v_ref, e_ref, facts_ref, ga_ref, gm_ref, index_ref, w_ref, packed_ref, other_ref, ig_ref, gs_ref, *refs, pieces,
):
    x_ref, norm_ref, q_ref, k_ref, att_ref = [five_ref.at[:, i] for i in range(5)]
    aux_ref, inv_ref = facts_ref.at[:, :8], facts_ref.at[:, 8:]
    gw_refs = refs[:-11]
    (
        proj_ref, w_acc, norm_cat, soft_ref, logit_ref, gn_ref, acc_ref, col_ref, n_ref, g_ref, turn_ref
    ) = refs[-11:]
    rows, seq, width = v_ref.shape
    own = width // pieces
    head = width // HEADS
    step = pl.program_id(0)

    @pl.when(step == 0)
    def _():
        w_acc[...] = jnp.zeros_like(w_acc)
        acc_ref[...] = jnp.zeros_like(acc_ref)
        load_columns(packed_ref, col_ref, range(4))

    zero = jnp.zeros((head, seq), BF)
    work = [(r, p) for r in range(rows) for p in range(HEADS // 2)]

    def opening(r, p):
        grads, inners = [], []
        for h in (2 * p, 2 * p + 1):
            part = slice(h * head, (h + 1) * head)
            grad_att = ga_ref[r, part].astype(F32) * inv_ref[r, h : h + 1]
            inners.append(jnp.sum(grad_att * att_ref[r, part].astype(F32), axis=0, keepdims=True))
            grads.append(grad_att.astype(BF))
        low, high = grads
        both = jnp.concatenate([jnp.concatenate([low, zero], axis=1), jnp.concatenate([zero, high], axis=1)], axis=0)
        product = mm(v_ref[r, :, 2 * p * head : 2 * (p + 1) * head], both)
        soft_ref[r, 2 * p] = product[:, :seq]
        soft_ref[r, 2 * p + 1] = product[:, seq:]
        return jnp.concatenate(grads, axis=0), inners

    ready = opening(*work[0])
    for at, (r, p) in enumerate(work):
        grad_att, inners = ready
        if at + 1 < len(work):
            ready = opening(*work[at + 1])
        for i, h in enumerate((2 * p, 2 * p + 1)):
            for t in tiles(seq, 32):
                raised = e_ref[r, h, t].astype(F32)
                logit_ref[r, h, t] = (raised * (soft_ref[r, h, t] - inners[i])).astype(BF)
        part = slice(2 * p * head, 2 * (p + 1) * head)
        pair = slice(2 * p, 2 * p + 2)
        beside = jnp.concatenate([logit_ref[r, 2 * p], logit_ref[r, 2 * p + 1]], axis=1)
        grad_q = mm(k_ref[r, part], beside)
        grad_k = mm_nt(q_ref[r, part], logit_ref[r, pair].reshape(2 * seq, seq))
        grad_v = mm_nt(grad_att, e_ref[r, pair].reshape(2 * seq, seq))
        for i in range(2):
            place = slice(r * seq, (r + 1) * seq)
            own_rows, own_cols = slice(i * head, (i + 1) * head), slice(i * seq, (i + 1) * seq)
            for j, (grad, factor) in enumerate(((grad_q, head ** (-0.5)), (grad_k, math.log(2.0)), (grad_v, None))):
                first = j * width + (2 * p + i) * head
                mine = grad[own_rows, own_cols]
                proj_ref[first : first + head, place] = (mine if factor is None else mine * factor).astype(BF)
    gn_ref[...] = mm(w_ref[...], proj_ref[...])
    for r in range(rows):
        norm_cat[:, r * seq : (r + 1) * seq] = norm_ref[r]
    w_acc[...] += mm_nt(norm_cat[...], proj_ref[...])

    spots = tiles(seq, LANES)
    for r in range(rows):
        wide = [slice(r * seq + t.start, r * seq + t.stop) for t in spots]
        scales = []
        for t in spots:
            n, scale = norm_columns(mc_ref[r, :, t])
            n_ref[r, :, t] = n
            scales.append(scale)
        mean_e = [jnp.zeros((8, LANES), F32) for _ in spots]
        mean_en = [jnp.zeros((8, LANES), F32) for _ in spots]
        for d in tiles(width, 32):
            column = col_ref[3, d]
            gain_sum, shift_sum = acc_ref[3, d], acc_ref[4, d]
            for i, t in enumerate(spots):
                grad_n = gn_ref[d, wide[i]]
                product = grad_n * n_ref[r, d, t]
                gain_sum += product
                shift_sum += grad_n
                mean_e[i] += fold(grad_n * column)
                mean_en[i] += fold(product * column)
            acc_ref[3, d] = gain_sum
            acc_ref[4, d] = shift_sum
        for i, t in enumerate(spots):
            me = jnp.sum(mean_e[i], axis=0, keepdims=True) * (1.0 / width)
            men = jnp.sum(mean_en[i], axis=0, keepdims=True) * (1.0 / width)
            for d in tiles(width, 64):
                e = gn_ref[d, wide[i]] * col_ref[3, d]
                g_ref[r, d, t] = gm_ref[r, d, t] + scales[i] * (e - me - n_ref[r, d, t] * men)
        links, next_links = aux_ref[r, 0:1], aux_ref[r, 1:2]
        for d in tiles(width, 32):
            g = g_ref[r, d]
            base = x_ref[r, d].astype(F32)
            before = pltpu.roll(g, 1, 1) * links
            after = pltpu.roll(g, seq - 1, 1) * next_links
            acc_ref[0, d] += fold_lanes(base * after)
            acc_ref[1, d] += fold_lanes(base * g)
            acc_ref[2, d] += fold_lanes(base * before)
            conv0, conv1, conv2 = [twice(col_ref[i, d], seq) for i in range(3)]
            turn_ref[r, d] = (g + conv1 * g + conv0 * after + conv2 * before).astype(BF)
        ig_ref[r] = turn_ref[r].T

    @pl.when(step == pl.num_programs(0) - 1)
    def _():
        gs_ref[...] = other_ref[...]
        for i in range(5):
            gs_ref[i : i + 1] += jnp.sum(acc_ref[i].T, axis=0, keepdims=True)
        groups = len(gw_refs)
        for i in range(pieces):
            here = pl.ds(pl.multiple_of(index_ref[i] * own, 16), own)
            gw_refs[i % groups][i // groups] = w_acc[here, :].astype(BF)


def in_hbm(values):
    return pltpu.with_memory_space_constraint(values, pltpu.HBM)


def by_row(shape, rows, first=0):
    tail = tuple(shape[1:])
    return pl.BlockSpec((rows,) + tail, lambda i, *_: (i + first,) + (0,) * len(tail))


def whole(shape):
    place = (0,) * len(shape)
    return pl.BlockSpec(tuple(shape), lambda i, *_: place, pipeline_mode=pl.Buffered(1))


def step_rows(count, most):
    return max(r for r in range(1, most + 1) if count % r == 0)


def call(body, name, scalars, rows, row_args, args, row_outs, outs, scratch, span=None, into=None, near=(), only=None):
    first, count = span or (0, row_args[0].shape[0])
    skip = first // rows
    total = row_args[0].shape[0]

    def spec_of(shape):
        return by_row(shape, shape[0] * rows // total, skip)

    in_specs = [spec_of(a.shape) for a in row_args]
    if only:
        tail = row_args[0].shape[2:]
        in_specs[0] = pl.BlockSpec((rows, 1) + tail, lambda i, *_: (i, only) + (0,) * len(tail))
    in_specs += [whole(a.shape) for a in args]
    aliases = {}
    if into is not None:
        in_specs.append(pl.BlockSpec(memory_space=pl.ANY))
        aliases = {len(scalars) + len(in_specs) - 1: 0}
    spec = pltpu.PrefetchScalarGridSpec(
        num_scalar_prefetch=len(scalars),
        grid=(count // rows,),
        in_specs=in_specs,
        out_specs=[spec_of(s) for s, _ in row_outs] + [whole(s) for s, _ in outs],
        scratch_shapes=[pltpu.VMEM(s, t) for s, t in scratch],
    )
    return pl.pallas_call(
        body,
        grid_spec=spec,
        out_shape=[(jax.ShapeDtypeStruct if "out" + str(i) in near else pltpu.HBM)(s, t) for i, (s, t) in enumerate(row_outs)]
        + [jax.ShapeDtypeStruct(s, t) for s, t in outs],
        input_output_aliases=aliases,
        compiler_params=pltpu.CompilerParams(dimension_semantics=("arbitrary",), vmem_limit_bytes=VMEM_LIMITS[name] * MIB),
        name=name,
    )(*scalars, *[a if i in near else in_hbm(a) for i, a in enumerate(row_args)], *args, *(() if into is None else (into,)))


def small_call(body, name, args, outs, scratch=()):
    return pl.pallas_call(
        body,
        out_shape=[jax.ShapeDtypeStruct(s, t) for s, t in outs],
        scratch_shapes=[pltpu.VMEM(s, t) for s, t in scratch],
        compiler_params=pltpu.CompilerParams(vmem_limit_bytes=16 * MIB),
        name=name,
    )(*args)


def run_forward(index, tokens, segment_ids, valid_len, pieces):
    count, seq, width = tokens.shape
    flipped = (count, width, seq)
    rows = step_rows(count, 3)
    row_outs = [
        ((count, 5, width, seq), BF), (flipped, F32), ((count, seq, width), BF),
        ((count, HEADS, seq, seq), BF), ((count, 16, seq), F32),
    ]
    return call(
        functools.partial(forward_attention, pieces=index.shape[0]), "forward_attention", (index, in_hbm(valid_len)),
        rows, (tokens,), (in_hbm(segment_ids), *pieces),
        row_outs, [((width, VECTORS), BF), ((width, 3 * width), BF)],
        [
            ((3 * width, width), BF), ((width, 3 * width + VECTORS), BF), ((5, width, LANES), F32),
            ((rows, seq, LANES), BF), ((rows, LANES, seq), BF), ((rows, seq, width), BF), ((rows, width, seq), BF),
        ],
    )


def run_feed_forward(index, five, mixed, cotangent, packed, pieces, shards):
    count, seq, width = cotangent.shape
    own = width // index.shape[0]
    ff = shards * width
    groups = 2 if index.shape[0] > 1 else 1
    rows = step_rows(count, 2)
    wide = rows * seq
    row_outs = [
        ((count // rows, ff, wide), BF), ((count // rows, width, wide), F32),
        ((count, width, seq), F32), ((count, width, seq), BF),
    ]
    grads = ((index.shape[0] // groups, own, 2 * ff + width), BF)
    return call(
        functools.partial(feed_forward, pieces=index.shape[0], shards=shards), "feed_forward", (index,),
        rows, (five, mixed, cotangent), (packed, *pieces),
        row_outs, [((8, width), F32), ((width, ff), BF)] + [grads] * groups,
        [((width, ff), BF)] + [((ff, width), BF)] * 2 + [((width, width), BF)] * 2
        + [((width, ff), F32)] * 2 + [((width, width), F32), ((2, width, LANES), F32), ((2, width, LANES), F32)]
        + [((width, wide), F32), ((width, wide), BF), ((width, wide), BF)]
        + [((ff, wide), BF)]
        + [((width, wide), F32), ((8, wide), F32), ((width, wide), BF)],
        near=("out3",), only=4,
    )


def run_layer_output(hidden, mixed, down, shape, into, low, high):
    steps = hidden.shape[0]
    span = (int(low * steps), int(high * steps) - int(low * steps))

    def body(*refs):
        layer_output(*refs[:3], refs[-1])

    return call(body, "layer_output", (), 1, (hidden, mixed), (down,), [(shape, BF)], [], [], span=span, into=into)[0]


def run_backward(index, weight, kept, grads, packed, other, pieces):
    count, seq, width = kept[2].shape
    own = width // pieces
    groups = 2 if pieces > 1 else 1
    rows = step_rows(count, 3)
    row_args = (*kept, *grads)
    many = len(row_args)

    def body(index_ref, *refs):
        backward(*refs[:many], index_ref, *refs[many:], pieces=pieces)

    return call(
        body, "backward", (index,), rows, row_args, (weight, packed, other),
        [((count, seq, width), BF)], [((8, width), F32)] + [((pieces // groups, own, 3 * width), BF)] * groups,
        [
            ((3 * width, rows * seq), BF), ((width, 3 * width), F32), ((width, rows * seq), BF),
            ((rows, HEADS, seq, seq), F32), ((rows, HEADS, seq, seq), BF), ((width, rows * seq), F32),
            ((5, width, LANES), F32), ((4, width, LANES), F32), ((rows, width, seq), F32), ((rows, width, seq), F32),
            ((rows, width, seq), BF),
        ],
        near=(5,),
    )


def exchange(values, axis, offset):
    size = lax.axis_size(axis)
    return lax.ppermute(values, axis, [(i, i ^ offset) for i in range(size)])


def add_halves(mine, received):
    count, own, cols = mine.shape

    def body(mine_ref, received_ref, *out_refs):
        for i, ref in enumerate(out_refs):
            ref[...] = (mine_ref[i].astype(F32) + received_ref[i].astype(F32)).astype(BF)

    return small_call(body, "add_halves", (mine, received), [((own, cols), BF)] * count)


def add_wide(*items):
    return tree_sum(item.astype(F32) for item in items)


def store_high_low(ref, cols, values):
    high = values.astype(BF)
    low = (values - high.astype(F32)).astype(BF)
    ref[:, cols:] = jnp.concatenate([high, low, jnp.zeros((ref.shape[0] - 16, LANES), BF)], axis=0)


def load_high_low(ref, cols):
    both = ref[:16, cols:].astype(F32)
    return both[:8] + both[8:]


def add_halves_and_sums(index, mine, received, sums, received_sums):
    count, own, cols = mine.shape
    width = sums.shape[1]

    def body(index_ref, mine_ref, received_ref, sums_ref, received_sums_ref, *out_refs):
        total = sums_ref[...] + received_sums_ref[...]
        for i, ref in enumerate(out_refs):
            ref[:, :cols] = (mine_ref[i].astype(F32) + received_ref[i].astype(F32)).astype(BF)
            turned = pltpu.roll(total, lax.rem(width - index_ref[2 * i] * own, width), 1)[:, :LANES]
            store_high_low(ref, cols, turned)

    spec = pltpu.PrefetchScalarGridSpec(
        num_scalar_prefetch=1, grid=(1,),
        in_specs=[whole(a.shape) for a in (mine, received, sums, received_sums)],
        out_specs=[whole((own, cols + LANES))] * count,
    )
    return pl.pallas_call(
        body, grid_spec=spec, out_shape=[jax.ShapeDtypeStruct((own, cols + LANES), BF)] * count,
        compiler_params=pltpu.CompilerParams(vmem_limit_bytes=16 * MIB), name="add_halves_and_sums",
    )(index, mine, received, sums, received_sums)


def add_packed(name, items):
    cols = items[0].shape[1] - LANES

    def body(*refs):
        out_ref = refs[-1]
        out_ref[:, :cols] = tree_sum(ref[:, :cols].astype(F32) for ref in refs[:-1]).astype(BF)
        store_high_low(out_ref, cols, tree_sum(load_high_low(ref, cols) for ref in refs[:-1]))

    return small_call(body, name, items, [(items[0].shape, BF)])[0]


def add_last(items):
    own, cols = items[0].shape[0], items[0].shape[1] - LANES

    def body(*refs):
        ins, outs = refs[: len(items)], refs[len(items) :]
        outs[0][...] = tree_sum(ref[:, :cols].astype(F32) for ref in ins)
        vectors = tree_sum(load_high_low(ref, cols) for ref in ins)
        outs[1][...] = vectors[0:3, :own]
        for i in range(4):
            outs[2 + i][...] = vectors[3 + i : 4 + i, :own]

    return small_call(body, "add_last", items, [((own, cols), F32), ((3, own), F32)] + [((1, own), F32)] * 4)


def direct_plan(tokens, segment_ids, valid_len, qkv_weight, out_weight, up_weight, down_weight, conv_weight, vectors, cotangent):
    count, seq, width = tokens.shape
    own, ffs = up_weight.shape
    dp, mp = lax.axis_size("dp"), lax.axis_size("mp")
    me = lax.axis_index("dp")
    offsets = [2 * p for p in range(dp // 2)]
    index = jnp.stack([me ^ (p ^ c) for p in offsets for c in range(2)]).astype(jnp.int32)
    narrow, ff_own = small_call(
        pack_weights, "pack_weights",
        [in_hbm(a) for a in (qkv_weight, up_weight, down_weight, conv_weight, *[v.reshape(1, own) for v in vectors])],
        [((own, 3 * width + VECTORS), BF), ((2 * own, ffs), BF)], [((VECTORS, VECTORS), F32)],
    )
    pair = jnp.concatenate([ff_own, exchange(ff_own, "mp", 1)], axis=0)
    plane = jnp.concatenate([narrow] + [exchange(narrow, "dp", p) for p in offsets[1:]], axis=0)
    pieces = [plane, exchange(plane, "dp", 1)]
    column = jnp.concatenate([pair, exchange(pair, "mp", 2), out_weight], axis=0)
    columns = [column] + [exchange(column, "dp", p) for p in offsets[1:]]
    five, mixed, v, raised, facts, packed, weight = run_forward(
        index, tokens, segment_ids, valid_len, pieces
    )
    columns, five = lax.optimization_barrier((columns, five))
    columns = jnp.concatenate(columns, axis=0)
    pieces = [columns, exchange(columns, "dp", 1)]
    hidden, mixed_attn, grad_mixed, grad_att, sums2, down, mine, theirs = run_feed_forward(
        index, five, mixed, cotangent, packed, pieces, mp
    )
    received = exchange(theirs, "dp", 1)
    shape = cotangent.shape
    layer_out = run_layer_output(hidden, mixed_attn, down, shape, None, 0, 0.34)
    received, layer_out = lax.optimization_barrier((received, layer_out))
    parts = list(add_halves(mine, received))
    parts[0], grad_att = lax.optimization_barrier((parts[0], grad_att))
    plane = [parts[0]] + [exchange(parts[i], "dp", p) for i, p in enumerate(offsets) if i]
    kept = (five, mixed, v, raised, facts)
    input_grad, sums, mine_a, theirs_a = run_backward(
        index, weight, kept, (grad_att, grad_mixed), packed, sums2, dp
    )
    plane, theirs_a, sums = lax.optimization_barrier((plane, theirs_a, sums))
    received_a = exchange(theirs_a, "dp", 1)
    received_s = exchange(sums, "dp", 1)
    total = add_wide(*plane).astype(BF)
    total, received_s = lax.optimization_barrier((total, received_s))
    part = 2 * ffs
    near = jnp.concatenate([total[:, :part], total[:, 2 * part : 3 * part]], axis=1)
    out_part = total[:, 4 * part :]
    far = jnp.concatenate([total[:, part : 2 * part], total[:, 3 * part :]], axis=1)
    parts = list(add_halves_and_sums(index, mine_a, received_a, sums, received_s))
    parts[0], hidden, layer_out = lax.optimization_barrier((parts[0], hidden, layer_out))
    plane_a = [parts[0]] + [exchange(parts[i], "dp", p) for i, p in enumerate(offsets) if i]
    received_f = exchange(far, "mp", 1)
    layer_out = run_layer_output(hidden, mixed_attn, down, shape, layer_out, 0.34, 0.67)
    plane_a, layer_out = lax.optimization_barrier((plane_a, layer_out))
    total = add_packed("add_plane", plane_a)
    received_1 = exchange(total, "mp", 1)
    received_f, _ = lax.optimization_barrier((received_f, total))
    near_sum = add_wide(near, received_f[:, : 2 * part])
    out_sum = lax.optimization_barrier(add_wide(out_part, received_f[:, 2 * part :]).astype(BF))
    keep = near_sum[:, :part]
    send = jnp.concatenate([near_sum[:, part:].astype(BF), out_sum], axis=1)
    received_n = exchange(send, "mp", 2)
    layer_out, _ = lax.optimization_barrier((layer_out, send))
    layer_out = run_layer_output(hidden, mixed_attn, down, shape, layer_out, 0.67, 0.84)
    received_1, layer_out = lax.optimization_barrier((received_1, layer_out))
    total = add_packed("add_near", (total, received_1))
    received_2 = exchange(total, "mp", 2)
    layer_out, received_n, _ = lax.optimization_barrier((layer_out, received_n, total))
    layer_out = run_layer_output(hidden, mixed_attn, down, shape, layer_out, 0.84, 1)
    received_2, layer_out = lax.optimization_barrier((received_2, layer_out))
    grad_up = keep[:, :ffs] + received_n[:, :ffs].astype(F32)
    grad_down = keep[:, ffs:] + received_n[:, ffs : 2 * ffs].astype(F32)
    grad_out = add_wide(out_sum, received_n[:, 2 * ffs :])
    grad_qkv, grad_conv, *grads = add_last((total, received_2))
    return (layer_out, input_grad, grad_qkv, grad_out, grad_up, grad_down, grad_conv, *[g.reshape(own) for g in grads])


def gathered_plan(tokens, segment_ids, valid_len, qkv_weight, out_weight, up_weight, down_weight, conv_weight, vectors, cotangent):
    count, seq, width = tokens.shape
    own = qkv_weight.shape[0]
    dp = width // own
    columns = jnp.stack([conv_weight[0], conv_weight[1], conv_weight[2], *vectors], axis=1)
    narrow = jnp.concatenate([qkv_weight, jnp.pad(columns, ((0, 0), (0, VECTORS - 7))), out_weight], axis=1)
    wide = lax.all_gather(narrow, "dp", axis=0, tiled=True)
    both = lax.all_gather(jnp.concatenate([up_weight, down_weight], axis=0), "mp", axis=1, tiled=True)
    ff = both.shape[1]
    shards = ff // width
    both = lax.all_gather(both, "dp", axis=0).reshape(dp, 2, own, shards, width)
    both = both.transpose(3, 1, 0, 2, 4).reshape(2 * ff, width)
    column = jnp.concatenate([both, wide[:, 3 * width + VECTORS :]], axis=0)
    index = jnp.zeros((1,), jnp.int32)
    five, mixed, v, raised, facts, packed, weight = run_forward(
        index, tokens, segment_ids, valid_len, [wide[:, : 3 * width + VECTORS]]
    )
    hidden, mixed_attn, grad_mixed, grad_att, sums2, down, grads = run_feed_forward(
        index, five, mixed, cotangent, packed, [column], shards
    )
    kept = (five, mixed, v, raised, facts)
    layer_out = run_layer_output(hidden, mixed_attn, down, cotangent.shape, None, 0, 1)
    input_grad, sums, grad_qkv = run_backward(index, weight, kept, (grad_att, grad_mixed), packed, sums2, 1)
    grad_ff = grads[0, :, : 2 * ff].reshape(width, shards, 2, width).transpose(0, 2, 1, 3).reshape(width, 2 * ff)
    grad_ff = lax.psum_scatter(grad_ff, "dp", scatter_dimension=0, tiled=True).reshape(own, 2, ff)
    grad_ff = lax.psum_scatter(grad_ff, "mp", scatter_dimension=2, tiled=True).astype(F32)
    grad_attn = jnp.concatenate([grad_qkv[0], grads[0, :, 2 * ff :]], axis=1)
    grad_attn = lax.psum_scatter(grad_attn, "dp", scatter_dimension=0, tiled=True)
    grad_attn = lax.psum(grad_attn, "mp").astype(F32)
    sums = lax.psum(sums, ("dp", "mp"))
    sums = lax.dynamic_slice_in_dim(sums, lax.axis_index("dp") * own, own, axis=1)
    return (
        layer_out, input_grad, grad_attn[:, : 3 * width], grad_attn[:, 3 * width :],
        grad_ff[:, 0], grad_ff[:, 1], sums[0:3], sums[3], sums[4], sums[5], sums[6],
    )


def on_device(
    tokens, segment_ids, valid_len, qkv_weight, out_weight, up_weight, down_weight, conv_weight,
    ln1_gain, ln1_shift, ln2_gain, ln2_shift, cotangent,
):
    own, ffs = up_weight.shape
    direct = own % 16 == 0 and ffs == tokens.shape[2] and own <= VECTORS and lax.axis_size("mp") == 4
    plan = direct_plan if direct else gathered_plan
    return plan(
        tokens, segment_ids, valid_len, qkv_weight, out_weight, up_weight, down_weight, conv_weight,
        (ln1_gain, ln1_shift, ln2_gain, ln2_shift), cotangent,
    )


def solution(mesh):
    rows = P(("dp", "mp"), None, None)
    weights = (P("dp", None), P("dp", None), P("dp", "mp"), P("dp", "mp"), P(None, "dp"))
    vectors = (P("dp"),) * 4
    return jax.shard_map(
        on_device,
        mesh=mesh,
        in_specs=(rows, P(("dp", "mp"), None), P(("dp", "mp"))) + weights + vectors + (rows,),
        out_specs=(rows, rows) + weights + vectors,
        check_vma=False,
    )
```

```python
import functools
import math

import jax
import jax.numpy as jnp
from jax import lax
from jax.experimental import pallas as pl
from jax.experimental.pallas import tpu as pltpu
from jax.sharding import PartitionSpec as P

HEADS = 6
VECTORS = 128
LANES = 128
BF = jnp.bfloat16
F32 = jnp.float32
MIB = 1024 * 1024
VMEM_LIMITS = dict(forward_attention=32, feed_forward=40, backward=42, layer_output=16)


def mm(lhs, rhs):
    return lax.dot_general(lhs, rhs, (((1,), (0,)), ((), ())), preferred_element_type=F32)


def mm_nt(lhs, rhs):
    return lax.dot_general(lhs, rhs, (((1,), (1,)), ((), ())), preferred_element_type=F32)


def tree_sum(items):
    items = list(items)
    while len(items) > 1:
        items = [a + b for a, b in zip(items[::2], items[1::2])]
    return items[0]


def pack_weights(qkv_ref, up_ref, down_ref, conv_ref, g1_ref, s1_ref, g2_ref, s2_ref, narrow_ref, ff_ref, rows_ref):
    own, ffs = up_ref.shape
    rows_ref[...] = jnp.zeros_like(rows_ref)
    rows_ref[0:3, :own] = conv_ref[...].astype(F32)
    for i, ref in enumerate((g1_ref, s1_ref, g2_ref, s2_ref)):
        rows_ref[3 + i : 4 + i, :own] = ref[...].astype(F32)
    wide = qkv_ref.shape[1]
    narrow_ref[:, :wide] = qkv_ref[...]
    narrow_ref[:, wide:] = rows_ref[...].T[:own].astype(BF)
    ff_ref[:own] = up_ref[...]
    ff_ref[own:] = down_ref[...]


def tiles(total, size):
    return [slice(at, at + size) for at in range(0, total, size)]


def weave(*strands):
    strands = [strand for strand in strands if strand]
    total = sum(len(strand) for strand in strands)
    pieces = [((i + 0.5) / len(strand), j, piece) for j, strand in enumerate(strands) for i, piece in enumerate(strand)]
    assert len(pieces) == total
    for _, _, piece in sorted(pieces, key=lambda item: item[:2]):
        piece()


def twice(tile, lanes):
    return jnp.concatenate([tile] * (lanes // LANES), axis=1)


def load_columns(packed_ref, col_ref, places):
    for i, place in enumerate(places):
        column = packed_ref[:, place : place + 1].astype(F32)
        col_ref[i] = jnp.broadcast_to(column, (column.shape[0], LANES))


def pairwise(items, combine):
    items = list(items)
    while len(items) > 1:
        odd = items[len(items) // 2 * 2 :]
        items = [combine(a, b) for a, b in zip(items[::2], items[1::2])] + odd
    return items[0]


def fold(values, combine=jnp.add):
    return pairwise([values[t] for t in tiles(values.shape[0], 8)], combine)


def column_mean(values):
    return jnp.sum(fold(values), axis=0, keepdims=True) * (1.0 / values.shape[0])


def norm_columns(values):
    centred = values - column_mean(values)
    scale = lax.rsqrt(column_mean(centred * centred) + 1e-06)
    return centred * scale, scale


def fold_lanes(values):
    return sum(values[:, t] for t in tiles(values.shape[1], LANES))


def forward_attention(index_ref, len_ref, tok_ref, seg_ref, *refs, pieces):
    cores = 2 if pieces > 1 else 1
    piece_refs = refs[:cores]
    (
        five_ref, mc_ref, v_ref, e_ref, facts_ref, packed_ref, w_ref,
        wt_ref, wide_ref, col_ref, key_mask_ref, query_mask_ref, key_ref, value_ref,
    ) = refs[cores:]
    x_ref, norm_ref, q_ref, k_ref, att_ref = [five_ref.at[:, i] for i in range(5)]
    aux_ref, inv_ref = facts_ref.at[:, :8], facts_ref.at[:, 8:]
    rows, seq, width = tok_ref.shape
    head = width // HEADS
    step = pl.program_id(0)

    @pl.when(step == 0)
    def _():
        own = width // pieces
        for i in range(pieces):
            here = pl.ds(pl.multiple_of(index_ref[i] * own, 16), own)
            wide_ref[here, :] = piece_refs[i % cores][i // cores * own : (i // cores + 1) * own]
        w_ref[...] = wide_ref[:, : 3 * width]
        wt_ref[...] = wide_ref[:, : 3 * width].T
        packed_ref[...] = wide_ref[:, 3 * width :]
        load_columns(packed_ref, col_ref, range(5))

    place = lax.broadcasted_iota(jnp.int32, (1, seq), 1)
    zero = jnp.zeros((head, seq), BF)

    def preparation(r):
        known = {}

        def start():
            segs = seg_ref[pl.ds(step * rows + r, 1), :].astype(F32)
            valid = place < len_ref[step * rows + r]
            number = jnp.where(valid, segs, -1.0)
            links = jnp.where(valid & (place > 0) & (number == pltpu.roll(number, 1, 1)), 1.0, 0.0)
            next_links = jnp.where(place < seq - 1, pltpu.roll(links, seq - 1, 1), 0.0)
            none = jnp.zeros_like(links)
            aux = jnp.concatenate([links, next_links, number, none, none, none, none, none], axis=0)
            aux_ref[r] = aux
            x_ref[r] = tok_ref[r].T
            known.update(segs=segs, links=links, next_links=next_links, key_number=aux.T[:, 2:3])

        def mask():
            number = known["key_number"]
            lane = lax.broadcasted_iota(jnp.int32, (seq, LANES), 1)
            itself = lax.broadcasted_iota(jnp.int32, (seq, LANES), 0) - (seq - LANES)
            chosen = (lane.astype(F32) == number) | ((number < 0.0) & (lane == itself))
            key_mask_ref[r] = jnp.where(chosen, 1.0, 0.0).astype(BF)
            slot = lax.broadcasted_iota(jnp.int32, (LANES, seq), 0)
            itself = lax.broadcasted_iota(jnp.int32, (LANES, seq), 1) - (seq - LANES)
            open_to = (slot.astype(F32) == known["segs"]) | ((slot >= LANES // 2) & (slot == itself))
            query_mask_ref[r] = jnp.where(open_to, 0.0, -1e30).astype(BF)

        def conv(t):
            base = x_ref[r, t].astype(F32)
            before = pltpu.roll(base, 1, 1) * known["links"]
            after = pltpu.roll(base, seq - 1, 1) * known["next_links"]
            conv0, conv1, conv2 = [twice(col_ref[i, t], seq) for i in range(3)]
            mc_ref[r, t] = base + before * conv0 + base * conv1 + after * conv2

        def norm(t):
            n, _ = norm_columns(mc_ref[r, :, t])
            norm_ref[r, :, t] = (n * col_ref[3] + col_ref[4]).astype(BF)

        pieces = [start] + [functools.partial(conv, t) for t in tiles(width, 32)]
        pieces += [functools.partial(norm, t) for t in tiles(seq, LANES)]
        return pieces + [mask]

    def project():
        normed = jnp.concatenate([norm_ref[r] for r in range(rows)], axis=1)
        for i, ref in enumerate((q_ref, k_ref, value_ref)):
            part = mm(wt_ref[i * width : (i + 1) * width], normed)
            part = (part * (head ** (-0.5) * math.log2(math.e)) if i == 0 else part).astype(BF)
            for r in range(rows):
                ref[r] = part[:, r * seq : (r + 1) * seq]
        for r in range(rows):
            key_ref[r] = k_ref[r].T
            v_ref[r] = value_ref[r].T

    def scores(r, p):
        low, high = [q_ref[r, h * head : (h + 1) * head] for h in (2 * p, 2 * p + 1)]
        both = jnp.concatenate([jnp.concatenate([low, zero], axis=1), jnp.concatenate([zero, high], axis=1)], axis=0)
        keys = jnp.concatenate([key_ref[r, :, 2 * p * head : 2 * (p + 1) * head], key_mask_ref[r]], axis=1)
        masks = jnp.concatenate([query_mask_ref[r], query_mask_ref[r]], axis=1)
        return mm(keys, jnp.concatenate([both, masks], axis=0))

    def attended(r, p):
        both = jnp.concatenate([e_ref[r, 2 * p], e_ref[r, 2 * p + 1]], axis=1)
        product = mm(value_ref[r, 2 * p * head : 2 * (p + 1) * head], both)
        parts = []
        for i in range(2):
            att = product[i * head : (i + 1) * head, i * seq : (i + 1) * seq] * inv_ref[r, 2 * p + i : 2 * p + i + 1]
            parts.append(att.astype(BF))
        return jnp.concatenate(parts, axis=0)

    def soften(r, p, product):
        for i in range(2):
            for t in tiles(seq, LANES):
                masked = product[:, i * seq + t.start : i * seq + t.stop]
                raised = jnp.exp2(masked - jnp.max(fold(masked, jnp.maximum), axis=0, keepdims=True))
                inv_ref[r, 2 * p + i : 2 * p + i + 1, t] = 1.0 / jnp.sum(fold(raised), axis=0, keepdims=True)
                e_ref[r, 2 * p + i, :, t] = raised.astype(BF)

    weave(*[preparation(r) for r in range(rows)])
    project()
    work = [(r, p) for r in range(rows) for p in range(HEADS // 2)]
    current, last = scores(*work[0]), None
    for at, (r, p) in enumerate(work):
        following = scores(*work[at + 1]) if at + 1 < len(work) else None
        finished = attended(*last) if last else None
        soften(r, p, current)
        if last:
            att_ref[last[0], 2 * last[1] * head : 2 * (last[1] + 1) * head] = finished
        current, last = following, (r, p)
    att_ref[last[0], 2 * last[1] * head : 2 * (last[1] + 1) * head] = attended(*last)


def gelu_parts(x):
    cdf = 0.5 * lax.erf(x * math.sqrt(0.5)) + 0.5
    bell = jnp.exp2(x * x * (-0.5 / math.log(2.0)) - 0.5 * math.log2(2.0 * math.pi))
    return x * cdf, cdf + x * bell


def feed_forward(index_ref, five_ref, mc_ref, ct_ref, packed_ref, *refs, pieces, shards):
    att_ref = five_ref.at[:, 0]
    groups = 2 if pieces > 1 else 1
    piece_refs = refs[:groups]
    hidden_out, mixed_out, gm_ref, ga_ref, gs_ref, down_ref = refs[groups : groups + 6]
    hidden_ref, mixed_ref = hidden_out.at[0], mixed_out.at[0]
    gw_refs = refs[groups + 6 : 2 * groups + 6]
    (
        up_ref, upt_ref, downt_ref, out_ref, outt_ref, up_acc, down_acc, out_acc, col_acc, col_ref,
        n_ref, norm_ref, ctt_ref, gp_ref, gn_ref, scale_ref, branch_ref,
    ) = refs[2 * groups + 6 :]
    rows, seq, width = ct_ref.shape
    ff = up_ref.shape[1]
    ffs = ff // shards
    own = width // pieces
    step = pl.program_id(0)

    @pl.when(step == 0)
    def _():
        for acc in (up_acc, down_acc, out_acc, col_acc):
            acc[...] = jnp.zeros_like(acc)
        for i in range(pieces):
            here = pl.ds(pl.multiple_of(index_ref[i] * own, 16), own)
            ref, first = piece_refs[i % groups], i // groups * (2 * shards + 1) * own
            for j in range(shards):
                at = first + 2 * j * own
                up_ref[here, j * ffs : (j + 1) * ffs] = ref[at : at + own]
                down_ref[here, j * ffs : (j + 1) * ffs] = ref[at + own : at + 2 * own]
            at = first + 2 * shards * own
            out_ref[here, :] = ref[at : at + own]
        upt_ref[...] = up_ref[...].T
        downt_ref[...] = down_ref[...].T
        outt_ref[...] = out_ref[...].T
        load_columns(packed_ref, col_ref, (5, 6))

    def lanes_of(r):
        return slice(r * seq, (r + 1) * seq)

    def spots_of(r):
        return [slice(at, at + LANES) for at in range(r * seq, (r + 1) * seq, LANES)]

    def preparation(r):
        lanes = lanes_of(r)

        def turn():
            ctt_ref[:, lanes] = ct_ref[r].T

        def norm(t):
            n, scale = norm_columns(mixed_ref[:, t])
            n_ref[:, t] = n
            scale_ref[0:1, t] = scale
            norm_ref[:, t] = (n * col_ref[0] + col_ref[1]).astype(BF)

        return [turn] + [functools.partial(norm, t) for t in spots_of(r)]

    def activation(block):
        pre = mm(upt_ref[block], norm_ref[...])
        grad_hidden = mm(downt_ref[block], ctt_ref[...])
        for low in range(0, block.stop - block.start, 16):
            part = slice(low, low + 16)
            here = slice(block.start + low, block.start + low + 16)
            hidden, slope = gelu_parts(pre[part])
            hidden_ref[here] = hidden.astype(BF)
            gp_ref[here] = (grad_hidden[part] * slope).astype(BF)

    def norm_back(r):
        spots = spots_of(r)
        mean_e = [jnp.zeros((8, LANES), F32) for _ in spots]
        mean_en = [jnp.zeros((8, LANES), F32) for _ in spots]
        means = []

        def sums(d):
            column = col_ref[0, d]
            gain_sum, shift_sum = col_acc[0, d], col_acc[1, d]
            for i, t in enumerate(spots):
                grad_n = gn_ref[d, t]
                product = grad_n * n_ref[d, t]
                gain_sum += product
                shift_sum += grad_n
                mean_e[i] += fold(grad_n * column)
                mean_en[i] += fold(product * column)
            col_acc[0, d] = gain_sum
            col_acc[1, d] = shift_sum

        def finish():
            for i in range(len(spots)):
                me = jnp.sum(mean_e[i], axis=0, keepdims=True) * (1.0 / width)
                men = jnp.sum(mean_en[i], axis=0, keepdims=True) * (1.0 / width)
                means.append((me, men))

        def apply(d):
            for i, t in enumerate(spots):
                me, men = means[i]
                change = scale_ref[0:1, t] * (gn_ref[d, t] * col_ref[0, d] - me - n_ref[d, t] * men)
                grad_mixed = ctt_ref[d, t].astype(F32) + change
                gm_ref[r, d, i * LANES : (i + 1) * LANES] = grad_mixed
                branch_ref[d, t] = grad_mixed.astype(BF)

        pieces = [functools.partial(sums, d) for d in tiles(width, 32)] + [finish]
        return pieces + [functools.partial(apply, d) for d in tiles(width, 32)]

    attended = jnp.concatenate([att_ref[r] for r in range(rows)], axis=1)
    branch = mm(outt_ref[...], attended)
    for r in range(rows):
        mixed_ref[:, lanes_of(r)] = mc_ref[r] + branch[:, lanes_of(r)]
    weave(*[preparation(r) for r in range(rows)])
    for block in tiles(ff, 128):
        activation(block)
    gn_ref[...] = mm(up_ref[...], gp_ref[...])
    down_acc[...] += mm_nt(ctt_ref[...], hidden_ref[...])
    up_acc[...] += mm_nt(norm_ref[...], gp_ref[...])
    weave(*[norm_back(r) for r in range(rows)])
    grad_attended = mm(out_ref[...], branch_ref[...]).astype(BF)
    for r in range(rows):
        ga_ref[r] = grad_attended[:, lanes_of(r)]
    out_acc[...] += mm_nt(attended, branch_ref[...])

    @pl.when(step == pl.num_programs(0) - 1)
    def _():
        for i in range(pieces):
            here = pl.ds(pl.multiple_of(index_ref[i] * own, 16), own)
            place = gw_refs[i % groups]
            for j in range(shards):
                cols = slice(j * ffs, (j + 1) * ffs)
                place[i // groups, :, 2 * j * ffs : (2 * j + 1) * ffs] = up_acc[here, cols].astype(BF)
                place[i // groups, :, (2 * j + 1) * ffs : (2 * j + 2) * ffs] = down_acc[here, cols].astype(BF)
            place[i // groups, :, 2 * ff :] = out_acc[here, :].astype(BF)
        gs_ref[...] = jnp.zeros_like(gs_ref)
        for i in range(2):
            gs_ref[5 + i : 6 + i] = jnp.sum(col_acc[i].T, axis=0, keepdims=True)


def layer_output(hidden_ref, mixed_ref, down_ref, lo_ref):
    rows, seq, _ = lo_ref.shape
    total = (mixed_ref[0] + mm(down_ref[...], hidden_ref[0])).astype(BF)
    for r in range(rows):
        lo_ref[r] = total[:, r * seq : (r + 1) * seq].T


def backward(
    five_ref, mc_ref, v_ref, e_ref, facts_ref, ga_ref, gm_ref, index_ref, w_ref, packed_ref, other_ref, ig_ref, gs_ref, *refs, pieces,
):
    x_ref, norm_ref, q_ref, k_ref, att_ref = [five_ref.at[:, i] for i in range(5)]
    aux_ref, inv_ref = facts_ref.at[:, :8], facts_ref.at[:, 8:]
    gw_refs = refs[:-11]
    (
        proj_ref, w_acc, norm_cat, soft_ref, logit_ref, gn_ref, acc_ref, col_ref, n_ref, g_ref, turn_ref
    ) = refs[-11:]
    rows, seq, width = v_ref.shape
    own = width // pieces
    head = width // HEADS
    step = pl.program_id(0)

    @pl.when(step == 0)
    def _():
        w_acc[...] = jnp.zeros_like(w_acc)
        acc_ref[...] = jnp.zeros_like(acc_ref)
        load_columns(packed_ref, col_ref, range(4))

    zero = jnp.zeros((head, seq), BF)
    work = [(r, p) for r in range(rows) for p in range(HEADS // 2)]

    def opening(r, p):
        grads, inners = [], []
        for h in (2 * p, 2 * p + 1):
            part = slice(h * head, (h + 1) * head)
            grad_att = ga_ref[r, part].astype(F32) * inv_ref[r, h : h + 1]
            inners.append(jnp.sum(fold(grad_att * att_ref[r, part].astype(F32)), axis=0, keepdims=True))
            grads.append(grad_att.astype(BF))
        low, high = grads
        both = jnp.concatenate([jnp.concatenate([low, zero], axis=1), jnp.concatenate([zero, high], axis=1)], axis=0)
        product = mm(v_ref[r, :, 2 * p * head : 2 * (p + 1) * head], both)
        soft_ref[r, 2 * p] = product[:, :seq]
        soft_ref[r, 2 * p + 1] = product[:, seq:]
        return jnp.concatenate(grads, axis=0), inners

    ready = opening(*work[0])
    for at, (r, p) in enumerate(work):
        grad_att, inners = ready
        if at + 1 < len(work):
            ready = opening(*work[at + 1])
        for i, h in enumerate((2 * p, 2 * p + 1)):
            for t in tiles(seq, 32):
                raised = e_ref[r, h, t].astype(F32)
                logit_ref[r, h, t] = (raised * (soft_ref[r, h, t] - inners[i])).astype(BF)
        part = slice(2 * p * head, 2 * (p + 1) * head)
        pair = slice(2 * p, 2 * p + 2)
        beside = jnp.concatenate([logit_ref[r, 2 * p], logit_ref[r, 2 * p + 1]], axis=1)
        grad_q = mm(k_ref[r, part], beside)
        grad_k = mm_nt(q_ref[r, part], logit_ref[r, pair].reshape(2 * seq, seq))
        grad_v = mm_nt(grad_att, e_ref[r, pair].reshape(2 * seq, seq))
        for i in range(2):
            place = slice(r * seq, (r + 1) * seq)
            own_rows, own_cols = slice(i * head, (i + 1) * head), slice(i * seq, (i + 1) * seq)
            for j, (grad, factor) in enumerate(((grad_q, head ** (-0.5)), (grad_k, math.log(2.0)), (grad_v, None))):
                first = j * width + (2 * p + i) * head
                mine = grad[own_rows, own_cols]
                proj_ref[first : first + head, place] = (mine if factor is None else mine * factor).astype(BF)
    gn_ref[...] = mm(w_ref[...], proj_ref[...])
    for r in range(rows):
        norm_cat[:, r * seq : (r + 1) * seq] = norm_ref[r]
    w_acc[...] += mm_nt(norm_cat[...], proj_ref[...])

    spots = tiles(seq, LANES)
    for r in range(rows):
        wide = [slice(r * seq + t.start, r * seq + t.stop) for t in spots]
        scales = []
        for t in spots:
            n, scale = norm_columns(mc_ref[r, :, t])
            n_ref[r, :, t] = n
            scales.append(scale)
        mean_e = [jnp.zeros((8, LANES), F32) for _ in spots]
        mean_en = [jnp.zeros((8, LANES), F32) for _ in spots]
        for d in tiles(width, 32):
            column = col_ref[3, d]
            gain_sum, shift_sum = acc_ref[3, d], acc_ref[4, d]
            for i, t in enumerate(spots):
                grad_n = gn_ref[d, wide[i]]
                product = grad_n * n_ref[r, d, t]
                gain_sum += product
                shift_sum += grad_n
                mean_e[i] += fold(grad_n * column)
                mean_en[i] += fold(product * column)
            acc_ref[3, d] = gain_sum
            acc_ref[4, d] = shift_sum
        for i, t in enumerate(spots):
            me = jnp.sum(mean_e[i], axis=0, keepdims=True) * (1.0 / width)
            men = jnp.sum(mean_en[i], axis=0, keepdims=True) * (1.0 / width)
            for d in tiles(width, 64):
                e = gn_ref[d, wide[i]] * col_ref[3, d]
                g_ref[r, d, t] = gm_ref[r, d, t] + scales[i] * (e - me - n_ref[r, d, t] * men)
        links, next_links = aux_ref[r, 0:1], aux_ref[r, 1:2]
        for d in tiles(width, 32):
            g = g_ref[r, d]
            base = x_ref[r, d].astype(F32)
            before = pltpu.roll(g, 1, 1) * links
            after = pltpu.roll(g, seq - 1, 1) * next_links
            acc_ref[0, d] += fold_lanes(base * after)
            acc_ref[1, d] += fold_lanes(base * g)
            acc_ref[2, d] += fold_lanes(base * before)
            conv0, conv1, conv2 = [twice(col_ref[i, d], seq) for i in range(3)]
            turn_ref[r, d] = (g + conv1 * g + conv0 * after + conv2 * before).astype(BF)
        ig_ref[r] = turn_ref[r].T

    @pl.when(step == pl.num_programs(0) - 1)
    def _():
        gs_ref[...] = other_ref[...]
        for i in range(5):
            gs_ref[i : i + 1] += jnp.sum(acc_ref[i].T, axis=0, keepdims=True)
        groups = len(gw_refs)
        for i in range(pieces):
            here = pl.ds(pl.multiple_of(index_ref[i] * own, 16), own)
            gw_refs[i % groups][i // groups] = w_acc[here, :].astype(BF)


def in_hbm(values):
    return pltpu.with_memory_space_constraint(values, pltpu.HBM)


def by_row(shape, rows, first=0):
    tail = tuple(shape[1:])
    return pl.BlockSpec((rows,) + tail, lambda i, *_: (i + first,) + (0,) * len(tail))


def whole(shape):
    place = (0,) * len(shape)
    return pl.BlockSpec(tuple(shape), lambda i, *_: place, pipeline_mode=pl.Buffered(1))


def step_rows(count, most):
    return max(r for r in range(1, most + 1) if count % r == 0)


def call(body, name, scalars, rows, row_args, args, row_outs, outs, scratch, span=None, into=None, near=(), only=None):
    first, count = span or (0, row_args[0].shape[0])
    skip = first // rows
    total = row_args[0].shape[0]

    def spec_of(shape):
        return by_row(shape, shape[0] * rows // total, skip)

    in_specs = [spec_of(a.shape) for a in row_args]
    if only:
        tail = row_args[0].shape[2:]
        in_specs[0] = pl.BlockSpec((rows, 1) + tail, lambda i, *_: (i, only) + (0,) * len(tail))
    in_specs += [whole(a.shape) for a in args]
    aliases = {}
    if into is not None:
        in_specs.append(pl.BlockSpec(memory_space=pl.ANY))
        aliases = {len(scalars) + len(in_specs) - 1: 0}
    spec = pltpu.PrefetchScalarGridSpec(
        num_scalar_prefetch=len(scalars),
        grid=(count // rows,),
        in_specs=in_specs,
        out_specs=[spec_of(s) for s, _ in row_outs] + [whole(s) for s, _ in outs],
        scratch_shapes=[pltpu.VMEM(s, t) for s, t in scratch],
    )
    return pl.pallas_call(
        body,
        grid_spec=spec,
        out_shape=[(jax.ShapeDtypeStruct if "out" + str(i) in near else pltpu.HBM)(s, t) for i, (s, t) in enumerate(row_outs)]
        + [jax.ShapeDtypeStruct(s, t) for s, t in outs],
        input_output_aliases=aliases,
        compiler_params=pltpu.CompilerParams(dimension_semantics=("arbitrary",), vmem_limit_bytes=VMEM_LIMITS[name] * MIB),
        name=name,
    )(*scalars, *[a if i in near else in_hbm(a) for i, a in enumerate(row_args)], *args, *(() if into is None else (into,)))


def small_call(body, name, args, outs, scratch=()):
    return pl.pallas_call(
        body,
        out_shape=[jax.ShapeDtypeStruct(s, t) for s, t in outs],
        scratch_shapes=[pltpu.VMEM(s, t) for s, t in scratch],
        compiler_params=pltpu.CompilerParams(vmem_limit_bytes=16 * MIB),
        name=name,
    )(*args)


def run_forward(index, tokens, segment_ids, valid_len, pieces):
    count, seq, width = tokens.shape
    flipped = (count, width, seq)
    rows = step_rows(count, 3)
    row_outs = [
        ((count, 5, width, seq), BF), (flipped, F32), ((count, seq, width), BF),
        ((count, HEADS, seq, seq), BF), ((count, 16, seq), F32),
    ]
    return call(
        functools.partial(forward_attention, pieces=index.shape[0]), "forward_attention", (index, in_hbm(valid_len)),
        rows, (tokens,), (in_hbm(segment_ids), *pieces),
        row_outs, [((width, VECTORS), BF), ((width, 3 * width), BF)],
        [
            ((3 * width, width), BF), ((width, 3 * width + VECTORS), BF), ((5, width, LANES), F32),
            ((rows, seq, LANES), BF), ((rows, LANES, seq), BF), ((rows, seq, width), BF), ((rows, width, seq), BF),
        ],
    )


def run_feed_forward(index, five, mixed, cotangent, packed, pieces, shards):
    count, seq, width = cotangent.shape
    own = width // index.shape[0]
    ff = shards * width
    groups = 2 if index.shape[0] > 1 else 1
    rows = step_rows(count, 2)
    wide = rows * seq
    row_outs = [
        ((count // rows, ff, wide), BF), ((count // rows, width, wide), F32),
        ((count, width, seq), F32), ((count, width, seq), BF),
    ]
    grads = ((index.shape[0] // groups, own, 2 * ff + width), BF)
    return call(
        functools.partial(feed_forward, pieces=index.shape[0], shards=shards), "feed_forward", (index,),
        rows, (five, mixed, cotangent), (packed, *pieces),
        row_outs, [((8, width), F32), ((width, ff), BF)] + [grads] * groups,
        [((width, ff), BF)] + [((ff, width), BF)] * 2 + [((width, width), BF)] * 2
        + [((width, ff), F32)] * 2 + [((width, width), F32), ((2, width, LANES), F32), ((2, width, LANES), F32)]
        + [((width, wide), F32), ((width, wide), BF), ((width, wide), BF)]
        + [((ff, wide), BF)]
        + [((width, wide), F32), ((8, wide), F32), ((width, wide), BF)],
        near=("out3",), only=4,
    )


def run_layer_output(hidden, mixed, down, shape, into, low, high):
    steps = hidden.shape[0]
    span = (int(low * steps), int(high * steps) - int(low * steps))

    def body(*refs):
        layer_output(*refs[:3], refs[-1])

    return call(body, "layer_output", (), 1, (hidden, mixed), (down,), [(shape, BF)], [], [], span=span, into=into)[0]


def run_backward(index, weight, kept, grads, packed, other, pieces):
    count, seq, width = kept[2].shape
    own = width // pieces
    groups = 2 if pieces > 1 else 1
    rows = step_rows(count, 3)
    row_args = (*kept, *grads)
    many = len(row_args)

    def body(index_ref, *refs):
        backward(*refs[:many], index_ref, *refs[many:], pieces=pieces)

    return call(
        body, "backward", (index,), rows, row_args, (weight, packed, other),
        [((count, seq, width), BF)], [((8, width), F32)] + [((pieces // groups, own, 3 * width), BF)] * groups,
        [
            ((3 * width, rows * seq), BF), ((width, 3 * width), F32), ((width, rows * seq), BF),
            ((rows, HEADS, seq, seq), F32), ((rows, HEADS, seq, seq), BF), ((width, rows * seq), F32),
            ((5, width, LANES), F32), ((4, width, LANES), F32), ((rows, width, seq), F32), ((rows, width, seq), F32),
            ((rows, width, seq), BF),
        ],
        near=(5,),
    )


def exchange(values, axis, offset):
    size = lax.axis_size(axis)
    return lax.ppermute(values, axis, [(i, i ^ offset) for i in range(size)])


def add_halves(mine, received):
    count, own, cols = mine.shape

    def body(mine_ref, received_ref, *out_refs):
        for i, ref in enumerate(out_refs):
            ref[...] = (mine_ref[i].astype(F32) + received_ref[i].astype(F32)).astype(BF)

    return small_call(body, "add_halves", (mine, received), [((own, cols), BF)] * count)


def add_wide(*items):
    return tree_sum(item.astype(F32) for item in items)


def store_high_low(ref, cols, values):
    high = values.astype(BF)
    low = (values - high.astype(F32)).astype(BF)
    ref[:, cols:] = jnp.concatenate([high, low, jnp.zeros((ref.shape[0] - 16, LANES), BF)], axis=0)


def load_high_low(ref, cols):
    both = ref[:16, cols:].astype(F32)
    return both[:8] + both[8:]


def add_halves_and_sums(index, mine, received, sums, received_sums):
    count, own, cols = mine.shape
    width = sums.shape[1]

    def body(index_ref, mine_ref, received_ref, sums_ref, received_sums_ref, *out_refs):
        total = sums_ref[...] + received_sums_ref[...]
        for i, ref in enumerate(out_refs):
            ref[:, :cols] = (mine_ref[i].astype(F32) + received_ref[i].astype(F32)).astype(BF)
            turned = pltpu.roll(total, lax.rem(width - index_ref[2 * i] * own, width), 1)[:, :LANES]
            store_high_low(ref, cols, turned)

    spec = pltpu.PrefetchScalarGridSpec(
        num_scalar_prefetch=1, grid=(1,),
        in_specs=[whole(a.shape) for a in (mine, received, sums, received_sums)],
        out_specs=[whole((own, cols + LANES))] * count,
    )
    return pl.pallas_call(
        body, grid_spec=spec, out_shape=[jax.ShapeDtypeStruct((own, cols + LANES), BF)] * count,
        compiler_params=pltpu.CompilerParams(vmem_limit_bytes=16 * MIB), name="add_halves_and_sums",
    )(index, mine, received, sums, received_sums)


def add_packed(name, items):
    cols = items[0].shape[1] - LANES

    def body(*refs):
        out_ref = refs[-1]
        out_ref[:, :cols] = tree_sum(ref[:, :cols].astype(F32) for ref in refs[:-1]).astype(BF)
        store_high_low(out_ref, cols, tree_sum(load_high_low(ref, cols) for ref in refs[:-1]))

    return small_call(body, name, items, [(items[0].shape, BF)])[0]


def add_last(items):
    own, cols = items[0].shape[0], items[0].shape[1] - LANES

    def body(*refs):
        ins, outs = refs[: len(items)], refs[len(items) :]
        outs[0][...] = tree_sum(ref[:, :cols].astype(F32) for ref in ins)
        vectors = tree_sum(load_high_low(ref, cols) for ref in ins)
        outs[1][...] = vectors[0:3, :own]
        for i in range(4):
            outs[2 + i][...] = vectors[3 + i : 4 + i, :own]

    return small_call(body, "add_last", items, [((own, cols), F32), ((3, own), F32)] + [((1, own), F32)] * 4)


def direct_plan(tokens, segment_ids, valid_len, qkv_weight, out_weight, up_weight, down_weight, conv_weight, vectors, cotangent):
    count, seq, width = tokens.shape
    own, ffs = up_weight.shape
    dp, mp = lax.axis_size("dp"), lax.axis_size("mp")
    me = lax.axis_index("dp")
    offsets = [2 * p for p in range(dp // 2)]
    index = jnp.stack([me ^ (p ^ c) for p in offsets for c in range(2)]).astype(jnp.int32)
    narrow, ff_own = small_call(
        pack_weights, "pack_weights",
        [in_hbm(a) for a in (qkv_weight, up_weight, down_weight, conv_weight, *[v.reshape(1, own) for v in vectors])],
        [((own, 3 * width + VECTORS), BF), ((2 * own, ffs), BF)], [((VECTORS, VECTORS), F32)],
    )
    shards = [ff_own] + [exchange(ff_own, "mp", j) for j in range(1, mp)]
    plane = jnp.concatenate([narrow] + [exchange(narrow, "dp", p) for p in offsets[1:]], axis=0)
    pieces = [plane, exchange(plane, "dp", 1)]
    column = jnp.concatenate(shards + [out_weight], axis=0)
    columns = [column] + [exchange(column, "dp", p) for p in offsets[1:]]
    five, mixed, v, raised, facts, packed, weight = run_forward(
        index, tokens, segment_ids, valid_len, pieces
    )
    columns, five = lax.optimization_barrier((columns, five))
    columns = jnp.concatenate(columns, axis=0)
    pieces = [columns, exchange(columns, "dp", 1)]
    hidden, mixed_attn, grad_mixed, grad_att, sums2, down, mine, theirs = run_feed_forward(
        index, five, mixed, cotangent, packed, pieces, mp
    )
    received = exchange(theirs, "dp", 1)
    shape = cotangent.shape
    layer_out = run_layer_output(hidden, mixed_attn, down, shape, None, 0, 0.34)
    received, layer_out = lax.optimization_barrier((received, layer_out))
    parts = list(add_halves(mine, received))
    parts[0], grad_att = lax.optimization_barrier((parts[0], grad_att))
    plane = [parts[0]] + [exchange(parts[i], "dp", p) for i, p in enumerate(offsets) if i]
    kept = (five, mixed, v, raised, facts)
    input_grad, sums, mine_a, theirs_a = run_backward(
        index, weight, kept, (grad_att, grad_mixed), packed, sums2, dp
    )
    plane, theirs_a, sums = lax.optimization_barrier((plane, theirs_a, sums))
    received_a = exchange(theirs_a, "dp", 1)
    received_s = exchange(sums, "dp", 1)
    total = add_wide(*plane).astype(BF)
    total, received_s = lax.optimization_barrier((total, received_s))
    part = 2 * ffs
    near = jnp.concatenate([total[:, :part], total[:, 2 * part : 3 * part]], axis=1)
    out_part = total[:, 4 * part :]
    far = jnp.concatenate([total[:, part : 2 * part], total[:, 3 * part :]], axis=1)
    parts = list(add_halves_and_sums(index, mine_a, received_a, sums, received_s))
    parts[0], hidden, layer_out = lax.optimization_barrier((parts[0], hidden, layer_out))
    plane_a = [parts[0]] + [exchange(parts[i], "dp", p) for i, p in enumerate(offsets) if i]
    received_f = exchange(far, "mp", 1)
    layer_out = run_layer_output(hidden, mixed_attn, down, shape, layer_out, 0.34, 0.67)
    plane_a, layer_out = lax.optimization_barrier((plane_a, layer_out))
    total = add_packed("add_plane", plane_a)
    received_1 = exchange(total, "mp", 1)
    received_f, _ = lax.optimization_barrier((received_f, total))
    near_sum = add_wide(near, received_f[:, : 2 * part])
    out_sum = lax.optimization_barrier(add_wide(out_part, received_f[:, 2 * part :]).astype(BF))
    keep = near_sum[:, :part]
    send = jnp.concatenate([near_sum[:, part:].astype(BF), out_sum], axis=1)
    received_n = exchange(send, "mp", 2)
    received_1, _ = lax.optimization_barrier((received_1, send))
    total = add_packed("add_near", (total, received_1))
    received_2 = exchange(total, "mp", 2)
    layer_out, _ = lax.optimization_barrier((layer_out, total))
    layer_out = run_layer_output(hidden, mixed_attn, down, shape, layer_out, 0.67, 1)
    received_n, layer_out = lax.optimization_barrier((received_n, layer_out))
    grad_up = keep[:, :ffs] + received_n[:, :ffs].astype(F32)
    grad_down = keep[:, ffs:] + received_n[:, ffs : 2 * ffs].astype(F32)
    grad_out = add_wide(out_sum, received_n[:, 2 * ffs :])
    grad_qkv, grad_conv, *grads = add_last((total, received_2))
    return (layer_out, input_grad, grad_qkv, grad_out, grad_up, grad_down, grad_conv, *[g.reshape(own) for g in grads])


def gathered_plan(tokens, segment_ids, valid_len, qkv_weight, out_weight, up_weight, down_weight, conv_weight, vectors, cotangent):
    count, seq, width = tokens.shape
    own = qkv_weight.shape[0]
    dp = width // own
    columns = jnp.stack([conv_weight[0], conv_weight[1], conv_weight[2], *vectors], axis=1)
    narrow = jnp.concatenate([qkv_weight, jnp.pad(columns, ((0, 0), (0, VECTORS - 7))), out_weight], axis=1)
    wide = lax.all_gather(narrow, "dp", axis=0, tiled=True)
    both = lax.all_gather(jnp.concatenate([up_weight, down_weight], axis=0), "mp", axis=1, tiled=True)
    ff = both.shape[1]
    shards = ff // width
    both = lax.all_gather(both, "dp", axis=0).reshape(dp, 2, own, shards, width)
    both = both.transpose(3, 1, 0, 2, 4).reshape(2 * ff, width)
    column = jnp.concatenate([both, wide[:, 3 * width + VECTORS :]], axis=0)
    index = jnp.zeros((1,), jnp.int32)
    five, mixed, v, raised, facts, packed, weight = run_forward(
        index, tokens, segment_ids, valid_len, [wide[:, : 3 * width + VECTORS]]
    )
    hidden, mixed_attn, grad_mixed, grad_att, sums2, down, grads = run_feed_forward(
        index, five, mixed, cotangent, packed, [column], shards
    )
    kept = (five, mixed, v, raised, facts)
    layer_out = run_layer_output(hidden, mixed_attn, down, cotangent.shape, None, 0, 1)
    input_grad, sums, grad_qkv = run_backward(index, weight, kept, (grad_att, grad_mixed), packed, sums2, 1)
    grad_ff = grads[0, :, : 2 * ff].reshape(width, shards, 2, width).transpose(0, 2, 1, 3).reshape(width, 2 * ff)
    grad_ff = lax.psum_scatter(grad_ff, "dp", scatter_dimension=0, tiled=True).reshape(own, 2, ff)
    grad_ff = lax.psum_scatter(grad_ff, "mp", scatter_dimension=2, tiled=True).astype(F32)
    grad_attn = jnp.concatenate([grad_qkv[0], grads[0, :, 2 * ff :]], axis=1)
    grad_attn = lax.psum_scatter(grad_attn, "dp", scatter_dimension=0, tiled=True)
    grad_attn = lax.psum(grad_attn, "mp").astype(F32)
    sums = lax.psum(sums, ("dp", "mp"))
    sums = lax.dynamic_slice_in_dim(sums, lax.axis_index("dp") * own, own, axis=1)
    return (
        layer_out, input_grad, grad_attn[:, : 3 * width], grad_attn[:, 3 * width :],
        grad_ff[:, 0], grad_ff[:, 1], sums[0:3], sums[3], sums[4], sums[5], sums[6],
    )


def on_device(
    tokens, segment_ids, valid_len, qkv_weight, out_weight, up_weight, down_weight, conv_weight,
    ln1_gain, ln1_shift, ln2_gain, ln2_shift, cotangent,
):
    own, ffs = up_weight.shape
    direct = own % 16 == 0 and ffs == tokens.shape[2] and own <= VECTORS and lax.axis_size("mp") == 4
    plan = direct_plan if direct else gathered_plan
    return plan(
        tokens, segment_ids, valid_len, qkv_weight, out_weight, up_weight, down_weight, conv_weight,
        (ln1_gain, ln1_shift, ln2_gain, ln2_shift), cotangent,
    )


def solution(mesh):
    rows = P(("dp", "mp"), None, None)
    weights = (P("dp", None), P("dp", None), P("dp", "mp"), P("dp", "mp"), P(None, "dp"))
    vectors = (P("dp"),) * 4
    return jax.shard_map(
        on_device,
        mesh=mesh,
        in_specs=(rows, P(("dp", "mp"), None), P(("dp", "mp"))) + weights + vectors + (rows,),
        out_specs=(rows, rows) + weights + vectors,
        check_vma=False,
    )
```

```python
import functools
import math

import jax
import jax.numpy as jnp
from jax import lax
from jax.experimental import pallas as pl
from jax.experimental.pallas import tpu as pltpu
from jax.sharding import PartitionSpec as P

HEADS = 6
VECTORS = 128
LANES = 128
BF = jnp.bfloat16
F32 = jnp.float32
MIB = 1024 * 1024
VMEM_LIMITS = dict(forward_attention=42, feed_forward=40, backward=42, layer_output=16)


def mm(lhs, rhs):
    return lax.dot_general(lhs, rhs, (((1,), (0,)), ((), ())), preferred_element_type=F32)


def mm_nt(lhs, rhs):
    return lax.dot_general(lhs, rhs, (((1,), (1,)), ((), ())), preferred_element_type=F32)


def tree_sum(items):
    items = list(items)
    while len(items) > 1:
        items = [a + b for a, b in zip(items[::2], items[1::2])]
    return items[0]


def pack_weights(qkv_ref, up_ref, down_ref, conv_ref, g1_ref, s1_ref, g2_ref, s2_ref, narrow_ref, ff_ref, rows_ref):
    own, ffs = up_ref.shape
    rows_ref[...] = jnp.zeros_like(rows_ref)
    rows_ref[0:3, :own] = conv_ref[...].astype(F32)
    for i, ref in enumerate((g1_ref, s1_ref, g2_ref, s2_ref)):
        rows_ref[3 + i : 4 + i, :own] = ref[...].astype(F32)
    wide = qkv_ref.shape[1]
    narrow_ref[:, :wide] = qkv_ref[...]
    narrow_ref[:, wide:] = rows_ref[...].T[:own].astype(BF)
    ff_ref[:own] = up_ref[...]
    ff_ref[own:] = down_ref[...]


def tiles(total, size):
    return [slice(at, at + size) for at in range(0, total, size)]


def weave(*strands):
    strands = [strand for strand in strands if strand]
    total = sum(len(strand) for strand in strands)
    pieces = [((i + 0.5) / len(strand), j, piece) for j, strand in enumerate(strands) for i, piece in enumerate(strand)]
    assert len(pieces) == total
    for _, _, piece in sorted(pieces, key=lambda item: item[:2]):
        piece()


def twice(tile, lanes):
    return jnp.concatenate([tile] * (lanes // LANES), axis=1)


def load_columns(packed_ref, col_ref, places):
    for i, place in enumerate(places):
        column = packed_ref[:, place : place + 1].astype(F32)
        col_ref[i] = jnp.broadcast_to(column, (column.shape[0], LANES))


def pairwise(items, combine):
    items = list(items)
    while len(items) > 1:
        odd = items[len(items) // 2 * 2 :]
        items = [combine(a, b) for a, b in zip(items[::2], items[1::2])] + odd
    return items[0]


def fold(values, combine=jnp.add):
    return pairwise([values[t] for t in tiles(values.shape[0], 8)], combine)


def column_mean(values):
    return jnp.sum(fold(values), axis=0, keepdims=True) * (1.0 / values.shape[0])


def norm_columns(values):
    centred = values - column_mean(values)
    scale = lax.rsqrt(column_mean(centred * centred) + 1e-06)
    return centred * scale, scale


def fold_lanes(values):
    return sum(values[:, t] for t in tiles(values.shape[1], LANES))


def forward_attention(index_ref, len_ref, tok_ref, seg_ref, *refs, pieces):
    cores = 2 if pieces > 1 else 1
    piece_refs = refs[:cores]
    (
        five_ref, mc_ref, v_ref, e_ref, facts_ref, packed_ref, w_ref,
        wt_ref, wide_ref, col_ref, key_mask_ref, query_mask_ref, key_ref, value_ref,
    ) = refs[cores:]
    x_ref, norm_ref, q_ref, k_ref, att_ref = [five_ref.at[:, i] for i in range(5)]
    aux_ref, inv_ref = facts_ref.at[:, :8], facts_ref.at[:, 8:]
    rows, seq, width = tok_ref.shape
    head = width // HEADS
    step = pl.program_id(0)

    @pl.when(step == 0)
    def _():
        own = width // pieces
        for i in range(pieces):
            here = pl.ds(pl.multiple_of(index_ref[i] * own, 16), own)
            wide_ref[here, :] = piece_refs[i % cores][i // cores * own : (i // cores + 1) * own]
        w_ref[...] = wide_ref[:, : 3 * width]
        wt_ref[...] = wide_ref[:, : 3 * width].T
        packed_ref[...] = wide_ref[:, 3 * width :]
        load_columns(packed_ref, col_ref, range(5))

    place = lax.broadcasted_iota(jnp.int32, (1, seq), 1)
    zero = jnp.zeros((head, seq), BF)

    def preparation(r):
        known = {}

        def start():
            segs = seg_ref[pl.ds(step * rows + r, 1), :].astype(F32)
            valid = place < len_ref[step * rows + r]
            number = jnp.where(valid, segs, -1.0)
            links = jnp.where(valid & (place > 0) & (number == pltpu.roll(number, 1, 1)), 1.0, 0.0)
            next_links = jnp.where(place < seq - 1, pltpu.roll(links, seq - 1, 1), 0.0)
            none = jnp.zeros_like(links)
            aux = jnp.concatenate([links, next_links, number, none, none, none, none, none], axis=0)
            aux_ref[r] = aux
            x_ref[r] = tok_ref[r].T
            known.update(segs=segs, links=links, next_links=next_links, key_number=aux.T[:, 2:3])

        def mask():
            number = known["key_number"]
            lane = lax.broadcasted_iota(jnp.int32, (seq, LANES), 1)
            itself = lax.broadcasted_iota(jnp.int32, (seq, LANES), 0) - (seq - LANES)
            chosen = (lane.astype(F32) == number) | ((number < 0.0) & (lane == itself))
            key_mask_ref[r] = jnp.where(chosen, 1.0, 0.0).astype(BF)
            slot = lax.broadcasted_iota(jnp.int32, (LANES, seq), 0)
            itself = lax.broadcasted_iota(jnp.int32, (LANES, seq), 1) - (seq - LANES)
            open_to = (slot.astype(F32) == known["segs"]) | ((slot >= LANES // 2) & (slot == itself))
            query_mask_ref[r] = jnp.where(open_to, 0.0, -1e30).astype(BF)

        def conv(t):
            base = x_ref[r, t].astype(F32)
            before = pltpu.roll(base, 1, 1) * known["links"]
            after = pltpu.roll(base, seq - 1, 1) * known["next_links"]
            conv0, conv1, conv2 = [twice(col_ref[i, t], seq) for i in range(3)]
            mc_ref[r, t] = base + before * conv0 + base * conv1 + after * conv2

        def norm(t):
            n, _ = norm_columns(mc_ref[r, :, t])
            norm_ref[r, :, t] = (n * col_ref[3] + col_ref[4]).astype(BF)

        pieces = [start] + [functools.partial(conv, t) for t in tiles(width, 32)]
        pieces += [functools.partial(norm, t) for t in tiles(seq, LANES)]
        return pieces + [mask]

    def project():
        normed = jnp.concatenate([norm_ref[r] for r in range(rows)], axis=1)
        for i, ref in enumerate((q_ref, k_ref, value_ref)):
            part = mm(wt_ref[i * width : (i + 1) * width], normed)
            part = (part * (head ** (-0.5) * math.log2(math.e)) if i == 0 else part).astype(BF)
            for r in range(rows):
                ref[r] = part[:, r * seq : (r + 1) * seq]
        for r in range(rows):
            key_ref[r] = k_ref[r].T
            v_ref[r] = value_ref[r].T

    def scores(r, p):
        low, high = [q_ref[r, h * head : (h + 1) * head] for h in (2 * p, 2 * p + 1)]
        both = jnp.concatenate([jnp.concatenate([low, zero], axis=1), jnp.concatenate([zero, high], axis=1)], axis=0)
        keys = jnp.concatenate([key_ref[r, :, 2 * p * head : 2 * (p + 1) * head], key_mask_ref[r]], axis=1)
        masks = jnp.concatenate([query_mask_ref[r], query_mask_ref[r]], axis=1)
        return mm(keys, jnp.concatenate([both, masks], axis=0))

    def attended(r, p):
        both = jnp.concatenate([e_ref[r, 2 * p], e_ref[r, 2 * p + 1]], axis=1)
        product = mm(value_ref[r, 2 * p * head : 2 * (p + 1) * head], both)
        parts = []
        for i in range(2):
            att = product[i * head : (i + 1) * head, i * seq : (i + 1) * seq] * inv_ref[r, 2 * p + i : 2 * p + i + 1]
            parts.append(att.astype(BF))
        return jnp.concatenate(parts, axis=0)

    def soften(r, p, product):
        for i in range(2):
            for t in tiles(seq, LANES):
                masked = product[:, i * seq + t.start : i * seq + t.stop]
                raised = jnp.exp2(masked - jnp.max(fold(masked, jnp.maximum), axis=0, keepdims=True))
                inv_ref[r, 2 * p + i : 2 * p + i + 1, t] = 1.0 / jnp.sum(fold(raised), axis=0, keepdims=True)
                e_ref[r, 2 * p + i, :, t] = raised.astype(BF)

    weave(*[preparation(r) for r in range(rows)])
    project()
    work = [(r, p) for r in range(rows) for p in range(HEADS // 2)]
    current, last = scores(*work[0]), None
    for at, (r, p) in enumerate(work):
        following = scores(*work[at + 1]) if at + 1 < len(work) else None
        finished = attended(*last) if last else None
        soften(r, p, current)
        if last:
            att_ref[last[0], 2 * last[1] * head : 2 * (last[1] + 1) * head] = finished
        current, last = following, (r, p)
    att_ref[last[0], 2 * last[1] * head : 2 * (last[1] + 1) * head] = attended(*last)


def gelu_parts(x):
    cdf = 0.5 * lax.erf(x * math.sqrt(0.5)) + 0.5
    bell = jnp.exp2(x * x * (-0.5 / math.log(2.0)) - 0.5 * math.log2(2.0 * math.pi))
    return x * cdf, cdf + x * bell


def feed_forward(index_ref, five_ref, mc_ref, ct_ref, packed_ref, *refs, pieces, shards):
    att_ref = five_ref.at[:, 0]
    groups = 2 if pieces > 1 else 1
    piece_refs = refs[:groups]
    hidden_out, mixed_out, gm_ref, ga_ref, gs_ref, down_ref = refs[groups : groups + 6]
    hidden_ref, mixed_ref = hidden_out.at[0], mixed_out.at[0]
    gw_refs = refs[groups + 6 : 2 * groups + 6]
    (
        up_ref, upt_ref, downt_ref, out_ref, outt_ref, up_acc, down_acc, out_acc, col_acc, col_ref,
        n_ref, norm_ref, ctt_ref, gp_ref, gn_ref, scale_ref, branch_ref,
    ) = refs[2 * groups + 6 :]
    rows, seq, width = ct_ref.shape
    ff = up_ref.shape[1]
    ffs = ff // shards
    own = width // pieces
    step = pl.program_id(0)

    @pl.when(step == 0)
    def _():
        for acc in (up_acc, down_acc, out_acc, col_acc):
            acc[...] = jnp.zeros_like(acc)
        for i in range(pieces):
            here = pl.ds(pl.multiple_of(index_ref[i] * own, 16), own)
            ref, first = piece_refs[i % groups], i // groups * (2 * shards + 1) * own
            for j in range(shards):
                at = first + 2 * j * own
                up_ref[here, j * ffs : (j + 1) * ffs] = ref[at : at + own]
                down_ref[here, j * ffs : (j + 1) * ffs] = ref[at + own : at + 2 * own]
            at = first + 2 * shards * own
            out_ref[here, :] = ref[at : at + own]
        upt_ref[...] = up_ref[...].T
        downt_ref[...] = down_ref[...].T
        outt_ref[...] = out_ref[...].T
        load_columns(packed_ref, col_ref, (5, 6))

    def lanes_of(r):
        return slice(r * seq, (r + 1) * seq)

    def spots_of(r):
        return [slice(at, at + LANES) for at in range(r * seq, (r + 1) * seq, LANES)]

    def preparation(r):
        lanes = lanes_of(r)

        def turn():
            ctt_ref[:, lanes] = ct_ref[r].T

        def norm(t):
            n, scale = norm_columns(mixed_ref[:, t])
            n_ref[:, t] = n
            scale_ref[0:1, t] = scale
            norm_ref[:, t] = (n * col_ref[0] + col_ref[1]).astype(BF)

        return [turn] + [functools.partial(norm, t) for t in spots_of(r)]

    def activation(block):
        pre = mm(upt_ref[block], norm_ref[...])
        grad_hidden = mm(downt_ref[block], ctt_ref[...])
        for low in range(0, block.stop - block.start, 16):
            part = slice(low, low + 16)
            here = slice(block.start + low, block.start + low + 16)
            hidden, slope = gelu_parts(pre[part])
            hidden_ref[here] = hidden.astype(BF)
            gp_ref[here] = (grad_hidden[part] * slope).astype(BF)

    def norm_back(r):
        spots = spots_of(r)
        mean_e = [jnp.zeros((8, LANES), F32) for _ in spots]
        mean_en = [jnp.zeros((8, LANES), F32) for _ in spots]
        means = []

        def sums(d):
            column = col_ref[0, d]
            gain_sum, shift_sum = col_acc[0, d], col_acc[1, d]
            for i, t in enumerate(spots):
                grad_n = gn_ref[d, t]
                product = grad_n * n_ref[d, t]
                gain_sum += product
                shift_sum += grad_n
                mean_e[i] += fold(grad_n * column)
                mean_en[i] += fold(product * column)
            col_acc[0, d] = gain_sum
            col_acc[1, d] = shift_sum

        def finish():
            for i in range(len(spots)):
                me = jnp.sum(mean_e[i], axis=0, keepdims=True) * (1.0 / width)
                men = jnp.sum(mean_en[i], axis=0, keepdims=True) * (1.0 / width)
                means.append((me, men))

        def apply(d):
            for i, t in enumerate(spots):
                me, men = means[i]
                change = scale_ref[0:1, t] * (gn_ref[d, t] * col_ref[0, d] - me - n_ref[d, t] * men)
                grad_mixed = ctt_ref[d, t].astype(F32) + change
                gm_ref[r, d, i * LANES : (i + 1) * LANES] = grad_mixed
                branch_ref[d, t] = grad_mixed.astype(BF)

        pieces = [functools.partial(sums, d) for d in tiles(width, 32)] + [finish]
        return pieces + [functools.partial(apply, d) for d in tiles(width, 32)]

    attended = jnp.concatenate([att_ref[r] for r in range(rows)], axis=1)
    branch = mm(outt_ref[...], attended)
    for r in range(rows):
        mixed_ref[:, lanes_of(r)] = mc_ref[r] + branch[:, lanes_of(r)]
    weave(*[preparation(r) for r in range(rows)])
    for block in tiles(ff, 128):
        activation(block)
    gn_ref[...] = mm(up_ref[...], gp_ref[...])
    down_acc[...] += mm_nt(ctt_ref[...], hidden_ref[...])
    up_acc[...] += mm_nt(norm_ref[...], gp_ref[...])
    weave(*[norm_back(r) for r in range(rows)])
    grad_attended = mm(out_ref[...], branch_ref[...]).astype(BF)
    for r in range(rows):
        ga_ref[r] = grad_attended[:, lanes_of(r)]
    out_acc[...] += mm_nt(attended, branch_ref[...])

    @pl.when(step == pl.num_programs(0) - 1)
    def _():
        for i in range(pieces):
            here = pl.ds(pl.multiple_of(index_ref[i] * own, 16), own)
            place = gw_refs[i % groups]
            for j in range(shards):
                cols = slice(j * ffs, (j + 1) * ffs)
                place[i // groups, :, 2 * j * ffs : (2 * j + 1) * ffs] = up_acc[here, cols].astype(BF)
                place[i // groups, :, (2 * j + 1) * ffs : (2 * j + 2) * ffs] = down_acc[here, cols].astype(BF)
            place[i // groups, :, 2 * ff :] = out_acc[here, :].astype(BF)
        gs_ref[...] = jnp.zeros_like(gs_ref)
        for i in range(2):
            gs_ref[5 + i : 6 + i] = jnp.sum(col_acc[i].T, axis=0, keepdims=True)


def layer_output(hidden_ref, mixed_ref, down_ref, lo_ref):
    rows, seq, _ = lo_ref.shape
    total = (mixed_ref[0] + mm(down_ref[...], hidden_ref[0])).astype(BF)
    for r in range(rows):
        lo_ref[r] = total[:, r * seq : (r + 1) * seq].T


def backward(
    five_ref, mc_ref, v_ref, e_ref, facts_ref, ga_ref, gm_ref, index_ref, w_ref, packed_ref, other_ref, ig_ref, gs_ref, *refs, pieces,
):
    x_ref, norm_ref, q_ref, k_ref, att_ref = [five_ref.at[:, i] for i in range(5)]
    aux_ref, inv_ref = facts_ref.at[:, :8], facts_ref.at[:, 8:]
    gw_refs = refs[:-11]
    (
        proj_ref, w_acc, norm_cat, soft_ref, logit_ref, gn_ref, acc_ref, col_ref, n_ref, g_ref, turn_ref
    ) = refs[-11:]
    rows, seq, width = v_ref.shape
    own = width // pieces
    head = width // HEADS
    step = pl.program_id(0)

    @pl.when(step == 0)
    def _():
        w_acc[...] = jnp.zeros_like(w_acc)
        acc_ref[...] = jnp.zeros_like(acc_ref)
        load_columns(packed_ref, col_ref, range(4))

    zero = jnp.zeros((head, seq), BF)
    work = [(r, p) for r in range(rows) for p in range(HEADS // 2)]

    def opening(r, p):
        grads, inners = [], []
        for h in (2 * p, 2 * p + 1):
            part = slice(h * head, (h + 1) * head)
            grad_att = ga_ref[r, part].astype(F32) * inv_ref[r, h : h + 1]
            inners.append(jnp.sum(fold(grad_att * att_ref[r, part].astype(F32)), axis=0, keepdims=True))
            grads.append(grad_att.astype(BF))
        low, high = grads
        both = jnp.concatenate([jnp.concatenate([low, zero], axis=1), jnp.concatenate([zero, high], axis=1)], axis=0)
        product = mm(v_ref[r, :, 2 * p * head : 2 * (p + 1) * head], both)
        soft_ref[r, 2 * p] = product[:, :seq]
        soft_ref[r, 2 * p + 1] = product[:, seq:]
        return jnp.concatenate(grads, axis=0), inners

    ready = opening(*work[0])
    for at, (r, p) in enumerate(work):
        grad_att, inners = ready
        if at + 1 < len(work):
            ready = opening(*work[at + 1])
        for i, h in enumerate((2 * p, 2 * p + 1)):
            for t in tiles(seq, 32):
                raised = e_ref[r, h, t].astype(F32)
                logit_ref[r, h, t] = (raised * (soft_ref[r, h, t] - inners[i])).astype(BF)
        part = slice(2 * p * head, 2 * (p + 1) * head)
        pair = slice(2 * p, 2 * p + 2)
        beside = jnp.concatenate([logit_ref[r, 2 * p], logit_ref[r, 2 * p + 1]], axis=1)
        grad_q = mm(k_ref[r, part], beside)
        grad_k = mm_nt(q_ref[r, part], logit_ref[r, pair].reshape(2 * seq, seq))
        grad_v = mm_nt(grad_att, e_ref[r, pair].reshape(2 * seq, seq))
        for i in range(2):
            place = slice(r * seq, (r + 1) * seq)
            own_rows, own_cols = slice(i * head, (i + 1) * head), slice(i * seq, (i + 1) * seq)
            for j, (grad, factor) in enumerate(((grad_q, head ** (-0.5)), (grad_k, math.log(2.0)), (grad_v, None))):
                first = j * width + (2 * p + i) * head
                mine = grad[own_rows, own_cols]
                proj_ref[first : first + head, place] = (mine if factor is None else mine * factor).astype(BF)
    gn_ref[...] = mm(w_ref[...], proj_ref[...])
    for r in range(rows):
        norm_cat[:, r * seq : (r + 1) * seq] = norm_ref[r]
    w_acc[...] += mm_nt(norm_cat[...], proj_ref[...])

    spots = tiles(seq, LANES)
    for r in range(rows):
        wide = [slice(r * seq + t.start, r * seq + t.stop) for t in spots]
        scales = []
        for t in spots:
            n, scale = norm_columns(mc_ref[r, :, t])
            n_ref[r, :, t] = n
            scales.append(scale)
        mean_e = [jnp.zeros((8, LANES), F32) for _ in spots]
        mean_en = [jnp.zeros((8, LANES), F32) for _ in spots]
        for d in tiles(width, 32):
            column = col_ref[3, d]
            gain_sum, shift_sum = acc_ref[3, d], acc_ref[4, d]
            for i, t in enumerate(spots):
                grad_n = gn_ref[d, wide[i]]
                product = grad_n * n_ref[r, d, t]
                gain_sum += product
                shift_sum += grad_n
                mean_e[i] += fold(grad_n * column)
                mean_en[i] += fold(product * column)
            acc_ref[3, d] = gain_sum
            acc_ref[4, d] = shift_sum
        for i, t in enumerate(spots):
            me = jnp.sum(mean_e[i], axis=0, keepdims=True) * (1.0 / width)
            men = jnp.sum(mean_en[i], axis=0, keepdims=True) * (1.0 / width)
            for d in tiles(width, 64):
                e = gn_ref[d, wide[i]] * col_ref[3, d]
                g_ref[r, d, t] = gm_ref[r, d, t] + scales[i] * (e - me - n_ref[r, d, t] * men)
        links, next_links = aux_ref[r, 0:1], aux_ref[r, 1:2]
        for d in tiles(width, 32):
            g = g_ref[r, d]
            base = x_ref[r, d].astype(F32)
            before = pltpu.roll(g, 1, 1) * links
            after = pltpu.roll(g, seq - 1, 1) * next_links
            acc_ref[0, d] += fold_lanes(base * after)
            acc_ref[1, d] += fold_lanes(base * g)
            acc_ref[2, d] += fold_lanes(base * before)
            conv0, conv1, conv2 = [twice(col_ref[i, d], seq) for i in range(3)]
            turn_ref[r, d] = (g + conv1 * g + conv0 * after + conv2 * before).astype(BF)
        ig_ref[r] = turn_ref[r].T

    @pl.when(step == pl.num_programs(0) - 1)
    def _():
        gs_ref[...] = other_ref[...]
        for i in range(5):
            gs_ref[i : i + 1] += jnp.sum(acc_ref[i].T, axis=0, keepdims=True)
        groups = len(gw_refs)
        for i in range(pieces):
            here = pl.ds(pl.multiple_of(index_ref[i] * own, 16), own)
            gw_refs[i % groups][i // groups] = w_acc[here, :].astype(BF)


def in_hbm(values):
    return pltpu.with_memory_space_constraint(values, pltpu.HBM)


def by_row(shape, rows, first=0):
    tail = tuple(shape[1:])
    return pl.BlockSpec((rows,) + tail, lambda i, *_: (i + first,) + (0,) * len(tail))


def whole(shape):
    place = (0,) * len(shape)
    return pl.BlockSpec(tuple(shape), lambda i, *_: place, pipeline_mode=pl.Buffered(1))


def step_rows(count, most):
    return max(r for r in range(1, most + 1) if count % r == 0)


def call(body, name, scalars, rows, row_args, args, row_outs, outs, scratch, span=None, into=None, near=(), only=None):
    first, count = span or (0, row_args[0].shape[0])
    skip = first // rows
    total = row_args[0].shape[0]

    def spec_of(shape):
        return by_row(shape, shape[0] * rows // total, skip)

    in_specs = [spec_of(a.shape) for a in row_args]
    if only:
        tail = row_args[0].shape[2:]
        in_specs[0] = pl.BlockSpec((rows, 1) + tail, lambda i, *_: (i, only) + (0,) * len(tail))
    in_specs += [whole(a.shape) for a in args]
    aliases = {}
    if into is not None:
        in_specs.append(pl.BlockSpec(memory_space=pl.ANY))
        aliases = {len(scalars) + len(in_specs) - 1: 0}
    spec = pltpu.PrefetchScalarGridSpec(
        num_scalar_prefetch=len(scalars),
        grid=(count // rows,),
        in_specs=in_specs,
        out_specs=[spec_of(s) for s, _ in row_outs] + [whole(s) for s, _ in outs],
        scratch_shapes=[pltpu.VMEM(s, t) for s, t in scratch],
    )
    return pl.pallas_call(
        body,
        grid_spec=spec,
        out_shape=[(jax.ShapeDtypeStruct if "out" + str(i) in near else pltpu.HBM)(s, t) for i, (s, t) in enumerate(row_outs)]
        + [jax.ShapeDtypeStruct(s, t) for s, t in outs],
        input_output_aliases=aliases,
        compiler_params=pltpu.CompilerParams(dimension_semantics=("arbitrary",), vmem_limit_bytes=VMEM_LIMITS[name] * MIB),
        name=name,
    )(*scalars, *[a if i in near else in_hbm(a) for i, a in enumerate(row_args)], *args, *(() if into is None else (into,)))


def small_call(body, name, args, outs, scratch=()):
    return pl.pallas_call(
        body,
        out_shape=[jax.ShapeDtypeStruct(s, t) for s, t in outs],
        scratch_shapes=[pltpu.VMEM(s, t) for s, t in scratch],
        compiler_params=pltpu.CompilerParams(vmem_limit_bytes=16 * MIB),
        name=name,
    )(*args)


def run_forward(index, tokens, segment_ids, valid_len, pieces):
    count, seq, width = tokens.shape
    flipped = (count, width, seq)
    rows = step_rows(count, 4)
    row_outs = [
        ((count, 5, width, seq), BF), (flipped, F32), ((count, seq, width), BF),
        ((count, HEADS, seq, seq), BF), ((count, 16, seq), F32),
    ]
    return call(
        functools.partial(forward_attention, pieces=index.shape[0]), "forward_attention", (index, in_hbm(valid_len)),
        rows, (tokens,), (in_hbm(segment_ids), *pieces),
        row_outs, [((width, VECTORS), BF), ((width, 3 * width), BF)],
        [
            ((3 * width, width), BF), ((width, 3 * width + VECTORS), BF), ((5, width, LANES), F32),
            ((rows, seq, LANES), BF), ((rows, LANES, seq), BF), ((rows, seq, width), BF), ((rows, width, seq), BF),
        ],
    )


def run_feed_forward(index, five, mixed, cotangent, packed, pieces, shards):
    count, seq, width = cotangent.shape
    own = width // index.shape[0]
    ff = shards * width
    groups = 2 if index.shape[0] > 1 else 1
    rows = step_rows(count, 2)
    wide = rows * seq
    row_outs = [
        ((count // rows, ff, wide), BF), ((count // rows, width, wide), F32),
        ((count, width, seq), F32), ((count, width, seq), BF),
    ]
    grads = ((index.shape[0] // groups, own, 2 * ff + width), BF)
    return call(
        functools.partial(feed_forward, pieces=index.shape[0], shards=shards), "feed_forward", (index,),
        rows, (five, mixed, cotangent), (packed, *pieces),
        row_outs, [((8, width), F32), ((width, ff), BF)] + [grads] * groups,
        [((width, ff), BF)] + [((ff, width), BF)] * 2 + [((width, width), BF)] * 2
        + [((width, ff), F32)] * 2 + [((width, width), F32), ((2, width, LANES), F32), ((2, width, LANES), F32)]
        + [((width, wide), F32), ((width, wide), BF), ((width, wide), BF)]
        + [((ff, wide), BF)]
        + [((width, wide), F32), ((8, wide), F32), ((width, wide), BF)],
        near=("out3",), only=4,
    )


def run_layer_output(hidden, mixed, down, shape, into, low, high):
    steps = hidden.shape[0]
    span = (int(low * steps), int(high * steps) - int(low * steps))

    def body(*refs):
        layer_output(*refs[:3], refs[-1])

    return call(body, "layer_output", (), 1, (hidden, mixed), (down,), [(shape, BF)], [], [], span=span, into=into)[0]


def run_backward(index, weight, kept, grads, packed, other, pieces):
    count, seq, width = kept[2].shape
    own = width // pieces
    groups = 2 if pieces > 1 else 1
    rows = step_rows(count, 3)
    row_args = (*kept, *grads)
    many = len(row_args)

    def body(index_ref, *refs):
        backward(*refs[:many], index_ref, *refs[many:], pieces=pieces)

    return call(
        body, "backward", (index,), rows, row_args, (weight, packed, other),
        [((count, seq, width), BF)], [((8, width), F32)] + [((pieces // groups, own, 3 * width), BF)] * groups,
        [
            ((3 * width, rows * seq), BF), ((width, 3 * width), F32), ((width, rows * seq), BF),
            ((rows, HEADS, seq, seq), F32), ((rows, HEADS, seq, seq), BF), ((width, rows * seq), F32),
            ((5, width, LANES), F32), ((4, width, LANES), F32), ((rows, width, seq), F32), ((rows, width, seq), F32),
            ((rows, width, seq), BF),
        ],
        near=(5,),
    )


def exchange(values, axis, offset):
    size = lax.axis_size(axis)
    return lax.ppermute(values, axis, [(i, i ^ offset) for i in range(size)])


def add_halves(mine, received):
    count, own, cols = mine.shape

    def body(mine_ref, received_ref, *out_refs):
        for i, ref in enumerate(out_refs):
            ref[...] = (mine_ref[i].astype(F32) + received_ref[i].astype(F32)).astype(BF)

    return small_call(body, "add_halves", (mine, received), [((own, cols), BF)] * count)


def add_wide(*items):
    return tree_sum(item.astype(F32) for item in items)


def store_high_low(ref, cols, values):
    high = values.astype(BF)
    low = (values - high.astype(F32)).astype(BF)
    ref[:, cols:] = jnp.concatenate([high, low, jnp.zeros((ref.shape[0] - 16, LANES), BF)], axis=0)


def load_high_low(ref, cols):
    both = ref[:16, cols:].astype(F32)
    return both[:8] + both[8:]


def add_halves_and_sums(index, mine, received, sums, received_sums):
    count, own, cols = mine.shape
    width = sums.shape[1]

    def body(index_ref, mine_ref, received_ref, sums_ref, received_sums_ref, *out_refs):
        total = sums_ref[...] + received_sums_ref[...]
        for i, ref in enumerate(out_refs):
            ref[:, :cols] = (mine_ref[i].astype(F32) + received_ref[i].astype(F32)).astype(BF)
            turned = pltpu.roll(total, lax.rem(width - index_ref[2 * i] * own, width), 1)[:, :LANES]
            store_high_low(ref, cols, turned)

    spec = pltpu.PrefetchScalarGridSpec(
        num_scalar_prefetch=1, grid=(1,),
        in_specs=[whole(a.shape) for a in (mine, received, sums, received_sums)],
        out_specs=[whole((own, cols + LANES))] * count,
    )
    return pl.pallas_call(
        body, grid_spec=spec, out_shape=[jax.ShapeDtypeStruct((own, cols + LANES), BF)] * count,
        compiler_params=pltpu.CompilerParams(vmem_limit_bytes=16 * MIB), name="add_halves_and_sums",
    )(index, mine, received, sums, received_sums)


def add_packed(name, items):
    cols = items[0].shape[1] - LANES

    def body(*refs):
        out_ref = refs[-1]
        out_ref[:, :cols] = tree_sum(ref[:, :cols].astype(F32) for ref in refs[:-1]).astype(BF)
        store_high_low(out_ref, cols, tree_sum(load_high_low(ref, cols) for ref in refs[:-1]))

    return small_call(body, name, items, [(items[0].shape, BF)])[0]


def add_last(items):
    own, cols = items[0].shape[0], items[0].shape[1] - LANES

    def body(*refs):
        ins, outs = refs[: len(items)], refs[len(items) :]
        outs[0][...] = tree_sum(ref[:, :cols].astype(F32) for ref in ins)
        vectors = tree_sum(load_high_low(ref, cols) for ref in ins)
        outs[1][...] = vectors[0:3, :own]
        for i in range(4):
            outs[2 + i][...] = vectors[3 + i : 4 + i, :own]

    return small_call(body, "add_last", items, [((own, cols), F32), ((3, own), F32)] + [((1, own), F32)] * 4)


def direct_plan(tokens, segment_ids, valid_len, qkv_weight, out_weight, up_weight, down_weight, conv_weight, vectors, cotangent):
    count, seq, width = tokens.shape
    own, ffs = up_weight.shape
    dp, mp = lax.axis_size("dp"), lax.axis_size("mp")
    me = lax.axis_index("dp")
    offsets = [2 * p for p in range(dp // 2)]
    index = jnp.stack([me ^ (p ^ c) for p in offsets for c in range(2)]).astype(jnp.int32)
    narrow, ff_own = small_call(
        pack_weights, "pack_weights",
        [in_hbm(a) for a in (qkv_weight, up_weight, down_weight, conv_weight, *[v.reshape(1, own) for v in vectors])],
        [((own, 3 * width + VECTORS), BF), ((2 * own, ffs), BF)], [((VECTORS, VECTORS), F32)],
    )
    across = [exchange(ff_own, "mp", j) for j in range(2, mp)]
    across[0], ff_own = lax.optimization_barrier((across[0], ff_own))
    shards = [ff_own, exchange(ff_own, "mp", 1)] + across
    plane = jnp.concatenate([narrow] + [exchange(narrow, "dp", p) for p in offsets[1:]], axis=0)
    pieces = [plane, exchange(plane, "dp", 1)]
    column = jnp.concatenate(shards + [out_weight], axis=0)
    columns = [column] + [exchange(column, "dp", p) for p in offsets[1:]]
    five, mixed, v, raised, facts, packed, weight = run_forward(
        index, tokens, segment_ids, valid_len, pieces
    )
    columns, five = lax.optimization_barrier((columns, five))
    columns = jnp.concatenate(columns, axis=0)
    pieces = [columns, exchange(columns, "dp", 1)]
    hidden, mixed_attn, grad_mixed, grad_att, sums2, down, mine, theirs = run_feed_forward(
        index, five, mixed, cotangent, packed, pieces, mp
    )
    received = exchange(theirs, "dp", 1)
    shape = cotangent.shape
    layer_out = run_layer_output(hidden, mixed_attn, down, shape, None, 0, 0.34)
    received, layer_out = lax.optimization_barrier((received, layer_out))
    parts = list(add_halves(mine, received))
    parts[0], grad_att = lax.optimization_barrier((parts[0], grad_att))
    plane = [parts[0]] + [exchange(parts[i], "dp", p) for i, p in enumerate(offsets) if i]
    kept = (five, mixed, v, raised, facts)
    input_grad, sums, mine_a, theirs_a = run_backward(
        index, weight, kept, (grad_att, grad_mixed), packed, sums2, dp
    )
    plane, theirs_a, sums = lax.optimization_barrier((plane, theirs_a, sums))
    received_a = exchange(theirs_a, "dp", 1)
    received_s = exchange(sums, "dp", 1)
    total = add_wide(*plane).astype(BF)
    part = 2 * ffs
    near, far, out_part = total[:, : 2 * part], total[:, 2 * part :], total[:, 4 * part :]
    parts = list(add_halves_and_sums(index, mine_a, received_a, sums, received_s))
    parts[0], far, hidden, layer_out = lax.optimization_barrier((parts[0], far, hidden, layer_out))
    plane_a = [parts[0]] + [exchange(parts[i], "dp", p) for i, p in enumerate(offsets) if i]
    received_f = exchange(far, "mp", 2)
    layer_out = run_layer_output(hidden, mixed_attn, down, shape, layer_out, 0.34, 0.67)
    plane_a, layer_out = lax.optimization_barrier((plane_a, layer_out))
    total = add_packed("add_plane", plane_a)
    received_1 = exchange(total, "mp", 1)
    total = add_packed("add_near", (total, received_1))
    received_2 = exchange(total, "mp", 2)
    received_f, _ = lax.optimization_barrier((received_f, total))
    near_sum = add_wide(near, received_f[:, : 2 * part])
    out_sum = lax.optimization_barrier(add_wide(out_part, received_f[:, 2 * part :]).astype(BF))
    keep = near_sum[:, :part]
    send = jnp.concatenate([near_sum[:, part:].astype(BF), out_sum], axis=1)
    received_n = exchange(send, "mp", 1)
    layer_out, _ = lax.optimization_barrier((layer_out, send))
    layer_out = run_layer_output(hidden, mixed_attn, down, shape, layer_out, 0.67, 1)
    received_2, layer_out = lax.optimization_barrier((received_2, layer_out))
    received_n, _ = lax.optimization_barrier((received_n, received_2))
    grad_up = keep[:, :ffs] + received_n[:, :ffs].astype(F32)
    grad_down = keep[:, ffs:] + received_n[:, ffs : 2 * ffs].astype(F32)
    grad_out = add_wide(out_sum, received_n[:, 2 * ffs :])
    grad_qkv, grad_conv, *grads = add_last((total, received_2))
    return (layer_out, input_grad, grad_qkv, grad_out, grad_up, grad_down, grad_conv, *[g.reshape(own) for g in grads])


def gathered_plan(tokens, segment_ids, valid_len, qkv_weight, out_weight, up_weight, down_weight, conv_weight, vectors, cotangent):
    count, seq, width = tokens.shape
    own = qkv_weight.shape[0]
    dp = width // own
    columns = jnp.stack([conv_weight[0], conv_weight[1], conv_weight[2], *vectors], axis=1)
    narrow = jnp.concatenate([qkv_weight, jnp.pad(columns, ((0, 0), (0, VECTORS - 7))), out_weight], axis=1)
    wide = lax.all_gather(narrow, "dp", axis=0, tiled=True)
    both = lax.all_gather(jnp.concatenate([up_weight, down_weight], axis=0), "mp", axis=1, tiled=True)
    ff = both.shape[1]
    shards = ff // width
    both = lax.all_gather(both, "dp", axis=0).reshape(dp, 2, own, shards, width)
    both = both.transpose(3, 1, 0, 2, 4).reshape(2 * ff, width)
    column = jnp.concatenate([both, wide[:, 3 * width + VECTORS :]], axis=0)
    index = jnp.zeros((1,), jnp.int32)
    five, mixed, v, raised, facts, packed, weight = run_forward(
        index, tokens, segment_ids, valid_len, [wide[:, : 3 * width + VECTORS]]
    )
    hidden, mixed_attn, grad_mixed, grad_att, sums2, down, grads = run_feed_forward(
        index, five, mixed, cotangent, packed, [column], shards
    )
    kept = (five, mixed, v, raised, facts)
    layer_out = run_layer_output(hidden, mixed_attn, down, cotangent.shape, None, 0, 1)
    input_grad, sums, grad_qkv = run_backward(index, weight, kept, (grad_att, grad_mixed), packed, sums2, 1)
    grad_ff = grads[0, :, : 2 * ff].reshape(width, shards, 2, width).transpose(0, 2, 1, 3).reshape(width, 2 * ff)
    grad_ff = lax.psum_scatter(grad_ff, "dp", scatter_dimension=0, tiled=True).reshape(own, 2, ff)
    grad_ff = lax.psum_scatter(grad_ff, "mp", scatter_dimension=2, tiled=True).astype(F32)
    grad_attn = jnp.concatenate([grad_qkv[0], grads[0, :, 2 * ff :]], axis=1)
    grad_attn = lax.psum_scatter(grad_attn, "dp", scatter_dimension=0, tiled=True)
    grad_attn = lax.psum(grad_attn, "mp").astype(F32)
    sums = lax.psum(sums, ("dp", "mp"))
    sums = lax.dynamic_slice_in_dim(sums, lax.axis_index("dp") * own, own, axis=1)
    return (
        layer_out, input_grad, grad_attn[:, : 3 * width], grad_attn[:, 3 * width :],
        grad_ff[:, 0], grad_ff[:, 1], sums[0:3], sums[3], sums[4], sums[5], sums[6],
    )


def on_device(
    tokens, segment_ids, valid_len, qkv_weight, out_weight, up_weight, down_weight, conv_weight,
    ln1_gain, ln1_shift, ln2_gain, ln2_shift, cotangent,
):
    own, ffs = up_weight.shape
    direct = own % 16 == 0 and ffs == tokens.shape[2] and own <= VECTORS and lax.axis_size("mp") == 4
    plan = direct_plan if direct else gathered_plan
    return plan(
        tokens, segment_ids, valid_len, qkv_weight, out_weight, up_weight, down_weight, conv_weight,
        (ln1_gain, ln1_shift, ln2_gain, ln2_shift), cotangent,
    )


def solution(mesh):
    rows = P(("dp", "mp"), None, None)
    weights = (P("dp", None), P("dp", None), P("dp", "mp"), P("dp", "mp"), P(None, "dp"))
    vectors = (P("dp"),) * 4
    return jax.shard_map(
        on_device,
        mesh=mesh,
        in_specs=(rows, P(("dp", "mp"), None), P(("dp", "mp"))) + weights + vectors + (rows,),
        out_specs=(rows, rows) + weights + vectors,
        check_vma=False,
    )
```

```python
import functools
import math

import jax
import jax.numpy as jnp
from jax import lax
from jax.experimental import pallas as pl
from jax.experimental.pallas import tpu as pltpu
from jax.sharding import PartitionSpec as P

HEADS = 6
VECTORS = 128
LANES = 128
BF = jnp.bfloat16
F32 = jnp.float32
MIB = 1024 * 1024
VMEM_LIMITS = dict(forward_attention=32, feed_forward=44, backward=42, layer_output=16)


def mm(lhs, rhs):
    return lax.dot_general(lhs, rhs, (((1,), (0,)), ((), ())), preferred_element_type=F32)


def mm_nt(lhs, rhs):
    return lax.dot_general(lhs, rhs, (((1,), (1,)), ((), ())), preferred_element_type=F32)


def tree_sum(items):
    items = list(items)
    while len(items) > 1:
        items = [a + b for a, b in zip(items[::2], items[1::2])]
    return items[0]


def pack_weights(qkv_ref, up_ref, down_ref, conv_ref, g1_ref, s1_ref, g2_ref, s2_ref, narrow_ref, ff_ref, rows_ref):
    own, ffs = up_ref.shape
    rows_ref[...] = jnp.zeros_like(rows_ref)
    rows_ref[0:3, :own] = conv_ref[...].astype(F32)
    for i, ref in enumerate((g1_ref, s1_ref, g2_ref, s2_ref)):
        rows_ref[3 + i : 4 + i, :own] = ref[...].astype(F32)
    wide = qkv_ref.shape[1]
    narrow_ref[:, :wide] = qkv_ref[...]
    narrow_ref[:, wide:] = rows_ref[...].T[:own].astype(BF)
    ff_ref[:own] = up_ref[...]
    ff_ref[own:] = down_ref[...]


def tiles(total, size):
    return [slice(at, at + size) for at in range(0, total, size)]


def weave(*strands):
    strands = [strand for strand in strands if strand]
    total = sum(len(strand) for strand in strands)
    pieces = [((i + 0.5) / len(strand), j, piece) for j, strand in enumerate(strands) for i, piece in enumerate(strand)]
    assert len(pieces) == total
    for _, _, piece in sorted(pieces, key=lambda item: item[:2]):
        piece()


def twice(tile, lanes):
    return jnp.concatenate([tile] * (lanes // LANES), axis=1)


def load_columns(packed_ref, col_ref, places):
    for i, place in enumerate(places):
        column = packed_ref[:, place : place + 1].astype(F32)
        col_ref[i] = jnp.broadcast_to(column, (column.shape[0], LANES))


def pairwise(items, combine):
    items = list(items)
    while len(items) > 1:
        odd = items[len(items) // 2 * 2 :]
        items = [combine(a, b) for a, b in zip(items[::2], items[1::2])] + odd
    return items[0]


def fold(values, combine=jnp.add):
    return pairwise([values[t] for t in tiles(values.shape[0], 8)], combine)


def column_mean(values):
    return jnp.sum(fold(values), axis=0, keepdims=True) * (1.0 / values.shape[0])


def norm_columns(values):
    centred = values - column_mean(values)
    scale = lax.rsqrt(column_mean(centred * centred) + 1e-06)
    return centred * scale, scale


def fold_lanes(values):
    return sum(values[:, t] for t in tiles(values.shape[1], LANES))


def forward_attention(index_ref, len_ref, tok_ref, seg_ref, *refs, pieces):
    cores = 2 if pieces > 1 else 1
    piece_refs = refs[:cores]
    (
        five_ref, mc_ref, v_ref, e_ref, facts_ref, packed_ref, w_ref,
        wt_ref, wide_ref, col_ref, key_mask_ref, query_mask_ref, key_ref, value_ref,
    ) = refs[cores:]
    x_ref, norm_ref, q_ref, k_ref, att_ref = [five_ref.at[:, i] for i in range(5)]
    aux_ref, inv_ref = facts_ref.at[:, :8], facts_ref.at[:, 8:]
    rows, seq, width = tok_ref.shape
    head = width // HEADS
    step = pl.program_id(0)

    @pl.when(step == 0)
    def _():
        own = width // pieces
        for i in range(pieces):
            here = pl.ds(pl.multiple_of(index_ref[i] * own, 16), own)
            wide_ref[here, :] = piece_refs[i % cores][i // cores * own : (i // cores + 1) * own]
        w_ref[...] = wide_ref[:, : 3 * width]
        wt_ref[...] = wide_ref[:, : 3 * width].T
        packed_ref[...] = wide_ref[:, 3 * width :]
        load_columns(packed_ref, col_ref, range(5))
        col_ref[1] = col_ref[1] + 1.0

    place = lax.broadcasted_iota(jnp.int32, (1, seq), 1)
    zero = jnp.zeros((head, seq), BF)

    def preparation(r):
        known = {}

        def start():
            segs = seg_ref[pl.ds(step * rows + r, 1), :].astype(F32)
            valid = place < len_ref[step * rows + r]
            number = jnp.where(valid, segs, -1.0)
            links = jnp.where(valid & (place > 0) & (number == pltpu.roll(number, 1, 1)), 1.0, 0.0)
            next_links = jnp.where(place < seq - 1, pltpu.roll(links, seq - 1, 1), 0.0)
            none = jnp.zeros_like(links)
            aux = jnp.concatenate([links, next_links, number, none, none, none, none, none], axis=0)
            aux_ref[r] = aux
            x_ref[r] = tok_ref[r].T
            known.update(segs=segs, links=links, next_links=next_links, key_number=aux.T[:, 2:3])

        def mask():
            number = known["key_number"]
            lane = lax.broadcasted_iota(jnp.int32, (seq, LANES), 1)
            itself = lax.broadcasted_iota(jnp.int32, (seq, LANES), 0) - (seq - LANES)
            chosen = (lane.astype(F32) == number) | ((number < 0.0) & (lane == itself))
            key_mask_ref[r] = jnp.where(chosen, 1.0, 0.0).astype(BF)
            slot = lax.broadcasted_iota(jnp.int32, (LANES, seq), 0)
            itself = lax.broadcasted_iota(jnp.int32, (LANES, seq), 1) - (seq - LANES)
            open_to = (slot.astype(F32) == known["segs"]) | ((slot >= LANES // 2) & (slot == itself))
            query_mask_ref[r] = jnp.where(open_to, 0.0, -1e30).astype(BF)

        def conv(t):
            base = x_ref[r, t].astype(F32)
            before = pltpu.roll(base, 1, 1) * known["links"]
            after = pltpu.roll(base, seq - 1, 1) * known["next_links"]
            conv0, conv1, conv2 = [twice(col_ref[i, t], seq) for i in range(3)]
            mc_ref[r, t] = before * conv0 + base * conv1 + after * conv2

        def norm(t):
            n, _ = norm_columns(mc_ref[r, :, t])
            norm_ref[r, :, t] = (n * col_ref[3] + col_ref[4]).astype(BF)

        pieces = [start] + [functools.partial(conv, t) for t in tiles(width, 32)]
        pieces += [functools.partial(norm, t) for t in tiles(seq, LANES)]
        return pieces + [mask]

    def project():
        normed = jnp.concatenate([norm_ref[r] for r in range(rows)], axis=1)
        for i, ref in enumerate((q_ref, k_ref, value_ref)):
            part = mm(wt_ref[i * width : (i + 1) * width], normed)
            part = (part * (head ** (-0.5) * math.log2(math.e)) if i == 0 else part).astype(BF)
            for r in range(rows):
                ref[r] = part[:, r * seq : (r + 1) * seq]
        for r in range(rows):
            key_ref[r] = k_ref[r].T
            v_ref[r] = value_ref[r].T

    def scores(r, p):
        low, high = [q_ref[r, h * head : (h + 1) * head] for h in (2 * p, 2 * p + 1)]
        both = jnp.concatenate([jnp.concatenate([low, zero], axis=1), jnp.concatenate([zero, high], axis=1)], axis=0)
        keys = jnp.concatenate([key_ref[r, :, 2 * p * head : 2 * (p + 1) * head], key_mask_ref[r]], axis=1)
        masks = jnp.concatenate([query_mask_ref[r], query_mask_ref[r]], axis=1)
        return mm(keys, jnp.concatenate([both, masks], axis=0))

    def attended(r, p):
        both = jnp.concatenate([e_ref[r, 2 * p], e_ref[r, 2 * p + 1]], axis=1)
        product = mm(value_ref[r, 2 * p * head : 2 * (p + 1) * head], both)
        parts = []
        for i in range(2):
            att = product[i * head : (i + 1) * head, i * seq : (i + 1) * seq] * inv_ref[r, 2 * p + i : 2 * p + i + 1]
            parts.append(att.astype(BF))
        return jnp.concatenate(parts, axis=0)

    def soften(r, p, product):
        for i in range(2):
            for t in tiles(seq, LANES):
                masked = product[:, i * seq + t.start : i * seq + t.stop]
                raised = jnp.exp2(masked - jnp.max(fold(masked, jnp.maximum), axis=0, keepdims=True))
                inv_ref[r, 2 * p + i : 2 * p + i + 1, t] = 1.0 / jnp.sum(fold(raised), axis=0, keepdims=True)
                e_ref[r, 2 * p + i, :, t] = raised.astype(BF)

    weave(*[preparation(r) for r in range(rows)])
    project()
    work = [(r, p) for r in range(rows) for p in range(HEADS // 2)]
    current, last = scores(*work[0]), None
    for at, (r, p) in enumerate(work):
        following = scores(*work[at + 1]) if at + 1 < len(work) else None
        finished = attended(*last) if last else None
        soften(r, p, current)
        if last:
            att_ref[last[0], 2 * last[1] * head : 2 * (last[1] + 1) * head] = finished
        current, last = following, (r, p)
    att_ref[last[0], 2 * last[1] * head : 2 * (last[1] + 1) * head] = attended(*last)


def gelu_parts(y):
    twice_cdf = lax.erf(y) + 1.0
    bell = jnp.exp2(y * y * -math.log2(math.e) + math.log2(2.0 / math.sqrt(math.pi)))
    return y * twice_cdf, twice_cdf + y * bell


def feed_forward(index_ref, five_ref, mc_ref, ct_ref, packed_ref, *refs, pieces, shards):
    att_ref = five_ref.at[:, 0]
    groups = 2 if pieces > 1 else 1
    piece_refs = refs[:groups]
    hidden_out, mixed_out, gm_ref, ga_ref, gs_ref, down_ref = refs[groups : groups + 6]
    gw_refs = refs[groups + 6 : 2 * groups + 6]
    (
        up_ref, upt_ref, downt_ref, out_ref, outt_ref, up_acc, down_acc, out_acc, col_acc, col_ref,
        n_ref, norm_ref, ctt_ref, gp_ref, gn_ref, scale_ref, branch_ref,
    ) = refs[2 * groups + 6 :]
    rows, seq, width = ct_ref.shape
    ff = up_ref.shape[1]
    ffs = ff // shards
    own = width // pieces
    step = pl.program_id(0)

    @pl.when(step == 0)
    def _():
        for acc in (up_acc, down_acc, out_acc, col_acc):
            acc[...] = jnp.zeros_like(acc)
        for i in range(pieces):
            here = pl.ds(pl.multiple_of(index_ref[i] * own, 16), own)
            ref, first = piece_refs[i % groups], i // groups * (2 * shards + 1) * own
            for j in range(shards):
                at = first + 2 * j * own
                up_ref[here, j * ffs : (j + 1) * ffs] = ref[at : at + own]
                down_ref[here, j * ffs : (j + 1) * ffs] = ref[at + own : at + 2 * own]
            at = first + 2 * shards * own
            out_ref[here, :] = ref[at : at + own]
        upt_ref[...] = up_ref[...].T
        downt_ref[...] = down_ref[...].T
        outt_ref[...] = out_ref[...].T
        load_columns(packed_ref, col_ref, (5, 6, 5))
        for i, factor in enumerate((0.5, math.sqrt(0.5), math.sqrt(0.5))):
            col_ref[i] = col_ref[i] * factor

    def begin(g):
        pair = range(g * paired, (g + 1) * paired)
        attended = jnp.concatenate([att_ref[r] for r in pair], axis=1)
        branch = mm(outt_ref[...], attended)
        for i, r in enumerate(pair):
            lanes = slice(i * seq, (i + 1) * seq)
            ctt_ref[g, :, lanes] = ct_ref[r].T
            mixed_out[g, :, lanes] = mc_ref[r] + branch[:, lanes]
        for t in spots:
            n, scale = norm_columns(mixed_out[g, :, t])
            n_ref[g, :, t] = n
            scale_ref[g, 0:1, t] = scale
            norm_ref[g, :, t] = (n * col_ref[2] + col_ref[1]).astype(BF)

    def activate(g, block):
        pre = mm(upt_ref[block], norm_ref[g])
        grad_hidden = mm(downt_ref[block], ctt_ref[g])
        for low in range(0, block.stop - block.start, 16):
            part = slice(low, low + 16)
            here = slice(block.start + low, block.start + low + 16)
            hidden, slope = gelu_parts(pre[part])
            hidden_out[g, here] = hidden.astype(BF)
            gp_ref[g, here] = (grad_hidden[part] * slope).astype(BF)

    def weigh(g):
        gn_ref[g] = mm(up_ref[...], gp_ref[g])
        down_acc[...] += mm_nt(ctt_ref[g], hidden_out[g])
        up_acc[...] += mm_nt(norm_ref[g], gp_ref[g])

    def norm_back(g):
        mean_e = [jnp.zeros((8, LANES), F32) for _ in spots]
        mean_en = [jnp.zeros((8, LANES), F32) for _ in spots]
        for d in tiles(width, 32):
            column = col_ref[0, d]
            gain_sum, shift_sum = col_acc[0, d], col_acc[1, d]
            for i, t in enumerate(spots):
                grad_n = gn_ref[g, d, t]
                product = grad_n * n_ref[g, d, t]
                gain_sum += product
                shift_sum += grad_n
                mean_e[i] += fold(grad_n * column)
                mean_en[i] += fold(product * column)
            col_acc[0, d] = gain_sum
            col_acc[1, d] = shift_sum
        for i, t in enumerate(spots):
            me = jnp.sum(mean_e[i], axis=0, keepdims=True) * (1.0 / width)
            men = jnp.sum(mean_en[i], axis=0, keepdims=True) * (1.0 / width)
            row, inside = divmod(t.start, seq)
            for d in tiles(width, 32):
                change = scale_ref[g, 0:1, t] * (gn_ref[g, d, t] * col_ref[0, d] - me - n_ref[g, d, t] * men)
                grad_mixed = ctt_ref[g, d, t].astype(F32) + change
                gm_ref[g * paired + row, d, inside : inside + LANES] = grad_mixed
                branch_ref[g, d, t] = grad_mixed.astype(BF)

    def end(g):
        pair = range(g * paired, (g + 1) * paired)
        attended = jnp.concatenate([att_ref[r] for r in pair], axis=1)
        grad_attended = mm(out_ref[...], branch_ref[g]).astype(BF)
        for i, r in enumerate(pair):
            ga_ref[r] = grad_attended[:, i * seq : (i + 1) * seq]
        out_acc[...] += mm_nt(attended, branch_ref[g])

    pairs = n_ref.shape[0]
    paired = rows // pairs
    spots = tiles(paired * seq, LANES)
    begin(0)
    for g in range(pairs):
        for block in tiles(ff, 128):
            activate(g, block)
        if g + 1 < pairs:
            begin(g + 1)
        weigh(g)
        norm_back(g)
        end(g)

    @pl.when(step == pl.num_programs(0) - 1)
    def _():
        for i in range(pieces):
            here = pl.ds(pl.multiple_of(index_ref[i] * own, 16), own)
            place = gw_refs[i % groups]
            for j in range(shards):
                cols = slice(j * ffs, (j + 1) * ffs)
                place[i // groups, :, 2 * j * ffs : (2 * j + 1) * ffs] = (up_acc[here, cols] * math.sqrt(0.5)).astype(BF)
                place[i // groups, :, (2 * j + 1) * ffs : (2 * j + 2) * ffs] = (down_acc[here, cols] * math.sqrt(0.5)).astype(BF)
            place[i // groups, :, 2 * ff :] = out_acc[here, :].astype(BF)
        gs_ref[...] = jnp.zeros_like(gs_ref)
        for i in range(2):
            gs_ref[5 + i : 6 + i] = jnp.sum(col_acc[i].T, axis=0, keepdims=True) * 0.5


def layer_output(hidden_ref, mixed_ref, down_ref, lo_ref):
    rows, seq, _ = lo_ref.shape
    total = (mixed_ref[0] + mm(down_ref[...], hidden_ref[0]) * math.sqrt(0.5)).astype(BF)
    for r in range(rows):
        lo_ref[r] = total[:, r * seq : (r + 1) * seq].T


def backward(
    five_ref, mc_ref, v_ref, e_ref, facts_ref, ga_ref, gm_ref, index_ref, w_ref, packed_ref, other_ref, ig_ref, gs_ref, *refs, pieces,
):
    x_ref, norm_ref, q_ref, k_ref, att_ref = [five_ref.at[:, i] for i in range(5)]
    aux_ref, inv_ref = facts_ref.at[:, :8], facts_ref.at[:, 8:]
    gw_refs = refs[:-11]
    (
        proj_ref, w_acc, norm_cat, soft_ref, logit_ref, gn_ref, acc_ref, col_ref, n_ref, g_ref, turn_ref
    ) = refs[-11:]
    rows, seq, width = v_ref.shape
    own = width // pieces
    head = width // HEADS
    step = pl.program_id(0)

    @pl.when(step == 0)
    def _():
        w_acc[...] = jnp.zeros_like(w_acc)
        acc_ref[...] = jnp.zeros_like(acc_ref)
        load_columns(packed_ref, col_ref, range(4))
        col_ref[1] = col_ref[1] + 1.0

    zero = jnp.zeros((head, seq), BF)
    work = [(r, p) for r in range(rows) for p in range(HEADS // 2)]

    def opening(r, p):
        grads, inners = [], []
        for h in (2 * p, 2 * p + 1):
            part = slice(h * head, (h + 1) * head)
            grad_att = ga_ref[r, part].astype(F32) * inv_ref[r, h : h + 1]
            inners.append(jnp.sum(fold(grad_att * att_ref[r, part].astype(F32)), axis=0, keepdims=True))
            grads.append(grad_att.astype(BF))
        low, high = grads
        both = jnp.concatenate([jnp.concatenate([low, zero], axis=1), jnp.concatenate([zero, high], axis=1)], axis=0)
        product = mm(v_ref[r, :, 2 * p * head : 2 * (p + 1) * head], both)
        soft_ref[r, 2 * p] = product[:, :seq]
        soft_ref[r, 2 * p + 1] = product[:, seq:]
        return jnp.concatenate(grads, axis=0), inners

    spots = tiles(seq, LANES)

    def finish_row(r):
        wide = [slice(r * seq + t.start, r * seq + t.stop) for t in spots]
        lanes = slice(r * seq, (r + 1) * seq)
        norm_cat[:, lanes] = norm_ref[r]
        gn_ref[:, lanes] = mm(w_ref[...], proj_ref[:, lanes])
        scales = []
        for t in spots:
            n, scale = norm_columns(mc_ref[r, :, t])
            n_ref[r, :, t] = n
            scales.append(scale)
        mean_e = [jnp.zeros((8, LANES), F32) for _ in spots]
        mean_en = [jnp.zeros((8, LANES), F32) for _ in spots]
        for d in tiles(width, 32):
            column = col_ref[3, d]
            gain_sum, shift_sum = acc_ref[3, d], acc_ref[4, d]
            for i, t in enumerate(spots):
                grad_n = gn_ref[d, wide[i]]
                product = grad_n * n_ref[r, d, t]
                gain_sum += product
                shift_sum += grad_n
                mean_e[i] += fold(grad_n * column)
                mean_en[i] += fold(product * column)
            acc_ref[3, d] = gain_sum
            acc_ref[4, d] = shift_sum
        for i, t in enumerate(spots):
            me = jnp.sum(mean_e[i], axis=0, keepdims=True) * (1.0 / width)
            men = jnp.sum(mean_en[i], axis=0, keepdims=True) * (1.0 / width)
            for d in tiles(width, 64):
                e = gn_ref[d, wide[i]] * col_ref[3, d]
                g_ref[r, d, t] = gm_ref[r, d, t] + scales[i] * (e - me - n_ref[r, d, t] * men)
        links, next_links = aux_ref[r, 0:1], aux_ref[r, 1:2]
        for d in tiles(width, 32):
            g = g_ref[r, d]
            base = x_ref[r, d].astype(F32)
            before = pltpu.roll(g, 1, 1) * links
            after = pltpu.roll(g, seq - 1, 1) * next_links
            acc_ref[0, d] += fold_lanes(base * after)
            acc_ref[1, d] += fold_lanes(base * g)
            acc_ref[2, d] += fold_lanes(base * before)
            conv0, conv1, conv2 = [twice(col_ref[i, d], seq) for i in range(3)]
            turn_ref[r, d] = (conv1 * g + conv0 * after + conv2 * before).astype(BF)
        ig_ref[r] = turn_ref[r].T

    ready = opening(*work[0])
    for at, (r, p) in enumerate(work):
        grad_att, inners = ready
        if at + 1 < len(work):
            ready = opening(*work[at + 1])
        for i, h in enumerate((2 * p, 2 * p + 1)):
            for t in tiles(seq, 32):
                raised = e_ref[r, h, t].astype(F32)
                logit_ref[r, h, t] = (raised * (soft_ref[r, h, t] - inners[i])).astype(BF)
        part = slice(2 * p * head, 2 * (p + 1) * head)
        pair = slice(2 * p, 2 * p + 2)
        beside = jnp.concatenate([logit_ref[r, 2 * p], logit_ref[r, 2 * p + 1]], axis=1)
        grad_q = mm(k_ref[r, part], beside)
        grad_k = mm_nt(q_ref[r, part], logit_ref[r, pair].reshape(2 * seq, seq))
        grad_v = mm_nt(grad_att, e_ref[r, pair].reshape(2 * seq, seq))
        for i in range(2):
            place = slice(r * seq, (r + 1) * seq)
            own_rows, own_cols = slice(i * head, (i + 1) * head), slice(i * seq, (i + 1) * seq)
            for j, (grad, factor) in enumerate(((grad_q, head ** (-0.5)), (grad_k, math.log(2.0)), (grad_v, None))):
                first = j * width + (2 * p + i) * head
                mine = grad[own_rows, own_cols]
                proj_ref[first : first + head, place] = (mine if factor is None else mine * factor).astype(BF)
        if p == HEADS // 2 - 1:
            finish_row(r)
    w_acc[...] += mm_nt(norm_cat[...], proj_ref[...])

    @pl.when(step == pl.num_programs(0) - 1)
    def _():
        gs_ref[...] = other_ref[...]
        for i in range(5):
            gs_ref[i : i + 1] += jnp.sum(acc_ref[i].T, axis=0, keepdims=True)
        groups = len(gw_refs)
        for i in range(pieces):
            here = pl.ds(pl.multiple_of(index_ref[i] * own, 16), own)
            gw_refs[i % groups][i // groups] = w_acc[here, :].astype(BF)


def in_hbm(values):
    return pltpu.with_memory_space_constraint(values, pltpu.HBM)


def by_row(shape, rows, first=0):
    tail = tuple(shape[1:])
    return pl.BlockSpec((rows,) + tail, lambda i, *_: (i + first,) + (0,) * len(tail))


def whole(shape):
    place = (0,) * len(shape)
    return pl.BlockSpec(tuple(shape), lambda i, *_: place, pipeline_mode=pl.Buffered(1))


def step_rows(count, most):
    return max(r for r in range(1, most + 1) if count % r == 0)


def call(body, name, scalars, rows, row_args, args, row_outs, outs, scratch, span=None, into=None, near=(), only=None):
    first, count = span or (0, row_args[0].shape[0])
    skip = first // rows
    total = row_args[0].shape[0]

    def spec_of(shape):
        return by_row(shape, shape[0] * rows // total, skip)

    in_specs = [spec_of(a.shape) for a in row_args]
    if only:
        tail = row_args[0].shape[2:]
        in_specs[0] = pl.BlockSpec((rows, 1) + tail, lambda i, *_: (i, only) + (0,) * len(tail))
    in_specs += [whole(a.shape) for a in args]
    aliases = {}
    if into is not None:
        in_specs.append(pl.BlockSpec(memory_space=pl.ANY))
        aliases = {len(scalars) + len(in_specs) - 1: 0}
    spec = pltpu.PrefetchScalarGridSpec(
        num_scalar_prefetch=len(scalars),
        grid=(count // rows,),
        in_specs=in_specs,
        out_specs=[spec_of(s) for s, _ in row_outs] + [whole(s) for s, _ in outs],
        scratch_shapes=[pltpu.VMEM(s, t) for s, t in scratch],
    )
    return pl.pallas_call(
        body,
        grid_spec=spec,
        out_shape=[(jax.ShapeDtypeStruct if "out" + str(i) in near else pltpu.HBM)(s, t) for i, (s, t) in enumerate(row_outs)]
        + [jax.ShapeDtypeStruct(s, t) for s, t in outs],
        input_output_aliases=aliases,
        compiler_params=pltpu.CompilerParams(dimension_semantics=("arbitrary",), vmem_limit_bytes=VMEM_LIMITS[name] * MIB),
        name=name,
    )(*scalars, *[a if i in near else in_hbm(a) for i, a in enumerate(row_args)], *args, *(() if into is None else (into,)))


def small_call(body, name, args, outs, scratch=()):
    return pl.pallas_call(
        body,
        out_shape=[jax.ShapeDtypeStruct(s, t) for s, t in outs],
        scratch_shapes=[pltpu.VMEM(s, t) for s, t in scratch],
        compiler_params=pltpu.CompilerParams(vmem_limit_bytes=16 * MIB),
        name=name,
    )(*args)


def run_forward(index, tokens, segment_ids, valid_len, pieces):
    count, seq, width = tokens.shape
    flipped = (count, width, seq)
    rows = step_rows(count, 3)
    row_outs = [
        ((count, 5, width, seq), BF), (flipped, F32), ((count, seq, width), BF),
        ((count, HEADS, seq, seq), BF), ((count, 16, seq), F32),
    ]
    return call(
        functools.partial(forward_attention, pieces=index.shape[0]), "forward_attention", (index, in_hbm(valid_len)),
        rows, (tokens,), (in_hbm(segment_ids), *pieces),
        row_outs, [((width, VECTORS), BF), ((width, 3 * width), BF)],
        [
            ((3 * width, width), BF), ((width, 3 * width + VECTORS), BF), ((5, width, LANES), F32),
            ((rows, seq, LANES), BF), ((rows, LANES, seq), BF), ((rows, seq, width), BF), ((rows, width, seq), BF),
        ],
    )


def run_feed_forward(index, five, mixed, cotangent, packed, pieces, shards):
    count, seq, width = cotangent.shape
    own = width // index.shape[0]
    ff = shards * width
    groups = 2 if index.shape[0] > 1 else 1
    paired = step_rows(count, 2)
    pairs = 2 if count // paired % 2 == 0 else 1
    rows = pairs * paired
    wide = paired * seq
    row_outs = [
        ((count // paired, ff, wide), BF), ((count // paired, width, wide), F32),
        ((count, width, seq), F32), ((count, width, seq), BF),
    ]
    grads = ((index.shape[0] // groups, own, 2 * ff + width), BF)
    return call(
        functools.partial(feed_forward, pieces=index.shape[0], shards=shards), "feed_forward", (index,),
        rows, (five, mixed, cotangent), (packed, *pieces),
        row_outs, [((8, width), F32), ((width, ff), BF)] + [grads] * groups,
        [((width, ff), BF)] + [((ff, width), BF)] * 2 + [((width, width), BF)] * 2
        + [((width, ff), F32)] * 2 + [((width, width), F32), ((2, width, LANES), F32), ((3, width, LANES), F32)]
        + [((pairs, width, wide), F32), ((pairs, width, wide), BF), ((pairs, width, wide), BF)]
        + [((pairs, ff, wide), BF)]
        + [((pairs, width, wide), F32), ((pairs, 8, wide), F32), ((pairs, width, wide), BF)],
        near=("out3",), only=4,
    )


def run_layer_output(hidden, mixed, down, shape, into, low, high):
    steps = hidden.shape[0]
    span = (int(low * steps), int(high * steps) - int(low * steps))

    def body(*refs):
        layer_output(*refs[:3], refs[-1])

    return call(body, "layer_output", (), 1, (hidden, mixed), (down,), [(shape, BF)], [], [], span=span, into=into)[0]


def run_backward(index, weight, kept, grads, packed, other, pieces):
    count, seq, width = kept[2].shape
    own = width // pieces
    groups = 2 if pieces > 1 else 1
    rows = step_rows(count, 3)
    row_args = (*kept, *grads)
    many = len(row_args)

    def body(index_ref, *refs):
        backward(*refs[:many], index_ref, *refs[many:], pieces=pieces)

    return call(
        body, "backward", (index,), rows, row_args, (weight, packed, other),
        [((count, seq, width), BF)], [((8, width), F32)] + [((pieces // groups, own, 3 * width), BF)] * groups,
        [
            ((3 * width, rows * seq), BF), ((width, 3 * width), F32), ((width, rows * seq), BF),
            ((rows, HEADS, seq, seq), F32), ((rows, HEADS, seq, seq), BF), ((width, rows * seq), F32),
            ((5, width, LANES), F32), ((4, width, LANES), F32), ((rows, width, seq), F32), ((rows, width, seq), F32),
            ((rows, width, seq), BF),
        ],
        near=(5,),
    )


def exchange(values, axis, offset):
    size = lax.axis_size(axis)
    return lax.ppermute(values, axis, [(i, i ^ offset) for i in range(size)])


def add_halves(mine, received):
    count, own, cols = mine.shape

    def body(mine_ref, received_ref, *out_refs):
        for i, ref in enumerate(out_refs):
            ref[...] = (mine_ref[i].astype(F32) + received_ref[i].astype(F32)).astype(BF)

    return small_call(body, "add_halves", (mine, received), [((own, cols), BF)] * count)


def add_wide(*items):
    return tree_sum(item.astype(F32) for item in items)


def store_high_low(ref, cols, values):
    high = values.astype(BF)
    low = (values - high.astype(F32)).astype(BF)
    ref[:, cols:] = jnp.concatenate([high, low, jnp.zeros((ref.shape[0] - 16, LANES), BF)], axis=0)


def load_high_low(ref, cols):
    both = ref[:16, cols:].astype(F32)
    return both[:8] + both[8:]


def add_halves_and_sums(index, mine, received, sums, received_sums):
    count, own, cols = mine.shape
    width = sums.shape[1]

    def body(index_ref, mine_ref, received_ref, sums_ref, received_sums_ref, *out_refs):
        total = sums_ref[...] + received_sums_ref[...]
        for i, ref in enumerate(out_refs):
            ref[:, :cols] = (mine_ref[i].astype(F32) + received_ref[i].astype(F32)).astype(BF)
            turned = pltpu.roll(total, lax.rem(width - index_ref[2 * i] * own, width), 1)[:, :LANES]
            store_high_low(ref, cols, turned)

    spec = pltpu.PrefetchScalarGridSpec(
        num_scalar_prefetch=1, grid=(1,),
        in_specs=[whole(a.shape) for a in (mine, received, sums, received_sums)],
        out_specs=[whole((own, cols + LANES))] * count,
    )
    return pl.pallas_call(
        body, grid_spec=spec, out_shape=[jax.ShapeDtypeStruct((own, cols + LANES), BF)] * count,
        compiler_params=pltpu.CompilerParams(vmem_limit_bytes=16 * MIB), name="add_halves_and_sums",
    )(index, mine, received, sums, received_sums)


def add_packed(name, items):
    cols = items[0].shape[1] - LANES

    def body(*refs):
        out_ref = refs[-1]
        out_ref[:, :cols] = tree_sum(ref[:, :cols].astype(F32) for ref in refs[:-1]).astype(BF)
        store_high_low(out_ref, cols, tree_sum(load_high_low(ref, cols) for ref in refs[:-1]))

    return small_call(body, name, items, [(items[0].shape, BF)])[0]


def add_last(items):
    own, cols = items[0].shape[0], items[0].shape[1] - LANES

    def body(*refs):
        ins, outs = refs[: len(items)], refs[len(items) :]
        outs[0][...] = tree_sum(ref[:, :cols].astype(F32) for ref in ins)
        vectors = tree_sum(load_high_low(ref, cols) for ref in ins)
        outs[1][...] = vectors[0:3, :own]
        for i in range(4):
            outs[2 + i][...] = vectors[3 + i : 4 + i, :own]

    return small_call(body, "add_last", items, [((own, cols), F32), ((3, own), F32)] + [((1, own), F32)] * 4)


def direct_plan(tokens, segment_ids, valid_len, qkv_weight, out_weight, up_weight, down_weight, conv_weight, vectors, cotangent):
    count, seq, width = tokens.shape
    own, ffs = up_weight.shape
    dp, mp = lax.axis_size("dp"), lax.axis_size("mp")
    me = lax.axis_index("dp")
    offsets = [2 * p for p in range(dp // 2)]
    index = jnp.stack([me ^ (p ^ c) for p in offsets for c in range(2)]).astype(jnp.int32)
    narrow, ff_own = small_call(
        pack_weights, "pack_weights",
        [in_hbm(a) for a in (qkv_weight, up_weight, down_weight, conv_weight, *[v.reshape(1, own) for v in vectors])],
        [((own, 3 * width + VECTORS), BF), ((2 * own, ffs), BF)], [((VECTORS, VECTORS), F32)],
    )
    shards = [ff_own] + [exchange(ff_own, "mp", j) for j in range(1, mp)]
    plane = jnp.concatenate([narrow] + [exchange(narrow, "dp", p) for p in offsets[1:]], axis=0)
    pieces = [plane, exchange(plane, "dp", 1)]
    column = jnp.concatenate(shards + [out_weight], axis=0)
    columns = [column] + [exchange(column, "dp", p) for p in offsets[1:]]
    five, mixed, v, raised, facts, packed, weight = run_forward(
        index, tokens, segment_ids, valid_len, pieces
    )
    columns, five = lax.optimization_barrier((columns, five))
    columns = jnp.concatenate(columns, axis=0)
    pieces = [columns, exchange(columns, "dp", 1)]
    hidden, mixed_attn, grad_mixed, grad_att, sums2, down, mine, theirs = run_feed_forward(
        index, five, mixed, cotangent, packed, pieces, mp
    )
    received = exchange(theirs, "dp", 1)
    shape = cotangent.shape
    layer_out = run_layer_output(hidden, mixed_attn, down, shape, None, 0, 0.34)
    received, layer_out = lax.optimization_barrier((received, layer_out))
    parts = list(add_halves(mine, received))
    parts[0], grad_att = lax.optimization_barrier((parts[0], grad_att))
    plane = [parts[0]] + [exchange(parts[i], "dp", p) for i, p in enumerate(offsets) if i]
    kept = (five, mixed, v, raised, facts)
    input_grad, sums, mine_a, theirs_a = run_backward(
        index, weight, kept, (grad_att, grad_mixed), packed, sums2, dp
    )
    plane, theirs_a, sums = lax.optimization_barrier((plane, theirs_a, sums))
    received_a = exchange(theirs_a, "dp", 1)
    received_s = exchange(sums, "dp", 1)
    total = add_wide(*plane).astype(BF)
    total, received_s = lax.optimization_barrier((total, received_s))
    part = 2 * ffs
    near = jnp.concatenate([total[:, :part], total[:, 2 * part : 3 * part]], axis=1)
    out_part = total[:, 4 * part :]
    far = jnp.concatenate([total[:, part : 2 * part], total[:, 3 * part :]], axis=1)
    parts = list(add_halves_and_sums(index, mine_a, received_a, sums, received_s))
    parts[0], hidden, layer_out = lax.optimization_barrier((parts[0], hidden, layer_out))
    plane_a = [parts[0]] + [exchange(parts[i], "dp", p) for i, p in enumerate(offsets) if i]
    received_f = exchange(far, "mp", 1)
    layer_out = run_layer_output(hidden, mixed_attn, down, shape, layer_out, 0.34, 0.67)
    plane_a, layer_out = lax.optimization_barrier((plane_a, layer_out))
    total = add_packed("add_plane", plane_a)
    received_1 = exchange(total, "mp", 1)
    received_f, _ = lax.optimization_barrier((received_f, total))
    near_sum = add_wide(near, received_f[:, : 2 * part])
    out_sum = lax.optimization_barrier(add_wide(out_part, received_f[:, 2 * part :]).astype(BF))
    keep = near_sum[:, :part]
    send = jnp.concatenate([near_sum[:, part:].astype(BF), out_sum], axis=1)
    received_n = exchange(send, "mp", 2)
    received_1, _ = lax.optimization_barrier((received_1, send))
    total = add_packed("add_near", (total, received_1))
    received_2 = exchange(total, "mp", 2)
    layer_out, _ = lax.optimization_barrier((layer_out, total))
    layer_out = run_layer_output(hidden, mixed_attn, down, shape, layer_out, 0.67, 1)
    received_n, layer_out = lax.optimization_barrier((received_n, layer_out))
    grad_up = keep[:, :ffs] + received_n[:, :ffs].astype(F32)
    grad_down = keep[:, ffs:] + received_n[:, ffs : 2 * ffs].astype(F32)
    grad_out = add_wide(out_sum, received_n[:, 2 * ffs :])
    grad_qkv, grad_conv, *grads = add_last((total, received_2))
    return (layer_out, input_grad, grad_qkv, grad_out, grad_up, grad_down, grad_conv, *[g.reshape(own) for g in grads])


def gathered_plan(tokens, segment_ids, valid_len, qkv_weight, out_weight, up_weight, down_weight, conv_weight, vectors, cotangent):
    count, seq, width = tokens.shape
    own = qkv_weight.shape[0]
    dp = width // own
    columns = jnp.stack([conv_weight[0], conv_weight[1], conv_weight[2], *vectors], axis=1)
    narrow = jnp.concatenate([qkv_weight, jnp.pad(columns, ((0, 0), (0, VECTORS - 7))), out_weight], axis=1)
    wide = lax.all_gather(narrow, "dp", axis=0, tiled=True)
    both = lax.all_gather(jnp.concatenate([up_weight, down_weight], axis=0), "mp", axis=1, tiled=True)
    ff = both.shape[1]
    shards = ff // width
    both = lax.all_gather(both, "dp", axis=0).reshape(dp, 2, own, shards, width)
    both = both.transpose(3, 1, 0, 2, 4).reshape(2 * ff, width)
    column = jnp.concatenate([both, wide[:, 3 * width + VECTORS :]], axis=0)
    index = jnp.zeros((1,), jnp.int32)
    five, mixed, v, raised, facts, packed, weight = run_forward(
        index, tokens, segment_ids, valid_len, [wide[:, : 3 * width + VECTORS]]
    )
    hidden, mixed_attn, grad_mixed, grad_att, sums2, down, grads = run_feed_forward(
        index, five, mixed, cotangent, packed, [column], shards
    )
    kept = (five, mixed, v, raised, facts)
    layer_out = run_layer_output(hidden, mixed_attn, down, cotangent.shape, None, 0, 1)
    input_grad, sums, grad_qkv = run_backward(index, weight, kept, (grad_att, grad_mixed), packed, sums2, 1)
    grad_ff = grads[0, :, : 2 * ff].reshape(width, shards, 2, width).transpose(0, 2, 1, 3).reshape(width, 2 * ff)
    grad_ff = lax.psum_scatter(grad_ff, "dp", scatter_dimension=0, tiled=True).reshape(own, 2, ff)
    grad_ff = lax.psum_scatter(grad_ff, "mp", scatter_dimension=2, tiled=True).astype(F32)
    grad_attn = jnp.concatenate([grad_qkv[0], grads[0, :, 2 * ff :]], axis=1)
    grad_attn = lax.psum_scatter(grad_attn, "dp", scatter_dimension=0, tiled=True)
    grad_attn = lax.psum(grad_attn, "mp").astype(F32)
    sums = lax.psum(sums, ("dp", "mp"))
    sums = lax.dynamic_slice_in_dim(sums, lax.axis_index("dp") * own, own, axis=1)
    return (
        layer_out, input_grad, grad_attn[:, : 3 * width], grad_attn[:, 3 * width :],
        grad_ff[:, 0], grad_ff[:, 1], sums[0:3], sums[3], sums[4], sums[5], sums[6],
    )


def on_device(
    tokens, segment_ids, valid_len, qkv_weight, out_weight, up_weight, down_weight, conv_weight,
    ln1_gain, ln1_shift, ln2_gain, ln2_shift, cotangent,
):
    own, ffs = up_weight.shape
    direct = own % 16 == 0 and ffs == tokens.shape[2] and own <= VECTORS and lax.axis_size("mp") == 4
    plan = direct_plan if direct else gathered_plan
    return plan(
        tokens, segment_ids, valid_len, qkv_weight, out_weight, up_weight, down_weight, conv_weight,
        (ln1_gain, ln1_shift, ln2_gain, ln2_shift), cotangent,
    )


def solution(mesh):
    rows = P(("dp", "mp"), None, None)
    weights = (P("dp", None), P("dp", None), P("dp", "mp"), P("dp", "mp"), P(None, "dp"))
    vectors = (P("dp"),) * 4
    return jax.shard_map(
        on_device,
        mesh=mesh,
        in_specs=(rows, P(("dp", "mp"), None), P(("dp", "mp"))) + weights + vectors + (rows,),
        out_specs=(rows, rows) + weights + vectors,
        check_vma=False,
    )
```

```python
import functools
import math

import jax
import jax.numpy as jnp
from jax import lax
from jax.experimental import pallas as pl
from jax.experimental.pallas import tpu as pltpu
from jax.sharding import PartitionSpec as P

HEADS = 6
VECTORS = 128
LANES = 128
BF = jnp.bfloat16
F32 = jnp.float32
MIB = 1024 * 1024
VMEM_LIMITS = dict(forward_attention=42, feed_forward=44, backward=42, layer_output=16)


def mm(lhs, rhs):
    return lax.dot_general(lhs, rhs, (((1,), (0,)), ((), ())), preferred_element_type=F32)


def mm_nt(lhs, rhs):
    return lax.dot_general(lhs, rhs, (((1,), (1,)), ((), ())), preferred_element_type=F32)


def tree_sum(items):
    items = list(items)
    while len(items) > 1:
        items = [a + b for a, b in zip(items[::2], items[1::2])]
    return items[0]


def pack_weights(qkv_ref, up_ref, down_ref, conv_ref, g1_ref, s1_ref, g2_ref, s2_ref, narrow_ref, ff_ref, rows_ref):
    own, ffs = up_ref.shape
    rows_ref[...] = jnp.zeros_like(rows_ref)
    rows_ref[0:3, :own] = conv_ref[...].astype(F32)
    for i, ref in enumerate((g1_ref, s1_ref, g2_ref, s2_ref)):
        rows_ref[3 + i : 4 + i, :own] = ref[...].astype(F32)
    wide = qkv_ref.shape[1]
    narrow_ref[:, :wide] = qkv_ref[...]
    narrow_ref[:, wide:] = rows_ref[...].T[:own].astype(BF)
    ff_ref[:own] = up_ref[...]
    ff_ref[own:] = down_ref[...]


def tiles(total, size):
    return [slice(at, at + size) for at in range(0, total, size)]


def weave(*strands):
    strands = [strand for strand in strands if strand]
    total = sum(len(strand) for strand in strands)
    pieces = [((i + 0.5) / len(strand), j, piece) for j, strand in enumerate(strands) for i, piece in enumerate(strand)]
    assert len(pieces) == total
    for _, _, piece in sorted(pieces, key=lambda item: item[:2]):
        piece()


def twice(tile, lanes):
    return jnp.concatenate([tile] * (lanes // LANES), axis=1)


def load_columns(packed_ref, col_ref, places):
    for i, place in enumerate(places):
        column = packed_ref[:, place : place + 1].astype(F32)
        col_ref[i] = jnp.broadcast_to(column, (column.shape[0], LANES))


def pairwise(items, combine):
    items = list(items)
    while len(items) > 1:
        odd = items[len(items) // 2 * 2 :]
        items = [combine(a, b) for a, b in zip(items[::2], items[1::2])] + odd
    return items[0]


def fold(values, combine=jnp.add):
    return pairwise([values[t] for t in tiles(values.shape[0], 8)], combine)


def column_mean(values):
    return jnp.sum(fold(values), axis=0, keepdims=True) * (1.0 / values.shape[0])


def norm_columns(values):
    centred = values - column_mean(values)
    scale = lax.rsqrt(column_mean(centred * centred) + 1e-06)
    return centred * scale, scale


def fold_lanes(values):
    return sum(values[:, t] for t in tiles(values.shape[1], LANES))


def forward_attention(index_ref, len_ref, tok_ref, seg_ref, *refs, pieces):
    cores = 2 if pieces > 1 else 1
    piece_refs = refs[:cores]
    (
        five_ref, mc_ref, v_ref, e_ref, facts_ref, packed_ref, w_ref,
        wt_ref, wide_ref, col_ref, key_mask_ref, query_mask_ref, key_ref, value_ref,
    ) = refs[cores:]
    x_ref, norm_ref, q_ref, k_ref, att_ref = [five_ref.at[:, i] for i in range(5)]
    aux_ref, inv_ref = facts_ref.at[:, :8], facts_ref.at[:, 8:]
    rows, seq, width = tok_ref.shape
    head = width // HEADS
    step = pl.program_id(0)

    @pl.when(step == 0)
    def _():
        own = width // pieces
        for i in range(pieces):
            here = pl.ds(pl.multiple_of(index_ref[i] * own, 16), own)
            wide_ref[here, :] = piece_refs[i % cores][i // cores * own : (i // cores + 1) * own]
        w_ref[...] = wide_ref[:, : 3 * width]
        wt_ref[...] = wide_ref[:, : 3 * width].T
        packed_ref[...] = wide_ref[:, 3 * width :]
        load_columns(packed_ref, col_ref, range(5))
        col_ref[1] = col_ref[1] + 1.0

    place = lax.broadcasted_iota(jnp.int32, (1, seq), 1)
    zero = jnp.zeros((head, seq), BF)

    def preparation(r):
        known = {}

        def start():
            segs = seg_ref[pl.ds(step * rows + r, 1), :].astype(F32)
            valid = place < len_ref[step * rows + r]
            number = jnp.where(valid, segs, -1.0)
            links = jnp.where(valid & (place > 0) & (number == pltpu.roll(number, 1, 1)), 1.0, 0.0)
            next_links = jnp.where(place < seq - 1, pltpu.roll(links, seq - 1, 1), 0.0)
            none = jnp.zeros_like(links)
            aux = jnp.concatenate([links, next_links, number, none, none, none, none, none], axis=0)
            aux_ref[r] = aux
            x_ref[r] = tok_ref[r].T
            known.update(segs=segs, links=links, next_links=next_links, key_number=aux.T[:, 2:3])

        def mask():
            number = known["key_number"]
            lane = lax.broadcasted_iota(jnp.int32, (seq, LANES), 1)
            itself = lax.broadcasted_iota(jnp.int32, (seq, LANES), 0) - (seq - LANES)
            chosen = (lane.astype(F32) == number) | ((number < 0.0) & (lane == itself))
            key_mask_ref[r] = jnp.where(chosen, 1.0, 0.0).astype(BF)
            slot = lax.broadcasted_iota(jnp.int32, (LANES, seq), 0)
            itself = lax.broadcasted_iota(jnp.int32, (LANES, seq), 1) - (seq - LANES)
            open_to = (slot.astype(F32) == known["segs"]) | ((slot >= LANES // 2) & (slot == itself))
            query_mask_ref[r] = jnp.where(open_to, 0.0, -1e30).astype(BF)

        def conv(t):
            base = x_ref[r, t].astype(F32)
            before = pltpu.roll(base, 1, 1) * known["links"]
            after = pltpu.roll(base, seq - 1, 1) * known["next_links"]
            conv0, conv1, conv2 = [twice(col_ref[i, t], seq) for i in range(3)]
            mc_ref[r, t] = before * conv0 + base * conv1 + after * conv2

        def norm(t):
            n, _ = norm_columns(mc_ref[r, :, t])
            norm_ref[r, :, t] = (n * col_ref[3] + col_ref[4]).astype(BF)

        pieces = [start] + [functools.partial(conv, t) for t in tiles(width, 32)]
        pieces += [functools.partial(norm, t) for t in tiles(seq, LANES)]
        return pieces + [mask]

    def project(pair):
        normed = jnp.concatenate([norm_ref[r] for r in pair], axis=1)
        for i, ref in enumerate((q_ref, k_ref, value_ref)):
            part = mm(wt_ref[i * width : (i + 1) * width], normed)
            part = (part * (head ** (-0.5) * math.log2(math.e)) if i == 0 else part).astype(BF)
            for j, r in enumerate(pair):
                ref[r] = part[:, j * seq : (j + 1) * seq]
        for r in pair:
            key_ref[r] = k_ref[r].T
            v_ref[r] = value_ref[r].T

    def scores(r, p):
        low, high = [q_ref[r, h * head : (h + 1) * head] for h in (2 * p, 2 * p + 1)]
        both = jnp.concatenate([jnp.concatenate([low, zero], axis=1), jnp.concatenate([zero, high], axis=1)], axis=0)
        keys = jnp.concatenate([key_ref[r, :, 2 * p * head : 2 * (p + 1) * head], key_mask_ref[r]], axis=1)
        masks = jnp.concatenate([query_mask_ref[r], query_mask_ref[r]], axis=1)
        return mm(keys, jnp.concatenate([both, masks], axis=0))

    def attended(r, p):
        both = jnp.concatenate([e_ref[r, 2 * p], e_ref[r, 2 * p + 1]], axis=1)
        product = mm(value_ref[r, 2 * p * head : 2 * (p + 1) * head], both)
        parts = []
        for i in range(2):
            att = product[i * head : (i + 1) * head, i * seq : (i + 1) * seq] * inv_ref[r, 2 * p + i : 2 * p + i + 1]
            parts.append(att.astype(BF))
        return jnp.concatenate(parts, axis=0)

    def soften(r, p, product):
        for i in range(2):
            for t in tiles(seq, LANES):
                masked = product[:, i * seq + t.start : i * seq + t.stop]
                raised = jnp.exp2(masked - jnp.max(fold(masked, jnp.maximum), axis=0, keepdims=True))
                inv_ref[r, 2 * p + i : 2 * p + i + 1, t] = 1.0 / jnp.sum(fold(raised), axis=0, keepdims=True)
                e_ref[r, 2 * p + i, :, t] = raised.astype(BF)

    def heads(pair):
        work = [(r, p) for r in pair for p in range(HEADS // 2)]
        current, last = scores(*work[0]), None
        for at, (r, p) in enumerate(work):
            following = scores(*work[at + 1]) if at + 1 < len(work) else None
            finished = attended(*last) if last else None
            soften(r, p, current)
            if last:
                att_ref[last[0], 2 * last[1] * head : 2 * (last[1] + 1) * head] = finished
            current, last = following, (r, p)
        att_ref[last[0], 2 * last[1] * head : 2 * (last[1] + 1) * head] = attended(*last)

    half = rows // 2 if rows % 4 == 0 else rows
    pairs = [range(first, first + half) for first in range(0, rows, half)]
    for pair in pairs:
        weave(*[preparation(r) for r in pair])
        project(pair)
        heads(pair)


def gelu_parts(y):
    twice_cdf = lax.erf(y) + 1.0
    bell = jnp.exp2(y * y * -math.log2(math.e) + math.log2(2.0 / math.sqrt(math.pi)))
    return y * twice_cdf, twice_cdf + y * bell


def feed_forward(index_ref, five_ref, mc_ref, ct_ref, packed_ref, *refs, pieces, shards):
    att_ref = five_ref.at[:, 0]
    groups = 2 if pieces > 1 else 1
    piece_refs = refs[:groups]
    hidden_out, mixed_out, gm_ref, ga_ref, gs_ref, down_ref = refs[groups : groups + 6]
    gw_refs = refs[groups + 6 : 2 * groups + 6]
    (
        up_ref, upt_ref, downt_ref, out_ref, outt_ref, up_acc, down_acc, out_acc, col_acc, col_ref,
        n_ref, norm_ref, ctt_ref, gp_ref, gn_ref, scale_ref, branch_ref, hidden_ref, mixed_ref, sems,
    ) = refs[2 * groups + 6 :]
    rows, seq, width = ct_ref.shape
    ff = up_ref.shape[1]
    ffs = ff // shards
    own = width // pieces
    step = pl.program_id(0)

    @pl.when(step == 0)
    def _():
        for acc in (up_acc, down_acc, out_acc, col_acc):
            acc[...] = jnp.zeros_like(acc)
        for i in range(pieces):
            here = pl.ds(pl.multiple_of(index_ref[i] * own, 16), own)
            ref, first = piece_refs[i % groups], i // groups * (2 * shards + 1) * own
            for j in range(shards):
                at = first + 2 * j * own
                up_ref[here, j * ffs : (j + 1) * ffs] = ref[at : at + own]
                down_ref[here, j * ffs : (j + 1) * ffs] = ref[at + own : at + 2 * own]
            at = first + 2 * shards * own
            out_ref[here, :] = ref[at : at + own]
        upt_ref[...] = up_ref[...].T
        downt_ref[...] = down_ref[...].T
        outt_ref[...] = out_ref[...].T
        load_columns(packed_ref, col_ref, (5, 6, 5))
        for i, factor in enumerate((0.5, math.sqrt(0.5), math.sqrt(0.5))):
            col_ref[i] = col_ref[i] * factor

    def copies(at, g):
        place = at * pairs + g
        return [
            pltpu.make_async_copy(hidden_ref.at[g], hidden_out.at[place], sems.at[0, g]),
            pltpu.make_async_copy(mixed_ref.at[g], mixed_out.at[place], sems.at[1, g]),
        ]

    pairs = n_ref.shape[0]

    @pl.when(step > 0)
    def _():
        for g in range(pairs):
            for copy in copies(step - 1, g):
                copy.wait()

    def begin(g):
        pair = range(g * paired, (g + 1) * paired)
        attended = jnp.concatenate([att_ref[r] for r in pair], axis=1)
        branch = mm(outt_ref[...], attended)
        for i, r in enumerate(pair):
            lanes = slice(i * seq, (i + 1) * seq)
            ctt_ref[g, :, lanes] = ct_ref[r].T
            mixed_ref[g, :, lanes] = mc_ref[r] + branch[:, lanes]
        for t in spots:
            n, scale = norm_columns(mixed_ref[g, :, t])
            n_ref[g, :, t] = n
            scale_ref[g, 0:1, t] = scale
            norm_ref[g, :, t] = (n * col_ref[2] + col_ref[1]).astype(BF)

    def activate(g, block):
        pre = mm(upt_ref[block], norm_ref[g])
        grad_hidden = mm(downt_ref[block], ctt_ref[g])
        for low in range(0, block.stop - block.start, 16):
            part = slice(low, low + 16)
            here = slice(block.start + low, block.start + low + 16)
            hidden, slope = gelu_parts(pre[part])
            hidden_ref[g, here] = hidden.astype(BF)
            gp_ref[g, here] = (grad_hidden[part] * slope).astype(BF)

    def weigh(g):
        gn_ref[g] = mm(up_ref[...], gp_ref[g])
        down_acc[...] += mm_nt(ctt_ref[g], hidden_ref[g])
        up_acc[...] += mm_nt(norm_ref[g], gp_ref[g])

    def norm_back(g):
        mean_e = [jnp.zeros((8, LANES), F32) for _ in spots]
        mean_en = [jnp.zeros((8, LANES), F32) for _ in spots]
        for d in tiles(width, 32):
            column = col_ref[0, d]
            gain_sum, shift_sum = col_acc[0, d], col_acc[1, d]
            for i, t in enumerate(spots):
                grad_n = gn_ref[g, d, t]
                product = grad_n * n_ref[g, d, t]
                gain_sum += product
                shift_sum += grad_n
                mean_e[i] += fold(grad_n * column)
                mean_en[i] += fold(product * column)
            col_acc[0, d] = gain_sum
            col_acc[1, d] = shift_sum
        for i, t in enumerate(spots):
            me = jnp.sum(mean_e[i], axis=0, keepdims=True) * (1.0 / width)
            men = jnp.sum(mean_en[i], axis=0, keepdims=True) * (1.0 / width)
            row, inside = divmod(t.start, seq)
            for d in tiles(width, 32):
                change = scale_ref[g, 0:1, t] * (gn_ref[g, d, t] * col_ref[0, d] - me - n_ref[g, d, t] * men)
                grad_mixed = ctt_ref[g, d, t].astype(F32) + change
                gm_ref[g * paired + row, d, inside : inside + LANES] = grad_mixed
                branch_ref[g, d, t] = grad_mixed.astype(BF)

    def end(g):
        pair = range(g * paired, (g + 1) * paired)
        attended = jnp.concatenate([att_ref[r] for r in pair], axis=1)
        grad_attended = mm(out_ref[...], branch_ref[g]).astype(BF)
        for i, r in enumerate(pair):
            ga_ref[r] = grad_attended[:, i * seq : (i + 1) * seq]
        out_acc[...] += mm_nt(attended, branch_ref[g])

    paired = rows // pairs
    spots = tiles(paired * seq, LANES)
    begin(0)
    copies(step, 0)[1].start()
    for g in range(pairs):
        for block in tiles(ff, 128):
            activate(g, block)
        copies(step, g)[0].start()
        if g + 1 < pairs:
            begin(g + 1)
            copies(step, g + 1)[1].start()
        weigh(g)
        norm_back(g)
        end(g)

    @pl.when(step == pl.num_programs(0) - 1)
    def _():
        for g in range(pairs):
            for copy in copies(step, g):
                copy.wait()
        for i in range(pieces):
            here = pl.ds(pl.multiple_of(index_ref[i] * own, 16), own)
            place = gw_refs[i % groups]
            for j in range(shards):
                cols = slice(j * ffs, (j + 1) * ffs)
                place[i // groups, :, 2 * j * ffs : (2 * j + 1) * ffs] = (up_acc[here, cols] * math.sqrt(0.5)).astype(BF)
                place[i // groups, :, (2 * j + 1) * ffs : (2 * j + 2) * ffs] = (down_acc[here, cols] * math.sqrt(0.5)).astype(BF)
            place[i // groups, :, 2 * ff :] = out_acc[here, :].astype(BF)
        gs_ref[...] = jnp.zeros_like(gs_ref)
        for i in range(2):
            gs_ref[5 + i : 6 + i] = jnp.sum(col_acc[i].T, axis=0, keepdims=True) * 0.5


def layer_output(hidden_ref, mixed_ref, down_ref, lo_ref):
    rows, seq, _ = lo_ref.shape
    total = (mixed_ref[0] + mm(down_ref[...], hidden_ref[0]) * math.sqrt(0.5)).astype(BF)
    for r in range(rows):
        lo_ref[r] = total[:, r * seq : (r + 1) * seq].T


def backward(
    five_ref, mc_ref, v_ref, e_ref, facts_ref, ga_ref, gm_ref, index_ref, w_ref, packed_ref, other_ref, ig_ref, gs_ref, *refs, pieces,
):
    x_ref, norm_ref, q_ref, k_ref, att_ref = [five_ref.at[:, i] for i in range(5)]
    aux_ref, inv_ref = facts_ref.at[:, :8], facts_ref.at[:, 8:]
    gw_refs = refs[:-11]
    (
        proj_ref, w_acc, norm_cat, soft_ref, logit_ref, gn_ref, acc_ref, col_ref, n_ref, g_ref, turn_ref
    ) = refs[-11:]
    rows, seq, width = v_ref.shape
    own = width // pieces
    head = width // HEADS
    step = pl.program_id(0)

    @pl.when(step == 0)
    def _():
        w_acc[...] = jnp.zeros_like(w_acc)
        acc_ref[...] = jnp.zeros_like(acc_ref)
        load_columns(packed_ref, col_ref, range(4))
        col_ref[1] = col_ref[1] + 1.0

    zero = jnp.zeros((head, seq), BF)
    work = [(r, p) for r in range(rows) for p in range(HEADS // 2)]

    def opening(r, p):
        grads, inners = [], []
        for h in (2 * p, 2 * p + 1):
            part = slice(h * head, (h + 1) * head)
            grad_att = ga_ref[r, part].astype(F32) * inv_ref[r, h : h + 1]
            inners.append(jnp.sum(fold(grad_att * att_ref[r, part].astype(F32)), axis=0, keepdims=True))
            grads.append(grad_att.astype(BF))
        low, high = grads
        both = jnp.concatenate([jnp.concatenate([low, zero], axis=1), jnp.concatenate([zero, high], axis=1)], axis=0)
        product = mm(v_ref[r, :, 2 * p * head : 2 * (p + 1) * head], both)
        soft_ref[r, 2 * p] = product[:, :seq]
        soft_ref[r, 2 * p + 1] = product[:, seq:]
        return jnp.concatenate(grads, axis=0), inners

    spots = tiles(seq, LANES)

    def finish_row(r):
        wide = [slice(r * seq + t.start, r * seq + t.stop) for t in spots]
        lanes = slice(r * seq, (r + 1) * seq)
        norm_cat[:, lanes] = norm_ref[r]
        gn_ref[:, lanes] = mm(w_ref[...], proj_ref[:, lanes])
        scales = []
        for t in spots:
            n, scale = norm_columns(mc_ref[r, :, t])
            n_ref[r, :, t] = n
            scales.append(scale)
        mean_e = [jnp.zeros((8, LANES), F32) for _ in spots]
        mean_en = [jnp.zeros((8, LANES), F32) for _ in spots]
        for d in tiles(width, 32):
            column = col_ref[3, d]
            gain_sum, shift_sum = acc_ref[3, d], acc_ref[4, d]
            for i, t in enumerate(spots):
                grad_n = gn_ref[d, wide[i]]
                product = grad_n * n_ref[r, d, t]
                gain_sum += product
                shift_sum += grad_n
                mean_e[i] += fold(grad_n * column)
                mean_en[i] += fold(product * column)
            acc_ref[3, d] = gain_sum
            acc_ref[4, d] = shift_sum
        for i, t in enumerate(spots):
            me = jnp.sum(mean_e[i], axis=0, keepdims=True) * (1.0 / width)
            men = jnp.sum(mean_en[i], axis=0, keepdims=True) * (1.0 / width)
            for d in tiles(width, 64):
                e = gn_ref[d, wide[i]] * col_ref[3, d]
                g_ref[r, d, t] = gm_ref[r, d, t] + scales[i] * (e - me - n_ref[r, d, t] * men)
        links, next_links = aux_ref[r, 0:1], aux_ref[r, 1:2]
        for d in tiles(width, 32):
            g = g_ref[r, d]
            base = x_ref[r, d].astype(F32)
            before = pltpu.roll(g, 1, 1) * links
            after = pltpu.roll(g, seq - 1, 1) * next_links
            acc_ref[0, d] += fold_lanes(base * after)
            acc_ref[1, d] += fold_lanes(base * g)
            acc_ref[2, d] += fold_lanes(base * before)
            conv0, conv1, conv2 = [twice(col_ref[i, d], seq) for i in range(3)]
            turn_ref[r, d] = (conv1 * g + conv0 * after + conv2 * before).astype(BF)
        ig_ref[r] = turn_ref[r].T

    ready = opening(*work[0])
    for at, (r, p) in enumerate(work):
        grad_att, inners = ready
        if at + 1 < len(work):
            ready = opening(*work[at + 1])
        for i, h in enumerate((2 * p, 2 * p + 1)):
            for t in tiles(seq, 32):
                raised = e_ref[r, h, t].astype(F32)
                logit_ref[r, h, t] = (raised * (soft_ref[r, h, t] - inners[i])).astype(BF)
        part = slice(2 * p * head, 2 * (p + 1) * head)
        pair = slice(2 * p, 2 * p + 2)
        beside = jnp.concatenate([logit_ref[r, 2 * p], logit_ref[r, 2 * p + 1]], axis=1)
        grad_q = mm(k_ref[r, part], beside)
        grad_k = mm_nt(q_ref[r, part], logit_ref[r, pair].reshape(2 * seq, seq))
        grad_v = mm_nt(grad_att, e_ref[r, pair].reshape(2 * seq, seq))
        for i in range(2):
            place = slice(r * seq, (r + 1) * seq)
            own_rows, own_cols = slice(i * head, (i + 1) * head), slice(i * seq, (i + 1) * seq)
            for j, (grad, factor) in enumerate(((grad_q, head ** (-0.5)), (grad_k, math.log(2.0)), (grad_v, None))):
                first = j * width + (2 * p + i) * head
                mine = grad[own_rows, own_cols]
                proj_ref[first : first + head, place] = (mine if factor is None else mine * factor).astype(BF)
        if p == HEADS // 2 - 1:
            finish_row(r)
    w_acc[...] += mm_nt(norm_cat[...], proj_ref[...])

    @pl.when(step == pl.num_programs(0) - 1)
    def _():
        gs_ref[...] = other_ref[...]
        for i in range(5):
            gs_ref[i : i + 1] += jnp.sum(acc_ref[i].T, axis=0, keepdims=True)
        groups = len(gw_refs)
        for i in range(pieces):
            here = pl.ds(pl.multiple_of(index_ref[i] * own, 16), own)
            gw_refs[i % groups][i // groups] = w_acc[here, :].astype(BF)


def in_hbm(values):
    return pltpu.with_memory_space_constraint(values, pltpu.HBM)


def by_row(shape, rows, first=0):
    tail = tuple(shape[1:])
    return pl.BlockSpec((rows,) + tail, lambda i, *_: (i + first,) + (0,) * len(tail))


def whole(shape):
    place = (0,) * len(shape)
    return pl.BlockSpec(tuple(shape), lambda i, *_: place, pipeline_mode=pl.Buffered(1))


def step_rows(count, most):
    return max(r for r in range(1, most + 1) if count % r == 0)


def call(body, name, scalars, rows, row_args, args, row_outs, outs, scratch, span=None, into=None, near=(), only=None, manual=()):
    first, count = span or (0, row_args[0].shape[0])
    skip = first // rows
    total = row_args[0].shape[0]

    def spec_of(shape):
        return by_row(shape, shape[0] * rows // total, skip)

    in_specs = [spec_of(a.shape) for a in row_args]
    if only:
        tail = row_args[0].shape[2:]
        in_specs[0] = pl.BlockSpec((rows, 1) + tail, lambda i, *_: (i, only) + (0,) * len(tail))
    in_specs += [whole(a.shape) for a in args]
    aliases = {}
    if into is not None:
        in_specs.append(pl.BlockSpec(memory_space=pl.ANY))
        aliases = {len(scalars) + len(in_specs) - 1: 0}
    spec = pltpu.PrefetchScalarGridSpec(
        num_scalar_prefetch=len(scalars),
        grid=(count // rows,),
        in_specs=in_specs,
        out_specs=[pl.BlockSpec(memory_space=pl.ANY) for _ in manual] + [spec_of(s) for s, _ in row_outs] + [whole(s) for s, _ in outs],
        scratch_shapes=[pltpu.VMEM(*s) if isinstance(s, tuple) else s for s in scratch],
    )
    return pl.pallas_call(
        body,
        grid_spec=spec,
        out_shape=[pltpu.HBM(s, t) for s, t in manual] + [(jax.ShapeDtypeStruct if "out" + str(i) in near else pltpu.HBM)(s, t) for i, (s, t) in enumerate(row_outs)]
        + [jax.ShapeDtypeStruct(s, t) for s, t in outs],
        input_output_aliases=aliases,
        compiler_params=pltpu.CompilerParams(dimension_semantics=("arbitrary",), vmem_limit_bytes=VMEM_LIMITS[name] * MIB),
        name=name,
    )(*scalars, *[a if i in near else in_hbm(a) for i, a in enumerate(row_args)], *args, *(() if into is None else (into,)))


def small_call(body, name, args, outs, scratch=()):
    return pl.pallas_call(
        body,
        out_shape=[jax.ShapeDtypeStruct(s, t) for s, t in outs],
        scratch_shapes=[pltpu.VMEM(s, t) for s, t in scratch],
        compiler_params=pltpu.CompilerParams(vmem_limit_bytes=16 * MIB),
        name=name,
    )(*args)


def run_forward(index, tokens, segment_ids, valid_len, pieces):
    count, seq, width = tokens.shape
    flipped = (count, width, seq)
    rows = step_rows(count, 4)
    row_outs = [
        ((count, 5, width, seq), BF), (flipped, F32), ((count, seq, width), BF),
        ((count, HEADS, seq, seq), BF), ((count, 16, seq), F32),
    ]
    return call(
        functools.partial(forward_attention, pieces=index.shape[0]), "forward_attention", (index, in_hbm(valid_len)),
        rows, (tokens,), (in_hbm(segment_ids), *pieces),
        row_outs, [((width, VECTORS), BF), ((width, 3 * width), BF)],
        [
            ((3 * width, width), BF), ((width, 3 * width + VECTORS), BF), ((5, width, LANES), F32),
            ((rows, seq, LANES), BF), ((rows, LANES, seq), BF), ((rows, seq, width), BF), ((rows, width, seq), BF),
        ],
    )


def run_feed_forward(index, five, mixed, cotangent, packed, pieces, shards):
    count, seq, width = cotangent.shape
    own = width // index.shape[0]
    ff = shards * width
    groups = 2 if index.shape[0] > 1 else 1
    paired = step_rows(count, 2)
    pairs = 2 if count // paired % 2 == 0 else 1
    rows = pairs * paired
    wide = paired * seq
    manual = [((count // paired, ff, wide), BF), ((count // paired, width, wide), F32)]
    row_outs = [((count, width, seq), F32), ((count, width, seq), BF)]
    grads = ((index.shape[0] // groups, own, 2 * ff + width), BF)
    return call(
        functools.partial(feed_forward, pieces=index.shape[0], shards=shards), "feed_forward", (index,),
        rows, (five, mixed, cotangent), (packed, *pieces),
        row_outs, [((8, width), F32), ((width, ff), BF)] + [grads] * groups,
        [((width, ff), BF)] + [((ff, width), BF)] * 2 + [((width, width), BF)] * 2
        + [((width, ff), F32)] * 2 + [((width, width), F32), ((2, width, LANES), F32), ((3, width, LANES), F32)]
        + [((pairs, width, wide), F32), ((pairs, width, wide), BF), ((pairs, width, wide), BF)]
        + [((pairs, ff, wide), BF)]
        + [((pairs, width, wide), F32), ((pairs, 8, wide), F32), ((pairs, width, wide), BF)]
        + [((pairs, ff, wide), BF), ((pairs, width, wide), F32), pltpu.SemaphoreType.DMA((2, pairs))],
        near=("out1",), only=4, manual=manual,
    )


def run_layer_output(hidden, mixed, down, shape, into, low, high):
    steps = hidden.shape[0]
    span = (int(low * steps), int(high * steps) - int(low * steps))

    def body(*refs):
        layer_output(*refs[:3], refs[-1])

    return call(body, "layer_output", (), 1, (hidden, mixed), (down,), [(shape, BF)], [], [], span=span, into=into)[0]


def run_backward(index, weight, kept, grads, packed, other, pieces):
    count, seq, width = kept[2].shape
    own = width // pieces
    groups = 2 if pieces > 1 else 1
    rows = step_rows(count, 3)
    row_args = (*kept, *grads)
    many = len(row_args)

    def body(index_ref, *refs):
        backward(*refs[:many], index_ref, *refs[many:], pieces=pieces)

    return call(
        body, "backward", (index,), rows, row_args, (weight, packed, other),
        [((count, seq, width), BF)], [((8, width), F32)] + [((pieces // groups, own, 3 * width), BF)] * groups,
        [
            ((3 * width, rows * seq), BF), ((width, 3 * width), F32), ((width, rows * seq), BF),
            ((rows, HEADS, seq, seq), F32), ((rows, HEADS, seq, seq), BF), ((width, rows * seq), F32),
            ((5, width, LANES), F32), ((4, width, LANES), F32), ((rows, width, seq), F32), ((rows, width, seq), F32),
            ((rows, width, seq), BF),
        ],
        near=(5,),
    )


def exchange(values, axis, offset):
    size = lax.axis_size(axis)
    return lax.ppermute(values, axis, [(i, i ^ offset) for i in range(size)])


def add_halves(mine, received):
    count, own, cols = mine.shape

    def body(mine_ref, received_ref, *out_refs):
        for i, ref in enumerate(out_refs):
            ref[...] = (mine_ref[i].astype(F32) + received_ref[i].astype(F32)).astype(BF)

    return small_call(body, "add_halves", (mine, received), [((own, cols), BF)] * count)


def add_wide(*items):
    return tree_sum(item.astype(F32) for item in items)


def store_high_low(ref, cols, values):
    high = values.astype(BF)
    low = (values - high.astype(F32)).astype(BF)
    ref[:, cols:] = jnp.concatenate([high, low, jnp.zeros((ref.shape[0] - 16, LANES), BF)], axis=0)


def load_high_low(ref, cols):
    both = ref[:16, cols:].astype(F32)
    return both[:8] + both[8:]


def add_halves_and_sums(index, mine, received, sums, received_sums):
    count, own, cols = mine.shape
    width = sums.shape[1]

    def body(index_ref, mine_ref, received_ref, sums_ref, received_sums_ref, *out_refs):
        total = sums_ref[...] + received_sums_ref[...]
        for i, ref in enumerate(out_refs):
            ref[:, :cols] = (mine_ref[i].astype(F32) + received_ref[i].astype(F32)).astype(BF)
            turned = pltpu.roll(total, lax.rem(width - index_ref[2 * i] * own, width), 1)[:, :LANES]
            store_high_low(ref, cols, turned)

    spec = pltpu.PrefetchScalarGridSpec(
        num_scalar_prefetch=1, grid=(1,),
        in_specs=[whole(a.shape) for a in (mine, received, sums, received_sums)],
        out_specs=[whole((own, cols + LANES))] * count,
    )
    return pl.pallas_call(
        body, grid_spec=spec, out_shape=[jax.ShapeDtypeStruct((own, cols + LANES), BF)] * count,
        compiler_params=pltpu.CompilerParams(vmem_limit_bytes=16 * MIB), name="add_halves_and_sums",
    )(index, mine, received, sums, received_sums)


def add_packed(name, items):
    cols = items[0].shape[1] - LANES

    def body(*refs):
        out_ref = refs[-1]
        out_ref[:, :cols] = tree_sum(ref[:, :cols].astype(F32) for ref in refs[:-1]).astype(BF)
        store_high_low(out_ref, cols, tree_sum(load_high_low(ref, cols) for ref in refs[:-1]))

    return small_call(body, name, items, [(items[0].shape, BF)])[0]


def add_last(items):
    own, cols = items[0].shape[0], items[0].shape[1] - LANES

    def body(*refs):
        ins, outs = refs[: len(items)], refs[len(items) :]
        outs[0][...] = tree_sum(ref[:, :cols].astype(F32) for ref in ins)
        vectors = tree_sum(load_high_low(ref, cols) for ref in ins)
        outs[1][...] = vectors[0:3, :own]
        for i in range(4):
            outs[2 + i][...] = vectors[3 + i : 4 + i, :own]

    return small_call(body, "add_last", items, [((own, cols), F32), ((3, own), F32)] + [((1, own), F32)] * 4)


def direct_plan(tokens, segment_ids, valid_len, qkv_weight, out_weight, up_weight, down_weight, conv_weight, vectors, cotangent):
    count, seq, width = tokens.shape
    own, ffs = up_weight.shape
    dp, mp = lax.axis_size("dp"), lax.axis_size("mp")
    me = lax.axis_index("dp")
    offsets = [2 * p for p in range(dp // 2)]
    index = jnp.stack([me ^ (p ^ c) for p in offsets for c in range(2)]).astype(jnp.int32)
    narrow, ff_own = small_call(
        pack_weights, "pack_weights",
        [in_hbm(a) for a in (qkv_weight, up_weight, down_weight, conv_weight, *[v.reshape(1, own) for v in vectors])],
        [((own, 3 * width + VECTORS), BF), ((2 * own, ffs), BF)], [((VECTORS, VECTORS), F32)],
    )
    shards = [ff_own] + [exchange(ff_own, "mp", j) for j in range(1, mp)]
    plane = jnp.concatenate([narrow] + [exchange(narrow, "dp", p) for p in offsets[1:]], axis=0)
    pieces = [plane, exchange(plane, "dp", 1)]
    column = jnp.concatenate(shards + [out_weight], axis=0)
    columns = [column] + [exchange(column, "dp", p) for p in offsets[1:]]
    five, mixed, v, raised, facts, packed, weight = run_forward(
        index, tokens, segment_ids, valid_len, pieces
    )
    columns, five = lax.optimization_barrier((columns, five))
    columns = jnp.concatenate(columns, axis=0)
    pieces = [columns, exchange(columns, "dp", 1)]
    hidden, mixed_attn, grad_mixed, grad_att, sums2, down, mine, theirs = run_feed_forward(
        index, five, mixed, cotangent, packed, pieces, mp
    )
    received = exchange(theirs, "dp", 1)
    shape = cotangent.shape
    layer_out = run_layer_output(hidden, mixed_attn, down, shape, None, 0, 0.34)
    received, layer_out = lax.optimization_barrier((received, layer_out))
    parts = list(add_halves(mine, received))
    parts[0], grad_att = lax.optimization_barrier((parts[0], grad_att))
    plane = [parts[0]] + [exchange(parts[i], "dp", p) for i, p in enumerate(offsets) if i]
    kept = (five, mixed, v, raised, facts)
    input_grad, sums, mine_a, theirs_a = run_backward(
        index, weight, kept, (grad_att, grad_mixed), packed, sums2, dp
    )
    plane, theirs_a, sums = lax.optimization_barrier((plane, theirs_a, sums))
    received_a = exchange(theirs_a, "dp", 1)
    received_s = exchange(sums, "dp", 1)
    total = add_wide(*plane).astype(BF)
    total, received_s = lax.optimization_barrier((total, received_s))
    part = 2 * ffs
    near = jnp.concatenate([total[:, :part], total[:, 2 * part : 3 * part]], axis=1)
    out_part = total[:, 4 * part :]
    far = jnp.concatenate([total[:, part : 2 * part], total[:, 3 * part :]], axis=1)
    parts = list(add_halves_and_sums(index, mine_a, received_a, sums, received_s))
    parts[0], hidden, layer_out = lax.optimization_barrier((parts[0], hidden, layer_out))
    plane_a = [parts[0]] + [exchange(parts[i], "dp", p) for i, p in enumerate(offsets) if i]
    received_f = exchange(far, "mp", 1)
    layer_out = run_layer_output(hidden, mixed_attn, down, shape, layer_out, 0.34, 0.67)
    plane_a, layer_out = lax.optimization_barrier((plane_a, layer_out))
    total = add_packed("add_plane", plane_a)
    received_1 = exchange(total, "mp", 1)
    received_f, _ = lax.optimization_barrier((received_f, total))
    near_sum = add_wide(near, received_f[:, : 2 * part])
    out_sum = lax.optimization_barrier(add_wide(out_part, received_f[:, 2 * part :]).astype(BF))
    keep = near_sum[:, :part]
    send = jnp.concatenate([near_sum[:, part:].astype(BF), out_sum], axis=1)
    received_n = exchange(send, "mp", 2)
    received_1, _ = lax.optimization_barrier((received_1, send))
    total = add_packed("add_near", (total, received_1))
    received_2 = exchange(total, "mp", 2)
    layer_out, _ = lax.optimization_barrier((layer_out, total))
    layer_out = run_layer_output(hidden, mixed_attn, down, shape, layer_out, 0.67, 1)
    received_n, layer_out = lax.optimization_barrier((received_n, layer_out))
    grad_up = keep[:, :ffs] + received_n[:, :ffs].astype(F32)
    grad_down = keep[:, ffs:] + received_n[:, ffs : 2 * ffs].astype(F32)
    grad_out = add_wide(out_sum, received_n[:, 2 * ffs :])
    grad_qkv, grad_conv, *grads = add_last((total, received_2))
    return (layer_out, input_grad, grad_qkv, grad_out, grad_up, grad_down, grad_conv, *[g.reshape(own) for g in grads])


def gathered_plan(tokens, segment_ids, valid_len, qkv_weight, out_weight, up_weight, down_weight, conv_weight, vectors, cotangent):
    count, seq, width = tokens.shape
    own = qkv_weight.shape[0]
    dp = width // own
    columns = jnp.stack([conv_weight[0], conv_weight[1], conv_weight[2], *vectors], axis=1)
    narrow = jnp.concatenate([qkv_weight, jnp.pad(columns, ((0, 0), (0, VECTORS - 7))), out_weight], axis=1)
    wide = lax.all_gather(narrow, "dp", axis=0, tiled=True)
    both = lax.all_gather(jnp.concatenate([up_weight, down_weight], axis=0), "mp", axis=1, tiled=True)
    ff = both.shape[1]
    shards = ff // width
    both = lax.all_gather(both, "dp", axis=0).reshape(dp, 2, own, shards, width)
    both = both.transpose(3, 1, 0, 2, 4).reshape(2 * ff, width)
    column = jnp.concatenate([both, wide[:, 3 * width + VECTORS :]], axis=0)
    index = jnp.zeros((1,), jnp.int32)
    five, mixed, v, raised, facts, packed, weight = run_forward(
        index, tokens, segment_ids, valid_len, [wide[:, : 3 * width + VECTORS]]
    )
    hidden, mixed_attn, grad_mixed, grad_att, sums2, down, grads = run_feed_forward(
        index, five, mixed, cotangent, packed, [column], shards
    )
    kept = (five, mixed, v, raised, facts)
    layer_out = run_layer_output(hidden, mixed_attn, down, cotangent.shape, None, 0, 1)
    input_grad, sums, grad_qkv = run_backward(index, weight, kept, (grad_att, grad_mixed), packed, sums2, 1)
    grad_ff = grads[0, :, : 2 * ff].reshape(width, shards, 2, width).transpose(0, 2, 1, 3).reshape(width, 2 * ff)
    grad_ff = lax.psum_scatter(grad_ff, "dp", scatter_dimension=0, tiled=True).reshape(own, 2, ff)
    grad_ff = lax.psum_scatter(grad_ff, "mp", scatter_dimension=2, tiled=True).astype(F32)
    grad_attn = jnp.concatenate([grad_qkv[0], grads[0, :, 2 * ff :]], axis=1)
    grad_attn = lax.psum_scatter(grad_attn, "dp", scatter_dimension=0, tiled=True)
    grad_attn = lax.psum(grad_attn, "mp").astype(F32)
    sums = lax.psum(sums, ("dp", "mp"))
    sums = lax.dynamic_slice_in_dim(sums, lax.axis_index("dp") * own, own, axis=1)
    return (
        layer_out, input_grad, grad_attn[:, : 3 * width], grad_attn[:, 3 * width :],
        grad_ff[:, 0], grad_ff[:, 1], sums[0:3], sums[3], sums[4], sums[5], sums[6],
    )


def on_device(
    tokens, segment_ids, valid_len, qkv_weight, out_weight, up_weight, down_weight, conv_weight,
    ln1_gain, ln1_shift, ln2_gain, ln2_shift, cotangent,
):
    own, ffs = up_weight.shape
    direct = own % 16 == 0 and ffs == tokens.shape[2] and own <= VECTORS and lax.axis_size("mp") == 4
    plan = direct_plan if direct else gathered_plan
    return plan(
        tokens, segment_ids, valid_len, qkv_weight, out_weight, up_weight, down_weight, conv_weight,
        (ln1_gain, ln1_shift, ln2_gain, ln2_shift), cotangent,
    )


def solution(mesh):
    rows = P(("dp", "mp"), None, None)
    weights = (P("dp", None), P("dp", None), P("dp", "mp"), P("dp", "mp"), P(None, "dp"))
    vectors = (P("dp"),) * 4
    return jax.shard_map(
        on_device,
        mesh=mesh,
        in_specs=(rows, P(("dp", "mp"), None), P(("dp", "mp"))) + weights + vectors + (rows,),
        out_specs=(rows, rows) + weights + vectors,
        check_vma=False,
    )
```

```python
import functools
import math

import jax
import jax.numpy as jnp
from jax import lax
from jax.experimental import pallas as pl
from jax.experimental.pallas import tpu as pltpu
from jax.sharding import PartitionSpec as P

HEADS = 6
VECTORS = 128
LANES = 128
BF = jnp.bfloat16
F32 = jnp.float32
MIB = 1024 * 1024
VMEM_LIMITS = dict(forward_attention=34, feed_forward=44, backward=42, layer_output=16)


def mm(lhs, rhs):
    return lax.dot_general(lhs, rhs, (((1,), (0,)), ((), ())), preferred_element_type=F32)


def mm_nt(lhs, rhs):
    return lax.dot_general(lhs, rhs, (((1,), (1,)), ((), ())), preferred_element_type=F32)


def tree_sum(items):
    items = list(items)
    while len(items) > 1:
        items = [a + b for a, b in zip(items[::2], items[1::2])]
    return items[0]


def pack_weights(qkv_ref, up_ref, down_ref, conv_ref, g1_ref, s1_ref, g2_ref, s2_ref, narrow_ref, ff_ref, rows_ref):
    own, ffs = up_ref.shape
    rows_ref[...] = jnp.zeros_like(rows_ref)
    rows_ref[0:3, :own] = conv_ref[...].astype(F32)
    for i, ref in enumerate((g1_ref, s1_ref, g2_ref, s2_ref)):
        rows_ref[3 + i : 4 + i, :own] = ref[...].astype(F32)
    wide = qkv_ref.shape[1]
    narrow_ref[:, :wide] = qkv_ref[...]
    narrow_ref[:, wide:] = rows_ref[...].T[:own].astype(BF)
    ff_ref[:own] = up_ref[...]
    ff_ref[own:] = down_ref[...]


def tiles(total, size):
    return [slice(at, at + size) for at in range(0, total, size)]


def weave(*strands):
    strands = [strand for strand in strands if strand]
    total = sum(len(strand) for strand in strands)
    pieces = [((i + 0.5) / len(strand), j, piece) for j, strand in enumerate(strands) for i, piece in enumerate(strand)]
    assert len(pieces) == total
    for _, _, piece in sorted(pieces, key=lambda item: item[:2]):
        piece()


def twice(tile, lanes):
    return jnp.concatenate([tile] * (lanes // LANES), axis=1)


def load_columns(packed_ref, col_ref, places):
    for i, place in enumerate(places):
        column = packed_ref[:, place : place + 1].astype(F32)
        col_ref[i] = jnp.broadcast_to(column, (column.shape[0], LANES))


def pairwise(items, combine):
    items = list(items)
    while len(items) > 1:
        odd = items[len(items) // 2 * 2 :]
        items = [combine(a, b) for a, b in zip(items[::2], items[1::2])] + odd
    return items[0]


def fold(values, combine=jnp.add):
    return pairwise([values[t] for t in tiles(values.shape[0], 8)], combine)


def column_mean(values):
    return jnp.sum(fold(values), axis=0, keepdims=True) * (1.0 / values.shape[0])


def norm_columns(values):
    centred = values - column_mean(values)
    scale = lax.rsqrt(column_mean(centred * centred) + 1e-06)
    return centred * scale, scale


def fold_lanes(values):
    return sum(values[:, t] for t in tiles(values.shape[1], LANES))


def forward_attention(index_ref, len_ref, tok_ref, seg_ref, *refs, pieces):
    cores = 2 if pieces > 1 else 1
    piece_refs = refs[:cores]
    (
        five_out, mc_out, v_out, e_out, facts_ref, packed_ref, w_ref,
        wt_ref, wide_ref, col_ref, key_mask_ref, query_mask_ref, key_ref, value_ref,
        five_slots, mc_slots, v_slots, e_slots, sems,
    ) = refs[cores:]
    rows, seq, width = tok_ref.shape
    head = width // HEADS
    step = pl.program_id(0)
    slot = lax.rem(step, 2)
    x_ref, norm_ref, q_ref, k_ref, att_ref = [five_slots.at[slot, :, i] for i in range(5)]
    mc_ref, v_ref, e_ref = mc_slots.at[slot], v_slots.at[slot], e_slots.at[slot]
    aux_ref, inv_ref = facts_ref.at[:, :8], facts_ref.at[:, 8:]

    def copies(at, r):
        here, row = lax.rem(at, 2), at * rows + r
        pairs = [
            (five_slots.at[here, r, :4], five_out.at[row, :4]),
            (mc_slots.at[here, r], mc_out.at[row]),
            (v_slots.at[here, r], v_out.at[row]),
            (five_slots.at[here, r, 4:], five_out.at[row, 4:]),
            (e_slots.at[here, r], e_out.at[row]),
        ]
        return [pltpu.make_async_copy(a, b, sems.at[here, r, i]) for i, (a, b) in enumerate(pairs)]

    def wait_for(at):
        for r in range(rows):
            for copy in copies(at, r):
                copy.wait()

    @pl.when(step >= 2)
    def _():
        wait_for(step - 2)

    @pl.when(step == 0)
    def _():
        own = width // pieces
        for i in range(pieces):
            here = pl.ds(pl.multiple_of(index_ref[i] * own, 16), own)
            wide_ref[here, :] = piece_refs[i % cores][i // cores * own : (i // cores + 1) * own]
        w_ref[...] = wide_ref[:, : 3 * width]
        wt_ref[...] = wide_ref[:, : 3 * width].T
        packed_ref[...] = wide_ref[:, 3 * width :]
        load_columns(packed_ref, col_ref, range(5))
        col_ref[1] = col_ref[1] + 1.0

    place = lax.broadcasted_iota(jnp.int32, (1, seq), 1)
    zero = jnp.zeros((head, seq), BF)

    def preparation(r):
        known = {}

        def start():
            segs = seg_ref[pl.ds(step * rows + r, 1), :].astype(F32)
            valid = place < len_ref[step * rows + r]
            number = jnp.where(valid, segs, -1.0)
            links = jnp.where(valid & (place > 0) & (number == pltpu.roll(number, 1, 1)), 1.0, 0.0)
            next_links = jnp.where(place < seq - 1, pltpu.roll(links, seq - 1, 1), 0.0)
            none = jnp.zeros_like(links)
            aux = jnp.concatenate([links, next_links, number, none, none, none, none, none], axis=0)
            aux_ref[r] = aux
            x_ref[r] = tok_ref[r].T
            known.update(segs=segs, links=links, next_links=next_links, key_number=aux.T[:, 2:3])

        def mask():
            number = known["key_number"]
            lane = lax.broadcasted_iota(jnp.int32, (seq, LANES), 1)
            itself = lax.broadcasted_iota(jnp.int32, (seq, LANES), 0) - (seq - LANES)
            chosen = (lane.astype(F32) == number) | ((number < 0.0) & (lane == itself))
            key_mask_ref[r] = jnp.where(chosen, 1.0, 0.0).astype(BF)
            slot = lax.broadcasted_iota(jnp.int32, (LANES, seq), 0)
            itself = lax.broadcasted_iota(jnp.int32, (LANES, seq), 1) - (seq - LANES)
            open_to = (slot.astype(F32) == known["segs"]) | ((slot >= LANES // 2) & (slot == itself))
            query_mask_ref[r] = jnp.where(open_to, 0.0, -1e30).astype(BF)

        def conv(t):
            base = x_ref[r, t].astype(F32)
            before = pltpu.roll(base, 1, 1) * known["links"]
            after = pltpu.roll(base, seq - 1, 1) * known["next_links"]
            conv0, conv1, conv2 = [twice(col_ref[i, t], seq) for i in range(3)]
            mc_ref[r, t] = before * conv0 + base * conv1 + after * conv2

        def norm(t):
            n, _ = norm_columns(mc_ref[r, :, t])
            norm_ref[r, :, t] = (n * col_ref[3] + col_ref[4]).astype(BF)

        pieces = [start] + [functools.partial(conv, t) for t in tiles(width, 32)]
        pieces += [functools.partial(norm, t) for t in tiles(seq, LANES)]
        return pieces + [mask]

    def project(pair):
        normed = jnp.concatenate([norm_ref[r] for r in pair], axis=1)
        for i, ref in enumerate((q_ref, k_ref, value_ref)):
            part = mm(wt_ref[i * width : (i + 1) * width], normed)
            part = (part * (head ** (-0.5) * math.log2(math.e)) if i == 0 else part).astype(BF)
            for j, r in enumerate(pair):
                ref[r] = part[:, j * seq : (j + 1) * seq]
        for r in pair:
            key_ref[r] = k_ref[r].T
            v_ref[r] = value_ref[r].T

    def scores(r, p):
        low, high = [q_ref[r, h * head : (h + 1) * head] for h in (2 * p, 2 * p + 1)]
        both = jnp.concatenate([jnp.concatenate([low, zero], axis=1), jnp.concatenate([zero, high], axis=1)], axis=0)
        keys = jnp.concatenate([key_ref[r, :, 2 * p * head : 2 * (p + 1) * head], key_mask_ref[r]], axis=1)
        masks = jnp.concatenate([query_mask_ref[r], query_mask_ref[r]], axis=1)
        return mm(keys, jnp.concatenate([both, masks], axis=0))

    def attended(r, p):
        both = jnp.concatenate([e_ref[r, 2 * p], e_ref[r, 2 * p + 1]], axis=1)
        product = mm(value_ref[r, 2 * p * head : 2 * (p + 1) * head], both)
        parts = []
        for i in range(2):
            att = product[i * head : (i + 1) * head, i * seq : (i + 1) * seq] * inv_ref[r, 2 * p + i : 2 * p + i + 1]
            parts.append(att.astype(BF))
        return jnp.concatenate(parts, axis=0)

    def soften(r, p, product):
        for i in range(2):
            for t in tiles(seq, LANES):
                masked = product[:, i * seq + t.start : i * seq + t.stop]
                raised = jnp.exp2(masked - jnp.max(fold(masked, jnp.maximum), axis=0, keepdims=True))
                inv_ref[r, 2 * p + i : 2 * p + i + 1, t] = 1.0 / jnp.sum(fold(raised), axis=0, keepdims=True)
                e_ref[r, 2 * p + i, :, t] = raised.astype(BF)

    def store(r, p, finished):
        att_ref[r, 2 * p * head : 2 * (p + 1) * head] = finished
        if p == HEADS // 2 - 1:
            for copy in copies(step, r)[3:]:
                copy.start()

    weave(*[preparation(r) for r in range(rows)])
    project(range(rows))
    for r in range(rows):
        for copy in copies(step, r)[:3]:
            copy.start()
    work = [(r, p) for r in range(rows) for p in range(HEADS // 2)]
    current, last = scores(*work[0]), None
    for at, (r, p) in enumerate(work):
        following = scores(*work[at + 1]) if at + 1 < len(work) else None
        finished = attended(*last) if last else None
        soften(r, p, current)
        if last:
            store(*last, finished)
        current, last = following, (r, p)
    store(*last, attended(*last))

    final = step == pl.num_programs(0) - 1

    @pl.when(final & (step > 0))
    def _():
        wait_for(step - 1)

    @pl.when(final)
    def _():
        wait_for(step)


def gelu_parts(y):
    twice_cdf = lax.erf(y) + 1.0
    bell = jnp.exp2(y * y * -math.log2(math.e) + math.log2(2.0 / math.sqrt(math.pi)))
    return y * twice_cdf, twice_cdf + y * bell


def feed_forward(index_ref, five_ref, mc_ref, ct_ref, packed_ref, *refs, pieces, shards):
    att_ref = five_ref.at[:, 0]
    groups = 2 if pieces > 1 else 1
    piece_refs = refs[:groups]
    hidden_out, mixed_out, gm_ref, ga_ref, gs_ref, down_ref = refs[groups : groups + 6]
    gw_refs = refs[groups + 6 : 2 * groups + 6]
    (
        up_ref, upt_ref, downt_ref, out_ref, outt_ref, up_acc, down_acc, out_acc, col_acc, col_ref,
        n_ref, norm_ref, ctt_ref, gp_ref, gn_ref, scale_ref, branch_ref, hidden_ref, mixed_ref, sems,
    ) = refs[2 * groups + 6 :]
    rows, seq, width = ct_ref.shape
    ff = up_ref.shape[1]
    ffs = ff // shards
    own = width // pieces
    step = pl.program_id(0)

    @pl.when(step == 0)
    def _():
        for acc in (up_acc, down_acc, out_acc, col_acc):
            acc[...] = jnp.zeros_like(acc)
        for i in range(pieces):
            here = pl.ds(pl.multiple_of(index_ref[i] * own, 16), own)
            ref, first = piece_refs[i % groups], i // groups * (2 * shards + 1) * own
            for j in range(shards):
                at = first + 2 * j * own
                up_ref[here, j * ffs : (j + 1) * ffs] = ref[at : at + own]
                down_ref[here, j * ffs : (j + 1) * ffs] = ref[at + own : at + 2 * own]
            at = first + 2 * shards * own
            out_ref[here, :] = ref[at : at + own]
        upt_ref[...] = up_ref[...].T
        downt_ref[...] = down_ref[...].T
        outt_ref[...] = out_ref[...].T
        load_columns(packed_ref, col_ref, (5, 6, 5))
        for i, factor in enumerate((0.5, math.sqrt(0.5), math.sqrt(0.5))):
            col_ref[i] = col_ref[i] * factor

    def copies(at, g):
        place = at * pairs + g
        return [
            pltpu.make_async_copy(hidden_ref.at[g], hidden_out.at[place], sems.at[0, g]),
            pltpu.make_async_copy(mixed_ref.at[g], mixed_out.at[place], sems.at[1, g]),
        ]

    pairs = n_ref.shape[0]

    @pl.when(step > 0)
    def _():
        for g in range(pairs):
            for copy in copies(step - 1, g):
                copy.wait()

    def begin(g):
        pair = range(g * paired, (g + 1) * paired)
        attended = jnp.concatenate([att_ref[r] for r in pair], axis=1)
        branch = mm(outt_ref[...], attended)
        for i, r in enumerate(pair):
            lanes = slice(i * seq, (i + 1) * seq)
            ctt_ref[g, :, lanes] = ct_ref[r].T
            mixed_ref[g, :, lanes] = mc_ref[r] + branch[:, lanes]
        for t in spots:
            n, scale = norm_columns(mixed_ref[g, :, t])
            n_ref[g, :, t] = n
            scale_ref[g, 0:1, t] = scale
            norm_ref[g, :, t] = (n * col_ref[2] + col_ref[1]).astype(BF)

    def activate(g, block):
        pre = mm(upt_ref[block], norm_ref[g])
        grad_hidden = mm(downt_ref[block], ctt_ref[g])
        for low in range(0, block.stop - block.start, 16):
            part = slice(low, low + 16)
            here = slice(block.start + low, block.start + low + 16)
            hidden, slope = gelu_parts(pre[part])
            hidden_ref[g, here] = hidden.astype(BF)
            gp_ref[g, here] = (grad_hidden[part] * slope).astype(BF)

    def weigh(g):
        gn_ref[g] = mm(up_ref[...], gp_ref[g])
        down_acc[...] += mm_nt(ctt_ref[g], hidden_ref[g])
        up_acc[...] += mm_nt(norm_ref[g], gp_ref[g])

    def norm_back(g):
        mean_e = [jnp.zeros((8, LANES), F32) for _ in spots]
        mean_en = [jnp.zeros((8, LANES), F32) for _ in spots]
        for d in tiles(width, 32):
            column = col_ref[0, d]
            gain_sum, shift_sum = col_acc[0, d], col_acc[1, d]
            for i, t in enumerate(spots):
                grad_n = gn_ref[g, d, t]
                product = grad_n * n_ref[g, d, t]
                gain_sum += product
                shift_sum += grad_n
                mean_e[i] += fold(grad_n * column)
                mean_en[i] += fold(product * column)
            col_acc[0, d] = gain_sum
            col_acc[1, d] = shift_sum
        for i, t in enumerate(spots):
            me = jnp.sum(mean_e[i], axis=0, keepdims=True) * (1.0 / width)
            men = jnp.sum(mean_en[i], axis=0, keepdims=True) * (1.0 / width)
            row, inside = divmod(t.start, seq)
            for d in tiles(width, 32):
                change = scale_ref[g, 0:1, t] * (gn_ref[g, d, t] * col_ref[0, d] - me - n_ref[g, d, t] * men)
                grad_mixed = ctt_ref[g, d, t].astype(F32) + change
                gm_ref[g * paired + row, d, inside : inside + LANES] = grad_mixed
                branch_ref[g, d, t] = grad_mixed.astype(BF)

    def end(g):
        pair = range(g * paired, (g + 1) * paired)
        attended = jnp.concatenate([att_ref[r] for r in pair], axis=1)
        grad_attended = mm(out_ref[...], branch_ref[g]).astype(BF)
        for i, r in enumerate(pair):
            ga_ref[r] = grad_attended[:, i * seq : (i + 1) * seq]
        out_acc[...] += mm_nt(attended, branch_ref[g])

    paired = rows // pairs
    spots = tiles(paired * seq, LANES)
    begin(0)
    copies(step, 0)[1].start()
    for g in range(pairs):
        for block in tiles(ff, 128):
            activate(g, block)
        copies(step, g)[0].start()
        if g + 1 < pairs:
            begin(g + 1)
            copies(step, g + 1)[1].start()
        weigh(g)
        norm_back(g)
        end(g)

    @pl.when(step == pl.num_programs(0) - 1)
    def _():
        for g in range(pairs):
            for copy in copies(step, g):
                copy.wait()
        for i in range(pieces):
            here = pl.ds(pl.multiple_of(index_ref[i] * own, 16), own)
            place = gw_refs[i % groups]
            for j in range(shards):
                cols = slice(j * ffs, (j + 1) * ffs)
                place[i // groups, :, 2 * j * ffs : (2 * j + 1) * ffs] = (up_acc[here, cols] * math.sqrt(0.5)).astype(BF)
                place[i // groups, :, (2 * j + 1) * ffs : (2 * j + 2) * ffs] = (down_acc[here, cols] * math.sqrt(0.5)).astype(BF)
            place[i // groups, :, 2 * ff :] = out_acc[here, :].astype(BF)
        gs_ref[...] = jnp.zeros_like(gs_ref)
        for i in range(2):
            gs_ref[5 + i : 6 + i] = jnp.sum(col_acc[i].T, axis=0, keepdims=True) * 0.5


def layer_output(hidden_ref, mixed_ref, down_ref, lo_ref):
    rows, seq, _ = lo_ref.shape
    total = (mixed_ref[0] + mm(down_ref[...], hidden_ref[0]) * math.sqrt(0.5)).astype(BF)
    for r in range(rows):
        lo_ref[r] = total[:, r * seq : (r + 1) * seq].T


def backward(
    five_ref, mc_ref, v_ref, e_ref, facts_ref, ga_ref, gm_ref, index_ref, w_ref, packed_ref, other_ref, ig_ref, gs_ref, *refs, pieces,
):
    x_ref, norm_ref, q_ref, k_ref, att_ref = [five_ref.at[:, i] for i in range(5)]
    aux_ref, inv_ref = facts_ref.at[:, :8], facts_ref.at[:, 8:]
    gw_refs = refs[:-11]
    (
        proj_ref, w_acc, norm_cat, soft_ref, logit_ref, gn_ref, acc_ref, col_ref, n_ref, g_ref, turn_ref
    ) = refs[-11:]
    rows, seq, width = v_ref.shape
    own = width // pieces
    head = width // HEADS
    step = pl.program_id(0)

    @pl.when(step == 0)
    def _():
        w_acc[...] = jnp.zeros_like(w_acc)
        acc_ref[...] = jnp.zeros_like(acc_ref)
        load_columns(packed_ref, col_ref, range(4))
        col_ref[1] = col_ref[1] + 1.0

    zero = jnp.zeros((head, seq), BF)
    work = [(r, p) for r in range(rows) for p in range(HEADS // 2)]

    def opening(r, p):
        grads, inners = [], []
        for h in (2 * p, 2 * p + 1):
            part = slice(h * head, (h + 1) * head)
            grad_att = ga_ref[r, part].astype(F32) * inv_ref[r, h : h + 1]
            inners.append(jnp.sum(fold(grad_att * att_ref[r, part].astype(F32)), axis=0, keepdims=True))
            grads.append(grad_att.astype(BF))
        low, high = grads
        both = jnp.concatenate([jnp.concatenate([low, zero], axis=1), jnp.concatenate([zero, high], axis=1)], axis=0)
        product = mm(v_ref[r, :, 2 * p * head : 2 * (p + 1) * head], both)
        soft_ref[r, 2 * p] = product[:, :seq]
        soft_ref[r, 2 * p + 1] = product[:, seq:]
        return jnp.concatenate(grads, axis=0), inners

    spots = tiles(seq, LANES)

    def finish_row(r):
        wide = [slice(r * seq + t.start, r * seq + t.stop) for t in spots]
        lanes = slice(r * seq, (r + 1) * seq)
        norm_cat[:, lanes] = norm_ref[r]
        gn_ref[:, lanes] = mm(w_ref[...], proj_ref[:, lanes])
        scales = []
        for t in spots:
            n, scale = norm_columns(mc_ref[r, :, t])
            n_ref[r, :, t] = n
            scales.append(scale)
        mean_e = [jnp.zeros((8, LANES), F32) for _ in spots]
        mean_en = [jnp.zeros((8, LANES), F32) for _ in spots]
        for d in tiles(width, 32):
            column = col_ref[3, d]
            gain_sum, shift_sum = acc_ref[3, d], acc_ref[4, d]
            for i, t in enumerate(spots):
                grad_n = gn_ref[d, wide[i]]
                product = grad_n * n_ref[r, d, t]
                gain_sum += product
                shift_sum += grad_n
                mean_e[i] += fold(grad_n * column)
                mean_en[i] += fold(product * column)
            acc_ref[3, d] = gain_sum
            acc_ref[4, d] = shift_sum
        for i, t in enumerate(spots):
            me = jnp.sum(mean_e[i], axis=0, keepdims=True) * (1.0 / width)
            men = jnp.sum(mean_en[i], axis=0, keepdims=True) * (1.0 / width)
            for d in tiles(width, 64):
                e = gn_ref[d, wide[i]] * col_ref[3, d]
                g_ref[r, d, t] = gm_ref[r, d, t] + scales[i] * (e - me - n_ref[r, d, t] * men)
        links, next_links = aux_ref[r, 0:1], aux_ref[r, 1:2]
        for d in tiles(width, 32):
            g = g_ref[r, d]
            base = x_ref[r, d].astype(F32)
            before = pltpu.roll(g, 1, 1) * links
            after = pltpu.roll(g, seq - 1, 1) * next_links
            acc_ref[0, d] += fold_lanes(base * after)
            acc_ref[1, d] += fold_lanes(base * g)
            acc_ref[2, d] += fold_lanes(base * before)
            conv0, conv1, conv2 = [twice(col_ref[i, d], seq) for i in range(3)]
            turn_ref[r, d] = (conv1 * g + conv0 * after + conv2 * before).astype(BF)
        ig_ref[r] = turn_ref[r].T

    ready = opening(*work[0])
    for at, (r, p) in enumerate(work):
        grad_att, inners = ready
        if at + 1 < len(work):
            ready = opening(*work[at + 1])
        for i, h in enumerate((2 * p, 2 * p + 1)):
            for t in tiles(seq, 32):
                raised = e_ref[r, h, t].astype(F32)
                logit_ref[r, h, t] = (raised * (soft_ref[r, h, t] - inners[i])).astype(BF)
        part = slice(2 * p * head, 2 * (p + 1) * head)
        pair = slice(2 * p, 2 * p + 2)
        beside = jnp.concatenate([logit_ref[r, 2 * p], logit_ref[r, 2 * p + 1]], axis=1)
        grad_q = mm(k_ref[r, part], beside)
        grad_k = mm_nt(q_ref[r, part], logit_ref[r, pair].reshape(2 * seq, seq))
        grad_v = mm_nt(grad_att, e_ref[r, pair].reshape(2 * seq, seq))
        for i in range(2):
            place = slice(r * seq, (r + 1) * seq)
            own_rows, own_cols = slice(i * head, (i + 1) * head), slice(i * seq, (i + 1) * seq)
            for j, (grad, factor) in enumerate(((grad_q, head ** (-0.5)), (grad_k, math.log(2.0)), (grad_v, None))):
                first = j * width + (2 * p + i) * head
                mine = grad[own_rows, own_cols]
                proj_ref[first : first + head, place] = (mine if factor is None else mine * factor).astype(BF)
        if p == HEADS // 2 - 1:
            finish_row(r)
    w_acc[...] += mm_nt(norm_cat[...], proj_ref[...])

    @pl.when(step == pl.num_programs(0) - 1)
    def _():
        gs_ref[...] = other_ref[...]
        for i in range(5):
            gs_ref[i : i + 1] += jnp.sum(acc_ref[i].T, axis=0, keepdims=True)
        groups = len(gw_refs)
        for i in range(pieces):
            here = pl.ds(pl.multiple_of(index_ref[i] * own, 16), own)
            gw_refs[i % groups][i // groups] = w_acc[here, :].astype(BF)


def in_hbm(values):
    return pltpu.with_memory_space_constraint(values, pltpu.HBM)


def by_row(shape, rows, first=0):
    tail = tuple(shape[1:])
    return pl.BlockSpec((rows,) + tail, lambda i, *_: (i + first,) + (0,) * len(tail))


def whole(shape):
    place = (0,) * len(shape)
    return pl.BlockSpec(tuple(shape), lambda i, *_: place, pipeline_mode=pl.Buffered(1))


def step_rows(count, most):
    return max(r for r in range(1, most + 1) if count % r == 0)


def call(body, name, scalars, rows, row_args, args, row_outs, outs, scratch, span=None, into=None, near=(), only=None, manual=()):
    first, count = span or (0, row_args[0].shape[0])
    skip = first // rows
    total = row_args[0].shape[0]

    def spec_of(shape):
        return by_row(shape, shape[0] * rows // total, skip)

    in_specs = [spec_of(a.shape) for a in row_args]
    if only:
        tail = row_args[0].shape[2:]
        in_specs[0] = pl.BlockSpec((rows, 1) + tail, lambda i, *_: (i, only) + (0,) * len(tail))
    in_specs += [whole(a.shape) for a in args]
    aliases = {}
    if into is not None:
        in_specs.append(pl.BlockSpec(memory_space=pl.ANY))
        aliases = {len(scalars) + len(in_specs) - 1: 0}
    spec = pltpu.PrefetchScalarGridSpec(
        num_scalar_prefetch=len(scalars),
        grid=(count // rows,),
        in_specs=in_specs,
        out_specs=[pl.BlockSpec(memory_space=pl.ANY) for _ in manual] + [spec_of(s) for s, _ in row_outs] + [whole(s) for s, _ in outs],
        scratch_shapes=[pltpu.VMEM(*s) if isinstance(s, tuple) else s for s in scratch],
    )
    return pl.pallas_call(
        body,
        grid_spec=spec,
        out_shape=[pltpu.HBM(s, t) for s, t in manual] + [(jax.ShapeDtypeStruct if "out" + str(i) in near else pltpu.HBM)(s, t) for i, (s, t) in enumerate(row_outs)]
        + [jax.ShapeDtypeStruct(s, t) for s, t in outs],
        input_output_aliases=aliases,
        compiler_params=pltpu.CompilerParams(dimension_semantics=("arbitrary",), vmem_limit_bytes=VMEM_LIMITS[name] * MIB),
        name=name,
    )(*scalars, *[a if i in near else in_hbm(a) for i, a in enumerate(row_args)], *args, *(() if into is None else (into,)))


def small_call(body, name, args, outs, scratch=()):
    return pl.pallas_call(
        body,
        out_shape=[jax.ShapeDtypeStruct(s, t) for s, t in outs],
        scratch_shapes=[pltpu.VMEM(s, t) for s, t in scratch],
        compiler_params=pltpu.CompilerParams(vmem_limit_bytes=16 * MIB),
        name=name,
    )(*args)


def run_forward(index, tokens, segment_ids, valid_len, pieces):
    count, seq, width = tokens.shape
    rows = step_rows(count, 3)
    tails = [((5, width, seq), BF), ((width, seq), F32), ((seq, width), BF), ((HEADS, seq, seq), BF)]
    manual = [((count,) + s, t) for s, t in tails]
    return call(
        functools.partial(forward_attention, pieces=index.shape[0]), "forward_attention", (index, in_hbm(valid_len)),
        rows, (tokens,), (in_hbm(segment_ids), *pieces),
        [((count, 16, seq), F32)], [((width, VECTORS), BF), ((width, 3 * width), BF)],
        [
            ((3 * width, width), BF), ((width, 3 * width + VECTORS), BF), ((5, width, LANES), F32),
            ((rows, seq, LANES), BF), ((rows, LANES, seq), BF), ((rows, seq, width), BF), ((rows, width, seq), BF),
        ]
        + [((2, rows) + s, t) for s, t in tails] + [pltpu.SemaphoreType.DMA((2, rows, 5))],
        manual=manual,
    )


def run_feed_forward(index, five, mixed, cotangent, packed, pieces, shards):
    count, seq, width = cotangent.shape
    own = width // index.shape[0]
    ff = shards * width
    groups = 2 if index.shape[0] > 1 else 1
    paired = step_rows(count, 2)
    pairs = 2 if count // paired % 2 == 0 else 1
    rows = pairs * paired
    wide = paired * seq
    manual = [((count // paired, ff, wide), BF), ((count // paired, width, wide), F32)]
    row_outs = [((count, width, seq), F32), ((count, width, seq), BF)]
    grads = ((index.shape[0] // groups, own, 2 * ff + width), BF)
    return call(
        functools.partial(feed_forward, pieces=index.shape[0], shards=shards), "feed_forward", (index,),
        rows, (five, mixed, cotangent), (packed, *pieces),
        row_outs, [((8, width), F32), ((width, ff), BF)] + [grads] * groups,
        [((width, ff), BF)] + [((ff, width), BF)] * 2 + [((width, width), BF)] * 2
        + [((width, ff), F32)] * 2 + [((width, width), F32), ((2, width, LANES), F32), ((3, width, LANES), F32)]
        + [((pairs, width, wide), F32), ((pairs, width, wide), BF), ((pairs, width, wide), BF)]
        + [((pairs, ff, wide), BF)]
        + [((pairs, width, wide), F32), ((pairs, 8, wide), F32), ((pairs, width, wide), BF)]
        + [((pairs, ff, wide), BF), ((pairs, width, wide), F32), pltpu.SemaphoreType.DMA((2, pairs))],
        near=("out1",), only=4, manual=manual,
    )


def run_layer_output(hidden, mixed, down, shape, into, low, high):
    steps = hidden.shape[0]
    span = (int(low * steps), int(high * steps) - int(low * steps))

    def body(*refs):
        layer_output(*refs[:3], refs[-1])

    return call(body, "layer_output", (), 1, (hidden, mixed), (down,), [(shape, BF)], [], [], span=span, into=into)[0]


def run_backward(index, weight, kept, grads, packed, other, pieces):
    count, seq, width = kept[2].shape
    own = width // pieces
    groups = 2 if pieces > 1 else 1
    rows = step_rows(count, 3)
    row_args = (*kept, *grads)
    many = len(row_args)

    def body(index_ref, *refs):
        backward(*refs[:many], index_ref, *refs[many:], pieces=pieces)

    return call(
        body, "backward", (index,), rows, row_args, (weight, packed, other),
        [((count, seq, width), BF)], [((8, width), F32)] + [((pieces // groups, own, 3 * width), BF)] * groups,
        [
            ((3 * width, rows * seq), BF), ((width, 3 * width), F32), ((width, rows * seq), BF),
            ((rows, HEADS, seq, seq), F32), ((rows, HEADS, seq, seq), BF), ((width, rows * seq), F32),
            ((5, width, LANES), F32), ((4, width, LANES), F32), ((rows, width, seq), F32), ((rows, width, seq), F32),
            ((rows, width, seq), BF),
        ],
        near=(5,),
    )


def exchange(values, axis, offset):
    size = lax.axis_size(axis)
    return lax.ppermute(values, axis, [(i, i ^ offset) for i in range(size)])


def add_halves(mine, received):
    count, own, cols = mine.shape

    def body(mine_ref, received_ref, *out_refs):
        for i, ref in enumerate(out_refs):
            ref[...] = (mine_ref[i].astype(F32) + received_ref[i].astype(F32)).astype(BF)

    return small_call(body, "add_halves", (mine, received), [((own, cols), BF)] * count)


def add_wide(*items):
    return tree_sum(item.astype(F32) for item in items)


def store_high_low(ref, cols, values):
    high = values.astype(BF)
    low = (values - high.astype(F32)).astype(BF)
    ref[:, cols:] = jnp.concatenate([high, low, jnp.zeros((ref.shape[0] - 16, LANES), BF)], axis=0)


def load_high_low(ref, cols):
    both = ref[:16, cols:].astype(F32)
    return both[:8] + both[8:]


def add_halves_and_sums(index, mine, received, sums, received_sums):
    count, own, cols = mine.shape
    width = sums.shape[1]

    def body(index_ref, mine_ref, received_ref, sums_ref, received_sums_ref, *out_refs):
        total = sums_ref[...] + received_sums_ref[...]
        for i, ref in enumerate(out_refs):
            ref[:, :cols] = (mine_ref[i].astype(F32) + received_ref[i].astype(F32)).astype(BF)
            turned = pltpu.roll(total, lax.rem(width - index_ref[2 * i] * own, width), 1)[:, :LANES]
            store_high_low(ref, cols, turned)

    spec = pltpu.PrefetchScalarGridSpec(
        num_scalar_prefetch=1, grid=(1,),
        in_specs=[whole(a.shape) for a in (mine, received, sums, received_sums)],
        out_specs=[whole((own, cols + LANES))] * count,
    )
    return pl.pallas_call(
        body, grid_spec=spec, out_shape=[jax.ShapeDtypeStruct((own, cols + LANES), BF)] * count,
        compiler_params=pltpu.CompilerParams(vmem_limit_bytes=16 * MIB), name="add_halves_and_sums",
    )(index, mine, received, sums, received_sums)


def add_packed(name, items):
    cols = items[0].shape[1] - LANES

    def body(*refs):
        out_ref = refs[-1]
        out_ref[:, :cols] = tree_sum(ref[:, :cols].astype(F32) for ref in refs[:-1]).astype(BF)
        store_high_low(out_ref, cols, tree_sum(load_high_low(ref, cols) for ref in refs[:-1]))

    return small_call(body, name, items, [(items[0].shape, BF)])[0]


def add_last(items):
    own, cols = items[0].shape[0], items[0].shape[1] - LANES

    def body(*refs):
        ins, outs = refs[: len(items)], refs[len(items) :]
        outs[0][...] = tree_sum(ref[:, :cols].astype(F32) for ref in ins)
        vectors = tree_sum(load_high_low(ref, cols) for ref in ins)
        outs[1][...] = vectors[0:3, :own]
        for i in range(4):
            outs[2 + i][...] = vectors[3 + i : 4 + i, :own]

    return small_call(body, "add_last", items, [((own, cols), F32), ((3, own), F32)] + [((1, own), F32)] * 4)


def direct_plan(tokens, segment_ids, valid_len, qkv_weight, out_weight, up_weight, down_weight, conv_weight, vectors, cotangent):
    count, seq, width = tokens.shape
    own, ffs = up_weight.shape
    dp, mp = lax.axis_size("dp"), lax.axis_size("mp")
    me = lax.axis_index("dp")
    offsets = [2 * p for p in range(dp // 2)]
    index = jnp.stack([me ^ (p ^ c) for p in offsets for c in range(2)]).astype(jnp.int32)
    narrow, ff_own = small_call(
        pack_weights, "pack_weights",
        [in_hbm(a) for a in (qkv_weight, up_weight, down_weight, conv_weight, *[v.reshape(1, own) for v in vectors])],
        [((own, 3 * width + VECTORS), BF), ((2 * own, ffs), BF)], [((VECTORS, VECTORS), F32)],
    )
    shards = [ff_own] + [exchange(ff_own, "mp", j) for j in range(1, mp)]
    plane = jnp.concatenate([narrow] + [exchange(narrow, "dp", p) for p in offsets[1:]], axis=0)
    pieces = [plane, exchange(plane, "dp", 1)]
    column = jnp.concatenate(shards + [out_weight], axis=0)
    columns = [column] + [exchange(column, "dp", p) for p in offsets[1:]]
    five, mixed, v, raised, facts, packed, weight = run_forward(
        index, tokens, segment_ids, valid_len, pieces
    )
    columns, five = lax.optimization_barrier((columns, five))
    columns = jnp.concatenate(columns, axis=0)
    pieces = [columns, exchange(columns, "dp", 1)]
    hidden, mixed_attn, grad_mixed, grad_att, sums2, down, mine, theirs = run_feed_forward(
        index, five, mixed, cotangent, packed, pieces, mp
    )
    received = exchange(theirs, "dp", 1)
    shape = cotangent.shape
    layer_out = run_layer_output(hidden, mixed_attn, down, shape, None, 0, 0.17)
    received, layer_out = lax.optimization_barrier((received, layer_out))
    parts = list(add_halves(mine, received))
    parts[0], grad_att = lax.optimization_barrier((parts[0], grad_att))
    plane = [parts[0]] + [exchange(parts[i], "dp", p) for i, p in enumerate(offsets) if i]
    kept = (five, mixed, v, raised, facts)
    input_grad, sums, mine_a, theirs_a = run_backward(
        index, weight, kept, (grad_att, grad_mixed), packed, sums2, dp
    )
    plane, theirs_a, sums = lax.optimization_barrier((plane, theirs_a, sums))
    received_a = exchange(theirs_a, "dp", 1)
    received_s = exchange(sums, "dp", 1)
    total = add_wide(*plane).astype(BF)
    total, received_s = lax.optimization_barrier((total, received_s))
    part = 2 * ffs
    near = jnp.concatenate([total[:, :part], total[:, 2 * part : 3 * part]], axis=1)
    out_part = total[:, 4 * part :]
    far = jnp.concatenate([total[:, part : 2 * part], total[:, 3 * part :]], axis=1)
    parts = list(add_halves_and_sums(index, mine_a, received_a, sums, received_s))
    parts[0], hidden, layer_out = lax.optimization_barrier((parts[0], hidden, layer_out))
    plane_a = [parts[0]] + [exchange(parts[i], "dp", p) for i, p in enumerate(offsets) if i]
    received_f = exchange(far, "mp", 1)
    layer_out = run_layer_output(hidden, mixed_attn, down, shape, layer_out, 0.17, 0.51)
    plane_a, layer_out = lax.optimization_barrier((plane_a, layer_out))
    total = add_packed("add_plane", plane_a)
    received_1 = exchange(total, "mp", 1)
    received_f, _ = lax.optimization_barrier((received_f, total))
    near_sum = add_wide(near, received_f[:, : 2 * part])
    out_sum = lax.optimization_barrier(add_wide(out_part, received_f[:, 2 * part :]).astype(BF))
    keep = near_sum[:, :part]
    send = jnp.concatenate([near_sum[:, part:].astype(BF), out_sum], axis=1)
    received_n = exchange(send, "mp", 2)
    layer_out, _ = lax.optimization_barrier((layer_out, send))
    layer_out = run_layer_output(hidden, mixed_attn, down, shape, layer_out, 0.51, 0.67)
    received_1, layer_out = lax.optimization_barrier((received_1, layer_out))
    total = add_packed("add_near", (total, received_1))
    received_2 = exchange(total, "mp", 2)
    layer_out, _ = lax.optimization_barrier((layer_out, total))
    layer_out = run_layer_output(hidden, mixed_attn, down, shape, layer_out, 0.67, 1)
    received_n, layer_out = lax.optimization_barrier((received_n, layer_out))
    grad_up = keep[:, :ffs] + received_n[:, :ffs].astype(F32)
    grad_down = keep[:, ffs:] + received_n[:, ffs : 2 * ffs].astype(F32)
    grad_out = add_wide(out_sum, received_n[:, 2 * ffs :])
    grad_qkv, grad_conv, *grads = add_last((total, received_2))
    return (layer_out, input_grad, grad_qkv, grad_out, grad_up, grad_down, grad_conv, *[g.reshape(own) for g in grads])


def gathered_plan(tokens, segment_ids, valid_len, qkv_weight, out_weight, up_weight, down_weight, conv_weight, vectors, cotangent):
    count, seq, width = tokens.shape
    own = qkv_weight.shape[0]
    dp = width // own
    columns = jnp.stack([conv_weight[0], conv_weight[1], conv_weight[2], *vectors], axis=1)
    narrow = jnp.concatenate([qkv_weight, jnp.pad(columns, ((0, 0), (0, VECTORS - 7))), out_weight], axis=1)
    wide = lax.all_gather(narrow, "dp", axis=0, tiled=True)
    both = lax.all_gather(jnp.concatenate([up_weight, down_weight], axis=0), "mp", axis=1, tiled=True)
    ff = both.shape[1]
    shards = ff // width
    both = lax.all_gather(both, "dp", axis=0).reshape(dp, 2, own, shards, width)
    both = both.transpose(3, 1, 0, 2, 4).reshape(2 * ff, width)
    column = jnp.concatenate([both, wide[:, 3 * width + VECTORS :]], axis=0)
    index = jnp.zeros((1,), jnp.int32)
    five, mixed, v, raised, facts, packed, weight = run_forward(
        index, tokens, segment_ids, valid_len, [wide[:, : 3 * width + VECTORS]]
    )
    hidden, mixed_attn, grad_mixed, grad_att, sums2, down, grads = run_feed_forward(
        index, five, mixed, cotangent, packed, [column], shards
    )
    kept = (five, mixed, v, raised, facts)
    layer_out = run_layer_output(hidden, mixed_attn, down, cotangent.shape, None, 0, 1)
    input_grad, sums, grad_qkv = run_backward(index, weight, kept, (grad_att, grad_mixed), packed, sums2, 1)
    grad_ff = grads[0, :, : 2 * ff].reshape(width, shards, 2, width).transpose(0, 2, 1, 3).reshape(width, 2 * ff)
    grad_ff = lax.psum_scatter(grad_ff, "dp", scatter_dimension=0, tiled=True).reshape(own, 2, ff)
    grad_ff = lax.psum_scatter(grad_ff, "mp", scatter_dimension=2, tiled=True).astype(F32)
    grad_attn = jnp.concatenate([grad_qkv[0], grads[0, :, 2 * ff :]], axis=1)
    grad_attn = lax.psum_scatter(grad_attn, "dp", scatter_dimension=0, tiled=True)
    grad_attn = lax.psum(grad_attn, "mp").astype(F32)
    sums = lax.psum(sums, ("dp", "mp"))
    sums = lax.dynamic_slice_in_dim(sums, lax.axis_index("dp") * own, own, axis=1)
    return (
        layer_out, input_grad, grad_attn[:, : 3 * width], grad_attn[:, 3 * width :],
        grad_ff[:, 0], grad_ff[:, 1], sums[0:3], sums[3], sums[4], sums[5], sums[6],
    )


def on_device(
    tokens, segment_ids, valid_len, qkv_weight, out_weight, up_weight, down_weight, conv_weight,
    ln1_gain, ln1_shift, ln2_gain, ln2_shift, cotangent,
):
    own, ffs = up_weight.shape
    direct = own % 16 == 0 and ffs == tokens.shape[2] and own <= VECTORS and lax.axis_size("mp") == 4
    plan = direct_plan if direct else gathered_plan
    return plan(
        tokens, segment_ids, valid_len, qkv_weight, out_weight, up_weight, down_weight, conv_weight,
        (ln1_gain, ln1_shift, ln2_gain, ln2_shift), cotangent,
    )


def solution(mesh):
    rows = P(("dp", "mp"), None, None)
    weights = (P("dp", None), P("dp", None), P("dp", "mp"), P("dp", "mp"), P(None, "dp"))
    vectors = (P("dp"),) * 4
    return jax.shard_map(
        on_device,
        mesh=mesh,
        in_specs=(rows, P(("dp", "mp"), None), P(("dp", "mp"))) + weights + vectors + (rows,),
        out_specs=(rows, rows) + weights + vectors,
        check_vma=False,
    )
```

```python
import functools
import math

import jax
import jax.numpy as jnp
from jax import lax
from jax.experimental import pallas as pl
from jax.experimental.pallas import tpu as pltpu
from jax.sharding import PartitionSpec as P

HEADS = 6
VECTORS = 128
LANES = 128
BF = jnp.bfloat16
F32 = jnp.float32
MIB = 1024 * 1024
VMEM_LIMITS = dict(forward_attention=32, feed_forward=44, backward=42, layer_output=16)


def mm(lhs, rhs):
    return lax.dot_general(lhs, rhs, (((1,), (0,)), ((), ())), preferred_element_type=F32)


def mm_nt(lhs, rhs):
    return lax.dot_general(lhs, rhs, (((1,), (1,)), ((), ())), preferred_element_type=F32)


def tree_sum(items):
    items = list(items)
    while len(items) > 1:
        items = [a + b for a, b in zip(items[::2], items[1::2])]
    return items[0]


def pack_weights(qkv_ref, up_ref, down_ref, conv_ref, g1_ref, s1_ref, g2_ref, s2_ref, narrow_ref, ff_ref, rows_ref):
    own, ffs = up_ref.shape
    rows_ref[...] = jnp.zeros_like(rows_ref)
    rows_ref[0:3, :own] = conv_ref[...].astype(F32)
    for i, ref in enumerate((g1_ref, s1_ref, g2_ref, s2_ref)):
        rows_ref[3 + i : 4 + i, :own] = ref[...].astype(F32)
    wide = qkv_ref.shape[1]
    narrow_ref[:, :wide] = qkv_ref[...]
    narrow_ref[:, wide:] = rows_ref[...].T[:own].astype(BF)
    ff_ref[:own] = up_ref[...]
    ff_ref[own:] = down_ref[...]


def tiles(total, size):
    return [slice(at, at + size) for at in range(0, total, size)]


def weave(*strands):
    strands = [strand for strand in strands if strand]
    total = sum(len(strand) for strand in strands)
    pieces = [((i + 0.5) / len(strand), j, piece) for j, strand in enumerate(strands) for i, piece in enumerate(strand)]
    assert len(pieces) == total
    for _, _, piece in sorted(pieces, key=lambda item: item[:2]):
        piece()


def twice(tile, lanes):
    return jnp.concatenate([tile] * (lanes // LANES), axis=1)


def load_columns(packed_ref, col_ref, places):
    for i, place in enumerate(places):
        column = packed_ref[:, place : place + 1].astype(F32)
        col_ref[i] = jnp.broadcast_to(column, (column.shape[0], LANES))


def pairwise(items, combine):
    items = list(items)
    while len(items) > 1:
        odd = items[len(items) // 2 * 2 :]
        items = [combine(a, b) for a, b in zip(items[::2], items[1::2])] + odd
    return items[0]


def fold(values, combine=jnp.add):
    return pairwise([values[t] for t in tiles(values.shape[0], 8)], combine)


def column_mean(values):
    return jnp.sum(fold(values), axis=0, keepdims=True) * (1.0 / values.shape[0])


def norm_columns(values):
    centred = values - column_mean(values)
    scale = lax.rsqrt(column_mean(centred * centred) + 1e-06)
    return centred * scale, scale


def fold_lanes(values):
    return sum(values[:, t] for t in tiles(values.shape[1], LANES))


def forward_attention(index_ref, len_ref, tok_ref, seg_ref, *refs, pieces):
    cores = 2 if pieces > 1 else 1
    piece_refs = refs[:cores]
    (
        five_ref, mc_ref, v_ref, e_ref, facts_ref, packed_ref, w_ref,
        wt_ref, wide_ref, col_ref, key_mask_ref, query_mask_ref, key_ref, value_ref,
    ) = refs[cores:]
    x_ref, norm_ref, q_ref, k_ref, att_ref = [five_ref.at[:, i] for i in range(5)]
    aux_ref, inv_ref = facts_ref.at[:, :8], facts_ref.at[:, 8:]
    rows, seq, width = tok_ref.shape
    head = width // HEADS
    step = pl.program_id(0)

    @pl.when(step == 0)
    def _():
        own = width // pieces
        for i in range(pieces):
            here = pl.ds(pl.multiple_of(index_ref[i] * own, 16), own)
            wide_ref[here, :] = piece_refs[i % cores][i // cores * own : (i // cores + 1) * own]
        w_ref[...] = wide_ref[:, : 3 * width]
        wt_ref[...] = wide_ref[:, : 3 * width].T
        packed_ref[...] = wide_ref[:, 3 * width :]
        load_columns(packed_ref, col_ref, range(5))
        col_ref[1] = col_ref[1] + 1.0

    place = lax.broadcasted_iota(jnp.int32, (1, seq), 1)
    zero = jnp.zeros((head, seq), BF)

    def preparation(r):
        known = {}

        def start():
            segs = seg_ref[pl.ds(step * rows + r, 1), :].astype(F32)
            valid = place < len_ref[step * rows + r]
            number = jnp.where(valid, segs, -1.0)
            links = jnp.where(valid & (place > 0) & (number == pltpu.roll(number, 1, 1)), 1.0, 0.0)
            next_links = jnp.where(place < seq - 1, pltpu.roll(links, seq - 1, 1), 0.0)
            none = jnp.zeros_like(links)
            aux = jnp.concatenate([links, next_links, number, none, none, none, none, none], axis=0)
            aux_ref[r] = aux
            x_ref[r] = tok_ref[r].T
            known.update(segs=segs, links=links, next_links=next_links, key_number=aux.T[:, 2:3])

        def mask():
            number = known["key_number"]
            lane = lax.broadcasted_iota(jnp.int32, (seq, LANES), 1)
            itself = lax.broadcasted_iota(jnp.int32, (seq, LANES), 0) - (seq - LANES)
            chosen = (lane.astype(F32) == number) | ((number < 0.0) & (lane == itself))
            key_mask_ref[r] = jnp.where(chosen, 1.0, 0.0).astype(BF)
            slot = lax.broadcasted_iota(jnp.int32, (LANES, seq), 0)
            itself = lax.broadcasted_iota(jnp.int32, (LANES, seq), 1) - (seq - LANES)
            open_to = (slot.astype(F32) == known["segs"]) | ((slot >= LANES // 2) & (slot == itself))
            query_mask_ref[r] = jnp.where(open_to, 0.0, -1e30).astype(BF)

        def conv(t):
            base = x_ref[r, t].astype(F32)
            before = pltpu.roll(base, 1, 1) * known["links"]
            after = pltpu.roll(base, seq - 1, 1) * known["next_links"]
            conv0, conv1, conv2 = [twice(col_ref[i, t], seq) for i in range(3)]
            mc_ref[r, t] = before * conv0 + base * conv1 + after * conv2

        def norm(t):
            n, _ = norm_columns(mc_ref[r, :, t])
            norm_ref[r, :, t] = (n * col_ref[3] + col_ref[4]).astype(BF)

        pieces = [start] + [functools.partial(conv, t) for t in tiles(width, 32)]
        pieces += [functools.partial(norm, t) for t in tiles(seq, LANES)]
        return pieces + [mask]

    def project():
        normed = jnp.concatenate([norm_ref[r] for r in range(rows)], axis=1)
        for i, ref in enumerate((q_ref, k_ref, value_ref)):
            part = mm(wt_ref[i * width : (i + 1) * width], normed)
            part = (part * (head ** (-0.5) * math.log2(math.e)) if i == 0 else part).astype(BF)
            for r in range(rows):
                ref[r] = part[:, r * seq : (r + 1) * seq]
        for r in range(rows):
            key_ref[r] = k_ref[r].T
            v_ref[r] = value_ref[r].T

    def scores(r, p):
        low, high = [q_ref[r, h * head : (h + 1) * head] for h in (2 * p, 2 * p + 1)]
        both = jnp.concatenate([jnp.concatenate([low, zero], axis=1), jnp.concatenate([zero, high], axis=1)], axis=0)
        keys = jnp.concatenate([key_ref[r, :, 2 * p * head : 2 * (p + 1) * head], key_mask_ref[r]], axis=1)
        masks = jnp.concatenate([query_mask_ref[r], query_mask_ref[r]], axis=1)
        return mm(keys, jnp.concatenate([both, masks], axis=0))

    def attended(r, p):
        both = jnp.concatenate([e_ref[r, 2 * p], e_ref[r, 2 * p + 1]], axis=1)
        product = mm(value_ref[r, 2 * p * head : 2 * (p + 1) * head], both)
        parts = []
        for i in range(2):
            att = product[i * head : (i + 1) * head, i * seq : (i + 1) * seq] * inv_ref[r, 2 * p + i : 2 * p + i + 1]
            parts.append(att.astype(BF))
        return jnp.concatenate(parts, axis=0)

    def soften(r, p, product):
        for i in range(2):
            for t in tiles(seq, LANES):
                masked = product[:, i * seq + t.start : i * seq + t.stop]
                raised = jnp.exp2(masked - jnp.max(fold(masked, jnp.maximum), axis=0, keepdims=True))
                inv_ref[r, 2 * p + i : 2 * p + i + 1, t] = 1.0 / jnp.sum(fold(raised), axis=0, keepdims=True)
                e_ref[r, 2 * p + i, :, t] = raised.astype(BF)

    weave(*[preparation(r) for r in range(rows)])
    project()
    work = [(r, p) for r in range(rows) for p in range(HEADS // 2)]
    current, last = scores(*work[0]), None
    for at, (r, p) in enumerate(work):
        following = scores(*work[at + 1]) if at + 1 < len(work) else None
        finished = attended(*last) if last else None
        soften(r, p, current)
        if last:
            att_ref[last[0], 2 * last[1] * head : 2 * (last[1] + 1) * head] = finished
        current, last = following, (r, p)
    att_ref[last[0], 2 * last[1] * head : 2 * (last[1] + 1) * head] = attended(*last)


def gelu_parts(y):
    twice_cdf = lax.erf(y) + 1.0
    bell = jnp.exp2(y * y * -math.log2(math.e) + math.log2(2.0 / math.sqrt(math.pi)))
    return y * twice_cdf, twice_cdf + y * bell


def feed_forward(index_ref, five_ref, mc_ref, ct_ref, packed_ref, *refs, pieces, shards):
    att_ref = five_ref.at[:, 0]
    groups = 2 if pieces > 1 else 1
    piece_refs = refs[:groups]
    hidden_out, mixed_out, gm_ref, ga_ref, gs_ref, down_ref = refs[groups : groups + 6]
    gw_refs = refs[groups + 6 : 2 * groups + 6]
    (
        up_ref, upt_ref, downt_ref, out_ref, outt_ref, up_acc, down_acc, out_acc, col_acc, col_ref,
        n_ref, norm_ref, ctt_ref, gp_ref, gn_ref, scale_ref, branch_ref, hidden_ref, mixed_ref, sems,
    ) = refs[2 * groups + 6 :]
    rows, seq, width = ct_ref.shape
    ff = up_ref.shape[1]
    ffs = ff // shards
    own = width // pieces
    step = pl.program_id(0)

    @pl.when(step == 0)
    def _():
        for acc in (up_acc, down_acc, out_acc, col_acc):
            acc[...] = jnp.zeros_like(acc)
        for i in range(pieces):
            here = pl.ds(pl.multiple_of(index_ref[i] * own, 16), own)
            ref, first = piece_refs[i % groups], i // groups * (2 * shards + 1) * own
            for j in range(shards):
                at = first + 2 * j * own
                up_ref[here, j * ffs : (j + 1) * ffs] = ref[at : at + own]
                down_ref[here, j * ffs : (j + 1) * ffs] = ref[at + own : at + 2 * own]
            at = first + 2 * shards * own
            out_ref[here, :] = ref[at : at + own]
        upt_ref[...] = up_ref[...].T
        downt_ref[...] = down_ref[...].T
        outt_ref[...] = out_ref[...].T
        load_columns(packed_ref, col_ref, (5, 6, 5))
        for i, factor in enumerate((0.5, math.sqrt(0.5), math.sqrt(0.5))):
            col_ref[i] = col_ref[i] * factor

    def copies(at, g):
        place = at * pairs + g
        return [
            pltpu.make_async_copy(hidden_ref.at[g], hidden_out.at[place], sems.at[0, g]),
            pltpu.make_async_copy(mixed_ref.at[g], mixed_out.at[place], sems.at[1, g]),
        ]

    pairs = n_ref.shape[0]

    @pl.when(step > 0)
    def _():
        for g in range(pairs):
            for copy in copies(step - 1, g):
                copy.wait()

    def begin(g):
        pair = range(g * paired, (g + 1) * paired)
        attended = jnp.concatenate([att_ref[r] for r in pair], axis=1)
        branch = mm(outt_ref[...], attended)
        for i, r in enumerate(pair):
            lanes = slice(i * seq, (i + 1) * seq)
            ctt_ref[g, :, lanes] = ct_ref[r].T
            mixed_ref[g, :, lanes] = mc_ref[r] + branch[:, lanes]
        for t in spots:
            n, scale = norm_columns(mixed_ref[g, :, t])
            n_ref[g, :, t] = n
            scale_ref[g, 0:1, t] = scale
            norm_ref[g, :, t] = (n * col_ref[2] + col_ref[1]).astype(BF)

    def activate(g, block):
        pre = mm(upt_ref[block], norm_ref[g])
        grad_hidden = mm(downt_ref[block], ctt_ref[g])
        for low in range(0, block.stop - block.start, 16):
            part = slice(low, low + 16)
            here = slice(block.start + low, block.start + low + 16)
            hidden, slope = gelu_parts(pre[part])
            hidden_ref[g, here] = hidden.astype(BF)
            gp_ref[g, here] = (grad_hidden[part] * slope).astype(BF)

    def weigh(g):
        gn_ref[g] = mm(up_ref[...], gp_ref[g])
        down_acc[...] += mm_nt(ctt_ref[g], hidden_ref[g])
        up_acc[...] += mm_nt(norm_ref[g], gp_ref[g])

    def norm_back(g):
        mean_e = [jnp.zeros((8, LANES), F32) for _ in spots]
        mean_en = [jnp.zeros((8, LANES), F32) for _ in spots]
        for d in tiles(width, 32):
            column = col_ref[0, d]
            gain_sum, shift_sum = col_acc[0, d], col_acc[1, d]
            for i, t in enumerate(spots):
                grad_n = gn_ref[g, d, t]
                product = grad_n * n_ref[g, d, t]
                gain_sum += product
                shift_sum += grad_n
                mean_e[i] += fold(grad_n * column)
                mean_en[i] += fold(product * column)
            col_acc[0, d] = gain_sum
            col_acc[1, d] = shift_sum
        for i, t in enumerate(spots):
            me = jnp.sum(mean_e[i], axis=0, keepdims=True) * (1.0 / width)
            men = jnp.sum(mean_en[i], axis=0, keepdims=True) * (1.0 / width)
            row, inside = divmod(t.start, seq)
            for d in tiles(width, 32):
                change = scale_ref[g, 0:1, t] * (gn_ref[g, d, t] * col_ref[0, d] - me - n_ref[g, d, t] * men)
                grad_mixed = ctt_ref[g, d, t].astype(F32) + change
                gm_ref[g * paired + row, d, inside : inside + LANES] = grad_mixed
                branch_ref[g, d, t] = grad_mixed.astype(BF)

    def end(g):
        pair = range(g * paired, (g + 1) * paired)
        attended = jnp.concatenate([att_ref[r] for r in pair], axis=1)
        grad_attended = mm(out_ref[...], branch_ref[g]).astype(BF)
        for i, r in enumerate(pair):
            ga_ref[r] = grad_attended[:, i * seq : (i + 1) * seq]
        out_acc[...] += mm_nt(attended, branch_ref[g])

    paired = rows // pairs
    spots = tiles(paired * seq, LANES)
    begin(0)
    copies(step, 0)[1].start()
    for g in range(pairs):
        for block in tiles(ff, 128):
            activate(g, block)
        copies(step, g)[0].start()
        if g + 1 < pairs:
            begin(g + 1)
            copies(step, g + 1)[1].start()
        weigh(g)
        norm_back(g)
        end(g)

    @pl.when(step == pl.num_programs(0) - 1)
    def _():
        for g in range(pairs):
            for copy in copies(step, g):
                copy.wait()
        for i in range(pieces):
            here = pl.ds(pl.multiple_of(index_ref[i] * own, 16), own)
            place = gw_refs[i % groups]
            for j in range(shards):
                cols = slice(j * ffs, (j + 1) * ffs)
                place[i // groups, :, 2 * j * ffs : (2 * j + 1) * ffs] = (up_acc[here, cols] * math.sqrt(0.5)).astype(BF)
                place[i // groups, :, (2 * j + 1) * ffs : (2 * j + 2) * ffs] = (down_acc[here, cols] * math.sqrt(0.5)).astype(BF)
            place[i // groups, :, 2 * ff :] = out_acc[here, :].astype(BF)
        gs_ref[...] = jnp.zeros_like(gs_ref)
        for i in range(2):
            gs_ref[5 + i : 6 + i] = jnp.sum(col_acc[i].T, axis=0, keepdims=True) * 0.5


def layer_output(hidden_ref, mixed_ref, down_ref, lo_ref):
    rows, seq, _ = lo_ref.shape
    total = (mixed_ref[0] + mm(down_ref[...], hidden_ref[0]) * math.sqrt(0.5)).astype(BF)
    for r in range(rows):
        lo_ref[r] = total[:, r * seq : (r + 1) * seq].T


def backward(
    five_ref, mc_ref, v_ref, e_ref, facts_ref, ga_ref, gm_ref, index_ref, w_ref, packed_ref, other_ref, ig_ref, gs_ref, *refs, pieces,
):
    x_ref, norm_ref, q_ref, k_ref, att_ref = [five_ref.at[:, i] for i in range(5)]
    aux_ref, inv_ref = facts_ref.at[:, :8], facts_ref.at[:, 8:]
    gw_refs = refs[:-11]
    (
        proj_ref, w_acc, norm_cat, soft_ref, logit_ref, gn_ref, acc_ref, col_ref, n_ref, g_ref, turn_ref
    ) = refs[-11:]
    rows, seq, width = v_ref.shape
    own = width // pieces
    head = width // HEADS
    step = pl.program_id(0)

    @pl.when(step == 0)
    def _():
        w_acc[...] = jnp.zeros_like(w_acc)
        acc_ref[...] = jnp.zeros_like(acc_ref)
        load_columns(packed_ref, col_ref, range(4))
        col_ref[1] = col_ref[1] + 1.0

    zero = jnp.zeros((head, seq), BF)
    work = [(r, p) for r in range(rows) for p in range(HEADS // 2)]

    def opening(r, p):
        grads, inners = [], []
        for h in (2 * p, 2 * p + 1):
            part = slice(h * head, (h + 1) * head)
            grad_att = ga_ref[r, part].astype(F32) * inv_ref[r, h : h + 1]
            inners.append(jnp.sum(fold(grad_att * att_ref[r, part].astype(F32)), axis=0, keepdims=True))
            grads.append(grad_att.astype(BF))
        low, high = grads
        both = jnp.concatenate([jnp.concatenate([low, zero], axis=1), jnp.concatenate([zero, high], axis=1)], axis=0)
        product = mm(v_ref[r, :, 2 * p * head : 2 * (p + 1) * head], both)
        soft_ref[r, 2 * p] = product[:, :seq]
        soft_ref[r, 2 * p + 1] = product[:, seq:]
        return jnp.concatenate(grads, axis=0), inners

    spots = tiles(seq, LANES)

    def finish_row(r):
        wide = [slice(r * seq + t.start, r * seq + t.stop) for t in spots]
        lanes = slice(r * seq, (r + 1) * seq)
        norm_cat[:, lanes] = norm_ref[r]
        gn_ref[:, lanes] = mm(w_ref[...], proj_ref[:, lanes])
        scales = []
        for t in spots:
            n, scale = norm_columns(mc_ref[r, :, t])
            n_ref[r, :, t] = n
            scales.append(scale)
        mean_e = [jnp.zeros((8, LANES), F32) for _ in spots]
        mean_en = [jnp.zeros((8, LANES), F32) for _ in spots]
        for d in tiles(width, 32):
            column = col_ref[3, d]
            gain_sum, shift_sum = acc_ref[3, d], acc_ref[4, d]
            for i, t in enumerate(spots):
                grad_n = gn_ref[d, wide[i]]
                product = grad_n * n_ref[r, d, t]
                gain_sum += product
                shift_sum += grad_n
                mean_e[i] += fold(grad_n * column)
                mean_en[i] += fold(product * column)
            acc_ref[3, d] = gain_sum
            acc_ref[4, d] = shift_sum
        for i, t in enumerate(spots):
            me = jnp.sum(mean_e[i], axis=0, keepdims=True) * (1.0 / width)
            men = jnp.sum(mean_en[i], axis=0, keepdims=True) * (1.0 / width)
            for d in tiles(width, 64):
                e = gn_ref[d, wide[i]] * col_ref[3, d]
                g_ref[r, d, t] = gm_ref[r, d, t] + scales[i] * (e - me - n_ref[r, d, t] * men)
        links, next_links = aux_ref[r, 0:1], aux_ref[r, 1:2]
        for d in tiles(width, 32):
            g = g_ref[r, d]
            base = x_ref[r, d].astype(F32)
            before = pltpu.roll(g, 1, 1) * links
            after = pltpu.roll(g, seq - 1, 1) * next_links
            acc_ref[0, d] += fold_lanes(base * after)
            acc_ref[1, d] += fold_lanes(base * g)
            acc_ref[2, d] += fold_lanes(base * before)
            conv0, conv1, conv2 = [twice(col_ref[i, d], seq) for i in range(3)]
            turn_ref[r, d] = (conv1 * g + conv0 * after + conv2 * before).astype(BF)
        ig_ref[r] = turn_ref[r].T

    ready = opening(*work[0])
    for at, (r, p) in enumerate(work):
        grad_att, inners = ready
        if at + 1 < len(work):
            ready = opening(*work[at + 1])
        for i, h in enumerate((2 * p, 2 * p + 1)):
            for t in tiles(seq, 32):
                raised = e_ref[r, h, t].astype(F32)
                logit_ref[r, h, t] = (raised * (soft_ref[r, h, t] - inners[i])).astype(BF)
        place = slice(r * seq, (r + 1) * seq)
        for i, h in enumerate((2 * p, 2 * p + 1)):
            part = slice(h * head, (h + 1) * head)
            grad_q = mm(k_ref[r, part], logit_ref[r, h]) * head ** (-0.5)
            grad_k = mm_nt(q_ref[r, part], logit_ref[r, h]) * math.log(2.0)
            grad_v = mm_nt(grad_att[i * head : (i + 1) * head], e_ref[r, h])
            for j, grad in enumerate((grad_q, grad_k, grad_v)):
                proj_ref[j * width + h * head : j * width + (h + 1) * head, place] = grad.astype(BF)
        if p == HEADS // 2 - 1:
            finish_row(r)
    w_acc[...] += mm_nt(norm_cat[...], proj_ref[...])

    @pl.when(step == pl.num_programs(0) - 1)
    def _():
        gs_ref[...] = other_ref[...]
        for i in range(5):
            gs_ref[i : i + 1] += jnp.sum(acc_ref[i].T, axis=0, keepdims=True)
        groups = len(gw_refs)
        for i in range(pieces):
            here = pl.ds(pl.multiple_of(index_ref[i] * own, 16), own)
            gw_refs[i % groups][i // groups] = w_acc[here, :].astype(BF)


def in_hbm(values):
    return pltpu.with_memory_space_constraint(values, pltpu.HBM)


def by_row(shape, rows, first=0):
    tail = tuple(shape[1:])
    return pl.BlockSpec((rows,) + tail, lambda i, *_: (i + first,) + (0,) * len(tail))


def whole(shape):
    place = (0,) * len(shape)
    return pl.BlockSpec(tuple(shape), lambda i, *_: place, pipeline_mode=pl.Buffered(1))


def step_rows(count, most):
    return max(r for r in range(1, most + 1) if count % r == 0)


def call(body, name, scalars, rows, row_args, args, row_outs, outs, scratch, span=None, into=None, near=(), only=None, manual=()):
    first, count = span or (0, row_args[0].shape[0])
    skip = first // rows
    total = row_args[0].shape[0]

    def spec_of(shape):
        return by_row(shape, shape[0] * rows // total, skip)

    in_specs = [spec_of(a.shape) for a in row_args]
    if only:
        tail = row_args[0].shape[2:]
        in_specs[0] = pl.BlockSpec((rows, 1) + tail, lambda i, *_: (i, only) + (0,) * len(tail))
    in_specs += [whole(a.shape) for a in args]
    aliases = {}
    if into is not None:
        in_specs.append(pl.BlockSpec(memory_space=pl.ANY))
        aliases = {len(scalars) + len(in_specs) - 1: 0}
    spec = pltpu.PrefetchScalarGridSpec(
        num_scalar_prefetch=len(scalars),
        grid=(count // rows,),
        in_specs=in_specs,
        out_specs=[pl.BlockSpec(memory_space=pl.ANY) for _ in manual] + [spec_of(s) for s, _ in row_outs] + [whole(s) for s, _ in outs],
        scratch_shapes=[pltpu.VMEM(*s) if isinstance(s, tuple) else s for s in scratch],
    )
    return pl.pallas_call(
        body,
        grid_spec=spec,
        out_shape=[pltpu.HBM(s, t) for s, t in manual] + [(jax.ShapeDtypeStruct if "out" + str(i) in near else pltpu.HBM)(s, t) for i, (s, t) in enumerate(row_outs)]
        + [jax.ShapeDtypeStruct(s, t) for s, t in outs],
        input_output_aliases=aliases,
        compiler_params=pltpu.CompilerParams(dimension_semantics=("arbitrary",), vmem_limit_bytes=VMEM_LIMITS[name] * MIB),
        name=name,
    )(*scalars, *[a if i in near else in_hbm(a) for i, a in enumerate(row_args)], *args, *(() if into is None else (into,)))


def small_call(body, name, args, outs, scratch=()):
    return pl.pallas_call(
        body,
        out_shape=[jax.ShapeDtypeStruct(s, t) for s, t in outs],
        scratch_shapes=[pltpu.VMEM(s, t) for s, t in scratch],
        compiler_params=pltpu.CompilerParams(vmem_limit_bytes=16 * MIB),
        name=name,
    )(*args)


def run_forward(index, tokens, segment_ids, valid_len, pieces):
    count, seq, width = tokens.shape
    flipped = (count, width, seq)
    rows = step_rows(count, 3)
    row_outs = [
        ((count, 5, width, seq), BF), (flipped, F32), ((count, seq, width), BF),
        ((count, HEADS, seq, seq), BF), ((count, 16, seq), F32),
    ]
    return call(
        functools.partial(forward_attention, pieces=index.shape[0]), "forward_attention", (index, in_hbm(valid_len)),
        rows, (tokens,), (in_hbm(segment_ids), *pieces),
        row_outs, [((width, VECTORS), BF), ((width, 3 * width), BF)],
        [
            ((3 * width, width), BF), ((width, 3 * width + VECTORS), BF), ((5, width, LANES), F32),
            ((rows, seq, LANES), BF), ((rows, LANES, seq), BF), ((rows, seq, width), BF), ((rows, width, seq), BF),
        ],
    )


def run_feed_forward(index, five, mixed, cotangent, packed, pieces, shards):
    count, seq, width = cotangent.shape
    own = width // index.shape[0]
    ff = shards * width
    groups = 2 if index.shape[0] > 1 else 1
    paired = step_rows(count, 2)
    pairs = 2 if count // paired % 2 == 0 else 1
    rows = pairs * paired
    wide = paired * seq
    manual = [((count // paired, ff, wide), BF), ((count // paired, width, wide), F32)]
    row_outs = [((count, width, seq), F32), ((count, width, seq), BF)]
    grads = ((index.shape[0] // groups, own, 2 * ff + width), BF)
    return call(
        functools.partial(feed_forward, pieces=index.shape[0], shards=shards), "feed_forward", (index,),
        rows, (five, mixed, cotangent), (packed, *pieces),
        row_outs, [((8, width), F32), ((width, ff), BF)] + [grads] * groups,
        [((width, ff), BF)] + [((ff, width), BF)] * 2 + [((width, width), BF)] * 2
        + [((width, ff), F32)] * 2 + [((width, width), F32), ((2, width, LANES), F32), ((3, width, LANES), F32)]
        + [((pairs, width, wide), F32), ((pairs, width, wide), BF), ((pairs, width, wide), BF)]
        + [((pairs, ff, wide), BF)]
        + [((pairs, width, wide), F32), ((pairs, 8, wide), F32), ((pairs, width, wide), BF)]
        + [((pairs, ff, wide), BF), ((pairs, width, wide), F32), pltpu.SemaphoreType.DMA((2, pairs))],
        near=("out1",), only=4, manual=manual,
    )


def run_layer_output(hidden, mixed, down, shape, into, low, high):
    steps = hidden.shape[0]
    span = (int(low * steps), int(high * steps) - int(low * steps))

    def body(*refs):
        layer_output(*refs[:3], refs[-1])

    return call(body, "layer_output", (), 1, (hidden, mixed), (down,), [(shape, BF)], [], [], span=span, into=into)[0]


def run_backward(index, weight, kept, grads, packed, other, pieces):
    count, seq, width = kept[2].shape
    own = width // pieces
    groups = 2 if pieces > 1 else 1
    rows = step_rows(count, 3)
    row_args = (*kept, *grads)
    many = len(row_args)

    def body(index_ref, *refs):
        backward(*refs[:many], index_ref, *refs[many:], pieces=pieces)

    return call(
        body, "backward", (index,), rows, row_args, (weight, packed, other),
        [((count, seq, width), BF)], [((8, width), F32)] + [((pieces // groups, own, 3 * width), BF)] * groups,
        [
            ((3 * width, rows * seq), BF), ((width, 3 * width), F32), ((width, rows * seq), BF),
            ((rows, HEADS, seq, seq), F32), ((rows, HEADS, seq, seq), BF), ((width, rows * seq), F32),
            ((5, width, LANES), F32), ((4, width, LANES), F32), ((rows, width, seq), F32), ((rows, width, seq), F32),
            ((rows, width, seq), BF),
        ],
        near=(5,),
    )


def exchange(values, axis, offset):
    size = lax.axis_size(axis)
    return lax.ppermute(values, axis, [(i, i ^ offset) for i in range(size)])


def add_halves(mine, received):
    count, own, cols = mine.shape

    def body(mine_ref, received_ref, *out_refs):
        for i, ref in enumerate(out_refs):
            ref[...] = (mine_ref[i].astype(F32) + received_ref[i].astype(F32)).astype(BF)

    return small_call(body, "add_halves", (mine, received), [((own, cols), BF)] * count)


def add_wide(*items):
    return tree_sum(item.astype(F32) for item in items)


def store_high_low(ref, cols, values):
    high = values.astype(BF)
    low = (values - high.astype(F32)).astype(BF)
    ref[:, cols:] = jnp.concatenate([high, low, jnp.zeros((ref.shape[0] - 16, LANES), BF)], axis=0)


def load_high_low(ref, cols):
    both = ref[:16, cols:].astype(F32)
    return both[:8] + both[8:]


def add_halves_and_sums(index, mine, received, sums, received_sums):
    count, own, cols = mine.shape
    width = sums.shape[1]

    def body(index_ref, mine_ref, received_ref, sums_ref, received_sums_ref, *out_refs):
        total = sums_ref[...] + received_sums_ref[...]
        for i, ref in enumerate(out_refs):
            ref[:, :cols] = (mine_ref[i].astype(F32) + received_ref[i].astype(F32)).astype(BF)
            turned = pltpu.roll(total, lax.rem(width - index_ref[2 * i] * own, width), 1)[:, :LANES]
            store_high_low(ref, cols, turned)

    spec = pltpu.PrefetchScalarGridSpec(
        num_scalar_prefetch=1, grid=(1,),
        in_specs=[whole(a.shape) for a in (mine, received, sums, received_sums)],
        out_specs=[whole((own, cols + LANES))] * count,
    )
    return pl.pallas_call(
        body, grid_spec=spec, out_shape=[jax.ShapeDtypeStruct((own, cols + LANES), BF)] * count,
        compiler_params=pltpu.CompilerParams(vmem_limit_bytes=16 * MIB), name="add_halves_and_sums",
    )(index, mine, received, sums, received_sums)


def add_packed(name, items):
    cols = items[0].shape[1] - LANES

    def body(*refs):
        out_ref = refs[-1]
        out_ref[:, :cols] = tree_sum(ref[:, :cols].astype(F32) for ref in refs[:-1]).astype(BF)
        store_high_low(out_ref, cols, tree_sum(load_high_low(ref, cols) for ref in refs[:-1]))

    return small_call(body, name, items, [(items[0].shape, BF)])[0]


def add_last(items):
    own, cols = items[0].shape[0], items[0].shape[1] - LANES

    def body(*refs):
        ins, outs = refs[: len(items)], refs[len(items) :]
        outs[0][...] = tree_sum(ref[:, :cols].astype(F32) for ref in ins)
        vectors = tree_sum(load_high_low(ref, cols) for ref in ins)
        outs[1][...] = vectors[0:3, :own]
        for i in range(4):
            outs[2 + i][...] = vectors[3 + i : 4 + i, :own]

    return small_call(body, "add_last", items, [((own, cols), F32), ((3, own), F32)] + [((1, own), F32)] * 4)


def direct_plan(tokens, segment_ids, valid_len, qkv_weight, out_weight, up_weight, down_weight, conv_weight, vectors, cotangent):
    count, seq, width = tokens.shape
    own, ffs = up_weight.shape
    dp, mp = lax.axis_size("dp"), lax.axis_size("mp")
    me = lax.axis_index("dp")
    offsets = [2 * p for p in range(dp // 2)]
    index = jnp.stack([me ^ (p ^ c) for p in offsets for c in range(2)]).astype(jnp.int32)
    narrow, ff_own = small_call(
        pack_weights, "pack_weights",
        [in_hbm(a) for a in (qkv_weight, up_weight, down_weight, conv_weight, *[v.reshape(1, own) for v in vectors])],
        [((own, 3 * width + VECTORS), BF), ((2 * own, ffs), BF)], [((VECTORS, VECTORS), F32)],
    )
    shards = [ff_own] + [exchange(ff_own, "mp", j) for j in range(1, mp)]
    plane = jnp.concatenate([narrow] + [exchange(narrow, "dp", p) for p in offsets[1:]], axis=0)
    pieces = [plane, exchange(plane, "dp", 1)]
    column = jnp.concatenate(shards + [out_weight], axis=0)
    columns = [column] + [exchange(column, "dp", p) for p in offsets[1:]]
    five, mixed, v, raised, facts, packed, weight = run_forward(
        index, tokens, segment_ids, valid_len, pieces
    )
    columns, five = lax.optimization_barrier((columns, five))
    columns = jnp.concatenate(columns, axis=0)
    pieces = [columns, exchange(columns, "dp", 1)]
    hidden, mixed_attn, grad_mixed, grad_att, sums2, down, mine, theirs = run_feed_forward(
        index, five, mixed, cotangent, packed, pieces, mp
    )
    received = exchange(theirs, "dp", 1)
    shape = cotangent.shape
    layer_out = run_layer_output(hidden, mixed_attn, down, shape, None, 0, 0.17)
    received, layer_out = lax.optimization_barrier((received, layer_out))
    parts = list(add_halves(mine, received))
    parts[0], grad_att = lax.optimization_barrier((parts[0], grad_att))
    plane = [parts[0]] + [exchange(parts[i], "dp", p) for i, p in enumerate(offsets) if i]
    kept = (five, mixed, v, raised, facts)
    input_grad, sums, mine_a, theirs_a = run_backward(
        index, weight, kept, (grad_att, grad_mixed), packed, sums2, dp
    )
    plane, theirs_a, sums = lax.optimization_barrier((plane, theirs_a, sums))
    received_a = exchange(theirs_a, "dp", 1)
    received_s = exchange(sums, "dp", 1)
    total = add_wide(*plane).astype(BF)
    total, received_s = lax.optimization_barrier((total, received_s))
    part = 2 * ffs
    near = jnp.concatenate([total[:, :part], total[:, 2 * part : 3 * part]], axis=1)
    out_part = total[:, 4 * part :]
    far = jnp.concatenate([total[:, part : 2 * part], total[:, 3 * part :]], axis=1)
    parts = list(add_halves_and_sums(index, mine_a, received_a, sums, received_s))
    parts[0], hidden, layer_out = lax.optimization_barrier((parts[0], hidden, layer_out))
    plane_a = [parts[0]] + [exchange(parts[i], "dp", p) for i, p in enumerate(offsets) if i]
    received_f = exchange(far, "mp", 1)
    layer_out = run_layer_output(hidden, mixed_attn, down, shape, layer_out, 0.17, 0.51)
    plane_a, layer_out = lax.optimization_barrier((plane_a, layer_out))
    total = add_packed("add_plane", plane_a)
    received_1 = exchange(total, "mp", 1)
    received_f, _ = lax.optimization_barrier((received_f, total))
    near_sum = add_wide(near, received_f[:, : 2 * part])
    out_sum = lax.optimization_barrier(add_wide(out_part, received_f[:, 2 * part :]).astype(BF))
    keep = near_sum[:, :part]
    send = jnp.concatenate([near_sum[:, part:].astype(BF), out_sum], axis=1)
    received_n = exchange(send, "mp", 2)
    layer_out, _ = lax.optimization_barrier((layer_out, send))
    layer_out = run_layer_output(hidden, mixed_attn, down, shape, layer_out, 0.51, 0.67)
    received_1, layer_out = lax.optimization_barrier((received_1, layer_out))
    total = add_packed("add_near", (total, received_1))
    received_2 = exchange(total, "mp", 2)
    layer_out, _ = lax.optimization_barrier((layer_out, total))
    layer_out = run_layer_output(hidden, mixed_attn, down, shape, layer_out, 0.67, 1)
    received_n, layer_out = lax.optimization_barrier((received_n, layer_out))
    grad_up = keep[:, :ffs] + received_n[:, :ffs].astype(F32)
    grad_down = keep[:, ffs:] + received_n[:, ffs : 2 * ffs].astype(F32)
    grad_out = add_wide(out_sum, received_n[:, 2 * ffs :])
    grad_qkv, grad_conv, *grads = add_last((total, received_2))
    return (layer_out, input_grad, grad_qkv, grad_out, grad_up, grad_down, grad_conv, *[g.reshape(own) for g in grads])


def gathered_plan(tokens, segment_ids, valid_len, qkv_weight, out_weight, up_weight, down_weight, conv_weight, vectors, cotangent):
    count, seq, width = tokens.shape
    own = qkv_weight.shape[0]
    dp = width // own
    columns = jnp.stack([conv_weight[0], conv_weight[1], conv_weight[2], *vectors], axis=1)
    narrow = jnp.concatenate([qkv_weight, jnp.pad(columns, ((0, 0), (0, VECTORS - 7))), out_weight], axis=1)
    wide = lax.all_gather(narrow, "dp", axis=0, tiled=True)
    both = lax.all_gather(jnp.concatenate([up_weight, down_weight], axis=0), "mp", axis=1, tiled=True)
    ff = both.shape[1]
    shards = ff // width
    both = lax.all_gather(both, "dp", axis=0).reshape(dp, 2, own, shards, width)
    both = both.transpose(3, 1, 0, 2, 4).reshape(2 * ff, width)
    column = jnp.concatenate([both, wide[:, 3 * width + VECTORS :]], axis=0)
    index = jnp.zeros((1,), jnp.int32)
    five, mixed, v, raised, facts, packed, weight = run_forward(
        index, tokens, segment_ids, valid_len, [wide[:, : 3 * width + VECTORS]]
    )
    hidden, mixed_attn, grad_mixed, grad_att, sums2, down, grads = run_feed_forward(
        index, five, mixed, cotangent, packed, [column], shards
    )
    kept = (five, mixed, v, raised, facts)
    layer_out = run_layer_output(hidden, mixed_attn, down, cotangent.shape, None, 0, 1)
    input_grad, sums, grad_qkv = run_backward(index, weight, kept, (grad_att, grad_mixed), packed, sums2, 1)
    grad_ff = grads[0, :, : 2 * ff].reshape(width, shards, 2, width).transpose(0, 2, 1, 3).reshape(width, 2 * ff)
    grad_ff = lax.psum_scatter(grad_ff, "dp", scatter_dimension=0, tiled=True).reshape(own, 2, ff)
    grad_ff = lax.psum_scatter(grad_ff, "mp", scatter_dimension=2, tiled=True).astype(F32)
    grad_attn = jnp.concatenate([grad_qkv[0], grads[0, :, 2 * ff :]], axis=1)
    grad_attn = lax.psum_scatter(grad_attn, "dp", scatter_dimension=0, tiled=True)
    grad_attn = lax.psum(grad_attn, "mp").astype(F32)
    sums = lax.psum(sums, ("dp", "mp"))
    sums = lax.dynamic_slice_in_dim(sums, lax.axis_index("dp") * own, own, axis=1)
    return (
        layer_out, input_grad, grad_attn[:, : 3 * width], grad_attn[:, 3 * width :],
        grad_ff[:, 0], grad_ff[:, 1], sums[0:3], sums[3], sums[4], sums[5], sums[6],
    )


def on_device(
    tokens, segment_ids, valid_len, qkv_weight, out_weight, up_weight, down_weight, conv_weight,
    ln1_gain, ln1_shift, ln2_gain, ln2_shift, cotangent,
):
    own, ffs = up_weight.shape
    direct = own % 16 == 0 and ffs == tokens.shape[2] and own <= VECTORS and lax.axis_size("mp") == 4
    plan = direct_plan if direct else gathered_plan
    return plan(
        tokens, segment_ids, valid_len, qkv_weight, out_weight, up_weight, down_weight, conv_weight,
        (ln1_gain, ln1_shift, ln2_gain, ln2_shift), cotangent,
    )


def solution(mesh):
    rows = P(("dp", "mp"), None, None)
    weights = (P("dp", None), P("dp", None), P("dp", "mp"), P("dp", "mp"), P(None, "dp"))
    vectors = (P("dp"),) * 4
    return jax.shard_map(
        on_device,
        mesh=mesh,
        in_specs=(rows, P(("dp", "mp"), None), P(("dp", "mp"))) + weights + vectors + (rows,),
        out_specs=(rows, rows) + weights + vectors,
        check_vma=False,
    )
```

```python
import functools
import math

import jax
import jax.numpy as jnp
from jax import lax
from jax.experimental import pallas as pl
from jax.experimental.pallas import tpu as pltpu
from jax.sharding import PartitionSpec as P

HEADS = 6
VECTORS = 128
LANES = 128
BF = jnp.bfloat16
F32 = jnp.float32
MIB = 1024 * 1024
VMEM_LIMITS = dict(forward_attention=32, feed_forward=44, backward=42, layer_output=16)


def mm(lhs, rhs):
    return lax.dot_general(lhs, rhs, (((1,), (0,)), ((), ())), preferred_element_type=F32)


def mm_nt(lhs, rhs):
    return lax.dot_general(lhs, rhs, (((1,), (1,)), ((), ())), preferred_element_type=F32)


def tree_sum(items):
    items = list(items)
    while len(items) > 1:
        items = [a + b for a, b in zip(items[::2], items[1::2])]
    return items[0]


def pack_weights(qkv_ref, up_ref, down_ref, conv_ref, g1_ref, s1_ref, g2_ref, s2_ref, narrow_ref, ff_ref, rows_ref):
    own, ffs = up_ref.shape
    rows_ref[...] = jnp.zeros_like(rows_ref)
    rows_ref[0:3, :own] = conv_ref[...].astype(F32)
    for i, ref in enumerate((g1_ref, s1_ref, g2_ref, s2_ref)):
        rows_ref[3 + i : 4 + i, :own] = ref[...].astype(F32)
    wide = qkv_ref.shape[1]
    narrow_ref[:, :wide] = qkv_ref[...]
    narrow_ref[:, wide:] = rows_ref[...].T[:own].astype(BF)
    ff_ref[:own] = up_ref[...]
    ff_ref[own:] = down_ref[...]


def tiles(total, size):
    return [slice(at, at + size) for at in range(0, total, size)]


def weave(*strands):
    strands = [strand for strand in strands if strand]
    total = sum(len(strand) for strand in strands)
    pieces = [((i + 0.5) / len(strand), j, piece) for j, strand in enumerate(strands) for i, piece in enumerate(strand)]
    assert len(pieces) == total
    for _, _, piece in sorted(pieces, key=lambda item: item[:2]):
        piece()


def twice(tile, lanes):
    return jnp.concatenate([tile] * (lanes // LANES), axis=1)


def load_columns(packed_ref, col_ref, places):
    for i, place in enumerate(places):
        column = packed_ref[:, place : place + 1].astype(F32)
        col_ref[i] = jnp.broadcast_to(column, (column.shape[0], LANES))


def pairwise(items, combine):
    items = list(items)
    while len(items) > 1:
        odd = items[len(items) // 2 * 2 :]
        items = [combine(a, b) for a, b in zip(items[::2], items[1::2])] + odd
    return items[0]


def fold(values, combine=jnp.add):
    return pairwise([values[t] for t in tiles(values.shape[0], 8)], combine)


def column_mean(values):
    return jnp.sum(fold(values), axis=0, keepdims=True) * (1.0 / values.shape[0])


def norm_columns(values):
    centred = values - column_mean(values)
    scale = lax.rsqrt(column_mean(centred * centred) + 1e-06)
    return centred * scale, scale


def fold_lanes(values):
    return sum(values[:, t] for t in tiles(values.shape[1], LANES))


def forward_attention(index_ref, len_ref, tok_ref, seg_ref, *refs, pieces):
    cores = 2 if pieces > 1 else 1
    piece_refs = refs[:cores]
    (
        five_ref, mc_ref, v_ref, e_ref, facts_ref, packed_ref, w_ref,
        wt_ref, wide_ref, col_ref, key_mask_ref, query_mask_ref, key_ref, value_ref,
    ) = refs[cores:]
    x_ref, norm_ref, q_ref, k_ref, att_ref = [five_ref.at[:, i] for i in range(5)]
    aux_ref, inv_ref = facts_ref.at[:, :8], facts_ref.at[:, 8:]
    rows, seq, width = tok_ref.shape
    head = width // HEADS
    step = pl.program_id(0)

    @pl.when(step == 0)
    def _():
        own = width // pieces
        for i in range(pieces):
            here = pl.ds(pl.multiple_of(index_ref[i] * own, 16), own)
            wide_ref[here, :] = piece_refs[i % cores][i // cores * own : (i // cores + 1) * own]
        w_ref[...] = wide_ref[:, : 3 * width]
        wt_ref[...] = wide_ref[:, : 3 * width].T
        packed_ref[...] = wide_ref[:, 3 * width :]
        load_columns(packed_ref, col_ref, range(5))
        col_ref[1] = col_ref[1] + 1.0

    place = lax.broadcasted_iota(jnp.int32, (1, seq), 1)
    zero = jnp.zeros((head, seq), BF)

    def preparation(r):
        known = {}

        def start():
            segs = seg_ref[pl.ds(step * rows + r, 1), :].astype(F32)
            valid = place < len_ref[step * rows + r]
            number = jnp.where(valid, segs, -1.0)
            links = jnp.where(valid & (place > 0) & (number == pltpu.roll(number, 1, 1)), 1.0, 0.0)
            next_links = jnp.where(place < seq - 1, pltpu.roll(links, seq - 1, 1), 0.0)
            none = jnp.zeros_like(links)
            aux = jnp.concatenate([links, next_links, number, none, none, none, none, none], axis=0)
            aux_ref[r] = aux
            x_ref[r] = tok_ref[r].T
            known.update(segs=segs, links=links, next_links=next_links, key_number=aux.T[:, 2:3])

        def mask():
            number = known["key_number"]
            lane = lax.broadcasted_iota(jnp.int32, (seq, LANES), 1)
            itself = lax.broadcasted_iota(jnp.int32, (seq, LANES), 0) - (seq - LANES)
            chosen = (lane.astype(F32) == number) | ((number < 0.0) & (lane == itself))
            key_mask_ref[r] = jnp.where(chosen, 1.0, 0.0).astype(BF)
            slot = lax.broadcasted_iota(jnp.int32, (LANES, seq), 0)
            itself = lax.broadcasted_iota(jnp.int32, (LANES, seq), 1) - (seq - LANES)
            open_to = (slot.astype(F32) == known["segs"]) | ((slot >= LANES // 2) & (slot == itself))
            query_mask_ref[r] = jnp.where(open_to, 0.0, -1e30).astype(BF)

        def conv(t):
            base = x_ref[r, t].astype(F32)
            before = pltpu.roll(base, 1, 1) * known["links"]
            after = pltpu.roll(base, seq - 1, 1) * known["next_links"]
            conv0, conv1, conv2 = [twice(col_ref[i, t], seq) for i in range(3)]
            mc_ref[r, t] = before * conv0 + base * conv1 + after * conv2

        def norm(t):
            n, _ = norm_columns(mc_ref[r, :, t])
            norm_ref[r, :, t] = (n * col_ref[3] + col_ref[4]).astype(BF)

        pieces = [start] + [functools.partial(conv, t) for t in tiles(width, 32)]
        pieces += [functools.partial(norm, t) for t in tiles(seq, LANES)]
        return pieces + [mask]

    def project():
        normed = jnp.concatenate([norm_ref[r] for r in range(rows)], axis=1)
        for i, ref in enumerate((q_ref, k_ref, value_ref)):
            part = mm(wt_ref[i * width : (i + 1) * width], normed)
            part = (part * (head ** (-0.5) * math.log2(math.e)) if i == 0 else part).astype(BF)
            for r in range(rows):
                ref[r] = part[:, r * seq : (r + 1) * seq]
        for r in range(rows):
            key_ref[r] = k_ref[r].T
            v_ref[r] = value_ref[r].T

    def scores(r, p):
        low, high = [q_ref[r, h * head : (h + 1) * head] for h in (2 * p, 2 * p + 1)]
        both = jnp.concatenate([jnp.concatenate([low, zero], axis=1), jnp.concatenate([zero, high], axis=1)], axis=0)
        keys = jnp.concatenate([key_ref[r, :, 2 * p * head : 2 * (p + 1) * head], key_mask_ref[r]], axis=1)
        masks = jnp.concatenate([query_mask_ref[r], query_mask_ref[r]], axis=1)
        return mm(keys, jnp.concatenate([both, masks], axis=0))

    def attended(r, p):
        both = jnp.concatenate([e_ref[r, 2 * p], e_ref[r, 2 * p + 1]], axis=1)
        product = mm(value_ref[r, 2 * p * head : 2 * (p + 1) * head], both)
        parts = []
        for i in range(2):
            att = product[i * head : (i + 1) * head, i * seq : (i + 1) * seq] * inv_ref[r, 2 * p + i : 2 * p + i + 1]
            parts.append(att.astype(BF))
        return jnp.concatenate(parts, axis=0)

    def soften(r, p, product):
        for i in range(2):
            for t in tiles(seq, LANES):
                masked = product[:, i * seq + t.start : i * seq + t.stop]
                raised = jnp.exp2(masked - jnp.max(fold(masked, jnp.maximum), axis=0, keepdims=True))
                inv_ref[r, 2 * p + i : 2 * p + i + 1, t] = 1.0 / jnp.sum(fold(raised), axis=0, keepdims=True)
                e_ref[r, 2 * p + i, :, t] = raised.astype(BF)

    weave(*[preparation(r) for r in range(rows)])
    project()
    work = [(r, p) for r in range(rows) for p in range(HEADS // 2)]
    current, last = scores(*work[0]), None
    for at, (r, p) in enumerate(work):
        following = scores(*work[at + 1]) if at + 1 < len(work) else None
        finished = attended(*last) if last else None
        soften(r, p, current)
        if last:
            att_ref[last[0], 2 * last[1] * head : 2 * (last[1] + 1) * head] = finished
        current, last = following, (r, p)
    att_ref[last[0], 2 * last[1] * head : 2 * (last[1] + 1) * head] = attended(*last)


def gelu_parts(y):
    twice_cdf = lax.erf(y) + 1.0
    bell = jnp.exp2(y * y * -math.log2(math.e) + math.log2(2.0 / math.sqrt(math.pi)))
    return y * twice_cdf, twice_cdf + y * bell


def feed_forward(index_ref, five_ref, mc_ref, ct_ref, packed_ref, *refs, pieces, shards):
    att_ref = five_ref.at[:, 0]
    groups = 2 if pieces > 1 else 1
    piece_refs = refs[:groups]
    hidden_out, mixed_out, gm_ref, ga_ref, gs_ref, down_ref = refs[groups : groups + 6]
    gw_refs = refs[groups + 6 : 2 * groups + 6]
    (
        up_ref, upt_ref, downt_ref, out_ref, outt_ref, up_acc, down_acc, out_acc, col_acc, col_ref,
        n_ref, norm_ref, ctt_ref, gp_ref, gn_ref, scale_ref, branch_ref, hidden_ref, mixed_ref, sems,
    ) = refs[2 * groups + 6 :]
    rows, seq, width = ct_ref.shape
    ff = up_ref.shape[1]
    ffs = ff // shards
    own = width // pieces
    step = pl.program_id(0)

    @pl.when(step == 0)
    def _():
        for acc in (up_acc, down_acc, out_acc, col_acc):
            acc[...] = jnp.zeros_like(acc)
        for i in range(pieces):
            here = pl.ds(pl.multiple_of(index_ref[i] * own, 16), own)
            ref, first = piece_refs[i % groups], i // groups * (2 * shards + 1) * own
            for j in range(shards):
                at = first + 2 * j * own
                up_ref[here, j * ffs : (j + 1) * ffs] = ref[at : at + own]
                down_ref[here, j * ffs : (j + 1) * ffs] = ref[at + own : at + 2 * own]
            at = first + 2 * shards * own
            out_ref[here, :] = ref[at : at + own]
        upt_ref[...] = up_ref[...].T
        downt_ref[...] = down_ref[...].T
        outt_ref[...] = out_ref[...].T
        load_columns(packed_ref, col_ref, (5, 6, 5))
        for i, factor in enumerate((0.5, math.sqrt(0.5), math.sqrt(0.5))):
            col_ref[i] = col_ref[i] * factor

    def copies(at, g):
        place = at * pairs + g
        return [
            pltpu.make_async_copy(hidden_ref.at[g], hidden_out.at[place], sems.at[0, g]),
            pltpu.make_async_copy(mixed_ref.at[g], mixed_out.at[place], sems.at[1, g]),
        ]

    pairs = n_ref.shape[0]

    @pl.when(step > 0)
    def _():
        for g in range(pairs):
            for copy in copies(step - 1, g):
                copy.wait()

    def begin(g):
        pair = range(g * paired, (g + 1) * paired)
        attended = jnp.concatenate([att_ref[r] for r in pair], axis=1)
        branch = mm(outt_ref[...], attended)
        for i, r in enumerate(pair):
            lanes = slice(i * seq, (i + 1) * seq)
            ctt_ref[g, :, lanes] = ct_ref[r].T
            mixed_ref[g, :, lanes] = mc_ref[r] + branch[:, lanes]
        for t in spots:
            n, scale = norm_columns(mixed_ref[g, :, t])
            n_ref[g, :, t] = n
            scale_ref[g, 0:1, t] = scale
            norm_ref[g, :, t] = (n * col_ref[2] + col_ref[1]).astype(BF)

    def activate(g, block):
        pre = mm(upt_ref[block], norm_ref[g])
        grad_hidden = mm(downt_ref[block], ctt_ref[g])
        for low in range(0, block.stop - block.start, 16):
            part = slice(low, low + 16)
            here = slice(block.start + low, block.start + low + 16)
            hidden, slope = gelu_parts(pre[part])
            hidden_ref[g, here] = hidden.astype(BF)
            gp_ref[g, here] = (grad_hidden[part] * slope).astype(BF)

    def weigh(g):
        gn_ref[g] = mm(up_ref[...], gp_ref[g])
        down_acc[...] += mm_nt(ctt_ref[g], hidden_ref[g])
        up_acc[...] += mm_nt(norm_ref[g], gp_ref[g])

    def norm_back(g):
        mean_e = [jnp.zeros((8, LANES), F32) for _ in spots]
        mean_en = [jnp.zeros((8, LANES), F32) for _ in spots]
        for d in tiles(width, 32):
            column = col_ref[0, d]
            gain_sum, shift_sum = col_acc[0, d], col_acc[1, d]
            for i, t in enumerate(spots):
                grad_n = gn_ref[g, d, t]
                product = grad_n * n_ref[g, d, t]
                gain_sum += product
                shift_sum += grad_n
                mean_e[i] += fold(grad_n * column)
                mean_en[i] += fold(product * column)
            col_acc[0, d] = gain_sum
            col_acc[1, d] = shift_sum
        for i, t in enumerate(spots):
            me = jnp.sum(mean_e[i], axis=0, keepdims=True) * (1.0 / width)
            men = jnp.sum(mean_en[i], axis=0, keepdims=True) * (1.0 / width)
            row, inside = divmod(t.start, seq)
            for d in tiles(width, 32):
                change = scale_ref[g, 0:1, t] * (gn_ref[g, d, t] * col_ref[0, d] - me - n_ref[g, d, t] * men)
                grad_mixed = ctt_ref[g, d, t].astype(F32) + change
                gm_ref[g * paired + row, d, inside : inside + LANES] = grad_mixed
                branch_ref[g, d, t] = grad_mixed.astype(BF)

    def end(g):
        pair = range(g * paired, (g + 1) * paired)
        attended = jnp.concatenate([att_ref[r] for r in pair], axis=1)
        grad_attended = mm(out_ref[...], branch_ref[g]).astype(BF)
        for i, r in enumerate(pair):
            ga_ref[r] = grad_attended[:, i * seq : (i + 1) * seq]
        out_acc[...] += mm_nt(attended, branch_ref[g])

    paired = rows // pairs
    spots = tiles(paired * seq, LANES)
    begin(0)
    copies(step, 0)[1].start()
    for g in range(pairs):
        for block in tiles(ff, 128):
            activate(g, block)
        copies(step, g)[0].start()
        if g + 1 < pairs:
            begin(g + 1)
            copies(step, g + 1)[1].start()
        weigh(g)
        norm_back(g)
        end(g)

    @pl.when(step == pl.num_programs(0) - 1)
    def _():
        for g in range(pairs):
            for copy in copies(step, g):
                copy.wait()
        for i in range(pieces):
            here = pl.ds(pl.multiple_of(index_ref[i] * own, 16), own)
            place = gw_refs[i % groups]
            for j in range(shards):
                cols = slice(j * ffs, (j + 1) * ffs)
                place[i // groups, :, 2 * j * ffs : (2 * j + 1) * ffs] = (up_acc[here, cols] * math.sqrt(0.5)).astype(BF)
                place[i // groups, :, (2 * j + 1) * ffs : (2 * j + 2) * ffs] = (down_acc[here, cols] * math.sqrt(0.5)).astype(BF)
            place[i // groups, :, 2 * ff :] = out_acc[here, :].astype(BF)
        gs_ref[...] = jnp.zeros_like(gs_ref)
        for i in range(2):
            gs_ref[5 + i : 6 + i] = jnp.sum(col_acc[i].T, axis=0, keepdims=True) * 0.5


def layer_output(hidden_ref, mixed_ref, down_ref, lo_ref):
    rows, seq, _ = lo_ref.shape
    total = (mixed_ref[0] + mm(down_ref[...], hidden_ref[0]) * math.sqrt(0.5)).astype(BF)
    for r in range(rows):
        lo_ref[r] = total[:, r * seq : (r + 1) * seq].T


def backward(
    five_ref, mc_ref, v_ref, e_ref, facts_ref, ga_ref, gm_ref, index_ref, w_ref, packed_ref, other_ref, ig_ref, gs_ref, *refs, pieces,
):
    x_ref, norm_ref, q_ref, k_ref, att_ref = [five_ref.at[:, i] for i in range(5)]
    aux_ref, inv_ref = facts_ref.at[:, :8], facts_ref.at[:, 8:]
    gw_refs = refs[:-11]
    (
        proj_ref, w_acc, norm_cat, soft_ref, logit_ref, gn_ref, acc_ref, col_ref, n_ref, g_ref, turn_ref
    ) = refs[-11:]
    rows, seq, width = v_ref.shape
    own = width // pieces
    head = width // HEADS
    step = pl.program_id(0)

    @pl.when(step == 0)
    def _():
        w_acc[...] = jnp.zeros_like(w_acc)
        acc_ref[...] = jnp.zeros_like(acc_ref)
        load_columns(packed_ref, col_ref, range(4))
        col_ref[1] = col_ref[1] + 1.0

    zero = jnp.zeros((head, seq), BF)
    work = [(r, p) for r in range(rows) for p in range(HEADS // 2)]

    def opening(r, p):
        grads, inners = [], []
        for h in (2 * p, 2 * p + 1):
            part = slice(h * head, (h + 1) * head)
            grad_att = ga_ref[r, part].astype(F32) * inv_ref[r, h : h + 1]
            inners.append(jnp.sum(fold(grad_att * att_ref[r, part].astype(F32)), axis=0, keepdims=True))
            grads.append(grad_att.astype(BF))
        low, high = grads
        both = jnp.concatenate([jnp.concatenate([low, zero], axis=1), jnp.concatenate([zero, high], axis=1)], axis=0)
        product = mm(v_ref[r, :, 2 * p * head : 2 * (p + 1) * head], both)
        soft_ref[r, 2 * p] = product[:, :seq]
        soft_ref[r, 2 * p + 1] = product[:, seq:]
        return jnp.concatenate(grads, axis=0), inners

    spots = tiles(seq, LANES)

    def finish_row(r):
        wide = [slice(r * seq + t.start, r * seq + t.stop) for t in spots]
        lanes = slice(r * seq, (r + 1) * seq)
        norm_cat[:, lanes] = norm_ref[r]
        gn_ref[:, lanes] = mm(w_ref[...], proj_ref[:, lanes])
        scales = []
        for t in spots:
            n, scale = norm_columns(mc_ref[r, :, t])
            n_ref[r, :, t] = n
            scales.append(scale)
        mean_e = [jnp.zeros((8, LANES), F32) for _ in spots]
        mean_en = [jnp.zeros((8, LANES), F32) for _ in spots]
        for d in tiles(width, 32):
            column = col_ref[3, d]
            gain_sum, shift_sum = acc_ref[3, d], acc_ref[4, d]
            for i, t in enumerate(spots):
                grad_n = gn_ref[d, wide[i]]
                product = grad_n * n_ref[r, d, t]
                gain_sum += product
                shift_sum += grad_n
                mean_e[i] += fold(grad_n * column)
                mean_en[i] += fold(product * column)
            acc_ref[3, d] = gain_sum
            acc_ref[4, d] = shift_sum
        for i, t in enumerate(spots):
            me = jnp.sum(mean_e[i], axis=0, keepdims=True) * (1.0 / width)
            men = jnp.sum(mean_en[i], axis=0, keepdims=True) * (1.0 / width)
            for d in tiles(width, 64):
                e = gn_ref[d, wide[i]] * col_ref[3, d]
                g_ref[r, d, t] = gm_ref[r, d, t] + scales[i] * (e - me - n_ref[r, d, t] * men)
        links, next_links = aux_ref[r, 0:1], aux_ref[r, 1:2]
        for d in tiles(width, 32):
            g = g_ref[r, d]
            base = x_ref[r, d].astype(F32)
            before = pltpu.roll(g, 1, 1) * links
            after = pltpu.roll(g, seq - 1, 1) * next_links
            acc_ref[0, d] += fold_lanes(base * after)
            acc_ref[1, d] += fold_lanes(base * g)
            acc_ref[2, d] += fold_lanes(base * before)
            conv0, conv1, conv2 = [twice(col_ref[i, d], seq) for i in range(3)]
            turn_ref[r, d] = (conv1 * g + conv0 * after + conv2 * before).astype(BF)
        ig_ref[r] = turn_ref[r].T

    ready = opening(*work[0])
    for at, (r, p) in enumerate(work):
        grad_att, inners = ready
        if at + 1 < len(work):
            ready = opening(*work[at + 1])
        for i, h in enumerate((2 * p, 2 * p + 1)):
            for t in tiles(seq, 32):
                raised = e_ref[r, h, t].astype(F32)
                logit_ref[r, h, t] = (raised * (soft_ref[r, h, t] - inners[i])).astype(BF)
        place = slice(r * seq, (r + 1) * seq)
        for i, h in enumerate((2 * p, 2 * p + 1)):
            part = slice(h * head, (h + 1) * head)
            grad_q = mm(k_ref[r, part], logit_ref[r, h]) * head ** (-0.5)
            grad_k = mm_nt(q_ref[r, part], logit_ref[r, h]) * math.log(2.0)
            grad_v = mm_nt(grad_att[i * head : (i + 1) * head], e_ref[r, h])
            for j, grad in enumerate((grad_q, grad_k, grad_v)):
                proj_ref[j * width + h * head : j * width + (h + 1) * head, place] = grad.astype(BF)
        if p == HEADS // 2 - 1:
            finish_row(r)
    w_acc[...] += mm_nt(norm_cat[...], proj_ref[...])

    @pl.when(step == pl.num_programs(0) - 1)
    def _():
        gs_ref[...] = other_ref[...]
        for i in range(5):
            gs_ref[i : i + 1] += jnp.sum(acc_ref[i].T, axis=0, keepdims=True)
        groups = len(gw_refs)
        for i in range(pieces):
            here = pl.ds(pl.multiple_of(index_ref[i] * own, 16), own)
            gw_refs[i % groups][i // groups] = w_acc[here, :].astype(BF)


def in_hbm(values):
    return pltpu.with_memory_space_constraint(values, pltpu.HBM)


def in_vmem(values):
    return pltpu.with_memory_space_constraint(values, pltpu.VMEM)


def by_row(shape, rows, first=0):
    tail = tuple(shape[1:])
    return pl.BlockSpec((rows,) + tail, lambda i, *_: (i + first,) + (0,) * len(tail))


def whole(shape):
    place = (0,) * len(shape)
    return pl.BlockSpec(tuple(shape), lambda i, *_: place, pipeline_mode=pl.Buffered(1))


def step_rows(count, most):
    return max(r for r in range(1, most + 1) if count % r == 0)


def call(body, name, scalars, rows, row_args, args, row_outs, outs, scratch, span=None, into=None, near=(), only=None, manual=()):
    first, count = span or (0, row_args[0].shape[0])
    skip = first // rows
    total = row_args[0].shape[0]

    def spec_of(shape):
        return by_row(shape, shape[0] * rows // total, skip)

    in_specs = [spec_of(a.shape) for a in row_args]
    if only:
        tail = row_args[0].shape[2:]
        in_specs[0] = pl.BlockSpec((rows, 1) + tail, lambda i, *_: (i, only) + (0,) * len(tail))
    in_specs += [whole(a.shape) if a.dtype == jnp.int32 else pl.BlockSpec(memory_space=pltpu.VMEM) for a in args]
    aliases = {}
    if into is not None:
        in_specs.append(pl.BlockSpec(memory_space=pl.ANY))
        aliases = {len(scalars) + len(in_specs) - 1: 0}
    spec = pltpu.PrefetchScalarGridSpec(
        num_scalar_prefetch=len(scalars),
        grid=(count // rows,),
        in_specs=in_specs,
        out_specs=[pl.BlockSpec(memory_space=pl.ANY) for _ in manual] + [spec_of(s) for s, _ in row_outs] + [whole(s) for s, _ in outs],
        scratch_shapes=[pltpu.VMEM(*s) if isinstance(s, tuple) else s for s in scratch],
    )
    return pl.pallas_call(
        body,
        grid_spec=spec,
        out_shape=[pltpu.HBM(s, t) for s, t in manual] + [(jax.ShapeDtypeStruct if "out" + str(i) in near else pltpu.HBM)(s, t) for i, (s, t) in enumerate(row_outs)]
        + [jax.ShapeDtypeStruct(s, t) for s, t in outs],
        input_output_aliases=aliases,
        compiler_params=pltpu.CompilerParams(dimension_semantics=("arbitrary",), vmem_limit_bytes=VMEM_LIMITS[name] * MIB),
        name=name,
    )(*scalars, *[a if i in near else in_hbm(a) for i, a in enumerate(row_args)], *[in_hbm(a) if a.dtype == jnp.int32 else in_vmem(a) for a in args], *(() if into is None else (into,)))


def small_call(body, name, args, outs, scratch=()):
    return pl.pallas_call(
        body,
        out_shape=[jax.ShapeDtypeStruct(s, t) for s, t in outs],
        scratch_shapes=[pltpu.VMEM(s, t) for s, t in scratch],
        compiler_params=pltpu.CompilerParams(vmem_limit_bytes=16 * MIB),
        name=name,
    )(*args)


def run_forward(index, tokens, segment_ids, valid_len, pieces):
    count, seq, width = tokens.shape
    flipped = (count, width, seq)
    rows = step_rows(count, 3)
    row_outs = [
        ((count, 5, width, seq), BF), (flipped, F32), ((count, seq, width), BF),
        ((count, HEADS, seq, seq), BF), ((count, 16, seq), F32),
    ]
    return call(
        functools.partial(forward_attention, pieces=index.shape[0]), "forward_attention", (index, in_hbm(valid_len)),
        rows, (tokens,), (segment_ids, *pieces),
        row_outs, [((width, VECTORS), BF), ((width, 3 * width), BF)],
        [
            ((3 * width, width), BF), ((width, 3 * width + VECTORS), BF), ((5, width, LANES), F32),
            ((rows, seq, LANES), BF), ((rows, LANES, seq), BF), ((rows, seq, width), BF), ((rows, width, seq), BF),
        ],
    )


def run_feed_forward(index, five, mixed, cotangent, packed, pieces, shards):
    count, seq, width = cotangent.shape
    own = width // index.shape[0]
    ff = shards * width
    groups = 2 if index.shape[0] > 1 else 1
    paired = step_rows(count, 2)
    pairs = 2 if count // paired % 2 == 0 else 1
    rows = pairs * paired
    wide = paired * seq
    manual = [((count // paired, ff, wide), BF), ((count // paired, width, wide), F32)]
    row_outs = [((count, width, seq), F32), ((count, width, seq), BF)]
    grads = ((index.shape[0] // groups, own, 2 * ff + width), BF)
    return call(
        functools.partial(feed_forward, pieces=index.shape[0], shards=shards), "feed_forward", (index,),
        rows, (five, mixed, cotangent), (packed, *pieces),
        row_outs, [((8, width), F32), ((width, ff), BF)] + [grads] * groups,
        [((width, ff), BF)] + [((ff, width), BF)] * 2 + [((width, width), BF)] * 2
        + [((width, ff), F32)] * 2 + [((width, width), F32), ((2, width, LANES), F32), ((3, width, LANES), F32)]
        + [((pairs, width, wide), F32), ((pairs, width, wide), BF), ((pairs, width, wide), BF)]
        + [((pairs, ff, wide), BF)]
        + [((pairs, width, wide), F32), ((pairs, 8, wide), F32), ((pairs, width, wide), BF)]
        + [((pairs, ff, wide), BF), ((pairs, width, wide), F32), pltpu.SemaphoreType.DMA((2, pairs))],
        near=("out1",), only=4, manual=manual,
    )


def run_layer_output(hidden, mixed, down, shape, into, low, high):
    steps = hidden.shape[0]
    span = (int(low * steps), int(high * steps) - int(low * steps))

    def body(*refs):
        layer_output(*refs[:3], refs[-1])

    return call(body, "layer_output", (), 1, (hidden, mixed), (down,), [(shape, BF)], [], [], span=span, into=into)[0]


def run_backward(index, weight, kept, grads, packed, other, pieces):
    count, seq, width = kept[2].shape
    own = width // pieces
    groups = 2 if pieces > 1 else 1
    rows = step_rows(count, 3)
    row_args = (*kept, *grads)
    many = len(row_args)

    def body(index_ref, *refs):
        backward(*refs[:many], index_ref, *refs[many:], pieces=pieces)

    return call(
        body, "backward", (index,), rows, row_args, (weight, packed, other),
        [((count, seq, width), BF)], [((8, width), F32)] + [((pieces // groups, own, 3 * width), BF)] * groups,
        [
            ((3 * width, rows * seq), BF), ((width, 3 * width), F32), ((width, rows * seq), BF),
            ((rows, HEADS, seq, seq), F32), ((rows, HEADS, seq, seq), BF), ((width, rows * seq), F32),
            ((5, width, LANES), F32), ((4, width, LANES), F32), ((rows, width, seq), F32), ((rows, width, seq), F32),
            ((rows, width, seq), BF),
        ],
        near=(5,),
    )


def exchange(values, axis, offset):
    size = lax.axis_size(axis)
    return lax.ppermute(values, axis, [(i, i ^ offset) for i in range(size)])


def add_halves(mine, received):
    count, own, cols = mine.shape

    def body(mine_ref, received_ref, *out_refs):
        for i, ref in enumerate(out_refs):
            ref[...] = (mine_ref[i].astype(F32) + received_ref[i].astype(F32)).astype(BF)

    return small_call(body, "add_halves", (mine, received), [((own, cols), BF)] * count)


def add_wide(*items):
    return tree_sum(item.astype(F32) for item in items)


def store_high_low(ref, cols, values):
    high = values.astype(BF)
    low = (values - high.astype(F32)).astype(BF)
    ref[:, cols:] = jnp.concatenate([high, low, jnp.zeros((ref.shape[0] - 16, LANES), BF)], axis=0)


def load_high_low(ref, cols):
    both = ref[:16, cols:].astype(F32)
    return both[:8] + both[8:]


def add_halves_and_sums(index, mine, received, sums, received_sums):
    count, own, cols = mine.shape
    width = sums.shape[1]

    def body(index_ref, mine_ref, received_ref, sums_ref, received_sums_ref, *out_refs):
        total = sums_ref[...] + received_sums_ref[...]
        for i, ref in enumerate(out_refs):
            ref[:, :cols] = (mine_ref[i].astype(F32) + received_ref[i].astype(F32)).astype(BF)
            turned = pltpu.roll(total, lax.rem(width - index_ref[2 * i] * own, width), 1)[:, :LANES]
            store_high_low(ref, cols, turned)

    spec = pltpu.PrefetchScalarGridSpec(
        num_scalar_prefetch=1, grid=(1,),
        in_specs=[whole(a.shape) for a in (mine, received, sums, received_sums)],
        out_specs=[whole((own, cols + LANES))] * count,
    )
    return pl.pallas_call(
        body, grid_spec=spec, out_shape=[jax.ShapeDtypeStruct((own, cols + LANES), BF)] * count,
        compiler_params=pltpu.CompilerParams(vmem_limit_bytes=16 * MIB), name="add_halves_and_sums",
    )(index, mine, received, sums, received_sums)


def add_packed(name, items):
    cols = items[0].shape[1] - LANES

    def body(*refs):
        out_ref = refs[-1]
        out_ref[:, :cols] = tree_sum(ref[:, :cols].astype(F32) for ref in refs[:-1]).astype(BF)
        store_high_low(out_ref, cols, tree_sum(load_high_low(ref, cols) for ref in refs[:-1]))

    return small_call(body, name, items, [(items[0].shape, BF)])[0]


def add_last(items):
    own, cols = items[0].shape[0], items[0].shape[1] - LANES

    def body(*refs):
        ins, outs = refs[: len(items)], refs[len(items) :]
        outs[0][...] = tree_sum(ref[:, :cols].astype(F32) for ref in ins)
        vectors = tree_sum(load_high_low(ref, cols) for ref in ins)
        outs[1][...] = vectors[0:3, :own]
        for i in range(4):
            outs[2 + i][...] = vectors[3 + i : 4 + i, :own]

    return small_call(body, "add_last", items, [((own, cols), F32), ((3, own), F32)] + [((1, own), F32)] * 4)


def direct_plan(tokens, segment_ids, valid_len, qkv_weight, out_weight, up_weight, down_weight, conv_weight, vectors, cotangent):
    count, seq, width = tokens.shape
    own, ffs = up_weight.shape
    dp, mp = lax.axis_size("dp"), lax.axis_size("mp")
    me = lax.axis_index("dp")
    offsets = [2 * p for p in range(dp // 2)]
    index = jnp.stack([me ^ (p ^ c) for p in offsets for c in range(2)]).astype(jnp.int32)
    narrow, ff_own = small_call(
        pack_weights, "pack_weights",
        [in_hbm(a) for a in (qkv_weight, up_weight, down_weight, conv_weight, *[v.reshape(1, own) for v in vectors])],
        [((own, 3 * width + VECTORS), BF), ((2 * own, ffs), BF)], [((VECTORS, VECTORS), F32)],
    )
    shards = [ff_own] + [exchange(ff_own, "mp", j) for j in range(1, mp)]
    plane = jnp.concatenate([narrow] + [exchange(narrow, "dp", p) for p in offsets[1:]], axis=0)
    pieces = [plane, exchange(plane, "dp", 1)]
    column = jnp.concatenate(shards + [out_weight], axis=0)
    columns = [column] + [exchange(column, "dp", p) for p in offsets[1:]]
    five, mixed, v, raised, facts, packed, weight = run_forward(
        index, tokens, segment_ids, valid_len, pieces
    )
    columns, five = lax.optimization_barrier((columns, five))
    columns = jnp.concatenate(columns, axis=0)
    pieces = [columns, exchange(columns, "dp", 1)]
    hidden, mixed_attn, grad_mixed, grad_att, sums2, down, mine, theirs = run_feed_forward(
        index, five, mixed, cotangent, packed, pieces, mp
    )
    received = exchange(theirs, "dp", 1)
    shape = cotangent.shape
    layer_out = run_layer_output(hidden, mixed_attn, down, shape, None, 0, 0.17)
    received, layer_out = lax.optimization_barrier((received, layer_out))
    parts = list(add_halves(mine, received))
    parts[0], grad_att = lax.optimization_barrier((parts[0], grad_att))
    plane = [parts[0]] + [exchange(parts[i], "dp", p) for i, p in enumerate(offsets) if i]
    kept = (five, mixed, v, raised, facts)
    input_grad, sums, mine_a, theirs_a = run_backward(
        index, weight, kept, (grad_att, grad_mixed), packed, sums2, dp
    )
    plane, theirs_a, sums = lax.optimization_barrier((plane, theirs_a, sums))
    received_a = exchange(theirs_a, "dp", 1)
    received_s = exchange(sums, "dp", 1)
    total = add_wide(*plane).astype(BF)
    total, received_s = lax.optimization_barrier((total, received_s))
    part = 2 * ffs
    near = jnp.concatenate([total[:, :part], total[:, 2 * part : 3 * part]], axis=1)
    out_part = total[:, 4 * part :]
    far = jnp.concatenate([total[:, part : 2 * part], total[:, 3 * part :]], axis=1)
    parts = list(add_halves_and_sums(index, mine_a, received_a, sums, received_s))
    parts[0], hidden, layer_out = lax.optimization_barrier((parts[0], hidden, layer_out))
    plane_a = [parts[0]] + [exchange(parts[i], "dp", p) for i, p in enumerate(offsets) if i]
    received_f = exchange(far, "mp", 1)
    layer_out = run_layer_output(hidden, mixed_attn, down, shape, layer_out, 0.17, 0.51)
    plane_a, layer_out = lax.optimization_barrier((plane_a, layer_out))
    total = add_packed("add_plane", plane_a)
    received_1 = exchange(total, "mp", 1)
    received_f, _ = lax.optimization_barrier((received_f, total))
    near_sum = add_wide(near, received_f[:, : 2 * part])
    out_sum = lax.optimization_barrier(add_wide(out_part, received_f[:, 2 * part :]).astype(BF))
    keep = near_sum[:, :part]
    send = jnp.concatenate([near_sum[:, part:].astype(BF), out_sum], axis=1)
    received_n = exchange(send, "mp", 2)
    layer_out, _ = lax.optimization_barrier((layer_out, send))
    layer_out = run_layer_output(hidden, mixed_attn, down, shape, layer_out, 0.51, 0.67)
    received_1, layer_out = lax.optimization_barrier((received_1, layer_out))
    total = add_packed("add_near", (total, received_1))
    received_2 = exchange(total, "mp", 2)
    layer_out, _ = lax.optimization_barrier((layer_out, total))
    layer_out = run_layer_output(hidden, mixed_attn, down, shape, layer_out, 0.67, 1)
    received_n, layer_out = lax.optimization_barrier((received_n, layer_out))
    grad_up = keep[:, :ffs] + received_n[:, :ffs].astype(F32)
    grad_down = keep[:, ffs:] + received_n[:, ffs : 2 * ffs].astype(F32)
    grad_out = add_wide(out_sum, received_n[:, 2 * ffs :])
    grad_qkv, grad_conv, *grads = add_last((total, received_2))
    return (layer_out, input_grad, grad_qkv, grad_out, grad_up, grad_down, grad_conv, *[g.reshape(own) for g in grads])


def gathered_plan(tokens, segment_ids, valid_len, qkv_weight, out_weight, up_weight, down_weight, conv_weight, vectors, cotangent):
    count, seq, width = tokens.shape
    own = qkv_weight.shape[0]
    dp = width // own
    columns = jnp.stack([conv_weight[0], conv_weight[1], conv_weight[2], *vectors], axis=1)
    narrow = jnp.concatenate([qkv_weight, jnp.pad(columns, ((0, 0), (0, VECTORS - 7))), out_weight], axis=1)
    wide = lax.all_gather(narrow, "dp", axis=0, tiled=True)
    both = lax.all_gather(jnp.concatenate([up_weight, down_weight], axis=0), "mp", axis=1, tiled=True)
    ff = both.shape[1]
    shards = ff // width
    both = lax.all_gather(both, "dp", axis=0).reshape(dp, 2, own, shards, width)
    both = both.transpose(3, 1, 0, 2, 4).reshape(2 * ff, width)
    column = jnp.concatenate([both, wide[:, 3 * width + VECTORS :]], axis=0)
    index = jnp.zeros((1,), jnp.int32)
    five, mixed, v, raised, facts, packed, weight = run_forward(
        index, tokens, segment_ids, valid_len, [wide[:, : 3 * width + VECTORS]]
    )
    hidden, mixed_attn, grad_mixed, grad_att, sums2, down, grads = run_feed_forward(
        index, five, mixed, cotangent, packed, [column], shards
    )
    kept = (five, mixed, v, raised, facts)
    layer_out = run_layer_output(hidden, mixed_attn, down, cotangent.shape, None, 0, 1)
    input_grad, sums, grad_qkv = run_backward(index, weight, kept, (grad_att, grad_mixed), packed, sums2, 1)
    grad_ff = grads[0, :, : 2 * ff].reshape(width, shards, 2, width).transpose(0, 2, 1, 3).reshape(width, 2 * ff)
    grad_ff = lax.psum_scatter(grad_ff, "dp", scatter_dimension=0, tiled=True).reshape(own, 2, ff)
    grad_ff = lax.psum_scatter(grad_ff, "mp", scatter_dimension=2, tiled=True).astype(F32)
    grad_attn = jnp.concatenate([grad_qkv[0], grads[0, :, 2 * ff :]], axis=1)
    grad_attn = lax.psum_scatter(grad_attn, "dp", scatter_dimension=0, tiled=True)
    grad_attn = lax.psum(grad_attn, "mp").astype(F32)
    sums = lax.psum(sums, ("dp", "mp"))
    sums = lax.dynamic_slice_in_dim(sums, lax.axis_index("dp") * own, own, axis=1)
    return (
        layer_out, input_grad, grad_attn[:, : 3 * width], grad_attn[:, 3 * width :],
        grad_ff[:, 0], grad_ff[:, 1], sums[0:3], sums[3], sums[4], sums[5], sums[6],
    )


def on_device(
    tokens, segment_ids, valid_len, qkv_weight, out_weight, up_weight, down_weight, conv_weight,
    ln1_gain, ln1_shift, ln2_gain, ln2_shift, cotangent,
):
    own, ffs = up_weight.shape
    direct = own % 16 == 0 and ffs == tokens.shape[2] and own <= VECTORS and lax.axis_size("mp") == 4
    plan = direct_plan if direct else gathered_plan
    return plan(
        tokens, segment_ids, valid_len, qkv_weight, out_weight, up_weight, down_weight, conv_weight,
        (ln1_gain, ln1_shift, ln2_gain, ln2_shift), cotangent,
    )


def solution(mesh):
    rows = P(("dp", "mp"), None, None)
    weights = (P("dp", None), P("dp", None), P("dp", "mp"), P("dp", "mp"), P(None, "dp"))
    vectors = (P("dp"),) * 4
    return jax.shard_map(
        on_device,
        mesh=mesh,
        in_specs=(rows, P(("dp", "mp"), None), P(("dp", "mp"))) + weights + vectors + (rows,),
        out_specs=(rows, rows) + weights + vectors,
        check_vma=False,
    )
```

```python
import functools
import math

import jax
import jax.numpy as jnp
from jax import lax
from jax.experimental import pallas as pl
from jax.experimental.pallas import tpu as pltpu
from jax.sharding import PartitionSpec as P

HEADS = 6
VECTORS = 128
LANES = 128
BF = jnp.bfloat16
F32 = jnp.float32
MIB = 1024 * 1024
VMEM_LIMITS = dict(forward_attention=32, feed_forward=44, backward=42, layer_output=16)


def mm(lhs, rhs):
    return lax.dot_general(lhs, rhs, (((1,), (0,)), ((), ())), preferred_element_type=F32)


def mm_nt(lhs, rhs):
    return lax.dot_general(lhs, rhs, (((1,), (1,)), ((), ())), preferred_element_type=F32)


def tree_sum(items):
    items = list(items)
    while len(items) > 1:
        items = [a + b for a, b in zip(items[::2], items[1::2])]
    return items[0]


def pack_weights(qkv_ref, up_ref, down_ref, conv_ref, g1_ref, s1_ref, g2_ref, s2_ref, narrow_ref, ff_ref, rows_ref):
    own, ffs = up_ref.shape
    rows_ref[...] = jnp.zeros_like(rows_ref)
    rows_ref[0:3, :own] = conv_ref[...].astype(F32)
    for i, ref in enumerate((g1_ref, s1_ref, g2_ref, s2_ref)):
        rows_ref[3 + i : 4 + i, :own] = ref[...].astype(F32)
    wide = qkv_ref.shape[1]
    narrow_ref[:, :wide] = qkv_ref[...]
    narrow_ref[:, wide:] = rows_ref[...].T[:own].astype(BF)
    ff_ref[:own] = up_ref[...]
    ff_ref[own:] = down_ref[...]


def tiles(total, size):
    return [slice(at, at + size) for at in range(0, total, size)]


def weave(*strands):
    strands = [strand for strand in strands if strand]
    total = sum(len(strand) for strand in strands)
    pieces = [((i + 0.5) / len(strand), j, piece) for j, strand in enumerate(strands) for i, piece in enumerate(strand)]
    assert len(pieces) == total
    for _, _, piece in sorted(pieces, key=lambda item: item[:2]):
        piece()


def twice(tile, lanes):
    return jnp.concatenate([tile] * (lanes // LANES), axis=1)


def load_columns(packed_ref, col_ref, places):
    for i, place in enumerate(places):
        column = packed_ref[:, place : place + 1].astype(F32)
        col_ref[i] = jnp.broadcast_to(column, (column.shape[0], LANES))


def pairwise(items, combine):
    items = list(items)
    while len(items) > 1:
        odd = items[len(items) // 2 * 2 :]
        items = [combine(a, b) for a, b in zip(items[::2], items[1::2])] + odd
    return items[0]


def fold(values, combine=jnp.add):
    return pairwise([values[t] for t in tiles(values.shape[0], 8)], combine)


def column_mean(values):
    return jnp.sum(fold(values), axis=0, keepdims=True) * (1.0 / values.shape[0])


def norm_columns(values):
    centred = values - column_mean(values)
    scale = lax.rsqrt(column_mean(centred * centred) + 1e-06)
    return centred * scale, scale


def fold_lanes(values):
    return sum(values[:, t] for t in tiles(values.shape[1], LANES))


def forward_attention(index_ref, len_ref, tok_ref, seg_ref, *refs, pieces):
    cores = 2 if pieces > 1 else 1
    piece_refs = refs[:cores]
    (
        five_ref, mc_ref, v_ref, e_ref, facts_ref, packed_ref, w_ref,
        wt_ref, wide_ref, col_ref, key_mask_ref, query_mask_ref, key_ref, value_ref,
    ) = refs[cores:]
    x_ref, norm_ref, q_ref, k_ref, att_ref = [five_ref.at[:, i] for i in range(5)]
    aux_ref, inv_ref = facts_ref.at[:, :8], facts_ref.at[:, 8:]
    rows, seq, width = tok_ref.shape
    head = width // HEADS
    step = pl.program_id(0)

    @pl.when(step == 0)
    def _():
        own = width // pieces
        for i in range(pieces):
            here = pl.ds(pl.multiple_of(index_ref[i] * own, 16), own)
            wide_ref[here, :] = piece_refs[i % cores][i // cores * own : (i // cores + 1) * own]
        w_ref[...] = wide_ref[:, : 3 * width]
        wt_ref[...] = wide_ref[:, : 3 * width].T
        packed_ref[...] = wide_ref[:, 3 * width :]
        load_columns(packed_ref, col_ref, range(5))
        col_ref[1] = col_ref[1] + 1.0

    place = lax.broadcasted_iota(jnp.int32, (1, seq), 1)
    zero = jnp.zeros((head, seq), BF)

    def preparation(r):
        known = {}

        def start():
            segs = seg_ref[pl.ds(step * rows + r, 1), :].astype(F32)
            valid = place < len_ref[step * rows + r]
            number = jnp.where(valid, segs, -1.0)
            links = jnp.where(valid & (place > 0) & (number == pltpu.roll(number, 1, 1)), 1.0, 0.0)
            next_links = jnp.where(place < seq - 1, pltpu.roll(links, seq - 1, 1), 0.0)
            none = jnp.zeros_like(links)
            aux = jnp.concatenate([links, next_links, number, none, none, none, none, none], axis=0)
            aux_ref[r] = aux
            x_ref[r] = tok_ref[r].T
            known.update(segs=segs, links=links, next_links=next_links, key_number=aux.T[:, 2:3])

        def mask():
            number = known["key_number"]
            lane = lax.broadcasted_iota(jnp.int32, (seq, LANES), 1)
            itself = lax.broadcasted_iota(jnp.int32, (seq, LANES), 0) - (seq - LANES)
            chosen = (lane.astype(F32) == number) | ((number < 0.0) & (lane == itself))
            key_mask_ref[r] = jnp.where(chosen, 1.0, 0.0).astype(BF)
            slot = lax.broadcasted_iota(jnp.int32, (LANES, seq), 0)
            itself = lax.broadcasted_iota(jnp.int32, (LANES, seq), 1) - (seq - LANES)
            open_to = (slot.astype(F32) == known["segs"]) | ((slot >= LANES // 2) & (slot == itself))
            query_mask_ref[r] = jnp.where(open_to, 0.0, -1e30).astype(BF)

        def conv(t):
            base = x_ref[r, t].astype(F32)
            before = pltpu.roll(base, 1, 1) * known["links"]
            after = pltpu.roll(base, seq - 1, 1) * known["next_links"]
            conv0, conv1, conv2 = [twice(col_ref[i, t], seq) for i in range(3)]
            mc_ref[r, t] = before * conv0 + base * conv1 + after * conv2

        def norm(t):
            n, _ = norm_columns(mc_ref[r, :, t])
            norm_ref[r, :, t] = (n * col_ref[3] + col_ref[4]).astype(BF)

        pieces = [start] + [functools.partial(conv, t) for t in tiles(width, 32)]
        pieces += [functools.partial(norm, t) for t in tiles(seq, LANES)]
        return pieces + [mask]

    def project():
        normed = jnp.concatenate([norm_ref[r] for r in range(rows)], axis=1)
        for i, ref in enumerate((q_ref, k_ref, value_ref)):
            part = mm(wt_ref[i * width : (i + 1) * width], normed)
            part = (part * (head ** (-0.5) * math.log2(math.e)) if i == 0 else part).astype(BF)
            for r in range(rows):
                ref[r] = part[:, r * seq : (r + 1) * seq]
        for r in range(rows):
            key_ref[r] = k_ref[r].T
            v_ref[r] = value_ref[r].T

    def scores(r, p):
        low, high = [q_ref[r, h * head : (h + 1) * head] for h in (2 * p, 2 * p + 1)]
        both = jnp.concatenate([jnp.concatenate([low, zero], axis=1), jnp.concatenate([zero, high], axis=1)], axis=0)
        keys = jnp.concatenate([key_ref[r, :, 2 * p * head : 2 * (p + 1) * head], key_mask_ref[r]], axis=1)
        masks = jnp.concatenate([query_mask_ref[r], query_mask_ref[r]], axis=1)
        return mm(keys, jnp.concatenate([both, masks], axis=0))

    def attended(r, p):
        both = jnp.concatenate([e_ref[r, 2 * p], e_ref[r, 2 * p + 1]], axis=1)
        product = mm(value_ref[r, 2 * p * head : 2 * (p + 1) * head], both)
        parts = []
        for i in range(2):
            att = product[i * head : (i + 1) * head, i * seq : (i + 1) * seq] * inv_ref[r, 2 * p + i : 2 * p + i + 1]
            parts.append(att.astype(BF))
        return jnp.concatenate(parts, axis=0)

    def soften(r, p, product):
        for i in range(2):
            for t in tiles(seq, LANES):
                masked = product[:, i * seq + t.start : i * seq + t.stop]
                raised = jnp.exp2(masked - jnp.max(fold(masked, jnp.maximum), axis=0, keepdims=True))
                inv_ref[r, 2 * p + i : 2 * p + i + 1, t] = 1.0 / jnp.sum(fold(raised), axis=0, keepdims=True)
                e_ref[r, 2 * p + i, :, t] = raised.astype(BF)

    weave(*[preparation(r) for r in range(rows)])
    project()
    work = [(r, p) for r in range(rows) for p in range(HEADS // 2)]
    current, last = scores(*work[0]), None
    for at, (r, p) in enumerate(work):
        following = scores(*work[at + 1]) if at + 1 < len(work) else None
        finished = attended(*last) if last else None
        soften(r, p, current)
        if last:
            att_ref[last[0], 2 * last[1] * head : 2 * (last[1] + 1) * head] = finished
        current, last = following, (r, p)
    att_ref[last[0], 2 * last[1] * head : 2 * (last[1] + 1) * head] = attended(*last)


def gelu_parts(y):
    twice_cdf = lax.erf(y) + 1.0
    bell = jnp.exp2(y * y * -math.log2(math.e) + math.log2(2.0 / math.sqrt(math.pi)))
    return y * twice_cdf, twice_cdf + y * bell


def feed_forward(index_ref, five_ref, mc_ref, ct_ref, packed_ref, *refs, pieces, shards):
    att_ref = five_ref.at[:, 0]
    groups = 2 if pieces > 1 else 1
    piece_refs = refs[:groups]
    hidden_out, mixed_out, gm_ref, ga_ref, gs_ref, down_ref = refs[groups : groups + 6]
    gw_refs = refs[groups + 6 : 2 * groups + 6]
    (
        up_ref, upt_ref, downt_ref, out_ref, outt_ref, up_acc, down_acc, out_acc, col_acc, col_ref,
        n_ref, norm_ref, ctt_ref, gp_ref, gn_ref, scale_ref, branch_ref, hidden_ref, mixed_ref, sems,
    ) = refs[2 * groups + 6 :]
    rows, seq, width = ct_ref.shape
    ff = up_ref.shape[1]
    ffs = ff // shards
    own = width // pieces
    step = pl.program_id(0)

    @pl.when(step == 0)
    def _():
        for acc in (up_acc, down_acc, out_acc, col_acc):
            acc[...] = jnp.zeros_like(acc)
        for i in range(pieces):
            here = pl.ds(pl.multiple_of(index_ref[i] * own, 16), own)
            ref, first = piece_refs[i % groups], i // groups * (2 * shards + 1) * own
            for j in range(shards):
                at = first + 2 * j * own
                up_ref[here, j * ffs : (j + 1) * ffs] = ref[at : at + own]
                down_ref[here, j * ffs : (j + 1) * ffs] = ref[at + own : at + 2 * own]
            at = first + 2 * shards * own
            out_ref[here, :] = ref[at : at + own]
        upt_ref[...] = up_ref[...].T
        downt_ref[...] = down_ref[...].T
        outt_ref[...] = out_ref[...].T
        load_columns(packed_ref, col_ref, (5, 6, 5))
        for i, factor in enumerate((0.5, math.sqrt(0.5), math.sqrt(0.5))):
            col_ref[i] = col_ref[i] * factor

    def copies(at, g):
        place = at * pairs + g
        return [
            pltpu.make_async_copy(hidden_ref.at[g], hidden_out.at[place], sems.at[0, g]),
            pltpu.make_async_copy(mixed_ref.at[g], mixed_out.at[place], sems.at[1, g]),
        ]

    pairs = n_ref.shape[0]

    @pl.when(step > 0)
    def _():
        for g in range(pairs):
            for copy in copies(step - 1, g):
                copy.wait()

    def begin(g):
        pair = range(g * paired, (g + 1) * paired)
        attended = jnp.concatenate([att_ref[r] for r in pair], axis=1)
        branch = mm(outt_ref[...], attended)
        for i, r in enumerate(pair):
            lanes = slice(i * seq, (i + 1) * seq)
            ctt_ref[g, :, lanes] = ct_ref[r].T
            mixed_ref[g, :, lanes] = mc_ref[r] + branch[:, lanes]
        for t in spots:
            n, scale = norm_columns(mixed_ref[g, :, t])
            n_ref[g, :, t] = n
            scale_ref[g, 0:1, t] = scale
            norm_ref[g, :, t] = (n * col_ref[2] + col_ref[1]).astype(BF)

    def activate(g, block):
        pre = mm(upt_ref[block], norm_ref[g])
        grad_hidden = mm(downt_ref[block], ctt_ref[g])
        for low in range(0, block.stop - block.start, 16):
            part = slice(low, low + 16)
            here = slice(block.start + low, block.start + low + 16)
            hidden, slope = gelu_parts(pre[part])
            hidden_ref[g, here] = hidden.astype(BF)
            gp_ref[g, here] = (grad_hidden[part] * slope).astype(BF)

    def weigh(g):
        gn_ref[g] = mm(up_ref[...], gp_ref[g])
        down_acc[...] += mm_nt(ctt_ref[g], hidden_ref[g])
        up_acc[...] += mm_nt(norm_ref[g], gp_ref[g])

    def norm_back(g):
        mean_e = [jnp.zeros((8, LANES), F32) for _ in spots]
        mean_en = [jnp.zeros((8, LANES), F32) for _ in spots]
        for d in tiles(width, 32):
            column = col_ref[0, d]
            gain_sum, shift_sum = col_acc[0, d], col_acc[1, d]
            for i, t in enumerate(spots):
                grad_n = gn_ref[g, d, t]
                product = grad_n * n_ref[g, d, t]
                gain_sum += product
                shift_sum += grad_n
                mean_e[i] += fold(grad_n * column)
                mean_en[i] += fold(product * column)
            col_acc[0, d] = gain_sum
            col_acc[1, d] = shift_sum
        for i, t in enumerate(spots):
            me = jnp.sum(mean_e[i], axis=0, keepdims=True) * (1.0 / width)
            men = jnp.sum(mean_en[i], axis=0, keepdims=True) * (1.0 / width)
            row, inside = divmod(t.start, seq)
            for d in tiles(width, 32):
                change = scale_ref[g, 0:1, t] * (gn_ref[g, d, t] * col_ref[0, d] - me - n_ref[g, d, t] * men)
                grad_mixed = ctt_ref[g, d, t].astype(F32) + change
                gm_ref[g * paired + row, d, inside : inside + LANES] = grad_mixed
                branch_ref[g, d, t] = grad_mixed.astype(BF)

    def end(g):
        pair = range(g * paired, (g + 1) * paired)
        attended = jnp.concatenate([att_ref[r] for r in pair], axis=1)
        grad_attended = mm(out_ref[...], branch_ref[g]).astype(BF)
        for i, r in enumerate(pair):
            ga_ref[r] = grad_attended[:, i * seq : (i + 1) * seq]
        out_acc[...] += mm_nt(attended, branch_ref[g])

    paired = rows // pairs
    spots = tiles(paired * seq, LANES)
    begin(0)
    copies(step, 0)[1].start()
    for g in range(pairs):
        for block in tiles(ff, 128):
            activate(g, block)
        copies(step, g)[0].start()
        if g + 1 < pairs:
            begin(g + 1)
            copies(step, g + 1)[1].start()
        weigh(g)
        norm_back(g)
        end(g)

    @pl.when(step == pl.num_programs(0) - 1)
    def _():
        for g in range(pairs):
            for copy in copies(step, g):
                copy.wait()
        for i in range(pieces):
            here = pl.ds(pl.multiple_of(index_ref[i] * own, 16), own)
            place = gw_refs[i % groups]
            for j in range(shards):
                cols = slice(j * ffs, (j + 1) * ffs)
                place[i // groups, :, 2 * j * ffs : (2 * j + 1) * ffs] = (up_acc[here, cols] * math.sqrt(0.5)).astype(BF)
                place[i // groups, :, (2 * j + 1) * ffs : (2 * j + 2) * ffs] = (down_acc[here, cols] * math.sqrt(0.5)).astype(BF)
            place[i // groups, :, 2 * ff :] = out_acc[here, :].astype(BF)
        gs_ref[...] = jnp.zeros_like(gs_ref)
        for i in range(2):
            gs_ref[5 + i : 6 + i] = jnp.sum(col_acc[i].T, axis=0, keepdims=True) * 0.5


def layer_output(hidden_ref, mixed_ref, down_ref, lo_ref):
    rows, seq, _ = lo_ref.shape
    total = (mixed_ref[0] + mm(down_ref[...], hidden_ref[0]) * math.sqrt(0.5)).astype(BF)
    for r in range(rows):
        lo_ref[r] = total[:, r * seq : (r + 1) * seq].T


def backward(
    five_ref, mc_ref, v_ref, e_ref, facts_ref, ga_ref, gm_ref, index_ref, w_ref, packed_ref, other_ref, ig_ref, gs_ref, *refs, pieces,
):
    x_ref, norm_ref, q_ref, k_ref, att_ref = [five_ref.at[:, i] for i in range(5)]
    aux_ref, inv_ref = facts_ref.at[:, :8], facts_ref.at[:, 8:]
    gw_refs = refs[:-11]
    (
        proj_ref, w_acc, norm_cat, soft_ref, logit_ref, gn_ref, acc_ref, col_ref, n_ref, g_ref, turn_ref
    ) = refs[-11:]
    rows, seq, width = v_ref.shape
    own = width // pieces
    head = width // HEADS
    step = pl.program_id(0)

    @pl.when(step == 0)
    def _():
        w_acc[...] = jnp.zeros_like(w_acc)
        acc_ref[...] = jnp.zeros_like(acc_ref)
        load_columns(packed_ref, col_ref, range(4))
        col_ref[1] = col_ref[1] + 1.0

    zero = jnp.zeros((head, seq), BF)
    work = [(r, p) for r in range(rows) for p in range(HEADS // 2)]

    def opening(r, p):
        grads, inners = [], []
        for h in (2 * p, 2 * p + 1):
            part = slice(h * head, (h + 1) * head)
            grad_att = ga_ref[r, part].astype(F32) * inv_ref[r, h : h + 1]
            inners.append(jnp.sum(fold(grad_att * att_ref[r, part].astype(F32)), axis=0, keepdims=True))
            grads.append(grad_att.astype(BF))
        low, high = grads
        both = jnp.concatenate([jnp.concatenate([low, zero], axis=1), jnp.concatenate([zero, high], axis=1)], axis=0)
        product = mm(v_ref[r, :, 2 * p * head : 2 * (p + 1) * head], both)
        soft_ref[r, 2 * p] = product[:, :seq]
        soft_ref[r, 2 * p + 1] = product[:, seq:]
        return jnp.concatenate(grads, axis=0), inners

    spots = tiles(seq, LANES)

    def finish_row(r):
        wide = [slice(r * seq + t.start, r * seq + t.stop) for t in spots]
        lanes = slice(r * seq, (r + 1) * seq)
        norm_cat[:, lanes] = norm_ref[r]
        gn_ref[:, lanes] = mm(w_ref[...], proj_ref[:, lanes])
        scales = []
        for t in spots:
            n, scale = norm_columns(mc_ref[r, :, t])
            n_ref[r, :, t] = n
            scales.append(scale)
        mean_e = [jnp.zeros((8, LANES), F32) for _ in spots]
        mean_en = [jnp.zeros((8, LANES), F32) for _ in spots]
        for d in tiles(width, 32):
            column = col_ref[3, d]
            gain_sum, shift_sum = acc_ref[3, d], acc_ref[4, d]
            for i, t in enumerate(spots):
                grad_n = gn_ref[d, wide[i]]
                product = grad_n * n_ref[r, d, t]
                gain_sum += product
                shift_sum += grad_n
                mean_e[i] += fold(grad_n * column)
                mean_en[i] += fold(product * column)
            acc_ref[3, d] = gain_sum
            acc_ref[4, d] = shift_sum
        for i, t in enumerate(spots):
            me = jnp.sum(mean_e[i], axis=0, keepdims=True) * (1.0 / width)
            men = jnp.sum(mean_en[i], axis=0, keepdims=True) * (1.0 / width)
            for d in tiles(width, 64):
                e = gn_ref[d, wide[i]] * col_ref[3, d]
                g_ref[r, d, t] = gm_ref[r, d, t] + scales[i] * (e - me - n_ref[r, d, t] * men)
        links, next_links = aux_ref[r, 0:1], aux_ref[r, 1:2]
        for d in tiles(width, 32):
            g = g_ref[r, d]
            base = x_ref[r, d].astype(F32)
            before = pltpu.roll(g, 1, 1) * links
            after = pltpu.roll(g, seq - 1, 1) * next_links
            acc_ref[0, d] += fold_lanes(base * after)
            acc_ref[1, d] += fold_lanes(base * g)
            acc_ref[2, d] += fold_lanes(base * before)
            conv0, conv1, conv2 = [twice(col_ref[i, d], seq) for i in range(3)]
            turn_ref[r, d] = (conv1 * g + conv0 * after + conv2 * before).astype(BF)
        ig_ref[r] = turn_ref[r].T

    ready = opening(*work[0])
    for at, (r, p) in enumerate(work):
        grad_att, inners = ready
        if at + 1 < len(work):
            ready = opening(*work[at + 1])
        for i, h in enumerate((2 * p, 2 * p + 1)):
            for t in tiles(seq, 32):
                raised = e_ref[r, h, t].astype(F32)
                logit_ref[r, h, t] = (raised * (soft_ref[r, h, t] - inners[i])).astype(BF)
        place = slice(r * seq, (r + 1) * seq)
        for i, h in enumerate((2 * p, 2 * p + 1)):
            part = slice(h * head, (h + 1) * head)
            grad_q = mm(k_ref[r, part], logit_ref[r, h]) * head ** (-0.5)
            grad_k = mm_nt(q_ref[r, part], logit_ref[r, h]) * math.log(2.0)
            grad_v = mm_nt(grad_att[i * head : (i + 1) * head], e_ref[r, h])
            for j, grad in enumerate((grad_q, grad_k, grad_v)):
                proj_ref[j * width + h * head : j * width + (h + 1) * head, place] = grad.astype(BF)
        if p == HEADS // 2 - 1:
            finish_row(r)
    w_acc[...] += mm_nt(norm_cat[...], proj_ref[...])

    @pl.when(step == pl.num_programs(0) - 1)
    def _():
        gs_ref[...] = other_ref[...]
        for i in range(5):
            gs_ref[i : i + 1] += jnp.sum(acc_ref[i].T, axis=0, keepdims=True)
        groups = len(gw_refs)
        for i in range(pieces):
            here = pl.ds(pl.multiple_of(index_ref[i] * own, 16), own)
            gw_refs[i % groups][i // groups] = w_acc[here, :].astype(BF)


def in_hbm(values):
    return pltpu.with_memory_space_constraint(values, pltpu.HBM)


def by_row(shape, rows, first=0):
    tail = tuple(shape[1:])
    return pl.BlockSpec((rows,) + tail, lambda i, *_: (i + first,) + (0,) * len(tail))


def whole(shape):
    place = (0,) * len(shape)
    return pl.BlockSpec(tuple(shape), lambda i, *_: place, pipeline_mode=pl.Buffered(1))


def step_rows(count, most):
    return max(r for r in range(1, most + 1) if count % r == 0)


def call(body, name, scalars, rows, row_args, args, row_outs, outs, scratch, span=None, into=None, near=(), only=None, manual=()):
    first, count = span or (0, row_args[0].shape[0])
    skip = first // rows
    total = row_args[0].shape[0]

    def spec_of(shape):
        return by_row(shape, shape[0] * rows // total, skip)

    in_specs = [spec_of(a.shape) for a in row_args]
    if only:
        tail = row_args[0].shape[2:]
        in_specs[0] = pl.BlockSpec((rows, 1) + tail, lambda i, *_: (i, only) + (0,) * len(tail))
    in_specs += [whole(a.shape) for a in args]
    aliases = {}
    if into is not None:
        in_specs.append(pl.BlockSpec(memory_space=pl.ANY))
        aliases = {len(scalars) + len(in_specs) - 1: 0}
    spec = pltpu.PrefetchScalarGridSpec(
        num_scalar_prefetch=len(scalars),
        grid=(count // rows,),
        in_specs=in_specs,
        out_specs=[pl.BlockSpec(memory_space=pl.ANY) for _ in manual] + [spec_of(s) for s, _ in row_outs] + [whole(s) for s, _ in outs],
        scratch_shapes=[pltpu.VMEM(*s) if isinstance(s, tuple) else s for s in scratch],
    )
    return pl.pallas_call(
        body,
        grid_spec=spec,
        out_shape=[pltpu.HBM(s, t) for s, t in manual] + [(jax.ShapeDtypeStruct if "out" + str(i) in near else pltpu.HBM)(s, t) for i, (s, t) in enumerate(row_outs)]
        + [jax.ShapeDtypeStruct(s, t) for s, t in outs],
        input_output_aliases=aliases,
        compiler_params=pltpu.CompilerParams(dimension_semantics=("arbitrary",), vmem_limit_bytes=VMEM_LIMITS[name] * MIB),
        name=name,
    )(*scalars, *[a if i in near else in_hbm(a) for i, a in enumerate(row_args)], *args, *(() if into is None else (into,)))


def small_call(body, name, args, outs, scratch=()):
    return pl.pallas_call(
        body,
        out_shape=[jax.ShapeDtypeStruct(s, t) for s, t in outs],
        scratch_shapes=[pltpu.VMEM(s, t) for s, t in scratch],
        compiler_params=pltpu.CompilerParams(vmem_limit_bytes=16 * MIB),
        name=name,
    )(*args)


def run_forward(index, tokens, segment_ids, valid_len, pieces):
    count, seq, width = tokens.shape
    flipped = (count, width, seq)
    rows = step_rows(count, 3)
    row_outs = [
        ((count, 5, width, seq), BF), (flipped, F32), ((count, seq, width), BF),
        ((count, HEADS, seq, seq), BF), ((count, 16, seq), F32),
    ]
    return call(
        functools.partial(forward_attention, pieces=index.shape[0]), "forward_attention", (index, in_hbm(valid_len)),
        rows, (tokens,), (in_hbm(segment_ids), *pieces),
        row_outs, [((width, VECTORS), BF), ((width, 3 * width), BF)],
        [
            ((3 * width, width), BF), ((width, 3 * width + VECTORS), BF), ((5, width, LANES), F32),
            ((rows, seq, LANES), BF), ((rows, LANES, seq), BF), ((rows, seq, width), BF), ((rows, width, seq), BF),
        ],
    )


def run_feed_forward(index, five, mixed, cotangent, packed, pieces, shards):
    count, seq, width = cotangent.shape
    own = width // index.shape[0]
    ff = shards * width
    groups = 2 if index.shape[0] > 1 else 1
    paired = step_rows(count, 2)
    pairs = 2 if count // paired % 2 == 0 else 1
    rows = pairs * paired
    wide = paired * seq
    manual = [((count // paired, ff, wide), BF), ((count // paired, width, wide), F32)]
    row_outs = [((count, width, seq), F32), ((count, width, seq), BF)]
    grads = ((index.shape[0] // groups, own, 2 * ff + width), BF)
    return call(
        functools.partial(feed_forward, pieces=index.shape[0], shards=shards), "feed_forward", (index,),
        rows, (five, mixed, cotangent), (packed, *pieces),
        row_outs, [((8, width), F32), ((width, ff), BF)] + [grads] * groups,
        [((width, ff), BF)] + [((ff, width), BF)] * 2 + [((width, width), BF)] * 2
        + [((width, ff), F32)] * 2 + [((width, width), F32), ((2, width, LANES), F32), ((3, width, LANES), F32)]
        + [((pairs, width, wide), F32), ((pairs, width, wide), BF), ((pairs, width, wide), BF)]
        + [((pairs, ff, wide), BF)]
        + [((pairs, width, wide), F32), ((pairs, 8, wide), F32), ((pairs, width, wide), BF)]
        + [((pairs, ff, wide), BF), ((pairs, width, wide), F32), pltpu.SemaphoreType.DMA((2, pairs))],
        near=("out1",), only=4, manual=manual,
    )


def run_layer_output(hidden, mixed, down, shape, into, low, high):
    steps = hidden.shape[0]
    span = (int(low * steps), int(high * steps) - int(low * steps))

    def body(*refs):
        layer_output(*refs[:3], refs[-1])

    return call(body, "layer_output", (), 1, (hidden, mixed), (down,), [(shape, BF)], [], [], span=span, into=into)[0]


def run_backward(index, weight, kept, grads, packed, other, pieces):
    count, seq, width = kept[2].shape
    own = width // pieces
    groups = 2 if pieces > 1 else 1
    rows = step_rows(count, 3)
    row_args = (*kept, *grads)
    many = len(row_args)

    def body(index_ref, *refs):
        backward(*refs[:many], index_ref, *refs[many:], pieces=pieces)

    return call(
        body, "backward", (index,), rows, row_args, (weight, packed, other),
        [((count, seq, width), BF)], [((8, width), F32)] + [((pieces // groups, own, 3 * width), BF)] * groups,
        [
            ((3 * width, rows * seq), BF), ((width, 3 * width), F32), ((width, rows * seq), BF),
            ((rows, HEADS, seq, seq), F32), ((rows, HEADS, seq, seq), BF), ((width, rows * seq), F32),
            ((5, width, LANES), F32), ((4, width, LANES), F32), ((rows, width, seq), F32), ((rows, width, seq), F32),
            ((rows, width, seq), BF),
        ],
        near=(5,),
    )


def exchange(values, axis, offset):
    size = lax.axis_size(axis)
    return lax.ppermute(values, axis, [(i, i ^ offset) for i in range(size)])


def add_halves(mine, received):
    count, own, cols = mine.shape

    def body(mine_ref, received_ref, *out_refs):
        for i, ref in enumerate(out_refs):
            ref[...] = (mine_ref[i].astype(F32) + received_ref[i].astype(F32)).astype(BF)

    return small_call(body, "add_halves", (mine, received), [((own, cols), BF)] * count)


def add_wide(*items):
    return tree_sum(item.astype(F32) for item in items)


def store_high_low(ref, cols, values):
    high = values.astype(BF)
    low = (values - high.astype(F32)).astype(BF)
    ref[:, cols:] = jnp.concatenate([high, low, jnp.zeros((ref.shape[0] - 16, LANES), BF)], axis=0)


def load_high_low(ref, cols):
    both = ref[:16, cols:].astype(F32)
    return both[:8] + both[8:]


def add_halves_and_sums(index, mine, received, sums, received_sums):
    count, own, cols = mine.shape
    width = sums.shape[1]

    def body(index_ref, mine_ref, received_ref, sums_ref, received_sums_ref, *out_refs):
        total = sums_ref[...] + received_sums_ref[...]
        for i, ref in enumerate(out_refs):
            ref[:, :cols] = (mine_ref[i].astype(F32) + received_ref[i].astype(F32)).astype(BF)
            turned = pltpu.roll(total, lax.rem(width - index_ref[2 * i] * own, width), 1)[:, :LANES]
            store_high_low(ref, cols, turned)

    spec = pltpu.PrefetchScalarGridSpec(
        num_scalar_prefetch=1, grid=(1,),
        in_specs=[whole(a.shape) for a in (mine, received, sums, received_sums)],
        out_specs=[whole((own, cols + LANES))] * count,
    )
    return pl.pallas_call(
        body, grid_spec=spec, out_shape=[jax.ShapeDtypeStruct((own, cols + LANES), BF)] * count,
        compiler_params=pltpu.CompilerParams(vmem_limit_bytes=16 * MIB), name="add_halves_and_sums",
    )(index, mine, received, sums, received_sums)


def add_packed(name, items):
    cols = items[0].shape[1] - LANES

    def body(*refs):
        out_ref = refs[-1]
        out_ref[:, :cols] = tree_sum(ref[:, :cols].astype(F32) for ref in refs[:-1]).astype(BF)
        store_high_low(out_ref, cols, tree_sum(load_high_low(ref, cols) for ref in refs[:-1]))

    return small_call(body, name, items, [(items[0].shape, BF)])[0]


def add_last(items):
    own, cols = items[0].shape[0], items[0].shape[1] - LANES

    def body(*refs):
        ins, outs = refs[: len(items)], refs[len(items) :]
        outs[0][...] = tree_sum(ref[:, :cols].astype(F32) for ref in ins)
        vectors = tree_sum(load_high_low(ref, cols) for ref in ins)
        outs[1][...] = vectors[0:3, :own]
        for i in range(4):
            outs[2 + i][...] = vectors[3 + i : 4 + i, :own]

    return small_call(body, "add_last", items, [((own, cols), F32), ((3, own), F32)] + [((1, own), F32)] * 4)


def direct_plan(tokens, segment_ids, valid_len, qkv_weight, out_weight, up_weight, down_weight, conv_weight, vectors, cotangent):
    count, seq, width = tokens.shape
    own, ffs = up_weight.shape
    dp, mp = lax.axis_size("dp"), lax.axis_size("mp")
    me = lax.axis_index("dp")
    offsets = [2 * p for p in range(dp // 2)]
    index = jnp.stack([me ^ (p ^ c) for p in offsets for c in range(2)]).astype(jnp.int32)
    narrow, ff_own = small_call(
        pack_weights, "pack_weights",
        [in_hbm(a) for a in (qkv_weight, up_weight, down_weight, conv_weight, *[v.reshape(1, own) for v in vectors])],
        [((own, 3 * width + VECTORS), BF), ((2 * own, ffs), BF)], [((VECTORS, VECTORS), F32)],
    )
    shards = [ff_own] + [exchange(ff_own, "mp", j) for j in range(1, mp)]
    plane = jnp.concatenate([narrow] + [exchange(narrow, "dp", p) for p in offsets[1:]], axis=0)
    pieces = [plane, exchange(plane, "dp", 1)]
    column = jnp.concatenate(shards + [out_weight], axis=0)
    columns = [column] + [exchange(column, "dp", p) for p in offsets[1:]]
    five, mixed, v, raised, facts, packed, weight = run_forward(
        index, tokens, segment_ids, valid_len, pieces
    )
    columns, five = lax.optimization_barrier((columns, five))
    columns = jnp.concatenate(columns, axis=0)
    pieces = [columns, exchange(columns, "dp", 1)]
    hidden, mixed_attn, grad_mixed, grad_att, sums2, down, mine, theirs = run_feed_forward(
        index, five, mixed, cotangent, packed, pieces, mp
    )
    received = exchange(theirs, "dp", 1)
    shape = cotangent.shape
    layer_out = run_layer_output(hidden, mixed_attn, down, shape, None, 0, 0.17)
    received, layer_out = lax.optimization_barrier((received, layer_out))
    parts = list(add_halves(mine, received))
    parts[0], grad_att = lax.optimization_barrier((parts[0], grad_att))
    plane = [parts[0]] + [exchange(parts[i], "dp", p) for i, p in enumerate(offsets) if i]
    kept = (five, mixed, v, raised, facts)
    input_grad, sums, mine_a, theirs_a = run_backward(
        index, weight, kept, (grad_att, grad_mixed), packed, sums2, dp
    )
    plane, theirs_a, sums = lax.optimization_barrier((plane, theirs_a, sums))
    received_a = exchange(theirs_a, "dp", 1)
    received_s = exchange(sums, "dp", 1)
    total = add_wide(*plane).astype(BF)
    part = 2 * ffs
    near = jnp.concatenate([total[:, :part], total[:, 2 * part : 3 * part]], axis=1)
    out_part = total[:, 4 * part :]
    far = jnp.concatenate([total[:, part : 2 * part], total[:, 3 * part :]], axis=1)
    parts = list(add_halves_and_sums(index, mine_a, received_a, sums, received_s))
    parts[0], far, hidden, layer_out = lax.optimization_barrier((parts[0], far, hidden, layer_out))
    plane_a = [parts[0]] + [exchange(parts[i], "dp", p) for i, p in enumerate(offsets) if i]
    cut = far.shape[1] // 2 // LANES * LANES
    received_f = [exchange(far[:, :cut], "mp", 1), exchange(far[:, cut:], "mp", 1)]
    layer_out = run_layer_output(hidden, mixed_attn, down, shape, layer_out, 0.17, 0.51)
    plane_a, layer_out = lax.optimization_barrier((plane_a, layer_out))
    total = add_packed("add_plane", plane_a)
    received_1 = exchange(total, "mp", 1)
    received_f, _ = lax.optimization_barrier((received_f, total))
    received_f = jnp.concatenate(received_f, axis=1)
    near_sum = add_wide(near, received_f[:, : 2 * part])
    out_sum = lax.optimization_barrier(add_wide(out_part, received_f[:, 2 * part :]).astype(BF))
    keep = near_sum[:, :part]
    send = jnp.concatenate([near_sum[:, part:].astype(BF), out_sum], axis=1)
    received_n = exchange(send, "mp", 2)
    layer_out, _ = lax.optimization_barrier((layer_out, send))
    layer_out = run_layer_output(hidden, mixed_attn, down, shape, layer_out, 0.51, 0.67)
    received_1, layer_out = lax.optimization_barrier((received_1, layer_out))
    total = add_packed("add_near", (total, received_1))
    received_2 = exchange(total, "mp", 2)
    layer_out, _ = lax.optimization_barrier((layer_out, total))
    layer_out = run_layer_output(hidden, mixed_attn, down, shape, layer_out, 0.67, 1)
    received_n, layer_out = lax.optimization_barrier((received_n, layer_out))
    grad_up = keep[:, :ffs] + received_n[:, :ffs].astype(F32)
    grad_down = keep[:, ffs:] + received_n[:, ffs : 2 * ffs].astype(F32)
    grad_out = add_wide(out_sum, received_n[:, 2 * ffs :])
    grad_qkv, grad_conv, *grads = add_last((total, received_2))
    return (layer_out, input_grad, grad_qkv, grad_out, grad_up, grad_down, grad_conv, *[g.reshape(own) for g in grads])


def gathered_plan(tokens, segment_ids, valid_len, qkv_weight, out_weight, up_weight, down_weight, conv_weight, vectors, cotangent):
    count, seq, width = tokens.shape
    own = qkv_weight.shape[0]
    dp = width // own
    columns = jnp.stack([conv_weight[0], conv_weight[1], conv_weight[2], *vectors], axis=1)
    narrow = jnp.concatenate([qkv_weight, jnp.pad(columns, ((0, 0), (0, VECTORS - 7))), out_weight], axis=1)
    wide = lax.all_gather(narrow, "dp", axis=0, tiled=True)
    both = lax.all_gather(jnp.concatenate([up_weight, down_weight], axis=0), "mp", axis=1, tiled=True)
    ff = both.shape[1]
    shards = ff // width
    both = lax.all_gather(both, "dp", axis=0).reshape(dp, 2, own, shards, width)
    both = both.transpose(3, 1, 0, 2, 4).reshape(2 * ff, width)
    column = jnp.concatenate([both, wide[:, 3 * width + VECTORS :]], axis=0)
    index = jnp.zeros((1,), jnp.int32)
    five, mixed, v, raised, facts, packed, weight = run_forward(
        index, tokens, segment_ids, valid_len, [wide[:, : 3 * width + VECTORS]]
    )
    hidden, mixed_attn, grad_mixed, grad_att, sums2, down, grads = run_feed_forward(
        index, five, mixed, cotangent, packed, [column], shards
    )
    kept = (five, mixed, v, raised, facts)
    layer_out = run_layer_output(hidden, mixed_attn, down, cotangent.shape, None, 0, 1)
    input_grad, sums, grad_qkv = run_backward(index, weight, kept, (grad_att, grad_mixed), packed, sums2, 1)
    grad_ff = grads[0, :, : 2 * ff].reshape(width, shards, 2, width).transpose(0, 2, 1, 3).reshape(width, 2 * ff)
    grad_ff = lax.psum_scatter(grad_ff, "dp", scatter_dimension=0, tiled=True).reshape(own, 2, ff)
    grad_ff = lax.psum_scatter(grad_ff, "mp", scatter_dimension=2, tiled=True).astype(F32)
    grad_attn = jnp.concatenate([grad_qkv[0], grads[0, :, 2 * ff :]], axis=1)
    grad_attn = lax.psum_scatter(grad_attn, "dp", scatter_dimension=0, tiled=True)
    grad_attn = lax.psum(grad_attn, "mp").astype(F32)
    sums = lax.psum(sums, ("dp", "mp"))
    sums = lax.dynamic_slice_in_dim(sums, lax.axis_index("dp") * own, own, axis=1)
    return (
        layer_out, input_grad, grad_attn[:, : 3 * width], grad_attn[:, 3 * width :],
        grad_ff[:, 0], grad_ff[:, 1], sums[0:3], sums[3], sums[4], sums[5], sums[6],
    )


def on_device(
    tokens, segment_ids, valid_len, qkv_weight, out_weight, up_weight, down_weight, conv_weight,
    ln1_gain, ln1_shift, ln2_gain, ln2_shift, cotangent,
):
    own, ffs = up_weight.shape
    direct = own % 16 == 0 and ffs == tokens.shape[2] and own <= VECTORS and lax.axis_size("mp") == 4
    plan = direct_plan if direct else gathered_plan
    return plan(
        tokens, segment_ids, valid_len, qkv_weight, out_weight, up_weight, down_weight, conv_weight,
        (ln1_gain, ln1_shift, ln2_gain, ln2_shift), cotangent,
    )


def solution(mesh):
    rows = P(("dp", "mp"), None, None)
    weights = (P("dp", None), P("dp", None), P("dp", "mp"), P("dp", "mp"), P(None, "dp"))
    vectors = (P("dp"),) * 4
    return jax.shard_map(
        on_device,
        mesh=mesh,
        in_specs=(rows, P(("dp", "mp"), None), P(("dp", "mp"))) + weights + vectors + (rows,),
        out_specs=(rows, rows) + weights + vectors,
        check_vma=False,
    )
```
